32 devices in a mesh: gx: 8 (over z, core), gy: 4 (over y, x).
Axes of the slice: x: 2, y: 2, z: 4, core: 2. Of those that a mesh axis runs over, the one named last changes fastest.
Arguments:
- checkpoint: float32 [19, 64, 1024], P(None, 'gx', 'gy'), may hold values from 0.02 to 0.1
- cotangent: float32 [19, 64, 1024], P(None, 'gx', 'gy'), may hold values from -6 to 6
- cell_codes: int32 [4, 64, 1024], P(None, 'gx', 'gy'), may hold values from 0 to 3, as said below
- porosity: float32 [64], replicated, may hold values from 0.2 to 0.9
- baffle_index: int32 [64, 1024], P('gx', 'gy'), may hold values from 0 to 63, as said below
Outputs:
- adjoint_start: float32 [19, 64, 1024], P(None, 'gx', 'gy')
- porosity_grad: float32 [64], replicated
The draws below stay inside these ranges and needn't reach their ends.
Inputs may be any that keep to these rules, and one draw needn't show every extreme that they name: `cell_codes`: in each step and column, the cells below the surface cell are all 1 or all 3, the surface cell is 2 and the cells above are 0; the surface cell's depth index lies between 8 and 24; the columns of code 3 fill whole tiles of 4 x 4 columns and are the same in all steps. `baffle_index`: constant over each tile of 4 x 4 columns and all depths; each value names exactly two tiles.
All inputs are finite; a program needn't handle non-finite values.
Results may differ from the reference program's by a relative error of at most 0.0003.
Values sent between devices are 32-bit elements; how exact they have to be, the bound alone decides.
No kernel may reach another device: no remote copies, remote signals or barrier semaphores. Data moves between devices by JAX's collectives and lax.ppermute only.
A program may use at most 128 MiB of HBM per device.

```python
import jax
import jax.numpy as jnp
import numpy as np
from jax import lax

Q = 19
STEPS = 4
TILE = 4
BX = 8
NZ = 32
NX = 64
NY = 32
NPANEL = 64


def draw_cell_codes(key, part):
    key = jax.random.fold_in(key, 11)
    height_key, tile_key = jax.random.split(key)
    heights = jax.random.randint(height_key, (STEPS, NX, NY, 1), NZ // 4, 3 * NZ // 4 + 1)
    flags = jax.random.randint(tile_key, (NX // TILE, NY // TILE), 0, 3) == 0
    flags = flags.at[0, 0].set(True)
    flags = jnp.repeat(jnp.repeat(flags, TILE, axis=0), TILE, axis=1)[None, :, :, None]
    depth = jnp.arange(NZ).reshape(1, 1, 1, NZ)
    below = jnp.where(flags, 3, 1)
    codes = jnp.where(depth < heights, below, jnp.where(depth == heights, 2, 0))
    return codes.reshape(STEPS, NX, NY * NZ).astype(jnp.int32)


def draw_baffle_index(key, part):
    key = jax.random.fold_in(key, 23)
    tiles = NX // TILE * (NY // TILE)
    order = jax.random.permutation(key, tiles) % (tiles // 2)
    grid = order.reshape(NX // TILE, NY // TILE)
    grid = jnp.repeat(jnp.repeat(grid, TILE, axis=0), TILE, axis=1)
    whole = jnp.broadcast_to(grid[:, :, None], (NX, NY, NZ))
    return whole.reshape(NX, NY * NZ).astype(jnp.int32)


def level_of(rng, dims, shards, low, high):
    loudness = 1.0
    for dim, shards_of in shards:
        steps = jax.random.uniform(jax.random.fold_in(jax.random.fold_in(rng, 6), dim), (shards_of,), jnp.float32, low / len(shards), high / len(shards))
        loudness = loudness * jnp.repeat(jnp.exp(steps), dims[dim] // shards_of).reshape((-1,) + (1,) * (len(dims) - 1 - dim))
    return loudness


def centred(stream_key, dims, deviation, bound, cuts=(), held_as=jnp.bfloat16):
    result = deviation * jax.random.normal(stream_key, dims, jnp.float32)
    if cuts:
        result = result * level_of(stream_key, dims, cuts, -0.22, 0.18)
    return jnp.clip(result, -bound, bound).astype(held_as)


def setup_inputs(seed: int = 0) -> dict:
    splits = jax.random.split(jax.random.key(seed), 6)
    return {
        "checkpoint": jnp.clip(0.02 + 0.08 * jax.random.uniform(splits[0], (Q, NX, NY * NZ), jnp.float32) ** level_of(splits[0], (Q, NX, NY * NZ), ((1, 8), (2, 4)), -0.2, 0.2), 0.02, 0.1),
        "cotangent": centred(splits[1], (Q, NX, NY * NZ), 1.0, 6.0, ((1, 8), (2, 4)), jnp.float32),
        "cell_codes": draw_cell_codes(jax.random.fold_in(splits[5], 71), 0),
        "porosity": jnp.clip(jax.random.uniform(splits[3], (NPANEL,), jnp.float32, 0.2, 0.9), 0.2, 0.9),
        "baffle_index": draw_baffle_index(jax.random.fold_in(splits[5], 71), 0),
    }


VELOCITIES = [(0, 0, 0), (1, 0, 0), (-1, 0, 0), (0, 1, 0), (0, -1, 0), (0, 0, 1), (0, 0, -1), (1, 1, 0), (-1, -1, 0), (1, -1, 0), (-1, 1, 0), (1, 0, 1), (-1, 0, -1), (1, 0, -1), (-1, 0, 1), (0, 1, 1), (0, -1, -1), (0, 1, -1), (0, -1, 1)]
OPPOSITE = [0, 2, 1, 4, 3, 6, 5, 8, 7, 10, 9, 12, 11, 14, 13, 16, 15, 18, 17]
WEIGHTS = [1.0 / 3.0] + [1.0 / 18.0] * 6 + [1.0 / 36.0] * 12
OMEGA = 1.6
ACCEL = (0.002, 0.0, -0.003)
VELOCITY_TABLE = np.array(VELOCITIES, np.float32)
WEIGHT_TABLE = np.array(WEIGHTS, np.float32)
OPPOSITE_TABLE = np.array(OPPOSITE, np.int32)

def collide(field, codes, phi):
    extent = (len(VELOCITIES),) + (1,) * (field.ndim - 1)
    density = lax.optimization_barrier(jnp.sum(field, axis=0))
    velocity = []
    for axis_number in range(3):
        column = jnp.asarray(VELOCITY_TABLE[:, axis_number].reshape(extent), field.dtype)
        velocity.append(lax.optimization_barrier(jnp.sum(column * field, axis=0)) / density + ACCEL[axis_number] / OMEGA)
    square = velocity[0] * velocity[0] + velocity[1] * velocity[1] + velocity[2] * velocity[2]
    along = jnp.zeros_like(field)
    for axis_number in range(3):
        column = jnp.asarray(VELOCITY_TABLE[:, axis_number].reshape(extent), field.dtype)
        along = along + column * velocity[axis_number][None]
    weight = jnp.asarray(WEIGHT_TABLE.reshape(extent), field.dtype)
    equilib = weight * (1.0 + 3.0 * along + 4.5 * along * along - 1.5 * square[None])
    bulk = field - OMEGA * (field - density[None] * equilib)
    surface = field - OMEGA * (field - equilib)
    porous = phi[None] * bulk + (1.0 - phi[None]) * field[OPPOSITE_TABLE]
    gas_value = jnp.zeros_like(field) + weight
    kinds = codes[None]
    return jnp.where(kinds == 1, bulk, jnp.where(kinds == 2, surface, jnp.where(kinds == 3, porous, gas_value)))

def bounce(padded, field, sign, coords, extents):
    xpos, ypos, zpos = coords
    size_x, size_y, size_z = (field.shape[1], field.shape[2], field.shape[3])
    results = []
    for number, vector in enumerate(VELOCITIES):
        shift_x, shift_y, shift_z = (sign * vector[0], sign * vector[1], sign * vector[2])
        pulled = padded[number, 1 - shift_x:1 - shift_x + size_x, 1 - shift_y:1 - shift_y + size_y, 1 - shift_z:1 - shift_z + size_z]
        outside = (xpos - shift_x < 0) | (xpos - shift_x >= extents[0]) | (ypos - shift_y < 0) | (ypos - shift_y >= extents[1]) | (zpos - shift_z < 0) | (zpos - shift_z >= extents[2])
        results.append(jnp.where(outside, field[OPPOSITE[number]], pulled))
    return jnp.stack(results)

def stream(field, coords):
    padded = jnp.pad(field, ((0, 0), (1, 1), (1, 1), (1, 1)))
    return bounce(padded, field, 1, coords, (NX, NY, NZ))

def reference(checkpoint, cotangent, cell_codes, porosity, baffle_index):
    coords = (jnp.arange(NX).reshape(NX, 1, 1), jnp.arange(NY).reshape(1, NY, 1), jnp.arange(NZ).reshape(1, 1, NZ))
    field = checkpoint.reshape(Q, NX, NY, NZ)
    codes_all = cell_codes.reshape(STEPS, NX, NY, NZ)
    panels = baffle_index.reshape(NX, NY, NZ)
    phi = porosity[panels]
    saved = []
    for moment in range(STEPS):
        saved.append(field)
        field = stream(collide(field, codes_all[moment], phi), coords)
    _, transpose = jax.vjp(lambda value: stream(value, coords), field)
    blocks = NX // BX

    def split(value):
        shape = value.shape
        if len(shape) == 4:
            return value.reshape(shape[0], blocks, BX, NY, NZ).transpose(1, 0, 2, 3, 4)
        return value.reshape(blocks, BX, NY, NZ)

    def join(value):
        if value.ndim == 5:
            return value.transpose(1, 0, 2, 3, 4).reshape(Q, NX, NY, NZ)
        return value.reshape(NX, NY, NZ)
    adjoint = cotangent.reshape(Q, NX, NY, NZ)
    grad_cells = jnp.zeros((NX, NY, NZ), jnp.float32)
    for moment in reversed(range(STEPS)):
        incoming, = transpose(adjoint)
        codes_now = codes_all[moment]

        def block_pull(pieces):
            state_piece, code_piece, phi_piece, back_piece = pieces
            _, pull = jax.vjp(lambda left, right: collide(left, code_piece, right), state_piece, phi_piece)
            return pull(back_piece)
        back, grad_phi = lax.map(block_pull, (split(saved[moment]), split(codes_now), split(phi), split(incoming)))
        adjoint = join(back)
        grad_cells = grad_cells + join(grad_phi)
    grad = jax.ops.segment_sum(grad_cells.reshape(-1), panels.reshape(-1), num_segments=NPANEL)
    return (adjoint.reshape(Q, NX, NY * NZ), grad)
```

```python
import functools

import jax
import jax.numpy as jnp
import numpy as np
from jax import lax
from jax.experimental import pallas as pl
from jax.experimental.pallas import tpu as pltpu
from jax.sharding import PartitionSpec as P

Q = 19
STEPS = 4
NZ = 32
ROWS = 8
LANES = 128
OMEGA = 1.6
ACCEL = (0.002, 0.0, -0.003)
SHIFT = tuple(a / OMEGA for a in ACCEL)

VELOCITIES = [
    (0, 0, 0),
    (1, 0, 0),
    (-1, 0, 0),
    (0, 1, 0),
    (0, -1, 0),
    (0, 0, 1),
    (0, 0, -1),
    (1, 1, 0),
    (-1, -1, 0),
    (1, -1, 0),
    (-1, 1, 0),
    (1, 0, 1),
    (-1, 0, -1),
    (1, 0, -1),
    (-1, 0, 1),
    (0, 1, 1),
    (0, -1, -1),
    (0, 1, -1),
    (0, -1, 1),
]
OPPOSITE = [0, 2, 1, 4, 3, 6, 5, 8, 7, 10, 9, 12, 11, 14, 13, 16, 15, 18, 17]
PAIRS = [(i, i + 1) for i in range(1, Q, 2)]
W_REST, W_AXIS, W_DIAG = 1.0 / 3.0, 1.0 / 18.0, 1.0 / 36.0

Y_COT, Y_CODE, Y_PHI, Y_HALF = 19, 38, 41, 42
HALVES = Q + 2
Y_TILES = Y_HALF + (HALVES + 1) // 2
X_COT = 5 * Q
X_CODE1 = X_COT + 4 * Q
X_CODE2 = X_CODE1 + 5
X_CODE3 = X_CODE2 + 4
X_PHI = X_CODE3 + 4
X_TILES = X_PHI + 5


def total(values):
    values = list(values)
    while len(values) > 1:
        values = [a + b for a, b in zip(values[::2], values[1::2])] + (
            [values[-1]] if len(values) % 2 else []
        )
    return values[0]


def along(vector, three):
    terms = None
    for c, value in zip(vector, three):
        if c == 0:
            continue
        if terms is None:
            terms = value if c > 0 else -value
        else:
            terms = terms + value if c > 0 else terms - value
    return terms


def moments(f):
    plus = {i: f[i] + f[o] for i, o in PAIRS}
    minus = {i: f[i] - f[o] for i, o in PAIRS}
    rho = total([f[0]] + [plus[i] for i, _ in PAIRS])
    rinv = 1.0 / rho
    u = []
    for axis in range(3):
        terms = [
            minus[i] if VELOCITIES[i][axis] > 0 else -minus[i]
            for i, _ in PAIRS
            if VELOCITIES[i][axis] != 0
        ]
        u.append(total(terms) * rinv + SHIFT[axis])
    return plus, minus, rho, rinv, u


def coefficients(kind, phi, rinv):
    baffle = kind == 3.0
    gas = kind == 0.0
    even = jnp.where(gas, 0.0, jnp.where(baffle, 0.5 - 0.5 * OMEGA * phi, 0.5 * (1.0 - OMEGA)))
    odd = jnp.where(
        gas, 0.0, jnp.where(baffle, (1.0 - 0.5 * OMEGA) * phi - 0.5, 0.5 * (1.0 - OMEGA))
    )
    slope = jnp.where(
        baffle,
        OMEGA * phi,
        jnp.where(kind == 1.0, OMEGA, jnp.where(kind == 2.0, OMEGA * rinv, 0.0)),
    )
    return even, odd, slope


def collide(f, kind, phi, parts):
    plus, minus, rho, rinv, u = parts
    even, odd, slope = coefficients(kind, phi, rinv)
    scale = slope * rho
    rest = 1.0 - 1.5 * (u[0] * u[0] + u[1] * u[1] + u[2] * u[2])
    base = scale * rest + jnp.where(kind == 0.0, 1.0, 0.0)
    out = [None] * Q
    out[0] = 2.0 * even * f[0] + W_REST * base
    for weight, pairs in ((W_AXIS, PAIRS[:3]), (W_DIAG, PAIRS[3:])):
        flat = weight * base
        three = (3.0 * weight) * scale
        for i, o in pairs:
            cu = along(VELOCITIES[i], u)
            lin = three * cu
            ev = even * plus[i] + (flat + 1.5 * lin * cu)
            od = odd * minus[i] + lin
            out[i] = ev + od
            out[o] = ev - od
    return out


def collide_back(b, kind, phi, rho, rinv, u, state=None):
    even, odd, slope = coefficients(kind, phi, rinv)
    plus = {i: b[i] + b[o] for i, o in PAIRS}
    minus = {i: b[i] - b[o] for i, o in PAIRS}
    rest = 1.0 - 1.5 * (u[0] * u[0] + u[1] * u[1] + u[2] * u[2])
    u_half = [1.5 * c for c in u]
    weighted = W_REST * b[0]
    energy = 0.0
    vector = [0.0, 0.0, 0.0]
    for weight, pairs in ((W_AXIS, PAIRS[:3]), (W_DIAG, PAIRS[3:])):
        weighted = weighted + weight * total([plus[i] for i, _ in pairs])
        energies, parts = [], ([], [], [])
        for i, _ in pairs:
            cu = along(VELOCITIES[i], u)
            half = along(VELOCITIES[i], u_half) * plus[i]
            first = minus[i] + half
            energies.append(cu * first)
            second = first + half
            for axis in range(3):
                c = VELOCITIES[i][axis]
                if c:
                    parts[axis].append(second if c > 0 else -second)
        energy = energy + (3.0 * weight) * total(energies)
        vector = [vector[k] + (3.0 * weight) * total(parts[k]) for k in range(3)]
    energy = energy + rest * weighted
    vector = [vector[k] - (3.0 * weighted) * u[k] for k in range(3)]
    push = [slope * v for v in vector]
    inner = total([push[k] * (u[k] - SHIFT[k]) for k in range(3)])
    shared = jnp.where(kind == 2.0, 0.0, slope) * energy - inner
    out = [None] * Q
    out[0] = 2.0 * even * b[0] + shared
    for i, o in PAIRS:
        ev = even * plus[i] + shared
        od = odd * minus[i] + along(VELOCITIES[i], push)
        out[i] = ev + od
        out[o] = ev - od
    if state is None:
        return out, None
    evens = total([plus[i] * (state[i] + state[o]) for i, o in PAIRS])
    odds = total([minus[i] * (state[i] - state[o]) for i, o in PAIRS])
    term = (
        -OMEGA * (b[0] * state[0] + 0.5 * evens)
        + (1.0 - 0.5 * OMEGA) * odds
        + OMEGA * rho * energy
    )
    return out, jnp.where(kind == 3.0, term, 0.0)


def wall_masks(sign_rows, own_low, own_high, edges):
    lane = lax.broadcasted_iota(jnp.int32, (ROWS, LANES), 1)
    row = lax.broadcasted_iota(jnp.int32, (ROWS, LANES), 0)
    x_low, x_high, y_low, y_high = edges
    depth = lane % NZ
    masks = {}
    masks[2, 1] = depth == 0
    masks[2, -1] = depth == NZ - 1
    masks[1, 1] = lane < jnp.where(own_low, y_low * NZ, 0)
    masks[1, -1] = lane >= jnp.where(own_high, LANES - y_high * NZ, LANES)
    if sign_rows:
        masks[0, 1] = row < x_low
        masks[0, -1] = row >= ROWS - x_high
    return masks


def stream_tile(load, sign, masks, lane):
    cross_low, cross_high = lane >= LANES - NZ, lane < NZ
    combined = {}
    out = []
    for i, vector in enumerate(VELOCITIES):
        v = tuple(sign * c for c in vector)
        value = load(i, 0, -v[0])
        if v[1] == 1:
            value = jnp.where(cross_low, load(i, -1, -v[0]), value)
        elif v[1] == -1:
            value = jnp.where(cross_high, load(i, 1, -v[0]), value)
        amount = (v[1] * NZ + v[2]) % LANES
        if amount:
            value = pltpu.roll(value, amount, 1)
        outside = None
        if v not in combined:
            for axis in range(3):
                if v[axis] and (axis, v[axis]) in masks:
                    wall = masks[axis, v[axis]]
                    outside = wall if outside is None else outside | wall
            combined[v] = outside
        outside = combined[v]
        if outside is not None:
            value = jnp.where(outside, load(OPPOSITE[i], 0, 0), value)
        out.append(value)
    return out


def panel_field(porosity_ref, panels_ref, tile):
    row = lax.broadcasted_iota(jnp.int32, (ROWS, LANES), 0)
    upper = porosity_ref[panels_ref[0, tile * LANES]]
    lower = porosity_ref[panels_ref[4, tile * LANES]]
    return jnp.where(row < 4, upper, lower)


def pack_y(porosity_ref, panels_ref, f_ref, cot_ref, codes_ref, up_ref, down_ref, own_ref):
    lane = lax.broadcasted_iota(jnp.int32, (ROWS, LANES), 1)
    high = lane >= LANES // 2
    for tile, out_ref in ((0, down_ref), (1, up_ref)):
        lanes = pl.ds(tile * LANES, LANES)
        phi = panel_field(porosity_ref, panels_ref, tile)
        f = [f_ref[i, :, lanes] for i in range(Q)]
        kinds = [codes_ref[s, :, lanes].astype(jnp.float32) for s in range(STEPS)]
        g = collide(f, kinds[0], phi, moments(f))
        for i in range(Q):
            own_ref[2 * i + tile] = g[i]
            out_ref[i] = g[i]
            out_ref[Y_COT + i] = cot_ref[i, :, lanes]
        for s in range(1, STEPS):
            out_ref[Y_CODE + s - 1] = kinds[s]
        out_ref[Y_PHI] = phi
        outer = g + [kinds[1], phi]
        other_ref = down_ref if tile == 1 else up_ref
        keep = high if tile == 0 else ~high
        for n in range(0, HALVES, 2):
            value = outer[n]
            if n + 1 < HALVES:
                value = jnp.where(keep, value, pltpu.roll(outer[n + 1], LANES // 2, 1))
            other_ref[Y_HALF + n // 2] = value


def pack_x(porosity_ref, panels_ref, own_ref, cot_ref, codes_ref, left_ref, right_ref, out_ref):
    lane = lax.broadcasted_iota(jnp.int32, (ROWS, LANES), 1)
    high = lane >= LANES // 2

    def outer(n):
        left, right = left_ref[Y_HALF + n // 2], right_ref[Y_HALF + n // 2]
        if n % 2 == 0:
            return jnp.where(high, left, right)
        return pltpu.roll(jnp.where(high, right, left), LANES // 2, 1)

    for i in range(Q):
        out_ref[5 * i] = outer(i)
        out_ref[5 * i + 1] = left_ref[i]
        out_ref[5 * i + 2] = own_ref[2 * i]
        out_ref[5 * i + 3] = own_ref[2 * i + 1]
        out_ref[5 * i + 4] = right_ref[i]
        out_ref[X_COT + 4 * i] = left_ref[Y_COT + i]
        out_ref[X_COT + 4 * i + 1] = cot_ref[i, :, pl.ds(0, LANES)]
        out_ref[X_COT + 4 * i + 2] = cot_ref[i, :, pl.ds(LANES, LANES)]
        out_ref[X_COT + 4 * i + 3] = right_ref[Y_COT + i]
    out_ref[X_CODE1] = outer(Q)
    for s, first in ((1, X_CODE1 + 1), (2, X_CODE2), (3, X_CODE3)):
        out_ref[first] = left_ref[Y_CODE + s - 1]
        for tile in range(2):
            out_ref[first + 1 + tile] = codes_ref[s, :, pl.ds(tile * LANES, LANES)].astype(
                jnp.float32
            )
        out_ref[first + 3] = right_ref[Y_CODE + s - 1]
    out_ref[X_PHI] = outer(Q + 1)
    out_ref[X_PHI + 1] = left_ref[Y_PHI]
    for tile in range(2):
        out_ref[X_PHI + 2 + tile] = panel_field(porosity_ref, panels_ref, tile)
    out_ref[X_PHI + 4] = right_ref[Y_PHI]


def steps_kernel(
    sizes,
    panels_ref,
    f_ref,
    codes_ref,
    below_ref,
    mid_ref,
    above_ref,
    adjoint_ref,
    panel_ref,
    pop_a,
    pop_b,
    cot,
    field,
    saved,
    mom,
    grad,
    sems,
):
    size_x, size_y = sizes
    copies = []
    for n, source in enumerate((below_ref, mid_ref, above_ref)):
        rows = pl.ds(ROWS * (n + 1), ROWS)
        for m, (target, first, count) in enumerate(
            (
                (pop_a, 0, X_COT),
                (cot, X_COT, X_CODE1 - X_COT),
                (field, X_CODE1, X_TILES - X_CODE1),
            )
        ):
            copy = pltpu.make_async_copy(
                source.at[pl.ds(first, count)], target.at[:, rows, :], sems.at[n, m]
            )
            copy.start()
            copies.append(copy)
    for copy in copies:
        copy.wait()

    at_x, at_y = lax.axis_index("gx"), lax.axis_index("gy")
    edges = (
        jnp.where(at_x == 0, 1, 0),
        jnp.where(at_x == size_x - 1, 1, 0),
        jnp.where(at_y == 0, 1, 0),
        jnp.where(at_y == size_y - 1, 1, 0),
    )
    lane = lax.broadcasted_iota(jnp.int32, (ROWS, LANES), 1)

    def streamed(ref, tile, tiles, r, sign, masks, four):
        step = {0: tile, -1: lax.rem(tile + tiles - 1, tiles), 1: lax.rem(tile + 1, tiles)}

        def load(i, tile_step, row_step):
            return ref[tiles * i + step[tile_step], pl.ds(ROWS * (r + 1) + row_step, ROWS), :]

        return stream_tile(load, sign, masks, lane)

    def masks_of(tile, first, r):
        return wall_masks(r == 1, tile == first, tile == first + 1, edges)

    def rows_of(r):
        return pl.ds(ROWS * (r + 1), ROWS)

    def forward(source, tiles, own, s, target, target_tiles, offset):
        def body(tile, carry):
            ring = tile - offset if target_tiles != tiles else tile
            for r in range(3):
                f = streamed(source, tile, tiles, r, 1, masks_of(tile, own, r), None)
                parts = moments(f)
                _, _, rho, rinv, u = parts
                place = tile if tiles == 4 else lax.rem(tile + 4, 5)
                for n, value in enumerate((rho, rinv, *u)):
                    mom[s - 1, n, place, pl.ds(ROWS * r, ROWS), :] = value
                if r == 1:
                    for i in range(Q):
                        saved[s - 1, i, place] = f[i]
                if target is not None:
                    at = tile if tiles == 5 else tile + 1
                    first = (X_CODE1 if s == 1 else X_CODE2 - 1) - X_CODE1
                    kind = field[first + at, rows_of(r), :]
                    phi = field[X_PHI - X_CODE1 + at, rows_of(r), :]
                    g = collide(f, kind, phi, parts)
                    for i in range(Q):
                        target[target_tiles * i + ring, rows_of(r), :] = g[i]
            return carry

        start, stop = (0, 5) if target_tiles == 5 else (1, 5)
        if tiles == 4:
            start, stop = 0, 4
        lax.fori_loop(start, stop, body, 0)

    forward(pop_a, 5, 2, 1, pop_b, 5, 0)
    forward(pop_b, 5, 2, 2, pop_a, 4, 1)
    forward(pop_a, 4, 1, 3, None, 4, 0)

    def backward(source, s, target):
        def body(tile, carry):
            for r in range(3):
                b = streamed(source, tile, 4, r, -1, masks_of(tile, 1, r), None)
                rho, rinv, *u = [
                    mom[s - 1, n, tile, pl.ds(ROWS * r, ROWS), :] for n in range(5)
                ]
                first = (X_CODE1 + 1, X_CODE2, X_CODE3)[s - 1] - X_CODE1
                kind = field[first + tile, rows_of(r), :]
                phi = field[X_PHI + 1 - X_CODE1 + tile, rows_of(r), :]
                state = [saved[s - 1, i, tile] for i in range(Q)] if r == 1 else None
                back, term = collide_back(b, kind, phi, rho, rinv, u, state)
                for i in range(Q):
                    target[4 * i + tile, rows_of(r), :] = back[i]
                if r == 1:
                    grad[tile] = term if s == 3 else grad[tile] + term
            return carry

        lax.fori_loop(0, 4, body, 0)

    backward(cot, 3, pop_a)
    backward(pop_a, 2, pop_b)
    backward(pop_b, 1, pop_a)

    row = lax.broadcasted_iota(jnp.int32, (ROWS, LANES), 0)
    panel = lax.broadcasted_iota(jnp.int32, panel_ref.shape, 1)
    sums = jnp.zeros(panel_ref.shape, jnp.float32)
    for tile in range(2):
        lanes = pl.ds(tile * LANES, LANES)
        b = streamed(pop_a, tile + 1, 4, 1, -1, masks_of(tile, 0, 1), None)
        f = [f_ref[i, :, lanes] for i in range(Q)]
        kind = codes_ref[0, :, lanes].astype(jnp.float32)
        phi = field[X_PHI + 2 - X_CODE1 + tile, rows_of(1), :]
        _, _, rho, rinv, u = moments(f)
        back, term = collide_back(b, kind, phi, rho, rinv, u, f)
        for i in range(Q):
            adjoint_ref[i, :, lanes] = back[i]
        term = term + grad[tile + 1]
        for part in range(2):
            inside = (row < 4) if part == 0 else (row >= 4)
            amount = jnp.sum(jnp.where(inside, term, 0.0))
            name = panels_ref[4 * part, tile * LANES]
            sums = sums + jnp.where(panel == name, amount, 0.0)
    panel_ref[...] = sums


VMEM = pl.BlockSpec(memory_space=pltpu.VMEM)
SMEM = pl.BlockSpec(memory_space=pltpu.SMEM)
ANY = pl.BlockSpec(memory_space=pl.ANY)


def shape_of(*dims):
    return jax.ShapeDtypeStruct(dims, jnp.float32)


def on_device(sizes, checkpoint, cotangent, cell_codes, porosity, baffle_index):
    size_x, size_y = sizes
    panels = porosity.shape[0]
    devices = size_x * size_y
    params = pltpu.CompilerParams(vmem_limit_bytes=32 * 1024 * 1024)

    up, down, own = pl.pallas_call(
        pack_y,
        out_shape=(
            shape_of(Y_TILES, ROWS, LANES),
            shape_of(Y_TILES, ROWS, LANES),
            shape_of(2 * Q, ROWS, LANES),
        ),
        in_specs=[SMEM, SMEM, VMEM, VMEM, VMEM],
        out_specs=(VMEM, VMEM, VMEM),
        compiler_params=params,
        name="pack_y",
    )(porosity, baffle_index, checkpoint, cotangent, cell_codes)

    def exchange(to_next, to_last, axis, size):
        ups = [(i, i + 1) for i in range(size - 1)]
        downs = [(i + 1, i) for i in range(size - 1)]
        return lax.ppermute(to_next, axis, ups), lax.ppermute(to_last, axis, downs)

    left, right = exchange(up, down, "gy", size_y)
    ext = pl.pallas_call(
        pack_x,
        out_shape=shape_of(X_TILES, ROWS, LANES),
        in_specs=[SMEM, SMEM, VMEM, VMEM, VMEM, VMEM, VMEM],
        out_specs=VMEM,
        compiler_params=params,
        name="pack_x",
    )(porosity, baffle_index, own, cotangent, cell_codes, left, right)
    below, above = exchange(ext, ext, "gx", size_x)

    adjoint, sums = pl.pallas_call(
        functools.partial(steps_kernel, sizes),
        out_shape=(shape_of(Q, ROWS, 2 * LANES), shape_of(devices, panels)),
        in_specs=[SMEM, VMEM, VMEM, ANY, ANY, ANY],
        out_specs=(VMEM, VMEM),
        scratch_shapes=[
            pltpu.VMEM((5 * Q, 5 * ROWS, LANES), jnp.float32),
            pltpu.VMEM((5 * Q, 5 * ROWS, LANES), jnp.float32),
            pltpu.VMEM((4 * Q, 5 * ROWS, LANES), jnp.float32),
            pltpu.VMEM((X_TILES - X_CODE1, 5 * ROWS, LANES), jnp.float32),
            pltpu.VMEM((3, Q, 5, ROWS, LANES), jnp.float32),
            pltpu.VMEM((3, 5, 5, 3 * ROWS, LANES), jnp.float32),
            pltpu.VMEM((4, ROWS, LANES), jnp.float32),
            pltpu.SemaphoreType.DMA((3, 3)),
        ],
        compiler_params=params,
        name="steps",
    )(baffle_index, checkpoint, cell_codes, below, ext, above)
    gathered = lax.all_to_all(sums, ("gx", "gy"), 0, 0, tiled=True)
    return adjoint, jnp.sum(gathered, axis=0)


def solution(mesh):
    sizes = (mesh.shape["gx"], mesh.shape["gy"])
    in_specs = (P(None, "gx", "gy"), P(None, "gx", "gy"), P(None, "gx", "gy"), P(), P("gx", "gy"))
    out_specs = (P(None, "gx", "gy"), P())
    return jax.shard_map(
        functools.partial(on_device, sizes),
        mesh=mesh,
        in_specs=in_specs,
        out_specs=out_specs,
        check_vma=False,
    )
```

```python
import functools

import jax
import jax.numpy as jnp
import numpy as np
from jax import lax
from jax.experimental import pallas as pl
from jax.experimental.pallas import tpu as pltpu
from jax.sharding import PartitionSpec as P

Q = 19
STEPS = 4
NZ = 32
ROWS = 8
LANES = 128
OMEGA = 1.6
ACCEL = (0.002, 0.0, -0.003)
SHIFT = tuple(a / OMEGA for a in ACCEL)

VELOCITIES = [
    (0, 0, 0),
    (1, 0, 0),
    (-1, 0, 0),
    (0, 1, 0),
    (0, -1, 0),
    (0, 0, 1),
    (0, 0, -1),
    (1, 1, 0),
    (-1, -1, 0),
    (1, -1, 0),
    (-1, 1, 0),
    (1, 0, 1),
    (-1, 0, -1),
    (1, 0, -1),
    (-1, 0, 1),
    (0, 1, 1),
    (0, -1, -1),
    (0, 1, -1),
    (0, -1, 1),
]
OPPOSITE = [0, 2, 1, 4, 3, 6, 5, 8, 7, 10, 9, 12, 11, 14, 13, 16, 15, 18, 17]
PAIRS = [(i, i + 1) for i in range(1, Q, 2)]
W_REST, W_AXIS, W_DIAG = 1.0 / 3.0, 1.0 / 18.0, 1.0 / 36.0

Y_COT, Y_CODE, Y_PHI, Y_HALF = 19, 38, 41, 42
HALVES = Q + 2
Y_TILES = Y_HALF + (HALVES + 1) // 2
X_COT = 5 * Q
X_CODE1 = X_COT + 4 * Q
X_CODE2 = X_CODE1 + 5
X_CODE3 = X_CODE2 + 4
X_PHI = X_CODE3 + 4
X_TILES = X_PHI + 5


def total(values):
    values = list(values)
    while len(values) > 1:
        values = [a + b for a, b in zip(values[::2], values[1::2])] + (
            [values[-1]] if len(values) % 2 else []
        )
    return values[0]


def along(vector, three):
    terms = None
    for c, value in zip(vector, three):
        if c == 0:
            continue
        if terms is None:
            terms = value if c > 0 else -value
        else:
            terms = terms + value if c > 0 else terms - value
    return terms


def moments(f):
    plus = {i: f[i] + f[o] for i, o in PAIRS}
    minus = {i: f[i] - f[o] for i, o in PAIRS}
    rho = total([f[0]] + [plus[i] for i, _ in PAIRS])
    rinv = 1.0 / rho
    u = []
    for axis in range(3):
        terms = [
            minus[i] if VELOCITIES[i][axis] > 0 else -minus[i]
            for i, _ in PAIRS
            if VELOCITIES[i][axis] != 0
        ]
        u.append(total(terms) * rinv + SHIFT[axis])
    return plus, minus, rho, rinv, u


def coefficients(kind, phi, rinv):
    baffle = kind == 3.0
    gas = kind == 0.0
    even = jnp.where(gas, 0.0, jnp.where(baffle, 0.5 - 0.5 * OMEGA * phi, 0.5 * (1.0 - OMEGA)))
    odd = jnp.where(
        gas, 0.0, jnp.where(baffle, (1.0 - 0.5 * OMEGA) * phi - 0.5, 0.5 * (1.0 - OMEGA))
    )
    slope = jnp.where(
        baffle,
        OMEGA * phi,
        jnp.where(kind == 1.0, OMEGA, jnp.where(kind == 2.0, OMEGA * rinv, 0.0)),
    )
    return even, odd, slope


def collide(f, kind, phi, parts):
    plus, minus, rho, rinv, u = parts
    even, odd, slope = coefficients(kind, phi, rinv)
    scale = slope * rho
    rest = 1.0 - 1.5 * (u[0] * u[0] + u[1] * u[1] + u[2] * u[2])
    base = scale * rest + jnp.where(kind == 0.0, 1.0, 0.0)
    out = [None] * Q
    out[0] = 2.0 * even * f[0] + W_REST * base
    for weight, pairs in ((W_AXIS, PAIRS[:3]), (W_DIAG, PAIRS[3:])):
        flat = weight * base
        three = (3.0 * weight) * scale
        for i, o in pairs:
            cu = along(VELOCITIES[i], u)
            lin = three * cu
            ev = even * plus[i] + (flat + 1.5 * lin * cu)
            od = odd * minus[i] + lin
            out[i] = ev + od
            out[o] = ev - od
    return out


def collide_back(b, kind, phi, rho, rinv, u, state=None):
    even, odd, slope = coefficients(kind, phi, rinv)
    plus = {i: b[i] + b[o] for i, o in PAIRS}
    minus = {i: b[i] - b[o] for i, o in PAIRS}
    rest = 1.0 - 1.5 * (u[0] * u[0] + u[1] * u[1] + u[2] * u[2])
    u_half = [1.5 * c for c in u]
    weighted = W_REST * b[0]
    energy = 0.0
    vector = [0.0, 0.0, 0.0]
    for weight, pairs in ((W_AXIS, PAIRS[:3]), (W_DIAG, PAIRS[3:])):
        weighted = weighted + weight * total([plus[i] for i, _ in pairs])
        energies, parts = [], ([], [], [])
        for i, _ in pairs:
            cu = along(VELOCITIES[i], u)
            half = along(VELOCITIES[i], u_half) * plus[i]
            first = minus[i] + half
            energies.append(cu * first)
            second = first + half
            for axis in range(3):
                c = VELOCITIES[i][axis]
                if c:
                    parts[axis].append(second if c > 0 else -second)
        energy = energy + (3.0 * weight) * total(energies)
        vector = [vector[k] + (3.0 * weight) * total(parts[k]) for k in range(3)]
    energy = energy + rest * weighted
    vector = [vector[k] - (3.0 * weighted) * u[k] for k in range(3)]
    push = [slope * v for v in vector]
    inner = total([push[k] * (u[k] - SHIFT[k]) for k in range(3)])
    shared = jnp.where(kind == 2.0, 0.0, slope) * energy - inner
    out = [None] * Q
    out[0] = 2.0 * even * b[0] + shared
    for i, o in PAIRS:
        ev = even * plus[i] + shared
        od = odd * minus[i] + along(VELOCITIES[i], push)
        out[i] = ev + od
        out[o] = ev - od
    if state is None:
        return out, None
    evens = total([plus[i] * (state[i] + state[o]) for i, o in PAIRS])
    odds = total([minus[i] * (state[i] - state[o]) for i, o in PAIRS])
    term = (
        -OMEGA * (b[0] * state[0] + 0.5 * evens)
        + (1.0 - 0.5 * OMEGA) * odds
        + OMEGA * rho * energy
    )
    return out, jnp.where(kind == 3.0, term, 0.0)


def wall_masks(sign_rows, own_low, own_high, edges):
    lane = lax.broadcasted_iota(jnp.int32, (ROWS, LANES), 1)
    row = lax.broadcasted_iota(jnp.int32, (ROWS, LANES), 0)
    x_low, x_high, y_low, y_high = edges
    depth = lane % NZ
    masks = {}
    masks[2, 1] = depth == 0
    masks[2, -1] = depth == NZ - 1
    masks[1, 1] = lane < jnp.where(own_low, y_low * NZ, 0)
    masks[1, -1] = lane >= jnp.where(own_high, LANES - y_high * NZ, LANES)
    if sign_rows:
        masks[0, 1] = row < x_low
        masks[0, -1] = row >= ROWS - x_high
    return masks


def stream_tile(load, sign, masks, lane):
    cross_low, cross_high = lane >= LANES - NZ, lane < NZ
    combined = {}
    out = []
    for i, vector in enumerate(VELOCITIES):
        v = tuple(sign * c for c in vector)
        value = load(i, 0, -v[0])
        if v[1] == 1:
            value = jnp.where(cross_low, load(i, -1, -v[0]), value)
        elif v[1] == -1:
            value = jnp.where(cross_high, load(i, 1, -v[0]), value)
        amount = (v[1] * NZ + v[2]) % LANES
        if amount:
            value = pltpu.roll(value, amount, 1)
        outside = None
        if v not in combined:
            for axis in range(3):
                if v[axis] and (axis, v[axis]) in masks:
                    wall = masks[axis, v[axis]]
                    outside = wall if outside is None else outside | wall
            combined[v] = outside
        outside = combined[v]
        if outside is not None:
            value = jnp.where(outside, load(OPPOSITE[i], 0, 0), value)
        out.append(value)
    return out


def panel_field(porosity_ref, panels_ref, tile):
    row = lax.broadcasted_iota(jnp.int32, (ROWS, LANES), 0)
    upper = porosity_ref[panels_ref[0, tile * LANES]]
    lower = porosity_ref[panels_ref[4, tile * LANES]]
    return jnp.where(row < 4, upper, lower)


def pack_y(porosity_ref, panels_ref, f_ref, cot_ref, codes_ref, up_ref, down_ref, own_ref):
    lane = lax.broadcasted_iota(jnp.int32, (ROWS, LANES), 1)
    high = lane >= LANES // 2
    for tile, out_ref in ((0, down_ref), (1, up_ref)):
        lanes = pl.ds(tile * LANES, LANES)
        phi = panel_field(porosity_ref, panels_ref, tile)
        f = [f_ref[i, :, lanes] for i in range(Q)]
        kinds = [codes_ref[s, :, lanes].astype(jnp.float32) for s in range(STEPS)]
        g = collide(f, kinds[0], phi, moments(f))
        for i in range(Q):
            own_ref[2 * i + tile] = g[i]
            out_ref[i] = g[i]
            out_ref[Y_COT + i] = cot_ref[i, :, lanes]
        for s in range(1, STEPS):
            out_ref[Y_CODE + s - 1] = kinds[s]
        out_ref[Y_PHI] = phi
        outer = g + [kinds[1], phi]
        other_ref = down_ref if tile == 1 else up_ref
        keep = high if tile == 0 else ~high
        for n in range(0, HALVES, 2):
            value = outer[n]
            if n + 1 < HALVES:
                value = jnp.where(keep, value, pltpu.roll(outer[n + 1], LANES // 2, 1))
            other_ref[Y_HALF + n // 2] = value


def pack_x(porosity_ref, panels_ref, own_ref, cot_ref, codes_ref, left_ref, right_ref, out_ref):
    lane = lax.broadcasted_iota(jnp.int32, (ROWS, LANES), 1)
    high = lane >= LANES // 2

    def outer(n):
        left, right = left_ref[Y_HALF + n // 2], right_ref[Y_HALF + n // 2]
        if n % 2 == 0:
            return jnp.where(high, left, right)
        return pltpu.roll(jnp.where(high, right, left), LANES // 2, 1)

    for i in range(Q):
        out_ref[5 * i] = outer(i)
        out_ref[5 * i + 1] = left_ref[i]
        out_ref[5 * i + 2] = own_ref[2 * i]
        out_ref[5 * i + 3] = own_ref[2 * i + 1]
        out_ref[5 * i + 4] = right_ref[i]
        out_ref[X_COT + 4 * i] = left_ref[Y_COT + i]
        out_ref[X_COT + 4 * i + 1] = cot_ref[i, :, pl.ds(0, LANES)]
        out_ref[X_COT + 4 * i + 2] = cot_ref[i, :, pl.ds(LANES, LANES)]
        out_ref[X_COT + 4 * i + 3] = right_ref[Y_COT + i]
    out_ref[X_CODE1] = outer(Q)
    for s, first in ((1, X_CODE1 + 1), (2, X_CODE2), (3, X_CODE3)):
        out_ref[first] = left_ref[Y_CODE + s - 1]
        for tile in range(2):
            out_ref[first + 1 + tile] = codes_ref[s, :, pl.ds(tile * LANES, LANES)].astype(
                jnp.float32
            )
        out_ref[first + 3] = right_ref[Y_CODE + s - 1]
    out_ref[X_PHI] = outer(Q + 1)
    out_ref[X_PHI + 1] = left_ref[Y_PHI]
    for tile in range(2):
        out_ref[X_PHI + 2 + tile] = panel_field(porosity_ref, panels_ref, tile)
    out_ref[X_PHI + 4] = right_ref[Y_PHI]


def steps_kernel(
    sizes,
    panels_ref,
    f_ref,
    codes_ref,
    below_ref,
    mid_ref,
    above_ref,
    adjoint_ref,
    panel_ref,
    pop_a,
    pop_b,
    cot,
    field,
    saved,
    mom,
    grad,
    sems,
):
    size_x, size_y = sizes
    copies = []
    for n, source in enumerate((below_ref, mid_ref, above_ref)):
        rows = pl.ds(ROWS * (n + 1), ROWS)
        for m, (target, first, count) in enumerate(
            (
                (pop_a, 0, X_COT),
                (cot, X_COT, X_CODE1 - X_COT),
                (field, X_CODE1, X_TILES - X_CODE1),
            )
        ):
            copy = pltpu.make_async_copy(
                source.at[pl.ds(first, count)], target.at[:, rows, :], sems.at[n, m]
            )
            copy.start()
            copies.append(copy)
    for copy in copies:
        copy.wait()

    at_x, at_y = lax.axis_index("gx"), lax.axis_index("gy")
    edges = (
        jnp.where(at_x == 0, 1, 0),
        jnp.where(at_x == size_x - 1, 1, 0),
        jnp.where(at_y == 0, 1, 0),
        jnp.where(at_y == size_y - 1, 1, 0),
    )
    lane = lax.broadcasted_iota(jnp.int32, (ROWS, LANES), 1)

    def streamed(ref, tile, tiles, r, sign, masks, four):
        step = {0: tile, -1: lax.rem(tile + tiles - 1, tiles), 1: lax.rem(tile + 1, tiles)}

        def load(i, tile_step, row_step):
            return ref[tiles * i + step[tile_step], pl.ds(ROWS * (r + 1) + row_step, ROWS), :]

        return stream_tile(load, sign, masks, lane)

    def masks_of(tile, first, r):
        return wall_masks(r == 1, tile == first, tile == first + 1, edges)

    def rows_of(r):
        return pl.ds(ROWS * (r + 1), ROWS)

    def forward(source, tiles, own, s, target, target_tiles, offset):
        def body(tile, carry):
            ring = tile - offset if target_tiles != tiles else tile
            for r in range(3):
                f = streamed(source, tile, tiles, r, 1, masks_of(tile, own, r), None)
                parts = moments(f)
                _, _, rho, rinv, u = parts
                place = tile if tiles == 4 else lax.rem(tile + 4, 5)
                for n, value in enumerate((rho, rinv, *u)):
                    mom[s - 1, n, place, pl.ds(ROWS * r, ROWS), :] = value
                if r == 1:
                    for i in range(Q):
                        saved[s - 1, i, place] = f[i]
                if target is not None:
                    at = tile if tiles == 5 else tile + 1
                    first = (X_CODE1 if s == 1 else X_CODE2 - 1) - X_CODE1
                    kind = field[first + at, rows_of(r), :]
                    phi = field[X_PHI - X_CODE1 + at, rows_of(r), :]
                    g = collide(f, kind, phi, parts)
                    for i in range(Q):
                        target[target_tiles * i + ring, rows_of(r), :] = g[i]
            return carry

        start, stop = (0, 5) if target_tiles == 5 else (1, 5)
        if tiles == 4:
            start, stop = 0, 4
        lax.fori_loop(start, stop, body, 0)

    forward(pop_a, 5, 2, 1, pop_b, 5, 0)
    forward(pop_b, 5, 2, 2, pop_a, 4, 1)
    forward(pop_a, 4, 1, 3, None, 4, 0)

    def backward(source, s, target):
        def body(tile, carry):
            for r in range(3):
                b = streamed(source, tile, 4, r, -1, masks_of(tile, 1, r), None)
                rho, rinv, *u = [
                    mom[s - 1, n, tile, pl.ds(ROWS * r, ROWS), :] for n in range(5)
                ]
                first = (X_CODE1 + 1, X_CODE2, X_CODE3)[s - 1] - X_CODE1
                kind = field[first + tile, rows_of(r), :]
                phi = field[X_PHI + 1 - X_CODE1 + tile, rows_of(r), :]
                state = [saved[s - 1, i, tile] for i in range(Q)] if r == 1 else None
                back, term = collide_back(b, kind, phi, rho, rinv, u, state)
                for i in range(Q):
                    target[4 * i + tile, rows_of(r), :] = back[i]
                if r == 1:
                    grad[tile] = term if s == 3 else grad[tile] + term
            return carry

        lax.fori_loop(0, 4, body, 0)

    backward(cot, 3, pop_a)
    backward(pop_a, 2, pop_b)
    backward(pop_b, 1, pop_a)

    row = lax.broadcasted_iota(jnp.int32, (ROWS, LANES), 0)
    panel = lax.broadcasted_iota(jnp.int32, panel_ref.shape, 1)
    sums = jnp.zeros(panel_ref.shape, jnp.float32)
    for tile in range(2):
        lanes = pl.ds(tile * LANES, LANES)
        b = streamed(pop_a, tile + 1, 4, 1, -1, masks_of(tile, 0, 1), None)
        f = [f_ref[i, :, lanes] for i in range(Q)]
        kind = codes_ref[0, :, lanes].astype(jnp.float32)
        phi = field[X_PHI + 2 - X_CODE1 + tile, rows_of(1), :]
        _, _, rho, rinv, u = moments(f)
        back, term = collide_back(b, kind, phi, rho, rinv, u, f)
        for i in range(Q):
            adjoint_ref[i, :, lanes] = back[i]
        term = term + grad[tile + 1]
        for part in range(2):
            inside = (row < 4) if part == 0 else (row >= 4)
            amount = jnp.sum(jnp.where(inside, term, 0.0))
            name = panels_ref[4 * part, tile * LANES]
            sums = sums + jnp.where(panel == name, amount, 0.0)
    panel_ref[...] = sums


VMEM = pl.BlockSpec(memory_space=pltpu.VMEM)
SMEM = pl.BlockSpec(memory_space=pltpu.SMEM)
ANY = pl.BlockSpec(memory_space=pl.ANY)


def shape_of(*dims):
    return jax.ShapeDtypeStruct(dims, jnp.float32)


def on_device(sizes, checkpoint, cotangent, cell_codes, porosity, baffle_index):
    size_x, size_y = sizes
    panels = porosity.shape[0]
    params = pltpu.CompilerParams(vmem_limit_bytes=32 * 1024 * 1024)

    up, down, own = pl.pallas_call(
        pack_y,
        out_shape=(
            shape_of(Y_TILES, ROWS, LANES),
            shape_of(Y_TILES, ROWS, LANES),
            shape_of(2 * Q, ROWS, LANES),
        ),
        in_specs=[SMEM, SMEM, VMEM, VMEM, VMEM],
        out_specs=(VMEM, VMEM, VMEM),
        compiler_params=params,
        name="pack_y",
    )(porosity, baffle_index, checkpoint, cotangent, cell_codes)

    def exchange(to_next, to_last, axis, size):
        ups = [(i, i + 1) for i in range(size - 1)]
        downs = [(i + 1, i) for i in range(size - 1)]
        return lax.ppermute(to_next, axis, ups), lax.ppermute(to_last, axis, downs)

    left, right = exchange(up, down, "gy", size_y)
    ext = pl.pallas_call(
        pack_x,
        out_shape=shape_of(X_TILES, ROWS, LANES),
        in_specs=[SMEM, SMEM, VMEM, VMEM, VMEM, VMEM, VMEM],
        out_specs=VMEM,
        compiler_params=params,
        name="pack_x",
    )(porosity, baffle_index, own, cotangent, cell_codes, left, right)
    below, above = exchange(ext, ext, "gx", size_x)

    adjoint, sums = pl.pallas_call(
        functools.partial(steps_kernel, sizes),
        out_shape=(shape_of(Q, ROWS, 2 * LANES), shape_of(size_x, panels)),
        in_specs=[SMEM, VMEM, VMEM, ANY, ANY, ANY],
        out_specs=(VMEM, VMEM),
        scratch_shapes=[
            pltpu.VMEM((5 * Q, 5 * ROWS, LANES), jnp.float32),
            pltpu.VMEM((5 * Q, 5 * ROWS, LANES), jnp.float32),
            pltpu.VMEM((4 * Q, 5 * ROWS, LANES), jnp.float32),
            pltpu.VMEM((X_TILES - X_CODE1, 5 * ROWS, LANES), jnp.float32),
            pltpu.VMEM((3, Q, 5, ROWS, LANES), jnp.float32),
            pltpu.VMEM((3, 5, 5, 3 * ROWS, LANES), jnp.float32),
            pltpu.VMEM((4, ROWS, LANES), jnp.float32),
            pltpu.SemaphoreType.DMA((3, 3)),
        ],
        compiler_params=params,
        name="steps",
    )(baffle_index, checkpoint, cell_codes, below, ext, above)
    for axis, size in (("gx", size_x), ("gy", size_y)):
        gathered = lax.all_to_all(sums, axis, 0, 0, tiled=True)
        sums = jnp.broadcast_to(jnp.sum(gathered, axis=0), (size_y, panels))
    return adjoint, sums[0]


def solution(mesh):
    sizes = (mesh.shape["gx"], mesh.shape["gy"])
    in_specs = (P(None, "gx", "gy"), P(None, "gx", "gy"), P(None, "gx", "gy"), P(), P("gx", "gy"))
    out_specs = (P(None, "gx", "gy"), P())
    return jax.shard_map(
        functools.partial(on_device, sizes),
        mesh=mesh,
        in_specs=in_specs,
        out_specs=out_specs,
        check_vma=False,
    )
```

```python
import functools

import jax
import jax.numpy as jnp
import numpy as np
from jax import lax
from jax.experimental import pallas as pl
from jax.experimental.pallas import tpu as pltpu
from jax.sharding import PartitionSpec as P

Q = 19
STEPS = 4
NZ = 32
ROWS = 8
LANES = 128
OMEGA = 1.6
ACCEL = (0.002, 0.0, -0.003)
SHIFT = tuple(a / OMEGA for a in ACCEL)

VELOCITIES = [
    (0, 0, 0),
    (1, 0, 0),
    (-1, 0, 0),
    (0, 1, 0),
    (0, -1, 0),
    (0, 0, 1),
    (0, 0, -1),
    (1, 1, 0),
    (-1, -1, 0),
    (1, -1, 0),
    (-1, 1, 0),
    (1, 0, 1),
    (-1, 0, -1),
    (1, 0, -1),
    (-1, 0, 1),
    (0, 1, 1),
    (0, -1, -1),
    (0, 1, -1),
    (0, -1, 1),
]
OPPOSITE = [0, 2, 1, 4, 3, 6, 5, 8, 7, 10, 9, 12, 11, 14, 13, 16, 15, 18, 17]
PAIRS = [(i, i + 1) for i in range(1, Q, 2)]
W_REST, W_AXIS, W_DIAG = 1.0 / 3.0, 1.0 / 18.0, 1.0 / 36.0

Y_CODE1, Y_CODE2, Y_CODE3, Y_POP, Y_COT = 38, 39, 40, 41, 42
Y_TILES = 43
X_EXTRA, X_CODE13, X_CODE2 = 19, 20, 21
X_LANE = 22
X_RING = 2 * X_LANE
X_CORNER = X_RING + Q + 1
F_CODE1, F_CODE2, F_CODE3, F_PHI = 0, 5, 9, 13
FIELDS = 18
OWN_PHI = 4


def turned(axis, outward):
    return [i for i, v in enumerate(VELOCITIES) if v[axis] == outward and sum(map(abs, v)) == 2]


def total(values):
    values = list(values)
    while len(values) > 1:
        values = [a + b for a, b in zip(values[::2], values[1::2])] + (
            [values[-1]] if len(values) % 2 else []
        )
    return values[0]


def along(vector, three):
    terms = None
    for c, value in zip(vector, three):
        if c == 0:
            continue
        if terms is None:
            terms = value if c > 0 else -value
        else:
            terms = terms + value if c > 0 else terms - value
    return terms


def moments(f):
    plus = {i: f[i] + f[o] for i, o in PAIRS}
    minus = {i: f[i] - f[o] for i, o in PAIRS}
    rho = total([f[0]] + [plus[i] for i, _ in PAIRS])
    rinv = 1.0 / rho
    u = []
    for axis in range(3):
        terms = [
            minus[i] if VELOCITIES[i][axis] > 0 else -minus[i]
            for i, _ in PAIRS
            if VELOCITIES[i][axis] != 0
        ]
        u.append(total(terms) * rinv + SHIFT[axis])
    return plus, minus, rho, rinv, u


def coefficients(kind, phi, rinv):
    baffle = kind == 3.0
    gas = kind == 0.0
    even = jnp.where(gas, 0.0, jnp.where(baffle, 0.5 - 0.5 * OMEGA * phi, 0.5 * (1.0 - OMEGA)))
    odd = jnp.where(
        gas, 0.0, jnp.where(baffle, (1.0 - 0.5 * OMEGA) * phi - 0.5, 0.5 * (1.0 - OMEGA))
    )
    slope = jnp.where(
        baffle,
        OMEGA * phi,
        jnp.where(kind == 1.0, OMEGA, jnp.where(kind == 2.0, OMEGA * rinv, 0.0)),
    )
    return even, odd, slope


def collide(f, kind, phi, parts):
    plus, minus, rho, rinv, u = parts
    even, odd, slope = coefficients(kind, phi, rinv)
    scale = slope * rho
    rest = 1.0 - 1.5 * (u[0] * u[0] + u[1] * u[1] + u[2] * u[2])
    base = scale * rest + jnp.where(kind == 0.0, 1.0, 0.0)
    out = [None] * Q
    out[0] = 2.0 * even * f[0] + W_REST * base
    for weight, pairs in ((W_AXIS, PAIRS[:3]), (W_DIAG, PAIRS[3:])):
        flat = weight * base
        three = (3.0 * weight) * scale
        for i, o in pairs:
            cu = along(VELOCITIES[i], u)
            lin = three * cu
            ev = even * plus[i] + (flat + 1.5 * lin * cu)
            od = odd * minus[i] + lin
            out[i] = ev + od
            out[o] = ev - od
    return out


def collide_back(b, kind, phi, rho, rinv, u, state=None):
    even, odd, slope = coefficients(kind, phi, rinv)
    plus = {i: b[i] + b[o] for i, o in PAIRS}
    minus = {i: b[i] - b[o] for i, o in PAIRS}
    rest = 1.0 - 1.5 * (u[0] * u[0] + u[1] * u[1] + u[2] * u[2])
    u_half = [1.5 * c for c in u]
    weighted = W_REST * b[0]
    energy = 0.0
    vector = [0.0, 0.0, 0.0]
    for weight, pairs in ((W_AXIS, PAIRS[:3]), (W_DIAG, PAIRS[3:])):
        weighted = weighted + weight * total([plus[i] for i, _ in pairs])
        energies, parts = [], ([], [], [])
        for i, _ in pairs:
            cu = along(VELOCITIES[i], u)
            half = along(VELOCITIES[i], u_half) * plus[i]
            first = minus[i] + half
            energies.append(cu * first)
            second = first + half
            for axis in range(3):
                c = VELOCITIES[i][axis]
                if c:
                    parts[axis].append(second if c > 0 else -second)
        energy = energy + (3.0 * weight) * total(energies)
        vector = [vector[k] + (3.0 * weight) * total(parts[k]) for k in range(3)]
    energy = energy + rest * weighted
    vector = [vector[k] - (3.0 * weighted) * u[k] for k in range(3)]
    push = [slope * v for v in vector]
    inner = total([push[k] * (u[k] - SHIFT[k]) for k in range(3)])
    shared = jnp.where(kind == 2.0, 0.0, slope) * energy - inner
    out = [None] * Q
    out[0] = 2.0 * even * b[0] + shared
    for i, o in PAIRS:
        ev = even * plus[i] + shared
        od = odd * minus[i] + along(VELOCITIES[i], push)
        out[i] = ev + od
        out[o] = ev - od
    if state is None:
        return out, None
    evens = total([plus[i] * (state[i] + state[o]) for i, o in PAIRS])
    odds = total([minus[i] * (state[i] - state[o]) for i, o in PAIRS])
    term = (
        -OMEGA * (b[0] * state[0] + 0.5 * evens)
        + (1.0 - 0.5 * OMEGA) * odds
        + OMEGA * rho * energy
    )
    return out, jnp.where(kind == 3.0, term, 0.0)


def wall_masks(sign_rows, own_low, own_high, edges):
    lane = lax.broadcasted_iota(jnp.int32, (ROWS, LANES), 1)
    row = lax.broadcasted_iota(jnp.int32, (ROWS, LANES), 0)
    x_low, x_high, y_low, y_high = edges
    depth = lane % NZ
    masks = {}
    masks[2, 1] = depth == 0
    masks[2, -1] = depth == NZ - 1
    masks[1, 1] = lane < jnp.where(own_low, y_low * NZ, 0)
    masks[1, -1] = lane >= jnp.where(own_high, LANES - y_high * NZ, LANES)
    if sign_rows:
        masks[0, 1] = row < x_low
        masks[0, -1] = row >= ROWS - x_high
    return masks


def stream_tile(load, sign, masks, lane):
    cross_low, cross_high = lane >= LANES - NZ, lane < NZ
    combined = {}
    out = []
    for i, vector in enumerate(VELOCITIES):
        v = tuple(sign * c for c in vector)
        value = load(i, 0, -v[0])
        if v[1] == 1:
            value = jnp.where(cross_low, load(i, -1, -v[0]), value)
        elif v[1] == -1:
            value = jnp.where(cross_high, load(i, 1, -v[0]), value)
        amount = (v[1] * NZ + v[2]) % LANES
        if amount:
            value = pltpu.roll(value, amount, 1)
        outside = None
        if v not in combined:
            for axis in range(3):
                if v[axis] and (axis, v[axis]) in masks:
                    wall = masks[axis, v[axis]]
                    outside = wall if outside is None else outside | wall
            combined[v] = outside
        outside = combined[v]
        if outside is not None:
            value = jnp.where(outside, load(OPPOSITE[i], 0, 0), value)
        out.append(value)
    return out


def iotas():
    row = lax.broadcasted_iota(jnp.int32, (ROWS, LANES), 0)
    lane = lax.broadcasted_iota(jnp.int32, (ROWS, LANES), 1)
    return row, lane, lane // NZ, lane % NZ


def columns(value, count):
    amount = (count * NZ) % LANES
    return pltpu.roll(value, amount, 1) if amount else value


def lines(value, count):
    amount = count % ROWS
    return pltpu.roll(value, amount, 0) if amount else value


def pack_y(
    f_hbm,
    cot_hbm,
    codes_hbm,
    panels_hbm,
    porosity_hbm,
    up_ref,
    down_ref,
    own_ref,
    field_ref,
    f_ref,
    cot_ref,
    codes_ref,
    panels_ref,
    porosity_ref,
    sems,
):
    pieces = (
        (panels_hbm, panels_ref),
        (porosity_hbm, porosity_ref),
        (f_hbm, f_ref),
        (codes_hbm, codes_ref),
        (cot_hbm, cot_ref),
    )
    copies = [
        pltpu.make_async_copy(source, target, sems.at[n])
        for n, (source, target) in enumerate(pieces)
    ]
    for copy in copies:
        copy.start()
    for copy in copies[:4]:
        copy.wait()
    row, lane, column, depth = iotas()
    top = depth == NZ - 1

    def tile_of(ref, i, t):
        return ref[i, :, pl.ds(t * LANES, LANES)]

    codes, phis = [], []
    for t in range(2):
        upper = porosity_ref[panels_ref[0, t * LANES]]
        lower = porosity_ref[panels_ref[4, t * LANES]]
        phi = jnp.where(row < 4, upper, lower)
        kinds = [tile_of(codes_ref, s, t).astype(jnp.float32) for s in range(STEPS)]
        f = [tile_of(f_ref, i, t) for i in range(Q)]
        g = collide(f, kinds[0], phi, moments(f))
        for i in range(Q):
            own_ref[2 * i + t] = g[i]
        for s in range(STEPS):
            field_ref[2 * s + t] = kinds[s]
        field_ref[2 * OWN_PHI + t] = phi
        codes.append([jnp.where(top, phi, kinds[1]), kinds[2], kinds[3]])
    copies[4].wait()
    for out_ref, way in ((up_ref, 1), (down_ref, -1)):
        near, far = (1, 0) if way == 1 else (0, 1)
        for i in range(Q):
            deep = 3 - way * VELOCITIES[i][1]
            cot = tile_of(cot_ref, i, near)
            g_far = own_ref[2 * i + far]
            if way == 1:
                mixed = jnp.where(column >= deep, g_far, columns(cot, deep - 4))
            else:
                mixed = jnp.where(column < 4 - deep, g_far, columns(cot, 4 - deep))
            out_ref[2 * i + near] = own_ref[2 * i + near]
            out_ref[2 * i + far] = mixed
        outer = 3 if way == 1 else 0
        out_ref[Y_CODE1] = codes[near][0]
        out_ref[Y_CODE2] = codes[near][1]
        out_ref[Y_CODE3] = jnp.where(
            column == 3 - outer, columns(codes[far][0], 3 - 2 * outer), codes[near][2]
        )
        extra = None
        for k, i in enumerate(turned(1, -way)):
            value = columns(own_ref[2 * i + far], k - outer)
            extra = value if extra is None else jnp.where(column == k, value, extra)
        out_ref[Y_POP] = extra
        extra = None
        for k, i in enumerate(turned(1, way)):
            value = columns(tile_of(cot_ref, i, near), k - (1 if way == 1 else 2))
            extra = value if extra is None else jnp.where(column == k, value, extra)
        out_ref[Y_COT] = extra


def from_y(left_ref, right_ref):
    row, lane, column, depth = iotas()
    high = lane >= LANES // 2

    def population(i, c):
        if c == 1:
            return left_ref[2 * i + 1]
        if c == 4:
            return right_ref[2 * i]
        along_y = VELOCITIES[i][1]
        left, right = left_ref[2 * i], right_ref[2 * i + 1]
        if along_y == 1 and i in turned(1, 1):
            right = columns(right_ref[Y_POP], -turned(1, 1).index(i))
        if along_y == -1 and i in turned(1, -1):
            left = columns(left_ref[Y_POP], 3 - turned(1, -1).index(i))
        return jnp.where(high, left, right)

    def cotangent(i, c):
        ref, way, place, far = (left_ref, 1, 1, 0) if c == 1 else (right_ref, -1, 2, 1)
        deep = 3 - way * VELOCITIES[i][1]
        value = columns(ref[2 * i + far], way * (4 - deep))
        if i in turned(1, way):
            extra = columns(ref[Y_COT], place - turned(1, way).index(i))
            value = jnp.where(column == place, extra, value)
        return value

    def codes(s, c):
        if c == 0:
            left, right = columns(left_ref[Y_CODE3], 3), columns(right_ref[Y_CODE3], 1)
            return jnp.where(high, left, right)
        return (left_ref if c == 1 else right_ref)[(Y_CODE1, Y_CODE2, Y_CODE3)[s - 1]]

    return population, cotangent, codes


def pack_lines(out_ref, first, way, population, cotangent, codes):
    row, lane, column, depth = iotas()

    def mixed(pop, cot, deep):
        if way == 1:
            return jnp.where(row >= deep, pop, lines(cot, deep))
        return jnp.where(row < ROWS - deep, pop, lines(cot, -deep))

    for i in range(Q):
        out_ref[first + i] = mixed(population(i), cotangent(i), 3 - way * VELOCITIES[i][0])
    extra = None
    for k, i in enumerate(turned(0, -way)):
        value = lines(population(i), k - (3 if way == 1 else 4))
        extra = value if extra is None else jnp.where(row == k, value, extra)
    for k, i in enumerate(turned(0, way)):
        value = lines(cotangent(i), 4 + k - (5 if way == 1 else 2))
        extra = jnp.where(row == 4 + k, value, extra)
    out_ref[first + X_EXTRA] = extra
    out_ref[first + X_CODE13] = mixed(codes(1), codes(3), 3)
    out_ref[first + X_CODE2] = codes(2)


def from_x(ref, first, way):
    row, lane, column, depth = iotas()

    def population(i):
        value = ref[first + i]
        if i in turned(0, -way):
            place = 3 if way == 1 else 4
            extra = lines(ref[first + X_EXTRA], place - turned(0, -way).index(i))
            value = jnp.where(row == place, extra, value)
        return value

    def cotangent(i):
        value = lines(ref[first + i], -way * (3 - way * VELOCITIES[i][0]))
        if i in turned(0, way):
            place = 5 if way == 1 else 2
            extra = lines(ref[first + X_EXTRA], place - 4 - turned(0, way).index(i))
            value = jnp.where(row == place, extra, value)
        return value

    def codes(s):
        if s == 2:
            return ref[first + X_CODE2]
        value = ref[first + X_CODE13]
        return value if s == 1 else lines(value, -3 * way)

    return population, cotangent, codes


def pack_x(own_ref, cot_ref, field_ref, up_ref, down_ref):
    row, lane, column, depth = iotas()
    for t in range(2):

        def codes(s):
            value = field_ref[2 * s + t]
            return jnp.where(depth == NZ - 1, field_ref[2 * OWN_PHI + t], value) if s == 1 else value

        for out_ref, way in ((up_ref, 1), (down_ref, -1)):
            pack_lines(
                out_ref,
                X_LANE * t,
                way,
                lambda i: own_ref[2 * i + t],
                lambda i: cot_ref[i, :, pl.ds(t * LANES, LANES)],
                codes,
            )


def pack_corner(left_ref, right_ref, up_ref, down_ref):
    population, cotangent, codes = from_y(left_ref, right_ref)
    for n, c in enumerate((1, 4)):
        for out_ref, way in ((up_ref, 1), (down_ref, -1)):
            pack_lines(
                out_ref,
                X_LANE * n,
                way,
                lambda i: population(i, c),
                lambda i: cotangent(i, c),
                lambda s: codes(s, c),
            )
    for n in range(Q + 1):
        value = population(n, 0) if n < Q else codes(1, 0)
        up_ref[X_RING + n] = value
        down_ref[X_RING + n] = value


def add_panels(parts_ref, out_ref):
    out_ref[...] = jnp.sum(parts_ref[...], axis=0)


def fill(
    left_ref, right_ref, own_ref, field_ref, cot_ref, own_x, corner_x, pop, cot, field
):
    row, lane, column, depth = iotas()
    top = depth == NZ - 1
    from_left = from_y(left_ref, right_ref)

    def put(c, r, population, cotangent, codes):
        rows = pl.ds(ROWS * (r + 1), ROWS)
        for i in range(Q):
            pop[5 * i + c, rows, :] = population(i)
            if c:
                cot[4 * i + c - 1, rows, :] = cotangent(i)
        code = codes(1)
        phi = jnp.where(top, code, 0.0)
        for step in (1, 2, 4, 8, 16):
            phi = phi + pltpu.roll(phi, LANES - step, 1)
        field[F_CODE1 + c, rows, :] = jnp.where(top, 0.0, code)
        field[F_PHI + c, rows, :] = phi
        if c:
            field[F_CODE2 + c - 1, rows, :] = codes(2)
            field[F_CODE3 + c - 1, rows, :] = codes(3)

    for c in (0, 1, 4):
        put(c, 1, *(functools.partial(lambda g, n: g(n, c), get) for get in from_left))
    for t in range(2):
        rows = pl.ds(2 * ROWS, ROWS)
        for i in range(Q):
            pop[5 * i + 2 + t, rows, :] = own_ref[2 * i + t]
            cot[4 * i + 1 + t, rows, :] = cot_ref[i, :, pl.ds(t * LANES, LANES)]
        field[F_CODE1 + 2 + t, rows, :] = field_ref[2 + t]
        field[F_CODE2 + 1 + t, rows, :] = field_ref[4 + t]
        field[F_CODE3 + 1 + t, rows, :] = field_ref[6 + t]
        field[F_PHI + 2 + t, rows, :] = field_ref[2 * OWN_PHI + t]
    for way, r, side_ref, corner_ref in (
        (1, 0, own_x[0], corner_x[0]),
        (-1, 2, own_x[1], corner_x[1]),
    ):
        for t in range(2):
            put(2 + t, r, *from_x(side_ref, X_LANE * t, way))
        for n, c in enumerate((1, 4)):
            put(c, r, *from_x(corner_ref, X_LANE * n, way))
        put(
            0,
            r,
            lambda i: corner_ref[X_RING + i],
            None,
            lambda s: corner_ref[X_RING + Q],
        )


def steps_kernel(
    sizes,
    panels_hbm,
    f_ref,
    cot_ref,
    own_ref,
    own_field_ref,
    left_ref,
    right_ref,
    below_ref,
    above_ref,
    below_corner_ref,
    above_corner_ref,
    adjoint_ref,
    panel_ref,
    pop_a,
    pop_b,
    cot,
    field,
    saved,
    mom,
    grad,
    panels_ref,
    sem,
):
    size_x, size_y = sizes
    names = pltpu.make_async_copy(panels_hbm, panels_ref, sem)
    names.start()
    fill(
        left_ref,
        right_ref,
        own_ref,
        own_field_ref,
        cot_ref,
        (below_ref, above_ref),
        (below_corner_ref, above_corner_ref),
        pop_a,
        cot,
        field,
    )

    at_x, at_y = lax.axis_index("gx"), lax.axis_index("gy")
    edges = (
        jnp.where(at_x == 0, 1, 0),
        jnp.where(at_x == size_x - 1, 1, 0),
        jnp.where(at_y == 0, 1, 0),
        jnp.where(at_y == size_y - 1, 1, 0),
    )
    lane = lax.broadcasted_iota(jnp.int32, (ROWS, LANES), 1)

    def streamed(ref, tile, tiles, r, sign, masks, four):
        step = {0: tile, -1: lax.rem(tile + tiles - 1, tiles), 1: lax.rem(tile + 1, tiles)}

        def load(i, tile_step, row_step):
            return ref[tiles * i + step[tile_step], pl.ds(ROWS * (r + 1) + row_step, ROWS), :]

        return stream_tile(load, sign, masks, lane)

    def masks_of(tile, first, r):
        return wall_masks(r == 1, tile == first, tile == first + 1, edges)

    def rows_of(r):
        return pl.ds(ROWS * (r + 1), ROWS)

    def forward(source, tiles, own, s, target, target_tiles, offset):
        def body(tile, carry):
            ring = tile - offset if target_tiles != tiles else tile
            for r in range(3):
                f = streamed(source, tile, tiles, r, 1, masks_of(tile, own, r), None)
                parts = moments(f)
                _, _, rho, rinv, u = parts
                place = tile if tiles == 4 else lax.rem(tile + 4, 5)
                for n, value in enumerate((rho, rinv, *u)):
                    mom[s - 1, n, place, pl.ds(ROWS * r, ROWS), :] = value
                if r == 1:
                    for i in range(Q):
                        saved[s - 1, i, place] = f[i]
                if target is not None:
                    at = tile if tiles == 5 else tile + 1
                    first = F_CODE1 if s == 1 else F_CODE2 - 1
                    kind = field[first + at, rows_of(r), :]
                    phi = field[F_PHI + at, rows_of(r), :]
                    g = collide(f, kind, phi, parts)
                    for i in range(Q):
                        target[target_tiles * i + ring, rows_of(r), :] = g[i]
            return carry

        start, stop = (0, 5) if target_tiles == 5 else (1, 5)
        if tiles == 4:
            start, stop = 0, 4
        lax.fori_loop(start, stop, body, 0)

    forward(pop_a, 5, 2, 1, pop_b, 5, 0)
    forward(pop_b, 5, 2, 2, pop_a, 4, 1)
    forward(pop_a, 4, 1, 3, None, 4, 0)

    def backward(source, s, target):
        def body(tile, carry):
            for r in range(3):
                b = streamed(source, tile, 4, r, -1, masks_of(tile, 1, r), None)
                rho, rinv, *u = [
                    mom[s - 1, n, tile, pl.ds(ROWS * r, ROWS), :] for n in range(5)
                ]
                first = (F_CODE1 + 1, F_CODE2, F_CODE3)[s - 1]
                kind = field[first + tile, rows_of(r), :]
                phi = field[F_PHI + 1 + tile, rows_of(r), :]
                state = [saved[s - 1, i, tile] for i in range(Q)] if r == 1 else None
                back, term = collide_back(b, kind, phi, rho, rinv, u, state)
                for i in range(Q):
                    target[4 * i + tile, rows_of(r), :] = back[i]
                if r == 1:
                    grad[tile] = term if s == 3 else grad[tile] + term
            return carry

        lax.fori_loop(0, 4, body, 0)

    backward(cot, 3, pop_a)
    backward(pop_a, 2, pop_b)
    backward(pop_b, 1, pop_a)

    names.wait()
    row = lax.broadcasted_iota(jnp.int32, (ROWS, LANES), 0)
    panel = lax.broadcasted_iota(jnp.int32, panel_ref.shape, 1)
    sums = jnp.zeros(panel_ref.shape, jnp.float32)
    for tile in range(2):
        lanes = pl.ds(tile * LANES, LANES)
        b = streamed(pop_a, tile + 1, 4, 1, -1, masks_of(tile, 0, 1), None)
        f = [f_ref[i, :, lanes] for i in range(Q)]
        kind = own_field_ref[tile]
        phi = own_field_ref[2 * OWN_PHI + tile]
        _, _, rho, rinv, u = moments(f)
        back, term = collide_back(b, kind, phi, rho, rinv, u, f)
        for i in range(Q):
            adjoint_ref[i, :, lanes] = back[i]
        term = term + grad[tile + 1]
        for part in range(2):
            inside = (row < 4) if part == 0 else (row >= 4)
            amount = jnp.sum(jnp.where(inside, term, 0.0))
            name = panels_ref[4 * part, tile * LANES]
            sums = sums + jnp.where(panel == name, amount, 0.0)
    panel_ref[...] = sums


VMEM = pl.BlockSpec(memory_space=pltpu.VMEM)
HBM = pl.BlockSpec(memory_space=pltpu.HBM)


def shape_of(*dims):
    return jax.ShapeDtypeStruct(dims, jnp.float32)


def tiles_of(count):
    return shape_of(count, ROWS, LANES)


def on_device(sizes, checkpoint, cotangent, cell_codes, porosity, baffle_index):
    size_x, size_y = sizes
    panels = porosity.shape[0]
    devices = size_x * size_y

    def call(kernel, out_shape, in_specs, scratch=(), name=None):
        return pl.pallas_call(
            kernel,
            out_shape=out_shape,
            in_specs=in_specs,
            out_specs=jax.tree.map(lambda _: VMEM, out_shape),
            scratch_shapes=scratch,
            compiler_params=pltpu.CompilerParams(vmem_limit_bytes=32 * 1024 * 1024),
            name=name,
        )

    def exchange(to_next, to_last, axis, size):
        ups = [(i, i + 1) for i in range(size - 1)]
        downs = [(i + 1, i) for i in range(size - 1)]
        return lax.ppermute(to_next, axis, ups), lax.ppermute(to_last, axis, downs)

    up, down, own, field = call(
        pack_y,
        (tiles_of(Y_TILES), tiles_of(Y_TILES), tiles_of(2 * Q), tiles_of(2 * OWN_PHI + 2)),
        [HBM] * 5,
        [
            pltpu.VMEM((Q, ROWS, 2 * LANES), jnp.float32),
            pltpu.VMEM((Q, ROWS, 2 * LANES), jnp.float32),
            pltpu.VMEM((STEPS, ROWS, 2 * LANES), jnp.int32),
            pltpu.SMEM(baffle_index.shape, jnp.int32),
            pltpu.SMEM(porosity.shape, jnp.float32),
            pltpu.SemaphoreType.DMA((5,)),
        ],
        name="pack_y",
    )(checkpoint, cotangent, cell_codes, baffle_index, porosity)
    left, right = exchange(up, down, "gy", size_y)
    side_up, side_down = call(
        pack_x, (tiles_of(2 * X_LANE), tiles_of(2 * X_LANE)), [VMEM] * 3, name="pack_x"
    )(own, cotangent, field)
    below, above = exchange(side_up, side_down, "gx", size_x)
    corner_up, corner_down = call(
        pack_corner, (tiles_of(X_CORNER), tiles_of(X_CORNER)), [VMEM] * 2, name="pack_corner"
    )(left, right)
    below_corner, above_corner = exchange(corner_up, corner_down, "gx", size_x)

    adjoint, sums = call(
        functools.partial(steps_kernel, sizes),
        (shape_of(Q, ROWS, 2 * LANES), shape_of(devices, panels)),
        [HBM] + [VMEM] * 10,
        [
            pltpu.VMEM((5 * Q, 5 * ROWS, LANES), jnp.float32),
            pltpu.VMEM((5 * Q, 5 * ROWS, LANES), jnp.float32),
            pltpu.VMEM((4 * Q, 5 * ROWS, LANES), jnp.float32),
            pltpu.VMEM((FIELDS, 5 * ROWS, LANES), jnp.float32),
            pltpu.VMEM((3, Q, 5, ROWS, LANES), jnp.float32),
            pltpu.VMEM((3, 5, 5, 3 * ROWS, LANES), jnp.float32),
            pltpu.VMEM((4, ROWS, LANES), jnp.float32),
            pltpu.SMEM(baffle_index.shape, jnp.int32),
            pltpu.SemaphoreType.DMA,
        ],
        name="steps",
    )(
        baffle_index,
        checkpoint,
        cotangent,
        own,
        field,
        left,
        right,
        below,
        above,
        below_corner,
        above_corner,
    )
    gathered = lax.all_to_all(sums, ("gx", "gy"), 0, 0, tiled=True)
    totals = call(add_panels, shape_of(1, panels), [VMEM], name="add_panels")(
        gathered.reshape(devices, 1, panels)
    )
    return adjoint, totals.reshape(panels)


def solution(mesh):
    sizes = (mesh.shape["gx"], mesh.shape["gy"])
    in_specs = (P(None, "gx", "gy"), P(None, "gx", "gy"), P(None, "gx", "gy"), P(), P("gx", "gy"))
    out_specs = (P(None, "gx", "gy"), P())
    return jax.shard_map(
        functools.partial(on_device, sizes),
        mesh=mesh,
        in_specs=in_specs,
        out_specs=out_specs,
        check_vma=False,
    )
```

```python
import functools

import jax
import jax.numpy as jnp
import numpy as np
from jax import lax
from jax.experimental import pallas as pl
from jax.experimental.pallas import tpu as pltpu
from jax.sharding import PartitionSpec as P

Q = 19
STEPS = 4
NZ = 32
ROWS = 8
LANES = 128
OMEGA = 1.6
ACCEL = (0.002, 0.0, -0.003)
SHIFT = tuple(a / OMEGA for a in ACCEL)

VELOCITIES = [
    (0, 0, 0),
    (1, 0, 0),
    (-1, 0, 0),
    (0, 1, 0),
    (0, -1, 0),
    (0, 0, 1),
    (0, 0, -1),
    (1, 1, 0),
    (-1, -1, 0),
    (1, -1, 0),
    (-1, 1, 0),
    (1, 0, 1),
    (-1, 0, -1),
    (1, 0, -1),
    (-1, 0, 1),
    (0, 1, 1),
    (0, -1, -1),
    (0, 1, -1),
    (0, -1, 1),
]
OPPOSITE = [0, 2, 1, 4, 3, 6, 5, 8, 7, 10, 9, 12, 11, 14, 13, 16, 15, 18, 17]
PAIRS = [(i, i + 1) for i in range(1, Q, 2)]
W_REST, W_AXIS, W_DIAG = 1.0 / 3.0, 1.0 / 18.0, 1.0 / 36.0

Y_CODE1, Y_CODE2, Y_CODE3, Y_POP, Y_COT = 38, 39, 40, 41, 42
Y_TILES = 43
X_EXTRA, X_CODE13, X_CODE2 = 19, 20, 21
X_LANE = 22
X_RING = 2 * X_LANE
X_OWN2 = X_RING + Q + 1
X_CORNER = X_OWN2 + 1
X_SIDE = X_LANE - 1
F_CODE1, F_CODE2, F_CODE3, F_PHI = 0, 5, 9, 13
FIELDS = 18
OWN_PHI = 4


def turned(axis, outward):
    return [i for i, v in enumerate(VELOCITIES) if v[axis] == outward and sum(map(abs, v)) == 2]


def total(values):
    values = list(values)
    while len(values) > 1:
        values = [a + b for a, b in zip(values[::2], values[1::2])] + (
            [values[-1]] if len(values) % 2 else []
        )
    return values[0]


def along(vector, three):
    terms = None
    for c, value in zip(vector, three):
        if c == 0:
            continue
        if terms is None:
            terms = value if c > 0 else -value
        else:
            terms = terms + value if c > 0 else terms - value
    return terms


def moments(f):
    plus = {i: f[i] + f[o] for i, o in PAIRS}
    minus = {i: f[i] - f[o] for i, o in PAIRS}
    rho = total([f[0]] + [plus[i] for i, _ in PAIRS])
    rinv = 1.0 / rho
    u = []
    for axis in range(3):
        terms = [
            minus[i] if VELOCITIES[i][axis] > 0 else -minus[i]
            for i, _ in PAIRS
            if VELOCITIES[i][axis] != 0
        ]
        u.append(total(terms) * rinv + SHIFT[axis])
    return plus, minus, rho, rinv, u


def coefficients(kind, phi, rinv):
    baffle = kind == 3.0
    gas = kind == 0.0
    even = jnp.where(gas, 0.0, jnp.where(baffle, 0.5 - 0.5 * OMEGA * phi, 0.5 * (1.0 - OMEGA)))
    odd = jnp.where(
        gas, 0.0, jnp.where(baffle, (1.0 - 0.5 * OMEGA) * phi - 0.5, 0.5 * (1.0 - OMEGA))
    )
    slope = jnp.where(
        baffle,
        OMEGA * phi,
        jnp.where(kind == 1.0, OMEGA, jnp.where(kind == 2.0, OMEGA * rinv, 0.0)),
    )
    return even, odd, slope


def collide(f, kind, phi, parts):
    plus, minus, rho, rinv, u = parts
    even, odd, slope = coefficients(kind, phi, rinv)
    scale = slope * rho
    rest = 1.0 - 1.5 * (u[0] * u[0] + u[1] * u[1] + u[2] * u[2])
    base = scale * rest + jnp.where(kind == 0.0, 1.0, 0.0)
    out = [None] * Q
    out[0] = 2.0 * even * f[0] + W_REST * base
    for weight, pairs in ((W_AXIS, PAIRS[:3]), (W_DIAG, PAIRS[3:])):
        flat = weight * base
        three = (3.0 * weight) * scale
        for i, o in pairs:
            cu = along(VELOCITIES[i], u)
            lin = three * cu
            ev = even * plus[i] + (flat + 1.5 * lin * cu)
            od = odd * minus[i] + lin
            out[i] = ev + od
            out[o] = ev - od
    return out


def collide_back(b, kind, phi, rho, rinv, u, state=None):
    even, odd, slope = coefficients(kind, phi, rinv)
    plus = {i: b[i] + b[o] for i, o in PAIRS}
    minus = {i: b[i] - b[o] for i, o in PAIRS}
    rest = 1.0 - 1.5 * (u[0] * u[0] + u[1] * u[1] + u[2] * u[2])
    u_half = [1.5 * c for c in u]
    weighted = W_REST * b[0]
    energy = 0.0
    vector = [0.0, 0.0, 0.0]
    for weight, pairs in ((W_AXIS, PAIRS[:3]), (W_DIAG, PAIRS[3:])):
        weighted = weighted + weight * total([plus[i] for i, _ in pairs])
        energies, parts = [], ([], [], [])
        for i, _ in pairs:
            cu = along(VELOCITIES[i], u)
            half = along(VELOCITIES[i], u_half) * plus[i]
            first = minus[i] + half
            energies.append(cu * first)
            second = first + half
            for axis in range(3):
                c = VELOCITIES[i][axis]
                if c:
                    parts[axis].append(second if c > 0 else -second)
        energy = energy + (3.0 * weight) * total(energies)
        vector = [vector[k] + (3.0 * weight) * total(parts[k]) for k in range(3)]
    energy = energy + rest * weighted
    vector = [vector[k] - (3.0 * weighted) * u[k] for k in range(3)]
    push = [slope * v for v in vector]
    inner = total([push[k] * (u[k] - SHIFT[k]) for k in range(3)])
    shared = jnp.where(kind == 2.0, 0.0, slope) * energy - inner
    out = [None] * Q
    out[0] = 2.0 * even * b[0] + shared
    for i, o in PAIRS:
        ev = even * plus[i] + shared
        od = odd * minus[i] + along(VELOCITIES[i], push)
        out[i] = ev + od
        out[o] = ev - od
    if state is None:
        return out, None
    evens = total([plus[i] * (state[i] + state[o]) for i, o in PAIRS])
    odds = total([minus[i] * (state[i] - state[o]) for i, o in PAIRS])
    term = (
        -OMEGA * (b[0] * state[0] + 0.5 * evens)
        + (1.0 - 0.5 * OMEGA) * odds
        + OMEGA * rho * energy
    )
    return out, jnp.where(kind == 3.0, term, 0.0)


def wall_masks(sign_rows, own_low, own_high, edges):
    lane = lax.broadcasted_iota(jnp.int32, (ROWS, LANES), 1)
    row = lax.broadcasted_iota(jnp.int32, (ROWS, LANES), 0)
    x_low, x_high, y_low, y_high = edges
    depth = lane % NZ
    masks = {}
    masks[2, 1] = depth == 0
    masks[2, -1] = depth == NZ - 1
    masks[1, 1] = lane < jnp.where(own_low, y_low * NZ, 0)
    masks[1, -1] = lane >= jnp.where(own_high, LANES - y_high * NZ, LANES)
    if sign_rows:
        masks[0, 1] = row < x_low
        masks[0, -1] = row >= ROWS - x_high
    return masks


def stream_tile(load, sign, masks, lane):
    cross_low, cross_high = lane >= LANES - NZ, lane < NZ
    combined = {}
    out = []
    for i, vector in enumerate(VELOCITIES):
        v = tuple(sign * c for c in vector)
        value = load(i, 0, -v[0])
        if v[1] == 1:
            value = jnp.where(cross_low, load(i, -1, -v[0]), value)
        elif v[1] == -1:
            value = jnp.where(cross_high, load(i, 1, -v[0]), value)
        amount = (v[1] * NZ + v[2]) % LANES
        if amount:
            value = pltpu.roll(value, amount, 1)
        outside = None
        if v not in combined:
            for axis in range(3):
                if v[axis] and (axis, v[axis]) in masks:
                    wall = masks[axis, v[axis]]
                    outside = wall if outside is None else outside | wall
            combined[v] = outside
        outside = combined[v]
        if outside is not None:
            value = jnp.where(outside, load(OPPOSITE[i], 0, 0), value)
        out.append(value)
    return out


def iotas():
    row = lax.broadcasted_iota(jnp.int32, (ROWS, LANES), 0)
    lane = lax.broadcasted_iota(jnp.int32, (ROWS, LANES), 1)
    return row, lane, lane // NZ, lane % NZ


def columns(value, count):
    amount = (count * NZ) % LANES
    return pltpu.roll(value, amount, 1) if amount else value


def lines(value, count):
    amount = count % ROWS
    return pltpu.roll(value, amount, 0) if amount else value


def pack_own(
    f_hbm,
    cot_hbm,
    codes_hbm,
    panels_hbm,
    porosity_hbm,
    up_ref,
    down_ref,
    side_up_ref,
    side_down_ref,
    own_ref,
    field_ref,
    f_ref,
    cot_ref,
    codes_ref,
    panels_ref,
    porosity_ref,
    sems,
):
    pieces = (
        (panels_hbm, panels_ref),
        (porosity_hbm, porosity_ref),
        (f_hbm, f_ref),
        (codes_hbm, codes_ref),
        (cot_hbm, cot_ref),
    )
    copies = [
        pltpu.make_async_copy(source, target, sems.at[n])
        for n, (source, target) in enumerate(pieces)
    ]
    for copy in copies:
        copy.start()
    for copy in copies[:4]:
        copy.wait()
    row, lane, column, depth = iotas()
    top = depth == NZ - 1

    def tile_of(ref, i, t):
        return ref[i, :, pl.ds(t * LANES, LANES)]

    codes, phis = [], []
    for t in range(2):
        upper = porosity_ref[panels_ref[0, t * LANES]]
        lower = porosity_ref[panels_ref[4, t * LANES]]
        phi = jnp.where(row < 4, upper, lower)
        kinds = [tile_of(codes_ref, s, t).astype(jnp.float32) for s in range(STEPS)]
        f = [tile_of(f_ref, i, t) for i in range(Q)]
        g = collide(f, kinds[0], phi, moments(f))
        for i in range(Q):
            own_ref[2 * i + t] = g[i]
        for s in range(STEPS):
            field_ref[2 * s + t] = kinds[s]
        field_ref[2 * OWN_PHI + t] = phi
        codes.append([jnp.where(top, phi, kinds[1]), kinds[2], kinds[3]])
    copies[4].wait()
    for out_ref, way in ((up_ref, 1), (down_ref, -1)):
        near, far = (1, 0) if way == 1 else (0, 1)
        for i in range(Q):
            deep = 3 - way * VELOCITIES[i][1]
            cot = tile_of(cot_ref, i, near)
            g_far = own_ref[2 * i + far]
            if way == 1:
                mixed = jnp.where(column >= deep, g_far, columns(cot, deep - 4))
            else:
                mixed = jnp.where(column < 4 - deep, g_far, columns(cot, 4 - deep))
            out_ref[2 * i + near] = own_ref[2 * i + near]
            out_ref[2 * i + far] = mixed
        outer = 3 if way == 1 else 0
        out_ref[Y_CODE1] = codes[near][0]
        out_ref[Y_CODE2] = codes[near][1]
        out_ref[Y_CODE3] = jnp.where(
            column == 3 - outer, columns(codes[far][0], 3 - 2 * outer), codes[near][2]
        )
        extra = None
        for k, i in enumerate(turned(1, -way)):
            value = columns(own_ref[2 * i + far], k - outer)
            extra = value if extra is None else jnp.where(column == k, value, extra)
        out_ref[Y_POP] = extra
        extra = None
        for k, i in enumerate(turned(1, way)):
            value = columns(tile_of(cot_ref, i, near), k - (1 if way == 1 else 2))
            extra = value if extra is None else jnp.where(column == k, value, extra)
        out_ref[Y_COT] = extra
    for t in range(2):
        for out_ref, way in ((side_up_ref, 1), (side_down_ref, -1)):
            pack_lines(
                out_ref,
                X_SIDE * t,
                way,
                lambda i: own_ref[2 * i + t],
                lambda i: tile_of(cot_ref, i, t),
                lambda s: codes[t][s - 1],
            )


def from_y(left_ref, right_ref):
    row, lane, column, depth = iotas()
    high = lane >= LANES // 2

    def population(i, c):
        if c == 1:
            return left_ref[2 * i + 1]
        if c == 4:
            return right_ref[2 * i]
        along_y = VELOCITIES[i][1]
        left, right = left_ref[2 * i], right_ref[2 * i + 1]
        if along_y == 1 and i in turned(1, 1):
            right = columns(right_ref[Y_POP], -turned(1, 1).index(i))
        if along_y == -1 and i in turned(1, -1):
            left = columns(left_ref[Y_POP], 3 - turned(1, -1).index(i))
        return jnp.where(high, left, right)

    def cotangent(i, c):
        ref, way, place, far = (left_ref, 1, 1, 0) if c == 1 else (right_ref, -1, 2, 1)
        deep = 3 - way * VELOCITIES[i][1]
        value = columns(ref[2 * i + far], way * (4 - deep))
        if i in turned(1, way):
            extra = columns(ref[Y_COT], place - turned(1, way).index(i))
            value = jnp.where(column == place, extra, value)
        return value

    def codes(s, c):
        if c == 0:
            left, right = columns(left_ref[Y_CODE3], 3), columns(right_ref[Y_CODE3], 1)
            return jnp.where(high, left, right)
        return (left_ref if c == 1 else right_ref)[(Y_CODE1, Y_CODE2, Y_CODE3)[s - 1]]

    return population, cotangent, codes


def pack_lines(out_ref, first, way, population, cotangent, codes):
    row, lane, column, depth = iotas()

    def mixed(pop, cot, deep):
        if way == 1:
            return jnp.where(row >= deep, pop, lines(cot, deep))
        return jnp.where(row < ROWS - deep, pop, lines(cot, -deep))

    for i in range(Q):
        out_ref[first + i] = mixed(population(i), cotangent(i), 3 - way * VELOCITIES[i][0])
    extra = None
    for k, i in enumerate(turned(0, -way)):
        value = lines(population(i), k - (3 if way == 1 else 4))
        extra = value if extra is None else jnp.where(row == k, value, extra)
    for k, i in enumerate(turned(0, way)):
        value = lines(cotangent(i), 4 + k - (5 if way == 1 else 2))
        extra = jnp.where(row == 4 + k, value, extra)
    out_ref[first + X_EXTRA] = extra
    out_ref[first + X_CODE13] = mixed(codes(1), codes(3), 3)


def from_x(ref, first, way, second):
    row, lane, column, depth = iotas()

    def population(i):
        value = ref[first + i]
        if i in turned(0, -way):
            place = 3 if way == 1 else 4
            extra = lines(ref[first + X_EXTRA], place - turned(0, -way).index(i))
            value = jnp.where(row == place, extra, value)
        return value

    def cotangent(i):
        value = lines(ref[first + i], -way * (3 - way * VELOCITIES[i][0]))
        if i in turned(0, way):
            place = 5 if way == 1 else 2
            extra = lines(ref[first + X_EXTRA], place - 4 - turned(0, way).index(i))
            value = jnp.where(row == place, extra, value)
        return value

    def codes(s):
        if s == 2:
            return second
        value = ref[first + X_CODE13]
        return value if s == 1 else lines(value, -3 * way)

    return population, cotangent, codes


def pack_corner(left_ref, right_ref, field_ref, below_ref, above_ref, up_ref, down_ref):
    row, lane, column, depth = iotas()
    population, cotangent, codes = from_y(left_ref, right_ref)
    for n, c in enumerate((1, 4)):
        for out_ref, way in ((up_ref, 1), (down_ref, -1)):
            pack_lines(
                out_ref,
                X_LANE * n,
                way,
                lambda i: population(i, c),
                lambda i: cotangent(i, c),
                lambda s: codes(s, c),
            )
            out_ref[X_LANE * n + X_CODE2] = codes(2, c)
    for n in range(Q + 1):
        value = population(n, 0) if n < Q else codes(1, 0)
        up_ref[X_RING + n] = value
        down_ref[X_RING + n] = value
    first, second = field_ref[4], lines(field_ref[5], 4)
    up_ref[X_OWN2] = jnp.where(row >= 4, first, second)
    down_ref[X_OWN2] = jnp.where(row < 4, first, second)


def add_panels(parts_ref, out_ref):
    out_ref[...] = jnp.sum(parts_ref[...], axis=0)


def fill(
    left_ref, right_ref, own_ref, field_ref, cot_ref, own_x, corner_x, pop, cot, field
):
    row, lane, column, depth = iotas()
    top = depth == NZ - 1
    from_left = from_y(left_ref, right_ref)

    def put(c, r, population, cotangent, codes):
        rows = pl.ds(ROWS * (r + 1), ROWS)
        for i in range(Q):
            pop[5 * i + c, rows, :] = population(i)
            if c:
                cot[4 * i + c - 1, rows, :] = cotangent(i)
        code = codes(1)
        phi = jnp.where(top, code, 0.0)
        for step in (1, 2, 4, 8, 16):
            phi = phi + pltpu.roll(phi, LANES - step, 1)
        field[F_CODE1 + c, rows, :] = jnp.where(top, 0.0, code)
        field[F_PHI + c, rows, :] = phi
        if c:
            field[F_CODE2 + c - 1, rows, :] = codes(2)
            field[F_CODE3 + c - 1, rows, :] = codes(3)

    for c in (0, 1, 4):
        put(c, 1, *(functools.partial(lambda g, n: g(n, c), get) for get in from_left))
    for t in range(2):
        rows = pl.ds(2 * ROWS, ROWS)
        for i in range(Q):
            pop[5 * i + 2 + t, rows, :] = own_ref[2 * i + t]
            cot[4 * i + 1 + t, rows, :] = cot_ref[i, :, pl.ds(t * LANES, LANES)]
        field[F_CODE1 + 2 + t, rows, :] = field_ref[2 + t]
        field[F_CODE2 + 1 + t, rows, :] = field_ref[4 + t]
        field[F_CODE3 + 1 + t, rows, :] = field_ref[6 + t]
        field[F_PHI + 2 + t, rows, :] = field_ref[2 * OWN_PHI + t]
    for way, r, side_ref, corner_ref in (
        (1, 0, own_x[0], corner_x[0]),
        (-1, 2, own_x[1], corner_x[1]),
    ):
        for t in range(2):
            second = corner_ref[X_OWN2]
            second = lines(second, 4) if t else second
            put(2 + t, r, *from_x(side_ref, X_SIDE * t, way, second))
        for n, c in enumerate((1, 4)):
            second = corner_ref[X_LANE * n + X_CODE2]
            put(c, r, *from_x(corner_ref, X_LANE * n, way, second))
        put(
            0,
            r,
            lambda i: corner_ref[X_RING + i],
            None,
            lambda s: corner_ref[X_RING + Q],
        )


def steps_kernel(
    sizes,
    panels_hbm,
    f_ref,
    cot_ref,
    own_ref,
    own_field_ref,
    left_ref,
    right_ref,
    below_ref,
    above_ref,
    below_corner_ref,
    above_corner_ref,
    adjoint_ref,
    panel_ref,
    pop_a,
    pop_b,
    cot,
    field,
    saved,
    mom,
    grad,
    panels_ref,
    sem,
):
    size_x, size_y = sizes
    names = pltpu.make_async_copy(panels_hbm, panels_ref, sem)
    names.start()
    fill(
        left_ref,
        right_ref,
        own_ref,
        own_field_ref,
        cot_ref,
        (below_ref, above_ref),
        (below_corner_ref, above_corner_ref),
        pop_a,
        cot,
        field,
    )

    at_x, at_y = lax.axis_index("gx"), lax.axis_index("gy")
    edges = (
        jnp.where(at_x == 0, 1, 0),
        jnp.where(at_x == size_x - 1, 1, 0),
        jnp.where(at_y == 0, 1, 0),
        jnp.where(at_y == size_y - 1, 1, 0),
    )
    lane = lax.broadcasted_iota(jnp.int32, (ROWS, LANES), 1)

    def streamed(ref, tile, tiles, r, sign, masks, four):
        step = {0: tile, -1: lax.rem(tile + tiles - 1, tiles), 1: lax.rem(tile + 1, tiles)}

        def load(i, tile_step, row_step):
            return ref[tiles * i + step[tile_step], pl.ds(ROWS * (r + 1) + row_step, ROWS), :]

        return stream_tile(load, sign, masks, lane)

    def masks_of(tile, first, r):
        return wall_masks(r == 1, tile == first, tile == first + 1, edges)

    def rows_of(r):
        return pl.ds(ROWS * (r + 1), ROWS)

    def forward(source, tiles, own, s, target, target_tiles, offset):
        def body(tile, carry):
            ring = tile - offset if target_tiles != tiles else tile
            for r in range(3):
                f = streamed(source, tile, tiles, r, 1, masks_of(tile, own, r), None)
                parts = moments(f)
                _, _, rho, rinv, u = parts
                place = tile if tiles == 4 else lax.rem(tile + 4, 5)
                for n, value in enumerate((rho, rinv, *u)):
                    mom[s - 1, n, place, pl.ds(ROWS * r, ROWS), :] = value
                if r == 1:
                    for i in range(Q):
                        saved[s - 1, i, place] = f[i]
                if target is not None:
                    at = tile if tiles == 5 else tile + 1
                    first = F_CODE1 if s == 1 else F_CODE2 - 1
                    kind = field[first + at, rows_of(r), :]
                    phi = field[F_PHI + at, rows_of(r), :]
                    g = collide(f, kind, phi, parts)
                    for i in range(Q):
                        target[target_tiles * i + ring, rows_of(r), :] = g[i]
            return carry

        start, stop = (0, 5) if target_tiles == 5 else (1, 5)
        if tiles == 4:
            start, stop = 0, 4
        lax.fori_loop(start, stop, body, 0)

    forward(pop_a, 5, 2, 1, pop_b, 5, 0)
    forward(pop_b, 5, 2, 2, pop_a, 4, 1)
    forward(pop_a, 4, 1, 3, None, 4, 0)

    def backward(source, s, target):
        def body(tile, carry):
            for r in range(3):
                b = streamed(source, tile, 4, r, -1, masks_of(tile, 1, r), None)
                rho, rinv, *u = [
                    mom[s - 1, n, tile, pl.ds(ROWS * r, ROWS), :] for n in range(5)
                ]
                first = (F_CODE1 + 1, F_CODE2, F_CODE3)[s - 1]
                kind = field[first + tile, rows_of(r), :]
                phi = field[F_PHI + 1 + tile, rows_of(r), :]
                state = [saved[s - 1, i, tile] for i in range(Q)] if r == 1 else None
                back, term = collide_back(b, kind, phi, rho, rinv, u, state)
                for i in range(Q):
                    target[4 * i + tile, rows_of(r), :] = back[i]
                if r == 1:
                    grad[tile] = term if s == 3 else grad[tile] + term
            return carry

        lax.fori_loop(0, 4, body, 0)

    backward(cot, 3, pop_a)
    backward(pop_a, 2, pop_b)
    backward(pop_b, 1, pop_a)

    names.wait()
    row = lax.broadcasted_iota(jnp.int32, (ROWS, LANES), 0)
    panel = lax.broadcasted_iota(jnp.int32, panel_ref.shape, 1)
    sums = jnp.zeros(panel_ref.shape, jnp.float32)
    for tile in range(2):
        lanes = pl.ds(tile * LANES, LANES)
        b = streamed(pop_a, tile + 1, 4, 1, -1, masks_of(tile, 0, 1), None)
        f = [f_ref[i, :, lanes] for i in range(Q)]
        kind = own_field_ref[tile]
        phi = own_field_ref[2 * OWN_PHI + tile]
        _, _, rho, rinv, u = moments(f)
        back, term = collide_back(b, kind, phi, rho, rinv, u, f)
        for i in range(Q):
            adjoint_ref[i, :, lanes] = back[i]
        term = term + grad[tile + 1]
        for part in range(2):
            inside = (row < 4) if part == 0 else (row >= 4)
            amount = jnp.sum(jnp.where(inside, term, 0.0))
            name = panels_ref[4 * part, tile * LANES]
            sums = sums + jnp.where(panel == name, amount, 0.0)
    panel_ref[...] = sums


VMEM = pl.BlockSpec(memory_space=pltpu.VMEM)
HBM = pl.BlockSpec(memory_space=pltpu.HBM)
ANY = pl.BlockSpec(memory_space=pl.ANY)


def shape_of(*dims):
    return jax.ShapeDtypeStruct(dims, jnp.float32)


def tiles_of(count):
    return shape_of(count, ROWS, LANES)


def on_device(sizes, checkpoint, cotangent, cell_codes, porosity, baffle_index):
    size_x, size_y = sizes
    panels = porosity.shape[0]
    devices = size_x * size_y

    def call(kernel, out_shape, in_specs, scratch=(), name=None):
        return pl.pallas_call(
            kernel,
            out_shape=out_shape,
            in_specs=in_specs,
            out_specs=jax.tree.map(lambda _: VMEM, out_shape),
            scratch_shapes=scratch,
            compiler_params=pltpu.CompilerParams(vmem_limit_bytes=32 * 1024 * 1024),
            name=name,
        )

    def exchange(to_next, to_last, axis, size):
        ups = [(i, i + 1) for i in range(size - 1)]
        downs = [(i + 1, i) for i in range(size - 1)]
        return lax.ppermute(to_next, axis, ups), lax.ppermute(to_last, axis, downs)

    arguments = [
        pltpu.with_memory_space_constraint(value, pltpu.HBM)
        for value in (checkpoint, cotangent, cell_codes, baffle_index, porosity)
    ]
    up, down, side_up, side_down, own, field = call(
        pack_own,
        (tiles_of(Y_TILES),) * 2
        + (tiles_of(2 * X_SIDE),) * 2
        + (tiles_of(2 * Q), tiles_of(2 * OWN_PHI + 2)),
        [HBM] * 5,
        [
            pltpu.VMEM((Q, ROWS, 2 * LANES), jnp.float32),
            pltpu.VMEM((Q, ROWS, 2 * LANES), jnp.float32),
            pltpu.VMEM((STEPS, ROWS, 2 * LANES), jnp.int32),
            pltpu.SMEM(baffle_index.shape, jnp.int32),
            pltpu.SMEM(porosity.shape, jnp.float32),
            pltpu.SemaphoreType.DMA((5,)),
        ],
        name="pack_own",
    )(*arguments)
    left, right = exchange(up, down, "gy", size_y)
    below, above = exchange(side_up, side_down, "gx", size_x)
    corner_up, corner_down = call(
        pack_corner, (tiles_of(X_CORNER),) * 2, [VMEM] * 3 + [ANY] * 2, name="pack_corner"
    )(left, right, field, below, above)
    below_corner, above_corner = exchange(corner_up, corner_down, "gx", size_x)

    adjoint, sums = call(
        functools.partial(steps_kernel, sizes),
        (shape_of(Q, ROWS, 2 * LANES), shape_of(devices, panels)),
        [HBM] + [VMEM] * 10,
        [
            pltpu.VMEM((5 * Q, 5 * ROWS, LANES), jnp.float32),
            pltpu.VMEM((5 * Q, 5 * ROWS, LANES), jnp.float32),
            pltpu.VMEM((4 * Q, 5 * ROWS, LANES), jnp.float32),
            pltpu.VMEM((FIELDS, 5 * ROWS, LANES), jnp.float32),
            pltpu.VMEM((3, Q, 5, ROWS, LANES), jnp.float32),
            pltpu.VMEM((3, 5, 5, 3 * ROWS, LANES), jnp.float32),
            pltpu.VMEM((4, ROWS, LANES), jnp.float32),
            pltpu.SMEM(baffle_index.shape, jnp.int32),
            pltpu.SemaphoreType.DMA,
        ],
        name="steps",
    )(
        baffle_index,
        checkpoint,
        cotangent,
        own,
        field,
        left,
        right,
        below,
        above,
        below_corner,
        above_corner,
    )
    gathered = lax.all_to_all(sums, ("gx", "gy"), 0, 0, tiled=True)
    totals = call(add_panels, shape_of(1, panels), [VMEM], name="add_panels")(
        gathered.reshape(devices, 1, panels)
    )
    return adjoint, totals.reshape(panels)


def solution(mesh):
    sizes = (mesh.shape["gx"], mesh.shape["gy"])
    in_specs = (P(None, "gx", "gy"), P(None, "gx", "gy"), P(None, "gx", "gy"), P(), P("gx", "gy"))
    out_specs = (P(None, "gx", "gy"), P())
    return jax.shard_map(
        functools.partial(on_device, sizes),
        mesh=mesh,
        in_specs=in_specs,
        out_specs=out_specs,
        check_vma=False,
    )
```

```python
import functools

import jax
import jax.numpy as jnp
import numpy as np
from jax import lax
from jax.experimental import pallas as pl
from jax.experimental.pallas import tpu as pltpu
from jax.sharding import PartitionSpec as P

Q = 19
STEPS = 4
NZ = 32
ROWS = 8
LANES = 128
OMEGA = 1.6
ACCEL = (0.002, 0.0, -0.003)
SHIFT = tuple(a / OMEGA for a in ACCEL)

VELOCITIES = [
    (0, 0, 0),
    (1, 0, 0),
    (-1, 0, 0),
    (0, 1, 0),
    (0, -1, 0),
    (0, 0, 1),
    (0, 0, -1),
    (1, 1, 0),
    (-1, -1, 0),
    (1, -1, 0),
    (-1, 1, 0),
    (1, 0, 1),
    (-1, 0, -1),
    (1, 0, -1),
    (-1, 0, 1),
    (0, 1, 1),
    (0, -1, -1),
    (0, 1, -1),
    (0, -1, 1),
]
OPPOSITE = [0, 2, 1, 4, 3, 6, 5, 8, 7, 10, 9, 12, 11, 14, 13, 16, 15, 18, 17]
PAIRS = [(i, i + 1) for i in range(1, Q, 2)]
W_REST, W_AXIS, W_DIAG = 1.0 / 3.0, 1.0 / 18.0, 1.0 / 36.0

Y_CODE1, Y_CODE2, Y_CODE3, Y_POP, Y_COT = 38, 39, 40, 41, 42
Y_TILES = 43
X_EXTRA, X_CODE13 = 19, 20
X_LANE = 21
X_RING = 4 * X_LANE
X_CODE2 = X_RING + Q + 1
X_TILES = X_CODE2 + 2
F_CODE1, F_CODE2, F_CODE3, F_PHI = 0, 5, 9, 13
FIELDS = 18
OWN_PHI = 4


def turned(axis, outward):
    return [i for i, v in enumerate(VELOCITIES) if v[axis] == outward and sum(map(abs, v)) == 2]


def total(values):
    values = list(values)
    while len(values) > 1:
        values = [a + b for a, b in zip(values[::2], values[1::2])] + (
            [values[-1]] if len(values) % 2 else []
        )
    return values[0]


def along(vector, three):
    terms = None
    for c, value in zip(vector, three):
        if c == 0:
            continue
        if terms is None:
            terms = value if c > 0 else -value
        else:
            terms = terms + value if c > 0 else terms - value
    return terms


def moments(f):
    plus = {i: f[i] + f[o] for i, o in PAIRS}
    minus = {i: f[i] - f[o] for i, o in PAIRS}
    rho = total([f[0]] + [plus[i] for i, _ in PAIRS])
    rinv = 1.0 / rho
    u = []
    for axis in range(3):
        terms = [
            minus[i] if VELOCITIES[i][axis] > 0 else -minus[i]
            for i, _ in PAIRS
            if VELOCITIES[i][axis] != 0
        ]
        u.append(total(terms) * rinv + SHIFT[axis])
    return plus, minus, rho, rinv, u


def coefficients(kind, phi, rinv):
    baffle = kind == 3.0
    gas = kind == 0.0
    even = jnp.where(gas, 0.0, jnp.where(baffle, 0.5 - 0.5 * OMEGA * phi, 0.5 * (1.0 - OMEGA)))
    odd = jnp.where(
        gas, 0.0, jnp.where(baffle, (1.0 - 0.5 * OMEGA) * phi - 0.5, 0.5 * (1.0 - OMEGA))
    )
    slope = jnp.where(
        baffle,
        OMEGA * phi,
        jnp.where(kind == 1.0, OMEGA, jnp.where(kind == 2.0, OMEGA * rinv, 0.0)),
    )
    return even, odd, slope


def collide(f, kind, phi, parts):
    plus, minus, rho, rinv, u = parts
    even, odd, slope = coefficients(kind, phi, rinv)
    scale = slope * rho
    rest = 1.0 - 1.5 * (u[0] * u[0] + u[1] * u[1] + u[2] * u[2])
    base = scale * rest + jnp.where(kind == 0.0, 1.0, 0.0)
    out = [None] * Q
    out[0] = 2.0 * even * f[0] + W_REST * base
    for weight, pairs in ((W_AXIS, PAIRS[:3]), (W_DIAG, PAIRS[3:])):
        flat = weight * base
        three = (3.0 * weight) * scale
        for i, o in pairs:
            cu = along(VELOCITIES[i], u)
            lin = three * cu
            ev = even * plus[i] + (flat + 1.5 * lin * cu)
            od = odd * minus[i] + lin
            out[i] = ev + od
            out[o] = ev - od
    return out


def collide_back(b, kind, phi, rho, rinv, u, state=None):
    even, odd, slope = coefficients(kind, phi, rinv)
    plus = {i: b[i] + b[o] for i, o in PAIRS}
    minus = {i: b[i] - b[o] for i, o in PAIRS}
    rest = 1.0 - 1.5 * (u[0] * u[0] + u[1] * u[1] + u[2] * u[2])
    u_half = [1.5 * c for c in u]
    weighted = W_REST * b[0]
    energy = 0.0
    vector = [0.0, 0.0, 0.0]
    for weight, pairs in ((W_AXIS, PAIRS[:3]), (W_DIAG, PAIRS[3:])):
        weighted = weighted + weight * total([plus[i] for i, _ in pairs])
        energies, parts = [], ([], [], [])
        for i, _ in pairs:
            cu = along(VELOCITIES[i], u)
            half = along(VELOCITIES[i], u_half) * plus[i]
            first = minus[i] + half
            energies.append(cu * first)
            second = first + half
            for axis in range(3):
                c = VELOCITIES[i][axis]
                if c:
                    parts[axis].append(second if c > 0 else -second)
        energy = energy + (3.0 * weight) * total(energies)
        vector = [vector[k] + (3.0 * weight) * total(parts[k]) for k in range(3)]
    energy = energy + rest * weighted
    vector = [vector[k] - (3.0 * weighted) * u[k] for k in range(3)]
    push = [slope * v for v in vector]
    inner = total([push[k] * (u[k] - SHIFT[k]) for k in range(3)])
    shared = jnp.where(kind == 2.0, 0.0, slope) * energy - inner
    out = [None] * Q
    out[0] = 2.0 * even * b[0] + shared
    for i, o in PAIRS:
        ev = even * plus[i] + shared
        od = odd * minus[i] + along(VELOCITIES[i], push)
        out[i] = ev + od
        out[o] = ev - od
    if state is None:
        return out, None
    evens = total([plus[i] * (state[i] + state[o]) for i, o in PAIRS])
    odds = total([minus[i] * (state[i] - state[o]) for i, o in PAIRS])
    term = (
        -OMEGA * (b[0] * state[0] + 0.5 * evens)
        + (1.0 - 0.5 * OMEGA) * odds
        + OMEGA * rho * energy
    )
    return out, jnp.where(kind == 3.0, term, 0.0)


def wall_masks(sign_rows, own_low, own_high, edges):
    lane = lax.broadcasted_iota(jnp.int32, (ROWS, LANES), 1)
    row = lax.broadcasted_iota(jnp.int32, (ROWS, LANES), 0)
    x_low, x_high, y_low, y_high = edges
    depth = lane % NZ
    masks = {}
    masks[2, 1] = depth == 0
    masks[2, -1] = depth == NZ - 1
    masks[1, 1] = lane < jnp.where(own_low, y_low * NZ, 0)
    masks[1, -1] = lane >= jnp.where(own_high, LANES - y_high * NZ, LANES)
    if sign_rows:
        masks[0, 1] = row < x_low
        masks[0, -1] = row >= ROWS - x_high
    return masks


def stream_tile(load, sign, masks, lane):
    cross_low, cross_high = lane >= LANES - NZ, lane < NZ
    combined = {}
    out = []
    for i, vector in enumerate(VELOCITIES):
        v = tuple(sign * c for c in vector)
        value = load(i, 0, -v[0])
        if v[1] == 1:
            value = jnp.where(cross_low, load(i, -1, -v[0]), value)
        elif v[1] == -1:
            value = jnp.where(cross_high, load(i, 1, -v[0]), value)
        amount = (v[1] * NZ + v[2]) % LANES
        if amount:
            value = pltpu.roll(value, amount, 1)
        outside = None
        if v not in combined:
            for axis in range(3):
                if v[axis] and (axis, v[axis]) in masks:
                    wall = masks[axis, v[axis]]
                    outside = wall if outside is None else outside | wall
            combined[v] = outside
        outside = combined[v]
        if outside is not None:
            value = jnp.where(outside, load(OPPOSITE[i], 0, 0), value)
        out.append(value)
    return out


def iotas():
    row = lax.broadcasted_iota(jnp.int32, (ROWS, LANES), 0)
    lane = lax.broadcasted_iota(jnp.int32, (ROWS, LANES), 1)
    return row, lane, lane // NZ, lane % NZ


def columns(value, count):
    amount = (count * NZ) % LANES
    return pltpu.roll(value, amount, 1) if amount else value


def lines(value, count):
    amount = count % ROWS
    return pltpu.roll(value, amount, 0) if amount else value


class Pick:
    def __init__(self, flag, first, second):
        self.flag, self.first, self.second = flag, first, second

    def __getitem__(self, at):
        return jnp.where(self.flag, self.first[at], self.second[at])


class Deal:
    def __init__(self, even, first, second):
        self.even, self.refs, self.held = even, (first, second), {}

    def put(self, way, at, value):
        if (-way, at) not in self.held:
            self.held[way, at] = value
            return
        other = self.held.pop((-way, at))
        up, down = (value, other) if way == 1 else (other, value)
        self.refs[0][at] = jnp.where(self.even, up, down)
        self.refs[1][at] = jnp.where(self.even, down, up)


def is_even(axis):
    return lax.rem(lax.axis_index(axis), 2) == 0


def pack_own(
    f_hbm,
    cot_hbm,
    codes_hbm,
    panels_hbm,
    porosity_hbm,
    first_ref,
    second_ref,
    own_ref,
    state_ref,
    own_cot_ref,
    field_ref,
    names_ref,
    f_ref,
    cot_ref,
    codes_ref,
    panels_ref,
    porosity_ref,
    sems,
):
    pieces = (
        (panels_hbm, panels_ref),
        (porosity_hbm, porosity_ref),
        (f_hbm, f_ref),
        (codes_hbm, codes_ref),
        (cot_hbm, cot_ref),
    )
    copies = [
        pltpu.make_async_copy(source, target, sems.at[n])
        for n, (source, target) in enumerate(pieces)
    ]
    for copy in copies:
        copy.start()
    for copy in copies[:4]:
        copy.wait()
    deal = Deal(is_even("gy"), first_ref, second_ref)
    row, lane, column, depth = iotas()
    top = depth == NZ - 1

    def tile_of(ref, i, t):
        return ref[i, :, pl.ds(t * LANES, LANES)]

    codes, phis = [], []
    for t in range(2):
        names = panels_ref[0, t * LANES], panels_ref[4, t * LANES]
        phi = jnp.where(row < 4, porosity_ref[names[0]], porosity_ref[names[1]])
        names_ref[t] = jnp.where(row < 4, names[0], names[1])
        kinds = [tile_of(codes_ref, s, t).astype(jnp.float32) for s in range(STEPS)]
        f = [tile_of(f_ref, i, t) for i in range(Q)]
        g = collide(f, kinds[0], phi, moments(f))
        for i in range(Q):
            own_ref[2 * i + t] = g[i]
            state_ref[2 * i + t] = f[i]
        for s in range(STEPS):
            field_ref[2 * s + t] = kinds[s]
        field_ref[2 * OWN_PHI + t] = phi
        codes.append([jnp.where(top, phi, kinds[1]), kinds[2], kinds[3]])
    copies[4].wait()
    for i in range(Q):
        for way in (1, -1):
            near, far = (1, 0) if way == 1 else (0, 1)
            deep = 3 - way * VELOCITIES[i][1]
            cot = tile_of(cot_ref, i, near)
            g_far = own_ref[2 * i + far]
            if way == 1:
                mixed = jnp.where(column >= deep, g_far, columns(cot, deep - 4))
            else:
                mixed = jnp.where(column < 4 - deep, g_far, columns(cot, 4 - deep))
            deal.put(way, 2 * i, mixed if far == 0 else own_ref[2 * i])
            deal.put(way, 2 * i + 1, mixed if far == 1 else own_ref[2 * i + 1])
    for way in (1, -1):
        near, far = (1, 0) if way == 1 else (0, 1)
        outer = 3 if way == 1 else 0
        deal.put(way, Y_CODE1, codes[near][0])
        deal.put(way, Y_CODE2, codes[near][1])
        outside = columns(codes[far][0], 3 - 2 * outer)
        deal.put(way, Y_CODE3, jnp.where(column == 3 - outer, outside, codes[near][2]))
        extra = None
        for k, i in enumerate(turned(1, -way)):
            value = columns(own_ref[2 * i + far], k - outer)
            extra = value if extra is None else jnp.where(column == k, value, extra)
        deal.put(way, Y_POP, extra)
        extra = None
        for k, i in enumerate(turned(1, way)):
            value = columns(tile_of(cot_ref, i, near), k - (1 if way == 1 else 2))
            extra = value if extra is None else jnp.where(column == k, value, extra)
        deal.put(way, Y_COT, extra)
    for t in range(2):
        for i in range(Q):
            own_cot_ref[2 * i + t] = tile_of(cot_ref, i, t)


def from_y(left_ref, right_ref):
    row, lane, column, depth = iotas()
    high = lane >= LANES // 2

    def population(i, c):
        if c == 1:
            return left_ref[2 * i + 1]
        if c == 4:
            return right_ref[2 * i]
        along_y = VELOCITIES[i][1]
        left, right = left_ref[2 * i], right_ref[2 * i + 1]
        if along_y == 1 and i in turned(1, 1):
            right = columns(right_ref[Y_POP], -turned(1, 1).index(i))
        if along_y == -1 and i in turned(1, -1):
            left = columns(left_ref[Y_POP], 3 - turned(1, -1).index(i))
        return jnp.where(high, left, right)

    def cotangent(i, c):
        ref, way, place, far = (left_ref, 1, 1, 0) if c == 1 else (right_ref, -1, 2, 1)
        deep = 3 - way * VELOCITIES[i][1]
        value = columns(ref[2 * i + far], way * (4 - deep))
        if i in turned(1, way):
            extra = columns(ref[Y_COT], place - turned(1, way).index(i))
            value = jnp.where(column == place, extra, value)
        return value

    def codes(s, c):
        if c == 0:
            left, right = columns(left_ref[Y_CODE3], 3), columns(right_ref[Y_CODE3], 1)
            return jnp.where(high, left, right)
        return (left_ref if c == 1 else right_ref)[(Y_CODE1, Y_CODE2, Y_CODE3)[s - 1]]

    return population, cotangent, codes


def pack_lines(deal, first, population, cotangent, codes):
    row, lane, column, depth = iotas()

    def put(at, pop, cot, deep, way):
        if way == 1:
            mixed = jnp.where(row >= deep, pop, lines(cot, deep))
        else:
            mixed = jnp.where(row < ROWS - deep, pop, lines(cot, -deep))
        deal.put(way, first + at, mixed)

    for i in range(Q):
        pop, cot = population(i), cotangent(i)
        for way in (1, -1):
            put(i, pop, cot, 3 - way * VELOCITIES[i][0], way)
    for way in (1, -1):
        extra = None
        for k, i in enumerate(turned(0, -way)):
            value = lines(population(i), k - (3 if way == 1 else 4))
            extra = value if extra is None else jnp.where(row == k, value, extra)
        for k, i in enumerate(turned(0, way)):
            value = lines(cotangent(i), 4 + k - (5 if way == 1 else 2))
            extra = jnp.where(row == 4 + k, value, extra)
        deal.put(way, first + X_EXTRA, extra)
        put(X_CODE13, codes(1), codes(3), 3, way)


def from_x(ref, n, way):
    row, lane, column, depth = iotas()
    first = X_LANE * n

    def population(i):
        value = ref[first + i]
        if i in turned(0, -way):
            place = 3 if way == 1 else 4
            extra = lines(ref[first + X_EXTRA], place - turned(0, -way).index(i))
            value = jnp.where(row == place, extra, value)
        return value

    def cotangent(i):
        value = lines(ref[first + i], -way * (3 - way * VELOCITIES[i][0]))
        if i in turned(0, way):
            place = 5 if way == 1 else 2
            extra = lines(ref[first + X_EXTRA], place - 4 - turned(0, way).index(i))
            value = jnp.where(row == place, extra, value)
        return value

    def codes(s):
        if s == 2:
            return lines(ref[X_CODE2 + n // 2], 4 * (n % 2))
        value = ref[first + X_CODE13]
        return value if s == 1 else lines(value, -3 * way)

    return population, cotangent, codes


def pack_x(own_ref, cot_ref, field_ref, first_y_ref, second_y_ref, first_ref, second_ref):
    row, lane, column, depth = iotas()
    deal = Deal(is_even("gx"), first_ref, second_ref)
    population, cotangent, codes = from_y(*sides(first_y_ref, second_y_ref, "gy"))

    def own_codes(s, t):
        value = field_ref[2 * s + t]
        return jnp.where(depth == NZ - 1, field_ref[2 * OWN_PHI + t], value) if s == 1 else value

    def both_codes(at, first, second):
        second = lines(second, 4)
        deal.put(1, at, jnp.where(row >= 4, first, second))
        deal.put(-1, at, jnp.where(row < 4, first, second))

    for t in range(2):
        pack_lines(
            deal,
            X_LANE * t,
            lambda i: own_ref[2 * i + t],
            lambda i: cot_ref[2 * i + t],
            lambda s: own_codes(s, t),
        )
    for n, c in ((2, 1), (3, 4)):
        pack_lines(
            deal,
            X_LANE * n,
            lambda i: population(i, c),
            lambda i: cotangent(i, c),
            lambda s: codes(s, c),
        )
    for n in range(Q + 1):
        value = population(n, 0) if n < Q else codes(1, 0)
        first_ref[X_RING + n] = value
        second_ref[X_RING + n] = value
    both_codes(X_CODE2, own_codes(2, 0), own_codes(2, 1))
    both_codes(X_CODE2 + 1, codes(2, 1), codes(2, 4))


def sides(first_ref, second_ref, axis):
    even = is_even(axis)
    return Pick(even, second_ref, first_ref), Pick(even, first_ref, second_ref)


def add_panels(parts_ref, out_ref):
    out_ref[...] = jnp.sum(parts_ref[...], axis=0)


def fill(from_left, own_ref, field_ref, cot_ref, from_below, pop, cot, field):
    row, lane, column, depth = iotas()
    top = depth == NZ - 1

    def put(c, r, population, cotangent, codes):
        rows = pl.ds(ROWS * (r + 1), ROWS)
        for i in range(Q):
            pop[5 * i + c, rows, :] = population(i)
            if c:
                cot[4 * i + c - 1, rows, :] = cotangent(i)
        code = codes(1)
        phi = jnp.where(top, code, 0.0)
        for step in (1, 2, 4, 8, 16):
            phi = phi + pltpu.roll(phi, LANES - step, 1)
        field[F_CODE1 + c, rows, :] = jnp.where(top, 0.0, code)
        field[F_PHI + c, rows, :] = phi
        if c:
            field[F_CODE2 + c - 1, rows, :] = codes(2)
            field[F_CODE3 + c - 1, rows, :] = codes(3)

    for c in (0, 1, 4):
        put(c, 1, *(functools.partial(lambda g, n: g(n, c), get) for get in from_left))
    for t in range(2):
        rows = pl.ds(2 * ROWS, ROWS)
        for i in range(Q):
            pop[5 * i + 2 + t, rows, :] = own_ref[2 * i + t]
            cot[4 * i + 1 + t, rows, :] = cot_ref[2 * i + t]
        field[F_CODE1 + 2 + t, rows, :] = field_ref[2 + t]
        field[F_CODE2 + 1 + t, rows, :] = field_ref[4 + t]
        field[F_CODE3 + 1 + t, rows, :] = field_ref[6 + t]
        field[F_PHI + 2 + t, rows, :] = field_ref[2 * OWN_PHI + t]
    for way, r, ref in ((1, 0, from_below[0]), (-1, 2, from_below[1])):
        for n, c in enumerate((2, 3, 1, 4)):
            put(c, r, *from_x(ref, n, way))
        put(0, r, lambda i: ref[X_RING + i], None, lambda s: ref[X_RING + Q])


def steps_kernel(
    sizes,
    state_ref,
    cot_ref,
    own_ref,
    own_field_ref,
    names_ref,
    first_y_ref,
    second_y_ref,
    first_x_ref,
    second_x_ref,
    adjoint_ref,
    panel_ref,
    pop_a,
    pop_b,
    cot,
    field,
    saved,
    mom,
    grad,
):
    size_x, size_y = sizes
    fill(
        from_y(*sides(first_y_ref, second_y_ref, "gy")),
        own_ref,
        own_field_ref,
        cot_ref,
        sides(first_x_ref, second_x_ref, "gx"),
        pop_a,
        cot,
        field,
    )

    at_x, at_y = lax.axis_index("gx"), lax.axis_index("gy")
    edges = (
        jnp.where(at_x == 0, 1, 0),
        jnp.where(at_x == size_x - 1, 1, 0),
        jnp.where(at_y == 0, 1, 0),
        jnp.where(at_y == size_y - 1, 1, 0),
    )
    lane = lax.broadcasted_iota(jnp.int32, (ROWS, LANES), 1)

    def streamed(ref, tile, tiles, r, sign, masks, four):
        step = {0: tile, -1: lax.rem(tile + tiles - 1, tiles), 1: lax.rem(tile + 1, tiles)}

        def load(i, tile_step, row_step):
            return ref[tiles * i + step[tile_step], pl.ds(ROWS * (r + 1) + row_step, ROWS), :]

        return stream_tile(load, sign, masks, lane)

    def masks_of(tile, first, r):
        return wall_masks(r == 1, tile == first, tile == first + 1, edges)

    def rows_of(r):
        return pl.ds(ROWS * (r + 1), ROWS)

    def forward(source, tiles, own, s, target, target_tiles, offset):
        def body(tile, carry):
            ring = tile - offset if target_tiles != tiles else tile
            for r in range(3):
                f = streamed(source, tile, tiles, r, 1, masks_of(tile, own, r), None)
                parts = moments(f)
                _, _, rho, rinv, u = parts
                place = tile if tiles == 4 else lax.rem(tile + 4, 5)
                for n, value in enumerate((rho, rinv, *u)):
                    mom[s - 1, n, place, pl.ds(ROWS * r, ROWS), :] = value
                if r == 1:
                    for i in range(Q):
                        saved[s - 1, i, place] = f[i]
                if target is not None:
                    at = tile if tiles == 5 else tile + 1
                    first = F_CODE1 if s == 1 else F_CODE2 - 1
                    kind = field[first + at, rows_of(r), :]
                    phi = field[F_PHI + at, rows_of(r), :]
                    g = collide(f, kind, phi, parts)
                    for i in range(Q):
                        target[target_tiles * i + ring, rows_of(r), :] = g[i]
            return carry

        start, stop = (0, 5) if target_tiles == 5 else (1, 5)
        if tiles == 4:
            start, stop = 0, 4
        lax.fori_loop(start, stop, body, 0)

    forward(pop_a, 5, 2, 1, pop_b, 5, 0)
    forward(pop_b, 5, 2, 2, pop_a, 4, 1)
    forward(pop_a, 4, 1, 3, None, 4, 0)

    def backward(source, s, target):
        def body(tile, carry):
            for r in range(3):
                b = streamed(source, tile, 4, r, -1, masks_of(tile, 1, r), None)
                rho, rinv, *u = [
                    mom[s - 1, n, tile, pl.ds(ROWS * r, ROWS), :] for n in range(5)
                ]
                first = (F_CODE1 + 1, F_CODE2, F_CODE3)[s - 1]
                kind = field[first + tile, rows_of(r), :]
                phi = field[F_PHI + 1 + tile, rows_of(r), :]
                state = [saved[s - 1, i, tile] for i in range(Q)] if r == 1 else None
                back, term = collide_back(b, kind, phi, rho, rinv, u, state)
                for i in range(Q):
                    target[4 * i + tile, rows_of(r), :] = back[i]
                if r == 1:
                    grad[tile] = term if s == 3 else grad[tile] + term
            return carry

        lax.fori_loop(0, 4, body, 0)

    backward(cot, 3, pop_a)
    backward(pop_a, 2, pop_b)
    backward(pop_b, 1, pop_a)

    row = lax.broadcasted_iota(jnp.int32, (ROWS, LANES), 0)
    panel = lax.broadcasted_iota(jnp.int32, panel_ref.shape, 1)
    sums = jnp.zeros(panel_ref.shape, jnp.float32)
    for tile in range(2):
        lanes = pl.ds(tile * LANES, LANES)
        b = streamed(pop_a, tile + 1, 4, 1, -1, masks_of(tile, 0, 1), None)
        f = [state_ref[2 * i + tile] for i in range(Q)]
        kind = own_field_ref[tile]
        phi = own_field_ref[2 * OWN_PHI + tile]
        _, _, rho, rinv, u = moments(f)
        back, term = collide_back(b, kind, phi, rho, rinv, u, f)
        for i in range(Q):
            adjoint_ref[i, :, lanes] = back[i]
        term = term + grad[tile + 1]
        for part in range(2):
            inside = (row < 4) if part == 0 else (row >= 4)
            amount = jnp.sum(jnp.where(inside, term, 0.0))
            name = names_ref[tile, 4 * part : 4 * part + 1, 0:1]
            sums = sums + jnp.where(panel == name, amount, 0.0)
    panel_ref[...] = sums


VMEM = pl.BlockSpec(memory_space=pltpu.VMEM)
HBM = pl.BlockSpec(memory_space=pltpu.HBM)


def shape_of(*dims):
    return jax.ShapeDtypeStruct(dims, jnp.float32)


def tiles_of(count):
    return shape_of(count, ROWS, LANES)


def on_device(sizes, checkpoint, cotangent, cell_codes, porosity, baffle_index):
    size_x, size_y = sizes
    panels = porosity.shape[0]
    devices = size_x * size_y

    def call(kernel, out_shape, in_specs, scratch=(), name=None):
        return pl.pallas_call(
            kernel,
            out_shape=out_shape,
            in_specs=in_specs,
            out_specs=jax.tree.map(lambda _: VMEM, out_shape),
            scratch_shapes=scratch,
            compiler_params=pltpu.CompilerParams(vmem_limit_bytes=32 * 1024 * 1024),
            name=name,
        )

    def exchange(first, second, axis, size):
        pairs = [(i, i ^ 1) for i in range(size) if i ^ 1 < size]
        between = [(i, i + 1) for i in range(1, size - 1, 2)]
        between += [(j, i) for i, j in between]
        return lax.ppermute(first, axis, pairs), lax.ppermute(second, axis, between)

    arguments = [
        pltpu.with_memory_space_constraint(value, pltpu.HBM)
        for value in (checkpoint, cotangent, cell_codes, baffle_index, porosity)
    ]
    first_y, second_y, own, state, cot, field, names = call(
        pack_own,
        (tiles_of(Y_TILES),) * 2
        + (tiles_of(2 * Q),) * 3
        + (tiles_of(2 * OWN_PHI + 2), jax.ShapeDtypeStruct((2, ROWS, LANES), jnp.int32)),
        [HBM] * 5,
        [
            pltpu.VMEM((Q, ROWS, 2 * LANES), jnp.float32),
            pltpu.VMEM((Q, ROWS, 2 * LANES), jnp.float32),
            pltpu.VMEM((STEPS, ROWS, 2 * LANES), jnp.int32),
            pltpu.SMEM(baffle_index.shape, jnp.int32),
            pltpu.SMEM(porosity.shape, jnp.float32),
            pltpu.SemaphoreType.DMA((5,)),
        ],
        name="pack_own",
    )(*arguments)
    first_y, second_y = exchange(first_y, second_y, "gy", size_y)
    first_x, second_x = call(pack_x, (tiles_of(X_TILES),) * 2, [VMEM] * 5, name="pack_x")(
        own, cot, field, first_y, second_y
    )
    first_x, second_x = exchange(first_x, second_x, "gx", size_x)

    adjoint, sums = call(
        functools.partial(steps_kernel, sizes),
        (shape_of(Q, ROWS, 2 * LANES), shape_of(devices, panels)),
        [VMEM] * 9,
        [
            pltpu.VMEM((5 * Q, 5 * ROWS, LANES), jnp.float32),
            pltpu.VMEM((5 * Q, 5 * ROWS, LANES), jnp.float32),
            pltpu.VMEM((4 * Q, 5 * ROWS, LANES), jnp.float32),
            pltpu.VMEM((FIELDS, 5 * ROWS, LANES), jnp.float32),
            pltpu.VMEM((3, Q, 5, ROWS, LANES), jnp.float32),
            pltpu.VMEM((3, 5, 5, 3 * ROWS, LANES), jnp.float32),
            pltpu.VMEM((4, ROWS, LANES), jnp.float32),
        ],
        name="steps",
    )(state, cot, own, field, names, first_y, second_y, first_x, second_x)
    gathered = lax.all_to_all(sums, ("gx", "gy"), 0, 0, tiled=True)
    totals = call(add_panels, shape_of(1, panels), [VMEM], name="add_panels")(
        gathered.reshape(devices, 1, panels)
    )
    return adjoint, totals.reshape(panels)


def solution(mesh):
    sizes = (mesh.shape["gx"], mesh.shape["gy"])
    in_specs = (P(None, "gx", "gy"), P(None, "gx", "gy"), P(None, "gx", "gy"), P(), P("gx", "gy"))
    out_specs = (P(None, "gx", "gy"), P())
    return jax.shard_map(
        functools.partial(on_device, sizes),
        mesh=mesh,
        in_specs=in_specs,
        out_specs=out_specs,
        check_vma=False,
    )
```

```python
import functools

import jax
import jax.numpy as jnp
import numpy as np
from jax import lax
from jax.experimental import pallas as pl
from jax.experimental.pallas import tpu as pltpu
from jax.sharding import PartitionSpec as P

Q = 19
STEPS = 4
NZ = 32
ROWS = 8
LANES = 128
OMEGA = 1.6
ACCEL = (0.002, 0.0, -0.003)
SHIFT = tuple(a / OMEGA for a in ACCEL)

VELOCITIES = [
    (0, 0, 0),
    (1, 0, 0),
    (-1, 0, 0),
    (0, 1, 0),
    (0, -1, 0),
    (0, 0, 1),
    (0, 0, -1),
    (1, 1, 0),
    (-1, -1, 0),
    (1, -1, 0),
    (-1, 1, 0),
    (1, 0, 1),
    (-1, 0, -1),
    (1, 0, -1),
    (-1, 0, 1),
    (0, 1, 1),
    (0, -1, -1),
    (0, 1, -1),
    (0, -1, 1),
]
OPPOSITE = [0, 2, 1, 4, 3, 6, 5, 8, 7, 10, 9, 12, 11, 14, 13, 16, 15, 18, 17]
PAIRS = [(i, i + 1) for i in range(1, Q, 2)]
W_REST, W_AXIS, W_DIAG = 1.0 / 3.0, 1.0 / 18.0, 1.0 / 36.0

Y_CODE1, Y_CODE2, Y_CODE3, Y_POP, Y_COT = 38, 39, 40, 41, 42
Y_TILES = 43
SPARE = 1
X_EXTRA, X_CODE13 = 19, 20
X_LANE = 21
X_RING = 4 * X_LANE
X_CODE2 = X_RING + Q + 1
X_TILES = X_CODE2 + 2
X_SIDE = 2 * X_LANE
F_CODE1, F_CODE2, F_CODE3, F_PHI = 0, 5, 9, 13
FIELDS = 18
OWN_PHI = 4


def turned(axis, outward):
    return [i for i, v in enumerate(VELOCITIES) if v[axis] == outward and sum(map(abs, v)) == 2]


def total(values):
    values = list(values)
    while len(values) > 1:
        values = [a + b for a, b in zip(values[::2], values[1::2])] + (
            [values[-1]] if len(values) % 2 else []
        )
    return values[0]


def along(vector, three):
    terms = None
    for c, value in zip(vector, three):
        if c == 0:
            continue
        if terms is None:
            terms = value if c > 0 else -value
        else:
            terms = terms + value if c > 0 else terms - value
    return terms


def moments(f):
    plus = {i: f[i] + f[o] for i, o in PAIRS}
    minus = {i: f[i] - f[o] for i, o in PAIRS}
    rho = total([f[0]] + [plus[i] for i, _ in PAIRS])
    rinv = 1.0 / rho
    u = []
    for axis in range(3):
        terms = [
            minus[i] if VELOCITIES[i][axis] > 0 else -minus[i]
            for i, _ in PAIRS
            if VELOCITIES[i][axis] != 0
        ]
        u.append(total(terms) * rinv + SHIFT[axis])
    return plus, minus, rho, rinv, u


def coefficients(kind, phi, rinv):
    baffle = kind == 3.0
    gas = kind == 0.0
    even = jnp.where(gas, 0.0, jnp.where(baffle, 0.5 - 0.5 * OMEGA * phi, 0.5 * (1.0 - OMEGA)))
    odd = jnp.where(
        gas, 0.0, jnp.where(baffle, (1.0 - 0.5 * OMEGA) * phi - 0.5, 0.5 * (1.0 - OMEGA))
    )
    slope = jnp.where(
        baffle,
        OMEGA * phi,
        jnp.where(kind == 1.0, OMEGA, jnp.where(kind == 2.0, OMEGA * rinv, 0.0)),
    )
    return even, odd, slope


def collide(f, kind, phi, parts):
    plus, minus, rho, rinv, u = parts
    even, odd, slope = coefficients(kind, phi, rinv)
    scale = slope * rho
    rest = 1.0 - 1.5 * (u[0] * u[0] + u[1] * u[1] + u[2] * u[2])
    base = scale * rest + jnp.where(kind == 0.0, 1.0, 0.0)
    out = [None] * Q
    out[0] = 2.0 * even * f[0] + W_REST * base
    for weight, pairs in ((W_AXIS, PAIRS[:3]), (W_DIAG, PAIRS[3:])):
        flat = weight * base
        three = (3.0 * weight) * scale
        for i, o in pairs:
            cu = along(VELOCITIES[i], u)
            lin = three * cu
            ev = even * plus[i] + (flat + 1.5 * lin * cu)
            od = odd * minus[i] + lin
            out[i] = ev + od
            out[o] = ev - od
    return out


def collide_back(b, kind, phi, rho, rinv, u, state=None):
    even, odd, slope = coefficients(kind, phi, rinv)
    plus = {i: b[i] + b[o] for i, o in PAIRS}
    minus = {i: b[i] - b[o] for i, o in PAIRS}
    rest = 1.0 - 1.5 * (u[0] * u[0] + u[1] * u[1] + u[2] * u[2])
    u_half = [1.5 * c for c in u]
    weighted = W_REST * b[0]
    energy = 0.0
    vector = [0.0, 0.0, 0.0]
    for weight, pairs in ((W_AXIS, PAIRS[:3]), (W_DIAG, PAIRS[3:])):
        weighted = weighted + weight * total([plus[i] for i, _ in pairs])
        energies, parts = [], ([], [], [])
        for i, _ in pairs:
            cu = along(VELOCITIES[i], u)
            half = along(VELOCITIES[i], u_half) * plus[i]
            first = minus[i] + half
            energies.append(cu * first)
            second = first + half
            for axis in range(3):
                c = VELOCITIES[i][axis]
                if c:
                    parts[axis].append(second if c > 0 else -second)
        energy = energy + (3.0 * weight) * total(energies)
        vector = [vector[k] + (3.0 * weight) * total(parts[k]) for k in range(3)]
    energy = energy + rest * weighted
    vector = [vector[k] - (3.0 * weighted) * u[k] for k in range(3)]
    push = [slope * v for v in vector]
    inner = total([push[k] * (u[k] - SHIFT[k]) for k in range(3)])
    shared = jnp.where(kind == 2.0, 0.0, slope) * energy - inner
    out = [None] * Q
    out[0] = 2.0 * even * b[0] + shared
    for i, o in PAIRS:
        ev = even * plus[i] + shared
        od = odd * minus[i] + along(VELOCITIES[i], push)
        out[i] = ev + od
        out[o] = ev - od
    if state is None:
        return out, None
    evens = total([plus[i] * (state[i] + state[o]) for i, o in PAIRS])
    odds = total([minus[i] * (state[i] - state[o]) for i, o in PAIRS])
    term = (
        -OMEGA * (b[0] * state[0] + 0.5 * evens)
        + (1.0 - 0.5 * OMEGA) * odds
        + OMEGA * rho * energy
    )
    return out, jnp.where(kind == 3.0, term, 0.0)


def wall_masks(sign_rows, own_low, own_high, edges):
    lane = lax.broadcasted_iota(jnp.int32, (ROWS, LANES), 1)
    row = lax.broadcasted_iota(jnp.int32, (ROWS, LANES), 0)
    x_low, x_high, y_low, y_high = edges
    depth = lane % NZ
    masks = {}
    masks[2, 1] = depth == 0
    masks[2, -1] = depth == NZ - 1
    masks[1, 1] = lane < jnp.where(own_low, y_low * NZ, 0)
    masks[1, -1] = lane >= jnp.where(own_high, LANES - y_high * NZ, LANES)
    if sign_rows:
        masks[0, 1] = row < x_low
        masks[0, -1] = row >= ROWS - x_high
    return masks


def stream_tile(load, sign, masks, lane):
    cross_low, cross_high = lane >= LANES - NZ, lane < NZ
    combined = {}
    out = []
    for i, vector in enumerate(VELOCITIES):
        v = tuple(sign * c for c in vector)
        value = load(i, 0, -v[0])
        if v[1] == 1:
            value = jnp.where(cross_low, load(i, -1, -v[0]), value)
        elif v[1] == -1:
            value = jnp.where(cross_high, load(i, 1, -v[0]), value)
        amount = (v[1] * NZ + v[2]) % LANES
        if amount:
            value = pltpu.roll(value, amount, 1)
        outside = None
        if v not in combined:
            for axis in range(3):
                if v[axis] and (axis, v[axis]) in masks:
                    wall = masks[axis, v[axis]]
                    outside = wall if outside is None else outside | wall
            combined[v] = outside
        outside = combined[v]
        if outside is not None:
            value = jnp.where(outside, load(OPPOSITE[i], 0, 0), value)
        out.append(value)
    return out


def iotas():
    row = lax.broadcasted_iota(jnp.int32, (ROWS, LANES), 0)
    lane = lax.broadcasted_iota(jnp.int32, (ROWS, LANES), 1)
    return row, lane, lane // NZ, lane % NZ


def columns(value, count):
    amount = (count * NZ) % LANES
    return pltpu.roll(value, amount, 1) if amount else value


def lines(value, count):
    amount = count % ROWS
    return pltpu.roll(value, amount, 0) if amount else value


class Pick:
    def __init__(self, flag, first, second):
        self.flag, self.first, self.second = flag, first, second

    def __getitem__(self, at):
        return jnp.where(self.flag, self.first[at], self.second[at])


class Deal:
    def __init__(self, even, first, second, skip=0):
        self.even, self.first, self.second, self.skip, self.held = even, first, second, skip, {}

    def put(self, way, at, value):
        if (-way, at) not in self.held:
            self.held[way, at] = value
            return
        other = self.held.pop((-way, at))
        up, down = (value, other) if way == 1 else (other, value)
        self.first[at - self.skip] = jnp.where(self.even, up, down)
        self.second[at - self.skip] = jnp.where(self.even, down, up)


class Joined:
    def __init__(self, first, second, cut):
        self.first, self.second, self.cut = first, second, cut

    def __getitem__(self, at):
        return self.first[at] if at < self.cut else self.second[at - self.cut]


def is_even(axis):
    return lax.rem(lax.axis_index(axis), 2) == 0


def pack_own(
    f_hbm,
    cot_hbm,
    codes_hbm,
    panels_hbm,
    porosity_hbm,
    first_ref,
    second_ref,
    first_side_ref,
    second_side_ref,
    own_ref,
    state_ref,
    own_cot_ref,
    field_ref,
    names_ref,
    f_ref,
    cot_ref,
    codes_ref,
    panels_ref,
    porosity_ref,
    sems,
):
    pieces = (
        (panels_hbm, panels_ref),
        (porosity_hbm, porosity_ref),
        (f_hbm, f_ref),
        (codes_hbm, codes_ref),
        (cot_hbm, cot_ref),
    )
    copies = [
        pltpu.make_async_copy(source, target, sems.at[n])
        for n, (source, target) in enumerate(pieces)
    ]
    for copy in copies:
        copy.start()
    for copy in copies[:4]:
        copy.wait()
    deal = Deal(is_even("gy"), first_ref, second_ref)
    row, lane, column, depth = iotas()
    top = depth == NZ - 1

    def tile_of(ref, i, t):
        return ref[i, :, pl.ds(t * LANES, LANES)]

    codes, phis = [], []
    for t in range(2):
        names = panels_ref[0, t * LANES], panels_ref[4, t * LANES]
        phi = jnp.where(row < 4, porosity_ref[names[0]], porosity_ref[names[1]])
        names_ref[t] = jnp.where(row < 4, names[0], names[1])
        kinds = [tile_of(codes_ref, s, t).astype(jnp.float32) for s in range(STEPS)]
        f = [tile_of(f_ref, i, t) for i in range(Q)]
        g = collide(f, kinds[0], phi, moments(f))
        for i in range(Q):
            own_ref[2 * i + t] = g[i]
            state_ref[2 * i + t] = f[i]
        for s in range(STEPS):
            field_ref[2 * s + t] = kinds[s]
        field_ref[2 * OWN_PHI + t] = phi
        codes.append([jnp.where(top, phi, kinds[1]), kinds[2], kinds[3]])
    copies[4].wait()
    for i in range(Q):
        for way in (1, -1):
            near, far = (1, 0) if way == 1 else (0, 1)
            deep = 3 - way * VELOCITIES[i][1]
            cot = tile_of(cot_ref, i, near)
            g_far = own_ref[2 * i + far]
            if way == 1:
                mixed = jnp.where(column >= deep, g_far, columns(cot, deep - 4))
            else:
                mixed = jnp.where(column < 4 - deep, g_far, columns(cot, 4 - deep))
            deal.put(way, 2 * i, mixed if far == 0 else own_ref[2 * i])
            deal.put(way, 2 * i + 1, mixed if far == 1 else own_ref[2 * i + 1])
    for way in (1, -1):
        near, far = (1, 0) if way == 1 else (0, 1)
        outer = 3 if way == 1 else 0
        deal.put(way, Y_CODE1, codes[near][0])
        deal.put(way, Y_CODE2, codes[near][1])
        outside = columns(codes[far][0], 3 - 2 * outer)
        deal.put(way, Y_CODE3, jnp.where(column == 3 - outer, outside, codes[near][2]))
        extra = None
        for k, i in enumerate(turned(1, -way)):
            value = columns(own_ref[2 * i + far], k - outer)
            extra = value if extra is None else jnp.where(column == k, value, extra)
        deal.put(way, Y_POP, extra)
        extra = None
        for k, i in enumerate(turned(1, way)):
            value = columns(tile_of(cot_ref, i, near), k - (1 if way == 1 else 2))
            extra = value if extra is None else jnp.where(column == k, value, extra)
        deal.put(way, Y_COT, extra)
    second_ref[Y_TILES] = jnp.zeros((ROWS, LANES), jnp.float32)
    for t in range(2):
        for i in range(Q):
            own_cot_ref[2 * i + t] = tile_of(cot_ref, i, t)
        pack_lines(
            Deal(is_even("gx"), first_side_ref, second_side_ref),
            X_LANE * t,
            lambda i: own_ref[2 * i + t],
            lambda i: tile_of(cot_ref, i, t),
            lambda s: codes[t][s - 1],
        )


def from_y(left_ref, right_ref):
    row, lane, column, depth = iotas()
    high = lane >= LANES // 2

    def population(i, c):
        if c == 1:
            return left_ref[2 * i + 1]
        if c == 4:
            return right_ref[2 * i]
        along_y = VELOCITIES[i][1]
        left, right = left_ref[2 * i], right_ref[2 * i + 1]
        if along_y == 1 and i in turned(1, 1):
            right = columns(right_ref[Y_POP], -turned(1, 1).index(i))
        if along_y == -1 and i in turned(1, -1):
            left = columns(left_ref[Y_POP], 3 - turned(1, -1).index(i))
        return jnp.where(high, left, right)

    def cotangent(i, c):
        ref, way, place, far = (left_ref, 1, 1, 0) if c == 1 else (right_ref, -1, 2, 1)
        deep = 3 - way * VELOCITIES[i][1]
        value = columns(ref[2 * i + far], way * (4 - deep))
        if i in turned(1, way):
            extra = columns(ref[Y_COT], place - turned(1, way).index(i))
            value = jnp.where(column == place, extra, value)
        return value

    def codes(s, c):
        if c == 0:
            left, right = columns(left_ref[Y_CODE3], 3), columns(right_ref[Y_CODE3], 1)
            return jnp.where(high, left, right)
        return (left_ref if c == 1 else right_ref)[(Y_CODE1, Y_CODE2, Y_CODE3)[s - 1]]

    return population, cotangent, codes


def pack_lines(deal, first, population, cotangent, codes):
    row, lane, column, depth = iotas()

    def put(at, pop, cot, deep, way):
        if way == 1:
            mixed = jnp.where(row >= deep, pop, lines(cot, deep))
        else:
            mixed = jnp.where(row < ROWS - deep, pop, lines(cot, -deep))
        deal.put(way, first + at, mixed)

    for i in range(Q):
        pop, cot = population(i), cotangent(i)
        for way in (1, -1):
            put(i, pop, cot, 3 - way * VELOCITIES[i][0], way)
    for way in (1, -1):
        extra = None
        for k, i in enumerate(turned(0, -way)):
            value = lines(population(i), k - (3 if way == 1 else 4))
            extra = value if extra is None else jnp.where(row == k, value, extra)
        for k, i in enumerate(turned(0, way)):
            value = lines(cotangent(i), 4 + k - (5 if way == 1 else 2))
            extra = jnp.where(row == 4 + k, value, extra)
        deal.put(way, first + X_EXTRA, extra)
        put(X_CODE13, codes(1), codes(3), 3, way)


def from_x(ref, n, way):
    row, lane, column, depth = iotas()
    first = X_LANE * n

    def population(i):
        value = ref[first + i]
        if i in turned(0, -way):
            place = 3 if way == 1 else 4
            extra = lines(ref[first + X_EXTRA], place - turned(0, -way).index(i))
            value = jnp.where(row == place, extra, value)
        return value

    def cotangent(i):
        value = lines(ref[first + i], -way * (3 - way * VELOCITIES[i][0]))
        if i in turned(0, way):
            place = 5 if way == 1 else 2
            extra = lines(ref[first + X_EXTRA], place - 4 - turned(0, way).index(i))
            value = jnp.where(row == place, extra, value)
        return value

    def codes(s):
        if s == 2:
            return lines(ref[X_CODE2 + n // 2], 4 * (n % 2))
        value = ref[first + X_CODE13]
        return value if s == 1 else lines(value, -3 * way)

    return population, cotangent, codes


def pack_x(field_ref, first_y_ref, second_y_ref, early_a, early_b, first_ref, second_ref):
    row, lane, column, depth = iotas()
    deal = Deal(is_even("gx"), first_ref, second_ref, X_SIDE)
    population, cotangent, codes = from_y(*sides(first_y_ref, second_y_ref, "gy"))

    def both_codes(at, first, second):
        second = lines(second, 4)
        deal.put(1, at, jnp.where(row >= 4, first, second))
        deal.put(-1, at, jnp.where(row < 4, first, second))

    for n, c in ((2, 1), (3, 4)):
        pack_lines(
            deal,
            X_LANE * n,
            lambda i: population(i, c),
            lambda i: cotangent(i, c),
            lambda s: codes(s, c),
        )
    for n in range(Q + 1):
        value = population(n, 0) if n < Q else codes(1, 0)
        first_ref[X_RING + n - X_SIDE] = value
        second_ref[X_RING + n - X_SIDE] = value
    both_codes(X_CODE2, field_ref[4], field_ref[5])
    both_codes(X_CODE2 + 1, codes(2, 1), codes(2, 4))
    second_ref[X_TILES - X_SIDE] = jnp.zeros((ROWS, LANES), jnp.float32)


def sides(first_ref, second_ref, axis):
    even = is_even(axis)
    return Pick(even, second_ref, first_ref), Pick(even, first_ref, second_ref)


def add_panels(parts_ref, out_ref):
    out_ref[...] = jnp.sum(parts_ref[...], axis=0)


def fill(from_left, own_ref, field_ref, cot_ref, from_below, pop, cot, field):
    row, lane, column, depth = iotas()
    top = depth == NZ - 1

    def put(c, r, population, cotangent, codes):
        rows = pl.ds(ROWS * (r + 1), ROWS)
        for i in range(Q):
            pop[5 * i + c, rows, :] = population(i)
            if c:
                cot[4 * i + c - 1, rows, :] = cotangent(i)
        code = codes(1)
        phi = jnp.where(top, code, 0.0)
        for step in (1, 2, 4, 8, 16):
            phi = phi + pltpu.roll(phi, LANES - step, 1)
        field[F_CODE1 + c, rows, :] = jnp.where(top, 0.0, code)
        field[F_PHI + c, rows, :] = phi
        if c:
            field[F_CODE2 + c - 1, rows, :] = codes(2)
            field[F_CODE3 + c - 1, rows, :] = codes(3)

    for c in (0, 1, 4):
        put(c, 1, *(functools.partial(lambda g, n: g(n, c), get) for get in from_left))
    for t in range(2):
        rows = pl.ds(2 * ROWS, ROWS)
        for i in range(Q):
            pop[5 * i + 2 + t, rows, :] = own_ref[2 * i + t]
            cot[4 * i + 1 + t, rows, :] = cot_ref[2 * i + t]
        field[F_CODE1 + 2 + t, rows, :] = field_ref[2 + t]
        field[F_CODE2 + 1 + t, rows, :] = field_ref[4 + t]
        field[F_CODE3 + 1 + t, rows, :] = field_ref[6 + t]
        field[F_PHI + 2 + t, rows, :] = field_ref[2 * OWN_PHI + t]
    for way, r, ref in ((1, 0, from_below[0]), (-1, 2, from_below[1])):
        for n, c in enumerate((2, 3, 1, 4)):
            put(c, r, *from_x(ref, n, way))
        put(0, r, lambda i: ref[X_RING + i], None, lambda s: ref[X_RING + Q])


def steps_kernel(
    sizes,
    state_ref,
    cot_ref,
    own_ref,
    own_field_ref,
    names_ref,
    first_y_ref,
    second_y_ref,
    first_side_ref,
    second_side_ref,
    first_x_ref,
    second_x_ref,
    adjoint_ref,
    panel_ref,
    pop_a,
    pop_b,
    cot,
    field,
    saved,
    mom,
    grad,
):
    size_x, size_y = sizes
    fill(
        from_y(*sides(first_y_ref, second_y_ref, "gy")),
        own_ref,
        own_field_ref,
        cot_ref,
        sides(
            Joined(first_side_ref, first_x_ref, X_SIDE),
            Joined(second_side_ref, second_x_ref, X_SIDE),
            "gx",
        ),
        pop_a,
        cot,
        field,
    )

    at_x, at_y = lax.axis_index("gx"), lax.axis_index("gy")
    edges = (
        jnp.where(at_x == 0, 1, 0),
        jnp.where(at_x == size_x - 1, 1, 0),
        jnp.where(at_y == 0, 1, 0),
        jnp.where(at_y == size_y - 1, 1, 0),
    )
    lane = lax.broadcasted_iota(jnp.int32, (ROWS, LANES), 1)

    def streamed(ref, tile, tiles, r, sign, masks, four):
        step = {0: tile, -1: lax.rem(tile + tiles - 1, tiles), 1: lax.rem(tile + 1, tiles)}

        def load(i, tile_step, row_step):
            return ref[tiles * i + step[tile_step], pl.ds(ROWS * (r + 1) + row_step, ROWS), :]

        return stream_tile(load, sign, masks, lane)

    def masks_of(tile, first, r):
        return wall_masks(r == 1, tile == first, tile == first + 1, edges)

    def rows_of(r):
        return pl.ds(ROWS * (r + 1), ROWS)

    def forward(source, tiles, own, s, target, target_tiles, offset):
        def body(tile, carry):
            ring = tile - offset if target_tiles != tiles else tile
            for r in range(3):
                f = streamed(source, tile, tiles, r, 1, masks_of(tile, own, r), None)
                parts = moments(f)
                _, _, rho, rinv, u = parts
                place = tile if tiles == 4 else lax.rem(tile + 4, 5)
                for n, value in enumerate((rho, rinv, *u)):
                    mom[s - 1, n, place, pl.ds(ROWS * r, ROWS), :] = value
                if r == 1:
                    for i in range(Q):
                        saved[s - 1, i, place] = f[i]
                if target is not None:
                    at = tile if tiles == 5 else tile + 1
                    first = F_CODE1 if s == 1 else F_CODE2 - 1
                    kind = field[first + at, rows_of(r), :]
                    phi = field[F_PHI + at, rows_of(r), :]
                    g = collide(f, kind, phi, parts)
                    for i in range(Q):
                        target[target_tiles * i + ring, rows_of(r), :] = g[i]
            return carry

        start, stop = (0, 5) if target_tiles == 5 else (1, 5)
        if tiles == 4:
            start, stop = 0, 4
        lax.fori_loop(start, stop, body, 0)

    forward(pop_a, 5, 2, 1, pop_b, 5, 0)
    forward(pop_b, 5, 2, 2, pop_a, 4, 1)
    forward(pop_a, 4, 1, 3, None, 4, 0)

    def backward(source, s, target):
        def body(tile, carry):
            for r in range(3):
                b = streamed(source, tile, 4, r, -1, masks_of(tile, 1, r), None)
                rho, rinv, *u = [
                    mom[s - 1, n, tile, pl.ds(ROWS * r, ROWS), :] for n in range(5)
                ]
                first = (F_CODE1 + 1, F_CODE2, F_CODE3)[s - 1]
                kind = field[first + tile, rows_of(r), :]
                phi = field[F_PHI + 1 + tile, rows_of(r), :]
                state = [saved[s - 1, i, tile] for i in range(Q)] if r == 1 else None
                back, term = collide_back(b, kind, phi, rho, rinv, u, state)
                for i in range(Q):
                    target[4 * i + tile, rows_of(r), :] = back[i]
                if r == 1:
                    grad[tile] = term if s == 3 else grad[tile] + term
            return carry

        lax.fori_loop(0, 4, body, 0)

    backward(cot, 3, pop_a)
    backward(pop_a, 2, pop_b)
    backward(pop_b, 1, pop_a)

    row = lax.broadcasted_iota(jnp.int32, (ROWS, LANES), 0)
    panel = lax.broadcasted_iota(jnp.int32, panel_ref.shape, 1)
    sums = jnp.zeros(panel_ref.shape, jnp.float32)
    for tile in range(2):
        lanes = pl.ds(tile * LANES, LANES)
        b = streamed(pop_a, tile + 1, 4, 1, -1, masks_of(tile, 0, 1), None)
        f = [state_ref[2 * i + tile] for i in range(Q)]
        kind = own_field_ref[tile]
        phi = own_field_ref[2 * OWN_PHI + tile]
        _, _, rho, rinv, u = moments(f)
        back, term = collide_back(b, kind, phi, rho, rinv, u, f)
        for i in range(Q):
            adjoint_ref[i, :, lanes] = back[i]
        term = term + grad[tile + 1]
        for part in range(2):
            inside = (row < 4) if part == 0 else (row >= 4)
            amount = jnp.sum(jnp.where(inside, term, 0.0))
            name = names_ref[tile, 4 * part : 4 * part + 1, 0:1]
            sums = sums + jnp.where(panel == name, amount, 0.0)
    panel_ref[...] = sums


VMEM = pl.BlockSpec(memory_space=pltpu.VMEM)
HBM = pl.BlockSpec(memory_space=pltpu.HBM)
ANY = pl.BlockSpec(memory_space=pl.ANY)


def shape_of(*dims):
    return jax.ShapeDtypeStruct(dims, jnp.float32)


def tiles_of(count):
    return shape_of(count, ROWS, LANES)


def on_device(sizes, checkpoint, cotangent, cell_codes, porosity, baffle_index):
    size_x, size_y = sizes
    panels = porosity.shape[0]
    devices = size_x * size_y

    def call(kernel, out_shape, in_specs, scratch=(), name=None):
        return pl.pallas_call(
            kernel,
            out_shape=out_shape,
            in_specs=in_specs,
            out_specs=jax.tree.map(lambda _: VMEM, out_shape),
            scratch_shapes=scratch,
            compiler_params=pltpu.CompilerParams(vmem_limit_bytes=32 * 1024 * 1024),
            name=name,
        )

    def swap(value, axis, size):
        return lax.ppermute(value, axis, [(i, i ^ 1) for i in range(size) if i ^ 1 < size])

    def swap_between(value, axis, size):
        pairs = [(i, i + 1) for i in range(1, size - 1, 2)]
        return lax.ppermute(value, axis, pairs + [(j, i) for i, j in pairs])

    arguments = [
        pltpu.with_memory_space_constraint(value, pltpu.HBM)
        for value in (checkpoint, cotangent, cell_codes, baffle_index, porosity)
    ]
    first_y, second_y, first_side, second_side, own, state, cot, field, names = call(
        pack_own,
        (tiles_of(Y_TILES), tiles_of(Y_TILES + SPARE))
        + (tiles_of(X_SIDE),) * 2
        + (tiles_of(2 * Q),) * 3
        + (tiles_of(2 * OWN_PHI + 2), jax.ShapeDtypeStruct((2, ROWS, LANES), jnp.int32)),
        [HBM] * 5,
        [
            pltpu.VMEM((Q, ROWS, 2 * LANES), jnp.float32),
            pltpu.VMEM((Q, ROWS, 2 * LANES), jnp.float32),
            pltpu.VMEM((STEPS, ROWS, 2 * LANES), jnp.int32),
            pltpu.SMEM(baffle_index.shape, jnp.int32),
            pltpu.SMEM(porosity.shape, jnp.float32),
            pltpu.SemaphoreType.DMA((5,)),
        ],
        name="pack_own",
    )(*arguments)
    second_y = swap_between(second_y, "gy", size_y)
    first_y = swap(first_y, "gy", size_y)
    second_side = swap_between(second_side, "gx", size_x)
    first_side = swap(first_side, "gx", size_x)
    rest = X_TILES - X_SIDE
    first_x, second_x = call(
        pack_x,
        (tiles_of(rest), tiles_of(rest + SPARE)),
        [VMEM] * 3 + [ANY] * 2,
        name="pack_x",
    )(field, first_y, second_y, first_side, second_side)
    second_x = swap_between(second_x, "gx", size_x)
    first_x = swap(first_x, "gx", size_x)

    adjoint, sums = call(
        functools.partial(steps_kernel, sizes),
        (shape_of(Q, ROWS, 2 * LANES), shape_of(devices, panels)),
        [VMEM] * 11,
        [
            pltpu.VMEM((5 * Q, 5 * ROWS, LANES), jnp.float32),
            pltpu.VMEM((5 * Q, 5 * ROWS, LANES), jnp.float32),
            pltpu.VMEM((4 * Q, 5 * ROWS, LANES), jnp.float32),
            pltpu.VMEM((FIELDS, 5 * ROWS, LANES), jnp.float32),
            pltpu.VMEM((3, Q, 5, ROWS, LANES), jnp.float32),
            pltpu.VMEM((3, 5, 5, 3 * ROWS, LANES), jnp.float32),
            pltpu.VMEM((4, ROWS, LANES), jnp.float32),
        ],
        name="steps",
    )(state, cot, own, field, names, first_y, second_y, first_side, second_side, first_x, second_x)
    gathered = lax.all_to_all(sums, ("gx", "gy"), 0, 0, tiled=True)
    totals = call(add_panels, shape_of(1, panels), [VMEM], name="add_panels")(
        gathered.reshape(devices, 1, panels)
    )
    return adjoint, totals.reshape(panels)


def solution(mesh):
    sizes = (mesh.shape["gx"], mesh.shape["gy"])
    in_specs = (P(None, "gx", "gy"), P(None, "gx", "gy"), P(None, "gx", "gy"), P(), P("gx", "gy"))
    out_specs = (P(None, "gx", "gy"), P())
    return jax.shard_map(
        functools.partial(on_device, sizes),
        mesh=mesh,
        in_specs=in_specs,
        out_specs=out_specs,
        check_vma=False,
    )
```

```python
import functools

import jax
import jax.numpy as jnp
import numpy as np
from jax import lax
from jax.experimental import pallas as pl
from jax.experimental.pallas import tpu as pltpu
from jax.sharding import PartitionSpec as P

Q = 19
STEPS = 4
NZ = 32
ROWS = 8
LANES = 128
OMEGA = 1.6
ACCEL = (0.002, 0.0, -0.003)
SHIFT = tuple(a / OMEGA for a in ACCEL)

VELOCITIES = [
    (0, 0, 0),
    (1, 0, 0),
    (-1, 0, 0),
    (0, 1, 0),
    (0, -1, 0),
    (0, 0, 1),
    (0, 0, -1),
    (1, 1, 0),
    (-1, -1, 0),
    (1, -1, 0),
    (-1, 1, 0),
    (1, 0, 1),
    (-1, 0, -1),
    (1, 0, -1),
    (-1, 0, 1),
    (0, 1, 1),
    (0, -1, -1),
    (0, 1, -1),
    (0, -1, 1),
]
OPPOSITE = [0, 2, 1, 4, 3, 6, 5, 8, 7, 10, 9, 12, 11, 14, 13, 16, 15, 18, 17]
PAIRS = [(i, i + 1) for i in range(1, Q, 2)]
W_REST, W_AXIS, W_DIAG = 1.0 / 3.0, 1.0 / 18.0, 1.0 / 36.0

Y_CODE1, Y_CODE2, Y_CODE3, Y_POP, Y_COT = 38, 39, 40, 41, 42
Y_TILES = 43
SPARE = 1
X_EXTRA, X_CODE13 = 19, 20
X_LANE = 21
X_RING = 4 * X_LANE
X_CODE2 = X_RING + Q + 1
X_TILES = X_CODE2 + 2
X_SIDE = 2 * X_LANE
F_CODE1, F_CODE2, F_CODE3, F_PHI = 0, 5, 9, 13
FIELDS = 18
OWN_PHI = 4


def turned(axis, outward):
    return [i for i, v in enumerate(VELOCITIES) if v[axis] == outward and sum(map(abs, v)) == 2]


def total(values):
    values = list(values)
    while len(values) > 1:
        values = [a + b for a, b in zip(values[::2], values[1::2])] + (
            [values[-1]] if len(values) % 2 else []
        )
    return values[0]


def along(vector, three):
    terms = None
    for c, value in zip(vector, three):
        if c == 0:
            continue
        if terms is None:
            terms = value if c > 0 else -value
        else:
            terms = terms + value if c > 0 else terms - value
    return terms


def moments(f):
    plus = {i: f[i] + f[o] for i, o in PAIRS}
    minus = {i: f[i] - f[o] for i, o in PAIRS}
    rho = total([f[0]] + [plus[i] for i, _ in PAIRS])
    rinv = 1.0 / rho
    u = []
    for axis in range(3):
        terms = [
            minus[i] if VELOCITIES[i][axis] > 0 else -minus[i]
            for i, _ in PAIRS
            if VELOCITIES[i][axis] != 0
        ]
        u.append(total(terms) * rinv + SHIFT[axis])
    return plus, minus, rho, rinv, u


def coefficients(kind, phi, rinv):
    baffle = kind == 3.0
    gas = kind == 0.0
    even = jnp.where(gas, 0.0, jnp.where(baffle, 0.5 - 0.5 * OMEGA * phi, 0.5 * (1.0 - OMEGA)))
    odd = jnp.where(
        gas, 0.0, jnp.where(baffle, (1.0 - 0.5 * OMEGA) * phi - 0.5, 0.5 * (1.0 - OMEGA))
    )
    slope = jnp.where(
        baffle,
        OMEGA * phi,
        jnp.where(kind == 1.0, OMEGA, jnp.where(kind == 2.0, OMEGA * rinv, 0.0)),
    )
    return even, odd, slope


def collide(f, kind, phi, parts):
    plus, minus, rho, rinv, u = parts
    even, odd, slope = coefficients(kind, phi, rinv)
    scale = slope * rho
    rest = 1.0 - 1.5 * (u[0] * u[0] + u[1] * u[1] + u[2] * u[2])
    base = scale * rest + jnp.where(kind == 0.0, 1.0, 0.0)
    out = [None] * Q
    out[0] = 2.0 * even * f[0] + W_REST * base
    for weight, pairs in ((W_AXIS, PAIRS[:3]), (W_DIAG, PAIRS[3:])):
        flat = weight * base
        three = (3.0 * weight) * scale
        for i, o in pairs:
            cu = along(VELOCITIES[i], u)
            lin = three * cu
            ev = even * plus[i] + (flat + 1.5 * lin * cu)
            od = odd * minus[i] + lin
            out[i] = ev + od
            out[o] = ev - od
    return out


def collide_back(b, kind, phi, rho, rinv, u, state=None):
    even, odd, slope = coefficients(kind, phi, rinv)
    plus = {i: b[i] + b[o] for i, o in PAIRS}
    minus = {i: b[i] - b[o] for i, o in PAIRS}
    rest = 1.0 - 1.5 * (u[0] * u[0] + u[1] * u[1] + u[2] * u[2])
    u_half = [1.5 * c for c in u]
    weighted = W_REST * b[0]
    energy = 0.0
    vector = [0.0, 0.0, 0.0]
    for weight, pairs in ((W_AXIS, PAIRS[:3]), (W_DIAG, PAIRS[3:])):
        weighted = weighted + weight * total([plus[i] for i, _ in pairs])
        energies, parts = [], ([], [], [])
        for i, _ in pairs:
            cu = along(VELOCITIES[i], u)
            half = along(VELOCITIES[i], u_half) * plus[i]
            first = minus[i] + half
            energies.append(cu * first)
            second = first + half
            for axis in range(3):
                c = VELOCITIES[i][axis]
                if c:
                    parts[axis].append(second if c > 0 else -second)
        energy = energy + (3.0 * weight) * total(energies)
        vector = [vector[k] + (3.0 * weight) * total(parts[k]) for k in range(3)]
    energy = energy + rest * weighted
    vector = [vector[k] - (3.0 * weighted) * u[k] for k in range(3)]
    push = [slope * v for v in vector]
    inner = total([push[k] * (u[k] - SHIFT[k]) for k in range(3)])
    shared = jnp.where(kind == 2.0, 0.0, slope) * energy - inner
    out = [None] * Q
    out[0] = 2.0 * even * b[0] + shared
    for i, o in PAIRS:
        ev = even * plus[i] + shared
        od = odd * minus[i] + along(VELOCITIES[i], push)
        out[i] = ev + od
        out[o] = ev - od
    if state is None:
        return out, None
    evens = total([plus[i] * (state[i] + state[o]) for i, o in PAIRS])
    odds = total([minus[i] * (state[i] - state[o]) for i, o in PAIRS])
    term = (
        -OMEGA * (b[0] * state[0] + 0.5 * evens)
        + (1.0 - 0.5 * OMEGA) * odds
        + OMEGA * rho * energy
    )
    return out, jnp.where(kind == 3.0, term, 0.0)


def wall_masks(sign_rows, own_low, own_high, edges):
    lane = lax.broadcasted_iota(jnp.int32, (ROWS, LANES), 1)
    row = lax.broadcasted_iota(jnp.int32, (ROWS, LANES), 0)
    x_low, x_high, y_low, y_high = edges
    depth = lane % NZ
    masks = {}
    masks[2, 1] = depth == 0
    masks[2, -1] = depth == NZ - 1
    masks[1, 1] = lane < jnp.where(own_low, y_low * NZ, 0)
    masks[1, -1] = lane >= jnp.where(own_high, LANES - y_high * NZ, LANES)
    if sign_rows:
        masks[0, 1] = row < x_low
        masks[0, -1] = row >= ROWS - x_high
    return masks


def stream_tile(load, sign, masks, lane):
    cross_low, cross_high = lane >= LANES - NZ, lane < NZ
    combined = {}
    out = []
    for i, vector in enumerate(VELOCITIES):
        v = tuple(sign * c for c in vector)
        value = load(i, 0, -v[0])
        if v[1] == 1:
            value = jnp.where(cross_low, load(i, -1, -v[0]), value)
        elif v[1] == -1:
            value = jnp.where(cross_high, load(i, 1, -v[0]), value)
        amount = (v[1] * NZ + v[2]) % LANES
        if amount:
            value = pltpu.roll(value, amount, 1)
        outside = None
        if v not in combined:
            for axis in range(3):
                if v[axis] and (axis, v[axis]) in masks:
                    wall = masks[axis, v[axis]]
                    outside = wall if outside is None else outside | wall
            combined[v] = outside
        outside = combined[v]
        if outside is not None:
            value = jnp.where(outside, load(OPPOSITE[i], 0, 0), value)
        out.append(value)
    return out


def iotas():
    row = lax.broadcasted_iota(jnp.int32, (ROWS, LANES), 0)
    lane = lax.broadcasted_iota(jnp.int32, (ROWS, LANES), 1)
    return row, lane, lane // NZ, lane % NZ


def columns(value, count):
    amount = (count * NZ) % LANES
    return pltpu.roll(value, amount, 1) if amount else value


def lines(value, count):
    amount = count % ROWS
    return pltpu.roll(value, amount, 0) if amount else value


class Pick:
    def __init__(self, flag, first, second):
        self.flag, self.first, self.second = flag, first, second

    def __getitem__(self, at):
        return jnp.where(self.flag, self.first[at], self.second[at])


class Deal:
    def __init__(self, even, first, second, skip=0):
        self.even, self.first, self.second, self.skip, self.held = even, first, second, skip, {}

    def put(self, way, at, value):
        if (-way, at) not in self.held:
            self.held[way, at] = value
            return
        other = self.held.pop((-way, at))
        up, down = (value, other) if way == 1 else (other, value)
        self.first[at - self.skip] = jnp.where(self.even, up, down)
        self.second[at - self.skip] = jnp.where(self.even, down, up)


class Joined:
    def __init__(self, first, second, cut):
        self.first, self.second, self.cut = first, second, cut

    def __getitem__(self, at):
        return self.first[at] if at < self.cut else self.second[at - self.cut]


def is_even(axis):
    return lax.rem(lax.axis_index(axis), 2) == 0


def pack_own(
    f_hbm,
    cot_hbm,
    codes_hbm,
    panels_hbm,
    porosity_hbm,
    first_ref,
    second_ref,
    first_side_ref,
    second_side_ref,
    own_ref,
    state_ref,
    own_cot_ref,
    field_ref,
    names_ref,
    f_ref,
    cot_ref,
    codes_ref,
    panels_ref,
    porosity_ref,
    sems,
):
    pieces = (
        (panels_hbm, panels_ref),
        (porosity_hbm, porosity_ref),
        (f_hbm, f_ref),
        (codes_hbm, codes_ref),
        (cot_hbm, cot_ref),
    )
    copies = [
        pltpu.make_async_copy(source, target, sems.at[n])
        for n, (source, target) in enumerate(pieces)
    ]
    for copy in copies:
        copy.start()
    for copy in copies[:4]:
        copy.wait()
    deal = Deal(is_even("gy"), first_ref, second_ref)
    row, lane, column, depth = iotas()
    top = depth == NZ - 1

    def tile_of(ref, i, t):
        return ref[i, :, pl.ds(t * LANES, LANES)]

    codes, phis = [], []
    for t in range(2):
        names = panels_ref[0, t * LANES], panels_ref[4, t * LANES]
        phi = jnp.where(row < 4, porosity_ref[names[0]], porosity_ref[names[1]])
        names_ref[t] = jnp.where(row < 4, names[0], names[1])
        kinds = [tile_of(codes_ref, s, t).astype(jnp.float32) for s in range(STEPS)]
        f = [tile_of(f_ref, i, t) for i in range(Q)]
        g = collide(f, kinds[0], phi, moments(f))
        for i in range(Q):
            own_ref[2 * i + t] = g[i]
            state_ref[2 * i + t] = f[i]
        for s in range(STEPS):
            field_ref[2 * s + t] = kinds[s]
        field_ref[2 * OWN_PHI + t] = phi
        codes.append([jnp.where(top, phi, kinds[1]), kinds[2], kinds[3]])
    copies[4].wait()
    for i in range(Q):
        for way in (1, -1):
            near, far = (1, 0) if way == 1 else (0, 1)
            deep = 3 - way * VELOCITIES[i][1]
            cot = tile_of(cot_ref, i, near)
            g_far = own_ref[2 * i + far]
            if way == 1:
                mixed = jnp.where(column >= deep, g_far, columns(cot, deep - 4))
            else:
                mixed = jnp.where(column < 4 - deep, g_far, columns(cot, 4 - deep))
            deal.put(way, 2 * i, mixed if far == 0 else own_ref[2 * i])
            deal.put(way, 2 * i + 1, mixed if far == 1 else own_ref[2 * i + 1])
    for way in (1, -1):
        near, far = (1, 0) if way == 1 else (0, 1)
        outer = 3 if way == 1 else 0
        deal.put(way, Y_CODE1, codes[near][0])
        deal.put(way, Y_CODE2, codes[near][1])
        outside = columns(codes[far][0], 3 - 2 * outer)
        deal.put(way, Y_CODE3, jnp.where(column == 3 - outer, outside, codes[near][2]))
        extra = None
        for k, i in enumerate(turned(1, -way)):
            value = columns(own_ref[2 * i + far], k - outer)
            extra = value if extra is None else jnp.where(column == k, value, extra)
        deal.put(way, Y_POP, extra)
        extra = None
        for k, i in enumerate(turned(1, way)):
            value = columns(tile_of(cot_ref, i, near), k - (1 if way == 1 else 2))
            extra = value if extra is None else jnp.where(column == k, value, extra)
        deal.put(way, Y_COT, extra)
    for t in range(2):
        for i in range(Q):
            own_cot_ref[2 * i + t] = tile_of(cot_ref, i, t)
        pack_lines(
            Deal(is_even("gx"), first_side_ref, second_side_ref),
            X_LANE * t,
            lambda i: own_ref[2 * i + t],
            lambda i: tile_of(cot_ref, i, t),
            lambda s: codes[t][s - 1],
        )


def from_y(left_ref, right_ref):
    row, lane, column, depth = iotas()
    high = lane >= LANES // 2

    def population(i, c):
        if c == 1:
            return left_ref[2 * i + 1]
        if c == 4:
            return right_ref[2 * i]
        along_y = VELOCITIES[i][1]
        left, right = left_ref[2 * i], right_ref[2 * i + 1]
        if along_y == 1 and i in turned(1, 1):
            right = columns(right_ref[Y_POP], -turned(1, 1).index(i))
        if along_y == -1 and i in turned(1, -1):
            left = columns(left_ref[Y_POP], 3 - turned(1, -1).index(i))
        return jnp.where(high, left, right)

    def cotangent(i, c):
        ref, way, place, far = (left_ref, 1, 1, 0) if c == 1 else (right_ref, -1, 2, 1)
        deep = 3 - way * VELOCITIES[i][1]
        value = columns(ref[2 * i + far], way * (4 - deep))
        if i in turned(1, way):
            extra = columns(ref[Y_COT], place - turned(1, way).index(i))
            value = jnp.where(column == place, extra, value)
        return value

    def codes(s, c):
        if c == 0:
            left, right = columns(left_ref[Y_CODE3], 3), columns(right_ref[Y_CODE3], 1)
            return jnp.where(high, left, right)
        return (left_ref if c == 1 else right_ref)[(Y_CODE1, Y_CODE2, Y_CODE3)[s - 1]]

    return population, cotangent, codes


def pack_lines(deal, first, population, cotangent, codes):
    row, lane, column, depth = iotas()

    def put(at, pop, cot, deep, way):
        if way == 1:
            mixed = jnp.where(row >= deep, pop, lines(cot, deep))
        else:
            mixed = jnp.where(row < ROWS - deep, pop, lines(cot, -deep))
        deal.put(way, first + at, mixed)

    for i in range(Q):
        pop, cot = population(i), cotangent(i)
        for way in (1, -1):
            put(i, pop, cot, 3 - way * VELOCITIES[i][0], way)
    for way in (1, -1):
        extra = None
        for k, i in enumerate(turned(0, -way)):
            value = lines(population(i), k - (3 if way == 1 else 4))
            extra = value if extra is None else jnp.where(row == k, value, extra)
        for k, i in enumerate(turned(0, way)):
            value = lines(cotangent(i), 4 + k - (5 if way == 1 else 2))
            extra = jnp.where(row == 4 + k, value, extra)
        deal.put(way, first + X_EXTRA, extra)
        put(X_CODE13, codes(1), codes(3), 3, way)


def from_x(ref, n, way):
    row, lane, column, depth = iotas()
    first = X_LANE * n

    def population(i):
        value = ref[first + i]
        if i in turned(0, -way):
            place = 3 if way == 1 else 4
            extra = lines(ref[first + X_EXTRA], place - turned(0, -way).index(i))
            value = jnp.where(row == place, extra, value)
        return value

    def cotangent(i):
        value = lines(ref[first + i], -way * (3 - way * VELOCITIES[i][0]))
        if i in turned(0, way):
            place = 5 if way == 1 else 2
            extra = lines(ref[first + X_EXTRA], place - 4 - turned(0, way).index(i))
            value = jnp.where(row == place, extra, value)
        return value

    def codes(s):
        if s == 2:
            return lines(ref[X_CODE2 + n // 2], 4 * (n % 2))
        value = ref[first + X_CODE13]
        return value if s == 1 else lines(value, -3 * way)

    return population, cotangent, codes


def pack_x(field_ref, first_y_ref, second_y_ref, early_a, early_b, first_ref, second_ref):
    row, lane, column, depth = iotas()
    deal = Deal(is_even("gx"), first_ref, second_ref, X_SIDE)
    population, cotangent, codes = from_y(*sides(first_y_ref, second_y_ref, "gy"))

    def both_codes(at, first, second):
        second = lines(second, 4)
        deal.put(1, at, jnp.where(row >= 4, first, second))
        deal.put(-1, at, jnp.where(row < 4, first, second))

    for n, c in ((2, 1), (3, 4)):
        pack_lines(
            deal,
            X_LANE * n,
            lambda i: population(i, c),
            lambda i: cotangent(i, c),
            lambda s: codes(s, c),
        )
    for n in range(Q + 1):
        value = population(n, 0) if n < Q else codes(1, 0)
        first_ref[X_RING + n - X_SIDE] = value
        second_ref[X_RING + n - X_SIDE] = value
    both_codes(X_CODE2, field_ref[4], field_ref[5])
    both_codes(X_CODE2 + 1, codes(2, 1), codes(2, 4))
    second_ref[X_TILES - X_SIDE] = jnp.zeros((ROWS, LANES), jnp.float32)


def sides(first_ref, second_ref, axis):
    even = is_even(axis)
    return Pick(even, second_ref, first_ref), Pick(even, first_ref, second_ref)


def add_panels(parts_ref, out_ref):
    out_ref[...] = jnp.sum(parts_ref[...], axis=0)


def fill(from_left, own_ref, field_ref, cot_ref, from_below, pop, cot, field):
    row, lane, column, depth = iotas()
    top = depth == NZ - 1

    def put(c, r, population, cotangent, codes):
        rows = pl.ds(ROWS * (r + 1), ROWS)
        for i in range(Q):
            pop[5 * i + c, rows, :] = population(i)
            if c:
                cot[4 * i + c - 1, rows, :] = cotangent(i)
        code = codes(1)
        phi = jnp.where(top, code, 0.0)
        for step in (1, 2, 4, 8, 16):
            phi = phi + pltpu.roll(phi, LANES - step, 1)
        field[F_CODE1 + c, rows, :] = jnp.where(top, 0.0, code)
        field[F_PHI + c, rows, :] = phi
        if c:
            field[F_CODE2 + c - 1, rows, :] = codes(2)
            field[F_CODE3 + c - 1, rows, :] = codes(3)

    for c in (0, 1, 4):
        put(c, 1, *(functools.partial(lambda g, n: g(n, c), get) for get in from_left))
    for t in range(2):
        rows = pl.ds(2 * ROWS, ROWS)
        for i in range(Q):
            pop[5 * i + 2 + t, rows, :] = own_ref[2 * i + t]
            cot[4 * i + 1 + t, rows, :] = cot_ref[2 * i + t]
        field[F_CODE1 + 2 + t, rows, :] = field_ref[2 + t]
        field[F_CODE2 + 1 + t, rows, :] = field_ref[4 + t]
        field[F_CODE3 + 1 + t, rows, :] = field_ref[6 + t]
        field[F_PHI + 2 + t, rows, :] = field_ref[2 * OWN_PHI + t]
    for way, r, ref in ((1, 0, from_below[0]), (-1, 2, from_below[1])):
        for n, c in enumerate((2, 3, 1, 4)):
            put(c, r, *from_x(ref, n, way))
        put(0, r, lambda i: ref[X_RING + i], None, lambda s: ref[X_RING + Q])


def steps_kernel(
    sizes,
    state_ref,
    cot_ref,
    own_ref,
    own_field_ref,
    names_ref,
    first_y_ref,
    second_y_ref,
    first_side_ref,
    second_side_ref,
    first_x_ref,
    second_x_ref,
    adjoint_ref,
    panel_ref,
    pop_a,
    pop_b,
    cot,
    field,
    saved,
    mom,
    grad,
):
    size_x, size_y = sizes
    fill(
        from_y(*sides(first_y_ref, second_y_ref, "gy")),
        own_ref,
        own_field_ref,
        cot_ref,
        sides(
            Joined(first_side_ref, first_x_ref, X_SIDE),
            Joined(second_side_ref, second_x_ref, X_SIDE),
            "gx",
        ),
        pop_a,
        cot,
        field,
    )

    at_x, at_y = lax.axis_index("gx"), lax.axis_index("gy")
    edges = (
        jnp.where(at_x == 0, 1, 0),
        jnp.where(at_x == size_x - 1, 1, 0),
        jnp.where(at_y == 0, 1, 0),
        jnp.where(at_y == size_y - 1, 1, 0),
    )
    lane = lax.broadcasted_iota(jnp.int32, (ROWS, LANES), 1)

    def streamed(ref, tile, tiles, r, sign, masks, four):
        step = {0: tile, -1: lax.rem(tile + tiles - 1, tiles), 1: lax.rem(tile + 1, tiles)}

        def load(i, tile_step, row_step):
            return ref[tiles * i + step[tile_step], pl.ds(ROWS * (r + 1) + row_step, ROWS), :]

        return stream_tile(load, sign, masks, lane)

    def masks_of(tile, first, r):
        return wall_masks(r == 1, tile == first, tile == first + 1, edges)

    def rows_of(r):
        return pl.ds(ROWS * (r + 1), ROWS)

    def forward(source, tiles, own, s, target, target_tiles, offset):
        def body(tile, carry):
            ring = tile - offset if target_tiles != tiles else tile
            for r in range(3):
                f = streamed(source, tile, tiles, r, 1, masks_of(tile, own, r), None)
                parts = moments(f)
                _, _, rho, rinv, u = parts
                place = tile if tiles == 4 else lax.rem(tile + 4, 5)
                for n, value in enumerate((rho, rinv, *u)):
                    mom[s - 1, n, place, pl.ds(ROWS * r, ROWS), :] = value
                if r == 1:
                    for i in range(Q):
                        saved[s - 1, i, place] = f[i]
                if target is not None:
                    at = tile if tiles == 5 else tile + 1
                    first = F_CODE1 if s == 1 else F_CODE2 - 1
                    kind = field[first + at, rows_of(r), :]
                    phi = field[F_PHI + at, rows_of(r), :]
                    g = collide(f, kind, phi, parts)
                    for i in range(Q):
                        target[target_tiles * i + ring, rows_of(r), :] = g[i]
            return carry

        start, stop = (0, 5) if target_tiles == 5 else (1, 5)
        if tiles == 4:
            start, stop = 0, 4
        lax.fori_loop(start, stop, body, 0)

    forward(pop_a, 5, 2, 1, pop_b, 5, 0)
    forward(pop_b, 5, 2, 2, pop_a, 4, 1)
    forward(pop_a, 4, 1, 3, None, 4, 0)

    def backward(source, s, target):
        def body(tile, carry):
            for r in range(3):
                b = streamed(source, tile, 4, r, -1, masks_of(tile, 1, r), None)
                rho, rinv, *u = [
                    mom[s - 1, n, tile, pl.ds(ROWS * r, ROWS), :] for n in range(5)
                ]
                first = (F_CODE1 + 1, F_CODE2, F_CODE3)[s - 1]
                kind = field[first + tile, rows_of(r), :]
                phi = field[F_PHI + 1 + tile, rows_of(r), :]
                state = [saved[s - 1, i, tile] for i in range(Q)] if r == 1 else None
                back, term = collide_back(b, kind, phi, rho, rinv, u, state)
                for i in range(Q):
                    target[4 * i + tile, rows_of(r), :] = back[i]
                if r == 1:
                    grad[tile] = term if s == 3 else grad[tile] + term
            return carry

        lax.fori_loop(0, 4, body, 0)

    backward(cot, 3, pop_a)
    backward(pop_a, 2, pop_b)
    backward(pop_b, 1, pop_a)

    row = lax.broadcasted_iota(jnp.int32, (ROWS, LANES), 0)
    panel = lax.broadcasted_iota(jnp.int32, panel_ref.shape, 1)
    sums = jnp.zeros(panel_ref.shape, jnp.float32)
    for tile in range(2):
        lanes = pl.ds(tile * LANES, LANES)
        b = streamed(pop_a, tile + 1, 4, 1, -1, masks_of(tile, 0, 1), None)
        f = [state_ref[2 * i + tile] for i in range(Q)]
        kind = own_field_ref[tile]
        phi = own_field_ref[2 * OWN_PHI + tile]
        _, _, rho, rinv, u = moments(f)
        back, term = collide_back(b, kind, phi, rho, rinv, u, f)
        for i in range(Q):
            adjoint_ref[i, :, lanes] = back[i]
        term = term + grad[tile + 1]
        for part in range(2):
            inside = (row < 4) if part == 0 else (row >= 4)
            amount = jnp.sum(jnp.where(inside, term, 0.0))
            name = names_ref[tile, 4 * part : 4 * part + 1, 0:1]
            sums = sums + jnp.where(panel == name, amount, 0.0)
    panel_ref[...] = sums


VMEM = pl.BlockSpec(memory_space=pltpu.VMEM)
HBM = pl.BlockSpec(memory_space=pltpu.HBM)
ANY = pl.BlockSpec(memory_space=pl.ANY)


def shape_of(*dims):
    return jax.ShapeDtypeStruct(dims, jnp.float32)


def tiles_of(count):
    return shape_of(count, ROWS, LANES)


def on_device(sizes, checkpoint, cotangent, cell_codes, porosity, baffle_index):
    size_x, size_y = sizes
    panels = porosity.shape[0]
    devices = size_x * size_y

    def call(kernel, out_shape, in_specs, scratch=(), name=None):
        return pl.pallas_call(
            kernel,
            out_shape=out_shape,
            in_specs=in_specs,
            out_specs=jax.tree.map(lambda _: VMEM, out_shape),
            scratch_shapes=scratch,
            compiler_params=pltpu.CompilerParams(vmem_limit_bytes=32 * 1024 * 1024),
            name=name,
        )

    def swap(value, axis, size):
        return lax.ppermute(value, axis, [(i, i ^ 1) for i in range(size) if i ^ 1 < size])

    def swap_between(value, axis, size):
        pairs = [(i, i + 1) for i in range(1, size - 1, 2)]
        return lax.ppermute(value, axis, pairs + [(j, i) for i, j in pairs])

    arguments = [
        pltpu.with_memory_space_constraint(value, pltpu.HBM)
        for value in (checkpoint, cotangent, cell_codes, baffle_index, porosity)
    ]
    first_y, second_y, first_side, second_side, own, state, cot, field, names = call(
        pack_own,
        (tiles_of(Y_TILES),) * 2
        + (tiles_of(X_SIDE),) * 2
        + (tiles_of(2 * Q),) * 3
        + (tiles_of(2 * OWN_PHI + 2), jax.ShapeDtypeStruct((2, ROWS, LANES), jnp.int32)),
        [HBM] * 5,
        [
            pltpu.VMEM((Q, ROWS, 2 * LANES), jnp.float32),
            pltpu.VMEM((Q, ROWS, 2 * LANES), jnp.float32),
            pltpu.VMEM((STEPS, ROWS, 2 * LANES), jnp.int32),
            pltpu.SMEM(baffle_index.shape, jnp.int32),
            pltpu.SMEM(porosity.shape, jnp.float32),
            pltpu.SemaphoreType.DMA((5,)),
        ],
        name="pack_own",
    )(*arguments)
    second_y = swap_between(second_y, "gy", size_y)
    first_y = swap(first_y, "gy", size_y)
    second_side = swap_between(second_side, "gx", size_x)
    first_side = swap(first_side, "gx", size_x)
    rest = X_TILES - X_SIDE
    first_x, second_x = call(
        pack_x,
        (tiles_of(rest), tiles_of(rest + SPARE)),
        [VMEM] * 3 + [ANY] * 2,
        name="pack_x",
    )(field, first_y, second_y, first_side, second_side)
    second_x = swap_between(second_x, "gx", size_x)
    first_x = swap(first_x, "gx", size_x)

    adjoint, sums = call(
        functools.partial(steps_kernel, sizes),
        (shape_of(Q, ROWS, 2 * LANES), shape_of(devices, panels)),
        [VMEM] * 11,
        [
            pltpu.VMEM((5 * Q, 5 * ROWS, LANES), jnp.float32),
            pltpu.VMEM((5 * Q, 5 * ROWS, LANES), jnp.float32),
            pltpu.VMEM((4 * Q, 5 * ROWS, LANES), jnp.float32),
            pltpu.VMEM((FIELDS, 5 * ROWS, LANES), jnp.float32),
            pltpu.VMEM((3, Q, 5, ROWS, LANES), jnp.float32),
            pltpu.VMEM((3, 5, 5, 3 * ROWS, LANES), jnp.float32),
            pltpu.VMEM((4, ROWS, LANES), jnp.float32),
        ],
        name="steps",
    )(state, cot, own, field, names, first_y, second_y, first_side, second_side, first_x, second_x)
    gathered = lax.all_to_all(sums, ("gx", "gy"), 0, 0, tiled=True)
    totals = call(add_panels, shape_of(1, panels), [VMEM], name="add_panels")(
        gathered.reshape(devices, 1, panels)
    )
    return adjoint, totals.reshape(panels)


def solution(mesh):
    sizes = (mesh.shape["gx"], mesh.shape["gy"])
    in_specs = (P(None, "gx", "gy"), P(None, "gx", "gy"), P(None, "gx", "gy"), P(), P("gx", "gy"))
    out_specs = (P(None, "gx", "gy"), P())
    return jax.shard_map(
        functools.partial(on_device, sizes),
        mesh=mesh,
        in_specs=in_specs,
        out_specs=out_specs,
        check_vma=False,
    )
```

```python
import functools

import jax
import jax.numpy as jnp
import numpy as np
from jax import lax
from jax.experimental import pallas as pl
from jax.experimental.pallas import tpu as pltpu
from jax.sharding import PartitionSpec as P

Q = 19
STEPS = 4
NZ = 32
ROWS = 8
LANES = 128
OMEGA = 1.6
ACCEL = (0.002, 0.0, -0.003)
SHIFT = tuple(a / OMEGA for a in ACCEL)

VELOCITIES = [
    (0, 0, 0),
    (1, 0, 0),
    (-1, 0, 0),
    (0, 1, 0),
    (0, -1, 0),
    (0, 0, 1),
    (0, 0, -1),
    (1, 1, 0),
    (-1, -1, 0),
    (1, -1, 0),
    (-1, 1, 0),
    (1, 0, 1),
    (-1, 0, -1),
    (1, 0, -1),
    (-1, 0, 1),
    (0, 1, 1),
    (0, -1, -1),
    (0, 1, -1),
    (0, -1, 1),
]
OPPOSITE = [0, 2, 1, 4, 3, 6, 5, 8, 7, 10, 9, 12, 11, 14, 13, 16, 15, 18, 17]
PAIRS = [(i, i + 1) for i in range(1, Q, 2)]
W_REST, W_AXIS, W_DIAG = 1.0 / 3.0, 1.0 / 18.0, 1.0 / 36.0

Y_CODE1, Y_CODE2, Y_CODE3, Y_POP, Y_COT = 38, 39, 40, 41, 42
Y_TILES = 43
SPARE = 1
X_EXTRA, X_CODE13 = 19, 20
X_LANE = 21
X_RING = 4 * X_LANE
X_CODE2 = X_RING + Q + 1
X_TILES = X_CODE2 + 2
X_SIDE = 2 * X_LANE
F_CODE1, F_CODE2, F_CODE3, F_PHI = 0, 5, 9, 13
FIELDS = 18
OWN_PHI = 4


def turned(axis, outward):
    return [i for i, v in enumerate(VELOCITIES) if v[axis] == outward and sum(map(abs, v)) == 2]


def total(values):
    values = list(values)
    while len(values) > 1:
        values = [a + b for a, b in zip(values[::2], values[1::2])] + (
            [values[-1]] if len(values) % 2 else []
        )
    return values[0]


def along(vector, three):
    terms = None
    for c, value in zip(vector, three):
        if c == 0:
            continue
        if terms is None:
            terms = value if c > 0 else -value
        else:
            terms = terms + value if c > 0 else terms - value
    return terms


def moments(f):
    plus = {i: f[i] + f[o] for i, o in PAIRS}
    minus = {i: f[i] - f[o] for i, o in PAIRS}
    rho = total([f[0]] + [plus[i] for i, _ in PAIRS])
    rinv = 1.0 / rho
    u = []
    for axis in range(3):
        terms = [
            minus[i] if VELOCITIES[i][axis] > 0 else -minus[i]
            for i, _ in PAIRS
            if VELOCITIES[i][axis] != 0
        ]
        u.append(total(terms) * rinv + SHIFT[axis])
    return plus, minus, rho, rinv, u


def coefficients(kind, phi, rinv):
    baffle = kind == 3.0
    gas = kind == 0.0
    even = jnp.where(gas, 0.0, jnp.where(baffle, 0.5 - 0.5 * OMEGA * phi, 0.5 * (1.0 - OMEGA)))
    odd = jnp.where(
        gas, 0.0, jnp.where(baffle, (1.0 - 0.5 * OMEGA) * phi - 0.5, 0.5 * (1.0 - OMEGA))
    )
    slope = jnp.where(
        baffle,
        OMEGA * phi,
        jnp.where(kind == 1.0, OMEGA, jnp.where(kind == 2.0, OMEGA * rinv, 0.0)),
    )
    return even, odd, slope


def collide(f, kind, phi, parts):
    plus, minus, rho, rinv, u = parts
    even, odd, slope = coefficients(kind, phi, rinv)
    scale = slope * rho
    rest = 1.0 - 1.5 * (u[0] * u[0] + u[1] * u[1] + u[2] * u[2])
    base = scale * rest + jnp.where(kind == 0.0, 1.0, 0.0)
    out = [None] * Q
    out[0] = 2.0 * even * f[0] + W_REST * base
    for weight, pairs in ((W_AXIS, PAIRS[:3]), (W_DIAG, PAIRS[3:])):
        flat = weight * base
        three = (3.0 * weight) * scale
        for i, o in pairs:
            cu = along(VELOCITIES[i], u)
            lin = three * cu
            ev = even * plus[i] + (flat + 1.5 * lin * cu)
            od = odd * minus[i] + lin
            out[i] = ev + od
            out[o] = ev - od
    return out


def collide_back(b, kind, phi, rho, rinv, u, state=None):
    even, odd, slope = coefficients(kind, phi, rinv)
    plus = {i: b[i] + b[o] for i, o in PAIRS}
    minus = {i: b[i] - b[o] for i, o in PAIRS}
    rest = 1.0 - 1.5 * (u[0] * u[0] + u[1] * u[1] + u[2] * u[2])
    u_half = [1.5 * c for c in u]
    weighted = W_REST * b[0]
    energy = 0.0
    vector = [0.0, 0.0, 0.0]
    for weight, pairs in ((W_AXIS, PAIRS[:3]), (W_DIAG, PAIRS[3:])):
        weighted = weighted + weight * total([plus[i] for i, _ in pairs])
        energies, parts = [], ([], [], [])
        for i, _ in pairs:
            cu = along(VELOCITIES[i], u)
            half = along(VELOCITIES[i], u_half) * plus[i]
            first = minus[i] + half
            energies.append(cu * first)
            second = first + half
            for axis in range(3):
                c = VELOCITIES[i][axis]
                if c:
                    parts[axis].append(second if c > 0 else -second)
        energy = energy + (3.0 * weight) * total(energies)
        vector = [vector[k] + (3.0 * weight) * total(parts[k]) for k in range(3)]
    energy = energy + rest * weighted
    vector = [vector[k] - (3.0 * weighted) * u[k] for k in range(3)]
    push = [slope * v for v in vector]
    inner = total([push[k] * (u[k] - SHIFT[k]) for k in range(3)])
    shared = jnp.where(kind == 2.0, 0.0, slope) * energy - inner
    out = [None] * Q
    out[0] = 2.0 * even * b[0] + shared
    for i, o in PAIRS:
        ev = even * plus[i] + shared
        od = odd * minus[i] + along(VELOCITIES[i], push)
        out[i] = ev + od
        out[o] = ev - od
    if state is None:
        return out, None
    evens = total([plus[i] * (state[i] + state[o]) for i, o in PAIRS])
    odds = total([minus[i] * (state[i] - state[o]) for i, o in PAIRS])
    term = (
        -OMEGA * (b[0] * state[0] + 0.5 * evens)
        + (1.0 - 0.5 * OMEGA) * odds
        + OMEGA * rho * energy
    )
    return out, jnp.where(kind == 3.0, term, 0.0)


def wall_masks(sign_rows, own_low, own_high, edges):
    lane = lax.broadcasted_iota(jnp.int32, (ROWS, LANES), 1)
    row = lax.broadcasted_iota(jnp.int32, (ROWS, LANES), 0)
    x_low, x_high, y_low, y_high = edges
    depth = lane % NZ
    masks = {}
    masks[2, 1] = depth == 0
    masks[2, -1] = depth == NZ - 1
    masks[1, 1] = lane < jnp.where(own_low, y_low * NZ, 0)
    masks[1, -1] = lane >= jnp.where(own_high, LANES - y_high * NZ, LANES)
    if sign_rows:
        masks[0, 1] = row < x_low
        masks[0, -1] = row >= ROWS - x_high
    return masks


def stream_tile(load, sign, masks, lane):
    cross_low, cross_high = lane >= LANES - NZ, lane < NZ
    combined = {}
    out = []
    for i, vector in enumerate(VELOCITIES):
        v = tuple(sign * c for c in vector)
        value = load(i, 0, -v[0])
        if v[1] == 1:
            value = jnp.where(cross_low, load(i, -1, -v[0]), value)
        elif v[1] == -1:
            value = jnp.where(cross_high, load(i, 1, -v[0]), value)
        amount = (v[1] * NZ + v[2]) % LANES
        if amount:
            value = pltpu.roll(value, amount, 1)
        outside = None
        if v not in combined:
            for axis in range(3):
                if v[axis] and (axis, v[axis]) in masks:
                    wall = masks[axis, v[axis]]
                    outside = wall if outside is None else outside | wall
            combined[v] = outside
        outside = combined[v]
        if outside is not None:
            value = jnp.where(outside, load(OPPOSITE[i], 0, 0), value)
        out.append(value)
    return out


def iotas():
    row = lax.broadcasted_iota(jnp.int32, (ROWS, LANES), 0)
    lane = lax.broadcasted_iota(jnp.int32, (ROWS, LANES), 1)
    return row, lane, lane // NZ, lane % NZ


def columns(value, count):
    amount = (count * NZ) % LANES
    return pltpu.roll(value, amount, 1) if amount else value


def lines(value, count):
    amount = count % ROWS
    return pltpu.roll(value, amount, 0) if amount else value


class Pick:
    def __init__(self, flag, first, second):
        self.flag, self.first, self.second = flag, first, second

    def __getitem__(self, at):
        return jnp.where(self.flag, self.first[at], self.second[at])


class Deal:
    def __init__(self, even, first, second, skip=0):
        self.even, self.first, self.second, self.skip, self.held = even, first, second, skip, {}

    def put(self, way, at, value):
        if (-way, at) not in self.held:
            self.held[way, at] = value
            return
        other = self.held.pop((-way, at))
        up, down = (value, other) if way == 1 else (other, value)
        self.first[at - self.skip] = jnp.where(self.even, up, down)
        self.second[at - self.skip] = jnp.where(self.even, down, up)


class Joined:
    def __init__(self, first, second, cut):
        self.first, self.second, self.cut = first, second, cut

    def __getitem__(self, at):
        return self.first[at] if at < self.cut else self.second[at - self.cut]


def is_even(axis):
    return lax.rem(lax.axis_index(axis), 2) == 0


def pack_own(
    f_hbm,
    cot_hbm,
    codes_hbm,
    panels_hbm,
    porosity_hbm,
    first_ref,
    second_ref,
    first_side_ref,
    second_side_ref,
    own_ref,
    state_ref,
    own_cot_ref,
    field_ref,
    names_ref,
    f_ref,
    cot_ref,
    codes_ref,
    panels_ref,
    porosity_ref,
    sems,
):
    pieces = (
        (panels_hbm, panels_ref),
        (porosity_hbm, porosity_ref),
        (f_hbm, f_ref),
        (codes_hbm, codes_ref),
        (cot_hbm, cot_ref),
    )
    copies = [
        pltpu.make_async_copy(source, target, sems.at[n])
        for n, (source, target) in enumerate(pieces)
    ]
    for copy in copies:
        copy.start()
    for copy in copies[:4]:
        copy.wait()
    deal = Deal(is_even("gy"), first_ref, second_ref)
    row, lane, column, depth = iotas()
    top = depth == NZ - 1

    def tile_of(ref, i, t):
        return ref[i, :, pl.ds(t * LANES, LANES)]

    codes, phis = [], []
    for t in range(2):
        names = panels_ref[0, t * LANES], panels_ref[4, t * LANES]
        phi = jnp.where(row < 4, porosity_ref[names[0]], porosity_ref[names[1]])
        names_ref[t] = jnp.where(row < 4, names[0], names[1])
        kinds = [tile_of(codes_ref, s, t).astype(jnp.float32) for s in range(STEPS)]
        f = [tile_of(f_ref, i, t) for i in range(Q)]
        g = collide(f, kinds[0], phi, moments(f))
        for i in range(Q):
            own_ref[2 * i + t] = g[i]
            state_ref[2 * i + t] = f[i]
        for s in range(STEPS):
            field_ref[2 * s + t] = kinds[s]
        field_ref[2 * OWN_PHI + t] = phi
        codes.append([jnp.where(top, phi, kinds[1]), kinds[2], kinds[3]])
    copies[4].wait()
    for i in range(Q):
        for way in (1, -1):
            near, far = (1, 0) if way == 1 else (0, 1)
            deep = 3 - way * VELOCITIES[i][1]
            cot = tile_of(cot_ref, i, near)
            g_far = own_ref[2 * i + far]
            if way == 1:
                mixed = jnp.where(column >= deep, g_far, columns(cot, deep - 4))
            else:
                mixed = jnp.where(column < 4 - deep, g_far, columns(cot, 4 - deep))
            deal.put(way, 2 * i, mixed if far == 0 else own_ref[2 * i])
            deal.put(way, 2 * i + 1, mixed if far == 1 else own_ref[2 * i + 1])
    for way in (1, -1):
        near, far = (1, 0) if way == 1 else (0, 1)
        outer = 3 if way == 1 else 0
        deal.put(way, Y_CODE1, codes[near][0])
        deal.put(way, Y_CODE2, codes[near][1])
        outside = columns(codes[far][0], 3 - 2 * outer)
        deal.put(way, Y_CODE3, jnp.where(column == 3 - outer, outside, codes[near][2]))
        extra = None
        for k, i in enumerate(turned(1, -way)):
            value = columns(own_ref[2 * i + far], k - outer)
            extra = value if extra is None else jnp.where(column == k, value, extra)
        deal.put(way, Y_POP, extra)
        extra = None
        for k, i in enumerate(turned(1, way)):
            value = columns(tile_of(cot_ref, i, near), k - (1 if way == 1 else 2))
            extra = value if extra is None else jnp.where(column == k, value, extra)
        deal.put(way, Y_COT, extra)
    for t in range(2):
        for i in range(Q):
            own_cot_ref[2 * i + t] = tile_of(cot_ref, i, t)
        pack_lines(
            Deal(is_even("gx"), first_side_ref, second_side_ref),
            X_LANE * t,
            lambda i: own_ref[2 * i + t],
            lambda i: tile_of(cot_ref, i, t),
            lambda s: codes[t][s - 1],
        )


def from_y(left_ref, right_ref):
    row, lane, column, depth = iotas()
    high = lane >= LANES // 2

    def population(i, c):
        if c == 1:
            return left_ref[2 * i + 1]
        if c == 4:
            return right_ref[2 * i]
        along_y = VELOCITIES[i][1]
        left, right = left_ref[2 * i], right_ref[2 * i + 1]
        if along_y == 1 and i in turned(1, 1):
            right = columns(right_ref[Y_POP], -turned(1, 1).index(i))
        if along_y == -1 and i in turned(1, -1):
            left = columns(left_ref[Y_POP], 3 - turned(1, -1).index(i))
        return jnp.where(high, left, right)

    def cotangent(i, c):
        ref, way, place, far = (left_ref, 1, 1, 0) if c == 1 else (right_ref, -1, 2, 1)
        deep = 3 - way * VELOCITIES[i][1]
        value = columns(ref[2 * i + far], way * (4 - deep))
        if i in turned(1, way):
            extra = columns(ref[Y_COT], place - turned(1, way).index(i))
            value = jnp.where(column == place, extra, value)
        return value

    def codes(s, c):
        if c == 0:
            left, right = columns(left_ref[Y_CODE3], 3), columns(right_ref[Y_CODE3], 1)
            return jnp.where(high, left, right)
        return (left_ref if c == 1 else right_ref)[(Y_CODE1, Y_CODE2, Y_CODE3)[s - 1]]

    return population, cotangent, codes


def pack_lines(deal, first, population, cotangent, codes):
    row, lane, column, depth = iotas()

    def put(at, pop, cot, deep, way):
        if way == 1:
            mixed = jnp.where(row >= deep, pop, lines(cot, deep))
        else:
            mixed = jnp.where(row < ROWS - deep, pop, lines(cot, -deep))
        deal.put(way, first + at, mixed)

    for i in range(Q):
        pop, cot = population(i), cotangent(i)
        for way in (1, -1):
            put(i, pop, cot, 3 - way * VELOCITIES[i][0], way)
    for way in (1, -1):
        extra = None
        for k, i in enumerate(turned(0, -way)):
            value = lines(population(i), k - (3 if way == 1 else 4))
            extra = value if extra is None else jnp.where(row == k, value, extra)
        for k, i in enumerate(turned(0, way)):
            value = lines(cotangent(i), 4 + k - (5 if way == 1 else 2))
            extra = jnp.where(row == 4 + k, value, extra)
        deal.put(way, first + X_EXTRA, extra)
        put(X_CODE13, codes(1), codes(3), 3, way)


def from_x(ref, n, way):
    row, lane, column, depth = iotas()
    first = X_LANE * n

    def population(i):
        value = ref[first + i]
        if i in turned(0, -way):
            place = 3 if way == 1 else 4
            extra = lines(ref[first + X_EXTRA], place - turned(0, -way).index(i))
            value = jnp.where(row == place, extra, value)
        return value

    def cotangent(i):
        value = lines(ref[first + i], -way * (3 - way * VELOCITIES[i][0]))
        if i in turned(0, way):
            place = 5 if way == 1 else 2
            extra = lines(ref[first + X_EXTRA], place - 4 - turned(0, way).index(i))
            value = jnp.where(row == place, extra, value)
        return value

    def codes(s):
        if s == 2:
            return lines(ref[X_CODE2 + n // 2], 4 * (n % 2))
        value = ref[first + X_CODE13]
        return value if s == 1 else lines(value, -3 * way)

    return population, cotangent, codes


def pack_x(field_ref, first_y_ref, second_y_ref, early_a, early_b, first_ref, second_ref):
    row, lane, column, depth = iotas()
    deal = Deal(is_even("gx"), first_ref, second_ref, X_SIDE)
    population, cotangent, codes = from_y(*sides(first_y_ref, second_y_ref, "gy"))

    def both_codes(at, first, second):
        second = lines(second, 4)
        deal.put(1, at, jnp.where(row >= 4, first, second))
        deal.put(-1, at, jnp.where(row < 4, first, second))

    for n, c in ((2, 1), (3, 4)):
        pack_lines(
            deal,
            X_LANE * n,
            lambda i: population(i, c),
            lambda i: cotangent(i, c),
            lambda s: codes(s, c),
        )
    for n in range(Q + 1):
        value = population(n, 0) if n < Q else codes(1, 0)
        first_ref[X_RING + n - X_SIDE] = value
        second_ref[X_RING + n - X_SIDE] = value
    both_codes(X_CODE2, field_ref[4], field_ref[5])
    both_codes(X_CODE2 + 1, codes(2, 1), codes(2, 4))
    second_ref[X_TILES - X_SIDE] = jnp.zeros((ROWS, LANES), jnp.float32)


def sides(first_ref, second_ref, axis):
    even = is_even(axis)
    return Pick(even, second_ref, first_ref), Pick(even, first_ref, second_ref)


def add_panels(parts_ref, out_ref):
    out_ref[...] = jnp.sum(parts_ref[...], axis=0)


def fill(from_left, own_ref, field_ref, cot_ref, from_below, pop, cot, field):
    row, lane, column, depth = iotas()
    top = depth == NZ - 1

    def put(c, r, population, cotangent, codes):
        rows = pl.ds(ROWS * (r + 1), ROWS)
        for i in range(Q):
            pop[5 * i + c, rows, :] = population(i)
            if c:
                cot[4 * i + c - 1, rows, :] = cotangent(i)
        code = codes(1)
        phi = jnp.where(top, code, 0.0)
        for step in (1, 2, 4, 8, 16):
            phi = phi + pltpu.roll(phi, LANES - step, 1)
        field[F_CODE1 + c, rows, :] = jnp.where(top, 0.0, code)
        field[F_PHI + c, rows, :] = phi
        if c:
            field[F_CODE2 + c - 1, rows, :] = codes(2)
            field[F_CODE3 + c - 1, rows, :] = codes(3)

    for c in (0, 1, 4):
        put(c, 1, *(functools.partial(lambda g, n: g(n, c), get) for get in from_left))
    for t in range(2):
        rows = pl.ds(2 * ROWS, ROWS)
        for i in range(Q):
            pop[5 * i + 2 + t, rows, :] = own_ref[2 * i + t]
            cot[4 * i + 1 + t, rows, :] = cot_ref[2 * i + t]
        field[F_CODE1 + 2 + t, rows, :] = field_ref[2 + t]
        field[F_CODE2 + 1 + t, rows, :] = field_ref[4 + t]
        field[F_CODE3 + 1 + t, rows, :] = field_ref[6 + t]
        field[F_PHI + 2 + t, rows, :] = field_ref[2 * OWN_PHI + t]
    for way, r, ref in ((1, 0, from_below[0]), (-1, 2, from_below[1])):
        for n, c in enumerate((2, 3, 1, 4)):
            put(c, r, *from_x(ref, n, way))
        put(0, r, lambda i: ref[X_RING + i], None, lambda s: ref[X_RING + Q])


def steps_kernel(
    sizes,
    state_ref,
    cot_ref,
    own_ref,
    own_field_ref,
    names_ref,
    first_y_ref,
    second_y_ref,
    first_side_ref,
    second_side_ref,
    first_x_ref,
    second_x_ref,
    adjoint_ref,
    panel_ref,
    pop_a,
    pop_b,
    cot,
    field,
    saved,
    mom,
    grad,
):
    size_x, size_y = sizes
    fill(
        from_y(*sides(first_y_ref, second_y_ref, "gy")),
        own_ref,
        own_field_ref,
        cot_ref,
        sides(
            Joined(first_side_ref, first_x_ref, X_SIDE),
            Joined(second_side_ref, second_x_ref, X_SIDE),
            "gx",
        ),
        pop_a,
        cot,
        field,
    )

    at_x, at_y = lax.axis_index("gx"), lax.axis_index("gy")
    edges = (
        jnp.where(at_x == 0, 1, 0),
        jnp.where(at_x == size_x - 1, 1, 0),
        jnp.where(at_y == 0, 1, 0),
        jnp.where(at_y == size_y - 1, 1, 0),
    )
    lane = lax.broadcasted_iota(jnp.int32, (ROWS, LANES), 1)

    def streamed(ref, tile, tiles, r, sign, masks, four):
        step = {0: tile, -1: lax.rem(tile + tiles - 1, tiles), 1: lax.rem(tile + 1, tiles)}

        def load(i, tile_step, row_step):
            return ref[tiles * i + step[tile_step], pl.ds(ROWS * (r + 1) + row_step, ROWS), :]

        return stream_tile(load, sign, masks, lane)

    def masks_of(tile, first, r):
        return wall_masks(r == 1, tile == first, tile == first + 1, edges)

    def rows_of(r):
        return pl.ds(ROWS * (r + 1), ROWS)

    def forward(source, tiles, own, s, target, target_tiles, offset):
        def body(tile, carry):
            ring = tile - offset if target_tiles != tiles else tile
            for r in range(3):
                f = streamed(source, tile, tiles, r, 1, masks_of(tile, own, r), None)
                parts = moments(f)
                _, _, rho, rinv, u = parts
                place = tile if tiles == 4 else lax.rem(tile + 4, 5)
                for n, value in enumerate((rho, rinv, *u)):
                    mom[s - 1, n, place, pl.ds(ROWS * r, ROWS), :] = value
                if r == 1:
                    for i in range(Q):
                        saved[s - 1, i, place] = f[i]
                if target is not None:
                    at = tile if tiles == 5 else tile + 1
                    first = F_CODE1 if s == 1 else F_CODE2 - 1
                    kind = field[first + at, rows_of(r), :]
                    phi = field[F_PHI + at, rows_of(r), :]
                    g = collide(f, kind, phi, parts)
                    for i in range(Q):
                        target[target_tiles * i + ring, rows_of(r), :] = g[i]
            return carry

        start, stop = (0, 5) if target_tiles == 5 else (1, 5)
        if tiles == 4:
            start, stop = 0, 4
        lax.fori_loop(start, stop, body, 0)

    forward(pop_a, 5, 2, 1, pop_b, 5, 0)
    forward(pop_b, 5, 2, 2, pop_a, 4, 1)
    forward(pop_a, 4, 1, 3, None, 4, 0)

    def backward(source, s, target):
        def body(tile, carry):
            for r in range(3):
                b = streamed(source, tile, 4, r, -1, masks_of(tile, 1, r), None)
                rho, rinv, *u = [
                    mom[s - 1, n, tile, pl.ds(ROWS * r, ROWS), :] for n in range(5)
                ]
                first = (F_CODE1 + 1, F_CODE2, F_CODE3)[s - 1]
                kind = field[first + tile, rows_of(r), :]
                phi = field[F_PHI + 1 + tile, rows_of(r), :]
                state = [saved[s - 1, i, tile] for i in range(Q)] if r == 1 else None
                back, term = collide_back(b, kind, phi, rho, rinv, u, state)
                for i in range(Q):
                    target[4 * i + tile, rows_of(r), :] = back[i]
                if r == 1:
                    grad[tile] = term if s == 3 else grad[tile] + term
            return carry

        lax.fori_loop(0, 4, body, 0)

    backward(cot, 3, pop_a)
    backward(pop_a, 2, pop_b)
    backward(pop_b, 1, pop_a)

    row = lax.broadcasted_iota(jnp.int32, (ROWS, LANES), 0)
    panel = lax.broadcasted_iota(jnp.int32, panel_ref.shape, 1)
    sums = jnp.zeros(panel_ref.shape, jnp.float32)
    for tile in range(2):
        lanes = pl.ds(tile * LANES, LANES)
        b = streamed(pop_a, tile + 1, 4, 1, -1, masks_of(tile, 0, 1), None)
        f = [state_ref[2 * i + tile] for i in range(Q)]
        kind = own_field_ref[tile]
        phi = own_field_ref[2 * OWN_PHI + tile]
        _, _, rho, rinv, u = moments(f)
        back, term = collide_back(b, kind, phi, rho, rinv, u, f)
        for i in range(Q):
            adjoint_ref[i, :, lanes] = back[i]
        term = term + grad[tile + 1]
        for part in range(2):
            inside = (row < 4) if part == 0 else (row >= 4)
            amount = jnp.sum(jnp.where(inside, term, 0.0))
            name = names_ref[tile, 4 * part : 4 * part + 1, 0:1]
            sums = sums + jnp.where(panel == name, amount, 0.0)
    panel_ref[...] = sums


VMEM = pl.BlockSpec(memory_space=pltpu.VMEM)
HBM = pl.BlockSpec(memory_space=pltpu.HBM)
ANY = pl.BlockSpec(memory_space=pl.ANY)


def shape_of(*dims):
    return jax.ShapeDtypeStruct(dims, jnp.float32)


def tiles_of(count):
    return shape_of(count, ROWS, LANES)


def on_device(sizes, checkpoint, cotangent, cell_codes, porosity, baffle_index):
    size_x, size_y = sizes
    panels = porosity.shape[0]
    devices = size_x * size_y

    def call(kernel, out_shape, in_specs, scratch=(), name=None):
        return pl.pallas_call(
            kernel,
            out_shape=out_shape,
            in_specs=in_specs,
            out_specs=jax.tree.map(lambda _: VMEM, out_shape),
            scratch_shapes=scratch,
            compiler_params=pltpu.CompilerParams(vmem_limit_bytes=32 * 1024 * 1024),
            name=name,
        )

    def swap(value, axis, size):
        return lax.ppermute(value, axis, [(i, i ^ 1) for i in range(size) if i ^ 1 < size])

    def swap_between(value, axis, size):
        pairs = [(i, i + 1) for i in range(1, size - 1, 2)]
        return lax.ppermute(value, axis, pairs + [(j, i) for i, j in pairs])

    arguments = [
        pltpu.with_memory_space_constraint(value, pltpu.HBM)
        for value in (checkpoint, cotangent, cell_codes, baffle_index, porosity)
    ]
    first_y, second_y, first_side, second_side, own, state, cot, field, names = call(
        pack_own,
        (tiles_of(Y_TILES),) * 2
        + (tiles_of(X_SIDE),) * 2
        + (tiles_of(2 * Q),) * 3
        + (tiles_of(2 * OWN_PHI + 2), jax.ShapeDtypeStruct((2, ROWS, LANES), jnp.int32)),
        [HBM] * 5,
        [
            pltpu.VMEM((Q, ROWS, 2 * LANES), jnp.float32),
            pltpu.VMEM((Q, ROWS, 2 * LANES), jnp.float32),
            pltpu.VMEM((STEPS, ROWS, 2 * LANES), jnp.int32),
            pltpu.SMEM(baffle_index.shape, jnp.int32),
            pltpu.SMEM(porosity.shape, jnp.float32),
            pltpu.SemaphoreType.DMA((5,)),
        ],
        name="pack_own",
    )(*arguments)
    second_y = swap_between(second_y, "gy", size_y)
    first_y = swap(first_y, "gy", size_y)
    second_side = swap_between(second_side, "gx", size_x)
    first_side = swap(first_side, "gx", size_x)
    rest = X_TILES - X_SIDE
    first_x, second_x = call(
        pack_x,
        (tiles_of(rest), tiles_of(rest + SPARE)),
        [VMEM] * 3 + [ANY] * 2,
        name="pack_x",
    )(field, first_y, second_y, first_side, second_side)
    second_x = swap_between(second_x, "gx", size_x)
    first_x = swap(first_x, "gx", size_x)

    adjoint, sums = call(
        functools.partial(steps_kernel, sizes),
        (shape_of(Q, ROWS, 2 * LANES), shape_of(1, panels)),
        [VMEM] * 11,
        [
            pltpu.VMEM((5 * Q, 5 * ROWS, LANES), jnp.float32),
            pltpu.VMEM((5 * Q, 5 * ROWS, LANES), jnp.float32),
            pltpu.VMEM((4 * Q, 5 * ROWS, LANES), jnp.float32),
            pltpu.VMEM((FIELDS, 5 * ROWS, LANES), jnp.float32),
            pltpu.VMEM((3, Q, 5, ROWS, LANES), jnp.float32),
            pltpu.VMEM((3, 5, 5, 3 * ROWS, LANES), jnp.float32),
            pltpu.VMEM((4, ROWS, LANES), jnp.float32),
        ],
        name="steps",
    )(state, cot, own, field, names, first_y, second_y, first_side, second_side, first_x, second_x)
    gathered = lax.all_gather(sums, ("gx", "gy"), tiled=True)
    totals = call(add_panels, shape_of(1, panels), [VMEM], name="add_panels")(
        gathered.reshape(devices, 1, panels)
    )
    return adjoint, totals.reshape(panels)


def solution(mesh):
    sizes = (mesh.shape["gx"], mesh.shape["gy"])
    in_specs = (P(None, "gx", "gy"), P(None, "gx", "gy"), P(None, "gx", "gy"), P(), P("gx", "gy"))
    out_specs = (P(None, "gx", "gy"), P())
    return jax.shard_map(
        functools.partial(on_device, sizes),
        mesh=mesh,
        in_specs=in_specs,
        out_specs=out_specs,
        check_vma=False,
    )
```

```python
import functools

import jax
import jax.numpy as jnp
import numpy as np
from jax import lax
from jax.experimental import pallas as pl
from jax.experimental.pallas import tpu as pltpu
from jax.sharding import PartitionSpec as P

Q = 19
STEPS = 4
NZ = 32
ROWS = 8
LANES = 128
OMEGA = 1.6
ACCEL = (0.002, 0.0, -0.003)
SHIFT = tuple(a / OMEGA for a in ACCEL)

VELOCITIES = [
    (0, 0, 0),
    (1, 0, 0),
    (-1, 0, 0),
    (0, 1, 0),
    (0, -1, 0),
    (0, 0, 1),
    (0, 0, -1),
    (1, 1, 0),
    (-1, -1, 0),
    (1, -1, 0),
    (-1, 1, 0),
    (1, 0, 1),
    (-1, 0, -1),
    (1, 0, -1),
    (-1, 0, 1),
    (0, 1, 1),
    (0, -1, -1),
    (0, 1, -1),
    (0, -1, 1),
]
OPPOSITE = [0, 2, 1, 4, 3, 6, 5, 8, 7, 10, 9, 12, 11, 14, 13, 16, 15, 18, 17]
PAIRS = [(i, i + 1) for i in range(1, Q, 2)]
W_REST, W_AXIS, W_DIAG = 1.0 / 3.0, 1.0 / 18.0, 1.0 / 36.0

Y_CODE1, Y_CODE2, Y_CODE3, Y_POP, Y_COT = 38, 39, 40, 41, 42
Y_TILES = 43
SPARE = 1
X_EXTRA, X_CODE13 = 19, 20
X_LANE = 21
X_RING = 4 * X_LANE
X_CODE2 = X_RING + Q + 1
X_TILES = X_CODE2 + 2
X_SIDE = 2 * X_LANE
OWN_PHI = 4


def turned(axis, outward):
    return [i for i, v in enumerate(VELOCITIES) if v[axis] == outward and sum(map(abs, v)) == 2]


def total(values):
    values = list(values)
    while len(values) > 1:
        values = [a + b for a, b in zip(values[::2], values[1::2])] + (
            [values[-1]] if len(values) % 2 else []
        )
    return values[0]


def along(vector, three):
    terms = None
    for c, value in zip(vector, three):
        if c == 0:
            continue
        if terms is None:
            terms = value if c > 0 else -value
        else:
            terms = terms + value if c > 0 else terms - value
    return terms


def moments(f):
    plus = {i: f[i] + f[o] for i, o in PAIRS}
    minus = {i: f[i] - f[o] for i, o in PAIRS}
    rho = total([f[0]] + [plus[i] for i, _ in PAIRS])
    rinv = 1.0 / rho
    u = []
    for axis in range(3):
        terms = [
            minus[i] if VELOCITIES[i][axis] > 0 else -minus[i]
            for i, _ in PAIRS
            if VELOCITIES[i][axis] != 0
        ]
        u.append(total(terms) * rinv + SHIFT[axis])
    return plus, minus, rho, rinv, u


def coefficients(kind, phi, rinv):
    baffle = kind == 3.0
    gas = kind == 0.0
    even = jnp.where(gas, 0.0, jnp.where(baffle, 0.5 - 0.5 * OMEGA * phi, 0.5 * (1.0 - OMEGA)))
    odd = jnp.where(
        gas, 0.0, jnp.where(baffle, (1.0 - 0.5 * OMEGA) * phi - 0.5, 0.5 * (1.0 - OMEGA))
    )
    slope = jnp.where(
        baffle,
        OMEGA * phi,
        jnp.where(kind == 1.0, OMEGA, jnp.where(kind == 2.0, OMEGA * rinv, 0.0)),
    )
    return even, odd, slope


def collide(f, kind, phi, parts):
    plus, minus, rho, rinv, u = parts
    even, odd, slope = coefficients(kind, phi, rinv)
    scale = slope * rho
    rest = 1.0 - 1.5 * (u[0] * u[0] + u[1] * u[1] + u[2] * u[2])
    base = scale * rest + jnp.where(kind == 0.0, 1.0, 0.0)
    out = [None] * Q
    out[0] = 2.0 * even * f[0] + W_REST * base
    for weight, pairs in ((W_AXIS, PAIRS[:3]), (W_DIAG, PAIRS[3:])):
        flat = weight * base
        three = (3.0 * weight) * scale
        for i, o in pairs:
            cu = along(VELOCITIES[i], u)
            lin = three * cu
            ev = even * plus[i] + (flat + 1.5 * lin * cu)
            od = odd * minus[i] + lin
            out[i] = ev + od
            out[o] = ev - od
    return out


def collide_back(b, kind, phi, rho, rinv, u, state=None):
    even, odd, slope = coefficients(kind, phi, rinv)
    plus = {i: b[i] + b[o] for i, o in PAIRS}
    minus = {i: b[i] - b[o] for i, o in PAIRS}
    rest = 1.0 - 1.5 * (u[0] * u[0] + u[1] * u[1] + u[2] * u[2])
    u_half = [1.5 * c for c in u]
    weighted = W_REST * b[0]
    energy = 0.0
    vector = [0.0, 0.0, 0.0]
    for weight, pairs in ((W_AXIS, PAIRS[:3]), (W_DIAG, PAIRS[3:])):
        weighted = weighted + weight * total([plus[i] for i, _ in pairs])
        energies, parts = [], ([], [], [])
        for i, _ in pairs:
            cu = along(VELOCITIES[i], u)
            half = along(VELOCITIES[i], u_half) * plus[i]
            first = minus[i] + half
            energies.append(cu * first)
            second = first + half
            for axis in range(3):
                c = VELOCITIES[i][axis]
                if c:
                    parts[axis].append(second if c > 0 else -second)
        energy = energy + (3.0 * weight) * total(energies)
        vector = [vector[k] + (3.0 * weight) * total(parts[k]) for k in range(3)]
    energy = energy + rest * weighted
    vector = [vector[k] - (3.0 * weighted) * u[k] for k in range(3)]
    push = [slope * v for v in vector]
    inner = total([push[k] * (u[k] - SHIFT[k]) for k in range(3)])
    shared = jnp.where(kind == 2.0, 0.0, slope) * energy - inner
    out = [None] * Q
    out[0] = 2.0 * even * b[0] + shared
    for i, o in PAIRS:
        ev = even * plus[i] + shared
        od = odd * minus[i] + along(VELOCITIES[i], push)
        out[i] = ev + od
        out[o] = ev - od
    if state is None:
        return out, None
    evens = total([plus[i] * (state[i] + state[o]) for i, o in PAIRS])
    odds = total([minus[i] * (state[i] - state[o]) for i, o in PAIRS])
    term = (
        -OMEGA * (b[0] * state[0] + 0.5 * evens)
        + (1.0 - 0.5 * OMEGA) * odds
        + OMEGA * rho * energy
    )
    return out, jnp.where(kind == 3.0, term, 0.0)


def wall_masks(sign_rows, own_low, own_high, edges):
    lane = lax.broadcasted_iota(jnp.int32, (ROWS, LANES), 1)
    row = lax.broadcasted_iota(jnp.int32, (ROWS, LANES), 0)
    x_low, x_high, y_low, y_high = edges
    depth = lane % NZ
    masks = {}
    masks[2, 1] = depth == 0
    masks[2, -1] = depth == NZ - 1
    masks[1, 1] = lane < jnp.where(own_low, y_low * NZ, 0)
    masks[1, -1] = lane >= jnp.where(own_high, LANES - y_high * NZ, LANES)
    if sign_rows:
        masks[0, 1] = row < x_low
        masks[0, -1] = row >= ROWS - x_high
    return masks


def stream_tile(load, sign, masks, lane):
    cross_low, cross_high = lane >= LANES - NZ, lane < NZ
    combined = {}
    out = []
    for i, vector in enumerate(VELOCITIES):
        v = tuple(sign * c for c in vector)
        value = load(i, 0, -v[0], v[1])
        if v[1] == 1:
            value = jnp.where(cross_low, load(i, -1, -v[0], 1), value)
        elif v[1] == -1:
            value = jnp.where(cross_high, load(i, 1, -v[0], -1), value)
        amount = (v[1] * NZ + v[2]) % LANES
        if amount:
            value = pltpu.roll(value, amount, 1)
        outside = None
        if v not in combined:
            for axis in range(3):
                if v[axis] and (axis, v[axis]) in masks:
                    wall = masks[axis, v[axis]]
                    outside = wall if outside is None else outside | wall
            combined[v] = outside
        outside = combined[v]
        if outside is not None:
            value = jnp.where(outside, load(OPPOSITE[i], 0, 0, 0), value)
        out.append(value)
    return out


def iotas():
    row = lax.broadcasted_iota(jnp.int32, (ROWS, LANES), 0)
    lane = lax.broadcasted_iota(jnp.int32, (ROWS, LANES), 1)
    return row, lane, lane // NZ, lane % NZ


def columns(value, count):
    amount = (count * NZ) % LANES
    return pltpu.roll(value, amount, 1) if amount else value


def lines(value, count):
    amount = count % ROWS
    return pltpu.roll(value, amount, 0) if amount else value


class Pick:
    def __init__(self, flag, first, second):
        self.flag, self.first, self.second = flag, first, second

    def __getitem__(self, at):
        return jnp.where(self.flag, self.first[at], self.second[at])


class Deal:
    def __init__(self, even, first, second, skip=0):
        self.even, self.first, self.second, self.skip, self.held = even, first, second, skip, {}

    def put(self, way, at, value):
        if (-way, at) not in self.held:
            self.held[way, at] = value
            return
        other = self.held.pop((-way, at))
        up, down = (value, other) if way == 1 else (other, value)
        self.first[at - self.skip] = jnp.where(self.even, up, down)
        self.second[at - self.skip] = jnp.where(self.even, down, up)


class Joined:
    def __init__(self, first, second, cut):
        self.first, self.second, self.cut = first, second, cut

    def __getitem__(self, at):
        return self.first[at] if at < self.cut else self.second[at - self.cut]


def is_even(axis):
    return lax.rem(lax.axis_index(axis), 2) == 0


def pack_own(
    f_hbm,
    cot_hbm,
    codes_hbm,
    panels_hbm,
    porosity_hbm,
    first_ref,
    second_ref,
    first_side_ref,
    second_side_ref,
    own_ref,
    state_ref,
    own_cot_ref,
    field_ref,
    names_ref,
    f_ref,
    cot_ref,
    codes_ref,
    panels_ref,
    porosity_ref,
    sems,
):
    pieces = (
        (panels_hbm, panels_ref),
        (porosity_hbm, porosity_ref),
        (f_hbm, f_ref),
        (codes_hbm, codes_ref),
        (cot_hbm, cot_ref),
    )
    copies = [
        pltpu.make_async_copy(source, target, sems.at[n])
        for n, (source, target) in enumerate(pieces)
    ]
    for copy in copies:
        copy.start()
    for copy in copies[:4]:
        copy.wait()
    deal = Deal(is_even("gy"), first_ref, second_ref)
    row, lane, column, depth = iotas()
    top = depth == NZ - 1

    def tile_of(ref, i, t):
        return ref[i, :, pl.ds(t * LANES, LANES)]

    codes, phis = [], []
    for t in range(2):
        names = panels_ref[0, t * LANES], panels_ref[4, t * LANES]
        phi = jnp.where(row < 4, porosity_ref[names[0]], porosity_ref[names[1]])
        names_ref[t] = jnp.where(row < 4, names[0], names[1])
        kinds = [tile_of(codes_ref, s, t).astype(jnp.float32) for s in range(STEPS)]
        f = [tile_of(f_ref, i, t) for i in range(Q)]
        g = collide(f, kinds[0], phi, moments(f))
        for i in range(Q):
            own_ref[2 * i + t] = g[i]
            state_ref[2 * i + t] = f[i]
        for s in range(STEPS):
            field_ref[2 * s + t] = kinds[s]
        field_ref[2 * OWN_PHI + t] = phi
        codes.append([jnp.where(top, phi, kinds[1]), kinds[2], kinds[3]])
    copies[4].wait()
    for i in range(Q):
        for way in (1, -1):
            near, far = (1, 0) if way == 1 else (0, 1)
            deep = 3 - way * VELOCITIES[i][1]
            cot = tile_of(cot_ref, i, near)
            g_far = own_ref[2 * i + far]
            if way == 1:
                mixed = jnp.where(column >= deep, g_far, columns(cot, deep - 4))
            else:
                mixed = jnp.where(column < 4 - deep, g_far, columns(cot, 4 - deep))
            deal.put(way, 2 * i, mixed if far == 0 else own_ref[2 * i])
            deal.put(way, 2 * i + 1, mixed if far == 1 else own_ref[2 * i + 1])
    for way in (1, -1):
        near, far = (1, 0) if way == 1 else (0, 1)
        outer = 3 if way == 1 else 0
        deal.put(way, Y_CODE1, codes[near][0])
        deal.put(way, Y_CODE2, codes[near][1])
        outside = columns(codes[far][0], 3 - 2 * outer)
        deal.put(way, Y_CODE3, jnp.where(column == 3 - outer, outside, codes[near][2]))
        extra = None
        for k, i in enumerate(turned(1, -way)):
            value = columns(own_ref[2 * i + far], k - outer)
            extra = value if extra is None else jnp.where(column == k, value, extra)
        deal.put(way, Y_POP, extra)
        extra = None
        for k, i in enumerate(turned(1, way)):
            value = columns(tile_of(cot_ref, i, near), k - (1 if way == 1 else 2))
            extra = value if extra is None else jnp.where(column == k, value, extra)
        deal.put(way, Y_COT, extra)
    for t in range(2):
        for i in range(Q):
            own_cot_ref[2 * i + t] = tile_of(cot_ref, i, t)
        pack_lines(
            Deal(is_even("gx"), first_side_ref, second_side_ref),
            X_LANE * t,
            lambda i: own_ref[2 * i + t],
            lambda i: tile_of(cot_ref, i, t),
            lambda s: codes[t][s - 1],
        )


def from_y(left_ref, right_ref):
    row, lane, column, depth = iotas()
    high = lane >= LANES // 2

    def population(i, c):
        if c == 1:
            return left_ref[2 * i + 1]
        if c == 4:
            return right_ref[2 * i]
        along_y = VELOCITIES[i][1]
        left, right = left_ref[2 * i], right_ref[2 * i + 1]
        if along_y == 1 and i in turned(1, 1):
            right = columns(right_ref[Y_POP], -turned(1, 1).index(i))
        if along_y == -1 and i in turned(1, -1):
            left = columns(left_ref[Y_POP], 3 - turned(1, -1).index(i))
        return jnp.where(high, left, right)

    def cotangent(i, c):
        ref, way, place, far = (left_ref, 1, 1, 0) if c == 1 else (right_ref, -1, 2, 1)
        deep = 3 - way * VELOCITIES[i][1]
        value = columns(ref[2 * i + far], way * (4 - deep))
        if i in turned(1, way):
            extra = columns(ref[Y_COT], place - turned(1, way).index(i))
            value = jnp.where(column == place, extra, value)
        return value

    def codes(s, c):
        if c == 0:
            left, right = columns(left_ref[Y_CODE3], 3), columns(right_ref[Y_CODE3], 1)
            return jnp.where(high, left, right)
        return (left_ref if c == 1 else right_ref)[(Y_CODE1, Y_CODE2, Y_CODE3)[s - 1]]

    return population, cotangent, codes


def pack_lines(deal, first, population, cotangent, codes):
    row, lane, column, depth = iotas()

    def put(at, pop, cot, deep, way):
        if way == 1:
            mixed = jnp.where(row >= deep, pop, lines(cot, deep))
        else:
            mixed = jnp.where(row < ROWS - deep, pop, lines(cot, -deep))
        deal.put(way, first + at, mixed)

    for i in range(Q):
        pop, cot = population(i), cotangent(i)
        for way in (1, -1):
            put(i, pop, cot, 3 - way * VELOCITIES[i][0], way)
    for way in (1, -1):
        extra = None
        for k, i in enumerate(turned(0, -way)):
            value = lines(population(i), k - (3 if way == 1 else 4))
            extra = value if extra is None else jnp.where(row == k, value, extra)
        for k, i in enumerate(turned(0, way)):
            value = lines(cotangent(i), 4 + k - (5 if way == 1 else 2))
            extra = jnp.where(row == 4 + k, value, extra)
        deal.put(way, first + X_EXTRA, extra)
        put(X_CODE13, codes(1), codes(3), 3, way)


def from_x(ref, n, way):
    row, lane, column, depth = iotas()
    first = X_LANE * n

    def population(i):
        value = ref[first + i]
        if i in turned(0, -way):
            place = 3 if way == 1 else 4
            extra = lines(ref[first + X_EXTRA], place - turned(0, -way).index(i))
            value = jnp.where(row == place, extra, value)
        return value

    def cotangent(i):
        value = lines(ref[first + i], -way * (3 - way * VELOCITIES[i][0]))
        if i in turned(0, way):
            place = 5 if way == 1 else 2
            extra = lines(ref[first + X_EXTRA], place - 4 - turned(0, way).index(i))
            value = jnp.where(row == place, extra, value)
        return value

    def codes(s):
        if s == 2:
            return lines(ref[X_CODE2 + n // 2], 4 * (n % 2))
        value = ref[first + X_CODE13]
        return value if s == 1 else lines(value, -3 * way)

    return population, cotangent, codes


def pack_x(field_ref, first_y_ref, second_y_ref, early_a, early_b, first_ref, second_ref):
    row, lane, column, depth = iotas()
    deal = Deal(is_even("gx"), first_ref, second_ref, X_SIDE)
    population, cotangent, codes = from_y(*sides(first_y_ref, second_y_ref, "gy"))

    def both_codes(at, first, second):
        second = lines(second, 4)
        deal.put(1, at, jnp.where(row >= 4, first, second))
        deal.put(-1, at, jnp.where(row < 4, first, second))

    for n, c in ((2, 1), (3, 4)):
        pack_lines(
            deal,
            X_LANE * n,
            lambda i: population(i, c),
            lambda i: cotangent(i, c),
            lambda s: codes(s, c),
        )
    for n in range(Q + 1):
        value = population(n, 0) if n < Q else codes(1, 0)
        first_ref[X_RING + n - X_SIDE] = value
        second_ref[X_RING + n - X_SIDE] = value
    both_codes(X_CODE2, field_ref[4], field_ref[5])
    both_codes(X_CODE2 + 1, codes(2, 1), codes(2, 4))
    second_ref[X_TILES - X_SIDE] = jnp.zeros((ROWS, LANES), jnp.float32)


def sides(first_ref, second_ref, axis):
    even = is_even(axis)
    return Pick(even, second_ref, first_ref), Pick(even, first_ref, second_ref)


def own_rows(step=0):
    return pl.ds(ROWS + step, ROWS)


def halo_rows(step=0):
    return pl.ds({0: 2 * ROWS, -1: 2 * ROWS - 1, 1: 1}[step], ROWS)


def put_ring(ref, at, own, halo):
    ref[at, own_rows(), :] = own
    ref[at, pl.ds(0, ROWS), :] = halo
    ref[at, halo_rows(), :] = halo


def fill(from_left, own_ref, field_ref, cot_ref, from_below, pop, cot, wide, field):
    row, lane, column, depth = iotas()
    top = depth == NZ - 1
    after = row < 4

    def expand(code):
        phi = jnp.where(top, code, 0.0)
        for step in (1, 2, 4, 8, 16):
            phi = phi + pltpu.roll(phi, LANES - step, 1)
        return jnp.where(top, 0.0, code), phi

    for c in range(5):
        t = c - 2
        if t in (0, 1):
            own = (
                lambda i: own_ref[2 * i + t],
                lambda i: cot_ref[2 * i + t],
                lambda s: field_ref[2 * s + t],
            )
            code_phi = field_ref[2 + t], field_ref[2 * OWN_PHI + t]
        else:
            own = tuple(functools.partial(lambda g, n: g(n, c), get) for get in from_left)
            code_phi = expand(own[2](1))
        if c:
            n = (None, 2, 0, 1, 3)[c]
            below, above = from_x(from_below[0], n, 1), from_x(from_below[1], n, -1)
        else:
            below, above = (
                (lambda i, ref=ref: ref[X_RING + i], None, lambda s, ref=ref: ref[X_RING + Q])
                for ref in from_below
            )
        parts = (expand(below[2](1)), code_phi, expand(above[2](1)))
        for i in range(Q):
            for r, side in enumerate((below, own, above)):
                pop[5 * i + c, pl.ds(ROWS * (r + 1), ROWS), :] = side[0](i)
        for n in range(2):
            for r in range(3):
                wide[n, c, r] = parts[r][n]
        if c:
            for i in range(Q):
                halo = jnp.where(after, above[1](i), below[1](i))
                put_ring(cot, 4 * i + c - 1, own[1](i), halo)
            for n, place in ((0, 1), (1, 0)):
                field[place, c - 1, 0] = parts[1][n]
                field[place, c - 1, 1] = jnp.where(after, parts[2][n], parts[0][n])
            for s in (2, 3):
                field[s, c - 1, 0] = own[2](s)
                field[s, c - 1, 1] = jnp.where(after, above[2](s), below[2](s))


def steps_kernel(
    sizes,
    state_ref,
    cot_ref,
    own_ref,
    own_field_ref,
    names_ref,
    first_y_ref,
    second_y_ref,
    first_side_ref,
    second_side_ref,
    first_x_ref,
    second_x_ref,
    adjoint_ref,
    panel_ref,
    pop_a,
    pop_b,
    ring_a,
    ring_b,
    wide,
    field,
    saved,
    mom,
    grad,
):
    size_x, size_y = sizes
    fill(
        from_y(*sides(first_y_ref, second_y_ref, "gy")),
        own_ref,
        own_field_ref,
        cot_ref,
        sides(
            Joined(first_side_ref, first_x_ref, X_SIDE),
            Joined(second_side_ref, second_x_ref, X_SIDE),
            "gx",
        ),
        pop_a,
        ring_a,
        wide,
        field,
    )

    at_x, at_y = lax.axis_index("gx"), lax.axis_index("gy")
    edges = (
        jnp.where(at_x == 0, 1, 0),
        jnp.where(at_x == size_x - 1, 1, 0),
        jnp.where(at_y == 0, 1, 0),
        jnp.where(at_y == size_y - 1, 1, 0),
    )
    row, lane, column, depth = iotas()
    after = row < 4

    def masks_of(tile, first, r):
        return wall_masks(r == 0, tile == first, tile == first + 1, edges)

    def neighbours(tile, tiles):
        if isinstance(tile, int):
            return {0: tile, -1: (tile - 1) % tiles, 1: (tile + 1) % tiles}
        return {0: tile, -1: lax.rem(tile + tiles - 1, tiles), 1: lax.rem(tile + 1, tiles)}

    def from_wide(ref, tile, r):
        step = neighbours(tile, 5)

        def load(i, tile_step, row_step, move):
            at = 5 * i + step[tile_step]
            before, own, behind = (ref[at, pl.ds(ROWS * n + row_step, ROWS), :] for n in (1, 2, 3))
            return (own, jnp.where(after, behind, before), before, behind)[r]

        return load

    def from_ring(ref, tile, tiles, r):
        step = neighbours(tile, tiles)

        def load(i, tile_step, row_step, move):
            rows = own_rows(row_step) if r == 0 else halo_rows(row_step)
            return ref[tiles * i + step[tile_step], rows, :]

        return load

    def from_outer(ref, r):
        def load(i, tile_step, row_step, move):
            rows = own_rows(row_step) if r == 0 else halo_rows(row_step)
            if tile_step:
                return ref[4 * i + (2 if tile_step < 0 else 1), rows, :]
            cut = {0: 2, 1: 1, -1: 3}[move]
            return jnp.where(column < cut, ref[4 * i + 3, rows, :], ref[4 * i, rows, :])

        return load

    def note(s, tile, r, parts):
        for n, value in enumerate(parts[2:4] + tuple(parts[4])):
            mom[s - 1, n, tile, r] = value

    def first_step(tile, carry):
        place = lax.rem(tile + 4, 5)
        halo = []
        for r in (2, 0, 3):
            f = stream_tile(from_wide(pop_a, tile, r), 1, masks_of(tile, 2, r), lane)
            parts = moments(f)
            if r == 0:
                note(1, place, 0, parts)
                for i in range(Q):
                    saved[0, i, place] = f[i]
            else:
                halo.append(parts[2:4] + tuple(parts[4]))
            at = {2: 0, 0: 1, 3: 2}[r]
            g = collide(f, wide[0, tile, at], wide[1, tile, at], parts)
            for i in range(Q):
                pop_b[5 * i + tile, pl.ds(ROWS * (at + 1), ROWS), :] = g[i]
        for n in range(5):
            mom[0, n, place, 1] = jnp.where(after, halo[1][n], halo[0][n])
        return carry

    lax.fori_loop(0, 5, first_step, 0)

    def second_step(tile, carry):
        out = []
        for r in range(2):
            f = stream_tile(from_wide(pop_b, tile + 1, r), 1, masks_of(tile, 1, r), lane)
            parts = moments(f)
            note(2, tile, r, parts)
            if r == 0:
                for i in range(Q):
                    saved[1, i, tile] = f[i]
            out.append(collide(f, field[2, tile, r], field[0, tile, r], parts))
        for i in range(Q):
            put_ring(ring_b, 4 * i + tile, out[0][i], out[1][i])
        return carry

    lax.fori_loop(0, 4, second_step, 0)

    def third_step(tile, carry):
        for r in range(2):
            f = stream_tile(from_ring(ring_b, tile, 4, r), 1, masks_of(tile, 1, r), lane)
            note(3, tile, r, moments(f))
            if r == 0:
                for i in range(Q):
                    saved[2, i, tile] = f[i]
        return carry

    lax.fori_loop(0, 4, third_step, 0)

    def back_tile(load, s, tile, r, own):
        b = stream_tile(load, -1, masks_of(4 if tile is None else tile, 1, r), lane)

        def read(get):
            return jnp.where(column < 2, get(3), get(0)) if tile is None else get(tile)

        rho, rinv, *u = [read(lambda at: mom[s - 1, n, at, r]) for n in range(5)]
        kind, phi = read(lambda at: field[s, at, r]), read(lambda at: field[0, at, r])
        state = [saved[s - 1, i, tile] for i in range(Q)] if own else None
        back, term = collide_back(b, kind, phi, rho, rinv, u, state)
        if own:
            grad[tile] = term if s == 3 else grad[tile] + term
        return back

    def last_step(tile, carry):
        out = [back_tile(from_ring(ring_a, tile, 4, r), 3, tile, r, r == 0) for r in range(2)]
        for i in range(Q):
            put_ring(ring_b, 4 * i + tile, out[0][i], out[1][i])
        return carry

    lax.fori_loop(0, 4, last_step, 0)

    for k, tile in enumerate((1, 2, None)):
        out = []
        for r in range(2):
            load = from_outer(ring_b, r) if tile is None else from_ring(ring_b, tile, 4, r)
            out.append(back_tile(load, 2, tile, r, r == 0 and tile is not None))
        for i in range(Q):
            put_ring(ring_a, 3 * i + k, out[0][i], out[1][i])

    for k, tile in enumerate((1, 2, None)):
        out = []
        for r in range(2):
            load = from_ring(ring_a, k, 3, r)
            out.append(back_tile(load, 1, tile, r, r == 0 and tile is not None))
        for i in range(Q):
            put_ring(ring_b, 3 * i + k, out[0][i], out[1][i])

    panel = lax.broadcasted_iota(jnp.int32, panel_ref.shape, 1)
    sums = jnp.zeros(panel_ref.shape, jnp.float32)
    for t in range(2):
        b = stream_tile(from_ring(ring_b, t, 3, 0), -1, masks_of(t, 0, 0), lane)
        f = [state_ref[2 * i + t] for i in range(Q)]
        kind, phi = own_field_ref[t], own_field_ref[2 * OWN_PHI + t]
        _, _, rho, rinv, u = moments(f)
        back, term = collide_back(b, kind, phi, rho, rinv, u, f)
        for i in range(Q):
            adjoint_ref[i, :, pl.ds(t * LANES, LANES)] = back[i]
        term = term + grad[t + 1]
        for part in range(2):
            amount = jnp.sum(jnp.where((row < 4) == (part == 0), term, 0.0))
            name = names_ref[t, 4 * part : 4 * part + 1, 0:1]
            sums = sums + jnp.where(panel == name, amount, 0.0)
    panel_ref[...] = sums


def add_panels(parts_ref, out_ref):
    out_ref[...] = jnp.sum(parts_ref[...], axis=0)


VMEM = pl.BlockSpec(memory_space=pltpu.VMEM)
HBM = pl.BlockSpec(memory_space=pltpu.HBM)
ANY = pl.BlockSpec(memory_space=pl.ANY)


def shape_of(*dims):
    return jax.ShapeDtypeStruct(dims, jnp.float32)


def tiles_of(count):
    return shape_of(count, ROWS, LANES)


def on_device(sizes, checkpoint, cotangent, cell_codes, porosity, baffle_index):
    size_x, size_y = sizes
    panels = porosity.shape[0]
    devices = size_x * size_y

    def call(kernel, out_shape, in_specs, scratch=(), name=None):
        return pl.pallas_call(
            kernel,
            out_shape=out_shape,
            in_specs=in_specs,
            out_specs=jax.tree.map(lambda _: VMEM, out_shape),
            scratch_shapes=scratch,
            compiler_params=pltpu.CompilerParams(vmem_limit_bytes=32 * 1024 * 1024),
            name=name,
        )

    def swap(value, axis, size):
        return lax.ppermute(value, axis, [(i, i ^ 1) for i in range(size) if i ^ 1 < size])

    def swap_between(value, axis, size):
        pairs = [(i, i + 1) for i in range(1, size - 1, 2)]
        return lax.ppermute(value, axis, pairs + [(j, i) for i, j in pairs])

    arguments = [
        pltpu.with_memory_space_constraint(value, pltpu.HBM)
        for value in (checkpoint, cotangent, cell_codes, baffle_index, porosity)
    ]
    first_y, second_y, first_side, second_side, own, state, cot, field, names = call(
        pack_own,
        (tiles_of(Y_TILES),) * 2
        + (tiles_of(X_SIDE),) * 2
        + (tiles_of(2 * Q),) * 3
        + (tiles_of(2 * OWN_PHI + 2), jax.ShapeDtypeStruct((2, ROWS, LANES), jnp.int32)),
        [HBM] * 5,
        [
            pltpu.VMEM((Q, ROWS, 2 * LANES), jnp.float32),
            pltpu.VMEM((Q, ROWS, 2 * LANES), jnp.float32),
            pltpu.VMEM((STEPS, ROWS, 2 * LANES), jnp.int32),
            pltpu.SMEM(baffle_index.shape, jnp.int32),
            pltpu.SMEM(porosity.shape, jnp.float32),
            pltpu.SemaphoreType.DMA((5,)),
        ],
        name="pack_own",
    )(*arguments)
    second_y = swap_between(second_y, "gy", size_y)
    first_y = swap(first_y, "gy", size_y)
    second_side = swap_between(second_side, "gx", size_x)
    first_side = swap(first_side, "gx", size_x)
    rest = X_TILES - X_SIDE
    first_x, second_x = call(
        pack_x,
        (tiles_of(rest), tiles_of(rest + SPARE)),
        [VMEM] * 3 + [ANY] * 2,
        name="pack_x",
    )(field, first_y, second_y, first_side, second_side)
    second_x = swap_between(second_x, "gx", size_x)
    first_x = swap(first_x, "gx", size_x)

    adjoint, sums = call(
        functools.partial(steps_kernel, sizes),
        (shape_of(Q, ROWS, 2 * LANES), shape_of(devices, panels)),
        [VMEM] * 11,
        [
            pltpu.VMEM((5 * Q, 5 * ROWS, LANES), jnp.float32),
            pltpu.VMEM((5 * Q, 5 * ROWS, LANES), jnp.float32),
            pltpu.VMEM((4 * Q, 3 * ROWS, LANES), jnp.float32),
            pltpu.VMEM((4 * Q, 3 * ROWS, LANES), jnp.float32),
            pltpu.VMEM((2, 5, 3, ROWS, LANES), jnp.float32),
            pltpu.VMEM((4, 4, 2, ROWS, LANES), jnp.float32),
            pltpu.VMEM((3, Q, 5, ROWS, LANES), jnp.float32),
            pltpu.VMEM((3, 5, 5, 2, ROWS, LANES), jnp.float32),
            pltpu.VMEM((4, ROWS, LANES), jnp.float32),
        ],
        name="steps",
    )(state, cot, own, field, names, first_y, second_y, first_side, second_side, first_x, second_x)
    gathered = lax.all_to_all(sums, ("gx", "gy"), 0, 0, tiled=True)
    totals = call(add_panels, shape_of(1, panels), [VMEM], name="add_panels")(
        gathered.reshape(devices, 1, panels)
    )
    return adjoint, totals.reshape(panels)


def solution(mesh):
    sizes = (mesh.shape["gx"], mesh.shape["gy"])
    in_specs = (P(None, "gx", "gy"), P(None, "gx", "gy"), P(None, "gx", "gy"), P(), P("gx", "gy"))
    out_specs = (P(None, "gx", "gy"), P())
    return jax.shard_map(
        functools.partial(on_device, sizes),
        mesh=mesh,
        in_specs=in_specs,
        out_specs=out_specs,
        check_vma=False,
    )
```

```python
import functools

import jax
import jax.numpy as jnp
import numpy as np
from jax import lax
from jax.experimental import pallas as pl
from jax.experimental.pallas import tpu as pltpu
from jax.sharding import PartitionSpec as P

Q = 19
STEPS = 4
NZ = 32
ROWS = 8
LANES = 128
OMEGA = 1.6
ACCEL = (0.002, 0.0, -0.003)
SHIFT = tuple(a / OMEGA for a in ACCEL)

VELOCITIES = [
    (0, 0, 0),
    (1, 0, 0),
    (-1, 0, 0),
    (0, 1, 0),
    (0, -1, 0),
    (0, 0, 1),
    (0, 0, -1),
    (1, 1, 0),
    (-1, -1, 0),
    (1, -1, 0),
    (-1, 1, 0),
    (1, 0, 1),
    (-1, 0, -1),
    (1, 0, -1),
    (-1, 0, 1),
    (0, 1, 1),
    (0, -1, -1),
    (0, 1, -1),
    (0, -1, 1),
]
OPPOSITE = [0, 2, 1, 4, 3, 6, 5, 8, 7, 10, 9, 12, 11, 14, 13, 16, 15, 18, 17]
PAIRS = [(i, i + 1) for i in range(1, Q, 2)]
W_REST, W_AXIS, W_DIAG = 1.0 / 3.0, 1.0 / 18.0, 1.0 / 36.0

Y_CODE1, Y_CODE2, Y_CODE3, Y_POP, Y_COT = 38, 39, 40, 41, 42
Y_TILES = 43
X_EXTRA, X_CODE13 = 19, 20
X_LANE = 21
X_RING = 4 * X_LANE
X_CODE2 = X_RING + Q + 1
X_TILES = X_CODE2 + 2
X_SIDE = 2 * X_LANE
EMPTY = 25
FREE = NZ - EMPTY
WEIGHTS = [W_REST] + [W_AXIS] * 6 + [W_DIAG] * 12
LEVEL = [i for i, v in enumerate(VELOCITIES) if v[2] < 1]
OWN_PHI = 4


def turned(axis, outward):
    return [i for i, v in enumerate(VELOCITIES) if v[axis] == outward and sum(map(abs, v)) == 2]


def total(values):
    values = list(values)
    while len(values) > 1:
        values = [a + b for a, b in zip(values[::2], values[1::2])] + (
            [values[-1]] if len(values) % 2 else []
        )
    return values[0]


def along(vector, three):
    terms = None
    for c, value in zip(vector, three):
        if c == 0:
            continue
        if terms is None:
            terms = value if c > 0 else -value
        else:
            terms = terms + value if c > 0 else terms - value
    return terms


def moments(f):
    plus = {i: f[i] + f[o] for i, o in PAIRS}
    minus = {i: f[i] - f[o] for i, o in PAIRS}
    rho = total([f[0]] + [plus[i] for i, _ in PAIRS])
    rinv = 1.0 / rho
    u = []
    for axis in range(3):
        terms = [
            minus[i] if VELOCITIES[i][axis] > 0 else -minus[i]
            for i, _ in PAIRS
            if VELOCITIES[i][axis] != 0
        ]
        u.append(total(terms) * rinv + SHIFT[axis])
    return plus, minus, rho, rinv, u


def coefficients(kind, phi, rinv):
    baffle = kind == 3.0
    gas = kind == 0.0
    even = jnp.where(gas, 0.0, jnp.where(baffle, 0.5 - 0.5 * OMEGA * phi, 0.5 * (1.0 - OMEGA)))
    odd = jnp.where(
        gas, 0.0, jnp.where(baffle, (1.0 - 0.5 * OMEGA) * phi - 0.5, 0.5 * (1.0 - OMEGA))
    )
    slope = jnp.where(
        baffle,
        OMEGA * phi,
        jnp.where(kind == 1.0, OMEGA, jnp.where(kind == 2.0, OMEGA * rinv, 0.0)),
    )
    return even, odd, slope


def collide(f, kind, phi, parts):
    plus, minus, rho, rinv, u = parts
    even, odd, slope = coefficients(kind, phi, rinv)
    scale = slope * rho
    rest = 1.0 - 1.5 * (u[0] * u[0] + u[1] * u[1] + u[2] * u[2])
    base = scale * rest + jnp.where(kind == 0.0, 1.0, 0.0)
    out = [None] * Q
    out[0] = 2.0 * even * f[0] + W_REST * base
    for weight, pairs in ((W_AXIS, PAIRS[:3]), (W_DIAG, PAIRS[3:])):
        flat = weight * base
        three = (3.0 * weight) * scale
        for i, o in pairs:
            cu = along(VELOCITIES[i], u)
            lin = three * cu
            ev = even * plus[i] + (flat + 1.5 * lin * cu)
            od = odd * minus[i] + lin
            out[i] = ev + od
            out[o] = ev - od
    return out


def collide_back(b, kind, phi, rho, rinv, u, state=None):
    even, odd, slope = coefficients(kind, phi, rinv)
    plus = {i: b[i] + b[o] for i, o in PAIRS}
    minus = {i: b[i] - b[o] for i, o in PAIRS}
    rest = 1.0 - 1.5 * (u[0] * u[0] + u[1] * u[1] + u[2] * u[2])
    u_half = [1.5 * c for c in u]
    weighted = W_REST * b[0]
    energy = 0.0
    vector = [0.0, 0.0, 0.0]
    for weight, pairs in ((W_AXIS, PAIRS[:3]), (W_DIAG, PAIRS[3:])):
        weighted = weighted + weight * total([plus[i] for i, _ in pairs])
        energies, parts = [], ([], [], [])
        for i, _ in pairs:
            cu = along(VELOCITIES[i], u)
            half = along(VELOCITIES[i], u_half) * plus[i]
            first = minus[i] + half
            energies.append(cu * first)
            second = first + half
            for axis in range(3):
                c = VELOCITIES[i][axis]
                if c:
                    parts[axis].append(second if c > 0 else -second)
        energy = energy + (3.0 * weight) * total(energies)
        vector = [vector[k] + (3.0 * weight) * total(parts[k]) for k in range(3)]
    energy = energy + rest * weighted
    vector = [vector[k] - (3.0 * weighted) * u[k] for k in range(3)]
    push = [slope * v for v in vector]
    inner = total([push[k] * (u[k] - SHIFT[k]) for k in range(3)])
    shared = jnp.where(kind == 2.0, 0.0, slope) * energy - inner
    out = [None] * Q
    out[0] = 2.0 * even * b[0] + shared
    for i, o in PAIRS:
        ev = even * plus[i] + shared
        od = odd * minus[i] + along(VELOCITIES[i], push)
        out[i] = ev + od
        out[o] = ev - od
    if state is None:
        return out, None
    evens = total([plus[i] * (state[i] + state[o]) for i, o in PAIRS])
    odds = total([minus[i] * (state[i] - state[o]) for i, o in PAIRS])
    term = (
        -OMEGA * (b[0] * state[0] + 0.5 * evens)
        + (1.0 - 0.5 * OMEGA) * odds
        + OMEGA * rho * energy
    )
    return out, jnp.where(kind == 3.0, term, 0.0)


def wall_masks(sign_rows, own_low, own_high, edges):
    lane = lax.broadcasted_iota(jnp.int32, (ROWS, LANES), 1)
    row = lax.broadcasted_iota(jnp.int32, (ROWS, LANES), 0)
    x_low, x_high, y_low, y_high = edges
    depth = lane % NZ
    masks = {}
    masks[2, 1] = depth == 0
    masks[2, -1] = depth == NZ - 1
    masks[1, 1] = lane < jnp.where(own_low, y_low * NZ, 0)
    masks[1, -1] = lane >= jnp.where(own_high, LANES - y_high * NZ, LANES)
    if sign_rows:
        masks[0, 1] = row < x_low
        masks[0, -1] = row >= ROWS - x_high
    return masks


def stream_tile(load, sign, masks, lane):
    cross_low, cross_high = lane >= LANES - NZ, lane < NZ
    combined = {}
    out = []
    for i, vector in enumerate(VELOCITIES):
        v = tuple(sign * c for c in vector)
        value = load(i, 0, -v[0], v[1])
        if v[1] == 1:
            value = jnp.where(cross_low, load(i, -1, -v[0], 1), value)
        elif v[1] == -1:
            value = jnp.where(cross_high, load(i, 1, -v[0], -1), value)
        amount = (v[1] * NZ + v[2]) % LANES
        if amount:
            value = pltpu.roll(value, amount, 1)
        outside = None
        if v not in combined:
            for axis in range(3):
                if v[axis] and (axis, v[axis]) in masks:
                    wall = masks[axis, v[axis]]
                    outside = wall if outside is None else outside | wall
            combined[v] = outside
        outside = combined[v]
        if outside is not None:
            value = jnp.where(outside, load(OPPOSITE[i], 0, 0, 0), value)
        out.append(value)
    return out


def iotas():
    row = lax.broadcasted_iota(jnp.int32, (ROWS, LANES), 0)
    lane = lax.broadcasted_iota(jnp.int32, (ROWS, LANES), 1)
    return row, lane, lane // NZ, lane % NZ


def columns(value, count):
    amount = (count * NZ) % LANES
    return pltpu.roll(value, amount, 1) if amount else value


def lines(value, count):
    amount = count % ROWS
    return pltpu.roll(value, amount, 0) if amount else value


class Layout:
    def __init__(self, count, guests, fills):
        self.fills = fills
        hosts = [at for at in fills if at not in guests]
        self.hosts = {at: hosts[4 * n : 4 * n + 4] for n, at in enumerate(guests)}
        self.guests = guests
        kept = [at for at in range(count) if at not in guests]
        self.place = {at: n for n, at in enumerate(kept)}
        self.size = len(kept)


class Packing:
    def __init__(self, ref, layout):
        self.ref, self.layout, self.held = ref, layout, {}

    def __setitem__(self, at, value):
        if at in self.layout.guests:
            self.held[at] = value
        else:
            self.ref[self.layout.place[at]] = value

    def finish(self):
        row, lane, column, depth = iotas()
        spare = depth >= EMPTY
        for at, value in self.held.items():
            for k, host in enumerate(self.layout.hosts[at]):
                place = self.layout.place[host]
                source = jnp.where(spare, NZ * k + FREE * column + depth - EMPTY, 0)
                moved = jnp.take_along_axis(value, source, axis=1, mode="promise_in_bounds")
                self.ref[place] = jnp.where(spare, moved, self.ref[place])
        for place in range(self.layout.size, self.ref.shape[0]):
            self.ref[place] = jnp.zeros((ROWS, LANES), jnp.float32)


class Unpacking:
    def __init__(self, source, layout):
        self.source, self.layout = source, layout

    def __getitem__(self, at):
        row, lane, column, depth = iotas()
        layout = self.layout
        if at in layout.guests:
            value = None
            lanes = jnp.where(depth < EMPTY, NZ * (depth // FREE) + EMPTY + depth % FREE, 0)
            for k, host in enumerate(layout.hosts[at]):
                tile = self.source[layout.place[host]]
                moved = jnp.take_along_axis(tile, lanes, axis=1, mode="promise_in_bounds")
                value = moved if value is None else jnp.where(column == k, moved, value)
        else:
            value = self.source[layout.place[at]]
        if at in layout.fills:
            value = jnp.where(depth >= EMPTY, layout.fills[at], value)
        return value


def layouts():
    y_fills = {2 * i + t: WEIGHTS[i] for i in LEVEL for t in range(2)}
    y_fills.update({Y_POP: W_DIAG, Y_CODE2: 0.0})
    x_fills = {X_LANE * n + i: WEIGHTS[i] for n in range(4) for i in LEVEL}
    side = {at: fill for at, fill in x_fills.items() if at < X_SIDE}
    rest = {at - X_SIDE: fill for at, fill in x_fills.items() if at >= X_SIDE}
    rest.update({X_CODE2 - X_SIDE: 0.0, X_CODE2 + 1 - X_SIDE: 0.0})
    rest.update({X_RING - X_SIDE + i: WEIGHTS[i] for i in range(Q)})
    ring = [X_RING - X_SIDE + i for i in range(9)]
    return (
        Layout(Y_TILES, [2 * i for i in LEVEL[:6]], y_fills),
        Layout(X_SIDE, LEVEL[:5], side),
        Layout(X_TILES - X_SIDE, ring, rest),
    )


class Pick:
    def __init__(self, flag, first, second):
        self.flag, self.first, self.second = flag, first, second

    def __getitem__(self, at):
        return jnp.where(self.flag, self.first[at], self.second[at])


class Deal:
    def __init__(self, even, first, second, layout, skip=0):
        self.even, self.skip, self.held = even, skip, {}
        self.first, self.second = Packing(first, layout), Packing(second, layout)

    def put(self, way, at, value):
        if (-way, at) not in self.held:
            self.held[way, at] = value
            return
        other = self.held.pop((-way, at))
        up, down = (value, other) if way == 1 else (other, value)
        self.first[at - self.skip] = jnp.where(self.even, up, down)
        self.second[at - self.skip] = jnp.where(self.even, down, up)

    def put_both(self, at, value):
        self.first[at - self.skip] = value
        self.second[at - self.skip] = value

    def finish(self):
        self.first.finish()
        self.second.finish()


class Joined:
    def __init__(self, first, second, cut):
        self.first, self.second, self.cut = first, second, cut

    def __getitem__(self, at):
        return self.first[at] if at < self.cut else self.second[at - self.cut]


def is_even(axis):
    return lax.rem(lax.axis_index(axis), 2) == 0


def pack_own(
    f_hbm,
    cot_hbm,
    codes_hbm,
    panels_hbm,
    porosity_hbm,
    first_ref,
    second_ref,
    first_side_ref,
    second_side_ref,
    own_ref,
    state_ref,
    own_cot_ref,
    field_ref,
    names_ref,
    f_ref,
    cot_ref,
    codes_ref,
    panels_ref,
    porosity_ref,
    sems,
):
    pieces = (
        (panels_hbm, panels_ref),
        (porosity_hbm, porosity_ref),
        (f_hbm, f_ref),
        (codes_hbm, codes_ref),
        (cot_hbm, cot_ref),
    )
    copies = [
        pltpu.make_async_copy(source, target, sems.at[n])
        for n, (source, target) in enumerate(pieces)
    ]
    for copy in copies:
        copy.start()
    for copy in copies[:4]:
        copy.wait()
    y_layout, side_layout, _ = layouts()
    deal = Deal(is_even("gy"), first_ref, second_ref, y_layout)
    side = Deal(is_even("gx"), first_side_ref, second_side_ref, side_layout)
    row, lane, column, depth = iotas()
    top = depth == NZ - 1

    def tile_of(ref, i, t):
        return ref[i, :, pl.ds(t * LANES, LANES)]

    codes, phis = [], []
    for t in range(2):
        names = panels_ref[0, t * LANES], panels_ref[4, t * LANES]
        phi = jnp.where(row < 4, porosity_ref[names[0]], porosity_ref[names[1]])
        names_ref[t] = jnp.where(row < 4, names[0], names[1])
        kinds = [tile_of(codes_ref, s, t).astype(jnp.float32) for s in range(STEPS)]
        f = [tile_of(f_ref, i, t) for i in range(Q)]
        g = collide(f, kinds[0], phi, moments(f))
        for i in range(Q):
            own_ref[2 * i + t] = g[i]
            state_ref[2 * i + t] = f[i]
        for s in range(STEPS):
            field_ref[2 * s + t] = kinds[s]
        field_ref[2 * OWN_PHI + t] = phi
        codes.append([jnp.where(top, phi, kinds[1]), kinds[2], kinds[3]])
    copies[4].wait()
    for i in range(Q):
        for way in (1, -1):
            near, far = (1, 0) if way == 1 else (0, 1)
            deep = 3 - way * VELOCITIES[i][1]
            cot = tile_of(cot_ref, i, near)
            g_far = own_ref[2 * i + far]
            if way == 1:
                mixed = jnp.where(column >= deep, g_far, columns(cot, deep - 4))
            else:
                mixed = jnp.where(column < 4 - deep, g_far, columns(cot, 4 - deep))
            deal.put(way, 2 * i, mixed if far == 0 else own_ref[2 * i])
            deal.put(way, 2 * i + 1, mixed if far == 1 else own_ref[2 * i + 1])
    for way in (1, -1):
        near, far = (1, 0) if way == 1 else (0, 1)
        outer = 3 if way == 1 else 0
        deal.put(way, Y_CODE1, codes[near][0])
        deal.put(way, Y_CODE2, codes[near][1])
        outside = columns(codes[far][0], 3 - 2 * outer)
        deal.put(way, Y_CODE3, jnp.where(column == 3 - outer, outside, codes[near][2]))
        extra = None
        for k, i in enumerate(turned(1, -way)):
            value = columns(own_ref[2 * i + far], k - outer)
            extra = value if extra is None else jnp.where(column == k, value, extra)
        deal.put(way, Y_POP, extra)
        extra = None
        for k, i in enumerate(turned(1, way)):
            value = columns(tile_of(cot_ref, i, near), k - (1 if way == 1 else 2))
            extra = value if extra is None else jnp.where(column == k, value, extra)
        deal.put(way, Y_COT, extra)
    deal.finish()
    for t in range(2):
        for i in range(Q):
            own_cot_ref[2 * i + t] = tile_of(cot_ref, i, t)
        pack_lines(
            side,
            X_LANE * t,
            lambda i: own_ref[2 * i + t],
            lambda i: tile_of(cot_ref, i, t),
            lambda s: codes[t][s - 1],
        )
    side.finish()


def from_y(left_ref, right_ref):
    row, lane, column, depth = iotas()
    high = lane >= LANES // 2

    def population(i, c):
        if c == 1:
            return left_ref[2 * i + 1]
        if c == 4:
            return right_ref[2 * i]
        along_y = VELOCITIES[i][1]
        left, right = left_ref[2 * i], right_ref[2 * i + 1]
        if along_y == 1 and i in turned(1, 1):
            right = columns(right_ref[Y_POP], -turned(1, 1).index(i))
        if along_y == -1 and i in turned(1, -1):
            left = columns(left_ref[Y_POP], 3 - turned(1, -1).index(i))
        return jnp.where(high, left, right)

    def cotangent(i, c):
        ref, way, place, far = (left_ref, 1, 1, 0) if c == 1 else (right_ref, -1, 2, 1)
        deep = 3 - way * VELOCITIES[i][1]
        value = columns(ref[2 * i + far], way * (4 - deep))
        if i in turned(1, way):
            extra = columns(ref[Y_COT], place - turned(1, way).index(i))
            value = jnp.where(column == place, extra, value)
        return value

    def codes(s, c):
        if c == 0:
            left, right = columns(left_ref[Y_CODE3], 3), columns(right_ref[Y_CODE3], 1)
            return jnp.where(high, left, right)
        return (left_ref if c == 1 else right_ref)[(Y_CODE1, Y_CODE2, Y_CODE3)[s - 1]]

    return population, cotangent, codes


def pack_lines(deal, first, population, cotangent, codes):
    row, lane, column, depth = iotas()

    def put(at, pop, cot, deep, way):
        if way == 1:
            mixed = jnp.where(row >= deep, pop, lines(cot, deep))
        else:
            mixed = jnp.where(row < ROWS - deep, pop, lines(cot, -deep))
        deal.put(way, first + at, mixed)

    for i in range(Q):
        pop, cot = population(i), cotangent(i)
        for way in (1, -1):
            put(i, pop, cot, 3 - way * VELOCITIES[i][0], way)
    for way in (1, -1):
        extra = None
        for k, i in enumerate(turned(0, -way)):
            value = lines(population(i), k - (3 if way == 1 else 4))
            extra = value if extra is None else jnp.where(row == k, value, extra)
        for k, i in enumerate(turned(0, way)):
            value = lines(cotangent(i), 4 + k - (5 if way == 1 else 2))
            extra = jnp.where(row == 4 + k, value, extra)
        deal.put(way, first + X_EXTRA, extra)
        put(X_CODE13, codes(1), codes(3), 3, way)


def from_x(ref, n, way):
    row, lane, column, depth = iotas()
    first = X_LANE * n

    def population(i):
        value = ref[first + i]
        if i in turned(0, -way):
            place = 3 if way == 1 else 4
            extra = lines(ref[first + X_EXTRA], place - turned(0, -way).index(i))
            value = jnp.where(row == place, extra, value)
        return value

    def cotangent(i):
        value = lines(ref[first + i], -way * (3 - way * VELOCITIES[i][0]))
        if i in turned(0, way):
            place = 5 if way == 1 else 2
            extra = lines(ref[first + X_EXTRA], place - 4 - turned(0, way).index(i))
            value = jnp.where(row == place, extra, value)
        return value

    def codes(s):
        if s == 2:
            return lines(ref[X_CODE2 + n // 2], 4 * (n % 2))
        value = ref[first + X_CODE13]
        return value if s == 1 else lines(value, -3 * way)

    return population, cotangent, codes


def pack_x(field_ref, first_y_ref, second_y_ref, early_a, early_b, first_ref, second_ref):
    row, lane, column, depth = iotas()
    y_layout, _, layout = layouts()
    deal = Deal(is_even("gx"), first_ref, second_ref, layout, X_SIDE)
    population, cotangent, codes = from_y(*sides(first_y_ref, second_y_ref, "gy", y_layout))

    def both_codes(at, first, second):
        second = lines(second, 4)
        deal.put(1, at, jnp.where(row >= 4, first, second))
        deal.put(-1, at, jnp.where(row < 4, first, second))

    for n, c in ((2, 1), (3, 4)):
        pack_lines(
            deal,
            X_LANE * n,
            lambda i: population(i, c),
            lambda i: cotangent(i, c),
            lambda s: codes(s, c),
        )
    for n in range(Q + 1):
        value = population(n, 0) if n < Q else codes(1, 0)
        deal.put_both(X_RING + n, value)
    both_codes(X_CODE2, field_ref[4], field_ref[5])
    both_codes(X_CODE2 + 1, codes(2, 1), codes(2, 4))
    deal.finish()


def sides(first_ref, second_ref, axis, layout):
    even = is_even(axis)
    picks = Pick(even, second_ref, first_ref), Pick(even, first_ref, second_ref)
    return [Unpacking(pick, layout) for pick in picks]


def own_rows(step=0):
    return pl.ds(ROWS + step, ROWS)


def halo_rows(step=0):
    return pl.ds({0: 2 * ROWS, -1: 2 * ROWS - 1, 1: 1}[step], ROWS)


def put_ring(ref, at, own, halo):
    ref[at, own_rows(), :] = own
    ref[at, pl.ds(0, ROWS), :] = halo
    ref[at, halo_rows(), :] = halo


def fill(from_left, own_ref, field_ref, cot_ref, from_below, pop, cot, wide, field):
    row, lane, column, depth = iotas()
    top = depth == NZ - 1
    after = row < 4

    def expand(code):
        phi = jnp.where(top, code, 0.0)
        for step in (1, 2, 4, 8, 16):
            phi = phi + pltpu.roll(phi, LANES - step, 1)
        return jnp.where(top, 0.0, code), phi

    for c in range(5):
        t = c - 2
        if t in (0, 1):
            own = (
                lambda i: own_ref[2 * i + t],
                lambda i: cot_ref[2 * i + t],
                lambda s: field_ref[2 * s + t],
            )
            code_phi = field_ref[2 + t], field_ref[2 * OWN_PHI + t]
        else:
            own = tuple(functools.partial(lambda g, n: g(n, c), get) for get in from_left)
            code_phi = expand(own[2](1))
        if c:
            n = (None, 2, 0, 1, 3)[c]
            below, above = from_x(from_below[0], n, 1), from_x(from_below[1], n, -1)
        else:
            below, above = (
                (lambda i, ref=ref: ref[X_RING + i], None, lambda s, ref=ref: ref[X_RING + Q])
                for ref in from_below
            )
        parts = (expand(below[2](1)), code_phi, expand(above[2](1)))
        for i in range(Q):
            for r, side in enumerate((below, own, above)):
                pop[5 * i + c, pl.ds(ROWS * (r + 1), ROWS), :] = side[0](i)
        for n in range(2):
            for r in range(3):
                wide[n, c, r] = parts[r][n]
        if c:
            for i in range(Q):
                halo = jnp.where(after, above[1](i), below[1](i))
                put_ring(cot, 4 * i + c - 1, own[1](i), halo)
            for n, place in ((0, 1), (1, 0)):
                field[place, c - 1, 0] = parts[1][n]
                field[place, c - 1, 1] = jnp.where(after, parts[2][n], parts[0][n])
            for s in (2, 3):
                field[s, c - 1, 0] = own[2](s)
                field[s, c - 1, 1] = jnp.where(after, above[2](s), below[2](s))


def steps_kernel(
    sizes,
    state_ref,
    cot_ref,
    own_ref,
    own_field_ref,
    names_ref,
    first_y_ref,
    second_y_ref,
    first_side_ref,
    second_side_ref,
    first_x_ref,
    second_x_ref,
    adjoint_ref,
    panel_ref,
    pop_a,
    pop_b,
    ring_a,
    ring_b,
    wide,
    field,
    saved,
    mom,
    grad,
):
    size_x, size_y = sizes
    y_layout, side_layout, rest_layout = layouts()
    fill(
        from_y(*sides(first_y_ref, second_y_ref, "gy", y_layout)),
        own_ref,
        own_field_ref,
        cot_ref,
        [
            Joined(side, rest, X_SIDE)
            for side, rest in zip(
                sides(first_side_ref, second_side_ref, "gx", side_layout),
                sides(first_x_ref, second_x_ref, "gx", rest_layout),
            )
        ],
        pop_a,
        ring_a,
        wide,
        field,
    )

    at_x, at_y = lax.axis_index("gx"), lax.axis_index("gy")
    edges = (
        jnp.where(at_x == 0, 1, 0),
        jnp.where(at_x == size_x - 1, 1, 0),
        jnp.where(at_y == 0, 1, 0),
        jnp.where(at_y == size_y - 1, 1, 0),
    )
    row, lane, column, depth = iotas()
    after = row < 4

    def masks_of(tile, first, r):
        return wall_masks(r == 0, tile == first, tile == first + 1, edges)

    def neighbours(tile, tiles):
        if isinstance(tile, int):
            return {0: tile, -1: (tile - 1) % tiles, 1: (tile + 1) % tiles}
        return {0: tile, -1: lax.rem(tile + tiles - 1, tiles), 1: lax.rem(tile + 1, tiles)}

    def from_wide(ref, tile, r):
        step = neighbours(tile, 5)

        def load(i, tile_step, row_step, move):
            at = 5 * i + step[tile_step]
            before, own, behind = (ref[at, pl.ds(ROWS * n + row_step, ROWS), :] for n in (1, 2, 3))
            return (own, jnp.where(after, behind, before), before, behind)[r]

        return load

    def from_ring(ref, tile, tiles, r):
        step = neighbours(tile, tiles)

        def load(i, tile_step, row_step, move):
            rows = own_rows(row_step) if r == 0 else halo_rows(row_step)
            return ref[tiles * i + step[tile_step], rows, :]

        return load

    def from_outer(ref, r):
        def load(i, tile_step, row_step, move):
            rows = own_rows(row_step) if r == 0 else halo_rows(row_step)
            if tile_step:
                return ref[4 * i + (2 if tile_step < 0 else 1), rows, :]
            cut = {0: 2, 1: 1, -1: 3}[move]
            return jnp.where(column < cut, ref[4 * i + 3, rows, :], ref[4 * i, rows, :])

        return load

    def note(s, tile, r, parts):
        for n, value in enumerate(parts[2:4] + tuple(parts[4])):
            mom[s - 1, n, tile, r] = value

    def first_step(tile, carry):
        place = lax.rem(tile + 4, 5)
        halo = []
        for r in (2, 0, 3):
            f = stream_tile(from_wide(pop_a, tile, r), 1, masks_of(tile, 2, r), lane)
            parts = moments(f)
            if r == 0:
                note(1, place, 0, parts)
                for i in range(Q):
                    saved[0, i, place] = f[i]
            else:
                halo.append(parts[2:4] + tuple(parts[4]))
            at = {2: 0, 0: 1, 3: 2}[r]
            g = collide(f, wide[0, tile, at], wide[1, tile, at], parts)
            for i in range(Q):
                pop_b[5 * i + tile, pl.ds(ROWS * (at + 1), ROWS), :] = g[i]
        for n in range(5):
            mom[0, n, place, 1] = jnp.where(after, halo[1][n], halo[0][n])
        return carry

    lax.fori_loop(0, 5, first_step, 0)

    def second_step(tile, carry):
        out = []
        for r in range(2):
            f = stream_tile(from_wide(pop_b, tile + 1, r), 1, masks_of(tile, 1, r), lane)
            parts = moments(f)
            note(2, tile, r, parts)
            if r == 0:
                for i in range(Q):
                    saved[1, i, tile] = f[i]
            out.append(collide(f, field[2, tile, r], field[0, tile, r], parts))
        for i in range(Q):
            put_ring(ring_b, 4 * i + tile, out[0][i], out[1][i])
        return carry

    lax.fori_loop(0, 4, second_step, 0)

    def third_step(tile, carry):
        for r in range(2):
            f = stream_tile(from_ring(ring_b, tile, 4, r), 1, masks_of(tile, 1, r), lane)
            note(3, tile, r, moments(f))
            if r == 0:
                for i in range(Q):
                    saved[2, i, tile] = f[i]
        return carry

    lax.fori_loop(0, 4, third_step, 0)

    def back_tile(load, s, tile, r, own):
        b = stream_tile(load, -1, masks_of(4 if tile is None else tile, 1, r), lane)

        def read(get):
            return jnp.where(column < 2, get(3), get(0)) if tile is None else get(tile)

        rho, rinv, *u = [read(lambda at: mom[s - 1, n, at, r]) for n in range(5)]
        kind, phi = read(lambda at: field[s, at, r]), read(lambda at: field[0, at, r])
        state = [saved[s - 1, i, tile] for i in range(Q)] if own else None
        back, term = collide_back(b, kind, phi, rho, rinv, u, state)
        if own:
            grad[tile] = term if s == 3 else grad[tile] + term
        return back

    def last_step(tile, carry):
        out = [back_tile(from_ring(ring_a, tile, 4, r), 3, tile, r, r == 0) for r in range(2)]
        for i in range(Q):
            put_ring(ring_b, 4 * i + tile, out[0][i], out[1][i])
        return carry

    lax.fori_loop(0, 4, last_step, 0)

    for k, tile in enumerate((1, 2, None)):
        out = []
        for r in range(2):
            load = from_outer(ring_b, r) if tile is None else from_ring(ring_b, tile, 4, r)
            out.append(back_tile(load, 2, tile, r, r == 0 and tile is not None))
        for i in range(Q):
            put_ring(ring_a, 3 * i + k, out[0][i], out[1][i])

    for k, tile in enumerate((1, 2, None)):
        out = []
        for r in range(2):
            load = from_ring(ring_a, k, 3, r)
            out.append(back_tile(load, 1, tile, r, r == 0 and tile is not None))
        for i in range(Q):
            put_ring(ring_b, 3 * i + k, out[0][i], out[1][i])

    panel = lax.broadcasted_iota(jnp.int32, panel_ref.shape, 1)
    sums = jnp.zeros(panel_ref.shape, jnp.float32)
    for t in range(2):
        b = stream_tile(from_ring(ring_b, t, 3, 0), -1, masks_of(t, 0, 0), lane)
        f = [state_ref[2 * i + t] for i in range(Q)]
        kind, phi = own_field_ref[t], own_field_ref[2 * OWN_PHI + t]
        _, _, rho, rinv, u = moments(f)
        back, term = collide_back(b, kind, phi, rho, rinv, u, f)
        for i in range(Q):
            adjoint_ref[i, :, pl.ds(t * LANES, LANES)] = back[i]
        term = term + grad[t + 1]
        for part in range(2):
            amount = jnp.sum(jnp.where((row < 4) == (part == 0), term, 0.0))
            name = names_ref[t, 4 * part : 4 * part + 1, 0:1]
            sums = sums + jnp.where(panel == name, amount, 0.0)
    panel_ref[...] = sums


def add_panels(parts_ref, out_ref):
    out_ref[...] = jnp.sum(parts_ref[...], axis=0)


VMEM = pl.BlockSpec(memory_space=pltpu.VMEM)
HBM = pl.BlockSpec(memory_space=pltpu.HBM)
ANY = pl.BlockSpec(memory_space=pl.ANY)


def shape_of(*dims):
    return jax.ShapeDtypeStruct(dims, jnp.float32)


def tiles_of(count):
    return shape_of(count, ROWS, LANES)


def on_device(sizes, checkpoint, cotangent, cell_codes, porosity, baffle_index):
    size_x, size_y = sizes
    panels = porosity.shape[0]
    devices = size_x * size_y
    y_layout, side_layout, rest_layout = layouts()

    def call(kernel, out_shape, in_specs, scratch=(), name=None):
        return pl.pallas_call(
            kernel,
            out_shape=out_shape,
            in_specs=in_specs,
            out_specs=jax.tree.map(lambda _: VMEM, out_shape),
            scratch_shapes=scratch,
            compiler_params=pltpu.CompilerParams(vmem_limit_bytes=32 * 1024 * 1024),
            name=name,
        )

    def swap(value, axis, size):
        return lax.ppermute(value, axis, [(i, i ^ 1) for i in range(size) if i ^ 1 < size])

    def swap_between(value, axis, size):
        pairs = [(i, i + 1) for i in range(1, size - 1, 2)]
        return lax.ppermute(value, axis, pairs + [(j, i) for i, j in pairs])

    arguments = [
        pltpu.with_memory_space_constraint(value, pltpu.HBM)
        for value in (checkpoint, cotangent, cell_codes, baffle_index, porosity)
    ]
    first_y, second_y, first_side, second_side, own, state, cot, field, names = call(
        pack_own,
        (tiles_of(y_layout.size + 2), tiles_of(y_layout.size))
        + (tiles_of(side_layout.size), tiles_of(y_layout.size + 1))
        + (tiles_of(2 * Q),) * 3
        + (tiles_of(2 * OWN_PHI + 2), jax.ShapeDtypeStruct((2, ROWS, LANES), jnp.int32)),
        [HBM] * 5,
        [
            pltpu.VMEM((Q, ROWS, 2 * LANES), jnp.float32),
            pltpu.VMEM((Q, ROWS, 2 * LANES), jnp.float32),
            pltpu.VMEM((STEPS, ROWS, 2 * LANES), jnp.int32),
            pltpu.SMEM(baffle_index.shape, jnp.int32),
            pltpu.SMEM(porosity.shape, jnp.float32),
            pltpu.SemaphoreType.DMA((5,)),
        ],
        name="pack_own",
    )(*arguments)
    second_y = swap_between(second_y, "gy", size_y)
    first_y = swap(first_y, "gy", size_y)
    second_side = swap_between(second_side, "gx", size_x)
    first_side = swap(first_side, "gx", size_x)
    first_x, second_x = call(
        pack_x,
        (tiles_of(rest_layout.size), tiles_of(rest_layout.size + 1)),
        [VMEM] * 3 + [ANY] * 2,
        name="pack_x",
    )(field, first_y, second_y, first_side, second_side)
    second_x = swap_between(second_x, "gx", size_x)
    first_x = swap(first_x, "gx", size_x)

    adjoint, sums = call(
        functools.partial(steps_kernel, sizes),
        (shape_of(Q, ROWS, 2 * LANES), shape_of(devices, panels)),
        [VMEM] * 11,
        [
            pltpu.VMEM((5 * Q, 5 * ROWS, LANES), jnp.float32),
            pltpu.VMEM((5 * Q, 5 * ROWS, LANES), jnp.float32),
            pltpu.VMEM((4 * Q, 3 * ROWS, LANES), jnp.float32),
            pltpu.VMEM((4 * Q, 3 * ROWS, LANES), jnp.float32),
            pltpu.VMEM((2, 5, 3, ROWS, LANES), jnp.float32),
            pltpu.VMEM((4, 4, 2, ROWS, LANES), jnp.float32),
            pltpu.VMEM((3, Q, 5, ROWS, LANES), jnp.float32),
            pltpu.VMEM((3, 5, 5, 2, ROWS, LANES), jnp.float32),
            pltpu.VMEM((4, ROWS, LANES), jnp.float32),
        ],
        name="steps",
    )(state, cot, own, field, names, first_y, second_y, first_side, second_side, first_x, second_x)
    gathered = lax.all_to_all(sums, ("gx", "gy"), 0, 0, tiled=True)
    totals = call(add_panels, shape_of(1, panels), [VMEM], name="add_panels")(
        gathered.reshape(devices, 1, panels)
    )
    return adjoint, totals.reshape(panels)


def solution(mesh):
    sizes = (mesh.shape["gx"], mesh.shape["gy"])
    in_specs = (P(None, "gx", "gy"), P(None, "gx", "gy"), P(None, "gx", "gy"), P(), P("gx", "gy"))
    out_specs = (P(None, "gx", "gy"), P())
    return jax.shard_map(
        functools.partial(on_device, sizes),
        mesh=mesh,
        in_specs=in_specs,
        out_specs=out_specs,
        check_vma=False,
    )
```

```python
import functools

import jax
import jax.numpy as jnp
import numpy as np
from jax import lax
from jax.experimental import pallas as pl
from jax.experimental.pallas import tpu as pltpu
from jax.sharding import PartitionSpec as P

Q = 19
STEPS = 4
NZ = 32
ROWS = 8
LANES = 128
OMEGA = 1.6
ACCEL = (0.002, 0.0, -0.003)
SHIFT = tuple(a / OMEGA for a in ACCEL)

VELOCITIES = [
    (0, 0, 0),
    (1, 0, 0),
    (-1, 0, 0),
    (0, 1, 0),
    (0, -1, 0),
    (0, 0, 1),
    (0, 0, -1),
    (1, 1, 0),
    (-1, -1, 0),
    (1, -1, 0),
    (-1, 1, 0),
    (1, 0, 1),
    (-1, 0, -1),
    (1, 0, -1),
    (-1, 0, 1),
    (0, 1, 1),
    (0, -1, -1),
    (0, 1, -1),
    (0, -1, 1),
]
OPPOSITE = [0, 2, 1, 4, 3, 6, 5, 8, 7, 10, 9, 12, 11, 14, 13, 16, 15, 18, 17]
PAIRS = [(i, i + 1) for i in range(1, Q, 2)]
W_REST, W_AXIS, W_DIAG = 1.0 / 3.0, 1.0 / 18.0, 1.0 / 36.0

Y_CODE1, Y_CODE2, Y_CODE3, Y_POP, Y_COT = 38, 39, 40, 41, 42
Y_TILES = 43
X_EXTRA = 19
X_LANE = 20
X_SIDE = 2 * X_LANE
X_RING = 4 * X_LANE
X_CODE13 = X_RING + Q + 1
X_CODE2 = X_CODE13 + 4
X_TILES = X_CODE2 + 2
EMPTY = 25
FREE = NZ - EMPTY
WEIGHTS = [W_REST] + [W_AXIS] * 6 + [W_DIAG] * 12
LEVEL = [i for i, v in enumerate(VELOCITIES) if v[2] < 1]
OWN_PHI = 4


def turned(axis, outward):
    return [i for i, v in enumerate(VELOCITIES) if v[axis] == outward and sum(map(abs, v)) == 2]


def total(values):
    values = list(values)
    while len(values) > 1:
        values = [a + b for a, b in zip(values[::2], values[1::2])] + (
            [values[-1]] if len(values) % 2 else []
        )
    return values[0]


def along(vector, three):
    terms = None
    for c, value in zip(vector, three):
        if c == 0:
            continue
        if terms is None:
            terms = value if c > 0 else -value
        else:
            terms = terms + value if c > 0 else terms - value
    return terms


def moments(f):
    plus = {i: f[i] + f[o] for i, o in PAIRS}
    minus = {i: f[i] - f[o] for i, o in PAIRS}
    rho = total([f[0]] + [plus[i] for i, _ in PAIRS])
    rinv = 1.0 / rho
    u = []
    for axis in range(3):
        terms = [
            minus[i] if VELOCITIES[i][axis] > 0 else -minus[i]
            for i, _ in PAIRS
            if VELOCITIES[i][axis] != 0
        ]
        u.append(total(terms) * rinv + SHIFT[axis])
    return plus, minus, rho, rinv, u


def coefficients(kind, phi, rinv):
    baffle = kind == 3.0
    gas = kind == 0.0
    even = jnp.where(gas, 0.0, jnp.where(baffle, 0.5 - 0.5 * OMEGA * phi, 0.5 * (1.0 - OMEGA)))
    odd = jnp.where(
        gas, 0.0, jnp.where(baffle, (1.0 - 0.5 * OMEGA) * phi - 0.5, 0.5 * (1.0 - OMEGA))
    )
    slope = jnp.where(
        baffle,
        OMEGA * phi,
        jnp.where(kind == 1.0, OMEGA, jnp.where(kind == 2.0, OMEGA * rinv, 0.0)),
    )
    return even, odd, slope


def collide(f, kind, phi, parts):
    plus, minus, rho, rinv, u = parts
    even, odd, slope = coefficients(kind, phi, rinv)
    scale = slope * rho
    rest = 1.0 - 1.5 * (u[0] * u[0] + u[1] * u[1] + u[2] * u[2])
    base = scale * rest + jnp.where(kind == 0.0, 1.0, 0.0)
    out = [None] * Q
    out[0] = 2.0 * even * f[0] + W_REST * base
    for weight, pairs in ((W_AXIS, PAIRS[:3]), (W_DIAG, PAIRS[3:])):
        flat = weight * base
        three = (3.0 * weight) * scale
        for i, o in pairs:
            cu = along(VELOCITIES[i], u)
            lin = three * cu
            ev = even * plus[i] + (flat + 1.5 * lin * cu)
            od = odd * minus[i] + lin
            out[i] = ev + od
            out[o] = ev - od
    return out


def collide_back(b, kind, phi, rho, rinv, u, state=None):
    even, odd, slope = coefficients(kind, phi, rinv)
    plus = {i: b[i] + b[o] for i, o in PAIRS}
    minus = {i: b[i] - b[o] for i, o in PAIRS}
    rest = 1.0 - 1.5 * (u[0] * u[0] + u[1] * u[1] + u[2] * u[2])
    u_half = [1.5 * c for c in u]
    weighted = W_REST * b[0]
    energy = 0.0
    vector = [0.0, 0.0, 0.0]
    for weight, pairs in ((W_AXIS, PAIRS[:3]), (W_DIAG, PAIRS[3:])):
        weighted = weighted + weight * total([plus[i] for i, _ in pairs])
        energies, parts = [], ([], [], [])
        for i, _ in pairs:
            cu = along(VELOCITIES[i], u)
            half = along(VELOCITIES[i], u_half) * plus[i]
            first = minus[i] + half
            energies.append(cu * first)
            second = first + half
            for axis in range(3):
                c = VELOCITIES[i][axis]
                if c:
                    parts[axis].append(second if c > 0 else -second)
        energy = energy + (3.0 * weight) * total(energies)
        vector = [vector[k] + (3.0 * weight) * total(parts[k]) for k in range(3)]
    energy = energy + rest * weighted
    vector = [vector[k] - (3.0 * weighted) * u[k] for k in range(3)]
    push = [slope * v for v in vector]
    inner = total([push[k] * (u[k] - SHIFT[k]) for k in range(3)])
    shared = jnp.where(kind == 2.0, 0.0, slope) * energy - inner
    out = [None] * Q
    out[0] = 2.0 * even * b[0] + shared
    for i, o in PAIRS:
        ev = even * plus[i] + shared
        od = odd * minus[i] + along(VELOCITIES[i], push)
        out[i] = ev + od
        out[o] = ev - od
    if state is None:
        return out, None
    evens = total([plus[i] * (state[i] + state[o]) for i, o in PAIRS])
    odds = total([minus[i] * (state[i] - state[o]) for i, o in PAIRS])
    term = (
        -OMEGA * (b[0] * state[0] + 0.5 * evens)
        + (1.0 - 0.5 * OMEGA) * odds
        + OMEGA * rho * energy
    )
    return out, jnp.where(kind == 3.0, term, 0.0)


def wall_masks(sign_rows, own_low, own_high, edges):
    lane = lax.broadcasted_iota(jnp.int32, (ROWS, LANES), 1)
    row = lax.broadcasted_iota(jnp.int32, (ROWS, LANES), 0)
    x_low, x_high, y_low, y_high = edges
    depth = lane % NZ
    masks = {}
    masks[2, 1] = depth == 0
    masks[2, -1] = depth == NZ - 1
    masks[1, 1] = lane < jnp.where(own_low, y_low * NZ, 0)
    masks[1, -1] = lane >= jnp.where(own_high, LANES - y_high * NZ, LANES)
    if sign_rows:
        masks[0, 1] = row < x_low
        masks[0, -1] = row >= ROWS - x_high
    return masks


def stream_tile(load, sign, masks, lane):
    cross_low, cross_high = lane >= LANES - NZ, lane < NZ
    combined = {}
    out = []
    for i, vector in enumerate(VELOCITIES):
        v = tuple(sign * c for c in vector)
        value = load(i, 0, -v[0], v[1])
        if v[1] == 1:
            value = jnp.where(cross_low, load(i, -1, -v[0], 1), value)
        elif v[1] == -1:
            value = jnp.where(cross_high, load(i, 1, -v[0], -1), value)
        amount = (v[1] * NZ + v[2]) % LANES
        if amount:
            value = pltpu.roll(value, amount, 1)
        outside = None
        if v not in combined:
            for axis in range(3):
                if v[axis] and (axis, v[axis]) in masks:
                    wall = masks[axis, v[axis]]
                    outside = wall if outside is None else outside | wall
            combined[v] = outside
        outside = combined[v]
        if outside is not None:
            value = jnp.where(outside, load(OPPOSITE[i], 0, 0, 0), value)
        out.append(value)
    return out


def iotas():
    row = lax.broadcasted_iota(jnp.int32, (ROWS, LANES), 0)
    lane = lax.broadcasted_iota(jnp.int32, (ROWS, LANES), 1)
    return row, lane, lane // NZ, lane % NZ


def columns(value, count):
    amount = (count * NZ) % LANES
    return pltpu.roll(value, amount, 1) if amount else value


def lines(value, count):
    amount = count % ROWS
    return pltpu.roll(value, amount, 0) if amount else value


class Layout:
    def __init__(self, count, guests, fills):
        self.fills = fills
        hosts = [at for at in fills if at not in guests]
        self.hosts = {at: hosts[4 * n : 4 * n + 4] for n, at in enumerate(guests)}
        self.guests = guests
        kept = [at for at in range(count) if at not in guests]
        self.place = {at: n for n, at in enumerate(kept)}
        self.size = len(kept)


class Packing:
    def __init__(self, ref, layout):
        self.ref, self.layout, self.held = ref, layout, {}

    def __setitem__(self, at, value):
        if at in self.layout.guests:
            self.held[at] = value
        else:
            self.ref[self.layout.place[at]] = value

    def finish(self):
        row, lane, column, depth = iotas()
        spare = depth >= EMPTY
        for at, value in self.held.items():
            for k, host in enumerate(self.layout.hosts[at]):
                place = self.layout.place[host]
                moved = pltpu.roll(value, EMPTY - FREE * k, 1)
                self.ref[place] = jnp.where(spare, moved, self.ref[place])
        for place in range(self.layout.size, self.ref.shape[0]):
            self.ref[place] = jnp.zeros((ROWS, LANES), jnp.float32)


class Unpacking:
    def __init__(self, source, layout):
        self.source, self.layout, self.cache = source, layout, {}
        self.changed = set(layout.guests).union(*layout.hosts.values())

    def __getitem__(self, at):
        if at not in self.cache:
            self.cache[at] = self.read(at)
        return self.cache[at]

    def read(self, at):
        row, lane, column, depth = iotas()
        layout = self.layout
        if at in layout.guests:
            value = None
            for k, host in enumerate(layout.hosts[at]):
                tile = self.source[layout.place[host]]
                moved = pltpu.roll(tile, LANES - (EMPTY - FREE * k), 1)
                value = moved if value is None else jnp.where(depth >= FREE * k, moved, value)
        else:
            value = self.source[layout.place[at]]
        if at in self.changed:
            value = jnp.where(depth >= EMPTY, layout.fills[at], value)
        return value


def layouts():
    y_fills = {2 * i + t: WEIGHTS[i] for i in LEVEL for t in range(2)}
    y_fills.update({Y_POP: W_DIAG, Y_CODE2: 0.0})
    x_fills = {X_LANE * n + i: WEIGHTS[i] for n in range(4) for i in LEVEL}
    side = {at: fill for at, fill in x_fills.items() if at < X_SIDE}
    rest = {at - X_SIDE: fill for at, fill in x_fills.items() if at >= X_SIDE}
    rest.update({X_CODE2 - X_SIDE: 0.0, X_CODE2 + 1 - X_SIDE: 0.0})
    rest.update({X_RING - X_SIDE + i: WEIGHTS[i] for i in range(Q)})
    ring = [X_RING - X_SIDE + i for i in range(9)]
    return (
        Layout(Y_TILES, [2 * i for i in LEVEL[:6]], y_fills),
        Layout(X_SIDE, LEVEL[:5], side),
        Layout(X_TILES - X_SIDE, ring, rest),
    )


class Pick:
    def __init__(self, flag, first, second):
        self.flag, self.first, self.second = flag, first, second

    def __getitem__(self, at):
        return jnp.where(self.flag, self.first[at], self.second[at])


class Deal:
    def __init__(self, even, first, second, layout, skip=0):
        self.even, self.skip, self.held = even, skip, {}
        self.first, self.second = Packing(first, layout), Packing(second, layout)

    def put(self, way, at, value):
        if (-way, at) not in self.held:
            self.held[way, at] = value
            return
        other = self.held.pop((-way, at))
        up, down = (value, other) if way == 1 else (other, value)
        self.first[at - self.skip] = jnp.where(self.even, up, down)
        self.second[at - self.skip] = jnp.where(self.even, down, up)

    def put_both(self, at, value):
        self.first[at - self.skip] = value
        self.second[at - self.skip] = value

    def finish(self):
        self.first.finish()
        self.second.finish()


class Joined:
    def __init__(self, first, second, cut):
        self.first, self.second, self.cut = first, second, cut

    def __getitem__(self, at):
        return self.first[at] if at < self.cut else self.second[at - self.cut]


def is_even(axis):
    return lax.rem(lax.axis_index(axis), 2) == 0


def pack_own(
    f_hbm,
    cot_hbm,
    codes_hbm,
    panels_hbm,
    porosity_hbm,
    first_ref,
    second_ref,
    first_side_ref,
    second_side_ref,
    own_ref,
    state_ref,
    own_cot_ref,
    field_ref,
    names_ref,
    f_ref,
    cot_ref,
    codes_ref,
    panels_ref,
    porosity_ref,
    sems,
):
    pieces = (
        (panels_hbm, panels_ref),
        (porosity_hbm, porosity_ref),
        (f_hbm, f_ref),
        (codes_hbm, codes_ref),
        (cot_hbm, cot_ref),
    )
    copies = [
        pltpu.make_async_copy(source, target, sems.at[n])
        for n, (source, target) in enumerate(pieces)
    ]
    for copy in copies:
        copy.start()
    for copy in copies[:4]:
        copy.wait()
    y_layout, side_layout, _ = layouts()
    deal = Deal(is_even("gy"), first_ref, second_ref, y_layout)
    side = Deal(is_even("gx"), first_side_ref, second_side_ref, side_layout)
    row, lane, column, depth = iotas()
    top = depth == NZ - 1

    def tile_of(ref, i, t):
        return ref[i, :, pl.ds(t * LANES, LANES)]

    codes, phis = [], []
    for t in range(2):
        names = panels_ref[0, t * LANES], panels_ref[4, t * LANES]
        phi = jnp.where(row < 4, porosity_ref[names[0]], porosity_ref[names[1]])
        names_ref[t] = jnp.where(row < 4, names[0], names[1])
        kinds = [tile_of(codes_ref, s, t).astype(jnp.float32) for s in range(STEPS)]
        f = [tile_of(f_ref, i, t) for i in range(Q)]
        g = collide(f, kinds[0], phi, moments(f))
        for i in range(Q):
            own_ref[2 * i + t] = g[i]
            state_ref[2 * i + t] = f[i]
        for s in range(STEPS):
            field_ref[2 * s + t] = kinds[s]
        field_ref[2 * OWN_PHI + t] = phi
        codes.append([jnp.where(top, phi, kinds[1]), kinds[2], kinds[3]])
    copies[4].wait()
    for i in range(Q):
        for way in (1, -1):
            near, far = (1, 0) if way == 1 else (0, 1)
            deep = 3 - way * VELOCITIES[i][1]
            cot = tile_of(cot_ref, i, near)
            g_far = own_ref[2 * i + far]
            if way == 1:
                mixed = jnp.where(column >= deep, g_far, columns(cot, deep - 4))
            else:
                mixed = jnp.where(column < 4 - deep, g_far, columns(cot, 4 - deep))
            deal.put(way, 2 * i, mixed if far == 0 else own_ref[2 * i])
            deal.put(way, 2 * i + 1, mixed if far == 1 else own_ref[2 * i + 1])
    for way in (1, -1):
        near, far = (1, 0) if way == 1 else (0, 1)
        outer = 3 if way == 1 else 0
        deal.put(way, Y_CODE1, codes[near][0])
        deal.put(way, Y_CODE2, codes[near][1])
        outside = columns(codes[far][0], 3 - 2 * outer)
        deal.put(way, Y_CODE3, jnp.where(column == 3 - outer, outside, codes[near][2]))
        extra = None
        for k, i in enumerate(turned(1, -way)):
            value = columns(own_ref[2 * i + far], k - outer)
            extra = value if extra is None else jnp.where(column == k, value, extra)
        deal.put(way, Y_POP, extra)
        extra = None
        for k, i in enumerate(turned(1, way)):
            value = columns(tile_of(cot_ref, i, near), k - (1 if way == 1 else 2))
            extra = value if extra is None else jnp.where(column == k, value, extra)
        deal.put(way, Y_COT, extra)
    deal.finish()
    for t in range(2):
        for i in range(Q):
            own_cot_ref[2 * i + t] = tile_of(cot_ref, i, t)
        pack_lines(
            side,
            X_LANE * t,
            lambda i: own_ref[2 * i + t],
            lambda i: tile_of(cot_ref, i, t),
        )
    side.finish()


def from_y(left_ref, right_ref):
    row, lane, column, depth = iotas()
    high = lane >= LANES // 2

    def population(i, c):
        if c == 1:
            return left_ref[2 * i + 1]
        if c == 4:
            return right_ref[2 * i]
        along_y = VELOCITIES[i][1]
        left, right = left_ref[2 * i], right_ref[2 * i + 1]
        if along_y == 1 and i in turned(1, 1):
            right = columns(right_ref[Y_POP], -turned(1, 1).index(i))
        if along_y == -1 and i in turned(1, -1):
            left = columns(left_ref[Y_POP], 3 - turned(1, -1).index(i))
        return jnp.where(high, left, right)

    def cotangent(i, c):
        ref, way, place, far = (left_ref, 1, 1, 0) if c == 1 else (right_ref, -1, 2, 1)
        deep = 3 - way * VELOCITIES[i][1]
        value = columns(ref[2 * i + far], way * (4 - deep))
        if i in turned(1, way):
            extra = columns(ref[Y_COT], place - turned(1, way).index(i))
            value = jnp.where(column == place, extra, value)
        return value

    def codes(s, c):
        if c == 0:
            left, right = columns(left_ref[Y_CODE3], 3), columns(right_ref[Y_CODE3], 1)
            return jnp.where(high, left, right)
        return (left_ref if c == 1 else right_ref)[(Y_CODE1, Y_CODE2, Y_CODE3)[s - 1]]

    return population, cotangent, codes


def mix_lines(deal, at, pop, cot, deep, way):
    row, lane, column, depth = iotas()
    if way == 1:
        mixed = jnp.where(row >= deep, pop, lines(cot, deep))
    else:
        mixed = jnp.where(row < ROWS - deep, pop, lines(cot, -deep))
    deal.put(way, at, mixed)


def pack_lines(deal, first, population, cotangent):
    row, lane, column, depth = iotas()

    for i in range(Q):
        pop, cot = population(i), cotangent(i)
        for way in (1, -1):
            mix_lines(deal, first + i, pop, cot, 3 - way * VELOCITIES[i][0], way)
    for way in (1, -1):
        extra = None
        for k, i in enumerate(turned(0, -way)):
            value = lines(population(i), k - (3 if way == 1 else 4))
            extra = value if extra is None else jnp.where(row == k, value, extra)
        for k, i in enumerate(turned(0, way)):
            value = lines(cotangent(i), 4 + k - (5 if way == 1 else 2))
            extra = jnp.where(row == 4 + k, value, extra)
        deal.put(way, first + X_EXTRA, extra)


def from_x(ref, n, way):
    row, lane, column, depth = iotas()
    first = X_LANE * n

    def population(i):
        value = ref[first + i]
        if i in turned(0, -way):
            place = 3 if way == 1 else 4
            extra = lines(ref[first + X_EXTRA], place - turned(0, -way).index(i))
            value = jnp.where(row == place, extra, value)
        return value

    def cotangent(i):
        value = lines(ref[first + i], -way * (3 - way * VELOCITIES[i][0]))
        if i in turned(0, way):
            place = 5 if way == 1 else 2
            extra = lines(ref[first + X_EXTRA], place - 4 - turned(0, way).index(i))
            value = jnp.where(row == place, extra, value)
        return value

    def codes(s):
        if s == 2:
            return lines(ref[X_CODE2 + n // 2], 4 * (n % 2))
        value = ref[X_CODE13 + n]
        return value if s == 1 else lines(value, -3 * way)

    return population, cotangent, codes


def pack_x(field_ref, first_y_ref, second_y_ref, early_a, early_b, first_ref, second_ref):
    row, lane, column, depth = iotas()
    y_layout, _, layout = layouts()
    deal = Deal(is_even("gx"), first_ref, second_ref, layout, X_SIDE)
    population, cotangent, codes = from_y(*sides(first_y_ref, second_y_ref, "gy", y_layout))

    def both_codes(at, first, second):
        second = lines(second, 4)
        deal.put(1, at, jnp.where(row >= 4, first, second))
        deal.put(-1, at, jnp.where(row < 4, first, second))

    for n, c in ((2, 1), (3, 4)):
        pack_lines(
            deal,
            X_LANE * n,
            lambda i: population(i, c),
            lambda i: cotangent(i, c),
        )
    for n in range(Q + 1):
        value = population(n, 0) if n < Q else codes(1, 0)
        deal.put_both(X_RING + n, value)
    for n in range(4):
        if n < 2:
            first = jnp.where(depth == NZ - 1, field_ref[2 * OWN_PHI + n], field_ref[2 + n])
            third = field_ref[6 + n]
        else:
            c = (1, 4)[n - 2]
            first, third = codes(1, c), codes(3, c)
        for way in (1, -1):
            mix_lines(deal, X_CODE13 + n, first, third, 3, way)
    both_codes(X_CODE2, field_ref[4], field_ref[5])
    both_codes(X_CODE2 + 1, codes(2, 1), codes(2, 4))
    deal.finish()


def sides(first_ref, second_ref, axis, layout):
    even = is_even(axis)
    picks = Pick(even, second_ref, first_ref), Pick(even, first_ref, second_ref)
    return [Unpacking(pick, layout) for pick in picks]


def own_rows(step=0):
    return pl.ds(ROWS + step, ROWS)


def halo_rows(step=0):
    return pl.ds({0: 2 * ROWS, -1: 2 * ROWS - 1, 1: 1}[step], ROWS)


def put_halo(ref, at, halo):
    ref[at, pl.ds(0, ROWS), :] = halo
    ref[at, halo_rows(), :] = halo


def put_ring(ref, at, own, halo):
    ref[at, own_rows(), :] = own
    put_halo(ref, at, halo)


def expand(code):
    row, lane, column, depth = iotas()
    top = depth == NZ - 1
    phi = jnp.where(top, code, 0.0)
    for step in (1, 2, 4, 8, 16):
        phi = phi + pltpu.roll(phi, LANES - step, 1)
    return jnp.where(top, 0.0, code), phi


def lay_own(c, population, cotangent, codes, code_phi, pop, cot, wide, field):
    for i in range(Q):
        pop[5 * i + c, pl.ds(2 * ROWS, ROWS), :] = population(i)
        if c:
            cot[4 * i + c - 1, own_rows(), :] = cotangent(i)
    for n in range(2):
        wide[n, c, 1] = code_phi[n]
    if c:
        field[0, c - 1, 0], field[1, c - 1, 0] = code_phi[1], code_phi[0]
        for s in (2, 3):
            field[s, c - 1, 0] = codes(s)


def lay_halo(c, below, above, pop, cot):
    row, lane, column, depth = iotas()
    for i in range(Q):
        pop[5 * i + c, pl.ds(ROWS, ROWS), :] = below[0](i)
        pop[5 * i + c, pl.ds(3 * ROWS, ROWS), :] = above[0](i)
        if c:
            put_halo(cot, 4 * i + c - 1, jnp.where(row < 4, above[1](i), below[1](i)))


def lay_codes(c, below, above, wide, field):
    row, lane, column, depth = iotas()
    before, after = expand(below[2](1)), expand(above[2](1))
    for n in range(2):
        wide[n, c, 0], wide[n, c, 2] = before[n], after[n]
    if c:
        for n, place in ((0, 1), (1, 0)):
            field[place, c - 1, 1] = jnp.where(row < 4, after[n], before[n])
        for s in (2, 3):
            field[s, c - 1, 1] = jnp.where(row < 4, above[2](s), below[2](s))


def lay_out(
    first_y_ref,
    second_y_ref,
    first_side_ref,
    second_side_ref,
    own_ref,
    field_ref,
    cot_ref,
    pop,
    cot,
    wide,
    field,
):
    y_layout, side_layout, _ = layouts()
    from_left = from_y(*sides(first_y_ref, second_y_ref, "gy", y_layout))
    below, above = sides(first_side_ref, second_side_ref, "gx", side_layout)
    for c in range(5):
        t = c - 2
        if t in (0, 1):
            lay_own(
                c,
                lambda i: own_ref[2 * i + t],
                lambda i: cot_ref[2 * i + t],
                lambda s: field_ref[2 * s + t],
                (field_ref[2 + t], field_ref[2 * OWN_PHI + t]),
                pop,
                cot,
                wide,
                field,
            )
            lay_halo(c, from_x(below, t, 1), from_x(above, t, -1), pop, cot)
        else:
            own = [functools.partial(lambda g, n: g(n, c), get) for get in from_left]
            lay_own(c, *own, expand(own[2](1)), pop, cot, wide, field)


def lay_corners(first_x_ref, second_x_ref, pop, cot, wide, field):
    _, _, layout = layouts()
    below, above = (
        Joined(None, side, X_SIDE) for side in sides(first_x_ref, second_x_ref, "gx", layout)
    )
    lay_halo(
        0, (lambda i: below[X_RING + i],), (lambda i: above[X_RING + i],), pop, cot
    )
    ring = [(None, None, lambda s, ref=ref: ref[X_RING + Q]) for ref in (below, above)]
    lay_codes(0, *ring, wide, field)
    for n, c in enumerate((2, 3, 1, 4)):
        halves = from_x(below, n, 1), from_x(above, n, -1)
        if n > 1:
            lay_halo(c, *halves, pop, cot)
        lay_codes(c, *halves, wide, field)


def steps_kernel(
    sizes,
    state_ref,
    own_field_ref,
    names_ref,
    first_x_ref,
    second_x_ref,
    *refs,
):
    adjoint_ref, panel_ref, pop_a, ring_a, wide, field, pop_b, ring_b, saved, mom, grad = refs[4:]
    size_x, size_y = sizes
    lay_corners(first_x_ref, second_x_ref, pop_a, ring_a, wide, field)

    at_x, at_y = lax.axis_index("gx"), lax.axis_index("gy")
    edges = (
        jnp.where(at_x == 0, 1, 0),
        jnp.where(at_x == size_x - 1, 1, 0),
        jnp.where(at_y == 0, 1, 0),
        jnp.where(at_y == size_y - 1, 1, 0),
    )
    row, lane, column, depth = iotas()
    after = row < 4

    def masks_of(tile, first, r):
        return wall_masks(r == 0, tile == first, tile == first + 1, edges)

    def neighbours(tile, tiles):
        if isinstance(tile, int):
            return {0: tile, -1: (tile - 1) % tiles, 1: (tile + 1) % tiles}
        return {0: tile, -1: lax.rem(tile + tiles - 1, tiles), 1: lax.rem(tile + 1, tiles)}

    def from_wide(ref, tile, r):
        step = neighbours(tile, 5)

        def load(i, tile_step, row_step, move):
            at = 5 * i + step[tile_step]
            before, own, behind = (ref[at, pl.ds(ROWS * n + row_step, ROWS), :] for n in (1, 2, 3))
            return (own, jnp.where(after, behind, before), before, behind)[r]

        return load

    def from_ring(ref, tile, tiles, r):
        step = neighbours(tile, tiles)

        def load(i, tile_step, row_step, move):
            rows = own_rows(row_step) if r == 0 else halo_rows(row_step)
            return ref[tiles * i + step[tile_step], rows, :]

        return load

    def from_outer(ref, r):
        def load(i, tile_step, row_step, move):
            rows = own_rows(row_step) if r == 0 else halo_rows(row_step)
            if tile_step:
                return ref[4 * i + (2 if tile_step < 0 else 1), rows, :]
            cut = {0: 2, 1: 1, -1: 3}[move]
            return jnp.where(column < cut, ref[4 * i + 3, rows, :], ref[4 * i, rows, :])

        return load

    def note(s, tile, r, parts):
        for n, value in enumerate(parts[2:4] + tuple(parts[4])):
            mom[s - 1, n, tile, r] = value

    def first_step(tile, carry):
        place = lax.rem(tile + 4, 5)
        halo = []
        for r in (2, 0, 3):
            f = stream_tile(from_wide(pop_a, tile, r), 1, masks_of(tile, 2, r), lane)
            parts = moments(f)
            if r == 0:
                note(1, place, 0, parts)
                for i in range(Q):
                    saved[0, i, place] = f[i]
            else:
                halo.append(parts[2:4] + tuple(parts[4]))
            at = {2: 0, 0: 1, 3: 2}[r]
            g = collide(f, wide[0, tile, at], wide[1, tile, at], parts)
            for i in range(Q):
                pop_b[5 * i + tile, pl.ds(ROWS * (at + 1), ROWS), :] = g[i]
        for n in range(5):
            mom[0, n, place, 1] = jnp.where(after, halo[1][n], halo[0][n])
        return carry

    lax.fori_loop(0, 5, first_step, 0)

    def second_step(tile, carry):
        out = []
        for r in range(2):
            f = stream_tile(from_wide(pop_b, tile + 1, r), 1, masks_of(tile, 1, r), lane)
            parts = moments(f)
            note(2, tile, r, parts)
            if r == 0:
                for i in range(Q):
                    saved[1, i, tile] = f[i]
            out.append(collide(f, field[2, tile, r], field[0, tile, r], parts))
        for i in range(Q):
            put_ring(ring_b, 4 * i + tile, out[0][i], out[1][i])
        return carry

    lax.fori_loop(0, 4, second_step, 0)

    def third_step(tile, carry):
        for r in range(2):
            f = stream_tile(from_ring(ring_b, tile, 4, r), 1, masks_of(tile, 1, r), lane)
            note(3, tile, r, moments(f))
            if r == 0:
                for i in range(Q):
                    saved[2, i, tile] = f[i]
        return carry

    lax.fori_loop(0, 4, third_step, 0)

    def back_tile(load, s, tile, r, own):
        b = stream_tile(load, -1, masks_of(4 if tile is None else tile, 1, r), lane)

        def read(get):
            return jnp.where(column < 2, get(3), get(0)) if tile is None else get(tile)

        rho, rinv, *u = [read(lambda at: mom[s - 1, n, at, r]) for n in range(5)]
        kind, phi = read(lambda at: field[s, at, r]), read(lambda at: field[0, at, r])
        state = [saved[s - 1, i, tile] for i in range(Q)] if own else None
        back, term = collide_back(b, kind, phi, rho, rinv, u, state)
        if own:
            grad[tile] = term if s == 3 else grad[tile] + term
        return back

    def last_step(tile, carry):
        out = [back_tile(from_ring(ring_a, tile, 4, r), 3, tile, r, r == 0) for r in range(2)]
        for i in range(Q):
            put_ring(ring_b, 4 * i + tile, out[0][i], out[1][i])
        return carry

    lax.fori_loop(0, 4, last_step, 0)

    for k, tile in enumerate((1, 2, None)):
        out = []
        for r in range(2):
            load = from_outer(ring_b, r) if tile is None else from_ring(ring_b, tile, 4, r)
            out.append(back_tile(load, 2, tile, r, r == 0 and tile is not None))
        for i in range(Q):
            put_ring(ring_a, 3 * i + k, out[0][i], out[1][i])

    for k, tile in enumerate((1, 2, None)):
        out = []
        for r in range(2):
            load = from_ring(ring_a, k, 3, r)
            out.append(back_tile(load, 1, tile, r, r == 0 and tile is not None))
        for i in range(Q):
            put_ring(ring_b, 3 * i + k, out[0][i], out[1][i])

    panel = lax.broadcasted_iota(jnp.int32, panel_ref.shape, 1)
    sums = jnp.zeros(panel_ref.shape, jnp.float32)
    for t in range(2):
        b = stream_tile(from_ring(ring_b, t, 3, 0), -1, masks_of(t, 0, 0), lane)
        f = [state_ref[2 * i + t] for i in range(Q)]
        kind, phi = own_field_ref[t], own_field_ref[2 * OWN_PHI + t]
        _, _, rho, rinv, u = moments(f)
        back, term = collide_back(b, kind, phi, rho, rinv, u, f)
        for i in range(Q):
            adjoint_ref[i, :, pl.ds(t * LANES, LANES)] = back[i]
        term = term + grad[t + 1]
        for part in range(2):
            amount = jnp.sum(jnp.where((row < 4) == (part == 0), term, 0.0))
            name = names_ref[t, 4 * part : 4 * part + 1, 0:1]
            sums = sums + jnp.where(panel == name, amount, 0.0)
    panel_ref[...] = sums


def add_panels(parts_ref, out_ref):
    out_ref[...] = jnp.sum(parts_ref[...], axis=0)


VMEM = pl.BlockSpec(memory_space=pltpu.VMEM)
HBM = pl.BlockSpec(memory_space=pltpu.HBM)
ANY = pl.BlockSpec(memory_space=pl.ANY)


def shape_of(*dims):
    return jax.ShapeDtypeStruct(dims, jnp.float32)


def tiles_of(count):
    return shape_of(count, ROWS, LANES)


def on_device(sizes, checkpoint, cotangent, cell_codes, porosity, baffle_index):
    size_x, size_y = sizes
    panels = porosity.shape[0]
    devices = size_x * size_y
    y_layout, side_layout, rest_layout = layouts()

    def call(kernel, out_shape, in_specs, scratch=(), name=None, aliases={}):
        return pl.pallas_call(
            kernel,
            out_shape=out_shape,
            in_specs=in_specs,
            out_specs=jax.tree.map(lambda _: VMEM, out_shape),
            scratch_shapes=scratch,
            input_output_aliases=aliases,
            compiler_params=pltpu.CompilerParams(vmem_limit_bytes=32 * 1024 * 1024),
            name=name,
        )

    def swap(value, axis, size):
        return lax.ppermute(value, axis, [(i, i ^ 1) for i in range(size) if i ^ 1 < size])

    def swap_between(value, axis, size):
        pairs = [(i, i + 1) for i in range(1, size - 1, 2)]
        return lax.ppermute(value, axis, pairs + [(j, i) for i, j in pairs])

    arguments = [
        pltpu.with_memory_space_constraint(value, pltpu.HBM)
        for value in (checkpoint, cotangent, cell_codes, baffle_index, porosity)
    ]
    first_y, second_y, first_side, second_side, own, state, cot, field, names = call(
        pack_own,
        (tiles_of(y_layout.size),) * 2
        + (tiles_of(side_layout.size), tiles_of(side_layout.size + 1))
        + (tiles_of(2 * Q),) * 3
        + (tiles_of(2 * OWN_PHI + 2), jax.ShapeDtypeStruct((2, ROWS, LANES), jnp.int32)),
        [HBM] * 5,
        [
            pltpu.VMEM((Q, ROWS, 2 * LANES), jnp.float32),
            pltpu.VMEM((Q, ROWS, 2 * LANES), jnp.float32),
            pltpu.VMEM((STEPS, ROWS, 2 * LANES), jnp.int32),
            pltpu.SMEM(baffle_index.shape, jnp.int32),
            pltpu.SMEM(porosity.shape, jnp.float32),
            pltpu.SemaphoreType.DMA((5,)),
        ],
        name="pack_own",
    )(*arguments)
    second_y = swap_between(second_y, "gy", size_y)
    first_y = swap(first_y, "gy", size_y)
    second_side = swap_between(second_side, "gx", size_x)
    first_side = swap(first_side, "gx", size_x)
    first_x, second_x = call(
        pack_x,
        (tiles_of(rest_layout.size), tiles_of(rest_layout.size + 1)),
        [VMEM] * 3 + [ANY] * 2,
        name="pack_x",
    )(field, first_y, second_y, first_side, second_side)
    second_x = swap_between(second_x, "gx", size_x)
    first_x = swap(first_x, "gx", size_x)

    spaces = (
        shape_of(5 * Q, 5 * ROWS, LANES),
        shape_of(4 * Q, 3 * ROWS, LANES),
        shape_of(2, 5, 3, ROWS, LANES),
        shape_of(4, 4, 2, ROWS, LANES),
    )
    laid = call(lay_out, spaces, [VMEM] * 7, name="lay_out")(
        first_y, second_y, first_side, second_side, own, field, cot
    )
    adjoint, sums, *_ = call(
        functools.partial(steps_kernel, sizes),
        (shape_of(Q, ROWS, 2 * LANES), shape_of(devices, panels)) + spaces,
        [VMEM] * 9,
        [
            pltpu.VMEM((5 * Q, 5 * ROWS, LANES), jnp.float32),
            pltpu.VMEM((4 * Q, 3 * ROWS, LANES), jnp.float32),
            pltpu.VMEM((3, Q, 5, ROWS, LANES), jnp.float32),
            pltpu.VMEM((3, 5, 5, 2, ROWS, LANES), jnp.float32),
            pltpu.VMEM((4, ROWS, LANES), jnp.float32),
        ],
        name="steps",
        aliases={5 + n: 2 + n for n in range(4)},
    )(state, field, names, first_x, second_x, *laid)
    gathered = lax.all_to_all(sums, ("gx", "gy"), 0, 0, tiled=True)
    totals = call(add_panels, shape_of(1, panels), [VMEM], name="add_panels")(
        gathered.reshape(devices, 1, panels)
    )
    return adjoint, totals.reshape(panels)


def solution(mesh):
    sizes = (mesh.shape["gx"], mesh.shape["gy"])
    in_specs = (P(None, "gx", "gy"), P(None, "gx", "gy"), P(None, "gx", "gy"), P(), P("gx", "gy"))
    out_specs = (P(None, "gx", "gy"), P())
    return jax.shard_map(
        functools.partial(on_device, sizes),
        mesh=mesh,
        in_specs=in_specs,
        out_specs=out_specs,
        check_vma=False,
    )
```

```python
import functools

import jax
import jax.numpy as jnp
import numpy as np
from jax import lax
from jax.experimental import pallas as pl
from jax.experimental.pallas import tpu as pltpu
from jax.sharding import PartitionSpec as P

Q = 19
STEPS = 4
NZ = 32
ROWS = 8
LANES = 128
OMEGA = 1.6
ACCEL = (0.002, 0.0, -0.003)
SHIFT = tuple(a / OMEGA for a in ACCEL)

VELOCITIES = [
    (0, 0, 0),
    (1, 0, 0),
    (-1, 0, 0),
    (0, 1, 0),
    (0, -1, 0),
    (0, 0, 1),
    (0, 0, -1),
    (1, 1, 0),
    (-1, -1, 0),
    (1, -1, 0),
    (-1, 1, 0),
    (1, 0, 1),
    (-1, 0, -1),
    (1, 0, -1),
    (-1, 0, 1),
    (0, 1, 1),
    (0, -1, -1),
    (0, 1, -1),
    (0, -1, 1),
]
OPPOSITE = [0, 2, 1, 4, 3, 6, 5, 8, 7, 10, 9, 12, 11, 14, 13, 16, 15, 18, 17]
PAIRS = [(i, i + 1) for i in range(1, Q, 2)]
W_REST, W_AXIS, W_DIAG = 1.0 / 3.0, 1.0 / 18.0, 1.0 / 36.0

Y_CODE1, Y_CODE2, Y_CODE3, Y_POP, Y_COT = 38, 39, 40, 41, 42
Y_TILES = 43
X_EXTRA = 19
X_LANE = 20
X_RING = 4 * X_LANE
X_CODE13 = X_RING + Q + 1
X_CODE2 = X_CODE13 + 4
X_TILES = X_CODE2 + 2
EMPTY = 25
FREE = NZ - EMPTY
WEIGHTS = [W_REST] + [W_AXIS] * 6 + [W_DIAG] * 12
LEVEL = [i for i, v in enumerate(VELOCITIES) if v[2] < 1]
OWN_PHI = 4


def turned(axis, outward):
    return [i for i, v in enumerate(VELOCITIES) if v[axis] == outward and sum(map(abs, v)) == 2]


def total(values):
    values = list(values)
    while len(values) > 1:
        values = [a + b for a, b in zip(values[::2], values[1::2])] + (
            [values[-1]] if len(values) % 2 else []
        )
    return values[0]


def along(vector, three):
    terms = None
    for c, value in zip(vector, three):
        if c == 0:
            continue
        if terms is None:
            terms = value if c > 0 else -value
        else:
            terms = terms + value if c > 0 else terms - value
    return terms


def moments(f):
    plus = {i: f[i] + f[o] for i, o in PAIRS}
    minus = {i: f[i] - f[o] for i, o in PAIRS}
    rho = total([f[0]] + [plus[i] for i, _ in PAIRS])
    rinv = 1.0 / rho
    u = []
    for axis in range(3):
        terms = [
            minus[i] if VELOCITIES[i][axis] > 0 else -minus[i]
            for i, _ in PAIRS
            if VELOCITIES[i][axis] != 0
        ]
        u.append(total(terms) * rinv + SHIFT[axis])
    return plus, minus, rho, rinv, u


def coefficients(kind, phi, rinv):
    baffle = kind == 3.0
    gas = kind == 0.0
    even = jnp.where(gas, 0.0, jnp.where(baffle, 0.5 - 0.5 * OMEGA * phi, 0.5 * (1.0 - OMEGA)))
    odd = jnp.where(
        gas, 0.0, jnp.where(baffle, (1.0 - 0.5 * OMEGA) * phi - 0.5, 0.5 * (1.0 - OMEGA))
    )
    slope = jnp.where(
        baffle,
        OMEGA * phi,
        jnp.where(kind == 1.0, OMEGA, jnp.where(kind == 2.0, OMEGA * rinv, 0.0)),
    )
    return even, odd, slope


def collide(f, kind, phi, parts):
    plus, minus, rho, rinv, u = parts
    even, odd, slope = coefficients(kind, phi, rinv)
    scale = slope * rho
    rest = 1.0 - 1.5 * (u[0] * u[0] + u[1] * u[1] + u[2] * u[2])
    base = scale * rest + jnp.where(kind == 0.0, 1.0, 0.0)
    out = [None] * Q
    out[0] = 2.0 * even * f[0] + W_REST * base
    for weight, pairs in ((W_AXIS, PAIRS[:3]), (W_DIAG, PAIRS[3:])):
        flat = weight * base
        three = (3.0 * weight) * scale
        for i, o in pairs:
            cu = along(VELOCITIES[i], u)
            lin = three * cu
            ev = even * plus[i] + (flat + 1.5 * lin * cu)
            od = odd * minus[i] + lin
            out[i] = ev + od
            out[o] = ev - od
    return out


def collide_back(b, kind, phi, rho, rinv, u, state=None):
    even, odd, slope = coefficients(kind, phi, rinv)
    plus = {i: b[i] + b[o] for i, o in PAIRS}
    minus = {i: b[i] - b[o] for i, o in PAIRS}
    rest = 1.0 - 1.5 * (u[0] * u[0] + u[1] * u[1] + u[2] * u[2])
    u_half = [1.5 * c for c in u]
    weighted = W_REST * b[0]
    energy = 0.0
    vector = [0.0, 0.0, 0.0]
    for weight, pairs in ((W_AXIS, PAIRS[:3]), (W_DIAG, PAIRS[3:])):
        weighted = weighted + weight * total([plus[i] for i, _ in pairs])
        energies, parts = [], ([], [], [])
        for i, _ in pairs:
            cu = along(VELOCITIES[i], u)
            half = along(VELOCITIES[i], u_half) * plus[i]
            first = minus[i] + half
            energies.append(cu * first)
            second = first + half
            for axis in range(3):
                c = VELOCITIES[i][axis]
                if c:
                    parts[axis].append(second if c > 0 else -second)
        energy = energy + (3.0 * weight) * total(energies)
        vector = [vector[k] + (3.0 * weight) * total(parts[k]) for k in range(3)]
    energy = energy + rest * weighted
    vector = [vector[k] - (3.0 * weighted) * u[k] for k in range(3)]
    push = [slope * v for v in vector]
    inner = total([push[k] * (u[k] - SHIFT[k]) for k in range(3)])
    shared = jnp.where(kind == 2.0, 0.0, slope) * energy - inner
    out = [None] * Q
    out[0] = 2.0 * even * b[0] + shared
    for i, o in PAIRS:
        ev = even * plus[i] + shared
        od = odd * minus[i] + along(VELOCITIES[i], push)
        out[i] = ev + od
        out[o] = ev - od
    if state is None:
        return out, None
    evens = total([plus[i] * (state[i] + state[o]) for i, o in PAIRS])
    odds = total([minus[i] * (state[i] - state[o]) for i, o in PAIRS])
    term = (
        -OMEGA * (b[0] * state[0] + 0.5 * evens)
        + (1.0 - 0.5 * OMEGA) * odds
        + OMEGA * rho * energy
    )
    return out, jnp.where(kind == 3.0, term, 0.0)


def wall_masks(sign_rows, own_low, own_high, edges):
    lane = lax.broadcasted_iota(jnp.int32, (ROWS, LANES), 1)
    row = lax.broadcasted_iota(jnp.int32, (ROWS, LANES), 0)
    x_low, x_high, y_low, y_high = edges
    depth = lane % NZ
    masks = {}
    masks[2, 1] = depth == 0
    masks[2, -1] = depth == NZ - 1
    masks[1, 1] = lane < jnp.where(own_low, y_low * NZ, 0)
    masks[1, -1] = lane >= jnp.where(own_high, LANES - y_high * NZ, LANES)
    if sign_rows:
        masks[0, 1] = row < x_low
        masks[0, -1] = row >= ROWS - x_high
    return masks


def stream_tile(load, sign, masks, lane):
    cross_low, cross_high = lane >= LANES - NZ, lane < NZ
    combined = {}
    out = []
    for i, vector in enumerate(VELOCITIES):
        v = tuple(sign * c for c in vector)
        value = load(i, 0, -v[0], v[1])
        if v[1] == 1:
            value = jnp.where(cross_low, load(i, -1, -v[0], 1), value)
        elif v[1] == -1:
            value = jnp.where(cross_high, load(i, 1, -v[0], -1), value)
        amount = (v[1] * NZ + v[2]) % LANES
        if amount:
            value = pltpu.roll(value, amount, 1)
        outside = None
        if v not in combined:
            for axis in range(3):
                if v[axis] and (axis, v[axis]) in masks:
                    wall = masks[axis, v[axis]]
                    outside = wall if outside is None else outside | wall
            combined[v] = outside
        outside = combined[v]
        if outside is not None:
            value = jnp.where(outside, load(OPPOSITE[i], 0, 0, 0), value)
        out.append(value)
    return out


def iotas():
    row = lax.broadcasted_iota(jnp.int32, (ROWS, LANES), 0)
    lane = lax.broadcasted_iota(jnp.int32, (ROWS, LANES), 1)
    return row, lane, lane // NZ, lane % NZ


def columns(value, count):
    amount = (count * NZ) % LANES
    return pltpu.roll(value, amount, 1) if amount else value


def lines(value, count):
    amount = count % ROWS
    return pltpu.roll(value, amount, 0) if amount else value


class Layout:
    def __init__(self, count, guests, fills):
        self.fills = fills
        hosts = [at for at in fills if at not in guests]
        self.hosts = {at: hosts[4 * n : 4 * n + 4] for n, at in enumerate(guests)}
        self.guests = guests
        kept = [at for at in range(count) if at not in guests]
        self.place = {at: n for n, at in enumerate(kept)}
        self.size = len(kept)


class Packing:
    def __init__(self, ref, layout):
        self.ref, self.layout, self.held = ref, layout, {}

    def __setitem__(self, at, value):
        if at in self.layout.guests:
            self.held[at] = value
        else:
            self.ref[self.layout.place[at]] = value

    def finish(self):
        row, lane, column, depth = iotas()
        spare = depth >= EMPTY
        for at, value in self.held.items():
            for k, host in enumerate(self.layout.hosts[at]):
                place = self.layout.place[host]
                moved = pltpu.roll(value, EMPTY - FREE * k, 1)
                self.ref[place] = jnp.where(spare, moved, self.ref[place])
        for place in range(self.layout.size, self.ref.shape[0]):
            self.ref[place] = jnp.zeros((ROWS, LANES), jnp.float32)


class Unpacking:
    def __init__(self, source, layout):
        self.source, self.layout, self.cache = source, layout, {}
        self.changed = set(layout.guests).union(*layout.hosts.values())

    def __getitem__(self, at):
        if at not in self.cache:
            self.cache[at] = self.read(at)
        return self.cache[at]

    def read(self, at):
        row, lane, column, depth = iotas()
        layout = self.layout
        if at in layout.guests:
            value = None
            for k, host in enumerate(layout.hosts[at]):
                tile = self.source[layout.place[host]]
                moved = pltpu.roll(tile, LANES - (EMPTY - FREE * k), 1)
                value = moved if value is None else jnp.where(depth >= FREE * k, moved, value)
        else:
            value = self.source[layout.place[at]]
        if at in self.changed:
            value = jnp.where(depth >= EMPTY, layout.fills[at], value)
        return value


def layouts():
    y_fills = {2 * i + t: WEIGHTS[i] for i in LEVEL for t in range(2)}
    y_fills.update({Y_POP: W_DIAG, Y_CODE2: 0.0})
    x_fills = {X_LANE * n + i: WEIGHTS[i] for n in range(4) for i in LEVEL}
    x_fills.update({X_CODE2: 0.0, X_CODE2 + 1: 0.0})
    x_fills.update({X_RING + i: WEIGHTS[i] for i in range(Q)})
    return (
        Layout(Y_TILES, [2 * i for i in LEVEL[:6]], y_fills),
        Layout(X_TILES, [X_RING + i for i in range(15)], x_fills),
    )


class Pick:
    def __init__(self, flag, first, second):
        self.flag, self.first, self.second = flag, first, second

    def __getitem__(self, at):
        return jnp.where(self.flag, self.first[at], self.second[at])


class Deal:
    def __init__(self, even, first, second, layout):
        self.even, self.held = even, {}
        self.first, self.second = Packing(first, layout), Packing(second, layout)

    def put(self, way, at, value):
        if (-way, at) not in self.held:
            self.held[way, at] = value
            return
        other = self.held.pop((-way, at))
        up, down = (value, other) if way == 1 else (other, value)
        self.first[at] = jnp.where(self.even, up, down)
        self.second[at] = jnp.where(self.even, down, up)

    def put_both(self, at, value):
        self.first[at] = value
        self.second[at] = value

    def finish(self):
        self.first.finish()
        self.second.finish()


def is_even(axis):
    return lax.rem(lax.axis_index(axis), 2) == 0


def pack_own(
    f_hbm,
    cot_hbm,
    codes_hbm,
    panels_hbm,
    porosity_hbm,
    first_ref,
    second_ref,
    own_ref,
    state_ref,
    own_cot_ref,
    field_ref,
    names_ref,
    f_ref,
    cot_ref,
    codes_ref,
    panels_ref,
    porosity_ref,
    sems,
):
    pieces = (
        (panels_hbm, panels_ref),
        (porosity_hbm, porosity_ref),
        (f_hbm, f_ref),
        (codes_hbm, codes_ref),
        (cot_hbm, cot_ref),
    )
    copies = [
        pltpu.make_async_copy(source, target, sems.at[n])
        for n, (source, target) in enumerate(pieces)
    ]
    for copy in copies:
        copy.start()
    for copy in copies[:4]:
        copy.wait()
    deal = Deal(is_even("gy"), first_ref, second_ref, layouts()[0])
    row, lane, column, depth = iotas()
    top = depth == NZ - 1

    def tile_of(ref, i, t):
        return ref[i, :, pl.ds(t * LANES, LANES)]

    codes, phis = [], []
    for t in range(2):
        names = panels_ref[0, t * LANES], panels_ref[4, t * LANES]
        phi = jnp.where(row < 4, porosity_ref[names[0]], porosity_ref[names[1]])
        names_ref[t] = jnp.where(row < 4, names[0], names[1])
        kinds = [tile_of(codes_ref, s, t).astype(jnp.float32) for s in range(STEPS)]
        f = [tile_of(f_ref, i, t) for i in range(Q)]
        g = collide(f, kinds[0], phi, moments(f))
        for i in range(Q):
            own_ref[2 * i + t] = g[i]
            state_ref[2 * i + t] = f[i]
        for s in range(STEPS):
            field_ref[2 * s + t] = kinds[s]
        field_ref[2 * OWN_PHI + t] = phi
        codes.append([jnp.where(top, phi, kinds[1]), kinds[2], kinds[3]])
    copies[4].wait()
    for i in range(Q):
        for way in (1, -1):
            near, far = (1, 0) if way == 1 else (0, 1)
            deep = 3 - way * VELOCITIES[i][1]
            cot = tile_of(cot_ref, i, near)
            g_far = own_ref[2 * i + far]
            if way == 1:
                mixed = jnp.where(column >= deep, g_far, columns(cot, deep - 4))
            else:
                mixed = jnp.where(column < 4 - deep, g_far, columns(cot, 4 - deep))
            deal.put(way, 2 * i, mixed if far == 0 else own_ref[2 * i])
            deal.put(way, 2 * i + 1, mixed if far == 1 else own_ref[2 * i + 1])
    for way in (1, -1):
        near, far = (1, 0) if way == 1 else (0, 1)
        outer = 3 if way == 1 else 0
        deal.put(way, Y_CODE1, codes[near][0])
        deal.put(way, Y_CODE2, codes[near][1])
        outside = columns(codes[far][0], 3 - 2 * outer)
        deal.put(way, Y_CODE3, jnp.where(column == 3 - outer, outside, codes[near][2]))
        extra = None
        for k, i in enumerate(turned(1, -way)):
            value = columns(own_ref[2 * i + far], k - outer)
            extra = value if extra is None else jnp.where(column == k, value, extra)
        deal.put(way, Y_POP, extra)
        extra = None
        for k, i in enumerate(turned(1, way)):
            value = columns(tile_of(cot_ref, i, near), k - (1 if way == 1 else 2))
            extra = value if extra is None else jnp.where(column == k, value, extra)
        deal.put(way, Y_COT, extra)
    deal.finish()
    for t in range(2):
        for i in range(Q):
            own_cot_ref[2 * i + t] = tile_of(cot_ref, i, t)


def from_y(left_ref, right_ref):
    row, lane, column, depth = iotas()
    high = lane >= LANES // 2

    def population(i, c):
        if c == 1:
            return left_ref[2 * i + 1]
        if c == 4:
            return right_ref[2 * i]
        along_y = VELOCITIES[i][1]
        left, right = left_ref[2 * i], right_ref[2 * i + 1]
        if along_y == 1 and i in turned(1, 1):
            right = columns(right_ref[Y_POP], -turned(1, 1).index(i))
        if along_y == -1 and i in turned(1, -1):
            left = columns(left_ref[Y_POP], 3 - turned(1, -1).index(i))
        return jnp.where(high, left, right)

    def cotangent(i, c):
        ref, way, place, far = (left_ref, 1, 1, 0) if c == 1 else (right_ref, -1, 2, 1)
        deep = 3 - way * VELOCITIES[i][1]
        value = columns(ref[2 * i + far], way * (4 - deep))
        if i in turned(1, way):
            extra = columns(ref[Y_COT], place - turned(1, way).index(i))
            value = jnp.where(column == place, extra, value)
        return value

    def codes(s, c):
        if c == 0:
            left, right = columns(left_ref[Y_CODE3], 3), columns(right_ref[Y_CODE3], 1)
            return jnp.where(high, left, right)
        return (left_ref if c == 1 else right_ref)[(Y_CODE1, Y_CODE2, Y_CODE3)[s - 1]]

    return population, cotangent, codes


def mix_lines(deal, at, pop, cot, deep, way):
    row, lane, column, depth = iotas()
    if way == 1:
        mixed = jnp.where(row >= deep, pop, lines(cot, deep))
    else:
        mixed = jnp.where(row < ROWS - deep, pop, lines(cot, -deep))
    deal.put(way, at, mixed)


def pack_lines(deal, first, population, cotangent):
    row, lane, column, depth = iotas()

    for i in range(Q):
        pop, cot = population(i), cotangent(i)
        for way in (1, -1):
            mix_lines(deal, first + i, pop, cot, 3 - way * VELOCITIES[i][0], way)
    for way in (1, -1):
        extra = None
        for k, i in enumerate(turned(0, -way)):
            value = lines(population(i), k - (3 if way == 1 else 4))
            extra = value if extra is None else jnp.where(row == k, value, extra)
        for k, i in enumerate(turned(0, way)):
            value = lines(cotangent(i), 4 + k - (5 if way == 1 else 2))
            extra = jnp.where(row == 4 + k, value, extra)
        deal.put(way, first + X_EXTRA, extra)


def from_x(ref, n, way):
    row, lane, column, depth = iotas()
    first = X_LANE * n

    def population(i):
        value = ref[first + i]
        if i in turned(0, -way):
            place = 3 if way == 1 else 4
            extra = lines(ref[first + X_EXTRA], place - turned(0, -way).index(i))
            value = jnp.where(row == place, extra, value)
        return value

    def cotangent(i):
        value = lines(ref[first + i], -way * (3 - way * VELOCITIES[i][0]))
        if i in turned(0, way):
            place = 5 if way == 1 else 2
            extra = lines(ref[first + X_EXTRA], place - 4 - turned(0, way).index(i))
            value = jnp.where(row == place, extra, value)
        return value

    def codes(s):
        if s == 2:
            return lines(ref[X_CODE2 + n // 2], 4 * (n % 2))
        value = ref[X_CODE13 + n]
        return value if s == 1 else lines(value, -3 * way)

    return population, cotangent, codes


def pack_x(own_ref, cot_ref, field_ref, first_y_ref, second_y_ref, first_ref, second_ref):
    row, lane, column, depth = iotas()
    y_layout, x_layout = layouts()
    deal = Deal(is_even("gx"), first_ref, second_ref, x_layout)
    population, cotangent, codes = from_y(*sides(first_y_ref, second_y_ref, "gy", y_layout))

    def both_codes(at, first, second):
        second = lines(second, 4)
        deal.put(1, at, jnp.where(row >= 4, first, second))
        deal.put(-1, at, jnp.where(row < 4, first, second))

    for t in range(2):
        pack_lines(
            deal,
            X_LANE * t,
            lambda i: own_ref[2 * i + t],
            lambda i: cot_ref[2 * i + t],
        )
    for n, c in ((2, 1), (3, 4)):
        pack_lines(
            deal,
            X_LANE * n,
            lambda i: population(i, c),
            lambda i: cotangent(i, c),
        )
    for n in range(Q + 1):
        value = population(n, 0) if n < Q else codes(1, 0)
        deal.put_both(X_RING + n, value)
    for n in range(4):
        if n < 2:
            first = jnp.where(depth == NZ - 1, field_ref[2 * OWN_PHI + n], field_ref[2 + n])
            third = field_ref[6 + n]
        else:
            c = (1, 4)[n - 2]
            first, third = codes(1, c), codes(3, c)
        for way in (1, -1):
            mix_lines(deal, X_CODE13 + n, first, third, 3, way)
    both_codes(X_CODE2, field_ref[4], field_ref[5])
    both_codes(X_CODE2 + 1, codes(2, 1), codes(2, 4))
    deal.finish()


def sides(first_ref, second_ref, axis, layout):
    even = is_even(axis)
    picks = Pick(even, second_ref, first_ref), Pick(even, first_ref, second_ref)
    return [Unpacking(pick, layout) for pick in picks]


def own_rows(step=0):
    return pl.ds(ROWS + step, ROWS)


def halo_rows(step=0):
    return pl.ds({0: 2 * ROWS, -1: 2 * ROWS - 1, 1: 1}[step], ROWS)


def put_halo(ref, at, halo):
    ref[at, pl.ds(0, ROWS), :] = halo
    ref[at, halo_rows(), :] = halo


def put_ring(ref, at, own, halo):
    ref[at, own_rows(), :] = own
    put_halo(ref, at, halo)


def expand(code):
    row, lane, column, depth = iotas()
    top = depth == NZ - 1
    phi = jnp.where(top, code, 0.0)
    for step in (1, 2, 4, 8, 16):
        phi = phi + pltpu.roll(phi, LANES - step, 1)
    return jnp.where(top, 0.0, code), phi


def lay_own(c, population, cotangent, codes, code_phi, pop, cot, wide, field):
    for i in range(Q):
        pop[5 * i + c, pl.ds(2 * ROWS, ROWS), :] = population(i)
        if c:
            cot[4 * i + c - 1, own_rows(), :] = cotangent(i)
    for n in range(2):
        wide[n, c, 1] = code_phi[n]
    if c:
        field[0, c - 1, 0], field[1, c - 1, 0] = code_phi[1], code_phi[0]
        for s in (2, 3):
            field[s, c - 1, 0] = codes(s)


def lay_halo(c, below, above, pop, cot):
    row, lane, column, depth = iotas()
    for i in range(Q):
        pop[5 * i + c, pl.ds(ROWS, ROWS), :] = below[0](i)
        pop[5 * i + c, pl.ds(3 * ROWS, ROWS), :] = above[0](i)
        if c:
            put_halo(cot, 4 * i + c - 1, jnp.where(row < 4, above[1](i), below[1](i)))


def lay_codes(c, below, above, wide, field):
    row, lane, column, depth = iotas()
    before, after = expand(below[2](1)), expand(above[2](1))
    for n in range(2):
        wide[n, c, 0], wide[n, c, 2] = before[n], after[n]
    if c:
        for n, place in ((0, 1), (1, 0)):
            field[place, c - 1, 1] = jnp.where(row < 4, after[n], before[n])
        for s in (2, 3):
            field[s, c - 1, 1] = jnp.where(row < 4, above[2](s), below[2](s))


def lay_out(first_y_ref, second_y_ref, own_ref, field_ref, cot_ref, pop, cot, wide, field):
    from_left = from_y(*sides(first_y_ref, second_y_ref, "gy", layouts()[0]))
    for c in range(5):
        t = c - 2
        if t in (0, 1):
            lay_own(
                c,
                lambda i: own_ref[2 * i + t],
                lambda i: cot_ref[2 * i + t],
                lambda s: field_ref[2 * s + t],
                (field_ref[2 + t], field_ref[2 * OWN_PHI + t]),
                pop,
                cot,
                wide,
                field,
            )
        else:
            own = [functools.partial(lambda g, n: g(n, c), get) for get in from_left]
            lay_own(c, *own, expand(own[2](1)), pop, cot, wide, field)


def lay_halos(first_x_ref, second_x_ref, pop, cot, wide, field):
    below, above = sides(first_x_ref, second_x_ref, "gx", layouts()[1])
    ring = [
        (lambda i, ref=ref: ref[X_RING + i], None, lambda s, ref=ref: ref[X_RING + Q])
        for ref in (below, above)
    ]
    lay_halo(0, *ring, pop, cot)
    lay_codes(0, *ring, wide, field)
    for n, c in enumerate((2, 3, 1, 4)):
        halves = from_x(below, n, 1), from_x(above, n, -1)
        lay_halo(c, *halves, pop, cot)
        lay_codes(c, *halves, wide, field)


def steps_kernel(
    sizes,
    state_ref,
    own_field_ref,
    names_ref,
    first_x_ref,
    second_x_ref,
    *refs,
):
    adjoint_ref, panel_ref, pop_a, ring_a, wide, field, pop_b, ring_b, saved, mom, grad = refs[4:]
    size_x, size_y = sizes
    lay_halos(first_x_ref, second_x_ref, pop_a, ring_a, wide, field)

    at_x, at_y = lax.axis_index("gx"), lax.axis_index("gy")
    edges = (
        jnp.where(at_x == 0, 1, 0),
        jnp.where(at_x == size_x - 1, 1, 0),
        jnp.where(at_y == 0, 1, 0),
        jnp.where(at_y == size_y - 1, 1, 0),
    )
    row, lane, column, depth = iotas()
    after = row < 4

    def masks_of(tile, first, r):
        return wall_masks(r == 0, tile == first, tile == first + 1, edges)

    def neighbours(tile, tiles):
        if isinstance(tile, int):
            return {0: tile, -1: (tile - 1) % tiles, 1: (tile + 1) % tiles}
        return {0: tile, -1: lax.rem(tile + tiles - 1, tiles), 1: lax.rem(tile + 1, tiles)}

    def from_wide(ref, tile, r):
        step = neighbours(tile, 5)

        def load(i, tile_step, row_step, move):
            at = 5 * i + step[tile_step]
            before, own, behind = (ref[at, pl.ds(ROWS * n + row_step, ROWS), :] for n in (1, 2, 3))
            return (own, jnp.where(after, behind, before), before, behind)[r]

        return load

    def from_ring(ref, tile, tiles, r):
        step = neighbours(tile, tiles)

        def load(i, tile_step, row_step, move):
            rows = own_rows(row_step) if r == 0 else halo_rows(row_step)
            return ref[tiles * i + step[tile_step], rows, :]

        return load

    def from_outer(ref, r):
        def load(i, tile_step, row_step, move):
            rows = own_rows(row_step) if r == 0 else halo_rows(row_step)
            if tile_step:
                return ref[4 * i + (2 if tile_step < 0 else 1), rows, :]
            cut = {0: 2, 1: 1, -1: 3}[move]
            return jnp.where(column < cut, ref[4 * i + 3, rows, :], ref[4 * i, rows, :])

        return load

    def note(s, tile, r, parts):
        for n, value in enumerate(parts[2:4] + tuple(parts[4])):
            mom[s - 1, n, tile, r] = value

    def first_step(tile, carry):
        place = lax.rem(tile + 4, 5)
        halo = []
        for r in (2, 0, 3):
            f = stream_tile(from_wide(pop_a, tile, r), 1, masks_of(tile, 2, r), lane)
            parts = moments(f)
            if r == 0:
                note(1, place, 0, parts)
                for i in range(Q):
                    saved[0, i, place] = f[i]
            else:
                halo.append(parts[2:4] + tuple(parts[4]))
            at = {2: 0, 0: 1, 3: 2}[r]
            g = collide(f, wide[0, tile, at], wide[1, tile, at], parts)
            for i in range(Q):
                pop_b[5 * i + tile, pl.ds(ROWS * (at + 1), ROWS), :] = g[i]
        for n in range(5):
            mom[0, n, place, 1] = jnp.where(after, halo[1][n], halo[0][n])
        return carry

    lax.fori_loop(0, 5, first_step, 0)

    def second_step(tile, carry):
        out = []
        for r in range(2):
            f = stream_tile(from_wide(pop_b, tile + 1, r), 1, masks_of(tile, 1, r), lane)
            parts = moments(f)
            note(2, tile, r, parts)
            if r == 0:
                for i in range(Q):
                    saved[1, i, tile] = f[i]
            out.append(collide(f, field[2, tile, r], field[0, tile, r], parts))
        for i in range(Q):
            put_ring(ring_b, 4 * i + tile, out[0][i], out[1][i])
        return carry

    lax.fori_loop(0, 4, second_step, 0)

    def third_step(tile, carry):
        for r in range(2):
            f = stream_tile(from_ring(ring_b, tile, 4, r), 1, masks_of(tile, 1, r), lane)
            note(3, tile, r, moments(f))
            if r == 0:
                for i in range(Q):
                    saved[2, i, tile] = f[i]
        return carry

    lax.fori_loop(0, 4, third_step, 0)

    def back_tile(load, s, tile, r, own):
        b = stream_tile(load, -1, masks_of(4 if tile is None else tile, 1, r), lane)

        def read(get):
            return jnp.where(column < 2, get(3), get(0)) if tile is None else get(tile)

        rho, rinv, *u = [read(lambda at: mom[s - 1, n, at, r]) for n in range(5)]
        kind, phi = read(lambda at: field[s, at, r]), read(lambda at: field[0, at, r])
        state = [saved[s - 1, i, tile] for i in range(Q)] if own else None
        back, term = collide_back(b, kind, phi, rho, rinv, u, state)
        if own:
            grad[tile] = term if s == 3 else grad[tile] + term
        return back

    def last_step(tile, carry):
        out = [back_tile(from_ring(ring_a, tile, 4, r), 3, tile, r, r == 0) for r in range(2)]
        for i in range(Q):
            put_ring(ring_b, 4 * i + tile, out[0][i], out[1][i])
        return carry

    lax.fori_loop(0, 4, last_step, 0)

    for k, tile in enumerate((1, 2, None)):
        out = []
        for r in range(2):
            load = from_outer(ring_b, r) if tile is None else from_ring(ring_b, tile, 4, r)
            out.append(back_tile(load, 2, tile, r, r == 0 and tile is not None))
        for i in range(Q):
            put_ring(ring_a, 3 * i + k, out[0][i], out[1][i])

    for k, tile in enumerate((1, 2, None)):
        out = []
        for r in range(2):
            load = from_ring(ring_a, k, 3, r)
            out.append(back_tile(load, 1, tile, r, r == 0 and tile is not None))
        for i in range(Q):
            put_ring(ring_b, 3 * i + k, out[0][i], out[1][i])

    panel = lax.broadcasted_iota(jnp.int32, panel_ref.shape, 1)
    sums = jnp.zeros(panel_ref.shape, jnp.float32)
    for t in range(2):
        b = stream_tile(from_ring(ring_b, t, 3, 0), -1, masks_of(t, 0, 0), lane)
        f = [state_ref[2 * i + t] for i in range(Q)]
        kind, phi = own_field_ref[t], own_field_ref[2 * OWN_PHI + t]
        _, _, rho, rinv, u = moments(f)
        back, term = collide_back(b, kind, phi, rho, rinv, u, f)
        for i in range(Q):
            adjoint_ref[i, :, pl.ds(t * LANES, LANES)] = back[i]
        term = term + grad[t + 1]
        for part in range(2):
            amount = jnp.sum(jnp.where((row < 4) == (part == 0), term, 0.0))
            name = names_ref[t, 4 * part : 4 * part + 1, 0:1]
            sums = sums + jnp.where(panel == name, amount, 0.0)
    panel_ref[...] = sums


def add_panels(parts_ref, out_ref):
    out_ref[...] = jnp.sum(parts_ref[...], axis=0)


VMEM = pl.BlockSpec(memory_space=pltpu.VMEM)
HBM = pl.BlockSpec(memory_space=pltpu.HBM)


def shape_of(*dims):
    return jax.ShapeDtypeStruct(dims, jnp.float32)


def tiles_of(count):
    return shape_of(count, ROWS, LANES)


def on_device(sizes, checkpoint, cotangent, cell_codes, porosity, baffle_index):
    size_x, size_y = sizes
    panels = porosity.shape[0]
    devices = size_x * size_y
    y_layout, x_layout = layouts()

    def call(kernel, out_shape, in_specs, scratch=(), name=None, aliases={}):
        return pl.pallas_call(
            kernel,
            out_shape=out_shape,
            in_specs=in_specs,
            out_specs=jax.tree.map(lambda _: VMEM, out_shape),
            scratch_shapes=scratch,
            input_output_aliases=aliases,
            compiler_params=pltpu.CompilerParams(vmem_limit_bytes=32 * 1024 * 1024),
            name=name,
        )

    def swap(value, axis, size):
        return lax.ppermute(value, axis, [(i, i ^ 1) for i in range(size) if i ^ 1 < size])

    def swap_between(value, axis, size):
        pairs = [(i, i + 1) for i in range(1, size - 1, 2)]
        return lax.ppermute(value, axis, pairs + [(j, i) for i, j in pairs])

    arguments = [
        pltpu.with_memory_space_constraint(value, pltpu.HBM)
        for value in (checkpoint, cotangent, cell_codes, baffle_index, porosity)
    ]
    first_y, second_y, own, state, cot, field, names = call(
        pack_own,
        (tiles_of(y_layout.size),) * 2
        + (tiles_of(2 * Q),) * 3
        + (tiles_of(2 * OWN_PHI + 2), jax.ShapeDtypeStruct((2, ROWS, LANES), jnp.int32)),
        [HBM] * 5,
        [
            pltpu.VMEM((Q, ROWS, 2 * LANES), jnp.float32),
            pltpu.VMEM((Q, ROWS, 2 * LANES), jnp.float32),
            pltpu.VMEM((STEPS, ROWS, 2 * LANES), jnp.int32),
            pltpu.SMEM(baffle_index.shape, jnp.int32),
            pltpu.SMEM(porosity.shape, jnp.float32),
            pltpu.SemaphoreType.DMA((5,)),
        ],
        name="pack_own",
    )(*arguments)
    first_y = swap(first_y, "gy", size_y)
    second_y = swap_between(second_y, "gy", size_y)
    first_x, second_x = call(
        pack_x,
        (tiles_of(x_layout.size), tiles_of(x_layout.size + 1)),
        [VMEM] * 5,
        name="pack_x",
    )(own, cot, field, first_y, second_y)
    second_x = swap_between(second_x, "gx", size_x)
    first_x = swap(first_x, "gx", size_x)
    spaces = (
        shape_of(5 * Q, 5 * ROWS, LANES),
        shape_of(4 * Q, 3 * ROWS, LANES),
        shape_of(2, 5, 3, ROWS, LANES),
        shape_of(4, 4, 2, ROWS, LANES),
    )
    laid = call(lay_out, spaces, [VMEM] * 5, name="lay_out")(first_y, second_y, own, field, cot)
    adjoint, sums, *_ = call(
        functools.partial(steps_kernel, sizes),
        (shape_of(Q, ROWS, 2 * LANES), shape_of(devices, panels)) + spaces,
        [VMEM] * 9,
        [
            pltpu.VMEM((5 * Q, 5 * ROWS, LANES), jnp.float32),
            pltpu.VMEM((4 * Q, 3 * ROWS, LANES), jnp.float32),
            pltpu.VMEM((3, Q, 5, ROWS, LANES), jnp.float32),
            pltpu.VMEM((3, 5, 5, 2, ROWS, LANES), jnp.float32),
            pltpu.VMEM((4, ROWS, LANES), jnp.float32),
        ],
        name="steps",
        aliases={5 + n: 2 + n for n in range(4)},
    )(state, field, names, first_x, second_x, *laid)
    gathered = lax.all_to_all(sums, ("gx", "gy"), 0, 0, tiled=True)
    totals = call(add_panels, shape_of(1, panels), [VMEM], name="add_panels")(
        gathered.reshape(devices, 1, panels)
    )
    return adjoint, totals.reshape(panels)


def solution(mesh):
    sizes = (mesh.shape["gx"], mesh.shape["gy"])
    in_specs = (P(None, "gx", "gy"), P(None, "gx", "gy"), P(None, "gx", "gy"), P(), P("gx", "gy"))
    out_specs = (P(None, "gx", "gy"), P())
    return jax.shard_map(
        functools.partial(on_device, sizes),
        mesh=mesh,
        in_specs=in_specs,
        out_specs=out_specs,
        check_vma=False,
    )
```

```python
import functools

import jax
import jax.numpy as jnp
import numpy as np
from jax import lax
from jax.experimental import pallas as pl
from jax.experimental.pallas import tpu as pltpu
from jax.sharding import PartitionSpec as P

Q = 19
STEPS = 4
NZ = 32
ROWS = 8
LANES = 128
OMEGA = 1.6
ACCEL = (0.002, 0.0, -0.003)
SHIFT = tuple(a / OMEGA for a in ACCEL)

VELOCITIES = [
    (0, 0, 0),
    (1, 0, 0),
    (-1, 0, 0),
    (0, 1, 0),
    (0, -1, 0),
    (0, 0, 1),
    (0, 0, -1),
    (1, 1, 0),
    (-1, -1, 0),
    (1, -1, 0),
    (-1, 1, 0),
    (1, 0, 1),
    (-1, 0, -1),
    (1, 0, -1),
    (-1, 0, 1),
    (0, 1, 1),
    (0, -1, -1),
    (0, 1, -1),
    (0, -1, 1),
]
OPPOSITE = [0, 2, 1, 4, 3, 6, 5, 8, 7, 10, 9, 12, 11, 14, 13, 16, 15, 18, 17]
PAIRS = [(i, i + 1) for i in range(1, Q, 2)]
W_REST, W_AXIS, W_DIAG = 1.0 / 3.0, 1.0 / 18.0, 1.0 / 36.0

Y_CODE1, Y_CODE2, Y_CODE3, Y_POP, Y_COT = 38, 39, 40, 41, 42
Y_TILES = 43
X_EXTRA = 19
X_LANE = 20
X_SIDE = 2 * X_LANE
X_RING = 4 * X_LANE
X_CODE13 = X_RING + Q + 1
X_CODE2 = X_CODE13 + 4
X_TILES = X_CODE2 + 2
EMPTY = 25
FREE = NZ - EMPTY
WEIGHTS = [W_REST] + [W_AXIS] * 6 + [W_DIAG] * 12
LEVEL = [i for i, v in enumerate(VELOCITIES) if v[2] < 1]
OWN_PHI = 4


def turned(axis, outward):
    return [i for i, v in enumerate(VELOCITIES) if v[axis] == outward and sum(map(abs, v)) == 2]


def total(values):
    values = list(values)
    while len(values) > 1:
        values = [a + b for a, b in zip(values[::2], values[1::2])] + (
            [values[-1]] if len(values) % 2 else []
        )
    return values[0]


def along(vector, three):
    terms = None
    for c, value in zip(vector, three):
        if c == 0:
            continue
        if terms is None:
            terms = value if c > 0 else -value
        else:
            terms = terms + value if c > 0 else terms - value
    return terms


def moments(f):
    plus = {i: f[i] + f[o] for i, o in PAIRS}
    minus = {i: f[i] - f[o] for i, o in PAIRS}
    rho = total([f[0]] + [plus[i] for i, _ in PAIRS])
    rinv = 1.0 / rho
    u = []
    for axis in range(3):
        terms = [
            minus[i] if VELOCITIES[i][axis] > 0 else -minus[i]
            for i, _ in PAIRS
            if VELOCITIES[i][axis] != 0
        ]
        u.append(total(terms) * rinv + SHIFT[axis])
    return plus, minus, rho, rinv, u


def coefficients(kind, phi, rinv):
    baffle = kind == 3.0
    gas = kind == 0.0
    even = jnp.where(gas, 0.0, jnp.where(baffle, 0.5 - 0.5 * OMEGA * phi, 0.5 * (1.0 - OMEGA)))
    odd = jnp.where(
        gas, 0.0, jnp.where(baffle, (1.0 - 0.5 * OMEGA) * phi - 0.5, 0.5 * (1.0 - OMEGA))
    )
    slope = jnp.where(
        baffle,
        OMEGA * phi,
        jnp.where(kind == 1.0, OMEGA, jnp.where(kind == 2.0, OMEGA * rinv, 0.0)),
    )
    return even, odd, slope


def collide(f, kind, phi, parts):
    plus, minus, rho, rinv, u = parts
    even, odd, slope = coefficients(kind, phi, rinv)
    scale = slope * rho
    rest = 1.0 - 1.5 * (u[0] * u[0] + u[1] * u[1] + u[2] * u[2])
    base = scale * rest + jnp.where(kind == 0.0, 1.0, 0.0)
    out = [None] * Q
    out[0] = 2.0 * even * f[0] + W_REST * base
    for weight, pairs in ((W_AXIS, PAIRS[:3]), (W_DIAG, PAIRS[3:])):
        flat = weight * base
        three = (3.0 * weight) * scale
        for i, o in pairs:
            cu = along(VELOCITIES[i], u)
            lin = three * cu
            ev = even * plus[i] + (flat + 1.5 * lin * cu)
            od = odd * minus[i] + lin
            out[i] = ev + od
            out[o] = ev - od
    return out


def collide_back(b, kind, phi, rho, rinv, u, state=None):
    even, odd, slope = coefficients(kind, phi, rinv)
    plus = {i: b[i] + b[o] for i, o in PAIRS}
    minus = {i: b[i] - b[o] for i, o in PAIRS}
    rest = 1.0 - 1.5 * (u[0] * u[0] + u[1] * u[1] + u[2] * u[2])
    u_half = [1.5 * c for c in u]
    weighted = W_REST * b[0]
    energy = 0.0
    vector = [0.0, 0.0, 0.0]
    for weight, pairs in ((W_AXIS, PAIRS[:3]), (W_DIAG, PAIRS[3:])):
        weighted = weighted + weight * total([plus[i] for i, _ in pairs])
        energies, parts = [], ([], [], [])
        for i, _ in pairs:
            cu = along(VELOCITIES[i], u)
            half = along(VELOCITIES[i], u_half) * plus[i]
            first = minus[i] + half
            energies.append(cu * first)
            second = first + half
            for axis in range(3):
                c = VELOCITIES[i][axis]
                if c:
                    parts[axis].append(second if c > 0 else -second)
        energy = energy + (3.0 * weight) * total(energies)
        vector = [vector[k] + (3.0 * weight) * total(parts[k]) for k in range(3)]
    energy = energy + rest * weighted
    vector = [vector[k] - (3.0 * weighted) * u[k] for k in range(3)]
    push = [slope * v for v in vector]
    inner = total([push[k] * (u[k] - SHIFT[k]) for k in range(3)])
    shared = jnp.where(kind == 2.0, 0.0, slope) * energy - inner
    out = [None] * Q
    out[0] = 2.0 * even * b[0] + shared
    for i, o in PAIRS:
        ev = even * plus[i] + shared
        od = odd * minus[i] + along(VELOCITIES[i], push)
        out[i] = ev + od
        out[o] = ev - od
    if state is None:
        return out, None
    evens = total([plus[i] * (state[i] + state[o]) for i, o in PAIRS])
    odds = total([minus[i] * (state[i] - state[o]) for i, o in PAIRS])
    term = (
        -OMEGA * (b[0] * state[0] + 0.5 * evens)
        + (1.0 - 0.5 * OMEGA) * odds
        + OMEGA * rho * energy
    )
    return out, jnp.where(kind == 3.0, term, 0.0)


def wall_masks(sign_rows, own_low, own_high, edges):
    lane = lax.broadcasted_iota(jnp.int32, (ROWS, LANES), 1)
    row = lax.broadcasted_iota(jnp.int32, (ROWS, LANES), 0)
    x_low, x_high, y_low, y_high = edges
    depth = lane % NZ
    masks = {}
    masks[2, 1] = depth == 0
    masks[2, -1] = depth == NZ - 1
    masks[1, 1] = lane < jnp.where(own_low, y_low * NZ, 0)
    masks[1, -1] = lane >= jnp.where(own_high, LANES - y_high * NZ, LANES)
    if sign_rows:
        masks[0, 1] = row < x_low
        masks[0, -1] = row >= ROWS - x_high
    return masks


def stream_tile(load, sign, masks, lane):
    cross_low, cross_high = lane >= LANES - NZ, lane < NZ
    combined = {}
    out = []
    for i, vector in enumerate(VELOCITIES):
        v = tuple(sign * c for c in vector)
        value = load(i, 0, -v[0], v[1])
        if v[1] == 1:
            value = jnp.where(cross_low, load(i, -1, -v[0], 1), value)
        elif v[1] == -1:
            value = jnp.where(cross_high, load(i, 1, -v[0], -1), value)
        amount = (v[1] * NZ + v[2]) % LANES
        if amount:
            value = pltpu.roll(value, amount, 1)
        outside = None
        if v not in combined:
            for axis in range(3):
                if v[axis] and (axis, v[axis]) in masks:
                    wall = masks[axis, v[axis]]
                    outside = wall if outside is None else outside | wall
            combined[v] = outside
        outside = combined[v]
        if outside is not None:
            value = jnp.where(outside, load(OPPOSITE[i], 0, 0, 0), value)
        out.append(value)
    return out


def iotas():
    row = lax.broadcasted_iota(jnp.int32, (ROWS, LANES), 0)
    lane = lax.broadcasted_iota(jnp.int32, (ROWS, LANES), 1)
    return row, lane, lane // NZ, lane % NZ


def columns(value, count):
    amount = (count * NZ) % LANES
    return pltpu.roll(value, amount, 1) if amount else value


def lines(value, count):
    amount = count % ROWS
    return pltpu.roll(value, amount, 0) if amount else value


class Layout:
    def __init__(self, count, guests, fills):
        self.fills = fills
        hosts = [at for at in fills if at not in guests]
        self.hosts = {at: hosts[4 * n : 4 * n + 4] for n, at in enumerate(guests)}
        self.guests = guests
        kept = [at for at in range(count) if at not in guests]
        self.place = {at: n for n, at in enumerate(kept)}
        self.size = len(kept)


class Packing:
    def __init__(self, ref, layout):
        self.ref, self.layout, self.held = ref, layout, {}

    def __setitem__(self, at, value):
        if at in self.layout.guests:
            self.held[at] = value
        else:
            self.ref[self.layout.place[at]] = value

    def finish(self):
        row, lane, column, depth = iotas()
        spare = depth >= EMPTY
        for at, value in self.held.items():
            for k, host in enumerate(self.layout.hosts[at]):
                place = self.layout.place[host]
                moved = pltpu.roll(value, EMPTY - FREE * k, 1)
                self.ref[place] = jnp.where(spare, moved, self.ref[place])
        for place in range(self.layout.size, self.ref.shape[0]):
            self.ref[place] = jnp.zeros((ROWS, LANES), jnp.float32)


class Unpacking:
    def __init__(self, source, layout):
        self.source, self.layout, self.cache = source, layout, {}
        self.changed = set(layout.guests).union(*layout.hosts.values())

    def __getitem__(self, at):
        if at not in self.cache:
            self.cache[at] = self.read(at)
        return self.cache[at]

    def read(self, at):
        row, lane, column, depth = iotas()
        layout = self.layout
        if at in layout.guests:
            value = None
            for k, host in enumerate(layout.hosts[at]):
                tile = self.source[layout.place[host]]
                moved = pltpu.roll(tile, LANES - (EMPTY - FREE * k), 1)
                value = moved if value is None else jnp.where(depth >= FREE * k, moved, value)
        else:
            value = self.source[layout.place[at]]
        if at in self.changed:
            value = jnp.where(depth >= EMPTY, layout.fills[at], value)
        return value


def layouts():
    y_fills = {2 * i + t: WEIGHTS[i] for i in LEVEL for t in range(2)}
    y_fills.update({Y_POP: W_DIAG, Y_CODE2: 0.0})
    x_fills = {X_LANE * n + i: WEIGHTS[i] for n in range(4) for i in LEVEL}
    side = {at: fill for at, fill in x_fills.items() if at < X_SIDE}
    rest = {at - X_SIDE: fill for at, fill in x_fills.items() if at >= X_SIDE}
    rest.update({X_CODE2 - X_SIDE: 0.0, X_CODE2 + 1 - X_SIDE: 0.0})
    rest.update({X_RING - X_SIDE + i: WEIGHTS[i] for i in range(Q)})
    ring = [X_RING - X_SIDE + i for i in range(9)]
    return (
        Layout(Y_TILES, [2 * i for i in LEVEL[:6]], y_fills),
        Layout(X_SIDE, LEVEL[:5], side),
        Layout(X_TILES - X_SIDE, ring, rest),
    )


class Pick:
    def __init__(self, flag, first, second):
        self.flag, self.first, self.second = flag, first, second

    def __getitem__(self, at):
        return jnp.where(self.flag, self.first[at], self.second[at])


class Deal:
    def __init__(self, even, first, second, layout, skip=0):
        self.even, self.skip, self.held = even, skip, {}
        self.first, self.second = Packing(first, layout), Packing(second, layout)

    def put(self, way, at, value):
        if (-way, at) not in self.held:
            self.held[way, at] = value
            return
        other = self.held.pop((-way, at))
        up, down = (value, other) if way == 1 else (other, value)
        self.first[at - self.skip] = jnp.where(self.even, up, down)
        self.second[at - self.skip] = jnp.where(self.even, down, up)

    def put_both(self, at, value):
        self.first[at - self.skip] = value
        self.second[at - self.skip] = value

    def finish(self):
        self.first.finish()
        self.second.finish()


class Joined:
    def __init__(self, first, second, cut):
        self.first, self.second, self.cut = first, second, cut

    def __getitem__(self, at):
        return self.first[at] if at < self.cut else self.second[at - self.cut]


def is_even(axis):
    return lax.rem(lax.axis_index(axis), 2) == 0


def pack_own(
    f_hbm,
    cot_hbm,
    codes_hbm,
    panels_hbm,
    porosity_hbm,
    first_ref,
    second_ref,
    first_side_ref,
    second_side_ref,
    own_ref,
    state_ref,
    own_cot_ref,
    field_ref,
    names_ref,
    f_ref,
    cot_ref,
    codes_ref,
    panels_ref,
    porosity_ref,
    sems,
):
    pieces = (
        (panels_hbm, panels_ref),
        (porosity_hbm, porosity_ref),
        (f_hbm, f_ref),
        (codes_hbm, codes_ref),
        (cot_hbm, cot_ref),
    )
    copies = [
        pltpu.make_async_copy(source, target, sems.at[n])
        for n, (source, target) in enumerate(pieces)
    ]
    for copy in copies:
        copy.start()
    for copy in copies[:4]:
        copy.wait()
    y_layout, side_layout, _ = layouts()
    deal = Deal(is_even("gy"), first_ref, second_ref, y_layout)
    side = Deal(is_even("gx"), first_side_ref, second_side_ref, side_layout)
    row, lane, column, depth = iotas()
    top = depth == NZ - 1

    def tile_of(ref, i, t):
        return ref[i, :, pl.ds(t * LANES, LANES)]

    codes, phis = [], []
    for t in range(2):
        names = panels_ref[0, t * LANES], panels_ref[4, t * LANES]
        phi = jnp.where(row < 4, porosity_ref[names[0]], porosity_ref[names[1]])
        names_ref[t] = jnp.where(row < 4, names[0], names[1])
        kinds = [tile_of(codes_ref, s, t).astype(jnp.float32) for s in range(STEPS)]
        f = [tile_of(f_ref, i, t) for i in range(Q)]
        g = collide(f, kinds[0], phi, moments(f))
        for i in range(Q):
            own_ref[2 * i + t] = g[i]
            state_ref[2 * i + t] = f[i]
        for s in range(STEPS):
            field_ref[2 * s + t] = kinds[s]
        field_ref[2 * OWN_PHI + t] = phi
        codes.append([jnp.where(top, phi, kinds[1]), kinds[2], kinds[3]])
    copies[4].wait()
    for i in range(Q):
        for way in (1, -1):
            near, far = (1, 0) if way == 1 else (0, 1)
            deep = 3 - way * VELOCITIES[i][1]
            cot = tile_of(cot_ref, i, near)
            g_far = own_ref[2 * i + far]
            if way == 1:
                mixed = jnp.where(column >= deep, g_far, columns(cot, deep - 4))
            else:
                mixed = jnp.where(column < 4 - deep, g_far, columns(cot, 4 - deep))
            deal.put(way, 2 * i, mixed if far == 0 else own_ref[2 * i])
            deal.put(way, 2 * i + 1, mixed if far == 1 else own_ref[2 * i + 1])
    for way in (1, -1):
        near, far = (1, 0) if way == 1 else (0, 1)
        outer = 3 if way == 1 else 0
        deal.put(way, Y_CODE1, codes[near][0])
        deal.put(way, Y_CODE2, codes[near][1])
        outside = columns(codes[far][0], 3 - 2 * outer)
        deal.put(way, Y_CODE3, jnp.where(column == 3 - outer, outside, codes[near][2]))
        extra = None
        for k, i in enumerate(turned(1, -way)):
            value = columns(own_ref[2 * i + far], k - outer)
            extra = value if extra is None else jnp.where(column == k, value, extra)
        deal.put(way, Y_POP, extra)
        extra = None
        for k, i in enumerate(turned(1, way)):
            value = columns(tile_of(cot_ref, i, near), k - (1 if way == 1 else 2))
            extra = value if extra is None else jnp.where(column == k, value, extra)
        deal.put(way, Y_COT, extra)
    deal.finish()
    for t in range(2):
        for i in range(Q):
            own_cot_ref[2 * i + t] = tile_of(cot_ref, i, t)
        pack_lines(
            side,
            X_LANE * t,
            lambda i: own_ref[2 * i + t],
            lambda i: tile_of(cot_ref, i, t),
        )
    side.finish()


def from_y(left_ref, right_ref):
    row, lane, column, depth = iotas()
    high = lane >= LANES // 2

    def population(i, c):
        if c == 1:
            return left_ref[2 * i + 1]
        if c == 4:
            return right_ref[2 * i]
        along_y = VELOCITIES[i][1]
        left, right = left_ref[2 * i], right_ref[2 * i + 1]
        if along_y == 1 and i in turned(1, 1):
            right = columns(right_ref[Y_POP], -turned(1, 1).index(i))
        if along_y == -1 and i in turned(1, -1):
            left = columns(left_ref[Y_POP], 3 - turned(1, -1).index(i))
        return jnp.where(high, left, right)

    def cotangent(i, c):
        ref, way, place, far = (left_ref, 1, 1, 0) if c == 1 else (right_ref, -1, 2, 1)
        deep = 3 - way * VELOCITIES[i][1]
        value = columns(ref[2 * i + far], way * (4 - deep))
        if i in turned(1, way):
            extra = columns(ref[Y_COT], place - turned(1, way).index(i))
            value = jnp.where(column == place, extra, value)
        return value

    def codes(s, c):
        if c == 0:
            left, right = columns(left_ref[Y_CODE3], 3), columns(right_ref[Y_CODE3], 1)
            return jnp.where(high, left, right)
        return (left_ref if c == 1 else right_ref)[(Y_CODE1, Y_CODE2, Y_CODE3)[s - 1]]

    return population, cotangent, codes


def mix_lines(deal, at, pop, cot, deep, way):
    row, lane, column, depth = iotas()
    if way == 1:
        mixed = jnp.where(row >= deep, pop, lines(cot, deep))
    else:
        mixed = jnp.where(row < ROWS - deep, pop, lines(cot, -deep))
    deal.put(way, at, mixed)


def pack_lines(deal, first, population, cotangent):
    row, lane, column, depth = iotas()

    for i in range(Q):
        pop, cot = population(i), cotangent(i)
        for way in (1, -1):
            mix_lines(deal, first + i, pop, cot, 3 - way * VELOCITIES[i][0], way)
    for way in (1, -1):
        extra = None
        for k, i in enumerate(turned(0, -way)):
            value = lines(population(i), k - (3 if way == 1 else 4))
            extra = value if extra is None else jnp.where(row == k, value, extra)
        for k, i in enumerate(turned(0, way)):
            value = lines(cotangent(i), 4 + k - (5 if way == 1 else 2))
            extra = jnp.where(row == 4 + k, value, extra)
        deal.put(way, first + X_EXTRA, extra)


def from_x(ref, n, way):
    row, lane, column, depth = iotas()
    first = X_LANE * n

    def population(i):
        value = ref[first + i]
        if i in turned(0, -way):
            place = 3 if way == 1 else 4
            extra = lines(ref[first + X_EXTRA], place - turned(0, -way).index(i))
            value = jnp.where(row == place, extra, value)
        return value

    def cotangent(i):
        value = lines(ref[first + i], -way * (3 - way * VELOCITIES[i][0]))
        if i in turned(0, way):
            place = 5 if way == 1 else 2
            extra = lines(ref[first + X_EXTRA], place - 4 - turned(0, way).index(i))
            value = jnp.where(row == place, extra, value)
        return value

    def codes(s):
        if s == 2:
            return lines(ref[X_CODE2 + n // 2], 4 * (n % 2))
        value = ref[X_CODE13 + n]
        return value if s == 1 else lines(value, -3 * way)

    return population, cotangent, codes


def pack_x(field_ref, first_y_ref, second_y_ref, first_ref, second_ref):
    row, lane, column, depth = iotas()
    y_layout, _, layout = layouts()
    deal = Deal(is_even("gx"), first_ref, second_ref, layout, X_SIDE)
    population, cotangent, codes = from_y(*sides(first_y_ref, second_y_ref, "gy", y_layout))

    def both_codes(at, first, second):
        second = lines(second, 4)
        deal.put(1, at, jnp.where(row >= 4, first, second))
        deal.put(-1, at, jnp.where(row < 4, first, second))

    for n, c in ((2, 1), (3, 4)):
        pack_lines(
            deal,
            X_LANE * n,
            lambda i: population(i, c),
            lambda i: cotangent(i, c),
        )
    for n in range(Q + 1):
        value = population(n, 0) if n < Q else codes(1, 0)
        deal.put_both(X_RING + n, value)
    for n in range(4):
        if n < 2:
            first = jnp.where(depth == NZ - 1, field_ref[2 * OWN_PHI + n], field_ref[2 + n])
            third = field_ref[6 + n]
        else:
            c = (1, 4)[n - 2]
            first, third = codes(1, c), codes(3, c)
        for way in (1, -1):
            mix_lines(deal, X_CODE13 + n, first, third, 3, way)
    both_codes(X_CODE2, field_ref[4], field_ref[5])
    both_codes(X_CODE2 + 1, codes(2, 1), codes(2, 4))
    deal.finish()


def sides(first_ref, second_ref, axis, layout):
    even = is_even(axis)
    picks = Pick(even, second_ref, first_ref), Pick(even, first_ref, second_ref)
    return [Unpacking(pick, layout) for pick in picks]


def own_rows(step=0):
    return pl.ds(ROWS + step, ROWS)


def halo_rows(step=0):
    return pl.ds({0: 2 * ROWS, -1: 2 * ROWS - 1, 1: 1}[step], ROWS)


def put_halo(ref, at, halo):
    ref[at, pl.ds(0, ROWS), :] = halo
    ref[at, halo_rows(), :] = halo


def put_ring(ref, at, own, halo):
    ref[at, own_rows(), :] = own
    put_halo(ref, at, halo)


def expand(code):
    row, lane, column, depth = iotas()
    top = depth == NZ - 1
    phi = jnp.where(top, code, 0.0)
    for step in (1, 2, 4, 8, 16):
        phi = phi + pltpu.roll(phi, LANES - step, 1)
    return jnp.where(top, 0.0, code), phi


def lay_own(c, population, cotangent, codes, code_phi, pop, cot, wide, field):
    for i in range(Q):
        pop[5 * i + c, pl.ds(2 * ROWS, ROWS), :] = population(i)
        if c:
            cot[4 * i + c - 1, own_rows(), :] = cotangent(i)
    for n in range(2):
        wide[n, c, 1] = code_phi[n]
    if c:
        field[0, c - 1, 0], field[1, c - 1, 0] = code_phi[1], code_phi[0]
        for s in (2, 3):
            field[s, c - 1, 0] = codes(s)


def lay_halo(c, below, above, pop, cot):
    row, lane, column, depth = iotas()
    for i in range(Q):
        pop[5 * i + c, pl.ds(ROWS, ROWS), :] = below[0](i)
        pop[5 * i + c, pl.ds(3 * ROWS, ROWS), :] = above[0](i)
        if c:
            put_halo(cot, 4 * i + c - 1, jnp.where(row < 4, above[1](i), below[1](i)))


def lay_codes(c, below, above, wide, field):
    row, lane, column, depth = iotas()
    before, after = expand(below[2](1)), expand(above[2](1))
    for n in range(2):
        wide[n, c, 0], wide[n, c, 2] = before[n], after[n]
    if c:
        for n, place in ((0, 1), (1, 0)):
            field[place, c - 1, 1] = jnp.where(row < 4, after[n], before[n])
        for s in (2, 3):
            field[s, c - 1, 1] = jnp.where(row < 4, above[2](s), below[2](s))


def lay_out(first_y_ref, second_y_ref, own_ref, field_ref, cot_ref, pop, cot, wide, field):
    from_left = from_y(*sides(first_y_ref, second_y_ref, "gy", layouts()[0]))
    for c in range(5):
        t = c - 2
        if t in (0, 1):
            lay_own(
                c,
                lambda i: own_ref[2 * i + t],
                lambda i: cot_ref[2 * i + t],
                lambda s: field_ref[2 * s + t],
                (field_ref[2 + t], field_ref[2 * OWN_PHI + t]),
                pop,
                cot,
                wide,
                field,
            )
        else:
            own = [functools.partial(lambda g, n: g(n, c), get) for get in from_left]
            lay_own(c, *own, expand(own[2](1)), pop, cot, wide, field)


def lay_halos(below, above, pop, cot, wide, field):
    ring = [
        (lambda i, ref=ref: ref[X_RING + i], None, lambda s, ref=ref: ref[X_RING + Q])
        for ref in (below, above)
    ]
    lay_halo(0, *ring, pop, cot)
    lay_codes(0, *ring, wide, field)
    for n, c in enumerate((2, 3, 1, 4)):
        halves = from_x(below, n, 1), from_x(above, n, -1)
        lay_halo(c, *halves, pop, cot)
        lay_codes(c, *halves, wide, field)


def steps_kernel(
    sizes,
    state_ref,
    own_field_ref,
    names_ref,
    first_side_ref,
    second_side_ref,
    first_x_ref,
    second_x_ref,
    *refs,
):
    adjoint_ref, panel_ref, pop_a, ring_a, wide, field, pop_b, ring_b, saved, mom, grad = refs[4:]
    size_x, size_y = sizes
    _, side_layout, rest_layout = layouts()
    below, above = (
        Joined(side, rest, X_SIDE)
        for side, rest in zip(
            sides(first_side_ref, second_side_ref, "gx", side_layout),
            sides(first_x_ref, second_x_ref, "gx", rest_layout),
        )
    )
    lay_halos(below, above, pop_a, ring_a, wide, field)

    at_x, at_y = lax.axis_index("gx"), lax.axis_index("gy")
    edges = (
        jnp.where(at_x == 0, 1, 0),
        jnp.where(at_x == size_x - 1, 1, 0),
        jnp.where(at_y == 0, 1, 0),
        jnp.where(at_y == size_y - 1, 1, 0),
    )
    row, lane, column, depth = iotas()
    after = row < 4

    def masks_of(tile, first, r):
        return wall_masks(r == 0, tile == first, tile == first + 1, edges)

    def neighbours(tile, tiles):
        if isinstance(tile, int):
            return {0: tile, -1: (tile - 1) % tiles, 1: (tile + 1) % tiles}
        return {0: tile, -1: lax.rem(tile + tiles - 1, tiles), 1: lax.rem(tile + 1, tiles)}

    def from_wide(ref, tile, r):
        step = neighbours(tile, 5)

        def load(i, tile_step, row_step, move):
            at = 5 * i + step[tile_step]
            before, own, behind = (ref[at, pl.ds(ROWS * n + row_step, ROWS), :] for n in (1, 2, 3))
            return (own, jnp.where(after, behind, before), before, behind)[r]

        return load

    def from_ring(ref, tile, tiles, r):
        step = neighbours(tile, tiles)

        def load(i, tile_step, row_step, move):
            rows = own_rows(row_step) if r == 0 else halo_rows(row_step)
            return ref[tiles * i + step[tile_step], rows, :]

        return load

    def from_outer(ref, r):
        def load(i, tile_step, row_step, move):
            rows = own_rows(row_step) if r == 0 else halo_rows(row_step)
            if tile_step:
                return ref[4 * i + (2 if tile_step < 0 else 1), rows, :]
            cut = {0: 2, 1: 1, -1: 3}[move]
            return jnp.where(column < cut, ref[4 * i + 3, rows, :], ref[4 * i, rows, :])

        return load

    def note(s, tile, r, parts):
        for n, value in enumerate(parts[2:4] + tuple(parts[4])):
            mom[s - 1, n, tile, r] = value

    def first_step(tile, carry):
        place = lax.rem(tile + 4, 5)
        halo = []
        for r in (2, 0, 3):
            f = stream_tile(from_wide(pop_a, tile, r), 1, masks_of(tile, 2, r), lane)
            parts = moments(f)
            if r == 0:
                note(1, place, 0, parts)
                for i in range(Q):
                    saved[0, i, place] = f[i]
            else:
                halo.append(parts[2:4] + tuple(parts[4]))
            at = {2: 0, 0: 1, 3: 2}[r]
            g = collide(f, wide[0, tile, at], wide[1, tile, at], parts)
            for i in range(Q):
                pop_b[5 * i + tile, pl.ds(ROWS * (at + 1), ROWS), :] = g[i]
        for n in range(5):
            mom[0, n, place, 1] = jnp.where(after, halo[1][n], halo[0][n])
        return carry

    lax.fori_loop(0, 5, first_step, 0)

    def second_step(tile, carry):
        out = []
        for r in range(2):
            f = stream_tile(from_wide(pop_b, tile + 1, r), 1, masks_of(tile, 1, r), lane)
            parts = moments(f)
            note(2, tile, r, parts)
            if r == 0:
                for i in range(Q):
                    saved[1, i, tile] = f[i]
            out.append(collide(f, field[2, tile, r], field[0, tile, r], parts))
        for i in range(Q):
            put_ring(ring_b, 4 * i + tile, out[0][i], out[1][i])
        return carry

    lax.fori_loop(0, 4, second_step, 0)

    def third_step(tile, carry):
        for r in range(2):
            f = stream_tile(from_ring(ring_b, tile, 4, r), 1, masks_of(tile, 1, r), lane)
            note(3, tile, r, moments(f))
            if r == 0:
                for i in range(Q):
                    saved[2, i, tile] = f[i]
        return carry

    lax.fori_loop(0, 4, third_step, 0)

    def back_tile(load, s, tile, r, own):
        b = stream_tile(load, -1, masks_of(4 if tile is None else tile, 1, r), lane)

        def read(get):
            return jnp.where(column < 2, get(3), get(0)) if tile is None else get(tile)

        rho, rinv, *u = [read(lambda at: mom[s - 1, n, at, r]) for n in range(5)]
        kind, phi = read(lambda at: field[s, at, r]), read(lambda at: field[0, at, r])
        state = [saved[s - 1, i, tile] for i in range(Q)] if own else None
        back, term = collide_back(b, kind, phi, rho, rinv, u, state)
        if own:
            grad[tile] = term if s == 3 else grad[tile] + term
        return back

    def last_step(tile, carry):
        out = [back_tile(from_ring(ring_a, tile, 4, r), 3, tile, r, r == 0) for r in range(2)]
        for i in range(Q):
            put_ring(ring_b, 4 * i + tile, out[0][i], out[1][i])
        return carry

    lax.fori_loop(0, 4, last_step, 0)

    for k, tile in enumerate((1, 2, None)):
        out = []
        for r in range(2):
            load = from_outer(ring_b, r) if tile is None else from_ring(ring_b, tile, 4, r)
            out.append(back_tile(load, 2, tile, r, r == 0 and tile is not None))
        for i in range(Q):
            put_ring(ring_a, 3 * i + k, out[0][i], out[1][i])

    for k, tile in enumerate((1, 2, None)):
        out = []
        for r in range(2):
            load = from_ring(ring_a, k, 3, r)
            out.append(back_tile(load, 1, tile, r, r == 0 and tile is not None))
        for i in range(Q):
            put_ring(ring_b, 3 * i + k, out[0][i], out[1][i])

    panel = lax.broadcasted_iota(jnp.int32, panel_ref.shape, 1)
    sums = jnp.zeros(panel_ref.shape, jnp.float32)
    for t in range(2):
        b = stream_tile(from_ring(ring_b, t, 3, 0), -1, masks_of(t, 0, 0), lane)
        f = [state_ref[2 * i + t] for i in range(Q)]
        kind, phi = own_field_ref[t], own_field_ref[2 * OWN_PHI + t]
        _, _, rho, rinv, u = moments(f)
        back, term = collide_back(b, kind, phi, rho, rinv, u, f)
        for i in range(Q):
            adjoint_ref[i, :, pl.ds(t * LANES, LANES)] = back[i]
        term = term + grad[t + 1]
        for part in range(2):
            amount = jnp.sum(jnp.where((row < 4) == (part == 0), term, 0.0))
            name = names_ref[t, 4 * part : 4 * part + 1, 0:1]
            sums = sums + jnp.where(panel == name, amount, 0.0)
    panel_ref[...] = sums


def add_panels(parts_ref, out_ref):
    out_ref[...] = jnp.sum(parts_ref[...], axis=0)


VMEM = pl.BlockSpec(memory_space=pltpu.VMEM)
HBM = pl.BlockSpec(memory_space=pltpu.HBM)


def shape_of(*dims):
    return jax.ShapeDtypeStruct(dims, jnp.float32)


def tiles_of(count):
    return shape_of(count, ROWS, LANES)


def on_device(sizes, checkpoint, cotangent, cell_codes, porosity, baffle_index):
    size_x, size_y = sizes
    panels = porosity.shape[0]
    devices = size_x * size_y
    y_layout, side_layout, rest_layout = layouts()

    def call(kernel, out_shape, in_specs, scratch=(), name=None, aliases={}):
        return pl.pallas_call(
            kernel,
            out_shape=out_shape,
            in_specs=in_specs,
            out_specs=jax.tree.map(lambda _: VMEM, out_shape),
            scratch_shapes=scratch,
            input_output_aliases=aliases,
            compiler_params=pltpu.CompilerParams(vmem_limit_bytes=32 * 1024 * 1024),
            name=name,
        )

    def swap(value, axis, size):
        return lax.ppermute(value, axis, [(i, i ^ 1) for i in range(size) if i ^ 1 < size])

    def swap_between(value, axis, size):
        pairs = [(i, i + 1) for i in range(1, size - 1, 2)]
        return lax.ppermute(value, axis, pairs + [(j, i) for i, j in pairs])

    arguments = [
        pltpu.with_memory_space_constraint(value, pltpu.HBM)
        for value in (checkpoint, cotangent, cell_codes, baffle_index, porosity)
    ]
    first_y, second_y, first_side, second_side, own, state, cot, field, names = call(
        pack_own,
        (tiles_of(y_layout.size),) * 2
        + (tiles_of(side_layout.size), tiles_of(rest_layout.size + 8))
        + (tiles_of(2 * Q),) * 3
        + (tiles_of(2 * OWN_PHI + 2), jax.ShapeDtypeStruct((2, ROWS, LANES), jnp.int32)),
        [HBM] * 5,
        [
            pltpu.VMEM((Q, ROWS, 2 * LANES), jnp.float32),
            pltpu.VMEM((Q, ROWS, 2 * LANES), jnp.float32),
            pltpu.VMEM((STEPS, ROWS, 2 * LANES), jnp.int32),
            pltpu.SMEM(baffle_index.shape, jnp.int32),
            pltpu.SMEM(porosity.shape, jnp.float32),
            pltpu.SemaphoreType.DMA((5,)),
        ],
        name="pack_own",
    )(*arguments)
    second_y = swap_between(second_y, "gy", size_y)
    first_y = swap(first_y, "gy", size_y)
    second_side = swap_between(second_side, "gx", size_x)
    first_side = swap(first_side, "gx", size_x)
    first_x, second_x = call(
        pack_x,
        (tiles_of(rest_layout.size), tiles_of(rest_layout.size + 1)),
        [VMEM] * 3,
        name="pack_x",
    )(field, first_y, second_y)
    second_x = swap_between(second_x, "gx", size_x)
    first_x = swap(first_x, "gx", size_x)

    spaces = (
        shape_of(5 * Q, 5 * ROWS, LANES),
        shape_of(4 * Q, 3 * ROWS, LANES),
        shape_of(2, 5, 3, ROWS, LANES),
        shape_of(4, 4, 2, ROWS, LANES),
    )
    laid = call(lay_out, spaces, [VMEM] * 5, name="lay_out")(first_y, second_y, own, field, cot)
    adjoint, sums, *_ = call(
        functools.partial(steps_kernel, sizes),
        (shape_of(Q, ROWS, 2 * LANES), shape_of(devices, panels)) + spaces,
        [VMEM] * 11,
        [
            pltpu.VMEM((5 * Q, 5 * ROWS, LANES), jnp.float32),
            pltpu.VMEM((4 * Q, 3 * ROWS, LANES), jnp.float32),
            pltpu.VMEM((3, Q, 5, ROWS, LANES), jnp.float32),
            pltpu.VMEM((3, 5, 5, 2, ROWS, LANES), jnp.float32),
            pltpu.VMEM((4, ROWS, LANES), jnp.float32),
        ],
        name="steps",
        aliases={7 + n: 2 + n for n in range(4)},
    )(state, field, names, first_side, second_side, first_x, second_x, *laid)
    gathered = lax.all_to_all(sums, ("gx", "gy"), 0, 0, tiled=True)
    totals = call(add_panels, shape_of(1, panels), [VMEM], name="add_panels")(
        gathered.reshape(devices, 1, panels)
    )
    return adjoint, totals.reshape(panels)


def solution(mesh):
    sizes = (mesh.shape["gx"], mesh.shape["gy"])
    in_specs = (P(None, "gx", "gy"), P(None, "gx", "gy"), P(None, "gx", "gy"), P(), P("gx", "gy"))
    out_specs = (P(None, "gx", "gy"), P())
    return jax.shard_map(
        functools.partial(on_device, sizes),
        mesh=mesh,
        in_specs=in_specs,
        out_specs=out_specs,
        check_vma=False,
    )
```

```python
import functools

import jax
import jax.numpy as jnp
import numpy as np
from jax import lax
from jax.experimental import pallas as pl
from jax.experimental.pallas import tpu as pltpu
from jax.sharding import PartitionSpec as P

Q = 19
STEPS = 4
NZ = 32
ROWS = 8
LANES = 128
OMEGA = 1.6
ACCEL = (0.002, 0.0, -0.003)
SHIFT = tuple(a / OMEGA for a in ACCEL)

VELOCITIES = [
    (0, 0, 0),
    (1, 0, 0),
    (-1, 0, 0),
    (0, 1, 0),
    (0, -1, 0),
    (0, 0, 1),
    (0, 0, -1),
    (1, 1, 0),
    (-1, -1, 0),
    (1, -1, 0),
    (-1, 1, 0),
    (1, 0, 1),
    (-1, 0, -1),
    (1, 0, -1),
    (-1, 0, 1),
    (0, 1, 1),
    (0, -1, -1),
    (0, 1, -1),
    (0, -1, 1),
]
OPPOSITE = [0, 2, 1, 4, 3, 6, 5, 8, 7, 10, 9, 12, 11, 14, 13, 16, 15, 18, 17]
PAIRS = [(i, i + 1) for i in range(1, Q, 2)]
W_REST, W_AXIS, W_DIAG = 1.0 / 3.0, 1.0 / 18.0, 1.0 / 36.0

Y_CODE1, Y_CODE2, Y_CODE3, Y_POP, Y_COT = 38, 39, 40, 41, 42
Y_TILES = 43
X_EXTRA = 19
X_LANE = 20
X_SIDE = 2 * X_LANE
X_RING = 4 * X_LANE
X_CODE13 = X_RING + Q + 1
X_CODE2 = X_CODE13 + 4
X_TILES = X_CODE2 + 2
EMPTY = 25
FREE = NZ - EMPTY
WEIGHTS = [W_REST] + [W_AXIS] * 6 + [W_DIAG] * 12
LEVEL = [i for i, v in enumerate(VELOCITIES) if v[2] < 1]
OWN_PHI = 4


def turned(axis, outward):
    return [i for i, v in enumerate(VELOCITIES) if v[axis] == outward and sum(map(abs, v)) == 2]


def total(values):
    values = list(values)
    while len(values) > 1:
        values = [a + b for a, b in zip(values[::2], values[1::2])] + (
            [values[-1]] if len(values) % 2 else []
        )
    return values[0]


def along(vector, three):
    terms = None
    for c, value in zip(vector, three):
        if c == 0:
            continue
        if terms is None:
            terms = value if c > 0 else -value
        else:
            terms = terms + value if c > 0 else terms - value
    return terms


def moments(f):
    plus = {i: f[i] + f[o] for i, o in PAIRS}
    minus = {i: f[i] - f[o] for i, o in PAIRS}
    rho = total([f[0]] + [plus[i] for i, _ in PAIRS])
    rinv = 1.0 / rho
    u = []
    for axis in range(3):
        terms = [
            minus[i] if VELOCITIES[i][axis] > 0 else -minus[i]
            for i, _ in PAIRS
            if VELOCITIES[i][axis] != 0
        ]
        u.append(total(terms) * rinv + SHIFT[axis])
    return plus, minus, rho, rinv, u


def coefficients(kind, phi, rinv):
    baffle = kind == 3.0
    gas = kind == 0.0
    even = jnp.where(gas, 0.0, jnp.where(baffle, 0.5 - 0.5 * OMEGA * phi, 0.5 * (1.0 - OMEGA)))
    odd = jnp.where(
        gas, 0.0, jnp.where(baffle, (1.0 - 0.5 * OMEGA) * phi - 0.5, 0.5 * (1.0 - OMEGA))
    )
    slope = jnp.where(
        baffle,
        OMEGA * phi,
        jnp.where(kind == 1.0, OMEGA, jnp.where(kind == 2.0, OMEGA * rinv, 0.0)),
    )
    return even, odd, slope


def collide(f, kind, phi, parts):
    plus, minus, rho, rinv, u = parts
    even, odd, slope = coefficients(kind, phi, rinv)
    scale = slope * rho
    rest = 1.0 - 1.5 * (u[0] * u[0] + u[1] * u[1] + u[2] * u[2])
    base = scale * rest + jnp.where(kind == 0.0, 1.0, 0.0)
    out = [None] * Q
    out[0] = 2.0 * even * f[0] + W_REST * base
    for weight, pairs in ((W_AXIS, PAIRS[:3]), (W_DIAG, PAIRS[3:])):
        flat = weight * base
        three = (3.0 * weight) * scale
        for i, o in pairs:
            cu = along(VELOCITIES[i], u)
            lin = three * cu
            ev = even * plus[i] + (flat + 1.5 * lin * cu)
            od = odd * minus[i] + lin
            out[i] = ev + od
            out[o] = ev - od
    return out


def collide_back(b, kind, phi, rho, rinv, u, state=None):
    even, odd, slope = coefficients(kind, phi, rinv)
    plus = {i: b[i] + b[o] for i, o in PAIRS}
    minus = {i: b[i] - b[o] for i, o in PAIRS}
    rest = 1.0 - 1.5 * (u[0] * u[0] + u[1] * u[1] + u[2] * u[2])
    u_half = [1.5 * c for c in u]
    weighted = W_REST * b[0]
    energy = 0.0
    vector = [0.0, 0.0, 0.0]
    for weight, pairs in ((W_AXIS, PAIRS[:3]), (W_DIAG, PAIRS[3:])):
        weighted = weighted + weight * total([plus[i] for i, _ in pairs])
        energies, parts = [], ([], [], [])
        for i, _ in pairs:
            cu = along(VELOCITIES[i], u)
            half = along(VELOCITIES[i], u_half) * plus[i]
            first = minus[i] + half
            energies.append(cu * first)
            second = first + half
            for axis in range(3):
                c = VELOCITIES[i][axis]
                if c:
                    parts[axis].append(second if c > 0 else -second)
        energy = energy + (3.0 * weight) * total(energies)
        vector = [vector[k] + (3.0 * weight) * total(parts[k]) for k in range(3)]
    energy = energy + rest * weighted
    vector = [vector[k] - (3.0 * weighted) * u[k] for k in range(3)]
    push = [slope * v for v in vector]
    inner = total([push[k] * (u[k] - SHIFT[k]) for k in range(3)])
    shared = jnp.where(kind == 2.0, 0.0, slope) * energy - inner
    out = [None] * Q
    out[0] = 2.0 * even * b[0] + shared
    for i, o in PAIRS:
        ev = even * plus[i] + shared
        od = odd * minus[i] + along(VELOCITIES[i], push)
        out[i] = ev + od
        out[o] = ev - od
    if state is None:
        return out, None
    evens = total([plus[i] * (state[i] + state[o]) for i, o in PAIRS])
    odds = total([minus[i] * (state[i] - state[o]) for i, o in PAIRS])
    term = (
        -OMEGA * (b[0] * state[0] + 0.5 * evens)
        + (1.0 - 0.5 * OMEGA) * odds
        + OMEGA * rho * energy
    )
    return out, jnp.where(kind == 3.0, term, 0.0)


def wall_masks(sign_rows, own_low, own_high, edges):
    lane = lax.broadcasted_iota(jnp.int32, (ROWS, LANES), 1)
    row = lax.broadcasted_iota(jnp.int32, (ROWS, LANES), 0)
    x_low, x_high, y_low, y_high = edges
    depth = lane % NZ
    masks = {}
    masks[2, 1] = depth == 0
    masks[2, -1] = depth == NZ - 1
    masks[1, 1] = lane < jnp.where(own_low, y_low * NZ, 0)
    masks[1, -1] = lane >= jnp.where(own_high, LANES - y_high * NZ, LANES)
    if sign_rows:
        masks[0, 1] = row < x_low
        masks[0, -1] = row >= ROWS - x_high
    return masks


def stream_tile(load, sign, masks, lane):
    cross_low, cross_high = lane >= LANES - NZ, lane < NZ
    combined = {}
    out = []
    for i, vector in enumerate(VELOCITIES):
        v = tuple(sign * c for c in vector)
        value = load(i, 0, -v[0], v[1])
        if v[1] == 1:
            value = jnp.where(cross_low, load(i, -1, -v[0], 1), value)
        elif v[1] == -1:
            value = jnp.where(cross_high, load(i, 1, -v[0], -1), value)
        amount = (v[1] * NZ + v[2]) % LANES
        if amount:
            value = pltpu.roll(value, amount, 1)
        outside = None
        if v not in combined:
            for axis in range(3):
                if v[axis] and (axis, v[axis]) in masks:
                    wall = masks[axis, v[axis]]
                    outside = wall if outside is None else outside | wall
            combined[v] = outside
        outside = combined[v]
        if outside is not None:
            value = jnp.where(outside, load(OPPOSITE[i], 0, 0, 0), value)
        out.append(value)
    return out


def iotas():
    row = lax.broadcasted_iota(jnp.int32, (ROWS, LANES), 0)
    lane = lax.broadcasted_iota(jnp.int32, (ROWS, LANES), 1)
    return row, lane, lane // NZ, lane % NZ


def columns(value, count):
    amount = (count * NZ) % LANES
    return pltpu.roll(value, amount, 1) if amount else value


def lines(value, count):
    amount = count % ROWS
    return pltpu.roll(value, amount, 0) if amount else value


class Layout:
    def __init__(self, count, guests, fills):
        self.fills = fills
        hosts = [at for at in fills if at not in guests]
        self.hosts = {at: hosts[4 * n : 4 * n + 4] for n, at in enumerate(guests)}
        self.guests = guests
        kept = [at for at in range(count) if at not in guests]
        self.place = {at: n for n, at in enumerate(kept)}
        self.size = len(kept)


class Packing:
    def __init__(self, ref, layout):
        self.ref, self.layout, self.held = ref, layout, {}

    def __setitem__(self, at, value):
        if at in self.layout.guests:
            self.held[at] = value
        else:
            self.ref[self.layout.place[at]] = value

    def finish(self):
        row, lane, column, depth = iotas()
        spare = depth >= EMPTY
        for at, value in self.held.items():
            for k, host in enumerate(self.layout.hosts[at]):
                place = self.layout.place[host]
                moved = pltpu.roll(value, EMPTY - FREE * k, 1)
                self.ref[place] = jnp.where(spare, moved, self.ref[place])
        for place in range(self.layout.size, self.ref.shape[0]):
            self.ref[place] = jnp.zeros((ROWS, LANES), jnp.float32)


class Unpacking:
    def __init__(self, source, layout):
        self.source, self.layout, self.cache = source, layout, {}
        self.changed = set(layout.guests).union(*layout.hosts.values())

    def __getitem__(self, at):
        if at not in self.cache:
            self.cache[at] = self.read(at)
        return self.cache[at]

    def read(self, at):
        row, lane, column, depth = iotas()
        layout = self.layout
        if at in layout.guests:
            value = None
            for k, host in enumerate(layout.hosts[at]):
                tile = self.source[layout.place[host]]
                moved = pltpu.roll(tile, LANES - (EMPTY - FREE * k), 1)
                value = moved if value is None else jnp.where(depth >= FREE * k, moved, value)
        else:
            value = self.source[layout.place[at]]
        if at in self.changed:
            value = jnp.where(depth >= EMPTY, layout.fills[at], value)
        return value


def layouts():
    y_fills = {2 * i + t: WEIGHTS[i] for i in LEVEL for t in range(2)}
    y_fills.update({Y_POP: W_DIAG, Y_CODE2: 0.0})
    x_fills = {X_LANE * n + i: WEIGHTS[i] for n in range(4) for i in LEVEL}
    side = {at: fill for at, fill in x_fills.items() if at < X_SIDE}
    rest = {at - X_SIDE: fill for at, fill in x_fills.items() if at >= X_SIDE}
    rest.update({X_CODE2 - X_SIDE: 0.0, X_CODE2 + 1 - X_SIDE: 0.0})
    rest.update({X_RING - X_SIDE + i: WEIGHTS[i] for i in range(Q)})
    ring = [X_RING - X_SIDE + i for i in range(9)]
    return (
        Layout(Y_TILES, [2 * i for i in LEVEL[:6]], y_fills),
        Layout(X_SIDE, LEVEL[:5], side),
        Layout(X_TILES - X_SIDE, ring, rest),
    )


class Pick:
    def __init__(self, flag, first, second):
        self.flag, self.first, self.second = flag, first, second

    def __getitem__(self, at):
        return jnp.where(self.flag, self.first[at], self.second[at])


class Deal:
    def __init__(self, even, first, second, layout, skip=0):
        self.even, self.skip, self.held = even, skip, {}
        self.first, self.second = Packing(first, layout), Packing(second, layout)

    def put(self, way, at, value):
        if (-way, at) not in self.held:
            self.held[way, at] = value
            return
        other = self.held.pop((-way, at))
        up, down = (value, other) if way == 1 else (other, value)
        self.first[at - self.skip] = jnp.where(self.even, up, down)
        self.second[at - self.skip] = jnp.where(self.even, down, up)

    def put_both(self, at, value):
        self.first[at - self.skip] = value
        self.second[at - self.skip] = value

    def finish(self):
        self.first.finish()
        self.second.finish()


class Shifted:
    def __init__(self, ref, start):
        self.ref, self.start = ref, start

    def __getitem__(self, at):
        return self.ref[at - self.start]


def is_even(axis):
    return lax.rem(lax.axis_index(axis), 2) == 0


def pack_own(
    f_hbm,
    cot_hbm,
    codes_hbm,
    panels_hbm,
    porosity_hbm,
    first_ref,
    second_ref,
    first_side_ref,
    second_side_ref,
    own_ref,
    state_ref,
    own_cot_ref,
    field_ref,
    names_ref,
    f_ref,
    cot_ref,
    codes_ref,
    panels_ref,
    porosity_ref,
    sems,
):
    pieces = (
        (panels_hbm, panels_ref),
        (porosity_hbm, porosity_ref),
        (f_hbm, f_ref),
        (codes_hbm, codes_ref),
        (cot_hbm, cot_ref),
    )
    copies = [
        pltpu.make_async_copy(source, target, sems.at[n])
        for n, (source, target) in enumerate(pieces)
    ]
    for copy in copies:
        copy.start()
    for copy in copies[:4]:
        copy.wait()
    y_layout, side_layout, _ = layouts()
    deal = Deal(is_even("gy"), first_ref, second_ref, y_layout)
    side = Deal(is_even("gx"), first_side_ref, second_side_ref, side_layout)
    row, lane, column, depth = iotas()
    top = depth == NZ - 1

    def tile_of(ref, i, t):
        return ref[i, :, pl.ds(t * LANES, LANES)]

    codes, phis = [], []
    for t in range(2):
        names = panels_ref[0, t * LANES], panels_ref[4, t * LANES]
        phi = jnp.where(row < 4, porosity_ref[names[0]], porosity_ref[names[1]])
        names_ref[t] = jnp.where(row < 4, names[0], names[1])
        kinds = [tile_of(codes_ref, s, t).astype(jnp.float32) for s in range(STEPS)]
        f = [tile_of(f_ref, i, t) for i in range(Q)]
        g = collide(f, kinds[0], phi, moments(f))
        for i in range(Q):
            own_ref[2 * i + t] = g[i]
            state_ref[2 * i + t] = f[i]
        for s in range(STEPS):
            field_ref[2 * s + t] = kinds[s]
        field_ref[2 * OWN_PHI + t] = phi
        codes.append([jnp.where(top, phi, kinds[1]), kinds[2], kinds[3]])
    copies[4].wait()
    for i in range(Q):
        for way in (1, -1):
            near, far = (1, 0) if way == 1 else (0, 1)
            deep = 3 - way * VELOCITIES[i][1]
            cot = tile_of(cot_ref, i, near)
            g_far = own_ref[2 * i + far]
            if way == 1:
                mixed = jnp.where(column >= deep, g_far, columns(cot, deep - 4))
            else:
                mixed = jnp.where(column < 4 - deep, g_far, columns(cot, 4 - deep))
            deal.put(way, 2 * i, mixed if far == 0 else own_ref[2 * i])
            deal.put(way, 2 * i + 1, mixed if far == 1 else own_ref[2 * i + 1])
    for way in (1, -1):
        near, far = (1, 0) if way == 1 else (0, 1)
        outer = 3 if way == 1 else 0
        deal.put(way, Y_CODE1, codes[near][0])
        deal.put(way, Y_CODE2, codes[near][1])
        outside = columns(codes[far][0], 3 - 2 * outer)
        deal.put(way, Y_CODE3, jnp.where(column == 3 - outer, outside, codes[near][2]))
        extra = None
        for k, i in enumerate(turned(1, -way)):
            value = columns(own_ref[2 * i + far], k - outer)
            extra = value if extra is None else jnp.where(column == k, value, extra)
        deal.put(way, Y_POP, extra)
        extra = None
        for k, i in enumerate(turned(1, way)):
            value = columns(tile_of(cot_ref, i, near), k - (1 if way == 1 else 2))
            extra = value if extra is None else jnp.where(column == k, value, extra)
        deal.put(way, Y_COT, extra)
    deal.finish()
    for t in range(2):
        for i in range(Q):
            own_cot_ref[2 * i + t] = tile_of(cot_ref, i, t)
        pack_lines(
            side,
            X_LANE * t,
            lambda i: own_ref[2 * i + t],
            lambda i: tile_of(cot_ref, i, t),
        )
    side.finish()


def from_y(left_ref, right_ref):
    row, lane, column, depth = iotas()
    high = lane >= LANES // 2

    def population(i, c):
        if c == 1:
            return left_ref[2 * i + 1]
        if c == 4:
            return right_ref[2 * i]
        along_y = VELOCITIES[i][1]
        left, right = left_ref[2 * i], right_ref[2 * i + 1]
        if along_y == 1 and i in turned(1, 1):
            right = columns(right_ref[Y_POP], -turned(1, 1).index(i))
        if along_y == -1 and i in turned(1, -1):
            left = columns(left_ref[Y_POP], 3 - turned(1, -1).index(i))
        return jnp.where(high, left, right)

    def cotangent(i, c):
        ref, way, place, far = (left_ref, 1, 1, 0) if c == 1 else (right_ref, -1, 2, 1)
        deep = 3 - way * VELOCITIES[i][1]
        value = columns(ref[2 * i + far], way * (4 - deep))
        if i in turned(1, way):
            extra = columns(ref[Y_COT], place - turned(1, way).index(i))
            value = jnp.where(column == place, extra, value)
        return value

    def codes(s, c):
        if c == 0:
            left, right = columns(left_ref[Y_CODE3], 3), columns(right_ref[Y_CODE3], 1)
            return jnp.where(high, left, right)
        return (left_ref if c == 1 else right_ref)[(Y_CODE1, Y_CODE2, Y_CODE3)[s - 1]]

    return population, cotangent, codes


def mix_lines(deal, at, pop, cot, deep, way):
    row, lane, column, depth = iotas()
    if way == 1:
        mixed = jnp.where(row >= deep, pop, lines(cot, deep))
    else:
        mixed = jnp.where(row < ROWS - deep, pop, lines(cot, -deep))
    deal.put(way, at, mixed)


def pack_lines(deal, first, population, cotangent):
    row, lane, column, depth = iotas()

    for i in range(Q):
        pop, cot = population(i), cotangent(i)
        for way in (1, -1):
            mix_lines(deal, first + i, pop, cot, 3 - way * VELOCITIES[i][0], way)
    for way in (1, -1):
        extra = None
        for k, i in enumerate(turned(0, -way)):
            value = lines(population(i), k - (3 if way == 1 else 4))
            extra = value if extra is None else jnp.where(row == k, value, extra)
        for k, i in enumerate(turned(0, way)):
            value = lines(cotangent(i), 4 + k - (5 if way == 1 else 2))
            extra = jnp.where(row == 4 + k, value, extra)
        deal.put(way, first + X_EXTRA, extra)


def from_x(ref, n, way):
    row, lane, column, depth = iotas()
    first = X_LANE * n

    def population(i):
        value = ref[first + i]
        if i in turned(0, -way):
            place = 3 if way == 1 else 4
            extra = lines(ref[first + X_EXTRA], place - turned(0, -way).index(i))
            value = jnp.where(row == place, extra, value)
        return value

    def cotangent(i):
        value = lines(ref[first + i], -way * (3 - way * VELOCITIES[i][0]))
        if i in turned(0, way):
            place = 5 if way == 1 else 2
            extra = lines(ref[first + X_EXTRA], place - 4 - turned(0, way).index(i))
            value = jnp.where(row == place, extra, value)
        return value

    def codes(s):
        if s == 2:
            return lines(ref[X_CODE2 + n // 2], 4 * (n % 2))
        value = ref[X_CODE13 + n]
        return value if s == 1 else lines(value, -3 * way)

    return population, cotangent, codes


def pack_x(field_ref, first_y_ref, second_y_ref, first_ref, second_ref):
    row, lane, column, depth = iotas()
    y_layout, _, layout = layouts()
    deal = Deal(is_even("gx"), first_ref, second_ref, layout, X_SIDE)
    population, cotangent, codes = from_y(*sides(first_y_ref, second_y_ref, "gy", y_layout))

    def both_codes(at, first, second):
        second = lines(second, 4)
        deal.put(1, at, jnp.where(row >= 4, first, second))
        deal.put(-1, at, jnp.where(row < 4, first, second))

    for n, c in ((2, 1), (3, 4)):
        pack_lines(
            deal,
            X_LANE * n,
            lambda i: population(i, c),
            lambda i: cotangent(i, c),
        )
    for n in range(Q + 1):
        value = population(n, 0) if n < Q else codes(1, 0)
        deal.put_both(X_RING + n, value)
    for n in range(4):
        if n < 2:
            first = jnp.where(depth == NZ - 1, field_ref[2 * OWN_PHI + n], field_ref[2 + n])
            third = field_ref[6 + n]
        else:
            c = (1, 4)[n - 2]
            first, third = codes(1, c), codes(3, c)
        for way in (1, -1):
            mix_lines(deal, X_CODE13 + n, first, third, 3, way)
    both_codes(X_CODE2, field_ref[4], field_ref[5])
    both_codes(X_CODE2 + 1, codes(2, 1), codes(2, 4))
    deal.finish()


def sides(first_ref, second_ref, axis, layout):
    even = is_even(axis)
    picks = Pick(even, second_ref, first_ref), Pick(even, first_ref, second_ref)
    return [Unpacking(pick, layout) for pick in picks]


def own_rows(step=0):
    return pl.ds(ROWS + step, ROWS)


def halo_rows(step=0):
    return pl.ds({0: 2 * ROWS, -1: 2 * ROWS - 1, 1: 1}[step], ROWS)


def put_halo(ref, at, halo):
    ref[at, pl.ds(0, ROWS), :] = halo
    ref[at, halo_rows(), :] = halo


def put_ring(ref, at, own, halo):
    ref[at, own_rows(), :] = own
    put_halo(ref, at, halo)


def expand(code):
    row, lane, column, depth = iotas()
    top = depth == NZ - 1
    phi = jnp.where(top, code, 0.0)
    for step in (1, 2, 4, 8, 16):
        phi = phi + pltpu.roll(phi, LANES - step, 1)
    return jnp.where(top, 0.0, code), phi


def lay_own(c, population, cotangent, codes, code_phi, pop, cot, wide, field):
    for i in range(Q):
        pop[5 * i + c, pl.ds(2 * ROWS, ROWS), :] = population(i)
        if c:
            cot[4 * i + c - 1, own_rows(), :] = cotangent(i)
    for n in range(2):
        wide[n, c, 1] = code_phi[n]
    if c:
        field[0, c - 1, 0], field[1, c - 1, 0] = code_phi[1], code_phi[0]
        for s in (2, 3):
            field[s, c - 1, 0] = codes(s)


def lay_halo(c, below, above, pop, cot):
    row, lane, column, depth = iotas()
    for i in range(Q):
        pop[5 * i + c, pl.ds(ROWS, ROWS), :] = below[0](i)
        pop[5 * i + c, pl.ds(3 * ROWS, ROWS), :] = above[0](i)
        if c:
            put_halo(cot, 4 * i + c - 1, jnp.where(row < 4, above[1](i), below[1](i)))


def lay_codes(c, below, above, wide, field):
    row, lane, column, depth = iotas()
    before, after = expand(below[2](1)), expand(above[2](1))
    for n in range(2):
        wide[n, c, 0], wide[n, c, 2] = before[n], after[n]
    if c:
        for n, place in ((0, 1), (1, 0)):
            field[place, c - 1, 1] = jnp.where(row < 4, after[n], before[n])
        for s in (2, 3):
            field[s, c - 1, 1] = jnp.where(row < 4, above[2](s), below[2](s))


def lay_out(
    first_y_ref,
    second_y_ref,
    first_side_ref,
    second_side_ref,
    own_ref,
    field_ref,
    cot_ref,
    pop,
    cot,
    wide,
    field,
):
    y_layout, side_layout, _ = layouts()
    from_left = from_y(*sides(first_y_ref, second_y_ref, "gy", y_layout))
    below, above = sides(first_side_ref, second_side_ref, "gx", side_layout)
    for c in range(5):
        t = c - 2
        if t in (0, 1):
            lay_own(
                c,
                lambda i: own_ref[2 * i + t],
                lambda i: cot_ref[2 * i + t],
                lambda s: field_ref[2 * s + t],
                (field_ref[2 + t], field_ref[2 * OWN_PHI + t]),
                pop,
                cot,
                wide,
                field,
            )
            lay_halo(c, from_x(below, t, 1), from_x(above, t, -1), pop, cot)
        else:
            own = [functools.partial(lambda g, n: g(n, c), get) for get in from_left]
            lay_own(c, *own, expand(own[2](1)), pop, cot, wide, field)


def lay_halos(below, above, pop, cot, wide, field):
    ring = [
        (lambda i, ref=ref: ref[X_RING + i], None, lambda s, ref=ref: ref[X_RING + Q])
        for ref in (below, above)
    ]
    lay_halo(0, *ring, pop, cot)
    lay_codes(0, *ring, wide, field)
    for n, c in enumerate((2, 3, 1, 4)):
        halves = from_x(below, n, 1), from_x(above, n, -1)
        if n > 1:
            lay_halo(c, *halves, pop, cot)
        lay_codes(c, *halves, wide, field)


def steps_kernel(
    sizes,
    state_ref,
    own_field_ref,
    names_ref,
    first_x_ref,
    second_x_ref,
    *refs,
):
    adjoint_ref, panel_ref, pop_a, ring_a, wide, field, pop_b, ring_b, saved, mom, grad = refs[4:]
    size_x, size_y = sizes
    halves = sides(first_x_ref, second_x_ref, "gx", layouts()[2])
    below, above = (Shifted(ref, X_SIDE) for ref in halves)
    lay_halos(below, above, pop_a, ring_a, wide, field)

    at_x, at_y = lax.axis_index("gx"), lax.axis_index("gy")
    edges = (
        jnp.where(at_x == 0, 1, 0),
        jnp.where(at_x == size_x - 1, 1, 0),
        jnp.where(at_y == 0, 1, 0),
        jnp.where(at_y == size_y - 1, 1, 0),
    )
    row, lane, column, depth = iotas()
    after = row < 4

    def masks_of(tile, first, r):
        return wall_masks(r == 0, tile == first, tile == first + 1, edges)

    def neighbours(tile, tiles):
        if isinstance(tile, int):
            return {0: tile, -1: (tile - 1) % tiles, 1: (tile + 1) % tiles}
        return {0: tile, -1: lax.rem(tile + tiles - 1, tiles), 1: lax.rem(tile + 1, tiles)}

    def from_wide(ref, tile, r):
        step = neighbours(tile, 5)

        def load(i, tile_step, row_step, move):
            at = 5 * i + step[tile_step]
            before, own, behind = (ref[at, pl.ds(ROWS * n + row_step, ROWS), :] for n in (1, 2, 3))
            return (own, jnp.where(after, behind, before), before, behind)[r]

        return load

    def from_ring(ref, tile, tiles, r):
        step = neighbours(tile, tiles)

        def load(i, tile_step, row_step, move):
            rows = own_rows(row_step) if r == 0 else halo_rows(row_step)
            return ref[tiles * i + step[tile_step], rows, :]

        return load

    def from_outer(ref, r):
        def load(i, tile_step, row_step, move):
            rows = own_rows(row_step) if r == 0 else halo_rows(row_step)
            if tile_step:
                return ref[4 * i + (2 if tile_step < 0 else 1), rows, :]
            cut = {0: 2, 1: 1, -1: 3}[move]
            return jnp.where(column < cut, ref[4 * i + 3, rows, :], ref[4 * i, rows, :])

        return load

    def note(s, tile, r, parts):
        for n, value in enumerate(parts[2:4] + tuple(parts[4])):
            mom[s - 1, n, tile, r] = value

    def first_step(tile, carry):
        place = lax.rem(tile + 4, 5)
        halo = []
        for r in (2, 0, 3):
            f = stream_tile(from_wide(pop_a, tile, r), 1, masks_of(tile, 2, r), lane)
            parts = moments(f)
            if r == 0:
                note(1, place, 0, parts)
                for i in range(Q):
                    saved[0, i, place] = f[i]
            else:
                halo.append(parts[2:4] + tuple(parts[4]))
            at = {2: 0, 0: 1, 3: 2}[r]
            g = collide(f, wide[0, tile, at], wide[1, tile, at], parts)
            for i in range(Q):
                pop_b[5 * i + tile, pl.ds(ROWS * (at + 1), ROWS), :] = g[i]
        for n in range(5):
            mom[0, n, place, 1] = jnp.where(after, halo[1][n], halo[0][n])
        return carry

    lax.fori_loop(0, 5, first_step, 0)

    def second_step(tile, carry):
        out = []
        for r in range(2):
            f = stream_tile(from_wide(pop_b, tile + 1, r), 1, masks_of(tile, 1, r), lane)
            parts = moments(f)
            note(2, tile, r, parts)
            if r == 0:
                for i in range(Q):
                    saved[1, i, tile] = f[i]
            out.append(collide(f, field[2, tile, r], field[0, tile, r], parts))
        for i in range(Q):
            put_ring(ring_b, 4 * i + tile, out[0][i], out[1][i])
        return carry

    lax.fori_loop(0, 4, second_step, 0)

    def third_step(tile, carry):
        for r in range(2):
            f = stream_tile(from_ring(ring_b, tile, 4, r), 1, masks_of(tile, 1, r), lane)
            note(3, tile, r, moments(f))
            if r == 0:
                for i in range(Q):
                    saved[2, i, tile] = f[i]
        return carry

    lax.fori_loop(0, 4, third_step, 0)

    def back_tile(load, s, tile, r, own):
        b = stream_tile(load, -1, masks_of(4 if tile is None else tile, 1, r), lane)

        def read(get):
            return jnp.where(column < 2, get(3), get(0)) if tile is None else get(tile)

        rho, rinv, *u = [read(lambda at: mom[s - 1, n, at, r]) for n in range(5)]
        kind, phi = read(lambda at: field[s, at, r]), read(lambda at: field[0, at, r])
        state = [saved[s - 1, i, tile] for i in range(Q)] if own else None
        back, term = collide_back(b, kind, phi, rho, rinv, u, state)
        if own:
            grad[tile] = term if s == 3 else grad[tile] + term
        return back

    def last_step(tile, carry):
        out = [back_tile(from_ring(ring_a, tile, 4, r), 3, tile, r, r == 0) for r in range(2)]
        for i in range(Q):
            put_ring(ring_b, 4 * i + tile, out[0][i], out[1][i])
        return carry

    lax.fori_loop(0, 4, last_step, 0)

    for k, tile in enumerate((1, 2, None)):
        out = []
        for r in range(2):
            load = from_outer(ring_b, r) if tile is None else from_ring(ring_b, tile, 4, r)
            out.append(back_tile(load, 2, tile, r, r == 0 and tile is not None))
        for i in range(Q):
            put_ring(ring_a, 3 * i + k, out[0][i], out[1][i])

    for k, tile in enumerate((1, 2, None)):
        out = []
        for r in range(2):
            load = from_ring(ring_a, k, 3, r)
            out.append(back_tile(load, 1, tile, r, r == 0 and tile is not None))
        for i in range(Q):
            put_ring(ring_b, 3 * i + k, out[0][i], out[1][i])

    panel = lax.broadcasted_iota(jnp.int32, panel_ref.shape, 1)
    sums = jnp.zeros(panel_ref.shape, jnp.float32)
    for t in range(2):
        b = stream_tile(from_ring(ring_b, t, 3, 0), -1, masks_of(t, 0, 0), lane)
        f = [state_ref[2 * i + t] for i in range(Q)]
        kind, phi = own_field_ref[t], own_field_ref[2 * OWN_PHI + t]
        _, _, rho, rinv, u = moments(f)
        back, term = collide_back(b, kind, phi, rho, rinv, u, f)
        for i in range(Q):
            adjoint_ref[i, :, pl.ds(t * LANES, LANES)] = back[i]
        term = term + grad[t + 1]
        for part in range(2):
            amount = jnp.sum(jnp.where((row < 4) == (part == 0), term, 0.0))
            name = names_ref[t, 4 * part : 4 * part + 1, 0:1]
            sums = sums + jnp.where(panel == name, amount, 0.0)
    panel_ref[...] = sums


def finish(parts_ref, adjoint_ref, sums_ref, adjoint_hbm, sem):
    copy = pltpu.make_async_copy(adjoint_ref, adjoint_hbm, sem)
    copy.start()
    sums_ref[...] = jnp.sum(parts_ref[...], axis=0)
    copy.wait()


VMEM = pl.BlockSpec(memory_space=pltpu.VMEM)
HBM = pl.BlockSpec(memory_space=pltpu.HBM)


def shape_of(*dims):
    return jax.ShapeDtypeStruct(dims, jnp.float32)


def tiles_of(count):
    return shape_of(count, ROWS, LANES)


def on_device(sizes, checkpoint, cotangent, cell_codes, porosity, baffle_index):
    size_x, size_y = sizes
    panels = porosity.shape[0]
    devices = size_x * size_y
    y_layout, side_layout, rest_layout = layouts()

    def call(kernel, out_shape, in_specs, scratch=(), name=None, aliases={}):
        return pl.pallas_call(
            kernel,
            out_shape=out_shape,
            in_specs=in_specs,
            out_specs=jax.tree.map(lambda _: VMEM, out_shape),
            scratch_shapes=scratch,
            input_output_aliases=aliases,
            compiler_params=pltpu.CompilerParams(vmem_limit_bytes=32 * 1024 * 1024),
            name=name,
        )

    def swap(value, axis, size):
        return lax.ppermute(value, axis, [(i, i ^ 1) for i in range(size) if i ^ 1 < size])

    def swap_between(value, axis, size):
        pairs = [(i, i + 1) for i in range(1, size - 1, 2)]
        return lax.ppermute(value, axis, pairs + [(j, i) for i, j in pairs])

    arguments = [
        pltpu.with_memory_space_constraint(value, pltpu.HBM)
        for value in (checkpoint, cotangent, cell_codes, baffle_index, porosity)
    ]
    first_y, second_y, first_side, second_side, own, state, cot, field, names = call(
        pack_own,
        (tiles_of(y_layout.size),) * 2
        + (tiles_of(side_layout.size), tiles_of(rest_layout.size + 8))
        + (tiles_of(2 * Q),) * 3
        + (tiles_of(2 * OWN_PHI + 2), jax.ShapeDtypeStruct((2, ROWS, LANES), jnp.int32)),
        [HBM] * 5,
        [
            pltpu.VMEM((Q, ROWS, 2 * LANES), jnp.float32),
            pltpu.VMEM((Q, ROWS, 2 * LANES), jnp.float32),
            pltpu.VMEM((STEPS, ROWS, 2 * LANES), jnp.int32),
            pltpu.SMEM(baffle_index.shape, jnp.int32),
            pltpu.SMEM(porosity.shape, jnp.float32),
            pltpu.SemaphoreType.DMA((5,)),
        ],
        name="pack_own",
    )(*arguments)
    second_y = swap_between(second_y, "gy", size_y)
    first_y = swap(first_y, "gy", size_y)
    second_side = swap_between(second_side, "gx", size_x)
    first_side = swap(first_side, "gx", size_x)
    first_x, second_x = call(
        pack_x,
        (tiles_of(rest_layout.size), tiles_of(rest_layout.size + 1)),
        [VMEM] * 3,
        name="pack_x",
    )(field, first_y, second_y)
    second_x = swap_between(second_x, "gx", size_x)
    first_x = swap(first_x, "gx", size_x)

    spaces = (
        shape_of(5 * Q, 5 * ROWS, LANES),
        shape_of(4 * Q, 3 * ROWS, LANES),
        shape_of(2, 5, 3, ROWS, LANES),
        shape_of(4, 4, 2, ROWS, LANES),
    )
    laid = call(lay_out, spaces, [VMEM] * 7, name="lay_out")(
        first_y, second_y, first_side, second_side, own, field, cot
    )
    adjoint, sums, *_ = call(
        functools.partial(steps_kernel, sizes),
        (pltpu.VMEM((Q, ROWS, 2 * LANES), jnp.float32), shape_of(devices, panels)) + spaces,
        [VMEM] * 9,
        [
            pltpu.VMEM((5 * Q, 5 * ROWS, LANES), jnp.float32),
            pltpu.VMEM((4 * Q, 3 * ROWS, LANES), jnp.float32),
            pltpu.VMEM((3, Q, 5, ROWS, LANES), jnp.float32),
            pltpu.VMEM((3, 5, 5, 2, ROWS, LANES), jnp.float32),
            pltpu.VMEM((4, ROWS, LANES), jnp.float32),
        ],
        name="steps",
        aliases={5 + n: 2 + n for n in range(4)},
    )(state, field, names, first_x, second_x, *laid)
    gathered = lax.all_to_all(sums, ("gx", "gy"), 0, 0, tiled=True)
    totals, adjoint = pl.pallas_call(
        finish,
        out_shape=(shape_of(1, panels), shape_of(Q, ROWS, 2 * LANES)),
        in_specs=[VMEM, VMEM],
        out_specs=(VMEM, HBM),
        scratch_shapes=[pltpu.SemaphoreType.DMA],
        name="finish",
    )(gathered.reshape(devices, 1, panels), adjoint)
    return adjoint, totals.reshape(panels)


def solution(mesh):
    sizes = (mesh.shape["gx"], mesh.shape["gy"])
    in_specs = (P(None, "gx", "gy"), P(None, "gx", "gy"), P(None, "gx", "gy"), P(), P("gx", "gy"))
    out_specs = (P(None, "gx", "gy"), P())
    return jax.shard_map(
        functools.partial(on_device, sizes),
        mesh=mesh,
        in_specs=in_specs,
        out_specs=out_specs,
        check_vma=False,
    )
```

```python
import functools

import jax
import jax.numpy as jnp
import numpy as np
from jax import lax
from jax.experimental import pallas as pl
from jax.experimental.pallas import tpu as pltpu
from jax.sharding import PartitionSpec as P

Q = 19
STEPS = 4
NZ = 32
ROWS = 8
LANES = 128
OMEGA = 1.6
ACCEL = (0.002, 0.0, -0.003)
SHIFT = tuple(a / OMEGA for a in ACCEL)

VELOCITIES = [
    (0, 0, 0),
    (1, 0, 0),
    (-1, 0, 0),
    (0, 1, 0),
    (0, -1, 0),
    (0, 0, 1),
    (0, 0, -1),
    (1, 1, 0),
    (-1, -1, 0),
    (1, -1, 0),
    (-1, 1, 0),
    (1, 0, 1),
    (-1, 0, -1),
    (1, 0, -1),
    (-1, 0, 1),
    (0, 1, 1),
    (0, -1, -1),
    (0, 1, -1),
    (0, -1, 1),
]
OPPOSITE = [0, 2, 1, 4, 3, 6, 5, 8, 7, 10, 9, 12, 11, 14, 13, 16, 15, 18, 17]
PAIRS = [(i, i + 1) for i in range(1, Q, 2)]
W_REST, W_AXIS, W_DIAG = 1.0 / 3.0, 1.0 / 18.0, 1.0 / 36.0

Y_CODE1, Y_CODE2, Y_CODE3, Y_POP, Y_COT = 38, 39, 40, 41, 42
Y_TILES = 43
X_EXTRA = 19
X_LANE = 20
X_SIDE = 2 * X_LANE
X_RING = 4 * X_LANE
X_CODE13 = X_RING + Q + 1
X_CODE2 = X_CODE13 + 4
X_TILES = X_CODE2 + 2
EMPTY = 25
FREE = NZ - EMPTY
WEIGHTS = [W_REST] + [W_AXIS] * 6 + [W_DIAG] * 12
LEVEL = [i for i, v in enumerate(VELOCITIES) if v[2] < 1]
OWN_PHI = 4


def turned(axis, outward):
    return [i for i, v in enumerate(VELOCITIES) if v[axis] == outward and sum(map(abs, v)) == 2]


def total(values):
    values = list(values)
    while len(values) > 1:
        values = [a + b for a, b in zip(values[::2], values[1::2])] + (
            [values[-1]] if len(values) % 2 else []
        )
    return values[0]


def along(vector, three):
    terms = None
    for c, value in zip(vector, three):
        if c == 0:
            continue
        if terms is None:
            terms = value if c > 0 else -value
        else:
            terms = terms + value if c > 0 else terms - value
    return terms


def moments(f):
    plus = {i: f[i] + f[o] for i, o in PAIRS}
    minus = {i: f[i] - f[o] for i, o in PAIRS}
    rho = total([f[0]] + [plus[i] for i, _ in PAIRS])
    rinv = 1.0 / rho
    u = []
    for axis in range(3):
        terms = [
            minus[i] if VELOCITIES[i][axis] > 0 else -minus[i]
            for i, _ in PAIRS
            if VELOCITIES[i][axis] != 0
        ]
        u.append(total(terms) * rinv + SHIFT[axis])
    return plus, minus, rho, rinv, u


def coefficients(kind, phi, rinv):
    baffle = kind == 3.0
    gas = kind == 0.0
    even = jnp.where(gas, 0.0, jnp.where(baffle, 0.5 - 0.5 * OMEGA * phi, 0.5 * (1.0 - OMEGA)))
    odd = jnp.where(
        gas, 0.0, jnp.where(baffle, (1.0 - 0.5 * OMEGA) * phi - 0.5, 0.5 * (1.0 - OMEGA))
    )
    slope = jnp.where(
        baffle,
        OMEGA * phi,
        jnp.where(kind == 1.0, OMEGA, jnp.where(kind == 2.0, OMEGA * rinv, 0.0)),
    )
    return even, odd, slope


def collide(f, kind, phi, parts):
    plus, minus, rho, rinv, u = parts
    even, odd, slope = coefficients(kind, phi, rinv)
    scale = slope * rho
    rest = 1.0 - 1.5 * (u[0] * u[0] + u[1] * u[1] + u[2] * u[2])
    base = scale * rest + jnp.where(kind == 0.0, 1.0, 0.0)
    out = [None] * Q
    out[0] = 2.0 * even * f[0] + W_REST * base
    for weight, pairs in ((W_AXIS, PAIRS[:3]), (W_DIAG, PAIRS[3:])):
        flat = weight * base
        three = (3.0 * weight) * scale
        for i, o in pairs:
            cu = along(VELOCITIES[i], u)
            lin = three * cu
            ev = even * plus[i] + (flat + 1.5 * lin * cu)
            od = odd * minus[i] + lin
            out[i] = ev + od
            out[o] = ev - od
    return out


def collide_back(b, kind, phi, rho, rinv, u, state=None):
    even, odd, slope = coefficients(kind, phi, rinv)
    plus = {i: b[i] + b[o] for i, o in PAIRS}
    minus = {i: b[i] - b[o] for i, o in PAIRS}
    rest = 1.0 - 1.5 * (u[0] * u[0] + u[1] * u[1] + u[2] * u[2])
    u_half = [1.5 * c for c in u]
    weighted = W_REST * b[0]
    energy = 0.0
    vector = [0.0, 0.0, 0.0]
    for weight, pairs in ((W_AXIS, PAIRS[:3]), (W_DIAG, PAIRS[3:])):
        weighted = weighted + weight * total([plus[i] for i, _ in pairs])
        energies, parts = [], ([], [], [])
        for i, _ in pairs:
            cu = along(VELOCITIES[i], u)
            half = along(VELOCITIES[i], u_half) * plus[i]
            first = minus[i] + half
            energies.append(cu * first)
            second = first + half
            for axis in range(3):
                c = VELOCITIES[i][axis]
                if c:
                    parts[axis].append(second if c > 0 else -second)
        energy = energy + (3.0 * weight) * total(energies)
        vector = [vector[k] + (3.0 * weight) * total(parts[k]) for k in range(3)]
    energy = energy + rest * weighted
    vector = [vector[k] - (3.0 * weighted) * u[k] for k in range(3)]
    push = [slope * v for v in vector]
    inner = total([push[k] * (u[k] - SHIFT[k]) for k in range(3)])
    shared = jnp.where(kind == 2.0, 0.0, slope) * energy - inner
    out = [None] * Q
    out[0] = 2.0 * even * b[0] + shared
    for i, o in PAIRS:
        ev = even * plus[i] + shared
        od = odd * minus[i] + along(VELOCITIES[i], push)
        out[i] = ev + od
        out[o] = ev - od
    if state is None:
        return out, None
    evens = total([plus[i] * (state[i] + state[o]) for i, o in PAIRS])
    odds = total([minus[i] * (state[i] - state[o]) for i, o in PAIRS])
    term = (
        -OMEGA * (b[0] * state[0] + 0.5 * evens)
        + (1.0 - 0.5 * OMEGA) * odds
        + OMEGA * rho * energy
    )
    return out, jnp.where(kind == 3.0, term, 0.0)


def wall_masks(sign_rows, own_low, own_high, edges):
    lane = lax.broadcasted_iota(jnp.int32, (ROWS, LANES), 1)
    row = lax.broadcasted_iota(jnp.int32, (ROWS, LANES), 0)
    x_low, x_high, y_low, y_high = edges
    depth = lane % NZ
    masks = {}
    masks[2, 1] = depth == 0
    masks[2, -1] = depth == NZ - 1
    masks[1, 1] = lane < jnp.where(own_low, y_low * NZ, 0)
    masks[1, -1] = lane >= jnp.where(own_high, LANES - y_high * NZ, LANES)
    if sign_rows:
        masks[0, 1] = row < x_low
        masks[0, -1] = row >= ROWS - x_high
    return masks


def stream_tile(load, sign, masks, lane):
    cross_low, cross_high = lane >= LANES - NZ, lane < NZ
    combined = {}
    out = []
    for i, vector in enumerate(VELOCITIES):
        v = tuple(sign * c for c in vector)
        value = load(i, 0, -v[0], v[1])
        if v[1] == 1:
            value = jnp.where(cross_low, load(i, -1, -v[0], 1), value)
        elif v[1] == -1:
            value = jnp.where(cross_high, load(i, 1, -v[0], -1), value)
        amount = (v[1] * NZ + v[2]) % LANES
        if amount:
            value = pltpu.roll(value, amount, 1)
        outside = None
        if v not in combined:
            for axis in range(3):
                if v[axis] and (axis, v[axis]) in masks:
                    wall = masks[axis, v[axis]]
                    outside = wall if outside is None else outside | wall
            combined[v] = outside
        outside = combined[v]
        if outside is not None:
            value = jnp.where(outside, load(OPPOSITE[i], 0, 0, 0), value)
        out.append(value)
    return out


def iotas():
    row = lax.broadcasted_iota(jnp.int32, (ROWS, LANES), 0)
    lane = lax.broadcasted_iota(jnp.int32, (ROWS, LANES), 1)
    return row, lane, lane // NZ, lane % NZ


def columns(value, count):
    amount = (count * NZ) % LANES
    return pltpu.roll(value, amount, 1) if amount else value


def lines(value, count):
    amount = count % ROWS
    return pltpu.roll(value, amount, 0) if amount else value


class Layout:
    def __init__(self, count, guests, fills):
        self.fills = fills
        hosts = [at for at in fills if at not in guests]
        self.hosts = {at: hosts[4 * n : 4 * n + 4] for n, at in enumerate(guests)}
        self.guests = guests
        kept = [at for at in range(count) if at not in guests]
        self.place = {at: n for n, at in enumerate(kept)}
        self.size = len(kept)


class Packing:
    def __init__(self, ref, layout):
        self.ref, self.layout, self.held = ref, layout, {}

    def __setitem__(self, at, value):
        if at in self.layout.guests:
            self.held[at] = value
        else:
            self.ref[self.layout.place[at]] = value

    def finish(self):
        row, lane, column, depth = iotas()
        spare = depth >= EMPTY
        for at, value in self.held.items():
            for k, host in enumerate(self.layout.hosts[at]):
                place = self.layout.place[host]
                moved = pltpu.roll(value, EMPTY - FREE * k, 1)
                self.ref[place] = jnp.where(spare, moved, self.ref[place])
        for place in range(self.layout.size, self.ref.shape[0]):
            self.ref[place] = jnp.zeros((ROWS, LANES), jnp.float32)


class Unpacking:
    def __init__(self, source, layout):
        self.source, self.layout, self.cache = source, layout, {}
        self.changed = set(layout.guests).union(*layout.hosts.values())

    def __getitem__(self, at):
        if at not in self.cache:
            self.cache[at] = self.read(at)
        return self.cache[at]

    def read(self, at):
        row, lane, column, depth = iotas()
        layout = self.layout
        if at in layout.guests:
            value = None
            for k, host in enumerate(layout.hosts[at]):
                tile = self.source[layout.place[host]]
                moved = pltpu.roll(tile, LANES - (EMPTY - FREE * k), 1)
                value = moved if value is None else jnp.where(depth >= FREE * k, moved, value)
        else:
            value = self.source[layout.place[at]]
        if at in self.changed:
            value = jnp.where(depth >= EMPTY, layout.fills[at], value)
        return value


def layouts():
    y_fills = {2 * i + t: WEIGHTS[i] for i in LEVEL for t in range(2)}
    y_fills.update({Y_POP: W_DIAG, Y_CODE2: 0.0})
    x_fills = {X_LANE * n + i: WEIGHTS[i] for n in range(4) for i in LEVEL}
    side = {at: fill for at, fill in x_fills.items() if at < X_SIDE}
    rest = {at - X_SIDE: fill for at, fill in x_fills.items() if at >= X_SIDE}
    rest.update({X_CODE2 - X_SIDE: 0.0, X_CODE2 + 1 - X_SIDE: 0.0})
    rest.update({X_RING - X_SIDE + i: WEIGHTS[i] for i in range(Q)})
    ring = [X_RING - X_SIDE + i for i in range(9)]
    return (
        Layout(Y_TILES, [2 * i for i in LEVEL[:6]], y_fills),
        Layout(X_SIDE, LEVEL[:5], side),
        Layout(X_TILES - X_SIDE, ring, rest),
    )


class Pick:
    def __init__(self, flag, first, second):
        self.flag, self.first, self.second = flag, first, second

    def __getitem__(self, at):
        return jnp.where(self.flag, self.first[at], self.second[at])


class Deal:
    def __init__(self, even, first, second, layout, skip=0):
        self.even, self.skip, self.held = even, skip, {}
        self.first, self.second = Packing(first, layout), Packing(second, layout)

    def put(self, way, at, value):
        if (-way, at) not in self.held:
            self.held[way, at] = value
            return
        other = self.held.pop((-way, at))
        up, down = (value, other) if way == 1 else (other, value)
        self.first[at - self.skip] = jnp.where(self.even, up, down)
        self.second[at - self.skip] = jnp.where(self.even, down, up)

    def put_both(self, at, value):
        self.first[at - self.skip] = value
        self.second[at - self.skip] = value

    def finish(self):
        self.first.finish()
        self.second.finish()


class Shifted:
    def __init__(self, ref, start):
        self.ref, self.start = ref, start

    def __getitem__(self, at):
        return self.ref[at - self.start]


def is_even(axis):
    return lax.rem(lax.axis_index(axis), 2) == 0


def pack_own(
    f_hbm,
    cot_hbm,
    codes_hbm,
    panels_hbm,
    porosity_hbm,
    first_ref,
    second_ref,
    first_side_ref,
    second_side_ref,
    own_ref,
    state_ref,
    own_cot_ref,
    field_ref,
    names_ref,
    f_ref,
    cot_ref,
    codes_ref,
    panels_ref,
    porosity_ref,
    sems,
):
    pieces = (
        (panels_hbm, panels_ref),
        (porosity_hbm, porosity_ref),
        (f_hbm, f_ref),
        (codes_hbm, codes_ref),
        (cot_hbm, cot_ref),
    )
    copies = [
        pltpu.make_async_copy(source, target, sems.at[n])
        for n, (source, target) in enumerate(pieces)
    ]
    for copy in copies:
        copy.start()
    for copy in copies[:4]:
        copy.wait()
    y_layout, side_layout, _ = layouts()
    deal = Deal(is_even("gy"), first_ref, second_ref, y_layout)
    side = Deal(is_even("gx"), first_side_ref, second_side_ref, side_layout)
    row, lane, column, depth = iotas()
    top = depth == NZ - 1

    def tile_of(ref, i, t):
        return ref[i, :, pl.ds(t * LANES, LANES)]

    codes, phis = [], []
    for t in range(2):
        names = panels_ref[0, t * LANES], panels_ref[4, t * LANES]
        phi = jnp.where(row < 4, porosity_ref[names[0]], porosity_ref[names[1]])
        names_ref[t] = jnp.where(row < 4, names[0], names[1])
        kinds = [tile_of(codes_ref, s, t).astype(jnp.float32) for s in range(STEPS)]
        f = [tile_of(f_ref, i, t) for i in range(Q)]
        g = collide(f, kinds[0], phi, moments(f))
        for i in range(Q):
            own_ref[2 * i + t] = g[i]
            state_ref[2 * i + t] = f[i]
        for s in range(STEPS):
            field_ref[2 * s + t] = kinds[s]
        field_ref[2 * OWN_PHI + t] = phi
        codes.append([jnp.where(top, phi, kinds[1]), kinds[2], kinds[3]])
    copies[4].wait()
    for i in range(Q):
        for way in (1, -1):
            near, far = (1, 0) if way == 1 else (0, 1)
            deep = 3 - way * VELOCITIES[i][1]
            cot = tile_of(cot_ref, i, near)
            g_far = own_ref[2 * i + far]
            if way == 1:
                mixed = jnp.where(column >= deep, g_far, columns(cot, deep - 4))
            else:
                mixed = jnp.where(column < 4 - deep, g_far, columns(cot, 4 - deep))
            deal.put(way, 2 * i, mixed if far == 0 else own_ref[2 * i])
            deal.put(way, 2 * i + 1, mixed if far == 1 else own_ref[2 * i + 1])
    for way in (1, -1):
        near, far = (1, 0) if way == 1 else (0, 1)
        outer = 3 if way == 1 else 0
        deal.put(way, Y_CODE1, codes[near][0])
        deal.put(way, Y_CODE2, codes[near][1])
        outside = columns(codes[far][0], 3 - 2 * outer)
        deal.put(way, Y_CODE3, jnp.where(column == 3 - outer, outside, codes[near][2]))
        extra = None
        for k, i in enumerate(turned(1, -way)):
            value = columns(own_ref[2 * i + far], k - outer)
            extra = value if extra is None else jnp.where(column == k, value, extra)
        deal.put(way, Y_POP, extra)
        extra = None
        for k, i in enumerate(turned(1, way)):
            value = columns(tile_of(cot_ref, i, near), k - (1 if way == 1 else 2))
            extra = value if extra is None else jnp.where(column == k, value, extra)
        deal.put(way, Y_COT, extra)
    deal.finish()
    for t in range(2):
        for i in range(Q):
            own_cot_ref[2 * i + t] = tile_of(cot_ref, i, t)
        pack_lines(
            side,
            X_LANE * t,
            lambda i: own_ref[2 * i + t],
            lambda i: tile_of(cot_ref, i, t),
        )
    side.finish()


def from_y(left_ref, right_ref):
    row, lane, column, depth = iotas()
    high = lane >= LANES // 2

    def population(i, c):
        if c == 1:
            return left_ref[2 * i + 1]
        if c == 4:
            return right_ref[2 * i]
        along_y = VELOCITIES[i][1]
        left, right = left_ref[2 * i], right_ref[2 * i + 1]
        if along_y == 1 and i in turned(1, 1):
            right = columns(right_ref[Y_POP], -turned(1, 1).index(i))
        if along_y == -1 and i in turned(1, -1):
            left = columns(left_ref[Y_POP], 3 - turned(1, -1).index(i))
        return jnp.where(high, left, right)

    def cotangent(i, c):
        ref, way, place, far = (left_ref, 1, 1, 0) if c == 1 else (right_ref, -1, 2, 1)
        deep = 3 - way * VELOCITIES[i][1]
        value = columns(ref[2 * i + far], way * (4 - deep))
        if i in turned(1, way):
            extra = columns(ref[Y_COT], place - turned(1, way).index(i))
            value = jnp.where(column == place, extra, value)
        return value

    def codes(s, c):
        if c == 0:
            left, right = columns(left_ref[Y_CODE3], 3), columns(right_ref[Y_CODE3], 1)
            return jnp.where(high, left, right)
        return (left_ref if c == 1 else right_ref)[(Y_CODE1, Y_CODE2, Y_CODE3)[s - 1]]

    return population, cotangent, codes


def mix_lines(deal, at, pop, cot, deep, way):
    row, lane, column, depth = iotas()
    if way == 1:
        mixed = jnp.where(row >= deep, pop, lines(cot, deep))
    else:
        mixed = jnp.where(row < ROWS - deep, pop, lines(cot, -deep))
    deal.put(way, at, mixed)


def pack_lines(deal, first, population, cotangent):
    row, lane, column, depth = iotas()

    for i in range(Q):
        pop, cot = population(i), cotangent(i)
        for way in (1, -1):
            mix_lines(deal, first + i, pop, cot, 3 - way * VELOCITIES[i][0], way)
    for way in (1, -1):
        extra = None
        for k, i in enumerate(turned(0, -way)):
            value = lines(population(i), k - (3 if way == 1 else 4))
            extra = value if extra is None else jnp.where(row == k, value, extra)
        for k, i in enumerate(turned(0, way)):
            value = lines(cotangent(i), 4 + k - (5 if way == 1 else 2))
            extra = jnp.where(row == 4 + k, value, extra)
        deal.put(way, first + X_EXTRA, extra)


def from_x(ref, n, way):
    row, lane, column, depth = iotas()
    first = X_LANE * n

    def population(i):
        value = ref[first + i]
        if i in turned(0, -way):
            place = 3 if way == 1 else 4
            extra = lines(ref[first + X_EXTRA], place - turned(0, -way).index(i))
            value = jnp.where(row == place, extra, value)
        return value

    def cotangent(i):
        value = lines(ref[first + i], -way * (3 - way * VELOCITIES[i][0]))
        if i in turned(0, way):
            place = 5 if way == 1 else 2
            extra = lines(ref[first + X_EXTRA], place - 4 - turned(0, way).index(i))
            value = jnp.where(row == place, extra, value)
        return value

    def codes(s):
        if s == 2:
            return lines(ref[X_CODE2 + n // 2], 4 * (n % 2))
        value = ref[X_CODE13 + n]
        return value if s == 1 else lines(value, -3 * way)

    return population, cotangent, codes


def pack_x(field_ref, first_y_ref, second_y_ref, first_ref, second_ref):
    row, lane, column, depth = iotas()
    y_layout, _, layout = layouts()
    deal = Deal(is_even("gx"), first_ref, second_ref, layout, X_SIDE)
    population, cotangent, codes = from_y(*sides(first_y_ref, second_y_ref, "gy", y_layout))

    def both_codes(at, first, second):
        second = lines(second, 4)
        deal.put(1, at, jnp.where(row >= 4, first, second))
        deal.put(-1, at, jnp.where(row < 4, first, second))

    for n, c in ((2, 1), (3, 4)):
        pack_lines(
            deal,
            X_LANE * n,
            lambda i: population(i, c),
            lambda i: cotangent(i, c),
        )
    for n in range(Q + 1):
        value = population(n, 0) if n < Q else codes(1, 0)
        deal.put_both(X_RING + n, value)
    for n in range(4):
        if n < 2:
            first = jnp.where(depth == NZ - 1, field_ref[2 * OWN_PHI + n], field_ref[2 + n])
            third = field_ref[6 + n]
        else:
            c = (1, 4)[n - 2]
            first, third = codes(1, c), codes(3, c)
        for way in (1, -1):
            mix_lines(deal, X_CODE13 + n, first, third, 3, way)
    both_codes(X_CODE2, field_ref[4], field_ref[5])
    both_codes(X_CODE2 + 1, codes(2, 1), codes(2, 4))
    deal.finish()


def sides(first_ref, second_ref, axis, layout):
    even = is_even(axis)
    picks = Pick(even, second_ref, first_ref), Pick(even, first_ref, second_ref)
    return [Unpacking(pick, layout) for pick in picks]


def own_rows(step=0):
    return pl.ds(ROWS + step, ROWS)


def halo_rows(step=0):
    return pl.ds({0: 2 * ROWS, -1: 2 * ROWS - 1, 1: 1}[step], ROWS)


def put_halo(ref, at, halo):
    ref[at, pl.ds(0, ROWS), :] = halo
    ref[at, halo_rows(), :] = halo


def put_ring(ref, at, own, halo):
    ref[at, own_rows(), :] = own
    put_halo(ref, at, halo)


def expand(code):
    row, lane, column, depth = iotas()
    top = depth == NZ - 1
    phi = jnp.where(top, code, 0.0)
    for step in (1, 2, 4, 8, 16):
        phi = phi + pltpu.roll(phi, LANES - step, 1)
    return jnp.where(top, 0.0, code), phi


def lay_own(c, population, cotangent, codes, code_phi, pop, cot, wide, field):
    for i in range(Q):
        pop[5 * i + c, pl.ds(2 * ROWS, ROWS), :] = population(i)
        if c:
            cot[4 * i + c - 1, own_rows(), :] = cotangent(i)
    for n in range(2):
        wide[n, c, 1] = code_phi[n]
    if c:
        field[0, c - 1, 0], field[1, c - 1, 0] = code_phi[1], code_phi[0]
        for s in (2, 3):
            field[s, c - 1, 0] = codes(s)


def lay_halo(c, below, above, pop, cot):
    row, lane, column, depth = iotas()
    for i in range(Q):
        pop[5 * i + c, pl.ds(ROWS, ROWS), :] = below[0](i)
        pop[5 * i + c, pl.ds(3 * ROWS, ROWS), :] = above[0](i)
        if c:
            put_halo(cot, 4 * i + c - 1, jnp.where(row < 4, above[1](i), below[1](i)))


def lay_codes(c, below, above, wide, field):
    row, lane, column, depth = iotas()
    before, after = expand(below[2](1)), expand(above[2](1))
    for n in range(2):
        wide[n, c, 0], wide[n, c, 2] = before[n], after[n]
    if c:
        for n, place in ((0, 1), (1, 0)):
            field[place, c - 1, 1] = jnp.where(row < 4, after[n], before[n])
        for s in (2, 3):
            field[s, c - 1, 1] = jnp.where(row < 4, above[2](s), below[2](s))


def lay_out(
    first_y_ref,
    second_y_ref,
    first_side_ref,
    second_side_ref,
    own_ref,
    field_ref,
    cot_ref,
    pop,
    cot,
    wide,
    field,
):
    y_layout, side_layout, _ = layouts()
    from_left = from_y(*sides(first_y_ref, second_y_ref, "gy", y_layout))
    below, above = sides(first_side_ref, second_side_ref, "gx", side_layout)
    for c in range(5):
        t = c - 2
        if t in (0, 1):
            lay_own(
                c,
                lambda i: own_ref[2 * i + t],
                lambda i: cot_ref[2 * i + t],
                lambda s: field_ref[2 * s + t],
                (field_ref[2 + t], field_ref[2 * OWN_PHI + t]),
                pop,
                cot,
                wide,
                field,
            )
            lay_halo(c, from_x(below, t, 1), from_x(above, t, -1), pop, cot)
        else:
            own = [functools.partial(lambda g, n: g(n, c), get) for get in from_left]
            lay_own(c, *own, expand(own[2](1)), pop, cot, wide, field)


def lay_halos(below, above, pop, cot, wide, field):
    ring = [
        (lambda i, ref=ref: ref[X_RING + i], None, lambda s, ref=ref: ref[X_RING + Q])
        for ref in (below, above)
    ]
    lay_halo(0, *ring, pop, cot)
    lay_codes(0, *ring, wide, field)
    for n, c in enumerate((2, 3, 1, 4)):
        halves = from_x(below, n, 1), from_x(above, n, -1)
        if n > 1:
            lay_halo(c, *halves, pop, cot)
        lay_codes(c, *halves, wide, field)


def steps_kernel(
    sizes,
    state_ref,
    own_field_ref,
    names_ref,
    first_x_ref,
    second_x_ref,
    *refs,
):
    adjoint_ref, panel_ref, pop_a, ring_a, wide, field, pop_b, ring_b, saved, mom, grad = refs[4:]
    size_x, size_y = sizes
    halves = sides(first_x_ref, second_x_ref, "gx", layouts()[2])
    below, above = (Shifted(ref, X_SIDE) for ref in halves)
    lay_halos(below, above, pop_a, ring_a, wide, field)

    at_x, at_y = lax.axis_index("gx"), lax.axis_index("gy")
    edges = (
        jnp.where(at_x == 0, 1, 0),
        jnp.where(at_x == size_x - 1, 1, 0),
        jnp.where(at_y == 0, 1, 0),
        jnp.where(at_y == size_y - 1, 1, 0),
    )
    row, lane, column, depth = iotas()
    after = row < 4

    def masks_of(tile, first, r):
        return wall_masks(r == 0, tile == first, tile == first + 1, edges)

    def neighbours(tile, tiles):
        if isinstance(tile, int):
            return {0: tile, -1: (tile - 1) % tiles, 1: (tile + 1) % tiles}
        return {0: tile, -1: lax.rem(tile + tiles - 1, tiles), 1: lax.rem(tile + 1, tiles)}

    def from_wide(ref, tile, r):
        step = neighbours(tile, 5)

        def load(i, tile_step, row_step, move):
            at = 5 * i + step[tile_step]
            before, own, behind = (ref[at, pl.ds(ROWS * n + row_step, ROWS), :] for n in (1, 2, 3))
            return (own, jnp.where(after, behind, before), before, behind)[r]

        return load

    def from_ring(ref, tile, tiles, r):
        step = neighbours(tile, tiles)

        def load(i, tile_step, row_step, move):
            rows = own_rows(row_step) if r == 0 else halo_rows(row_step)
            return ref[tiles * i + step[tile_step], rows, :]

        return load

    def from_outer(ref, r):
        def load(i, tile_step, row_step, move):
            rows = own_rows(row_step) if r == 0 else halo_rows(row_step)
            if tile_step:
                return ref[4 * i + (2 if tile_step < 0 else 1), rows, :]
            cut = {0: 2, 1: 1, -1: 3}[move]
            return jnp.where(column < cut, ref[4 * i + 3, rows, :], ref[4 * i, rows, :])

        return load

    def note(s, tile, r, parts):
        for n, value in enumerate(parts[2:4] + tuple(parts[4])):
            mom[s - 1, n, tile, r] = value

    def first_step(tile, carry):
        place = lax.rem(tile + 4, 5)
        halo = []
        for r in (2, 0, 3):
            f = stream_tile(from_wide(pop_a, tile, r), 1, masks_of(tile, 2, r), lane)
            parts = moments(f)
            if r == 0:
                note(1, place, 0, parts)
                for i in range(Q):
                    saved[0, i, place] = f[i]
            else:
                halo.append(parts[2:4] + tuple(parts[4]))
            at = {2: 0, 0: 1, 3: 2}[r]
            g = collide(f, wide[0, tile, at], wide[1, tile, at], parts)
            for i in range(Q):
                pop_b[5 * i + tile, pl.ds(ROWS * (at + 1), ROWS), :] = g[i]
        for n in range(5):
            mom[0, n, place, 1] = jnp.where(after, halo[1][n], halo[0][n])
        return carry

    lax.fori_loop(0, 5, first_step, 0)

    def second_step(tile, carry):
        out = []
        for r in range(2):
            f = stream_tile(from_wide(pop_b, tile + 1, r), 1, masks_of(tile, 1, r), lane)
            parts = moments(f)
            note(2, tile, r, parts)
            if r == 0:
                for i in range(Q):
                    saved[1, i, tile] = f[i]
            out.append(collide(f, field[2, tile, r], field[0, tile, r], parts))
        for i in range(Q):
            put_ring(ring_b, 4 * i + tile, out[0][i], out[1][i])
        return carry

    lax.fori_loop(0, 4, second_step, 0)

    def third_step(tile, carry):
        for r in range(2):
            f = stream_tile(from_ring(ring_b, tile, 4, r), 1, masks_of(tile, 1, r), lane)
            note(3, tile, r, moments(f))
            if r == 0:
                for i in range(Q):
                    saved[2, i, tile] = f[i]
        return carry

    lax.fori_loop(0, 4, third_step, 0)

    def back_tile(load, s, tile, r, own):
        b = stream_tile(load, -1, masks_of(4 if tile is None else tile, 1, r), lane)

        def read(get):
            return jnp.where(column < 2, get(3), get(0)) if tile is None else get(tile)

        rho, rinv, *u = [read(lambda at: mom[s - 1, n, at, r]) for n in range(5)]
        kind, phi = read(lambda at: field[s, at, r]), read(lambda at: field[0, at, r])
        state = [saved[s - 1, i, tile] for i in range(Q)] if own else None
        back, term = collide_back(b, kind, phi, rho, rinv, u, state)
        if own:
            grad[tile] = term if s == 3 else grad[tile] + term
        return back

    def last_step(tile, carry):
        out = [back_tile(from_ring(ring_a, tile, 4, r), 3, tile, r, r == 0) for r in range(2)]
        for i in range(Q):
            put_ring(ring_b, 4 * i + tile, out[0][i], out[1][i])
        return carry

    lax.fori_loop(0, 4, last_step, 0)

    for k, tile in enumerate((1, 2, None)):
        out = []
        for r in range(2):
            load = from_outer(ring_b, r) if tile is None else from_ring(ring_b, tile, 4, r)
            out.append(back_tile(load, 2, tile, r, r == 0 and tile is not None))
        for i in range(Q):
            put_ring(ring_a, 3 * i + k, out[0][i], out[1][i])

    for k, tile in enumerate((1, 2, None)):
        out = []
        for r in range(2):
            load = from_ring(ring_a, k, 3, r)
            out.append(back_tile(load, 1, tile, r, r == 0 and tile is not None))
        for i in range(Q):
            put_ring(ring_b, 3 * i + k, out[0][i], out[1][i])

    panel = lax.broadcasted_iota(jnp.int32, panel_ref.shape, 1)
    sums = jnp.zeros(panel_ref.shape, jnp.float32)
    for t in range(2):
        b = stream_tile(from_ring(ring_b, t, 3, 0), -1, masks_of(t, 0, 0), lane)
        f = [state_ref[2 * i + t] for i in range(Q)]
        kind, phi = own_field_ref[t], own_field_ref[2 * OWN_PHI + t]
        _, _, rho, rinv, u = moments(f)
        back, term = collide_back(b, kind, phi, rho, rinv, u, f)
        for i in range(Q):
            adjoint_ref[i, :, pl.ds(t * LANES, LANES)] = back[i]
        term = term + grad[t + 1]
        for part in range(2):
            amount = jnp.sum(jnp.where((row < 4) == (part == 0), term, 0.0))
            name = names_ref[t, 4 * part : 4 * part + 1, 0:1]
            sums = sums + jnp.where(panel == name, amount, 0.0)
    panel_ref[...] = sums


def finish(parts_ref, adjoint_ref, sums_ref, adjoint_hbm, sem):
    copy = pltpu.make_async_copy(adjoint_ref, adjoint_hbm, sem)
    copy.start()
    sums_ref[...] = jnp.sum(parts_ref[...], axis=0)
    copy.wait()


VMEM = pl.BlockSpec(memory_space=pltpu.VMEM)
HBM = pl.BlockSpec(memory_space=pltpu.HBM)


def shape_of(*dims):
    return jax.ShapeDtypeStruct(dims, jnp.float32)


def tiles_of(count):
    return shape_of(count, ROWS, LANES)


def on_device(sizes, checkpoint, cotangent, cell_codes, porosity, baffle_index):
    size_x, size_y = sizes
    panels = porosity.shape[0]
    devices = size_x * size_y
    y_layout, side_layout, rest_layout = layouts()

    params = pltpu.CompilerParams(vmem_limit_bytes=32 * 1024 * 1024)

    def call(kernel, out_shape, in_specs, scratch=(), name=None, aliases={}):
        return pl.pallas_call(
            kernel,
            out_shape=out_shape,
            in_specs=in_specs,
            out_specs=jax.tree.map(lambda _: VMEM, out_shape),
            scratch_shapes=scratch,
            input_output_aliases=aliases,
            compiler_params=params,
            name=name,
        )

    def swap(value, axis, size):
        return lax.ppermute(value, axis, [(i, i ^ 1) for i in range(size) if i ^ 1 < size])

    def swap_between(value, axis, size):
        pairs = [(i, i + 1) for i in range(1, size - 1, 2)]
        return lax.ppermute(value, axis, pairs + [(j, i) for i, j in pairs])

    arguments = [
        pltpu.with_memory_space_constraint(value, pltpu.HBM)
        for value in (checkpoint, cotangent, cell_codes, baffle_index, porosity)
    ]
    first_y, second_y, first_side, second_side, own, state, cot, field, names = call(
        pack_own,
        (tiles_of(y_layout.size),) * 2
        + (tiles_of(side_layout.size), tiles_of(rest_layout.size + 8))
        + (tiles_of(2 * Q),) * 3
        + (tiles_of(2 * OWN_PHI + 2), jax.ShapeDtypeStruct((2, ROWS, LANES), jnp.int32)),
        [HBM] * 5,
        [
            pltpu.VMEM((Q, ROWS, 2 * LANES), jnp.float32),
            pltpu.VMEM((Q, ROWS, 2 * LANES), jnp.float32),
            pltpu.VMEM((STEPS, ROWS, 2 * LANES), jnp.int32),
            pltpu.SMEM(baffle_index.shape, jnp.int32),
            pltpu.SMEM(porosity.shape, jnp.float32),
            pltpu.SemaphoreType.DMA((5,)),
        ],
        name="pack_own",
    )(*arguments)
    second_y = swap_between(second_y, "gy", size_y)
    first_y = swap(first_y, "gy", size_y)
    second_side = swap_between(second_side, "gx", size_x)
    first_side = swap(first_side, "gx", size_x)
    first_x, second_x = call(
        pack_x,
        (tiles_of(rest_layout.size), tiles_of(rest_layout.size + 1)),
        [VMEM] * 3,
        name="pack_x",
    )(field, first_y, second_y)
    second_x = swap_between(second_x, "gx", size_x)
    first_x = swap(first_x, "gx", size_x)

    spaces = (
        shape_of(5 * Q, 5 * ROWS, LANES),
        shape_of(4 * Q, 3 * ROWS, LANES),
        shape_of(2, 5, 3, ROWS, LANES),
        shape_of(4, 4, 2, ROWS, LANES),
    )
    laid = call(lay_out, spaces, [VMEM] * 7, name="lay_out")(
        first_y, second_y, first_side, second_side, own, field, cot
    )
    adjoint, sums, *_ = call(
        functools.partial(steps_kernel, sizes),
        (pltpu.VMEM((Q, ROWS, 2 * LANES), jnp.float32), shape_of(devices, panels)) + spaces,
        [VMEM] * 9,
        [
            pltpu.VMEM((5 * Q, 5 * ROWS, LANES), jnp.float32),
            pltpu.VMEM((4 * Q, 3 * ROWS, LANES), jnp.float32),
            pltpu.VMEM((3, Q, 5, ROWS, LANES), jnp.float32),
            pltpu.VMEM((3, 5, 5, 2, ROWS, LANES), jnp.float32),
            pltpu.VMEM((4, ROWS, LANES), jnp.float32),
        ],
        name="steps",
        aliases={5 + n: 2 + n for n in range(4)},
    )(state, field, names, first_x, second_x, *laid)
    gathered = lax.all_to_all(sums, ("gx", "gy"), 0, 0, tiled=True)
    totals, adjoint = pl.pallas_call(
        finish,
        out_shape=(shape_of(1, panels), shape_of(Q, ROWS, 2 * LANES)),
        in_specs=[VMEM, VMEM],
        out_specs=(VMEM, HBM),
        scratch_shapes=[pltpu.SemaphoreType.DMA],
        compiler_params=params,
        name="finish",
    )(gathered.reshape(devices, 1, panels), adjoint)
    return adjoint, totals.reshape(panels)


def solution(mesh):
    sizes = (mesh.shape["gx"], mesh.shape["gy"])
    in_specs = (P(None, "gx", "gy"), P(None, "gx", "gy"), P(None, "gx", "gy"), P(), P("gx", "gy"))
    out_specs = (P(None, "gx", "gy"), P())
    return jax.shard_map(
        functools.partial(on_device, sizes),
        mesh=mesh,
        in_specs=in_specs,
        out_specs=out_specs,
        check_vma=False,
    )
```

```python
import functools

import jax
import jax.numpy as jnp
import numpy as np
from jax import lax
from jax.experimental import pallas as pl
from jax.experimental.pallas import tpu as pltpu
from jax.sharding import PartitionSpec as P

Q = 19
STEPS = 4
NZ = 32
ROWS = 8
LANES = 128
OMEGA = 1.6
ACCEL = (0.002, 0.0, -0.003)
SHIFT = tuple(a / OMEGA for a in ACCEL)

VELOCITIES = [
    (0, 0, 0),
    (1, 0, 0),
    (-1, 0, 0),
    (0, 1, 0),
    (0, -1, 0),
    (0, 0, 1),
    (0, 0, -1),
    (1, 1, 0),
    (-1, -1, 0),
    (1, -1, 0),
    (-1, 1, 0),
    (1, 0, 1),
    (-1, 0, -1),
    (1, 0, -1),
    (-1, 0, 1),
    (0, 1, 1),
    (0, -1, -1),
    (0, 1, -1),
    (0, -1, 1),
]
OPPOSITE = [0, 2, 1, 4, 3, 6, 5, 8, 7, 10, 9, 12, 11, 14, 13, 16, 15, 18, 17]
PAIRS = [(i, i + 1) for i in range(1, Q, 2)]
W_REST, W_AXIS, W_DIAG = 1.0 / 3.0, 1.0 / 18.0, 1.0 / 36.0

Y_CODE1, Y_CODE2, Y_CODE3, Y_POP, Y_COT = 38, 39, 40, 41, 42
Y_TILES = 43
X_EXTRA = 19
X_LANE = 20
X_SIDE = 2 * X_LANE
X_RING = 4 * X_LANE
X_CODE13 = X_RING + Q + 1
X_CODE2 = X_CODE13 + 4
X_TILES = X_CODE2 + 2
EMPTY = 25
FREE = NZ - EMPTY
WEIGHTS = [W_REST] + [W_AXIS] * 6 + [W_DIAG] * 12
LEVEL = [i for i, v in enumerate(VELOCITIES) if v[2] < 1]
OWN_PHI = 4


def turned(axis, outward):
    return [i for i, v in enumerate(VELOCITIES) if v[axis] == outward and sum(map(abs, v)) == 2]


def total(values):
    values = list(values)
    while len(values) > 1:
        values = [a + b for a, b in zip(values[::2], values[1::2])] + (
            [values[-1]] if len(values) % 2 else []
        )
    return values[0]


def along(vector, three):
    terms = None
    for c, value in zip(vector, three):
        if c == 0:
            continue
        if terms is None:
            terms = value if c > 0 else -value
        else:
            terms = terms + value if c > 0 else terms - value
    return terms


def moments(f):
    plus = {i: f[i] + f[o] for i, o in PAIRS}
    minus = {i: f[i] - f[o] for i, o in PAIRS}
    rho = total([f[0]] + [plus[i] for i, _ in PAIRS])
    rinv = 1.0 / rho
    u = []
    for axis in range(3):
        terms = [
            minus[i] if VELOCITIES[i][axis] > 0 else -minus[i]
            for i, _ in PAIRS
            if VELOCITIES[i][axis] != 0
        ]
        u.append(total(terms) * rinv + SHIFT[axis])
    return plus, minus, rho, rinv, u


def coefficients(kind, phi, rinv):
    baffle = kind == 3.0
    gas = kind == 0.0
    even = jnp.where(gas, 0.0, jnp.where(baffle, 0.5 - 0.5 * OMEGA * phi, 0.5 * (1.0 - OMEGA)))
    odd = jnp.where(
        gas, 0.0, jnp.where(baffle, (1.0 - 0.5 * OMEGA) * phi - 0.5, 0.5 * (1.0 - OMEGA))
    )
    slope = jnp.where(
        baffle,
        OMEGA * phi,
        jnp.where(kind == 1.0, OMEGA, jnp.where(kind == 2.0, OMEGA * rinv, 0.0)),
    )
    return even, odd, slope


def collide(f, kind, phi, parts):
    plus, minus, rho, rinv, u = parts
    even, odd, slope = coefficients(kind, phi, rinv)
    scale = slope * rho
    rest = 1.0 - 1.5 * (u[0] * u[0] + u[1] * u[1] + u[2] * u[2])
    base = scale * rest + jnp.where(kind == 0.0, 1.0, 0.0)
    out = [None] * Q
    out[0] = 2.0 * even * f[0] + W_REST * base
    for weight, pairs in ((W_AXIS, PAIRS[:3]), (W_DIAG, PAIRS[3:])):
        flat = weight * base
        three = (3.0 * weight) * scale
        for i, o in pairs:
            cu = along(VELOCITIES[i], u)
            lin = three * cu
            ev = even * plus[i] + (flat + 1.5 * lin * cu)
            od = odd * minus[i] + lin
            out[i] = ev + od
            out[o] = ev - od
    return out


def collide_back(b, kind, phi, rho, rinv, u, state=None):
    even, odd, slope = coefficients(kind, phi, rinv)
    plus = {i: b[i] + b[o] for i, o in PAIRS}
    minus = {i: b[i] - b[o] for i, o in PAIRS}
    rest = 1.0 - 1.5 * (u[0] * u[0] + u[1] * u[1] + u[2] * u[2])
    u_half = [1.5 * c for c in u]
    weighted = W_REST * b[0]
    energy = 0.0
    vector = [0.0, 0.0, 0.0]
    for weight, pairs in ((W_AXIS, PAIRS[:3]), (W_DIAG, PAIRS[3:])):
        weighted = weighted + weight * total([plus[i] for i, _ in pairs])
        energies, parts = [], ([], [], [])
        for i, _ in pairs:
            cu = along(VELOCITIES[i], u)
            half = along(VELOCITIES[i], u_half) * plus[i]
            first = minus[i] + half
            energies.append(cu * first)
            second = first + half
            for axis in range(3):
                c = VELOCITIES[i][axis]
                if c:
                    parts[axis].append(second if c > 0 else -second)
        energy = energy + (3.0 * weight) * total(energies)
        vector = [vector[k] + (3.0 * weight) * total(parts[k]) for k in range(3)]
    energy = energy + rest * weighted
    vector = [vector[k] - (3.0 * weighted) * u[k] for k in range(3)]
    push = [slope * v for v in vector]
    inner = total([push[k] * (u[k] - SHIFT[k]) for k in range(3)])
    shared = jnp.where(kind == 2.0, 0.0, slope) * energy - inner
    out = [None] * Q
    out[0] = 2.0 * even * b[0] + shared
    for i, o in PAIRS:
        ev = even * plus[i] + shared
        od = odd * minus[i] + along(VELOCITIES[i], push)
        out[i] = ev + od
        out[o] = ev - od
    if state is None:
        return out, None
    evens = total([plus[i] * (state[i] + state[o]) for i, o in PAIRS])
    odds = total([minus[i] * (state[i] - state[o]) for i, o in PAIRS])
    term = (
        -OMEGA * (b[0] * state[0] + 0.5 * evens)
        + (1.0 - 0.5 * OMEGA) * odds
        + OMEGA * rho * energy
    )
    return out, jnp.where(kind == 3.0, term, 0.0)


def wall_masks(sign_rows, own_low, own_high, edges):
    lane = lax.broadcasted_iota(jnp.int32, (ROWS, LANES), 1)
    row = lax.broadcasted_iota(jnp.int32, (ROWS, LANES), 0)
    x_low, x_high, y_low, y_high = edges
    depth = lane % NZ
    masks = {}
    masks[2, 1] = depth == 0
    masks[2, -1] = depth == NZ - 1
    masks[1, 1] = lane < jnp.where(own_low, y_low * NZ, 0)
    masks[1, -1] = lane >= jnp.where(own_high, LANES - y_high * NZ, LANES)
    if sign_rows:
        masks[0, 1] = row < x_low
        masks[0, -1] = row >= ROWS - x_high
    return masks


def stream_tile(load, sign, masks, lane):
    cross_low, cross_high = lane >= LANES - NZ, lane < NZ
    combined = {}
    out = []
    for i, vector in enumerate(VELOCITIES):
        v = tuple(sign * c for c in vector)
        value = load(i, 0, -v[0], v[1])
        if v[1] == 1:
            value = jnp.where(cross_low, load(i, -1, -v[0], 1), value)
        elif v[1] == -1:
            value = jnp.where(cross_high, load(i, 1, -v[0], -1), value)
        amount = (v[1] * NZ + v[2]) % LANES
        if amount:
            value = pltpu.roll(value, amount, 1)
        outside = None
        if v not in combined:
            for axis in range(3):
                if v[axis] and (axis, v[axis]) in masks:
                    wall = masks[axis, v[axis]]
                    outside = wall if outside is None else outside | wall
            combined[v] = outside
        outside = combined[v]
        if outside is not None:
            value = jnp.where(outside, load(OPPOSITE[i], 0, 0, 0), value)
        out.append(value)
    return out


def iotas():
    row = lax.broadcasted_iota(jnp.int32, (ROWS, LANES), 0)
    lane = lax.broadcasted_iota(jnp.int32, (ROWS, LANES), 1)
    return row, lane, lane // NZ, lane % NZ


def columns(value, count):
    amount = (count * NZ) % LANES
    return pltpu.roll(value, amount, 1) if amount else value


def lines(value, count):
    amount = count % ROWS
    return pltpu.roll(value, amount, 0) if amount else value


class Layout:
    def __init__(self, count, guests, fills):
        self.fills = fills
        hosts = [at for at in fills if at not in guests]
        self.hosts = {at: hosts[4 * n : 4 * n + 4] for n, at in enumerate(guests)}
        self.guests = guests
        kept = [at for at in range(count) if at not in guests]
        self.place = {at: n for n, at in enumerate(kept)}
        self.size = len(kept)


class Packing:
    def __init__(self, ref, layout):
        self.ref, self.layout, self.held = ref, layout, {}

    def __setitem__(self, at, value):
        if at in self.layout.guests:
            self.held[at] = value
        else:
            self.ref[self.layout.place[at]] = value

    def finish(self):
        row, lane, column, depth = iotas()
        spare = depth >= EMPTY
        for at, value in self.held.items():
            for k, host in enumerate(self.layout.hosts[at]):
                place = self.layout.place[host]
                moved = pltpu.roll(value, EMPTY - FREE * k, 1)
                self.ref[place] = jnp.where(spare, moved, self.ref[place])
        for place in range(self.layout.size, self.ref.shape[0]):
            self.ref[place] = jnp.zeros((ROWS, LANES), jnp.float32)


class Unpacking:
    def __init__(self, source, layout):
        self.source, self.layout, self.cache = source, layout, {}
        self.changed = set(layout.guests).union(*layout.hosts.values())

    def __getitem__(self, at):
        if at not in self.cache:
            self.cache[at] = self.read(at)
        return self.cache[at]

    def read(self, at):
        row, lane, column, depth = iotas()
        layout = self.layout
        if at in layout.guests:
            value = None
            for k, host in enumerate(layout.hosts[at]):
                tile = self.source[layout.place[host]]
                moved = pltpu.roll(tile, LANES - (EMPTY - FREE * k), 1)
                value = moved if value is None else jnp.where(depth >= FREE * k, moved, value)
        else:
            value = self.source[layout.place[at]]
        if at in self.changed:
            value = jnp.where(depth >= EMPTY, layout.fills[at], value)
        return value


def layouts():
    y_fills = {2 * i + t: WEIGHTS[i] for i in LEVEL for t in range(2)}
    y_fills.update({Y_POP: W_DIAG, Y_CODE2: 0.0})
    x_fills = {X_LANE * n + i: WEIGHTS[i] for n in range(4) for i in LEVEL}
    side = {at: fill for at, fill in x_fills.items() if at < X_SIDE}
    rest = {at - X_SIDE: fill for at, fill in x_fills.items() if at >= X_SIDE}
    rest.update({X_CODE2 - X_SIDE: 0.0, X_CODE2 + 1 - X_SIDE: 0.0})
    rest.update({X_RING - X_SIDE + i: WEIGHTS[i] for i in range(Q)})
    ring = [X_RING - X_SIDE + i for i in range(9)]
    return (
        Layout(Y_TILES, [2 * i for i in LEVEL[:6]], y_fills),
        Layout(X_SIDE, LEVEL[:5], side),
        Layout(X_TILES - X_SIDE, ring, rest),
    )


class Pick:
    def __init__(self, flag, first, second):
        self.flag, self.first, self.second = flag, first, second

    def __getitem__(self, at):
        return jnp.where(self.flag, self.first[at], self.second[at])


class Deal:
    def __init__(self, even, first, second, layout, skip=0):
        self.even, self.skip, self.held = even, skip, {}
        self.first, self.second = Packing(first, layout), Packing(second, layout)

    def put(self, way, at, value):
        if (-way, at) not in self.held:
            self.held[way, at] = value
            return
        other = self.held.pop((-way, at))
        up, down = (value, other) if way == 1 else (other, value)
        self.first[at - self.skip] = jnp.where(self.even, up, down)
        self.second[at - self.skip] = jnp.where(self.even, down, up)

    def put_both(self, at, value):
        self.first[at - self.skip] = value
        self.second[at - self.skip] = value

    def finish(self):
        self.first.finish()
        self.second.finish()


class Shifted:
    def __init__(self, ref, start):
        self.ref, self.start = ref, start

    def __getitem__(self, at):
        return self.ref[at - self.start]


def is_even(axis):
    return lax.rem(lax.axis_index(axis), 2) == 0


def pack_own(
    f_hbm,
    cot_hbm,
    codes_hbm,
    panels_hbm,
    porosity_hbm,
    first_ref,
    second_ref,
    first_side_ref,
    second_side_ref,
    own_ref,
    state_ref,
    own_cot_ref,
    field_ref,
    names_ref,
    f_ref,
    cot_ref,
    codes_ref,
    panels_ref,
    porosity_ref,
    sems,
):
    pieces = (
        (panels_hbm, panels_ref),
        (porosity_hbm, porosity_ref),
        (f_hbm, f_ref),
        (codes_hbm, codes_ref),
        (cot_hbm, cot_ref),
    )
    copies = [
        pltpu.make_async_copy(source, target, sems.at[n])
        for n, (source, target) in enumerate(pieces)
    ]
    for copy in copies:
        copy.start()
    for copy in copies[:4]:
        copy.wait()
    y_layout, side_layout, _ = layouts()
    deal = Deal(is_even("gy"), first_ref, second_ref, y_layout)
    side = Deal(is_even("gx"), first_side_ref, second_side_ref, side_layout)
    row, lane, column, depth = iotas()
    top = depth == NZ - 1

    def tile_of(ref, i, t):
        return ref[i, :, pl.ds(t * LANES, LANES)]

    codes, phis = [], []
    for t in range(2):
        names = panels_ref[0, t * LANES], panels_ref[4, t * LANES]
        phi = jnp.where(row < 4, porosity_ref[names[0]], porosity_ref[names[1]])
        names_ref[t] = jnp.where(row < 4, names[0], names[1])
        kinds = [tile_of(codes_ref, s, t).astype(jnp.float32) for s in range(STEPS)]
        f = [tile_of(f_ref, i, t) for i in range(Q)]
        g = collide(f, kinds[0], phi, moments(f))
        for i in range(Q):
            own_ref[2 * i + t] = g[i]
            state_ref[2 * i + t] = f[i]
        for s in range(STEPS):
            field_ref[2 * s + t] = kinds[s]
        field_ref[2 * OWN_PHI + t] = phi
        codes.append([jnp.where(top, phi, kinds[1]), kinds[2], kinds[3]])
    copies[4].wait()
    for i in range(Q):
        for way in (1, -1):
            near, far = (1, 0) if way == 1 else (0, 1)
            deep = 3 - way * VELOCITIES[i][1]
            cot = tile_of(cot_ref, i, near)
            g_far = own_ref[2 * i + far]
            if way == 1:
                mixed = jnp.where(column >= deep, g_far, columns(cot, deep - 4))
            else:
                mixed = jnp.where(column < 4 - deep, g_far, columns(cot, 4 - deep))
            deal.put(way, 2 * i, mixed if far == 0 else own_ref[2 * i])
            deal.put(way, 2 * i + 1, mixed if far == 1 else own_ref[2 * i + 1])
    for way in (1, -1):
        near, far = (1, 0) if way == 1 else (0, 1)
        outer = 3 if way == 1 else 0
        deal.put(way, Y_CODE1, codes[near][0])
        deal.put(way, Y_CODE2, codes[near][1])
        outside = columns(codes[far][0], 3 - 2 * outer)
        deal.put(way, Y_CODE3, jnp.where(column == 3 - outer, outside, codes[near][2]))
        extra = None
        for k, i in enumerate(turned(1, -way)):
            value = columns(own_ref[2 * i + far], k - outer)
            extra = value if extra is None else jnp.where(column == k, value, extra)
        deal.put(way, Y_POP, extra)
        extra = None
        for k, i in enumerate(turned(1, way)):
            value = columns(tile_of(cot_ref, i, near), k - (1 if way == 1 else 2))
            extra = value if extra is None else jnp.where(column == k, value, extra)
        deal.put(way, Y_COT, extra)
    deal.finish()
    for t in range(2):
        for i in range(Q):
            own_cot_ref[2 * i + t] = tile_of(cot_ref, i, t)
        pack_lines(
            side,
            X_LANE * t,
            lambda i: own_ref[2 * i + t],
            lambda i: tile_of(cot_ref, i, t),
        )
    side.finish()


def from_y(left_ref, right_ref):
    row, lane, column, depth = iotas()
    high = lane >= LANES // 2

    def population(i, c):
        if c == 1:
            return left_ref[2 * i + 1]
        if c == 4:
            return right_ref[2 * i]
        along_y = VELOCITIES[i][1]
        left, right = left_ref[2 * i], right_ref[2 * i + 1]
        if along_y == 1 and i in turned(1, 1):
            right = columns(right_ref[Y_POP], -turned(1, 1).index(i))
        if along_y == -1 and i in turned(1, -1):
            left = columns(left_ref[Y_POP], 3 - turned(1, -1).index(i))
        return jnp.where(high, left, right)

    def cotangent(i, c):
        ref, way, place, far = (left_ref, 1, 1, 0) if c == 1 else (right_ref, -1, 2, 1)
        deep = 3 - way * VELOCITIES[i][1]
        value = columns(ref[2 * i + far], way * (4 - deep))
        if i in turned(1, way):
            extra = columns(ref[Y_COT], place - turned(1, way).index(i))
            value = jnp.where(column == place, extra, value)
        return value

    def codes(s, c):
        if c == 0:
            left, right = columns(left_ref[Y_CODE3], 3), columns(right_ref[Y_CODE3], 1)
            return jnp.where(high, left, right)
        return (left_ref if c == 1 else right_ref)[(Y_CODE1, Y_CODE2, Y_CODE3)[s - 1]]

    return population, cotangent, codes


def mix_lines(deal, at, pop, cot, deep, way):
    row, lane, column, depth = iotas()
    if way == 1:
        mixed = jnp.where(row >= deep, pop, lines(cot, deep))
    else:
        mixed = jnp.where(row < ROWS - deep, pop, lines(cot, -deep))
    deal.put(way, at, mixed)


def pack_lines(deal, first, population, cotangent):
    row, lane, column, depth = iotas()

    for i in range(Q):
        pop, cot = population(i), cotangent(i)
        for way in (1, -1):
            mix_lines(deal, first + i, pop, cot, 3 - way * VELOCITIES[i][0], way)
    for way in (1, -1):
        extra = None
        for k, i in enumerate(turned(0, -way)):
            value = lines(population(i), k - (3 if way == 1 else 4))
            extra = value if extra is None else jnp.where(row == k, value, extra)
        for k, i in enumerate(turned(0, way)):
            value = lines(cotangent(i), 4 + k - (5 if way == 1 else 2))
            extra = jnp.where(row == 4 + k, value, extra)
        deal.put(way, first + X_EXTRA, extra)


def from_x(ref, n, way):
    row, lane, column, depth = iotas()
    first = X_LANE * n

    def population(i):
        value = ref[first + i]
        if i in turned(0, -way):
            place = 3 if way == 1 else 4
            extra = lines(ref[first + X_EXTRA], place - turned(0, -way).index(i))
            value = jnp.where(row == place, extra, value)
        return value

    def cotangent(i):
        value = lines(ref[first + i], -way * (3 - way * VELOCITIES[i][0]))
        if i in turned(0, way):
            place = 5 if way == 1 else 2
            extra = lines(ref[first + X_EXTRA], place - 4 - turned(0, way).index(i))
            value = jnp.where(row == place, extra, value)
        return value

    def codes(s):
        if s == 2:
            return lines(ref[X_CODE2 + n // 2], 4 * (n % 2))
        value = ref[X_CODE13 + n]
        return value if s == 1 else lines(value, -3 * way)

    return population, cotangent, codes


def pack_x(field_ref, first_y_ref, second_y_ref, first_ref, second_ref):
    row, lane, column, depth = iotas()
    y_layout, _, layout = layouts()
    deal = Deal(is_even("gx"), first_ref, second_ref, layout, X_SIDE)
    population, cotangent, codes = from_y(*sides(first_y_ref, second_y_ref, "gy", y_layout))

    def both_codes(at, first, second):
        second = lines(second, 4)
        deal.put(1, at, jnp.where(row >= 4, first, second))
        deal.put(-1, at, jnp.where(row < 4, first, second))

    for n, c in ((2, 1), (3, 4)):
        pack_lines(
            deal,
            X_LANE * n,
            lambda i: population(i, c),
            lambda i: cotangent(i, c),
        )
    for n in range(Q + 1):
        value = population(n, 0) if n < Q else codes(1, 0)
        deal.put_both(X_RING + n, value)
    for n in range(4):
        if n < 2:
            first = jnp.where(depth == NZ - 1, field_ref[2 * OWN_PHI + n], field_ref[2 + n])
            third = field_ref[6 + n]
        else:
            c = (1, 4)[n - 2]
            first, third = codes(1, c), codes(3, c)
        for way in (1, -1):
            mix_lines(deal, X_CODE13 + n, first, third, 3, way)
    both_codes(X_CODE2, field_ref[4], field_ref[5])
    both_codes(X_CODE2 + 1, codes(2, 1), codes(2, 4))
    deal.finish()


def sides(first_ref, second_ref, axis, layout):
    even = is_even(axis)
    picks = Pick(even, second_ref, first_ref), Pick(even, first_ref, second_ref)
    return [Unpacking(pick, layout) for pick in picks]


def own_rows(step=0):
    return pl.ds(ROWS + step, ROWS)


def halo_rows(step=0):
    return pl.ds({0: 2 * ROWS, -1: 2 * ROWS - 1, 1: 1}[step], ROWS)


def put_halo(ref, at, halo):
    ref[at, pl.ds(0, ROWS), :] = halo
    ref[at, halo_rows(), :] = halo


def put_ring(ref, at, own, halo):
    ref[at, own_rows(), :] = own
    put_halo(ref, at, halo)


def expand(code):
    row, lane, column, depth = iotas()
    top = depth == NZ - 1
    phi = jnp.where(top, code, 0.0)
    for step in (1, 2, 4, 8, 16):
        phi = phi + pltpu.roll(phi, LANES - step, 1)
    return jnp.where(top, 0.0, code), phi


def lay_own(c, population, cotangent, codes, code_phi, pop, cot, wide, field):
    for i in range(Q):
        pop[5 * i + c, pl.ds(2 * ROWS, ROWS), :] = population(i)
        if c:
            cot[4 * i + c - 1, own_rows(), :] = cotangent(i)
    for n in range(2):
        wide[n, c, 1] = code_phi[n]
    if c:
        field[0, c - 1, 0], field[1, c - 1, 0] = code_phi[1], code_phi[0]
        for s in (2, 3):
            field[s, c - 1, 0] = codes(s)


def lay_halo(c, below, above, pop, cot):
    row, lane, column, depth = iotas()
    for i in range(Q):
        pop[5 * i + c, pl.ds(ROWS, ROWS), :] = below[0](i)
        pop[5 * i + c, pl.ds(3 * ROWS, ROWS), :] = above[0](i)
        if c:
            put_halo(cot, 4 * i + c - 1, jnp.where(row < 4, above[1](i), below[1](i)))


def lay_codes(c, below, above, wide, field):
    row, lane, column, depth = iotas()
    before, after = expand(below[2](1)), expand(above[2](1))
    for n in range(2):
        wide[n, c, 0], wide[n, c, 2] = before[n], after[n]
    if c:
        for n, place in ((0, 1), (1, 0)):
            field[place, c - 1, 1] = jnp.where(row < 4, after[n], before[n])
        for s in (2, 3):
            field[s, c - 1, 1] = jnp.where(row < 4, above[2](s), below[2](s))


def lay_out(
    first_y_ref,
    second_y_ref,
    first_side_ref,
    second_side_ref,
    own_ref,
    field_ref,
    cot_ref,
    pop,
    cot,
    wide,
    field,
):
    y_layout, side_layout, _ = layouts()
    from_left = from_y(*sides(first_y_ref, second_y_ref, "gy", y_layout))
    below, above = sides(first_side_ref, second_side_ref, "gx", side_layout)
    for c in range(5):
        t = c - 2
        if t in (0, 1):
            lay_own(
                c,
                lambda i: own_ref[2 * i + t],
                lambda i: cot_ref[2 * i + t],
                lambda s: field_ref[2 * s + t],
                (field_ref[2 + t], field_ref[2 * OWN_PHI + t]),
                pop,
                cot,
                wide,
                field,
            )
            lay_halo(c, from_x(below, t, 1), from_x(above, t, -1), pop, cot)
        else:
            own = [functools.partial(lambda g, n: g(n, c), get) for get in from_left]
            lay_own(c, *own, expand(own[2](1)), pop, cot, wide, field)


def lay_halos(below, above, pop, cot, wide, field):
    ring = [
        (lambda i, ref=ref: ref[X_RING + i], None, lambda s, ref=ref: ref[X_RING + Q])
        for ref in (below, above)
    ]
    lay_halo(0, *ring, pop, cot)
    lay_codes(0, *ring, wide, field)
    for n, c in enumerate((2, 3, 1, 4)):
        halves = from_x(below, n, 1), from_x(above, n, -1)
        if n > 1:
            lay_halo(c, *halves, pop, cot)
        lay_codes(c, *halves, wide, field)


def steps_kernel(
    sizes,
    state_ref,
    own_field_ref,
    names_ref,
    first_x_ref,
    second_x_ref,
    *refs,
):
    adjoint_ref, panel_ref, pop_a, ring_a, wide, field, pop_b, ring_b, saved, mom, grad = refs[4:]
    size_x, size_y = sizes
    halves = sides(first_x_ref, second_x_ref, "gx", layouts()[2])
    below, above = (Shifted(ref, X_SIDE) for ref in halves)
    lay_halos(below, above, pop_a, ring_a, wide, field)

    at_x, at_y = lax.axis_index("gx"), lax.axis_index("gy")
    edges = (
        jnp.where(at_x == 0, 1, 0),
        jnp.where(at_x == size_x - 1, 1, 0),
        jnp.where(at_y == 0, 1, 0),
        jnp.where(at_y == size_y - 1, 1, 0),
    )
    row, lane, column, depth = iotas()
    after = row < 4

    def masks_of(tile, first, r):
        return wall_masks(r == 0, tile == first, tile == first + 1, edges)

    def neighbours(tile, tiles):
        if isinstance(tile, int):
            return {0: tile, -1: (tile - 1) % tiles, 1: (tile + 1) % tiles}
        return {0: tile, -1: lax.rem(tile + tiles - 1, tiles), 1: lax.rem(tile + 1, tiles)}

    def from_wide(ref, tile, r):
        step = neighbours(tile, 5)

        def load(i, tile_step, row_step, move):
            at = 5 * i + step[tile_step]
            before, own, behind = (ref[at, pl.ds(ROWS * n + row_step, ROWS), :] for n in (1, 2, 3))
            return (own, jnp.where(after, behind, before), before, behind)[r]

        return load

    def from_ring(ref, tile, tiles, r):
        step = neighbours(tile, tiles)

        def load(i, tile_step, row_step, move):
            rows = own_rows(row_step) if r == 0 else halo_rows(row_step)
            return ref[tiles * i + step[tile_step], rows, :]

        return load

    def from_outer(ref, r):
        def load(i, tile_step, row_step, move):
            rows = own_rows(row_step) if r == 0 else halo_rows(row_step)
            if tile_step:
                return ref[4 * i + (2 if tile_step < 0 else 1), rows, :]
            cut = {0: 2, 1: 1, -1: 3}[move]
            return jnp.where(column < cut, ref[4 * i + 3, rows, :], ref[4 * i, rows, :])

        return load

    def note(s, tile, r, parts):
        for n, value in enumerate(parts[2:4] + tuple(parts[4])):
            mom[s - 1, n, tile, r] = value

    def first_step(tile, carry):
        place = lax.rem(tile + 4, 5)
        halo = []
        for r in (2, 0, 3):
            f = stream_tile(from_wide(pop_a, tile, r), 1, masks_of(tile, 2, r), lane)
            parts = moments(f)
            if r == 0:
                note(1, place, 0, parts)
                for i in range(Q):
                    saved[0, i, place] = f[i]
            else:
                halo.append(parts[2:4] + tuple(parts[4]))
            at = {2: 0, 0: 1, 3: 2}[r]
            g = collide(f, wide[0, tile, at], wide[1, tile, at], parts)
            for i in range(Q):
                pop_b[5 * i + tile, pl.ds(ROWS * (at + 1), ROWS), :] = g[i]
        for n in range(5):
            mom[0, n, place, 1] = jnp.where(after, halo[1][n], halo[0][n])
        return carry

    lax.fori_loop(0, 5, first_step, 0)

    def second_step(tile, carry):
        out = []
        for r in range(2):
            f = stream_tile(from_wide(pop_b, tile + 1, r), 1, masks_of(tile, 1, r), lane)
            parts = moments(f)
            note(2, tile, r, parts)
            if r == 0:
                for i in range(Q):
                    saved[1, i, tile] = f[i]
            out.append(collide(f, field[2, tile, r], field[0, tile, r], parts))
        for i in range(Q):
            put_ring(ring_b, 4 * i + tile, out[0][i], out[1][i])
        return carry

    lax.fori_loop(0, 4, second_step, 0)

    def third_step(tile, carry):
        for r in range(2):
            f = stream_tile(from_ring(ring_b, tile, 4, r), 1, masks_of(tile, 1, r), lane)
            note(3, tile, r, moments(f))
            if r == 0:
                for i in range(Q):
                    saved[2, i, tile] = f[i]
        return carry

    lax.fori_loop(0, 4, third_step, 0)

    def back_tile(load, s, tile, r, own):
        b = stream_tile(load, -1, masks_of(4 if tile is None else tile, 1, r), lane)

        def read(get):
            return jnp.where(column < 2, get(3), get(0)) if tile is None else get(tile)

        rho, rinv, *u = [read(lambda at: mom[s - 1, n, at, r]) for n in range(5)]
        kind, phi = read(lambda at: field[s, at, r]), read(lambda at: field[0, at, r])
        state = [saved[s - 1, i, tile] for i in range(Q)] if own else None
        back, term = collide_back(b, kind, phi, rho, rinv, u, state)
        if own:
            grad[tile] = term if s == 3 else grad[tile] + term
        return back

    def last_step(tile, carry):
        out = [back_tile(from_ring(ring_a, tile, 4, r), 3, tile, r, r == 0) for r in range(2)]
        for i in range(Q):
            put_ring(ring_b, 4 * i + tile, out[0][i], out[1][i])
        return carry

    lax.fori_loop(0, 4, last_step, 0)

    for k, tile in enumerate((1, 2, None)):
        out = []
        for r in range(2):
            load = from_outer(ring_b, r) if tile is None else from_ring(ring_b, tile, 4, r)
            out.append(back_tile(load, 2, tile, r, r == 0 and tile is not None))
        for i in range(Q):
            put_ring(ring_a, 3 * i + k, out[0][i], out[1][i])

    for k, tile in enumerate((1, 2, None)):
        out = []
        for r in range(2):
            load = from_ring(ring_a, k, 3, r)
            out.append(back_tile(load, 1, tile, r, r == 0 and tile is not None))
        for i in range(Q):
            put_ring(ring_b, 3 * i + k, out[0][i], out[1][i])

    panel = lax.broadcasted_iota(jnp.int32, panel_ref.shape, 1)
    sums = jnp.zeros(panel_ref.shape, jnp.float32)
    for t in range(2):
        b = stream_tile(from_ring(ring_b, t, 3, 0), -1, masks_of(t, 0, 0), lane)
        f = [state_ref[2 * i + t] for i in range(Q)]
        kind, phi = own_field_ref[t], own_field_ref[2 * OWN_PHI + t]
        _, _, rho, rinv, u = moments(f)
        back, term = collide_back(b, kind, phi, rho, rinv, u, f)
        for i in range(Q):
            adjoint_ref[i, :, pl.ds(t * LANES, LANES)] = back[i]
        term = term + grad[t + 1]
        for part in range(2):
            amount = jnp.sum(jnp.where((row < 4) == (part == 0), term, 0.0))
            name = names_ref[t, 4 * part : 4 * part + 1, 0:1]
            sums = sums + jnp.where(panel == name, amount, 0.0)
    panel_ref[...] = sums


def finish(parts_ref, adjoint_ref, sums_hbm, adjoint_hbm, sums_ref, sems):
    adjoint_copy = pltpu.make_async_copy(adjoint_ref, adjoint_hbm, sems.at[0])
    adjoint_copy.start()
    sums_ref[...] = jnp.sum(parts_ref[...], axis=0)
    sums_copy = pltpu.make_async_copy(sums_ref, sums_hbm, sems.at[1])
    sums_copy.start()
    sums_copy.wait()
    adjoint_copy.wait()


VMEM = pl.BlockSpec(memory_space=pltpu.VMEM)
HBM = pl.BlockSpec(memory_space=pltpu.HBM)


def shape_of(*dims):
    return jax.ShapeDtypeStruct(dims, jnp.float32)


def tiles_of(count):
    return shape_of(count, ROWS, LANES)


def on_device(sizes, checkpoint, cotangent, cell_codes, porosity, baffle_index):
    size_x, size_y = sizes
    panels = porosity.shape[0]
    devices = size_x * size_y
    y_layout, side_layout, rest_layout = layouts()

    params = pltpu.CompilerParams(vmem_limit_bytes=32 * 1024 * 1024)

    def call(kernel, out_shape, in_specs, scratch=(), name=None, aliases={}):
        return pl.pallas_call(
            kernel,
            out_shape=out_shape,
            in_specs=in_specs,
            out_specs=jax.tree.map(lambda _: VMEM, out_shape),
            scratch_shapes=scratch,
            input_output_aliases=aliases,
            compiler_params=params,
            name=name,
        )

    def swap(value, axis, size):
        return lax.ppermute(value, axis, [(i, i ^ 1) for i in range(size) if i ^ 1 < size])

    def swap_between(value, axis, size):
        pairs = [(i, i + 1) for i in range(1, size - 1, 2)]
        return lax.ppermute(value, axis, pairs + [(j, i) for i, j in pairs])

    arguments = [
        pltpu.with_memory_space_constraint(value, pltpu.HBM)
        for value in (checkpoint, cotangent, cell_codes, baffle_index, porosity)
    ]
    first_y, second_y, first_side, second_side, own, state, cot, field, names = call(
        pack_own,
        (tiles_of(y_layout.size),) * 2
        + (tiles_of(side_layout.size), tiles_of(rest_layout.size + 8))
        + (tiles_of(2 * Q),) * 3
        + (tiles_of(2 * OWN_PHI + 2), jax.ShapeDtypeStruct((2, ROWS, LANES), jnp.int32)),
        [HBM] * 5,
        [
            pltpu.VMEM((Q, ROWS, 2 * LANES), jnp.float32),
            pltpu.VMEM((Q, ROWS, 2 * LANES), jnp.float32),
            pltpu.VMEM((STEPS, ROWS, 2 * LANES), jnp.int32),
            pltpu.SMEM(baffle_index.shape, jnp.int32),
            pltpu.SMEM(porosity.shape, jnp.float32),
            pltpu.SemaphoreType.DMA((5,)),
        ],
        name="pack_own",
    )(*arguments)
    second_y = swap_between(second_y, "gy", size_y)
    first_y = swap(first_y, "gy", size_y)
    second_side = swap_between(second_side, "gx", size_x)
    first_side = swap(first_side, "gx", size_x)
    first_x, second_x = call(
        pack_x,
        (tiles_of(rest_layout.size), tiles_of(rest_layout.size + 1)),
        [VMEM] * 3,
        name="pack_x",
    )(field, first_y, second_y)
    second_x = swap_between(second_x, "gx", size_x)
    first_x = swap(first_x, "gx", size_x)

    spaces = (
        shape_of(5 * Q, 5 * ROWS, LANES),
        shape_of(4 * Q, 3 * ROWS, LANES),
        shape_of(2, 5, 3, ROWS, LANES),
        shape_of(4, 4, 2, ROWS, LANES),
    )
    laid = call(lay_out, spaces, [VMEM] * 7, name="lay_out")(
        first_y, second_y, first_side, second_side, own, field, cot
    )
    adjoint, sums, *_ = call(
        functools.partial(steps_kernel, sizes),
        (pltpu.VMEM((Q, ROWS, 2 * LANES), jnp.float32), shape_of(devices, panels)) + spaces,
        [VMEM] * 9,
        [
            pltpu.VMEM((5 * Q, 5 * ROWS, LANES), jnp.float32),
            pltpu.VMEM((4 * Q, 3 * ROWS, LANES), jnp.float32),
            pltpu.VMEM((3, Q, 5, ROWS, LANES), jnp.float32),
            pltpu.VMEM((3, 5, 5, 2, ROWS, LANES), jnp.float32),
            pltpu.VMEM((4, ROWS, LANES), jnp.float32),
        ],
        name="steps",
        aliases={5 + n: 2 + n for n in range(4)},
    )(state, field, names, first_x, second_x, *laid)
    gathered = lax.all_to_all(sums, ("gx", "gy"), 0, 0, tiled=True)
    totals, adjoint = pl.pallas_call(
        finish,
        out_shape=(shape_of(1, panels), shape_of(Q, ROWS, 2 * LANES)),
        in_specs=[VMEM, VMEM],
        out_specs=(HBM, HBM),
        scratch_shapes=[pltpu.VMEM((1, panels), jnp.float32), pltpu.SemaphoreType.DMA((2,))],
        compiler_params=params,
        name="finish",
    )(gathered.reshape(devices, 1, panels), adjoint)
    return adjoint, totals.reshape(panels)


def solution(mesh):
    sizes = (mesh.shape["gx"], mesh.shape["gy"])
    in_specs = (P(None, "gx", "gy"), P(None, "gx", "gy"), P(None, "gx", "gy"), P(), P("gx", "gy"))
    out_specs = (P(None, "gx", "gy"), P())
    return jax.shard_map(
        functools.partial(on_device, sizes),
        mesh=mesh,
        in_specs=in_specs,
        out_specs=out_specs,
        check_vma=False,
    )
```

```python
import functools

import jax
import jax.numpy as jnp
import numpy as np
from jax import lax
from jax.experimental import pallas as pl
from jax.experimental.pallas import tpu as pltpu
from jax.sharding import PartitionSpec as P

Q = 19
STEPS = 4
NZ = 32
ROWS = 8
LANES = 128
OMEGA = 1.6
ACCEL = (0.002, 0.0, -0.003)
SHIFT = tuple(a / OMEGA for a in ACCEL)

VELOCITIES = [
    (0, 0, 0),
    (1, 0, 0),
    (-1, 0, 0),
    (0, 1, 0),
    (0, -1, 0),
    (0, 0, 1),
    (0, 0, -1),
    (1, 1, 0),
    (-1, -1, 0),
    (1, -1, 0),
    (-1, 1, 0),
    (1, 0, 1),
    (-1, 0, -1),
    (1, 0, -1),
    (-1, 0, 1),
    (0, 1, 1),
    (0, -1, -1),
    (0, 1, -1),
    (0, -1, 1),
]
OPPOSITE = [0, 2, 1, 4, 3, 6, 5, 8, 7, 10, 9, 12, 11, 14, 13, 16, 15, 18, 17]
PAIRS = [(i, i + 1) for i in range(1, Q, 2)]
W_REST, W_AXIS, W_DIAG = 1.0 / 3.0, 1.0 / 18.0, 1.0 / 36.0

Y_CODE1, Y_CODE2, Y_CODE3, Y_POP, Y_COT = 38, 39, 40, 41, 42
Y_TILES = 43
X_EXTRA = 19
X_LANE = 20
X_SIDE = 2 * X_LANE
X_RING = 4 * X_LANE
X_CODE13 = X_RING + Q + 1
X_CODE2 = X_CODE13 + 4
X_TILES = X_CODE2 + 2
EMPTY = 25
FREE = NZ - EMPTY
WEIGHTS = [W_REST] + [W_AXIS] * 6 + [W_DIAG] * 12
LEVEL = [i for i, v in enumerate(VELOCITIES) if v[2] < 1]
OWN_PHI = 4


def turned(axis, outward):
    return [i for i, v in enumerate(VELOCITIES) if v[axis] == outward and sum(map(abs, v)) == 2]


def total(values):
    values = list(values)
    while len(values) > 1:
        values = [a + b for a, b in zip(values[::2], values[1::2])] + (
            [values[-1]] if len(values) % 2 else []
        )
    return values[0]


def along(vector, three):
    terms = None
    for c, value in zip(vector, three):
        if c == 0:
            continue
        if terms is None:
            terms = value if c > 0 else -value
        else:
            terms = terms + value if c > 0 else terms - value
    return terms


def moments(f):
    plus = {i: f[i] + f[o] for i, o in PAIRS}
    minus = {i: f[i] - f[o] for i, o in PAIRS}
    rho = total([f[0]] + [plus[i] for i, _ in PAIRS])
    rinv = 1.0 / rho
    u = []
    for axis in range(3):
        terms = [
            minus[i] if VELOCITIES[i][axis] > 0 else -minus[i]
            for i, _ in PAIRS
            if VELOCITIES[i][axis] != 0
        ]
        u.append(total(terms) * rinv + SHIFT[axis])
    return plus, minus, rho, rinv, u


def coefficients(kind, phi, rinv):
    baffle = kind == 3.0
    gas = kind == 0.0
    even = jnp.where(gas, 0.0, jnp.where(baffle, 0.5 - 0.5 * OMEGA * phi, 0.5 * (1.0 - OMEGA)))
    odd = jnp.where(
        gas, 0.0, jnp.where(baffle, (1.0 - 0.5 * OMEGA) * phi - 0.5, 0.5 * (1.0 - OMEGA))
    )
    slope = jnp.where(
        baffle,
        OMEGA * phi,
        jnp.where(kind == 1.0, OMEGA, jnp.where(kind == 2.0, OMEGA * rinv, 0.0)),
    )
    return even, odd, slope


def collide(f, kind, phi, parts):
    plus, minus, rho, rinv, u = parts
    even, odd, slope = coefficients(kind, phi, rinv)
    scale = slope * rho
    rest = 1.0 - 1.5 * (u[0] * u[0] + u[1] * u[1] + u[2] * u[2])
    base = scale * rest + jnp.where(kind == 0.0, 1.0, 0.0)
    out = [None] * Q
    out[0] = 2.0 * even * f[0] + W_REST * base
    for weight, pairs in ((W_AXIS, PAIRS[:3]), (W_DIAG, PAIRS[3:])):
        flat = weight * base
        three = (3.0 * weight) * scale
        for i, o in pairs:
            cu = along(VELOCITIES[i], u)
            lin = three * cu
            ev = even * plus[i] + (flat + 1.5 * lin * cu)
            od = odd * minus[i] + lin
            out[i] = ev + od
            out[o] = ev - od
    return out


def collide_back(b, kind, phi, rho, rinv, u, state=None):
    even, odd, slope = coefficients(kind, phi, rinv)
    plus = {i: b[i] + b[o] for i, o in PAIRS}
    minus = {i: b[i] - b[o] for i, o in PAIRS}
    rest = 1.0 - 1.5 * (u[0] * u[0] + u[1] * u[1] + u[2] * u[2])
    u_half = [1.5 * c for c in u]
    weighted = W_REST * b[0]
    energy = 0.0
    vector = [0.0, 0.0, 0.0]
    for weight, pairs in ((W_AXIS, PAIRS[:3]), (W_DIAG, PAIRS[3:])):
        weighted = weighted + weight * total([plus[i] for i, _ in pairs])
        energies, parts = [], ([], [], [])
        for i, _ in pairs:
            cu = along(VELOCITIES[i], u)
            half = along(VELOCITIES[i], u_half) * plus[i]
            first = minus[i] + half
            energies.append(cu * first)
            second = first + half
            for axis in range(3):
                c = VELOCITIES[i][axis]
                if c:
                    parts[axis].append(second if c > 0 else -second)
        energy = energy + (3.0 * weight) * total(energies)
        vector = [vector[k] + (3.0 * weight) * total(parts[k]) for k in range(3)]
    energy = energy + rest * weighted
    vector = [vector[k] - (3.0 * weighted) * u[k] for k in range(3)]
    push = [slope * v for v in vector]
    inner = total([push[k] * (u[k] - SHIFT[k]) for k in range(3)])
    shared = jnp.where(kind == 2.0, 0.0, slope) * energy - inner
    out = [None] * Q
    out[0] = 2.0 * even * b[0] + shared
    for i, o in PAIRS:
        ev = even * plus[i] + shared
        od = odd * minus[i] + along(VELOCITIES[i], push)
        out[i] = ev + od
        out[o] = ev - od
    if state is None:
        return out, None
    evens = total([plus[i] * (state[i] + state[o]) for i, o in PAIRS])
    odds = total([minus[i] * (state[i] - state[o]) for i, o in PAIRS])
    term = (
        -OMEGA * (b[0] * state[0] + 0.5 * evens)
        + (1.0 - 0.5 * OMEGA) * odds
        + OMEGA * rho * energy
    )
    return out, jnp.where(kind == 3.0, term, 0.0)


def wall_masks(sign_rows, own_low, own_high, edges):
    lane = lax.broadcasted_iota(jnp.int32, (ROWS, LANES), 1)
    row = lax.broadcasted_iota(jnp.int32, (ROWS, LANES), 0)
    x_low, x_high, y_low, y_high = edges
    depth = lane % NZ
    masks = {}
    masks[2, 1] = depth == 0
    masks[2, -1] = depth == NZ - 1
    masks[1, 1] = lane < jnp.where(own_low, y_low * NZ, 0)
    masks[1, -1] = lane >= jnp.where(own_high, LANES - y_high * NZ, LANES)
    if sign_rows:
        masks[0, 1] = row < x_low
        masks[0, -1] = row >= ROWS - x_high
    return masks


def stream_tile(load, sign, masks, lane):
    cross_low, cross_high = lane >= LANES - NZ, lane < NZ
    combined = {}
    out = []
    for i, vector in enumerate(VELOCITIES):
        v = tuple(sign * c for c in vector)
        value = load(i, 0, -v[0], v[1])
        if v[1] == 1:
            value = jnp.where(cross_low, load(i, -1, -v[0], 1), value)
        elif v[1] == -1:
            value = jnp.where(cross_high, load(i, 1, -v[0], -1), value)
        amount = (v[1] * NZ + v[2]) % LANES
        if amount:
            value = pltpu.roll(value, amount, 1)
        outside = None
        if v not in combined:
            for axis in range(3):
                if v[axis] and (axis, v[axis]) in masks:
                    wall = masks[axis, v[axis]]
                    outside = wall if outside is None else outside | wall
            combined[v] = outside
        outside = combined[v]
        if outside is not None:
            value = jnp.where(outside, load(OPPOSITE[i], 0, 0, 0), value)
        out.append(value)
    return out


def iotas():
    row = lax.broadcasted_iota(jnp.int32, (ROWS, LANES), 0)
    lane = lax.broadcasted_iota(jnp.int32, (ROWS, LANES), 1)
    return row, lane, lane // NZ, lane % NZ


def columns(value, count):
    amount = (count * NZ) % LANES
    return pltpu.roll(value, amount, 1) if amount else value


def lines(value, count):
    amount = count % ROWS
    return pltpu.roll(value, amount, 0) if amount else value


class Layout:
    def __init__(self, count, guests, fills):
        self.fills = fills
        hosts = [at for at in fills if at not in guests]
        self.hosts = {at: hosts[4 * n : 4 * n + 4] for n, at in enumerate(guests)}
        self.guests = guests
        kept = [at for at in range(count) if at not in guests]
        self.place = {at: n for n, at in enumerate(kept)}
        self.size = len(kept)


class Packing:
    def __init__(self, ref, layout):
        self.ref, self.layout, self.held = ref, layout, {}

    def __setitem__(self, at, value):
        if at in self.layout.guests:
            self.held[at] = value
        else:
            self.ref[self.layout.place[at]] = value

    def finish(self):
        row, lane, column, depth = iotas()
        spare = depth >= EMPTY
        for at, value in self.held.items():
            for k, host in enumerate(self.layout.hosts[at]):
                place = self.layout.place[host]
                moved = pltpu.roll(value, EMPTY - FREE * k, 1)
                self.ref[place] = jnp.where(spare, moved, self.ref[place])
        for place in range(self.layout.size, self.ref.shape[0]):
            self.ref[place] = jnp.zeros((ROWS, LANES), jnp.float32)


class Unpacking:
    def __init__(self, source, layout):
        self.source, self.layout, self.cache = source, layout, {}
        self.changed = set(layout.guests).union(*layout.hosts.values())

    def __getitem__(self, at):
        if at not in self.cache:
            self.cache[at] = self.read(at)
        return self.cache[at]

    def read(self, at):
        row, lane, column, depth = iotas()
        layout = self.layout
        if at in layout.guests:
            value = None
            for k, host in enumerate(layout.hosts[at]):
                tile = self.source[layout.place[host]]
                moved = pltpu.roll(tile, LANES - (EMPTY - FREE * k), 1)
                value = moved if value is None else jnp.where(depth >= FREE * k, moved, value)
        else:
            value = self.source[layout.place[at]]
        if at in self.changed:
            value = jnp.where(depth >= EMPTY, layout.fills[at], value)
        return value


def layouts():
    y_fills = {2 * i + t: WEIGHTS[i] for i in LEVEL for t in range(2)}
    y_fills.update({Y_POP: W_DIAG, Y_CODE2: 0.0})
    x_fills = {X_LANE * n + i: WEIGHTS[i] for n in range(4) for i in LEVEL}
    side = {at: fill for at, fill in x_fills.items() if at < X_SIDE}
    rest = {at - X_SIDE: fill for at, fill in x_fills.items() if at >= X_SIDE}
    rest.update({X_CODE2 - X_SIDE: 0.0, X_CODE2 + 1 - X_SIDE: 0.0})
    rest.update({X_RING - X_SIDE + i: WEIGHTS[i] for i in range(Q)})
    ring = [X_RING - X_SIDE + i for i in range(9)]
    return (
        Layout(Y_TILES, [2 * i for i in LEVEL[:6]], y_fills),
        Layout(X_SIDE, LEVEL[:5], side),
        Layout(X_TILES - X_SIDE, ring, rest),
    )


class Pick:
    def __init__(self, flag, first, second):
        self.flag, self.first, self.second = flag, first, second

    def __getitem__(self, at):
        return jnp.where(self.flag, self.first[at], self.second[at])


class Deal:
    def __init__(self, even, first, second, layout, skip=0):
        self.even, self.skip, self.held = even, skip, {}
        self.first, self.second = Packing(first, layout), Packing(second, layout)

    def put(self, way, at, value):
        if (-way, at) not in self.held:
            self.held[way, at] = value
            return
        other = self.held.pop((-way, at))
        up, down = (value, other) if way == 1 else (other, value)
        self.first[at - self.skip] = jnp.where(self.even, up, down)
        self.second[at - self.skip] = jnp.where(self.even, down, up)

    def put_both(self, at, value):
        self.first[at - self.skip] = value
        self.second[at - self.skip] = value

    def finish(self):
        self.first.finish()
        self.second.finish()


class Shifted:
    def __init__(self, ref, start):
        self.ref, self.start = ref, start

    def __getitem__(self, at):
        return self.ref[at - self.start]


def is_even(axis):
    return lax.rem(lax.axis_index(axis), 2) == 0


def pack_own(
    f_hbm,
    cot_hbm,
    codes_hbm,
    panels_hbm,
    porosity_hbm,
    first_ref,
    second_ref,
    first_side_ref,
    second_side_ref,
    own_ref,
    state_ref,
    own_cot_ref,
    field_ref,
    names_ref,
    f_ref,
    cot_ref,
    codes_ref,
    panels_ref,
    porosity_ref,
    sems,
):
    pieces = (
        (panels_hbm, panels_ref),
        (porosity_hbm, porosity_ref),
        (f_hbm, f_ref),
        (codes_hbm, codes_ref),
        (cot_hbm, cot_ref),
    )
    copies = [
        pltpu.make_async_copy(source, target, sems.at[n])
        for n, (source, target) in enumerate(pieces)
    ]
    for copy in copies:
        copy.start()
    for copy in copies[:4]:
        copy.wait()
    y_layout, side_layout, _ = layouts()
    deal = Deal(is_even("gy"), first_ref, second_ref, y_layout)
    side = Deal(is_even("gx"), first_side_ref, second_side_ref, side_layout)
    row, lane, column, depth = iotas()
    top = depth == NZ - 1

    def tile_of(ref, i, t):
        return ref[i, :, pl.ds(t * LANES, LANES)]

    codes, phis = [], []
    for t in range(2):
        names = panels_ref[0, t * LANES], panels_ref[4, t * LANES]
        phi = jnp.where(row < 4, porosity_ref[names[0]], porosity_ref[names[1]])
        names_ref[t] = jnp.where(row < 4, names[0], names[1])
        kinds = [tile_of(codes_ref, s, t).astype(jnp.float32) for s in range(STEPS)]
        f = [tile_of(f_ref, i, t) for i in range(Q)]
        g = collide(f, kinds[0], phi, moments(f))
        for i in range(Q):
            own_ref[2 * i + t] = g[i]
            state_ref[2 * i + t] = f[i]
        for s in range(STEPS):
            field_ref[2 * s + t] = kinds[s]
        field_ref[2 * OWN_PHI + t] = phi
        codes.append([jnp.where(top, phi, kinds[1]), kinds[2], kinds[3]])
    copies[4].wait()
    for i in range(Q):
        for way in (1, -1):
            near, far = (1, 0) if way == 1 else (0, 1)
            deep = 3 - way * VELOCITIES[i][1]
            cot = tile_of(cot_ref, i, near)
            g_far = own_ref[2 * i + far]
            if way == 1:
                mixed = jnp.where(column >= deep, g_far, columns(cot, deep - 4))
            else:
                mixed = jnp.where(column < 4 - deep, g_far, columns(cot, 4 - deep))
            deal.put(way, 2 * i, mixed if far == 0 else own_ref[2 * i])
            deal.put(way, 2 * i + 1, mixed if far == 1 else own_ref[2 * i + 1])
    for way in (1, -1):
        near, far = (1, 0) if way == 1 else (0, 1)
        outer = 3 if way == 1 else 0
        deal.put(way, Y_CODE1, codes[near][0])
        deal.put(way, Y_CODE2, codes[near][1])
        outside = columns(codes[far][0], 3 - 2 * outer)
        deal.put(way, Y_CODE3, jnp.where(column == 3 - outer, outside, codes[near][2]))
        extra = None
        for k, i in enumerate(turned(1, -way)):
            value = columns(own_ref[2 * i + far], k - outer)
            extra = value if extra is None else jnp.where(column == k, value, extra)
        deal.put(way, Y_POP, extra)
        extra = None
        for k, i in enumerate(turned(1, way)):
            value = columns(tile_of(cot_ref, i, near), k - (1 if way == 1 else 2))
            extra = value if extra is None else jnp.where(column == k, value, extra)
        deal.put(way, Y_COT, extra)
    deal.finish()
    for t in range(2):
        for i in range(Q):
            own_cot_ref[2 * i + t] = tile_of(cot_ref, i, t)
        pack_lines(
            side,
            X_LANE * t,
            lambda i: own_ref[2 * i + t],
            lambda i: tile_of(cot_ref, i, t),
        )
    side.finish()


def from_y(left_ref, right_ref):
    row, lane, column, depth = iotas()
    high = lane >= LANES // 2

    def population(i, c):
        if c == 1:
            return left_ref[2 * i + 1]
        if c == 4:
            return right_ref[2 * i]
        along_y = VELOCITIES[i][1]
        left, right = left_ref[2 * i], right_ref[2 * i + 1]
        if along_y == 1 and i in turned(1, 1):
            right = columns(right_ref[Y_POP], -turned(1, 1).index(i))
        if along_y == -1 and i in turned(1, -1):
            left = columns(left_ref[Y_POP], 3 - turned(1, -1).index(i))
        return jnp.where(high, left, right)

    def cotangent(i, c):
        ref, way, place, far = (left_ref, 1, 1, 0) if c == 1 else (right_ref, -1, 2, 1)
        deep = 3 - way * VELOCITIES[i][1]
        value = columns(ref[2 * i + far], way * (4 - deep))
        if i in turned(1, way):
            extra = columns(ref[Y_COT], place - turned(1, way).index(i))
            value = jnp.where(column == place, extra, value)
        return value

    def codes(s, c):
        if c == 0:
            left, right = columns(left_ref[Y_CODE3], 3), columns(right_ref[Y_CODE3], 1)
            return jnp.where(high, left, right)
        return (left_ref if c == 1 else right_ref)[(Y_CODE1, Y_CODE2, Y_CODE3)[s - 1]]

    return population, cotangent, codes


def mix_lines(deal, at, pop, cot, deep, way):
    row, lane, column, depth = iotas()
    if way == 1:
        mixed = jnp.where(row >= deep, pop, lines(cot, deep))
    else:
        mixed = jnp.where(row < ROWS - deep, pop, lines(cot, -deep))
    deal.put(way, at, mixed)


def pack_lines(deal, first, population, cotangent):
    row, lane, column, depth = iotas()

    for i in range(Q):
        pop, cot = population(i), cotangent(i)
        for way in (1, -1):
            mix_lines(deal, first + i, pop, cot, 3 - way * VELOCITIES[i][0], way)
    for way in (1, -1):
        extra = None
        for k, i in enumerate(turned(0, -way)):
            value = lines(population(i), k - (3 if way == 1 else 4))
            extra = value if extra is None else jnp.where(row == k, value, extra)
        for k, i in enumerate(turned(0, way)):
            value = lines(cotangent(i), 4 + k - (5 if way == 1 else 2))
            extra = jnp.where(row == 4 + k, value, extra)
        deal.put(way, first + X_EXTRA, extra)


def from_x(ref, n, way):
    row, lane, column, depth = iotas()
    first = X_LANE * n

    def population(i):
        value = ref[first + i]
        if i in turned(0, -way):
            place = 3 if way == 1 else 4
            extra = lines(ref[first + X_EXTRA], place - turned(0, -way).index(i))
            value = jnp.where(row == place, extra, value)
        return value

    def cotangent(i):
        value = lines(ref[first + i], -way * (3 - way * VELOCITIES[i][0]))
        if i in turned(0, way):
            place = 5 if way == 1 else 2
            extra = lines(ref[first + X_EXTRA], place - 4 - turned(0, way).index(i))
            value = jnp.where(row == place, extra, value)
        return value

    def codes(s):
        if s == 2:
            return lines(ref[X_CODE2 + n // 2], 4 * (n % 2))
        value = ref[X_CODE13 + n]
        return value if s == 1 else lines(value, -3 * way)

    return population, cotangent, codes


def pack_x(field_ref, first_y_ref, up_y_ref, down_y_ref, first_ref, second_ref):
    row, lane, column, depth = iotas()
    y_layout, _, layout = layouts()
    deal = Deal(is_even("gx"), first_ref, second_ref, layout, X_SIDE)
    population, cotangent, codes = from_y(*sides(first_y_ref, (up_y_ref, down_y_ref), "gy", y_layout))

    def both_codes(at, first, second):
        second = lines(second, 4)
        deal.put(1, at, jnp.where(row >= 4, first, second))
        deal.put(-1, at, jnp.where(row < 4, first, second))

    for n, c in ((2, 1), (3, 4)):
        pack_lines(
            deal,
            X_LANE * n,
            lambda i: population(i, c),
            lambda i: cotangent(i, c),
        )
    for n in range(Q + 1):
        value = population(n, 0) if n < Q else codes(1, 0)
        deal.put_both(X_RING + n, value)
    for n in range(4):
        if n < 2:
            first = jnp.where(depth == NZ - 1, field_ref[2 * OWN_PHI + n], field_ref[2 + n])
            third = field_ref[6 + n]
        else:
            c = (1, 4)[n - 2]
            first, third = codes(1, c), codes(3, c)
        for way in (1, -1):
            mix_lines(deal, X_CODE13 + n, first, third, 3, way)
    both_codes(X_CODE2, field_ref[4], field_ref[5])
    both_codes(X_CODE2 + 1, codes(2, 1), codes(2, 4))
    deal.finish()


def sides(first_ref, second_ref, axis, layout):
    even = is_even(axis)
    if isinstance(second_ref, tuple):
        second_ref = Pick(even, *second_ref)
    picks = Pick(even, second_ref, first_ref), Pick(even, first_ref, second_ref)
    return [Unpacking(pick, layout) for pick in picks]


def own_rows(step=0):
    return pl.ds(ROWS + step, ROWS)


def halo_rows(step=0):
    return pl.ds({0: 2 * ROWS, -1: 2 * ROWS - 1, 1: 1}[step], ROWS)


def put_halo(ref, at, halo):
    ref[at, pl.ds(0, ROWS), :] = halo
    ref[at, halo_rows(), :] = halo


def put_ring(ref, at, own, halo):
    ref[at, own_rows(), :] = own
    put_halo(ref, at, halo)


def expand(code):
    row, lane, column, depth = iotas()
    top = depth == NZ - 1
    phi = jnp.where(top, code, 0.0)
    for step in (1, 2, 4, 8, 16):
        phi = phi + pltpu.roll(phi, LANES - step, 1)
    return jnp.where(top, 0.0, code), phi


def lay_own(c, population, cotangent, codes, code_phi, pop, cot, wide, field):
    for i in range(Q):
        pop[5 * i + c, pl.ds(2 * ROWS, ROWS), :] = population(i)
        if c:
            cot[4 * i + c - 1, own_rows(), :] = cotangent(i)
    for n in range(2):
        wide[n, c, 1] = code_phi[n]
    if c:
        field[0, c - 1, 0], field[1, c - 1, 0] = code_phi[1], code_phi[0]
        for s in (2, 3):
            field[s, c - 1, 0] = codes(s)


def lay_halo(c, below, above, pop, cot):
    row, lane, column, depth = iotas()
    for i in range(Q):
        pop[5 * i + c, pl.ds(ROWS, ROWS), :] = below[0](i)
        pop[5 * i + c, pl.ds(3 * ROWS, ROWS), :] = above[0](i)
        if c:
            put_halo(cot, 4 * i + c - 1, jnp.where(row < 4, above[1](i), below[1](i)))


def lay_codes(c, below, above, wide, field):
    row, lane, column, depth = iotas()
    before, after = expand(below[2](1)), expand(above[2](1))
    for n in range(2):
        wide[n, c, 0], wide[n, c, 2] = before[n], after[n]
    if c:
        for n, place in ((0, 1), (1, 0)):
            field[place, c - 1, 1] = jnp.where(row < 4, after[n], before[n])
        for s in (2, 3):
            field[s, c - 1, 1] = jnp.where(row < 4, above[2](s), below[2](s))


def lay_out(
    first_y_ref,
    up_y_ref,
    down_y_ref,
    first_side_ref,
    second_side_ref,
    own_ref,
    field_ref,
    cot_ref,
    pop,
    cot,
    wide,
    field,
):
    y_layout, side_layout, _ = layouts()
    from_left = from_y(*sides(first_y_ref, (up_y_ref, down_y_ref), "gy", y_layout))
    below, above = sides(first_side_ref, second_side_ref, "gx", side_layout)
    for c in range(5):
        t = c - 2
        if t in (0, 1):
            lay_own(
                c,
                lambda i: own_ref[2 * i + t],
                lambda i: cot_ref[2 * i + t],
                lambda s: field_ref[2 * s + t],
                (field_ref[2 + t], field_ref[2 * OWN_PHI + t]),
                pop,
                cot,
                wide,
                field,
            )
            lay_halo(c, from_x(below, t, 1), from_x(above, t, -1), pop, cot)
        else:
            own = [functools.partial(lambda g, n: g(n, c), get) for get in from_left]
            lay_own(c, *own, expand(own[2](1)), pop, cot, wide, field)


def lay_halos(below, above, pop, cot, wide, field):
    ring = [
        (lambda i, ref=ref: ref[X_RING + i], None, lambda s, ref=ref: ref[X_RING + Q])
        for ref in (below, above)
    ]
    lay_halo(0, *ring, pop, cot)
    lay_codes(0, *ring, wide, field)
    for n, c in enumerate((2, 3, 1, 4)):
        halves = from_x(below, n, 1), from_x(above, n, -1)
        if n > 1:
            lay_halo(c, *halves, pop, cot)
        lay_codes(c, *halves, wide, field)


def steps_kernel(
    sizes,
    state_ref,
    own_field_ref,
    names_ref,
    first_x_ref,
    up_x_ref,
    down_x_ref,
    *refs,
):
    adjoint_ref, panel_ref, pop_a, ring_a, wide, field, pop_b, ring_b, saved, mom, grad = refs[4:]
    size_x, size_y = sizes
    halves = sides(first_x_ref, (up_x_ref, down_x_ref), "gx", layouts()[2])
    below, above = (Shifted(ref, X_SIDE) for ref in halves)
    lay_halos(below, above, pop_a, ring_a, wide, field)

    at_x, at_y = lax.axis_index("gx"), lax.axis_index("gy")
    edges = (
        jnp.where(at_x == 0, 1, 0),
        jnp.where(at_x == size_x - 1, 1, 0),
        jnp.where(at_y == 0, 1, 0),
        jnp.where(at_y == size_y - 1, 1, 0),
    )
    row, lane, column, depth = iotas()
    after = row < 4

    def masks_of(tile, first, r):
        return wall_masks(r == 0, tile == first, tile == first + 1, edges)

    def neighbours(tile, tiles):
        if isinstance(tile, int):
            return {0: tile, -1: (tile - 1) % tiles, 1: (tile + 1) % tiles}
        return {0: tile, -1: lax.rem(tile + tiles - 1, tiles), 1: lax.rem(tile + 1, tiles)}

    def from_wide(ref, tile, r):
        step = neighbours(tile, 5)

        def load(i, tile_step, row_step, move):
            at = 5 * i + step[tile_step]
            before, own, behind = (ref[at, pl.ds(ROWS * n + row_step, ROWS), :] for n in (1, 2, 3))
            return (own, jnp.where(after, behind, before), before, behind)[r]

        return load

    def from_ring(ref, tile, tiles, r):
        step = neighbours(tile, tiles)

        def load(i, tile_step, row_step, move):
            rows = own_rows(row_step) if r == 0 else halo_rows(row_step)
            return ref[tiles * i + step[tile_step], rows, :]

        return load

    def from_outer(ref, r):
        def load(i, tile_step, row_step, move):
            rows = own_rows(row_step) if r == 0 else halo_rows(row_step)
            if tile_step:
                return ref[4 * i + (2 if tile_step < 0 else 1), rows, :]
            cut = {0: 2, 1: 1, -1: 3}[move]
            return jnp.where(column < cut, ref[4 * i + 3, rows, :], ref[4 * i, rows, :])

        return load

    def note(s, tile, r, parts):
        for n, value in enumerate(parts[2:4] + tuple(parts[4])):
            mom[s - 1, n, tile, r] = value

    def first_step(tile, carry):
        place = lax.rem(tile + 4, 5)
        halo = []
        for r in (2, 0, 3):
            f = stream_tile(from_wide(pop_a, tile, r), 1, masks_of(tile, 2, r), lane)
            parts = moments(f)
            if r == 0:
                note(1, place, 0, parts)
                for i in range(Q):
                    saved[0, i, place] = f[i]
            else:
                halo.append(parts[2:4] + tuple(parts[4]))
            at = {2: 0, 0: 1, 3: 2}[r]
            g = collide(f, wide[0, tile, at], wide[1, tile, at], parts)
            for i in range(Q):
                pop_b[5 * i + tile, pl.ds(ROWS * (at + 1), ROWS), :] = g[i]
        for n in range(5):
            mom[0, n, place, 1] = jnp.where(after, halo[1][n], halo[0][n])
        return carry

    lax.fori_loop(0, 5, first_step, 0)

    def second_step(tile, carry):
        out = []
        for r in range(2):
            f = stream_tile(from_wide(pop_b, tile + 1, r), 1, masks_of(tile, 1, r), lane)
            parts = moments(f)
            note(2, tile, r, parts)
            if r == 0:
                for i in range(Q):
                    saved[1, i, tile] = f[i]
            out.append(collide(f, field[2, tile, r], field[0, tile, r], parts))
        for i in range(Q):
            put_ring(ring_b, 4 * i + tile, out[0][i], out[1][i])
        return carry

    lax.fori_loop(0, 4, second_step, 0)

    def third_step(tile, carry):
        for r in range(2):
            f = stream_tile(from_ring(ring_b, tile, 4, r), 1, masks_of(tile, 1, r), lane)
            note(3, tile, r, moments(f))
            if r == 0:
                for i in range(Q):
                    saved[2, i, tile] = f[i]
        return carry

    lax.fori_loop(0, 4, third_step, 0)

    def back_tile(load, s, tile, r, own):
        b = stream_tile(load, -1, masks_of(4 if tile is None else tile, 1, r), lane)

        def read(get):
            return jnp.where(column < 2, get(3), get(0)) if tile is None else get(tile)

        rho, rinv, *u = [read(lambda at: mom[s - 1, n, at, r]) for n in range(5)]
        kind, phi = read(lambda at: field[s, at, r]), read(lambda at: field[0, at, r])
        state = [saved[s - 1, i, tile] for i in range(Q)] if own else None
        back, term = collide_back(b, kind, phi, rho, rinv, u, state)
        if own:
            grad[tile] = term if s == 3 else grad[tile] + term
        return back

    def last_step(tile, carry):
        out = [back_tile(from_ring(ring_a, tile, 4, r), 3, tile, r, r == 0) for r in range(2)]
        for i in range(Q):
            put_ring(ring_b, 4 * i + tile, out[0][i], out[1][i])
        return carry

    lax.fori_loop(0, 4, last_step, 0)

    for k, tile in enumerate((1, 2, None)):
        out = []
        for r in range(2):
            load = from_outer(ring_b, r) if tile is None else from_ring(ring_b, tile, 4, r)
            out.append(back_tile(load, 2, tile, r, r == 0 and tile is not None))
        for i in range(Q):
            put_ring(ring_a, 3 * i + k, out[0][i], out[1][i])

    for k, tile in enumerate((1, 2, None)):
        out = []
        for r in range(2):
            load = from_ring(ring_a, k, 3, r)
            out.append(back_tile(load, 1, tile, r, r == 0 and tile is not None))
        for i in range(Q):
            put_ring(ring_b, 3 * i + k, out[0][i], out[1][i])

    panel = lax.broadcasted_iota(jnp.int32, panel_ref.shape, 1)
    sums = jnp.zeros(panel_ref.shape, jnp.float32)
    for t in range(2):
        b = stream_tile(from_ring(ring_b, t, 3, 0), -1, masks_of(t, 0, 0), lane)
        f = [state_ref[2 * i + t] for i in range(Q)]
        kind, phi = own_field_ref[t], own_field_ref[2 * OWN_PHI + t]
        _, _, rho, rinv, u = moments(f)
        back, term = collide_back(b, kind, phi, rho, rinv, u, f)
        for i in range(Q):
            adjoint_ref[i, :, pl.ds(t * LANES, LANES)] = back[i]
        term = term + grad[t + 1]
        for part in range(2):
            amount = jnp.sum(jnp.where((row < 4) == (part == 0), term, 0.0))
            name = names_ref[t, 4 * part : 4 * part + 1, 0:1]
            sums = sums + jnp.where(panel == name, amount, 0.0)
    panel_ref[...] = sums


def finish(parts_ref, adjoint_ref, sums_hbm, adjoint_hbm, sums_ref, sems):
    adjoint_copy = pltpu.make_async_copy(adjoint_ref, adjoint_hbm, sems.at[0])
    adjoint_copy.start()
    sums_ref[...] = jnp.sum(parts_ref[...], axis=0)
    sums_copy = pltpu.make_async_copy(sums_ref, sums_hbm, sems.at[1])
    sums_copy.start()
    sums_copy.wait()
    adjoint_copy.wait()


VMEM = pl.BlockSpec(memory_space=pltpu.VMEM)
HBM = pl.BlockSpec(memory_space=pltpu.HBM)


def shape_of(*dims):
    return jax.ShapeDtypeStruct(dims, jnp.float32)


def tiles_of(count):
    return shape_of(count, ROWS, LANES)


def on_device(sizes, checkpoint, cotangent, cell_codes, porosity, baffle_index):
    size_x, size_y = sizes
    panels = porosity.shape[0]
    devices = size_x * size_y
    y_layout, side_layout, rest_layout = layouts()

    params = pltpu.CompilerParams(vmem_limit_bytes=32 * 1024 * 1024)

    def call(kernel, out_shape, in_specs, scratch=(), name=None, aliases={}):
        return pl.pallas_call(
            kernel,
            out_shape=out_shape,
            in_specs=in_specs,
            out_specs=jax.tree.map(lambda _: VMEM, out_shape),
            scratch_shapes=scratch,
            input_output_aliases=aliases,
            compiler_params=params,
            name=name,
        )

    def swap(value, axis, size):
        return lax.ppermute(value, axis, [(i, i ^ 1) for i in range(size) if i ^ 1 < size])

    def swap_between(value, axis, size):
        pairs = [(i, i + 1) for i in range(1, size - 1, 2)]
        return lax.ppermute(value, axis, pairs + [(j, i) for i, j in pairs])

    def pass_between(value, axis, size):
        pairs = [(i, i + 1) for i in range(1, size - 1, 2)]
        return tuple(
            lax.ppermute(value, axis, way) for way in (pairs, [(j, i) for i, j in pairs])
        )

    arguments = [
        pltpu.with_memory_space_constraint(value, pltpu.HBM)
        for value in (checkpoint, cotangent, cell_codes, baffle_index, porosity)
    ]
    first_y, second_y, first_side, second_side, own, state, cot, field, names = call(
        pack_own,
        (tiles_of(y_layout.size),) * 2
        + (tiles_of(side_layout.size), tiles_of(rest_layout.size + 8))
        + (tiles_of(2 * Q),) * 3
        + (tiles_of(2 * OWN_PHI + 2), jax.ShapeDtypeStruct((2, ROWS, LANES), jnp.int32)),
        [HBM] * 5,
        [
            pltpu.VMEM((Q, ROWS, 2 * LANES), jnp.float32),
            pltpu.VMEM((Q, ROWS, 2 * LANES), jnp.float32),
            pltpu.VMEM((STEPS, ROWS, 2 * LANES), jnp.int32),
            pltpu.SMEM(baffle_index.shape, jnp.int32),
            pltpu.SMEM(porosity.shape, jnp.float32),
            pltpu.SemaphoreType.DMA((5,)),
        ],
        name="pack_own",
    )(*arguments)
    second_y = pass_between(second_y, "gy", size_y)
    first_y = swap(first_y, "gy", size_y)
    second_side = swap_between(second_side, "gx", size_x)
    first_side = swap(first_side, "gx", size_x)
    first_x, second_x = call(
        pack_x,
        (tiles_of(rest_layout.size), tiles_of(rest_layout.size + 1)),
        [VMEM] * 4,
        name="pack_x",
    )(field, first_y, *second_y)
    second_x = pass_between(second_x, "gx", size_x)
    first_x = swap(first_x, "gx", size_x)

    spaces = (
        shape_of(5 * Q, 5 * ROWS, LANES),
        shape_of(4 * Q, 3 * ROWS, LANES),
        shape_of(2, 5, 3, ROWS, LANES),
        shape_of(4, 4, 2, ROWS, LANES),
    )
    laid = call(lay_out, spaces, [VMEM] * 8, name="lay_out")(
        first_y, *second_y, first_side, second_side, own, field, cot
    )
    adjoint, sums, *_ = call(
        functools.partial(steps_kernel, sizes),
        (pltpu.VMEM((Q, ROWS, 2 * LANES), jnp.float32), shape_of(devices, panels)) + spaces,
        [VMEM] * 10,
        [
            pltpu.VMEM((5 * Q, 5 * ROWS, LANES), jnp.float32),
            pltpu.VMEM((4 * Q, 3 * ROWS, LANES), jnp.float32),
            pltpu.VMEM((3, Q, 5, ROWS, LANES), jnp.float32),
            pltpu.VMEM((3, 5, 5, 2, ROWS, LANES), jnp.float32),
            pltpu.VMEM((4, ROWS, LANES), jnp.float32),
        ],
        name="steps",
        aliases={6 + n: 2 + n for n in range(4)},
    )(state, field, names, first_x, *second_x, *laid)
    gathered = lax.all_to_all(sums, ("gx", "gy"), 0, 0, tiled=True)
    totals, adjoint = pl.pallas_call(
        finish,
        out_shape=(shape_of(1, panels), shape_of(Q, ROWS, 2 * LANES)),
        in_specs=[VMEM, VMEM],
        out_specs=(HBM, HBM),
        scratch_shapes=[pltpu.VMEM((1, panels), jnp.float32), pltpu.SemaphoreType.DMA((2,))],
        compiler_params=params,
        name="finish",
    )(gathered.reshape(devices, 1, panels), adjoint)
    return adjoint, totals.reshape(panels)


def solution(mesh):
    sizes = (mesh.shape["gx"], mesh.shape["gy"])
    in_specs = (P(None, "gx", "gy"), P(None, "gx", "gy"), P(None, "gx", "gy"), P(), P("gx", "gy"))
    out_specs = (P(None, "gx", "gy"), P())
    return jax.shard_map(
        functools.partial(on_device, sizes),
        mesh=mesh,
        in_specs=in_specs,
        out_specs=out_specs,
        check_vma=False,
    )
```

```python
import functools

import jax
import jax.numpy as jnp
import numpy as np
from jax import lax
from jax.experimental import pallas as pl
from jax.experimental.pallas import tpu as pltpu
from jax.sharding import PartitionSpec as P

Q = 19
STEPS = 4
NZ = 32
ROWS = 8
LANES = 128
OMEGA = 1.6
ACCEL = (0.002, 0.0, -0.003)
SHIFT = tuple(a / OMEGA for a in ACCEL)

VELOCITIES = [
    (0, 0, 0),
    (1, 0, 0),
    (-1, 0, 0),
    (0, 1, 0),
    (0, -1, 0),
    (0, 0, 1),
    (0, 0, -1),
    (1, 1, 0),
    (-1, -1, 0),
    (1, -1, 0),
    (-1, 1, 0),
    (1, 0, 1),
    (-1, 0, -1),
    (1, 0, -1),
    (-1, 0, 1),
    (0, 1, 1),
    (0, -1, -1),
    (0, 1, -1),
    (0, -1, 1),
]
OPPOSITE = [0, 2, 1, 4, 3, 6, 5, 8, 7, 10, 9, 12, 11, 14, 13, 16, 15, 18, 17]
PAIRS = [(i, i + 1) for i in range(1, Q, 2)]
W_REST, W_AXIS, W_DIAG = 1.0 / 3.0, 1.0 / 18.0, 1.0 / 36.0

Y_CODE1, Y_CODE2, Y_CODE3, Y_POP, Y_COT = 38, 39, 40, 41, 42
Y_TILES = 43
X_EXTRA = 19
X_LANE = 20
X_SIDE = 2 * X_LANE
X_RING = 4 * X_LANE
X_CODE13 = X_RING + Q + 1
X_CODE2 = X_CODE13 + 4
X_TILES = X_CODE2 + 2
EMPTY = 25
FREE = NZ - EMPTY
WEIGHTS = [W_REST] + [W_AXIS] * 6 + [W_DIAG] * 12
LEVEL = [i for i, v in enumerate(VELOCITIES) if v[2] < 1]
OWN_PHI = 4


def turned(axis, outward):
    return [i for i, v in enumerate(VELOCITIES) if v[axis] == outward and sum(map(abs, v)) == 2]


def total(values):
    values = list(values)
    while len(values) > 1:
        values = [a + b for a, b in zip(values[::2], values[1::2])] + (
            [values[-1]] if len(values) % 2 else []
        )
    return values[0]


def along(vector, three):
    terms = None
    for c, value in zip(vector, three):
        if c == 0:
            continue
        if terms is None:
            terms = value if c > 0 else -value
        else:
            terms = terms + value if c > 0 else terms - value
    return terms


def moments(f):
    plus = {i: f[i] + f[o] for i, o in PAIRS}
    minus = {i: f[i] - f[o] for i, o in PAIRS}
    rho = total([f[0]] + [plus[i] for i, _ in PAIRS])
    rinv = 1.0 / rho
    u = []
    for axis in range(3):
        terms = [
            minus[i] if VELOCITIES[i][axis] > 0 else -minus[i]
            for i, _ in PAIRS
            if VELOCITIES[i][axis] != 0
        ]
        u.append(total(terms) * rinv + SHIFT[axis])
    return plus, minus, rho, rinv, u


def coefficients(kind, phi, rinv):
    baffle = kind == 3.0
    gas = kind == 0.0
    even = jnp.where(gas, 0.0, jnp.where(baffle, 0.5 - 0.5 * OMEGA * phi, 0.5 * (1.0 - OMEGA)))
    odd = jnp.where(
        gas, 0.0, jnp.where(baffle, (1.0 - 0.5 * OMEGA) * phi - 0.5, 0.5 * (1.0 - OMEGA))
    )
    slope = jnp.where(
        baffle,
        OMEGA * phi,
        jnp.where(kind == 1.0, OMEGA, jnp.where(kind == 2.0, OMEGA * rinv, 0.0)),
    )
    return even, odd, slope


def collide(f, kind, phi, parts):
    plus, minus, rho, rinv, u = parts
    even, odd, slope = coefficients(kind, phi, rinv)
    scale = slope * rho
    rest = 1.0 - 1.5 * (u[0] * u[0] + u[1] * u[1] + u[2] * u[2])
    base = scale * rest + jnp.where(kind == 0.0, 1.0, 0.0)
    out = [None] * Q
    out[0] = 2.0 * even * f[0] + W_REST * base
    for weight, pairs in ((W_AXIS, PAIRS[:3]), (W_DIAG, PAIRS[3:])):
        flat = weight * base
        three = (3.0 * weight) * scale
        for i, o in pairs:
            cu = along(VELOCITIES[i], u)
            lin = three * cu
            ev = even * plus[i] + (flat + 1.5 * lin * cu)
            od = odd * minus[i] + lin
            out[i] = ev + od
            out[o] = ev - od
    return out


def collide_back(b, kind, phi, rho, rinv, u, state=None):
    even, odd, slope = coefficients(kind, phi, rinv)
    plus = {i: b[i] + b[o] for i, o in PAIRS}
    minus = {i: b[i] - b[o] for i, o in PAIRS}
    rest = 1.0 - 1.5 * (u[0] * u[0] + u[1] * u[1] + u[2] * u[2])
    u_half = [1.5 * c for c in u]
    weighted = W_REST * b[0]
    energy = 0.0
    vector = [0.0, 0.0, 0.0]
    for weight, pairs in ((W_AXIS, PAIRS[:3]), (W_DIAG, PAIRS[3:])):
        weighted = weighted + weight * total([plus[i] for i, _ in pairs])
        energies, parts = [], ([], [], [])
        for i, _ in pairs:
            cu = along(VELOCITIES[i], u)
            half = along(VELOCITIES[i], u_half) * plus[i]
            first = minus[i] + half
            energies.append(cu * first)
            second = first + half
            for axis in range(3):
                c = VELOCITIES[i][axis]
                if c:
                    parts[axis].append(second if c > 0 else -second)
        energy = energy + (3.0 * weight) * total(energies)
        vector = [vector[k] + (3.0 * weight) * total(parts[k]) for k in range(3)]
    energy = energy + rest * weighted
    vector = [vector[k] - (3.0 * weighted) * u[k] for k in range(3)]
    push = [slope * v for v in vector]
    inner = total([push[k] * (u[k] - SHIFT[k]) for k in range(3)])
    shared = jnp.where(kind == 2.0, 0.0, slope) * energy - inner
    out = [None] * Q
    out[0] = 2.0 * even * b[0] + shared
    for i, o in PAIRS:
        ev = even * plus[i] + shared
        od = odd * minus[i] + along(VELOCITIES[i], push)
        out[i] = ev + od
        out[o] = ev - od
    if state is None:
        return out, None
    evens = total([plus[i] * (state[i] + state[o]) for i, o in PAIRS])
    odds = total([minus[i] * (state[i] - state[o]) for i, o in PAIRS])
    term = (
        -OMEGA * (b[0] * state[0] + 0.5 * evens)
        + (1.0 - 0.5 * OMEGA) * odds
        + OMEGA * rho * energy
    )
    return out, jnp.where(kind == 3.0, term, 0.0)


def wall_masks(sign_rows, own_low, own_high, edges):
    lane = lax.broadcasted_iota(jnp.int32, (ROWS, LANES), 1)
    row = lax.broadcasted_iota(jnp.int32, (ROWS, LANES), 0)
    x_low, x_high, y_low, y_high = edges
    depth = lane % NZ
    masks = {}
    masks[2, 1] = depth == 0
    masks[2, -1] = depth == NZ - 1
    masks[1, 1] = lane < jnp.where(own_low, y_low * NZ, 0)
    masks[1, -1] = lane >= jnp.where(own_high, LANES - y_high * NZ, LANES)
    if sign_rows:
        masks[0, 1] = row < x_low
        masks[0, -1] = row >= ROWS - x_high
    return masks


def stream_tile(get, sign, masks, lane):
    loaded = {}

    def load(*at):
        if at not in loaded:
            loaded[at] = get(*at)
        return loaded[at]

    cross_low, cross_high = lane >= LANES - NZ, lane < NZ
    combined = {}
    out = []
    for i, vector in enumerate(VELOCITIES):
        v = tuple(sign * c for c in vector)
        value = load(i, 0, -v[0], v[1])
        if v[1] == 1:
            value = jnp.where(cross_low, load(i, -1, -v[0], 1), value)
        elif v[1] == -1:
            value = jnp.where(cross_high, load(i, 1, -v[0], -1), value)
        amount = (v[1] * NZ + v[2]) % LANES
        if amount:
            value = pltpu.roll(value, amount, 1)
        outside = None
        if v not in combined:
            for axis in range(3):
                if v[axis] and (axis, v[axis]) in masks:
                    wall = masks[axis, v[axis]]
                    outside = wall if outside is None else outside | wall
            combined[v] = outside
        outside = combined[v]
        if outside is not None:
            value = jnp.where(outside, load(OPPOSITE[i], 0, 0, 0), value)
        out.append(value)
    return out


def iotas():
    row = lax.broadcasted_iota(jnp.int32, (ROWS, LANES), 0)
    lane = lax.broadcasted_iota(jnp.int32, (ROWS, LANES), 1)
    return row, lane, lane // NZ, lane % NZ


def columns(value, count):
    amount = (count * NZ) % LANES
    return pltpu.roll(value, amount, 1) if amount else value


def lines(value, count):
    amount = count % ROWS
    return pltpu.roll(value, amount, 0) if amount else value


class Layout:
    def __init__(self, count, guests, fills):
        self.fills = fills
        hosts = [at for at in fills if at not in guests]
        self.hosts = {at: hosts[4 * n : 4 * n + 4] for n, at in enumerate(guests)}
        self.guests = guests
        kept = [at for at in range(count) if at not in guests]
        self.place = {at: n for n, at in enumerate(kept)}
        self.size = len(kept)


class Packing:
    def __init__(self, ref, layout):
        self.ref, self.layout, self.held = ref, layout, {}

    def __setitem__(self, at, value):
        if at in self.layout.guests:
            self.held[at] = value
        else:
            self.ref[self.layout.place[at]] = value

    def finish(self):
        row, lane, column, depth = iotas()
        spare = depth >= EMPTY
        for at, value in self.held.items():
            for k, host in enumerate(self.layout.hosts[at]):
                place = self.layout.place[host]
                moved = pltpu.roll(value, EMPTY - FREE * k, 1)
                self.ref[place] = jnp.where(spare, moved, self.ref[place])
        for place in range(self.layout.size, self.ref.shape[0]):
            self.ref[place] = jnp.zeros((ROWS, LANES), jnp.float32)


class Unpacking:
    def __init__(self, source, layout):
        self.source, self.layout, self.cache = source, layout, {}
        self.changed = set(layout.guests).union(*layout.hosts.values())

    def __getitem__(self, at):
        if at not in self.cache:
            self.cache[at] = self.read(at)
        return self.cache[at]

    def read(self, at):
        row, lane, column, depth = iotas()
        layout = self.layout
        if at in layout.guests:
            value = None
            for k, host in enumerate(layout.hosts[at]):
                tile = self.source[layout.place[host]]
                moved = pltpu.roll(tile, LANES - (EMPTY - FREE * k), 1)
                value = moved if value is None else jnp.where(depth >= FREE * k, moved, value)
        else:
            value = self.source[layout.place[at]]
        if at in self.changed:
            value = jnp.where(depth >= EMPTY, layout.fills[at], value)
        return value


def layouts():
    y_fills = {2 * i + t: WEIGHTS[i] for i in LEVEL for t in range(2)}
    y_fills.update({Y_POP: W_DIAG, Y_CODE2: 0.0})
    x_fills = {X_LANE * n + i: WEIGHTS[i] for n in range(4) for i in LEVEL}
    side = {at: fill for at, fill in x_fills.items() if at < X_SIDE}
    rest = {at - X_SIDE: fill for at, fill in x_fills.items() if at >= X_SIDE}
    rest.update({X_CODE2 - X_SIDE: 0.0, X_CODE2 + 1 - X_SIDE: 0.0})
    rest.update({X_RING - X_SIDE + i: WEIGHTS[i] for i in range(Q)})
    ring = [X_RING - X_SIDE + i for i in range(9)]
    return (
        Layout(Y_TILES, [2 * i for i in LEVEL[:6]], y_fills),
        Layout(X_SIDE, LEVEL[:5], side),
        Layout(X_TILES - X_SIDE, ring, rest),
    )


class Pick:
    def __init__(self, flag, first, second):
        self.flag, self.first, self.second = flag, first, second

    def __getitem__(self, at):
        return jnp.where(self.flag, self.first[at], self.second[at])


class Deal:
    def __init__(self, even, first, second, layout, skip=0):
        self.even, self.skip, self.held = even, skip, {}
        self.first, self.second = Packing(first, layout), Packing(second, layout)

    def put(self, way, at, value):
        if (-way, at) not in self.held:
            self.held[way, at] = value
            return
        other = self.held.pop((-way, at))
        up, down = (value, other) if way == 1 else (other, value)
        self.first[at - self.skip] = jnp.where(self.even, up, down)
        self.second[at - self.skip] = jnp.where(self.even, down, up)

    def put_both(self, at, value):
        self.first[at - self.skip] = value
        self.second[at - self.skip] = value

    def finish(self):
        self.first.finish()
        self.second.finish()


class Shifted:
    def __init__(self, ref, start):
        self.ref, self.start = ref, start

    def __getitem__(self, at):
        return self.ref[at - self.start]


def is_even(axis):
    return lax.rem(lax.axis_index(axis), 2) == 0


def pack_own(
    f_hbm,
    cot_hbm,
    codes_hbm,
    panels_hbm,
    porosity_hbm,
    first_ref,
    second_ref,
    first_side_ref,
    second_side_ref,
    own_ref,
    state_ref,
    own_cot_ref,
    field_ref,
    names_ref,
    f_ref,
    cot_ref,
    codes_ref,
    panels_ref,
    porosity_ref,
    sems,
):
    pieces = (
        (panels_hbm, panels_ref),
        (porosity_hbm, porosity_ref),
        (f_hbm, f_ref),
        (codes_hbm, codes_ref),
        (cot_hbm, cot_ref),
    )
    copies = [
        pltpu.make_async_copy(source, target, sems.at[n])
        for n, (source, target) in enumerate(pieces)
    ]
    for copy in copies:
        copy.start()
    for copy in copies[:4]:
        copy.wait()
    y_layout, side_layout, _ = layouts()
    deal = Deal(is_even("gy"), first_ref, second_ref, y_layout)
    side = Deal(is_even("gx"), first_side_ref, second_side_ref, side_layout)
    row, lane, column, depth = iotas()
    top = depth == NZ - 1

    def tile_of(ref, i, t):
        return ref[i, :, pl.ds(t * LANES, LANES)]

    codes, phis = [], []
    for t in range(2):
        names = panels_ref[0, t * LANES], panels_ref[4, t * LANES]
        phi = jnp.where(row < 4, porosity_ref[names[0]], porosity_ref[names[1]])
        names_ref[t] = jnp.where(row < 4, names[0], names[1])
        kinds = [tile_of(codes_ref, s, t).astype(jnp.float32) for s in range(STEPS)]
        f = [tile_of(f_ref, i, t) for i in range(Q)]
        g = collide(f, kinds[0], phi, moments(f))
        for i in range(Q):
            own_ref[2 * i + t] = g[i]
            state_ref[2 * i + t] = f[i]
        for s in range(STEPS):
            field_ref[2 * s + t] = kinds[s]
        field_ref[2 * OWN_PHI + t] = phi
        codes.append([jnp.where(top, phi, kinds[1]), kinds[2], kinds[3]])
    copies[4].wait()
    for i in range(Q):
        for way in (1, -1):
            near, far = (1, 0) if way == 1 else (0, 1)
            deep = 3 - way * VELOCITIES[i][1]
            cot = tile_of(cot_ref, i, near)
            g_far = own_ref[2 * i + far]
            if way == 1:
                mixed = jnp.where(column >= deep, g_far, columns(cot, deep - 4))
            else:
                mixed = jnp.where(column < 4 - deep, g_far, columns(cot, 4 - deep))
            deal.put(way, 2 * i, mixed if far == 0 else own_ref[2 * i])
            deal.put(way, 2 * i + 1, mixed if far == 1 else own_ref[2 * i + 1])
    for way in (1, -1):
        near, far = (1, 0) if way == 1 else (0, 1)
        outer = 3 if way == 1 else 0
        deal.put(way, Y_CODE1, codes[near][0])
        deal.put(way, Y_CODE2, codes[near][1])
        outside = columns(codes[far][0], 3 - 2 * outer)
        deal.put(way, Y_CODE3, jnp.where(column == 3 - outer, outside, codes[near][2]))
        extra = None
        for k, i in enumerate(turned(1, -way)):
            value = columns(own_ref[2 * i + far], k - outer)
            extra = value if extra is None else jnp.where(column == k, value, extra)
        deal.put(way, Y_POP, extra)
        extra = None
        for k, i in enumerate(turned(1, way)):
            value = columns(tile_of(cot_ref, i, near), k - (1 if way == 1 else 2))
            extra = value if extra is None else jnp.where(column == k, value, extra)
        deal.put(way, Y_COT, extra)
    deal.finish()
    for t in range(2):
        for i in range(Q):
            own_cot_ref[2 * i + t] = tile_of(cot_ref, i, t)
        pack_lines(
            side,
            X_LANE * t,
            lambda i: own_ref[2 * i + t],
            lambda i: tile_of(cot_ref, i, t),
        )
    side.finish()


def from_y(left_ref, right_ref):
    row, lane, column, depth = iotas()
    high = lane >= LANES // 2

    def population(i, c):
        if c == 1:
            return left_ref[2 * i + 1]
        if c == 4:
            return right_ref[2 * i]
        along_y = VELOCITIES[i][1]
        left, right = left_ref[2 * i], right_ref[2 * i + 1]
        if along_y == 1 and i in turned(1, 1):
            right = columns(right_ref[Y_POP], -turned(1, 1).index(i))
        if along_y == -1 and i in turned(1, -1):
            left = columns(left_ref[Y_POP], 3 - turned(1, -1).index(i))
        return jnp.where(high, left, right)

    def cotangent(i, c):
        ref, way, place, far = (left_ref, 1, 1, 0) if c == 1 else (right_ref, -1, 2, 1)
        deep = 3 - way * VELOCITIES[i][1]
        value = columns(ref[2 * i + far], way * (4 - deep))
        if i in turned(1, way):
            extra = columns(ref[Y_COT], place - turned(1, way).index(i))
            value = jnp.where(column == place, extra, value)
        return value

    def codes(s, c):
        if c == 0:
            left, right = columns(left_ref[Y_CODE3], 3), columns(right_ref[Y_CODE3], 1)
            return jnp.where(high, left, right)
        return (left_ref if c == 1 else right_ref)[(Y_CODE1, Y_CODE2, Y_CODE3)[s - 1]]

    return population, cotangent, codes


def mix_lines(deal, at, pop, cot, deep, way):
    row, lane, column, depth = iotas()
    if way == 1:
        mixed = jnp.where(row >= deep, pop, lines(cot, deep))
    else:
        mixed = jnp.where(row < ROWS - deep, pop, lines(cot, -deep))
    deal.put(way, at, mixed)


def pack_lines(deal, first, population, cotangent):
    row, lane, column, depth = iotas()

    for i in range(Q):
        pop, cot = population(i), cotangent(i)
        for way in (1, -1):
            mix_lines(deal, first + i, pop, cot, 3 - way * VELOCITIES[i][0], way)
    for way in (1, -1):
        extra = None
        for k, i in enumerate(turned(0, -way)):
            value = lines(population(i), k - (3 if way == 1 else 4))
            extra = value if extra is None else jnp.where(row == k, value, extra)
        for k, i in enumerate(turned(0, way)):
            value = lines(cotangent(i), 4 + k - (5 if way == 1 else 2))
            extra = jnp.where(row == 4 + k, value, extra)
        deal.put(way, first + X_EXTRA, extra)


def from_x(ref, n, way):
    row, lane, column, depth = iotas()
    first = X_LANE * n

    def population(i):
        value = ref[first + i]
        if i in turned(0, -way):
            place = 3 if way == 1 else 4
            extra = lines(ref[first + X_EXTRA], place - turned(0, -way).index(i))
            value = jnp.where(row == place, extra, value)
        return value

    def cotangent(i):
        value = lines(ref[first + i], -way * (3 - way * VELOCITIES[i][0]))
        if i in turned(0, way):
            place = 5 if way == 1 else 2
            extra = lines(ref[first + X_EXTRA], place - 4 - turned(0, way).index(i))
            value = jnp.where(row == place, extra, value)
        return value

    def codes(s):
        if s == 2:
            return lines(ref[X_CODE2 + n // 2], 4 * (n % 2))
        value = ref[X_CODE13 + n]
        return value if s == 1 else lines(value, -3 * way)

    return population, cotangent, codes


def pack_x(field_ref, first_y_ref, second_y_ref, first_ref, second_ref):
    row, lane, column, depth = iotas()
    y_layout, _, layout = layouts()
    deal = Deal(is_even("gx"), first_ref, second_ref, layout, X_SIDE)
    population, cotangent, codes = from_y(*sides(first_y_ref, second_y_ref, "gy", y_layout))

    def both_codes(at, first, second):
        second = lines(second, 4)
        deal.put(1, at, jnp.where(row >= 4, first, second))
        deal.put(-1, at, jnp.where(row < 4, first, second))

    for n, c in ((2, 1), (3, 4)):
        pack_lines(
            deal,
            X_LANE * n,
            lambda i: population(i, c),
            lambda i: cotangent(i, c),
        )
    for n in range(Q + 1):
        value = population(n, 0) if n < Q else codes(1, 0)
        deal.put_both(X_RING + n, value)
    for n in range(4):
        if n < 2:
            first = jnp.where(depth == NZ - 1, field_ref[2 * OWN_PHI + n], field_ref[2 + n])
            third = field_ref[6 + n]
        else:
            c = (1, 4)[n - 2]
            first, third = codes(1, c), codes(3, c)
        for way in (1, -1):
            mix_lines(deal, X_CODE13 + n, first, third, 3, way)
    both_codes(X_CODE2, field_ref[4], field_ref[5])
    both_codes(X_CODE2 + 1, codes(2, 1), codes(2, 4))
    deal.finish()


def sides(first_ref, second_ref, axis, layout):
    even = is_even(axis)
    picks = Pick(even, second_ref, first_ref), Pick(even, first_ref, second_ref)
    return [Unpacking(pick, layout) for pick in picks]


def own_rows(step=0):
    return pl.ds(ROWS + step, ROWS)


def halo_rows(step=0):
    return pl.ds({0: 2 * ROWS, -1: 2 * ROWS - 1, 1: 1}[step], ROWS)


def put_halo(ref, at, halo):
    ref[at, pl.ds(0, ROWS), :] = halo
    ref[at, halo_rows(), :] = halo


def put_ring(ref, at, own, halo):
    ref[at, own_rows(), :] = own
    put_halo(ref, at, halo)


def expand(code):
    row, lane, column, depth = iotas()
    top = depth == NZ - 1
    phi = jnp.where(top, code, 0.0)
    for step in (1, 2, 4, 8, 16):
        phi = phi + pltpu.roll(phi, LANES - step, 1)
    return jnp.where(top, 0.0, code), phi


def lay_own(c, population, cotangent, codes, code_phi, pop, cot, wide, field):
    for i in range(Q):
        pop[5 * i + c, pl.ds(2 * ROWS, ROWS), :] = population(i)
        if c:
            cot[4 * i + c - 1, own_rows(), :] = cotangent(i)
    for n in range(2):
        wide[n, c, 1] = code_phi[n]
    if c:
        field[0, c - 1, 0], field[1, c - 1, 0] = code_phi[1], code_phi[0]
        for s in (2, 3):
            field[s, c - 1, 0] = codes(s)


def lay_halo(c, below, above, pop, cot):
    row, lane, column, depth = iotas()
    for i in range(Q):
        pop[5 * i + c, pl.ds(ROWS, ROWS), :] = below[0](i)
        pop[5 * i + c, pl.ds(3 * ROWS, ROWS), :] = above[0](i)
        if c:
            put_halo(cot, 4 * i + c - 1, jnp.where(row < 4, above[1](i), below[1](i)))


def lay_codes(c, below, above, wide, field):
    row, lane, column, depth = iotas()
    before, after = expand(below[2](1)), expand(above[2](1))
    for n in range(2):
        wide[n, c, 0], wide[n, c, 2] = before[n], after[n]
    if c:
        for n, place in ((0, 1), (1, 0)):
            field[place, c - 1, 1] = jnp.where(row < 4, after[n], before[n])
        for s in (2, 3):
            field[s, c - 1, 1] = jnp.where(row < 4, above[2](s), below[2](s))


def lay_out(
    first_y_ref,
    second_y_ref,
    first_side_ref,
    second_side_ref,
    own_ref,
    field_ref,
    cot_ref,
    pop,
    cot,
    wide,
    field,
):
    y_layout, side_layout, _ = layouts()
    from_left = from_y(*sides(first_y_ref, second_y_ref, "gy", y_layout))
    below, above = sides(first_side_ref, second_side_ref, "gx", side_layout)
    for c in range(5):
        t = c - 2
        if t in (0, 1):
            lay_own(
                c,
                lambda i: own_ref[2 * i + t],
                lambda i: cot_ref[2 * i + t],
                lambda s: field_ref[2 * s + t],
                (field_ref[2 + t], field_ref[2 * OWN_PHI + t]),
                pop,
                cot,
                wide,
                field,
            )
            lay_halo(c, from_x(below, t, 1), from_x(above, t, -1), pop, cot)
        else:
            own = [functools.partial(lambda g, n: g(n, c), get) for get in from_left]
            lay_own(c, *own, expand(own[2](1)), pop, cot, wide, field)


def lay_halos(below, above, pop, cot, wide, field):
    ring = [
        (lambda i, ref=ref: ref[X_RING + i], None, lambda s, ref=ref: ref[X_RING + Q])
        for ref in (below, above)
    ]
    lay_halo(0, *ring, pop, cot)
    lay_codes(0, *ring, wide, field)
    for n, c in enumerate((2, 3, 1, 4)):
        halves = from_x(below, n, 1), from_x(above, n, -1)
        if n > 1:
            lay_halo(c, *halves, pop, cot)
        lay_codes(c, *halves, wide, field)


def steps_kernel(
    sizes,
    state_ref,
    own_field_ref,
    names_ref,
    first_x_ref,
    second_x_ref,
    *refs,
):
    adjoint_ref, panel_ref, pop_a, ring_a, wide, field, pop_b, ring_b, saved, mom, grad = refs[4:]
    size_x, size_y = sizes
    halves = sides(first_x_ref, second_x_ref, "gx", layouts()[2])
    below, above = (Shifted(ref, X_SIDE) for ref in halves)
    lay_halos(below, above, pop_a, ring_a, wide, field)

    at_x, at_y = lax.axis_index("gx"), lax.axis_index("gy")
    edges = (
        jnp.where(at_x == 0, 1, 0),
        jnp.where(at_x == size_x - 1, 1, 0),
        jnp.where(at_y == 0, 1, 0),
        jnp.where(at_y == size_y - 1, 1, 0),
    )
    row, lane, column, depth = iotas()
    after = row < 4

    def masks_of(tile, first, r):
        return wall_masks(r == 0, tile == first, tile == first + 1, edges)

    def neighbours(tile, tiles):
        if isinstance(tile, int):
            return {0: tile, -1: (tile - 1) % tiles, 1: (tile + 1) % tiles}
        return {0: tile, -1: lax.rem(tile + tiles - 1, tiles), 1: lax.rem(tile + 1, tiles)}

    def from_wide(ref, tile, r):
        step = neighbours(tile, 5)

        def load(i, tile_step, row_step, move):
            at = 5 * i + step[tile_step]
            def part(n):
                return ref[at, pl.ds(ROWS * n + row_step, ROWS), :]

            if r == 1:
                return jnp.where(after, part(3), part(1))
            return part({0: 2, 2: 1, 3: 3}[r])

        return load

    def from_ring(ref, tile, tiles, r):
        step = neighbours(tile, tiles)

        def load(i, tile_step, row_step, move):
            rows = own_rows(row_step) if r == 0 else halo_rows(row_step)
            return ref[tiles * i + step[tile_step], rows, :]

        return load

    def from_outer(ref, r):
        def load(i, tile_step, row_step, move):
            rows = own_rows(row_step) if r == 0 else halo_rows(row_step)
            if tile_step:
                return ref[4 * i + (2 if tile_step < 0 else 1), rows, :]
            cut = {0: 2, 1: 1, -1: 3}[move]
            return jnp.where(column < cut, ref[4 * i + 3, rows, :], ref[4 * i, rows, :])

        return load

    def note(s, tile, r, parts):
        for n, value in enumerate(parts[2:4] + tuple(parts[4])):
            mom[s - 1, n, tile, r] = value

    def first_step(tile, carry):
        place = lax.rem(tile + 4, 5)
        halo = []
        for r in (2, 0, 3):
            f = stream_tile(from_wide(pop_a, tile, r), 1, masks_of(tile, 2, r), lane)
            parts = moments(f)
            if r == 0:
                note(1, place, 0, parts)
                for i in range(Q):
                    saved[0, i, place] = f[i]
            else:
                halo.append(parts[2:4] + tuple(parts[4]))
            at = {2: 0, 0: 1, 3: 2}[r]
            g = collide(f, wide[0, tile, at], wide[1, tile, at], parts)
            for i in range(Q):
                pop_b[5 * i + tile, pl.ds(ROWS * (at + 1), ROWS), :] = g[i]
        for n in range(5):
            mom[0, n, place, 1] = jnp.where(after, halo[1][n], halo[0][n])
        return carry

    lax.fori_loop(0, 5, first_step, 0)

    def second_step(tile, carry):
        out = []
        for r in range(2):
            f = stream_tile(from_wide(pop_b, tile + 1, r), 1, masks_of(tile, 1, r), lane)
            parts = moments(f)
            note(2, tile, r, parts)
            if r == 0:
                for i in range(Q):
                    saved[1, i, tile] = f[i]
            out.append(collide(f, field[2, tile, r], field[0, tile, r], parts))
        for i in range(Q):
            put_ring(ring_b, 4 * i + tile, out[0][i], out[1][i])
        return carry

    lax.fori_loop(0, 4, second_step, 0)

    def third_step(tile, carry):
        for r in range(2):
            f = stream_tile(from_ring(ring_b, tile, 4, r), 1, masks_of(tile, 1, r), lane)
            note(3, tile, r, moments(f))
            if r == 0:
                for i in range(Q):
                    saved[2, i, tile] = f[i]
        return carry

    lax.fori_loop(0, 4, third_step, 0)

    def back_tile(load, s, tile, r, own):
        b = stream_tile(load, -1, masks_of(4 if tile is None else tile, 1, r), lane)

        def read(get):
            return jnp.where(column < 2, get(3), get(0)) if tile is None else get(tile)

        rho, rinv, *u = [read(lambda at: mom[s - 1, n, at, r]) for n in range(5)]
        kind, phi = read(lambda at: field[s, at, r]), read(lambda at: field[0, at, r])
        state = [saved[s - 1, i, tile] for i in range(Q)] if own else None
        back, term = collide_back(b, kind, phi, rho, rinv, u, state)
        if own:
            grad[tile] = term if s == 3 else grad[tile] + term
        return back

    def last_step(tile, carry):
        out = [back_tile(from_ring(ring_a, tile, 4, r), 3, tile, r, r == 0) for r in range(2)]
        for i in range(Q):
            put_ring(ring_b, 4 * i + tile, out[0][i], out[1][i])
        return carry

    lax.fori_loop(0, 4, last_step, 0)

    for k, tile in enumerate((1, 2, None)):
        out = []
        for r in range(2):
            load = from_outer(ring_b, r) if tile is None else from_ring(ring_b, tile, 4, r)
            out.append(back_tile(load, 2, tile, r, r == 0 and tile is not None))
        for i in range(Q):
            put_ring(ring_a, 3 * i + k, out[0][i], out[1][i])

    for k, tile in enumerate((1, 2, None)):
        out = []
        for r in range(2):
            load = from_ring(ring_a, k, 3, r)
            out.append(back_tile(load, 1, tile, r, r == 0 and tile is not None))
        for i in range(Q):
            put_ring(ring_b, 3 * i + k, out[0][i], out[1][i])

    panel = lax.broadcasted_iota(jnp.int32, panel_ref.shape, 1)
    sums = jnp.zeros(panel_ref.shape, jnp.float32)
    for t in range(2):
        b = stream_tile(from_ring(ring_b, t, 3, 0), -1, masks_of(t, 0, 0), lane)
        f = [state_ref[2 * i + t] for i in range(Q)]
        kind, phi = own_field_ref[t], own_field_ref[2 * OWN_PHI + t]
        _, _, rho, rinv, u = moments(f)
        back, term = collide_back(b, kind, phi, rho, rinv, u, f)
        for i in range(Q):
            adjoint_ref[i, :, pl.ds(t * LANES, LANES)] = back[i]
        term = term + grad[t + 1]
        for part in range(2):
            amount = jnp.sum(jnp.where((row < 4) == (part == 0), term, 0.0))
            name = names_ref[t, 4 * part : 4 * part + 1, 0:1]
            sums = sums + jnp.where(panel == name, amount, 0.0)
    panel_ref[...] = sums


def finish(parts_ref, adjoint_ref, sums_hbm, adjoint_hbm, sums_ref, sems):
    adjoint_copy = pltpu.make_async_copy(adjoint_ref, adjoint_hbm, sems.at[0])
    adjoint_copy.start()
    sums_ref[...] = jnp.sum(parts_ref[...], axis=0)
    sums_copy = pltpu.make_async_copy(sums_ref, sums_hbm, sems.at[1])
    sums_copy.start()
    sums_copy.wait()
    adjoint_copy.wait()


VMEM = pl.BlockSpec(memory_space=pltpu.VMEM)
HBM = pl.BlockSpec(memory_space=pltpu.HBM)


def shape_of(*dims):
    return jax.ShapeDtypeStruct(dims, jnp.float32)


def tiles_of(count):
    return shape_of(count, ROWS, LANES)


def on_device(sizes, checkpoint, cotangent, cell_codes, porosity, baffle_index):
    size_x, size_y = sizes
    panels = porosity.shape[0]
    devices = size_x * size_y
    y_layout, side_layout, rest_layout = layouts()

    params = pltpu.CompilerParams(vmem_limit_bytes=32 * 1024 * 1024)

    def call(kernel, out_shape, in_specs, scratch=(), name=None, aliases={}):
        return pl.pallas_call(
            kernel,
            out_shape=out_shape,
            in_specs=in_specs,
            out_specs=jax.tree.map(lambda _: VMEM, out_shape),
            scratch_shapes=scratch,
            input_output_aliases=aliases,
            compiler_params=params,
            name=name,
        )

    def swap(value, axis, size):
        return lax.ppermute(value, axis, [(i, i ^ 1) for i in range(size) if i ^ 1 < size])

    def swap_between(value, axis, size):
        pairs = [(i, i + 1) for i in range(1, size - 1, 2)]
        return lax.ppermute(value, axis, pairs + [(j, i) for i, j in pairs])

    arguments = [
        pltpu.with_memory_space_constraint(value, pltpu.HBM)
        for value in (checkpoint, cotangent, cell_codes, baffle_index, porosity)
    ]
    first_y, second_y, first_side, second_side, own, state, cot, field, names = call(
        pack_own,
        (tiles_of(y_layout.size),) * 2
        + (tiles_of(side_layout.size), tiles_of(rest_layout.size + 8))
        + (tiles_of(2 * Q),) * 3
        + (tiles_of(2 * OWN_PHI + 2), jax.ShapeDtypeStruct((2, ROWS, LANES), jnp.int32)),
        [HBM] * 5,
        [
            pltpu.VMEM((Q, ROWS, 2 * LANES), jnp.float32),
            pltpu.VMEM((Q, ROWS, 2 * LANES), jnp.float32),
            pltpu.VMEM((STEPS, ROWS, 2 * LANES), jnp.int32),
            pltpu.SMEM(baffle_index.shape, jnp.int32),
            pltpu.SMEM(porosity.shape, jnp.float32),
            pltpu.SemaphoreType.DMA((5,)),
        ],
        name="pack_own",
    )(*arguments)
    second_y = swap_between(second_y, "gy", size_y)
    first_y = swap(first_y, "gy", size_y)
    second_side = swap_between(second_side, "gx", size_x)
    first_side = swap(first_side, "gx", size_x)
    first_x, second_x = call(
        pack_x,
        (tiles_of(rest_layout.size), tiles_of(rest_layout.size + 1)),
        [VMEM] * 3,
        name="pack_x",
    )(field, first_y, second_y)
    second_x = swap_between(second_x, "gx", size_x)
    first_x = swap(first_x, "gx", size_x)

    spaces = (
        shape_of(5 * Q, 5 * ROWS, LANES),
        shape_of(4 * Q, 3 * ROWS, LANES),
        shape_of(2, 5, 3, ROWS, LANES),
        shape_of(4, 4, 2, ROWS, LANES),
    )
    laid = call(lay_out, spaces, [VMEM] * 7, name="lay_out")(
        first_y, second_y, first_side, second_side, own, field, cot
    )
    adjoint, sums, *_ = call(
        functools.partial(steps_kernel, sizes),
        (pltpu.VMEM((Q, ROWS, 2 * LANES), jnp.float32), shape_of(devices, panels)) + spaces,
        [VMEM] * 9,
        [
            pltpu.VMEM((5 * Q, 5 * ROWS, LANES), jnp.float32),
            pltpu.VMEM((4 * Q, 3 * ROWS, LANES), jnp.float32),
            pltpu.VMEM((3, Q, 5, ROWS, LANES), jnp.float32),
            pltpu.VMEM((3, 5, 5, 2, ROWS, LANES), jnp.float32),
            pltpu.VMEM((4, ROWS, LANES), jnp.float32),
        ],
        name="steps",
        aliases={5 + n: 2 + n for n in range(4)},
    )(state, field, names, first_x, second_x, *laid)
    gathered = lax.all_to_all(sums, ("gx", "gy"), 0, 0, tiled=True)
    totals, adjoint = pl.pallas_call(
        finish,
        out_shape=(shape_of(1, panels), shape_of(Q, ROWS, 2 * LANES)),
        in_specs=[VMEM, VMEM],
        out_specs=(HBM, HBM),
        scratch_shapes=[pltpu.VMEM((1, panels), jnp.float32), pltpu.SemaphoreType.DMA((2,))],
        compiler_params=params,
        name="finish",
    )(gathered.reshape(devices, 1, panels), adjoint)
    return adjoint, totals.reshape(panels)


def solution(mesh):
    sizes = (mesh.shape["gx"], mesh.shape["gy"])
    in_specs = (P(None, "gx", "gy"), P(None, "gx", "gy"), P(None, "gx", "gy"), P(), P("gx", "gy"))
    out_specs = (P(None, "gx", "gy"), P())
    return jax.shard_map(
        functools.partial(on_device, sizes),
        mesh=mesh,
        in_specs=in_specs,
        out_specs=out_specs,
        check_vma=False,
    )
```

```python
import functools

import jax
import jax.numpy as jnp
import numpy as np
from jax import lax
from jax.experimental import pallas as pl
from jax.experimental.pallas import tpu as pltpu
from jax.sharding import PartitionSpec as P

Q = 19
STEPS = 4
NZ = 32
ROWS = 8
LANES = 128
OMEGA = 1.6
ACCEL = (0.002, 0.0, -0.003)
SHIFT = tuple(a / OMEGA for a in ACCEL)

VELOCITIES = [
    (0, 0, 0),
    (1, 0, 0),
    (-1, 0, 0),
    (0, 1, 0),
    (0, -1, 0),
    (0, 0, 1),
    (0, 0, -1),
    (1, 1, 0),
    (-1, -1, 0),
    (1, -1, 0),
    (-1, 1, 0),
    (1, 0, 1),
    (-1, 0, -1),
    (1, 0, -1),
    (-1, 0, 1),
    (0, 1, 1),
    (0, -1, -1),
    (0, 1, -1),
    (0, -1, 1),
]
OPPOSITE = [0, 2, 1, 4, 3, 6, 5, 8, 7, 10, 9, 12, 11, 14, 13, 16, 15, 18, 17]
PAIRS = [(i, i + 1) for i in range(1, Q, 2)]
W_REST, W_AXIS, W_DIAG = 1.0 / 3.0, 1.0 / 18.0, 1.0 / 36.0

Y_CODE1, Y_CODE2, Y_CODE3, Y_POP, Y_COT = 38, 39, 40, 41, 42
Y_TILES = 43
X_EXTRA = 19
X_LANE = 20
X_HALVES = 10


def x_places(lanes):
    ring = X_LANE * lanes
    code13 = ring + X_HALVES
    code2 = code13 + lanes
    return ring, code13, code2, code2 + (lanes + 1) // 2


EMPTY = 25
FREE = NZ - EMPTY
WEIGHTS = [W_REST] + [W_AXIS] * 6 + [W_DIAG] * 12
LEVEL = [i for i, v in enumerate(VELOCITIES) if v[2] < 1]
OWN_PHI = 4


def turned(axis, outward):
    return [i for i, v in enumerate(VELOCITIES) if v[axis] == outward and sum(map(abs, v)) == 2]


def total(values):
    values = list(values)
    while len(values) > 1:
        values = [a + b for a, b in zip(values[::2], values[1::2])] + (
            [values[-1]] if len(values) % 2 else []
        )
    return values[0]


def along(vector, three):
    terms = None
    for c, value in zip(vector, three):
        if c == 0:
            continue
        if terms is None:
            terms = value if c > 0 else -value
        else:
            terms = terms + value if c > 0 else terms - value
    return terms


def moments(f):
    plus = {i: f[i] + f[o] for i, o in PAIRS}
    minus = {i: f[i] - f[o] for i, o in PAIRS}
    rho = total([f[0]] + [plus[i] for i, _ in PAIRS])
    rinv = 1.0 / rho
    u = []
    for axis in range(3):
        terms = [
            minus[i] if VELOCITIES[i][axis] > 0 else -minus[i]
            for i, _ in PAIRS
            if VELOCITIES[i][axis] != 0
        ]
        u.append(total(terms) * rinv + SHIFT[axis])
    return plus, minus, rho, rinv, u


def coefficients(kind, phi, rinv):
    baffle = kind == 3.0
    gas = kind == 0.0
    even = jnp.where(gas, 0.0, jnp.where(baffle, 0.5 - 0.5 * OMEGA * phi, 0.5 * (1.0 - OMEGA)))
    odd = jnp.where(
        gas, 0.0, jnp.where(baffle, (1.0 - 0.5 * OMEGA) * phi - 0.5, 0.5 * (1.0 - OMEGA))
    )
    slope = jnp.where(
        baffle,
        OMEGA * phi,
        jnp.where(kind == 1.0, OMEGA, jnp.where(kind == 2.0, OMEGA * rinv, 0.0)),
    )
    return even, odd, slope


def collide(f, kind, phi, parts):
    plus, minus, rho, rinv, u = parts
    even, odd, slope = coefficients(kind, phi, rinv)
    scale = slope * rho
    rest = 1.0 - 1.5 * (u[0] * u[0] + u[1] * u[1] + u[2] * u[2])
    base = scale * rest + jnp.where(kind == 0.0, 1.0, 0.0)
    out = [None] * Q
    out[0] = 2.0 * even * f[0] + W_REST * base
    for weight, pairs in ((W_AXIS, PAIRS[:3]), (W_DIAG, PAIRS[3:])):
        flat = weight * base
        three = (3.0 * weight) * scale
        for i, o in pairs:
            cu = along(VELOCITIES[i], u)
            lin = three * cu
            ev = even * plus[i] + (flat + 1.5 * lin * cu)
            od = odd * minus[i] + lin
            out[i] = ev + od
            out[o] = ev - od
    return out


def collide_back(b, kind, phi, rho, rinv, u, state=None):
    even, odd, slope = coefficients(kind, phi, rinv)
    plus = {i: b[i] + b[o] for i, o in PAIRS}
    minus = {i: b[i] - b[o] for i, o in PAIRS}
    rest = 1.0 - 1.5 * (u[0] * u[0] + u[1] * u[1] + u[2] * u[2])
    u_half = [1.5 * c for c in u]
    weighted = W_REST * b[0]
    energy = 0.0
    vector = [0.0, 0.0, 0.0]
    for weight, pairs in ((W_AXIS, PAIRS[:3]), (W_DIAG, PAIRS[3:])):
        weighted = weighted + weight * total([plus[i] for i, _ in pairs])
        energies, parts = [], ([], [], [])
        for i, _ in pairs:
            cu = along(VELOCITIES[i], u)
            half = along(VELOCITIES[i], u_half) * plus[i]
            first = minus[i] + half
            energies.append(cu * first)
            second = first + half
            for axis in range(3):
                c = VELOCITIES[i][axis]
                if c:
                    parts[axis].append(second if c > 0 else -second)
        energy = energy + (3.0 * weight) * total(energies)
        vector = [vector[k] + (3.0 * weight) * total(parts[k]) for k in range(3)]
    energy = energy + rest * weighted
    vector = [vector[k] - (3.0 * weighted) * u[k] for k in range(3)]
    push = [slope * v for v in vector]
    inner = total([push[k] * (u[k] - SHIFT[k]) for k in range(3)])
    shared = jnp.where(kind == 2.0, 0.0, slope) * energy - inner
    out = [None] * Q
    out[0] = 2.0 * even * b[0] + shared
    for i, o in PAIRS:
        ev = even * plus[i] + shared
        od = odd * minus[i] + along(VELOCITIES[i], push)
        out[i] = ev + od
        out[o] = ev - od
    if state is None:
        return out, None
    evens = total([plus[i] * (state[i] + state[o]) for i, o in PAIRS])
    odds = total([minus[i] * (state[i] - state[o]) for i, o in PAIRS])
    term = (
        -OMEGA * (b[0] * state[0] + 0.5 * evens)
        + (1.0 - 0.5 * OMEGA) * odds
        + OMEGA * rho * energy
    )
    return out, jnp.where(kind == 3.0, term, 0.0)


def wall_masks(sign_rows, own_low, own_high, edges):
    lane = lax.broadcasted_iota(jnp.int32, (ROWS, LANES), 1)
    row = lax.broadcasted_iota(jnp.int32, (ROWS, LANES), 0)
    x_low, x_high, y_low, y_high = edges
    depth = lane % NZ
    masks = {}
    masks[2, 1] = depth == 0
    masks[2, -1] = depth == NZ - 1
    masks[1, 1] = lane < jnp.where(own_low, y_low * NZ, 0)
    masks[1, -1] = lane >= jnp.where(own_high, LANES - y_high * NZ, LANES)
    if sign_rows:
        masks[0, 1] = row < x_low
        masks[0, -1] = row >= ROWS - x_high
    return masks


def stream_tile(load, sign, masks, lane):
    cross_low, cross_high = lane >= LANES - NZ, lane < NZ
    combined = {}
    out = []
    for i, vector in enumerate(VELOCITIES):
        v = tuple(sign * c for c in vector)
        value = load(i, 0, -v[0], v[1])
        if v[1] == 1:
            value = jnp.where(cross_low, load(i, -1, -v[0], 1), value)
        elif v[1] == -1:
            value = jnp.where(cross_high, load(i, 1, -v[0], -1), value)
        amount = (v[1] * NZ + v[2]) % LANES
        if amount:
            value = pltpu.roll(value, amount, 1)
        outside = None
        if v not in combined:
            for axis in range(3):
                if v[axis] and (axis, v[axis]) in masks:
                    wall = masks[axis, v[axis]]
                    outside = wall if outside is None else outside | wall
            combined[v] = outside
        outside = combined[v]
        if outside is not None:
            value = jnp.where(outside, load(OPPOSITE[i], 0, 0, 0), value)
        out.append(value)
    return out


def iotas():
    row = lax.broadcasted_iota(jnp.int32, (ROWS, LANES), 0)
    lane = lax.broadcasted_iota(jnp.int32, (ROWS, LANES), 1)
    return row, lane, lane // NZ, lane % NZ


def columns(value, count):
    amount = (count * NZ) % LANES
    return pltpu.roll(value, amount, 1) if amount else value


def lines(value, count):
    amount = count % ROWS
    return pltpu.roll(value, amount, 0) if amount else value


class Layout:
    def __init__(self, count, guests, fills):
        self.fills = fills
        hosts = [at for at in fills if at not in guests]
        self.hosts = {at: hosts[4 * n : 4 * n + 4] for n, at in enumerate(guests)}
        self.guests = guests
        kept = [at for at in range(count) if at not in guests]
        self.place = {at: n for n, at in enumerate(kept)}
        self.size = len(kept)


class Packing:
    def __init__(self, ref, layout):
        self.ref, self.layout, self.held = ref, layout, {}

    def __setitem__(self, at, value):
        if at in self.layout.guests:
            self.held[at] = value
        else:
            self.ref[self.layout.place[at]] = value

    def finish(self):
        row, lane, column, depth = iotas()
        spare = depth >= EMPTY
        for at, value in self.held.items():
            for k, host in enumerate(self.layout.hosts[at]):
                place = self.layout.place[host]
                moved = pltpu.roll(value, EMPTY - FREE * k, 1)
                self.ref[place] = jnp.where(spare, moved, self.ref[place])
        for place in range(self.layout.size, self.ref.shape[0]):
            self.ref[place] = jnp.zeros((ROWS, LANES), jnp.float32)


class Unpacking:
    def __init__(self, source, layout):
        self.source, self.layout, self.cache = source, layout, {}
        self.changed = set(layout.guests).union(*layout.hosts.values())

    def __getitem__(self, at):
        if at not in self.cache:
            self.cache[at] = self.read(at)
        return self.cache[at]

    def read(self, at):
        row, lane, column, depth = iotas()
        layout = self.layout
        if at in layout.guests:
            value = None
            for k, host in enumerate(layout.hosts[at]):
                tile = self.source[layout.place[host]]
                moved = pltpu.roll(tile, LANES - (EMPTY - FREE * k), 1)
                value = moved if value is None else jnp.where(depth >= FREE * k, moved, value)
        else:
            value = self.source[layout.place[at]]
        if at in self.changed:
            value = jnp.where(depth >= EMPTY, layout.fills[at], value)
        return value


def layouts():
    y_fills = {2 * i + t: WEIGHTS[i] for i in LEVEL for t in range(2)}
    y_fills.update({Y_POP: W_DIAG, Y_CODE2: 0.0})
    out = [Layout(Y_TILES, [2 * i for i in LEVEL[:6]], y_fills)]
    for lanes, count in ((3, 10), (1, 4)):
        ring, _, code2, tiles = x_places(lanes)
        fills = {ring + n: WEIGHTS[2 * n] for n in range(1, X_HALVES)}
        fills.update({at: 0.0 for at in range(code2, tiles)})
        fills.update({X_LANE * n + i: WEIGHTS[i] for n in range(lanes) for i in LEVEL})
        guests = [X_LANE * (lanes - 1) + i for i in LEVEL[:count]]
        out.append(Layout(tiles, guests, fills))
    return out


class Pick:
    def __init__(self, flag, first, second):
        self.flag, self.first, self.second = flag, first, second

    def __getitem__(self, at):
        return jnp.where(self.flag, self.first[at], self.second[at])


class Deal:
    def __init__(self, even, first, second, layout, skip=0):
        self.even, self.skip, self.held = even, skip, {}
        self.first, self.second = Packing(first, layout), Packing(second, layout)

    def put(self, way, at, value):
        if (-way, at) not in self.held:
            self.held[way, at] = value
            return
        other = self.held.pop((-way, at))
        up, down = (value, other) if way == 1 else (other, value)
        self.first[at - self.skip] = jnp.where(self.even, up, down)
        self.second[at - self.skip] = jnp.where(self.even, down, up)

    def put_both(self, at, value):
        self.first[at - self.skip] = value
        self.second[at - self.skip] = value

    def finish(self):
        self.first.finish()
        self.second.finish()


def is_even(axis):
    return lax.rem(lax.axis_index(axis), 2) == 0


def pack_own(
    f_hbm,
    cot_hbm,
    codes_hbm,
    panels_hbm,
    porosity_hbm,
    first_ref,
    second_ref,
    own_ref,
    state_ref,
    own_cot_ref,
    field_ref,
    names_ref,
    f_ref,
    cot_ref,
    codes_ref,
    panels_ref,
    porosity_ref,
    sems,
):
    pieces = (
        (panels_hbm, panels_ref),
        (porosity_hbm, porosity_ref),
        (f_hbm, f_ref),
        (codes_hbm, codes_ref),
        (cot_hbm, cot_ref),
    )
    copies = [
        pltpu.make_async_copy(source, target, sems.at[n])
        for n, (source, target) in enumerate(pieces)
    ]
    for copy in copies:
        copy.start()
    for copy in copies[:4]:
        copy.wait()
    deal = Deal(is_even("gy"), first_ref, second_ref, layouts()[0])
    row, lane, column, depth = iotas()
    top = depth == NZ - 1

    def tile_of(ref, i, t):
        return ref[i, :, pl.ds(t * LANES, LANES)]

    codes, phis = [], []
    for t in range(2):
        names = panels_ref[0, t * LANES], panels_ref[4, t * LANES]
        phi = jnp.where(row < 4, porosity_ref[names[0]], porosity_ref[names[1]])
        names_ref[t] = jnp.where(row < 4, names[0], names[1])
        kinds = [tile_of(codes_ref, s, t).astype(jnp.float32) for s in range(STEPS)]
        f = [tile_of(f_ref, i, t) for i in range(Q)]
        g = collide(f, kinds[0], phi, moments(f))
        for i in range(Q):
            own_ref[2 * i + t] = g[i]
            state_ref[2 * i + t] = f[i]
        for s in range(STEPS):
            field_ref[2 * s + t] = kinds[s]
        field_ref[2 * OWN_PHI + t] = phi
        codes.append([jnp.where(top, phi, kinds[1]), kinds[2], kinds[3]])
    copies[4].wait()
    for i in range(Q):
        for way in (1, -1):
            near, far = (1, 0) if way == 1 else (0, 1)
            deep = 3 - way * VELOCITIES[i][1]
            cot = tile_of(cot_ref, i, near)
            g_far = own_ref[2 * i + far]
            if way == 1:
                mixed = jnp.where(column >= deep, g_far, columns(cot, deep - 4))
            else:
                mixed = jnp.where(column < 4 - deep, g_far, columns(cot, 4 - deep))
            deal.put(way, 2 * i, mixed if far == 0 else own_ref[2 * i])
            deal.put(way, 2 * i + 1, mixed if far == 1 else own_ref[2 * i + 1])
    for way in (1, -1):
        near, far = (1, 0) if way == 1 else (0, 1)
        outer = 3 if way == 1 else 0
        deal.put(way, Y_CODE1, codes[near][0])
        deal.put(way, Y_CODE2, codes[near][1])
        outside = columns(codes[far][0], 3 - 2 * outer)
        deal.put(way, Y_CODE3, jnp.where(column == 3 - outer, outside, codes[near][2]))
        extra = None
        for k, i in enumerate(turned(1, -way)):
            value = columns(own_ref[2 * i + far], k - outer)
            extra = value if extra is None else jnp.where(column == k, value, extra)
        deal.put(way, Y_POP, extra)
        extra = None
        for k, i in enumerate(turned(1, way)):
            value = columns(tile_of(cot_ref, i, near), k - (1 if way == 1 else 2))
            extra = value if extra is None else jnp.where(column == k, value, extra)
        deal.put(way, Y_COT, extra)
    deal.finish()
    for t in range(2):
        for i in range(Q):
            own_cot_ref[2 * i + t] = tile_of(cot_ref, i, t)


def is_right(near):
    return is_even("gy") if near else jnp.logical_not(is_even("gy"))


def half_lanes(right):
    row, lane, column, depth = iotas()
    return lane // (LANES // 2) == jnp.where(right, 0, 1)


def from_y(message_ref, near):
    row, lane, column, depth = iotas()
    ref = Unpacking(message_ref, layouts()[0])
    right = is_right(near)

    def population(i):
        return jnp.where(right, ref[2 * i], ref[2 * i + 1])

    def cotangent(i):
        values = []
        for way, place, far in ((1, 1, 0), (-1, 2, 1)):
            deep = 3 - way * VELOCITIES[i][1]
            value = columns(ref[2 * i + far], way * (4 - deep))
            if i in turned(1, way):
                extra = columns(ref[Y_COT], place - turned(1, way).index(i))
                value = jnp.where(column == place, extra, value)
            values.append(value)
        return jnp.where(right, values[1], values[0])

    def codes(s):
        return ref[(Y_CODE1, Y_CODE2, Y_CODE3)[s - 1]]

    def outer(i):
        left, above = ref[2 * i], ref[2 * i + 1]
        if i in turned(1, 1):
            above = columns(ref[Y_POP], -turned(1, 1).index(i))
        if i in turned(1, -1):
            left = columns(ref[Y_POP], 3 - turned(1, -1).index(i))
        return jnp.where(right, above, left)

    def outer_code():
        return jnp.where(right, columns(ref[Y_CODE3], 1), columns(ref[Y_CODE3], 3))

    return population, cotangent, codes, outer, outer_code


def mix_lines(deal, at, pop, cot, deep, way):
    row, lane, column, depth = iotas()
    if way == 1:
        mixed = jnp.where(row >= deep, pop, lines(cot, deep))
    else:
        mixed = jnp.where(row < ROWS - deep, pop, lines(cot, -deep))
    deal.put(way, at, mixed)


def pack_lines(deal, first, population, cotangent):
    row, lane, column, depth = iotas()

    for i in range(Q):
        pop, cot = population(i), cotangent(i)
        for way in (1, -1):
            mix_lines(deal, first + i, pop, cot, 3 - way * VELOCITIES[i][0], way)
    for way in (1, -1):
        extra = None
        for k, i in enumerate(turned(0, -way)):
            value = lines(population(i), k - (3 if way == 1 else 4))
            extra = value if extra is None else jnp.where(row == k, value, extra)
        for k, i in enumerate(turned(0, way)):
            value = lines(cotangent(i), 4 + k - (5 if way == 1 else 2))
            extra = jnp.where(row == 4 + k, value, extra)
        deal.put(way, first + X_EXTRA, extra)


def pack_neighbour(deal, lanes, message_ref, near):
    ring, code13, code2, tiles = x_places(lanes)
    population, cotangent, codes, outer, outer_code = from_y(message_ref, near)
    pack_lines(deal, X_LANE * (lanes - 1), population, cotangent)
    kept = half_lanes(is_right(near))
    for n in range(X_HALVES):
        first, second = (outer(2 * n - 1), outer(2 * n)) if n else (outer(0), outer_code())
        deal.put_both(ring + n, jnp.where(kept, first, pltpu.roll(second, LANES // 2, 1)))
    for way in (1, -1):
        mix_lines(deal, code13 + lanes - 1, codes(1), codes(3), 3, way)
    deal.put_both(tiles - 1, codes(2))


def pack_near(own_ref, cot_ref, field_ref, message_ref, first_ref, second_ref):
    row, lane, column, depth = iotas()
    deal = Deal(is_even("gx"), first_ref, second_ref, layouts()[1])
    ring, code13, code2, tiles = x_places(3)
    for t in range(2):
        pack_lines(
            deal,
            X_LANE * t,
            lambda i: own_ref[2 * i + t],
            lambda i: cot_ref[2 * i + t],
        )
        code = jnp.where(depth == NZ - 1, field_ref[2 * OWN_PHI + t], field_ref[2 + t])
        for way in (1, -1):
            mix_lines(deal, code13 + t, code, field_ref[6 + t], 3, way)
    first, second = field_ref[4], lines(field_ref[5], 4)
    deal.put(1, code2, jnp.where(row >= 4, first, second))
    deal.put(-1, code2, jnp.where(row < 4, first, second))
    pack_neighbour(deal, 3, message_ref, True)
    deal.finish()


def pack_far(message_ref, first_ref, second_ref):
    deal = Deal(is_even("gx"), first_ref, second_ref, layouts()[2])
    pack_neighbour(deal, 1, message_ref, False)
    deal.finish()


def from_x(ref, n, way, lanes):
    row, lane, column, depth = iotas()
    ring, code13, code2, _ = x_places(lanes)
    first = X_LANE * n

    def population(i):
        value = ref[first + i]
        if i in turned(0, -way):
            place = 3 if way == 1 else 4
            extra = lines(ref[first + X_EXTRA], place - turned(0, -way).index(i))
            value = jnp.where(row == place, extra, value)
        return value

    def cotangent(i):
        value = lines(ref[first + i], -way * (3 - way * VELOCITIES[i][0]))
        if i in turned(0, way):
            place = 5 if way == 1 else 2
            extra = lines(ref[first + X_EXTRA], place - 4 - turned(0, way).index(i))
            value = jnp.where(row == place, extra, value)
        return value

    def codes(s):
        if s == 2:
            return lines(ref[code2 + n // 2], 4 * (n % 2))
        value = ref[code13 + n]
        return value if s == 1 else lines(value, -3 * way)

    def outer(i):
        value = ref[ring + (i + 1) // 2]
        return pltpu.roll(value, LANES // 2, 1) if i and i % 2 == 0 else value

    def outer_code():
        return pltpu.roll(ref[ring], LANES // 2, 1)

    return population, cotangent, codes, outer, outer_code


def sides(first_ref, second_ref, axis, layout):
    even = is_even(axis)
    picks = Pick(even, second_ref, first_ref), Pick(even, first_ref, second_ref)
    return [Unpacking(pick, layout) for pick in picks]


def own_rows(step=0):
    return pl.ds(ROWS + step, ROWS)


def halo_rows(step=0):
    return pl.ds({0: 2 * ROWS, -1: 2 * ROWS - 1, 1: 1}[step], ROWS)


def put_halo(ref, at, halo):
    ref[at, pl.ds(0, ROWS), :] = halo
    ref[at, halo_rows(), :] = halo


def put_ring(ref, at, own, halo):
    ref[at, own_rows(), :] = own
    put_halo(ref, at, halo)


def expand(code):
    row, lane, column, depth = iotas()
    top = depth == NZ - 1
    phi = jnp.where(top, code, 0.0)
    for step in (1, 2, 4, 8, 16):
        phi = phi + pltpu.roll(phi, LANES - step, 1)
    return jnp.where(top, 0.0, code), phi


def lay_own(c, population, cotangent, codes, code_phi, pop, cot, wide, field):
    for i in range(Q):
        pop[5 * i + c, pl.ds(2 * ROWS, ROWS), :] = population(i)
        if cotangent is not None:
            cot[4 * i + c - 1, own_rows(), :] = cotangent(i)
    for n in range(2):
        wide[n, c, 1] = code_phi[n]
    if cotangent is not None:
        field[0, c - 1, 0], field[1, c - 1, 0] = code_phi[1], code_phi[0]
        for s in (2, 3):
            field[s, c - 1, 0] = codes(s)


def lay_halo(c, below, above, pop, cot, wide, field):
    row, lane, column, depth = iotas()
    before, behind = expand(below[2](1)), expand(above[2](1))
    for n in range(2):
        wide[n, c, 0], wide[n, c, 2] = before[n], behind[n]
    for i in range(Q):
        pop[5 * i + c, pl.ds(ROWS, ROWS), :] = below[0](i)
        pop[5 * i + c, pl.ds(3 * ROWS, ROWS), :] = above[0](i)
        if below[1] is not None:
            put_halo(cot, 4 * i + c - 1, jnp.where(row < 4, above[1](i), below[1](i)))
    if below[1] is not None:
        for n, place in ((0, 1), (1, 0)):
            field[place, c - 1, 1] = jnp.where(row < 4, behind[n], before[n])
        for s in (2, 3):
            field[s, c - 1, 1] = jnp.where(row < 4, above[2](s), below[2](s))


def near_tile():
    return jnp.where(is_right(True), 4, 1)


def lay_out(
    near_y_ref,
    far_y_ref,
    first_near_ref,
    second_near_ref,
    own_ref,
    field_ref,
    cot_ref,
    pop,
    cot,
    wide,
    field,
):
    spaces = pop, cot, wide, field
    below, above = sides(first_near_ref, second_near_ref, "gx", layouts()[1])
    for t in range(2):
        lay_own(
            2 + t,
            lambda i: own_ref[2 * i + t],
            lambda i: cot_ref[2 * i + t],
            lambda s: field_ref[2 * s + t],
            (field_ref[2 + t], field_ref[2 * OWN_PHI + t]),
            *spaces,
        )
        lay_halo(2 + t, from_x(below, t, 1, 3), from_x(above, t, -1, 3), *spaces)
    near, far = from_y(near_y_ref, True), from_y(far_y_ref, False)
    for c, (population, cotangent, codes, _, _) in ((near_tile(), near), (5 - near_tile(), far)):
        lay_own(c, population, cotangent, codes, expand(codes(1)), *spaces)
    kept = half_lanes(is_right(True))
    lay_own(
        0,
        lambda i: jnp.where(kept, near[3](i), far[3](i)),
        None,
        None,
        expand(jnp.where(kept, near[4](), far[4]())),
        *spaces,
    )
    lay_halo(near_tile(), from_x(below, 2, 1, 3), from_x(above, 2, -1, 3), *spaces)


def lay_far(near_refs, far_refs, spaces):
    nears, fars = (
        [
            from_x(ref, lanes - 1, way, lanes)
            for ref, way in zip(sides(*refs, "gx", layout), (1, -1))
        ]
        for refs, layout, lanes in zip((near_refs, far_refs), layouts()[1:], (3, 1))
    )
    lay_halo(5 - near_tile(), *fars, *spaces)
    kept = half_lanes(is_right(True))
    ring = [
        (
            lambda i, near=near, far=far: jnp.where(kept, near[3](i), far[3](i)),
            None,
            lambda s, near=near, far=far: jnp.where(kept, near[4](), far[4]()),
        )
        for near, far in zip(nears, fars)
    ]
    lay_halo(0, *ring, *spaces)


def steps_kernel(
    sizes,
    state_ref,
    own_field_ref,
    names_ref,
    first_near_ref,
    second_near_ref,
    first_far_ref,
    second_far_ref,
    *refs,
):
    adjoint_ref, panel_ref, pop_a, ring_a, wide, field, pop_b, ring_b, saved, mom, grad = refs[4:]
    size_x, size_y = sizes
    lay_far(
        (first_near_ref, second_near_ref),
        (first_far_ref, second_far_ref),
        (pop_a, ring_a, wide, field),
    )

    at_x, at_y = lax.axis_index("gx"), lax.axis_index("gy")
    edges = (
        jnp.where(at_x == 0, 1, 0),
        jnp.where(at_x == size_x - 1, 1, 0),
        jnp.where(at_y == 0, 1, 0),
        jnp.where(at_y == size_y - 1, 1, 0),
    )
    row, lane, column, depth = iotas()
    after = row < 4

    def masks_of(tile, first, r):
        return wall_masks(r == 0, tile == first, tile == first + 1, edges)

    def neighbours(tile, tiles):
        if isinstance(tile, int):
            return {0: tile, -1: (tile - 1) % tiles, 1: (tile + 1) % tiles}
        return {0: tile, -1: lax.rem(tile + tiles - 1, tiles), 1: lax.rem(tile + 1, tiles)}

    def from_wide(ref, tile, r):
        step = neighbours(tile, 5)

        def load(i, tile_step, row_step, move):
            at = 5 * i + step[tile_step]
            before, own, behind = (ref[at, pl.ds(ROWS * n + row_step, ROWS), :] for n in (1, 2, 3))
            return (own, jnp.where(after, behind, before), before, behind)[r]

        return load

    def from_ring(ref, tile, tiles, r):
        step = neighbours(tile, tiles)

        def load(i, tile_step, row_step, move):
            rows = own_rows(row_step) if r == 0 else halo_rows(row_step)
            return ref[tiles * i + step[tile_step], rows, :]

        return load

    def from_outer(ref, r):
        def load(i, tile_step, row_step, move):
            rows = own_rows(row_step) if r == 0 else halo_rows(row_step)
            if tile_step:
                return ref[4 * i + (2 if tile_step < 0 else 1), rows, :]
            cut = {0: 2, 1: 1, -1: 3}[move]
            return jnp.where(column < cut, ref[4 * i + 3, rows, :], ref[4 * i, rows, :])

        return load

    def note(s, tile, r, parts):
        for n, value in enumerate(parts[2:4] + tuple(parts[4])):
            mom[s - 1, n, tile, r] = value

    def first_step(tile, carry):
        place = lax.rem(tile + 4, 5)
        halo = []
        for r in (2, 0, 3):
            f = stream_tile(from_wide(pop_a, tile, r), 1, masks_of(tile, 2, r), lane)
            parts = moments(f)
            if r == 0:
                note(1, place, 0, parts)
                for i in range(Q):
                    saved[0, i, place] = f[i]
            else:
                halo.append(parts[2:4] + tuple(parts[4]))
            at = {2: 0, 0: 1, 3: 2}[r]
            g = collide(f, wide[0, tile, at], wide[1, tile, at], parts)
            for i in range(Q):
                pop_b[5 * i + tile, pl.ds(ROWS * (at + 1), ROWS), :] = g[i]
        for n in range(5):
            mom[0, n, place, 1] = jnp.where(after, halo[1][n], halo[0][n])
        return carry

    lax.fori_loop(0, 5, first_step, 0)

    def second_step(tile, carry):
        out = []
        for r in range(2):
            f = stream_tile(from_wide(pop_b, tile + 1, r), 1, masks_of(tile, 1, r), lane)
            parts = moments(f)
            note(2, tile, r, parts)
            if r == 0:
                for i in range(Q):
                    saved[1, i, tile] = f[i]
            out.append(collide(f, field[2, tile, r], field[0, tile, r], parts))
        for i in range(Q):
            put_ring(ring_b, 4 * i + tile, out[0][i], out[1][i])
        return carry

    lax.fori_loop(0, 4, second_step, 0)

    def third_step(tile, carry):
        for r in range(2):
            f = stream_tile(from_ring(ring_b, tile, 4, r), 1, masks_of(tile, 1, r), lane)
            note(3, tile, r, moments(f))
            if r == 0:
                for i in range(Q):
                    saved[2, i, tile] = f[i]
        return carry

    lax.fori_loop(0, 4, third_step, 0)

    def back_tile(load, s, tile, r, own):
        b = stream_tile(load, -1, masks_of(4 if tile is None else tile, 1, r), lane)

        def read(get):
            return jnp.where(column < 2, get(3), get(0)) if tile is None else get(tile)

        rho, rinv, *u = [read(lambda at: mom[s - 1, n, at, r]) for n in range(5)]
        kind, phi = read(lambda at: field[s, at, r]), read(lambda at: field[0, at, r])
        state = [saved[s - 1, i, tile] for i in range(Q)] if own else None
        back, term = collide_back(b, kind, phi, rho, rinv, u, state)
        if own:
            grad[tile] = term if s == 3 else grad[tile] + term
        return back

    def last_step(tile, carry):
        out = [back_tile(from_ring(ring_a, tile, 4, r), 3, tile, r, r == 0) for r in range(2)]
        for i in range(Q):
            put_ring(ring_b, 4 * i + tile, out[0][i], out[1][i])
        return carry

    lax.fori_loop(0, 4, last_step, 0)

    for k, tile in enumerate((1, 2, None)):
        out = []
        for r in range(2):
            load = from_outer(ring_b, r) if tile is None else from_ring(ring_b, tile, 4, r)
            out.append(back_tile(load, 2, tile, r, r == 0 and tile is not None))
        for i in range(Q):
            put_ring(ring_a, 3 * i + k, out[0][i], out[1][i])

    for k, tile in enumerate((1, 2, None)):
        out = []
        for r in range(2):
            load = from_ring(ring_a, k, 3, r)
            out.append(back_tile(load, 1, tile, r, r == 0 and tile is not None))
        for i in range(Q):
            put_ring(ring_b, 3 * i + k, out[0][i], out[1][i])

    panel = lax.broadcasted_iota(jnp.int32, panel_ref.shape, 1)
    sums = jnp.zeros(panel_ref.shape, jnp.float32)
    for t in range(2):
        b = stream_tile(from_ring(ring_b, t, 3, 0), -1, masks_of(t, 0, 0), lane)
        f = [state_ref[2 * i + t] for i in range(Q)]
        kind, phi = own_field_ref[t], own_field_ref[2 * OWN_PHI + t]
        _, _, rho, rinv, u = moments(f)
        back, term = collide_back(b, kind, phi, rho, rinv, u, f)
        for i in range(Q):
            adjoint_ref[i, :, pl.ds(t * LANES, LANES)] = back[i]
        term = term + grad[t + 1]
        for part in range(2):
            amount = jnp.sum(jnp.where((row < 4) == (part == 0), term, 0.0))
            name = names_ref[t, 4 * part : 4 * part + 1, 0:1]
            sums = sums + jnp.where(panel == name, amount, 0.0)
    panel_ref[...] = sums


def finish(parts_ref, adjoint_ref, sums_hbm, adjoint_hbm, sums_ref, sems):
    adjoint_copy = pltpu.make_async_copy(adjoint_ref, adjoint_hbm, sems.at[0])
    adjoint_copy.start()
    sums_ref[...] = jnp.sum(parts_ref[...], axis=0)
    sums_copy = pltpu.make_async_copy(sums_ref, sums_hbm, sems.at[1])
    sums_copy.start()
    sums_copy.wait()
    adjoint_copy.wait()


VMEM = pl.BlockSpec(memory_space=pltpu.VMEM)
HBM = pl.BlockSpec(memory_space=pltpu.HBM)


def shape_of(*dims):
    return jax.ShapeDtypeStruct(dims, jnp.float32)


def tiles_of(count):
    return shape_of(count, ROWS, LANES)


def on_device(sizes, checkpoint, cotangent, cell_codes, porosity, baffle_index):
    size_x, size_y = sizes
    panels = porosity.shape[0]
    devices = size_x * size_y
    y_layout, near_layout, far_layout = layouts()

    params = pltpu.CompilerParams(vmem_limit_bytes=32 * 1024 * 1024)

    def call(kernel, out_shape, in_specs, scratch=(), name=None, aliases={}):
        return pl.pallas_call(
            kernel,
            out_shape=out_shape,
            in_specs=in_specs,
            out_specs=jax.tree.map(lambda _: VMEM, out_shape),
            scratch_shapes=scratch,
            input_output_aliases=aliases,
            compiler_params=params,
            name=name,
        )

    def swap(value, axis, size):
        return lax.ppermute(value, axis, [(i, i ^ 1) for i in range(size) if i ^ 1 < size])

    def swap_between(value, axis, size):
        pairs = [(i, i + 1) for i in range(1, size - 1, 2)]
        return lax.ppermute(value, axis, pairs + [(j, i) for i, j in pairs])

    arguments = [
        pltpu.with_memory_space_constraint(value, pltpu.HBM)
        for value in (checkpoint, cotangent, cell_codes, baffle_index, porosity)
    ]
    near_y, far_y, own, state, cot, field, names = call(
        pack_own,
        (tiles_of(y_layout.size),) * 2
        + (tiles_of(2 * Q),) * 3
        + (tiles_of(2 * OWN_PHI + 2), jax.ShapeDtypeStruct((2, ROWS, LANES), jnp.int32)),
        [HBM] * 5,
        [
            pltpu.VMEM((Q, ROWS, 2 * LANES), jnp.float32),
            pltpu.VMEM((Q, ROWS, 2 * LANES), jnp.float32),
            pltpu.VMEM((STEPS, ROWS, 2 * LANES), jnp.int32),
            pltpu.SMEM(baffle_index.shape, jnp.int32),
            pltpu.SMEM(porosity.shape, jnp.float32),
            pltpu.SemaphoreType.DMA((5,)),
        ],
        name="pack_own",
    )(*arguments)
    near_y = swap(near_y, "gy", size_y)
    far_y = swap_between(far_y, "gy", size_y)
    first_near, second_near = call(
        pack_near,
        (tiles_of(near_layout.size), tiles_of(near_layout.size + 1)),
        [VMEM] * 4,
        name="pack_near",
    )(own, cot, field, near_y)
    second_near = swap_between(second_near, "gx", size_x)
    first_near = swap(first_near, "gx", size_x)
    first_far, second_far = call(
        pack_far,
        (tiles_of(far_layout.size), tiles_of(far_layout.size + 1)),
        [VMEM],
        name="pack_far",
    )(far_y)
    second_far = swap_between(second_far, "gx", size_x)
    first_far = swap(first_far, "gx", size_x)
    spaces = (
        shape_of(5 * Q, 5 * ROWS, LANES),
        shape_of(4 * Q, 3 * ROWS, LANES),
        shape_of(2, 5, 3, ROWS, LANES),
        shape_of(4, 4, 2, ROWS, LANES),
    )
    laid = call(lay_out, spaces, [VMEM] * 7, name="lay_out")(
        near_y, far_y, first_near, second_near, own, field, cot
    )
    adjoint, sums, *_ = call(
        functools.partial(steps_kernel, sizes),
        (pltpu.VMEM((Q, ROWS, 2 * LANES), jnp.float32), shape_of(devices, panels)) + spaces,
        [VMEM] * 11,
        [
            pltpu.VMEM((5 * Q, 5 * ROWS, LANES), jnp.float32),
            pltpu.VMEM((4 * Q, 3 * ROWS, LANES), jnp.float32),
            pltpu.VMEM((3, Q, 5, ROWS, LANES), jnp.float32),
            pltpu.VMEM((3, 5, 5, 2, ROWS, LANES), jnp.float32),
            pltpu.VMEM((4, ROWS, LANES), jnp.float32),
        ],
        name="steps",
        aliases={7 + n: 2 + n for n in range(4)},
    )(state, field, names, first_near, second_near, first_far, second_far, *laid)
    gathered = lax.all_to_all(sums, ("gx", "gy"), 0, 0, tiled=True)
    totals, adjoint = pl.pallas_call(
        finish,
        out_shape=(shape_of(1, panels), shape_of(Q, ROWS, 2 * LANES)),
        in_specs=[VMEM, VMEM],
        out_specs=(HBM, HBM),
        scratch_shapes=[pltpu.VMEM((1, panels), jnp.float32), pltpu.SemaphoreType.DMA((2,))],
        compiler_params=params,
        name="finish",
    )(gathered.reshape(devices, 1, panels), adjoint)
    return adjoint, totals.reshape(panels)


def solution(mesh):
    sizes = (mesh.shape["gx"], mesh.shape["gy"])
    in_specs = (P(None, "gx", "gy"), P(None, "gx", "gy"), P(None, "gx", "gy"), P(), P("gx", "gy"))
    out_specs = (P(None, "gx", "gy"), P())
    return jax.shard_map(
        functools.partial(on_device, sizes),
        mesh=mesh,
        in_specs=in_specs,
        out_specs=out_specs,
        check_vma=False,
    )
```

```python
import functools

import jax
import jax.numpy as jnp
import numpy as np
from jax import lax
from jax.experimental import pallas as pl
from jax.experimental.pallas import tpu as pltpu
from jax.sharding import PartitionSpec as P

Q = 19
STEPS = 4
NZ = 32
ROWS = 8
LANES = 128
OMEGA = 1.6
ACCEL = (0.002, 0.0, -0.003)
SHIFT = tuple(a / OMEGA for a in ACCEL)

VELOCITIES = [
    (0, 0, 0),
    (1, 0, 0),
    (-1, 0, 0),
    (0, 1, 0),
    (0, -1, 0),
    (0, 0, 1),
    (0, 0, -1),
    (1, 1, 0),
    (-1, -1, 0),
    (1, -1, 0),
    (-1, 1, 0),
    (1, 0, 1),
    (-1, 0, -1),
    (1, 0, -1),
    (-1, 0, 1),
    (0, 1, 1),
    (0, -1, -1),
    (0, 1, -1),
    (0, -1, 1),
]
OPPOSITE = [0, 2, 1, 4, 3, 6, 5, 8, 7, 10, 9, 12, 11, 14, 13, 16, 15, 18, 17]
PAIRS = [(i, i + 1) for i in range(1, Q, 2)]
W_REST, W_AXIS, W_DIAG = 1.0 / 3.0, 1.0 / 18.0, 1.0 / 36.0

Y_CODE1, Y_CODE2, Y_CODE3, Y_POP, Y_COT = 38, 39, 40, 41, 42
Y_TILES = 43
X_EXTRA = 19
X_LANE = 20
X_HALVES = 10


def x_places(lanes):
    ring = X_LANE * lanes
    code13 = ring + X_HALVES
    code2 = code13 + lanes
    return ring, code13, code2, code2 + (lanes + 1) // 2


EMPTY = 25
FREE = NZ - EMPTY
WEIGHTS = [W_REST] + [W_AXIS] * 6 + [W_DIAG] * 12
LEVEL = [i for i, v in enumerate(VELOCITIES) if v[2] < 1]
OWN_PHI = 4


def turned(axis, outward):
    return [i for i, v in enumerate(VELOCITIES) if v[axis] == outward and sum(map(abs, v)) == 2]


def total(values):
    values = list(values)
    while len(values) > 1:
        values = [a + b for a, b in zip(values[::2], values[1::2])] + (
            [values[-1]] if len(values) % 2 else []
        )
    return values[0]


def along(vector, three):
    terms = None
    for c, value in zip(vector, three):
        if c == 0:
            continue
        if terms is None:
            terms = value if c > 0 else -value
        else:
            terms = terms + value if c > 0 else terms - value
    return terms


def moments(f):
    plus = {i: f[i] + f[o] for i, o in PAIRS}
    minus = {i: f[i] - f[o] for i, o in PAIRS}
    rho = total([f[0]] + [plus[i] for i, _ in PAIRS])
    rinv = 1.0 / rho
    u = []
    for axis in range(3):
        terms = [
            minus[i] if VELOCITIES[i][axis] > 0 else -minus[i]
            for i, _ in PAIRS
            if VELOCITIES[i][axis] != 0
        ]
        u.append(total(terms) * rinv + SHIFT[axis])
    return plus, minus, rho, rinv, u


def coefficients(kind, phi, rinv):
    baffle = kind == 3.0
    gas = kind == 0.0
    even = jnp.where(gas, 0.0, jnp.where(baffle, 0.5 - 0.5 * OMEGA * phi, 0.5 * (1.0 - OMEGA)))
    odd = jnp.where(
        gas, 0.0, jnp.where(baffle, (1.0 - 0.5 * OMEGA) * phi - 0.5, 0.5 * (1.0 - OMEGA))
    )
    slope = jnp.where(
        baffle,
        OMEGA * phi,
        jnp.where(kind == 1.0, OMEGA, jnp.where(kind == 2.0, OMEGA * rinv, 0.0)),
    )
    return even, odd, slope


def collide(f, kind, phi, parts):
    plus, minus, rho, rinv, u = parts
    even, odd, slope = coefficients(kind, phi, rinv)
    scale = slope * rho
    rest = 1.0 - 1.5 * (u[0] * u[0] + u[1] * u[1] + u[2] * u[2])
    base = scale * rest + jnp.where(kind == 0.0, 1.0, 0.0)
    out = [None] * Q
    out[0] = 2.0 * even * f[0] + W_REST * base
    for weight, pairs in ((W_AXIS, PAIRS[:3]), (W_DIAG, PAIRS[3:])):
        flat = weight * base
        three = (3.0 * weight) * scale
        for i, o in pairs:
            cu = along(VELOCITIES[i], u)
            lin = three * cu
            ev = even * plus[i] + (flat + 1.5 * lin * cu)
            od = odd * minus[i] + lin
            out[i] = ev + od
            out[o] = ev - od
    return out


def collide_back(b, kind, phi, rho, rinv, u, state=None):
    even, odd, slope = coefficients(kind, phi, rinv)
    plus = {i: b[i] + b[o] for i, o in PAIRS}
    minus = {i: b[i] - b[o] for i, o in PAIRS}
    rest = 1.0 - 1.5 * (u[0] * u[0] + u[1] * u[1] + u[2] * u[2])
    u_half = [1.5 * c for c in u]
    weighted = W_REST * b[0]
    energy = 0.0
    vector = [0.0, 0.0, 0.0]
    for weight, pairs in ((W_AXIS, PAIRS[:3]), (W_DIAG, PAIRS[3:])):
        weighted = weighted + weight * total([plus[i] for i, _ in pairs])
        energies, parts = [], ([], [], [])
        for i, _ in pairs:
            cu = along(VELOCITIES[i], u)
            half = along(VELOCITIES[i], u_half) * plus[i]
            first = minus[i] + half
            energies.append(cu * first)
            second = first + half
            for axis in range(3):
                c = VELOCITIES[i][axis]
                if c:
                    parts[axis].append(second if c > 0 else -second)
        energy = energy + (3.0 * weight) * total(energies)
        vector = [vector[k] + (3.0 * weight) * total(parts[k]) for k in range(3)]
    energy = energy + rest * weighted
    vector = [vector[k] - (3.0 * weighted) * u[k] for k in range(3)]
    push = [slope * v for v in vector]
    inner = total([push[k] * (u[k] - SHIFT[k]) for k in range(3)])
    shared = jnp.where(kind == 2.0, 0.0, slope) * energy - inner
    out = [None] * Q
    out[0] = 2.0 * even * b[0] + shared
    for i, o in PAIRS:
        ev = even * plus[i] + shared
        od = odd * minus[i] + along(VELOCITIES[i], push)
        out[i] = ev + od
        out[o] = ev - od
    if state is None:
        return out, None
    evens = total([plus[i] * (state[i] + state[o]) for i, o in PAIRS])
    odds = total([minus[i] * (state[i] - state[o]) for i, o in PAIRS])
    term = (
        -OMEGA * (b[0] * state[0] + 0.5 * evens)
        + (1.0 - 0.5 * OMEGA) * odds
        + OMEGA * rho * energy
    )
    return out, jnp.where(kind == 3.0, term, 0.0)


def wall_masks(sign_rows, own_low, own_high, edges):
    lane = lax.broadcasted_iota(jnp.int32, (ROWS, LANES), 1)
    row = lax.broadcasted_iota(jnp.int32, (ROWS, LANES), 0)
    x_low, x_high, y_low, y_high = edges
    depth = lane % NZ
    masks = {}
    masks[2, 1] = depth == 0
    masks[2, -1] = depth == NZ - 1
    masks[1, 1] = lane < jnp.where(own_low, y_low * NZ, 0)
    masks[1, -1] = lane >= jnp.where(own_high, LANES - y_high * NZ, LANES)
    if sign_rows:
        masks[0, 1] = row < x_low
        masks[0, -1] = row >= ROWS - x_high
    return masks


def stream_tile(load, sign, masks, lane):
    cross_low, cross_high = lane >= LANES - NZ, lane < NZ
    combined = {}
    out = []
    for i, vector in enumerate(VELOCITIES):
        v = tuple(sign * c for c in vector)
        value = load(i, 0, -v[0], v[1])
        if v[1] == 1:
            value = jnp.where(cross_low, load(i, -1, -v[0], 1), value)
        elif v[1] == -1:
            value = jnp.where(cross_high, load(i, 1, -v[0], -1), value)
        amount = (v[1] * NZ + v[2]) % LANES
        if amount:
            value = pltpu.roll(value, amount, 1)
        outside = None
        if v not in combined:
            for axis in range(3):
                if v[axis] and (axis, v[axis]) in masks:
                    wall = masks[axis, v[axis]]
                    outside = wall if outside is None else outside | wall
            combined[v] = outside
        outside = combined[v]
        if outside is not None:
            value = jnp.where(outside, load(OPPOSITE[i], 0, 0, 0), value)
        out.append(value)
    return out


def iotas():
    row = lax.broadcasted_iota(jnp.int32, (ROWS, LANES), 0)
    lane = lax.broadcasted_iota(jnp.int32, (ROWS, LANES), 1)
    return row, lane, lane // NZ, lane % NZ


def columns(value, count):
    amount = (count * NZ) % LANES
    return pltpu.roll(value, amount, 1) if amount else value


def lines(value, count):
    amount = count % ROWS
    return pltpu.roll(value, amount, 0) if amount else value


class Layout:
    def __init__(self, count, guests, fills):
        self.fills = fills
        hosts = [at for at in fills if at not in guests]
        self.hosts = {at: hosts[4 * n : 4 * n + 4] for n, at in enumerate(guests)}
        self.guests = guests
        kept = [at for at in range(count) if at not in guests]
        self.place = {at: n for n, at in enumerate(kept)}
        self.size = len(kept)


class Packing:
    def __init__(self, ref, layout):
        self.ref, self.layout, self.held = ref, layout, {}

    def __setitem__(self, at, value):
        if at in self.layout.guests:
            self.held[at] = value
        else:
            self.ref[self.layout.place[at]] = value

    def finish(self):
        row, lane, column, depth = iotas()
        spare = depth >= EMPTY
        for at, value in self.held.items():
            for k, host in enumerate(self.layout.hosts[at]):
                place = self.layout.place[host]
                moved = pltpu.roll(value, EMPTY - FREE * k, 1)
                self.ref[place] = jnp.where(spare, moved, self.ref[place])
        for place in range(self.layout.size, self.ref.shape[0]):
            self.ref[place] = jnp.zeros((ROWS, LANES), jnp.float32)


class Unpacking:
    def __init__(self, source, layout):
        self.source, self.layout, self.cache = source, layout, {}
        self.changed = set(layout.guests).union(*layout.hosts.values())

    def __getitem__(self, at):
        if at not in self.cache:
            self.cache[at] = self.read(at)
        return self.cache[at]

    def read(self, at):
        row, lane, column, depth = iotas()
        layout = self.layout
        if at in layout.guests:
            value = None
            for k, host in enumerate(layout.hosts[at]):
                tile = self.source[layout.place[host]]
                moved = pltpu.roll(tile, LANES - (EMPTY - FREE * k), 1)
                value = moved if value is None else jnp.where(depth >= FREE * k, moved, value)
        else:
            value = self.source[layout.place[at]]
        if at in self.changed:
            value = jnp.where(depth >= EMPTY, layout.fills[at], value)
        return value


def layouts():
    y_fills = {2 * i + t: WEIGHTS[i] for i in LEVEL for t in range(2)}
    y_fills.update({Y_POP: W_DIAG, Y_CODE2: 0.0})
    out = [Layout(Y_TILES, [2 * i for i in LEVEL[:6]], y_fills)]
    for lanes, count in ((3, 10), (1, 4)):
        ring, _, code2, tiles = x_places(lanes)
        fills = {ring + n: WEIGHTS[2 * n] for n in range(1, X_HALVES)}
        fills.update({at: 0.0 for at in range(code2, tiles)})
        fills.update({X_LANE * n + i: WEIGHTS[i] for n in range(lanes) for i in LEVEL})
        guests = [X_LANE * (lanes - 1) + i for i in LEVEL[:count]]
        out.append(Layout(tiles, guests, fills))
    return out


class Pick:
    def __init__(self, flag, first, second):
        self.flag, self.first, self.second = flag, first, second

    def __getitem__(self, at):
        return jnp.where(self.flag, self.first[at], self.second[at])


class Deal:
    def __init__(self, even, first, second, layout, skip=0):
        self.even, self.skip, self.held = even, skip, {}
        self.first, self.second = Packing(first, layout), Packing(second, layout)

    def put(self, way, at, value):
        if (-way, at) not in self.held:
            self.held[way, at] = value
            return
        other = self.held.pop((-way, at))
        up, down = (value, other) if way == 1 else (other, value)
        self.first[at - self.skip] = jnp.where(self.even, up, down)
        self.second[at - self.skip] = jnp.where(self.even, down, up)

    def put_both(self, at, value):
        self.first[at - self.skip] = value
        self.second[at - self.skip] = value

    def finish(self):
        self.first.finish()
        self.second.finish()


def is_even(axis):
    return lax.rem(lax.axis_index(axis), 2) == 0


def pack_own(
    f_hbm,
    cot_hbm,
    codes_hbm,
    panels_hbm,
    porosity_hbm,
    first_ref,
    second_ref,
    own_ref,
    state_ref,
    own_cot_ref,
    field_ref,
    names_ref,
    f_ref,
    cot_ref,
    codes_ref,
    panels_ref,
    porosity_ref,
    sems,
):
    pieces = (
        (panels_hbm, panels_ref),
        (porosity_hbm, porosity_ref),
        (f_hbm, f_ref),
        (codes_hbm, codes_ref),
        (cot_hbm, cot_ref),
    )
    copies = [
        pltpu.make_async_copy(source, target, sems.at[n])
        for n, (source, target) in enumerate(pieces)
    ]
    for copy in copies:
        copy.start()
    for copy in copies[:4]:
        copy.wait()
    deal = Deal(is_even("gy"), first_ref, second_ref, layouts()[0])
    row, lane, column, depth = iotas()
    top = depth == NZ - 1

    def tile_of(ref, i, t):
        return ref[i, :, pl.ds(t * LANES, LANES)]

    codes, phis = [], []
    for t in range(2):
        names = panels_ref[0, t * LANES], panels_ref[4, t * LANES]
        phi = jnp.where(row < 4, porosity_ref[names[0]], porosity_ref[names[1]])
        names_ref[t] = jnp.where(row < 4, names[0], names[1])
        kinds = [tile_of(codes_ref, s, t).astype(jnp.float32) for s in range(STEPS)]
        f = [tile_of(f_ref, i, t) for i in range(Q)]
        g = collide(f, kinds[0], phi, moments(f))
        for i in range(Q):
            own_ref[2 * i + t] = g[i]
            state_ref[2 * i + t] = f[i]
        for s in range(STEPS):
            field_ref[2 * s + t] = kinds[s]
        field_ref[2 * OWN_PHI + t] = phi
        codes.append([jnp.where(top, phi, kinds[1]), kinds[2], kinds[3]])
    copies[4].wait()
    for i in range(Q):
        for way in (1, -1):
            near, far = (1, 0) if way == 1 else (0, 1)
            deep = 3 - way * VELOCITIES[i][1]
            cot = tile_of(cot_ref, i, near)
            g_far = own_ref[2 * i + far]
            if way == 1:
                mixed = jnp.where(column >= deep, g_far, columns(cot, deep - 4))
            else:
                mixed = jnp.where(column < 4 - deep, g_far, columns(cot, 4 - deep))
            deal.put(way, 2 * i, mixed if far == 0 else own_ref[2 * i])
            deal.put(way, 2 * i + 1, mixed if far == 1 else own_ref[2 * i + 1])
    for way in (1, -1):
        near, far = (1, 0) if way == 1 else (0, 1)
        outer = 3 if way == 1 else 0
        deal.put(way, Y_CODE1, codes[near][0])
        deal.put(way, Y_CODE2, codes[near][1])
        outside = columns(codes[far][0], 3 - 2 * outer)
        deal.put(way, Y_CODE3, jnp.where(column == 3 - outer, outside, codes[near][2]))
        extra = None
        for k, i in enumerate(turned(1, -way)):
            value = columns(own_ref[2 * i + far], k - outer)
            extra = value if extra is None else jnp.where(column == k, value, extra)
        deal.put(way, Y_POP, extra)
        extra = None
        for k, i in enumerate(turned(1, way)):
            value = columns(tile_of(cot_ref, i, near), k - (1 if way == 1 else 2))
            extra = value if extra is None else jnp.where(column == k, value, extra)
        deal.put(way, Y_COT, extra)
    deal.finish()
    for t in range(2):
        for i in range(Q):
            own_cot_ref[2 * i + t] = tile_of(cot_ref, i, t)


def is_right(near):
    return is_even("gy") if near else jnp.logical_not(is_even("gy"))


def half_lanes(right):
    row, lane, column, depth = iotas()
    return lane // (LANES // 2) == jnp.where(right, 0, 1)


def from_y(message_ref, near):
    row, lane, column, depth = iotas()
    ref = Unpacking(message_ref, layouts()[0])
    right = is_right(near)

    def population(i):
        return jnp.where(right, ref[2 * i], ref[2 * i + 1])

    def cotangent(i):
        values = []
        for way, place, far in ((1, 1, 0), (-1, 2, 1)):
            deep = 3 - way * VELOCITIES[i][1]
            value = columns(ref[2 * i + far], way * (4 - deep))
            if i in turned(1, way):
                extra = columns(ref[Y_COT], place - turned(1, way).index(i))
                value = jnp.where(column == place, extra, value)
            values.append(value)
        return jnp.where(right, values[1], values[0])

    def codes(s):
        return ref[(Y_CODE1, Y_CODE2, Y_CODE3)[s - 1]]

    def outer(i):
        left, above = ref[2 * i], ref[2 * i + 1]
        if i in turned(1, 1):
            above = columns(ref[Y_POP], -turned(1, 1).index(i))
        if i in turned(1, -1):
            left = columns(ref[Y_POP], 3 - turned(1, -1).index(i))
        return jnp.where(right, above, left)

    def outer_code():
        return jnp.where(right, columns(ref[Y_CODE3], 1), columns(ref[Y_CODE3], 3))

    return population, cotangent, codes, outer, outer_code


def mix_lines(deal, at, pop, cot, deep, way):
    row, lane, column, depth = iotas()
    if way == 1:
        mixed = jnp.where(row >= deep, pop, lines(cot, deep))
    else:
        mixed = jnp.where(row < ROWS - deep, pop, lines(cot, -deep))
    deal.put(way, at, mixed)


def pack_lines(deal, first, population, cotangent):
    row, lane, column, depth = iotas()

    for i in range(Q):
        pop, cot = population(i), cotangent(i)
        for way in (1, -1):
            mix_lines(deal, first + i, pop, cot, 3 - way * VELOCITIES[i][0], way)
    for way in (1, -1):
        extra = None
        for k, i in enumerate(turned(0, -way)):
            value = lines(population(i), k - (3 if way == 1 else 4))
            extra = value if extra is None else jnp.where(row == k, value, extra)
        for k, i in enumerate(turned(0, way)):
            value = lines(cotangent(i), 4 + k - (5 if way == 1 else 2))
            extra = jnp.where(row == 4 + k, value, extra)
        deal.put(way, first + X_EXTRA, extra)


def pack_neighbour(deal, lanes, message_ref, near):
    ring, code13, code2, tiles = x_places(lanes)
    population, cotangent, codes, outer, outer_code = from_y(message_ref, near)
    pack_lines(deal, X_LANE * (lanes - 1), population, cotangent)
    kept = half_lanes(is_right(near))
    for n in range(X_HALVES):
        first, second = (outer(2 * n - 1), outer(2 * n)) if n else (outer(0), outer_code())
        deal.put_both(ring + n, jnp.where(kept, first, pltpu.roll(second, LANES // 2, 1)))
    for way in (1, -1):
        mix_lines(deal, code13 + lanes - 1, codes(1), codes(3), 3, way)
    deal.put_both(tiles - 1, codes(2))


def pack_near(own_ref, cot_ref, field_ref, message_ref, first_ref, second_ref):
    row, lane, column, depth = iotas()
    deal = Deal(is_even("gx"), first_ref, second_ref, layouts()[1])
    ring, code13, code2, tiles = x_places(3)
    for t in range(2):
        pack_lines(
            deal,
            X_LANE * t,
            lambda i: own_ref[2 * i + t],
            lambda i: cot_ref[2 * i + t],
        )
        code = jnp.where(depth == NZ - 1, field_ref[2 * OWN_PHI + t], field_ref[2 + t])
        for way in (1, -1):
            mix_lines(deal, code13 + t, code, field_ref[6 + t], 3, way)
    first, second = field_ref[4], lines(field_ref[5], 4)
    deal.put(1, code2, jnp.where(row >= 4, first, second))
    deal.put(-1, code2, jnp.where(row < 4, first, second))
    pack_neighbour(deal, 3, message_ref, True)
    deal.finish()


def pack_far(message_ref, first_ref, second_ref):
    deal = Deal(is_even("gx"), first_ref, second_ref, layouts()[2])
    pack_neighbour(deal, 1, message_ref, False)
    deal.finish()


def from_x(ref, n, way, lanes):
    row, lane, column, depth = iotas()
    ring, code13, code2, _ = x_places(lanes)
    first = X_LANE * n

    def population(i):
        value = ref[first + i]
        if i in turned(0, -way):
            place = 3 if way == 1 else 4
            extra = lines(ref[first + X_EXTRA], place - turned(0, -way).index(i))
            value = jnp.where(row == place, extra, value)
        return value

    def cotangent(i):
        value = lines(ref[first + i], -way * (3 - way * VELOCITIES[i][0]))
        if i in turned(0, way):
            place = 5 if way == 1 else 2
            extra = lines(ref[first + X_EXTRA], place - 4 - turned(0, way).index(i))
            value = jnp.where(row == place, extra, value)
        return value

    def codes(s):
        if s == 2:
            return lines(ref[code2 + n // 2], 4 * (n % 2))
        value = ref[code13 + n]
        return value if s == 1 else lines(value, -3 * way)

    def outer(i):
        value = ref[ring + (i + 1) // 2]
        return pltpu.roll(value, LANES // 2, 1) if i and i % 2 == 0 else value

    def outer_code():
        return pltpu.roll(ref[ring], LANES // 2, 1)

    return population, cotangent, codes, outer, outer_code


def sides(first_ref, second_ref, axis, layout):
    even = is_even(axis)
    picks = Pick(even, second_ref, first_ref), Pick(even, first_ref, second_ref)
    return [Unpacking(pick, layout) for pick in picks]


def own_rows(step=0):
    return pl.ds(ROWS + step, ROWS)


def halo_rows(step=0):
    return pl.ds({0: 2 * ROWS, -1: 2 * ROWS - 1, 1: 1}[step], ROWS)


def put_halo(ref, at, halo):
    ref[at, pl.ds(0, ROWS), :] = halo
    ref[at, halo_rows(), :] = halo


def put_ring(ref, at, own, halo):
    ref[at, own_rows(), :] = own
    put_halo(ref, at, halo)


def expand(code):
    row, lane, column, depth = iotas()
    top = depth == NZ - 1
    phi = jnp.where(top, code, 0.0)
    for step in (1, 2, 4, 8, 16):
        phi = phi + pltpu.roll(phi, LANES - step, 1)
    return jnp.where(top, 0.0, code), phi


def lay_own(c, population, cotangent, codes, code_phi, pop, cot, wide, field):
    for i in range(Q):
        pop[5 * i + c, pl.ds(2 * ROWS, ROWS), :] = population(i)
        if cotangent is not None:
            cot[4 * i + c - 1, own_rows(), :] = cotangent(i)
    for n in range(2):
        wide[n, c, 1] = code_phi[n]
    if cotangent is not None:
        field[0, c - 1, 0], field[1, c - 1, 0] = code_phi[1], code_phi[0]
        for s in (2, 3):
            field[s, c - 1, 0] = codes(s)


def lay_halo(c, below, above, pop, cot, wide, field):
    row, lane, column, depth = iotas()
    before, behind = expand(below[2](1)), expand(above[2](1))
    for n in range(2):
        wide[n, c, 0], wide[n, c, 2] = before[n], behind[n]
    for i in range(Q):
        pop[5 * i + c, pl.ds(ROWS, ROWS), :] = below[0](i)
        pop[5 * i + c, pl.ds(3 * ROWS, ROWS), :] = above[0](i)
        if below[1] is not None:
            put_halo(cot, 4 * i + c - 1, jnp.where(row < 4, above[1](i), below[1](i)))
    if below[1] is not None:
        for n, place in ((0, 1), (1, 0)):
            field[place, c - 1, 1] = jnp.where(row < 4, behind[n], before[n])
        for s in (2, 3):
            field[s, c - 1, 1] = jnp.where(row < 4, above[2](s), below[2](s))


def near_tile():
    return jnp.where(is_right(True), 4, 1)


def lay_out(
    near_y_ref,
    far_y_ref,
    first_near_ref,
    second_near_ref,
    own_ref,
    field_ref,
    cot_ref,
    pop,
    cot,
    wide,
    field,
):
    spaces = pop, cot, wide, field
    below, above = sides(first_near_ref, second_near_ref, "gx", layouts()[1])
    for t in range(2):
        lay_own(
            2 + t,
            lambda i: own_ref[2 * i + t],
            lambda i: cot_ref[2 * i + t],
            lambda s: field_ref[2 * s + t],
            (field_ref[2 + t], field_ref[2 * OWN_PHI + t]),
            *spaces,
        )
        lay_halo(2 + t, from_x(below, t, 1, 3), from_x(above, t, -1, 3), *spaces)
    near, far = from_y(near_y_ref, True), from_y(far_y_ref, False)
    for c, (population, cotangent, codes, _, _) in ((near_tile(), near), (5 - near_tile(), far)):
        lay_own(c, population, cotangent, codes, expand(codes(1)), *spaces)
    kept = half_lanes(is_right(True))
    lay_own(
        0,
        lambda i: jnp.where(kept, near[3](i), far[3](i)),
        None,
        None,
        expand(jnp.where(kept, near[4](), far[4]())),
        *spaces,
    )
    lay_halo(near_tile(), from_x(below, 2, 1, 3), from_x(above, 2, -1, 3), *spaces)


def lay_far(near_refs, far_refs, spaces):
    nears, fars = (
        [
            from_x(ref, lanes - 1, way, lanes)
            for ref, way in zip(sides(*refs, "gx", layout), (1, -1))
        ]
        for refs, layout, lanes in zip((near_refs, far_refs), layouts()[1:], (3, 1))
    )
    lay_halo(5 - near_tile(), *fars, *spaces)
    kept = half_lanes(is_right(True))
    ring = [
        (
            lambda i, near=near, far=far: jnp.where(kept, near[3](i), far[3](i)),
            None,
            lambda s, near=near, far=far: jnp.where(kept, near[4](), far[4]()),
        )
        for near, far in zip(nears, fars)
    ]
    lay_halo(0, *ring, *spaces)


def steps_kernel(
    sizes,
    state_ref,
    own_field_ref,
    names_ref,
    first_near_ref,
    second_near_ref,
    first_far_ref,
    second_far_ref,
    *refs,
):
    adjoint_ref, panel_ref, pop_a, ring_a, wide, field, pop_b, ring_b, saved, mom, grad = refs[4:]
    size_x, size_y = sizes
    lay_far(
        (first_near_ref, second_near_ref),
        (first_far_ref, second_far_ref),
        (pop_a, ring_a, wide, field),
    )

    at_x, at_y = lax.axis_index("gx"), lax.axis_index("gy")
    edges = (
        jnp.where(at_x == 0, 1, 0),
        jnp.where(at_x == size_x - 1, 1, 0),
        jnp.where(at_y == 0, 1, 0),
        jnp.where(at_y == size_y - 1, 1, 0),
    )
    row, lane, column, depth = iotas()
    after = row < 4

    def masks_of(tile, first, r):
        return wall_masks(r == 0, tile == first, tile == first + 1, edges)

    def neighbours(tile, tiles):
        if isinstance(tile, int):
            return {0: tile, -1: (tile - 1) % tiles, 1: (tile + 1) % tiles}
        return {0: tile, -1: lax.rem(tile + tiles - 1, tiles), 1: lax.rem(tile + 1, tiles)}

    def from_wide(ref, tile, r):
        step = neighbours(tile, 5)

        def load(i, tile_step, row_step, move):
            at = 5 * i + step[tile_step]
            before, own, behind = (ref[at, pl.ds(ROWS * n + row_step, ROWS), :] for n in (1, 2, 3))
            return (own, jnp.where(after, behind, before), before, behind)[r]

        return load

    def from_ring(ref, tile, tiles, r):
        step = neighbours(tile, tiles)

        def load(i, tile_step, row_step, move):
            rows = own_rows(row_step) if r == 0 else halo_rows(row_step)
            return ref[tiles * i + step[tile_step], rows, :]

        return load

    def from_outer(ref, r):
        def load(i, tile_step, row_step, move):
            rows = own_rows(row_step) if r == 0 else halo_rows(row_step)
            if tile_step:
                return ref[4 * i + (2 if tile_step < 0 else 1), rows, :]
            cut = {0: 2, 1: 1, -1: 3}[move]
            return jnp.where(column < cut, ref[4 * i + 3, rows, :], ref[4 * i, rows, :])

        return load

    def note(s, tile, r, parts):
        for n, value in enumerate(parts[2:4] + tuple(parts[4])):
            mom[s - 1, n, tile, r] = value

    def first_step(tile, carry):
        place = lax.rem(tile + 4, 5)
        halo = []
        for r in (2, 0, 3):
            f = stream_tile(from_wide(pop_a, tile, r), 1, masks_of(tile, 2, r), lane)
            parts = moments(f)
            if r == 0:
                note(1, place, 0, parts)
                for i in range(Q):
                    saved[0, i, place] = f[i]
            else:
                halo.append(parts[2:4] + tuple(parts[4]))
            at = {2: 0, 0: 1, 3: 2}[r]
            g = collide(f, wide[0, tile, at], wide[1, tile, at], parts)
            for i in range(Q):
                pop_b[5 * i + tile, pl.ds(ROWS * (at + 1), ROWS), :] = g[i]
        for n in range(5):
            mom[0, n, place, 1] = jnp.where(after, halo[1][n], halo[0][n])
        return carry

    lax.fori_loop(0, 5, first_step, 0)

    def second_step(tile, carry):
        out = []
        for r in range(2):
            f = stream_tile(from_wide(pop_b, tile + 1, r), 1, masks_of(tile, 1, r), lane)
            parts = moments(f)
            note(2, tile, r, parts)
            if r == 0:
                for i in range(Q):
                    saved[1, i, tile] = f[i]
            out.append(collide(f, field[2, tile, r], field[0, tile, r], parts))
        for i in range(Q):
            put_ring(ring_b, 4 * i + tile, out[0][i], out[1][i])
        return carry

    lax.fori_loop(0, 4, second_step, 0)

    def third_step(tile, carry):
        for r in range(2):
            f = stream_tile(from_ring(ring_b, tile, 4, r), 1, masks_of(tile, 1, r), lane)
            note(3, tile, r, moments(f))
            if r == 0:
                for i in range(Q):
                    saved[2, i, tile] = f[i]
        return carry

    lax.fori_loop(0, 4, third_step, 0)

    def back_tile(load, s, tile, r, own):
        b = stream_tile(load, -1, masks_of(4 if tile is None else tile, 1, r), lane)

        def read(get):
            return jnp.where(column < 2, get(3), get(0)) if tile is None else get(tile)

        rho, rinv, *u = [read(lambda at: mom[s - 1, n, at, r]) for n in range(5)]
        kind, phi = read(lambda at: field[s, at, r]), read(lambda at: field[0, at, r])
        state = [saved[s - 1, i, tile] for i in range(Q)] if own else None
        back, term = collide_back(b, kind, phi, rho, rinv, u, state)
        if own:
            grad[tile] = term if s == 3 else grad[tile] + term
        return back

    def last_step(tile, carry):
        out = [back_tile(from_ring(ring_a, tile, 4, r), 3, tile, r, r == 0) for r in range(2)]
        for i in range(Q):
            put_ring(ring_b, 4 * i + tile, out[0][i], out[1][i])
        return carry

    lax.fori_loop(0, 4, last_step, 0)

    for k, tile in enumerate((1, 2, None)):
        out = []
        for r in range(2):
            load = from_outer(ring_b, r) if tile is None else from_ring(ring_b, tile, 4, r)
            out.append(back_tile(load, 2, tile, r, r == 0 and tile is not None))
        for i in range(Q):
            put_ring(ring_a, 3 * i + k, out[0][i], out[1][i])

    for k, tile in enumerate((1, 2, None)):
        out = []
        for r in range(2):
            load = from_ring(ring_a, k, 3, r)
            out.append(back_tile(load, 1, tile, r, r == 0 and tile is not None))
        for i in range(Q):
            put_ring(ring_b, 3 * i + k, out[0][i], out[1][i])

    panel = lax.broadcasted_iota(jnp.int32, panel_ref.shape, 1)
    sums = jnp.zeros(panel_ref.shape, jnp.float32)
    for t in range(2):
        b = stream_tile(from_ring(ring_b, t, 3, 0), -1, masks_of(t, 0, 0), lane)
        f = [state_ref[2 * i + t] for i in range(Q)]
        kind, phi = own_field_ref[t], own_field_ref[2 * OWN_PHI + t]
        _, _, rho, rinv, u = moments(f)
        back, term = collide_back(b, kind, phi, rho, rinv, u, f)
        for i in range(Q):
            adjoint_ref[i, :, pl.ds(t * LANES, LANES)] = back[i]
        term = term + grad[t + 1]
        for part in range(2):
            amount = jnp.sum(jnp.where((row < 4) == (part == 0), term, 0.0))
            name = names_ref[t, 4 * part : 4 * part + 1, 0:1]
            sums = sums + jnp.where(panel == name, amount, 0.0)
    panel_ref[...] = sums


def finish(parts_ref, adjoint_ref, sums_hbm, adjoint_hbm, sums_ref, sems):
    adjoint_copy = pltpu.make_async_copy(adjoint_ref, adjoint_hbm, sems.at[0])
    adjoint_copy.start()
    sums_ref[...] = jnp.sum(parts_ref[...], axis=0)
    sums_copy = pltpu.make_async_copy(sums_ref, sums_hbm, sems.at[1])
    sums_copy.start()
    sums_copy.wait()
    adjoint_copy.wait()


VMEM = pl.BlockSpec(memory_space=pltpu.VMEM)
HBM = pl.BlockSpec(memory_space=pltpu.HBM)


def shape_of(*dims):
    return jax.ShapeDtypeStruct(dims, jnp.float32)


def tiles_of(count):
    return shape_of(count, ROWS, LANES)


def on_device(sizes, checkpoint, cotangent, cell_codes, porosity, baffle_index):
    size_x, size_y = sizes
    panels = porosity.shape[0]
    devices = size_x * size_y
    y_layout, near_layout, far_layout = layouts()

    params = pltpu.CompilerParams(vmem_limit_bytes=32 * 1024 * 1024)

    def call(kernel, out_shape, in_specs, scratch=(), name=None, aliases={}):
        return pl.pallas_call(
            kernel,
            out_shape=out_shape,
            in_specs=in_specs,
            out_specs=jax.tree.map(lambda _: VMEM, out_shape),
            scratch_shapes=scratch,
            input_output_aliases=aliases,
            compiler_params=params,
            name=name,
        )

    def swap(value, axis, size):
        return lax.ppermute(value, axis, [(i, i ^ 1) for i in range(size) if i ^ 1 < size])

    def swap_between(value, axis, size):
        pairs = [(i, i + 1) for i in range(1, size - 1, 2)]
        return lax.ppermute(value, axis, pairs + [(j, i) for i, j in pairs])

    def swap_inner(value, start):
        pairs = [
            (i * size_y + y, (i + 1) * size_y + y)
            for i in range(start, size_x - 1, 2)
            for y in range(1, size_y - 1)
        ]
        return lax.ppermute(value, ("gx", "gy"), pairs + [(j, i) for i, j in pairs])

    arguments = [
        pltpu.with_memory_space_constraint(value, pltpu.HBM)
        for value in (checkpoint, cotangent, cell_codes, baffle_index, porosity)
    ]
    near_y, far_y, own, state, cot, field, names = call(
        pack_own,
        (tiles_of(y_layout.size),) * 2
        + (tiles_of(2 * Q),) * 3
        + (tiles_of(2 * OWN_PHI + 2), jax.ShapeDtypeStruct((2, ROWS, LANES), jnp.int32)),
        [HBM] * 5,
        [
            pltpu.VMEM((Q, ROWS, 2 * LANES), jnp.float32),
            pltpu.VMEM((Q, ROWS, 2 * LANES), jnp.float32),
            pltpu.VMEM((STEPS, ROWS, 2 * LANES), jnp.int32),
            pltpu.SMEM(baffle_index.shape, jnp.int32),
            pltpu.SMEM(porosity.shape, jnp.float32),
            pltpu.SemaphoreType.DMA((5,)),
        ],
        name="pack_own",
    )(*arguments)
    near_y = swap(near_y, "gy", size_y)
    far_y = swap_between(far_y, "gy", size_y)
    first_near, second_near = call(
        pack_near,
        (tiles_of(near_layout.size), tiles_of(near_layout.size + 1)),
        [VMEM] * 4,
        name="pack_near",
    )(own, cot, field, near_y)
    second_near = swap_between(second_near, "gx", size_x)
    first_near = swap(first_near, "gx", size_x)
    first_far, second_far = call(
        pack_far,
        (tiles_of(far_layout.size), tiles_of(far_layout.size + 1)),
        [VMEM],
        name="pack_far",
    )(far_y)
    second_far = swap_inner(second_far, 1)
    first_far = swap_inner(first_far, 0)
    spaces = (
        shape_of(5 * Q, 5 * ROWS, LANES),
        shape_of(4 * Q, 3 * ROWS, LANES),
        shape_of(2, 5, 3, ROWS, LANES),
        shape_of(4, 4, 2, ROWS, LANES),
    )
    laid = call(lay_out, spaces, [VMEM] * 7, name="lay_out")(
        near_y, far_y, first_near, second_near, own, field, cot
    )
    adjoint, sums, *_ = call(
        functools.partial(steps_kernel, sizes),
        (pltpu.VMEM((Q, ROWS, 2 * LANES), jnp.float32), shape_of(devices, panels)) + spaces,
        [VMEM] * 11,
        [
            pltpu.VMEM((5 * Q, 5 * ROWS, LANES), jnp.float32),
            pltpu.VMEM((4 * Q, 3 * ROWS, LANES), jnp.float32),
            pltpu.VMEM((3, Q, 5, ROWS, LANES), jnp.float32),
            pltpu.VMEM((3, 5, 5, 2, ROWS, LANES), jnp.float32),
            pltpu.VMEM((4, ROWS, LANES), jnp.float32),
        ],
        name="steps",
        aliases={7 + n: 2 + n for n in range(4)},
    )(state, field, names, first_near, second_near, first_far, second_far, *laid)
    gathered = lax.all_to_all(sums, ("gx", "gy"), 0, 0, tiled=True)
    totals, adjoint = pl.pallas_call(
        finish,
        out_shape=(shape_of(1, panels), shape_of(Q, ROWS, 2 * LANES)),
        in_specs=[VMEM, VMEM],
        out_specs=(HBM, HBM),
        scratch_shapes=[pltpu.VMEM((1, panels), jnp.float32), pltpu.SemaphoreType.DMA((2,))],
        compiler_params=params,
        name="finish",
    )(gathered.reshape(devices, 1, panels), adjoint)
    return adjoint, totals.reshape(panels)


def solution(mesh):
    sizes = (mesh.shape["gx"], mesh.shape["gy"])
    in_specs = (P(None, "gx", "gy"), P(None, "gx", "gy"), P(None, "gx", "gy"), P(), P("gx", "gy"))
    out_specs = (P(None, "gx", "gy"), P())
    return jax.shard_map(
        functools.partial(on_device, sizes),
        mesh=mesh,
        in_specs=in_specs,
        out_specs=out_specs,
        check_vma=False,
    )
```

```python
import functools

import jax
import jax.numpy as jnp
import numpy as np
from jax import lax
from jax.experimental import pallas as pl
from jax.experimental.pallas import tpu as pltpu
from jax.sharding import PartitionSpec as P

Q = 19
STEPS = 4
NZ = 32
ROWS = 8
LANES = 128
OMEGA = 1.6
ACCEL = (0.002, 0.0, -0.003)
SHIFT = tuple(a / OMEGA for a in ACCEL)

VELOCITIES = [
    (0, 0, 0),
    (1, 0, 0),
    (-1, 0, 0),
    (0, 1, 0),
    (0, -1, 0),
    (0, 0, 1),
    (0, 0, -1),
    (1, 1, 0),
    (-1, -1, 0),
    (1, -1, 0),
    (-1, 1, 0),
    (1, 0, 1),
    (-1, 0, -1),
    (1, 0, -1),
    (-1, 0, 1),
    (0, 1, 1),
    (0, -1, -1),
    (0, 1, -1),
    (0, -1, 1),
]
OPPOSITE = [0, 2, 1, 4, 3, 6, 5, 8, 7, 10, 9, 12, 11, 14, 13, 16, 15, 18, 17]
PAIRS = [(i, i + 1) for i in range(1, Q, 2)]
W_REST, W_AXIS, W_DIAG = 1.0 / 3.0, 1.0 / 18.0, 1.0 / 36.0

Y_CODE1, Y_CODE2, Y_CODE3, Y_POP, Y_COT = 38, 39, 40, 41, 42
Y_TILES = 43
X_EXTRA = 19
X_LANE = 20
X_HALVES = 10


def x_places(lanes):
    ring = X_LANE * lanes
    code13 = ring + X_HALVES
    code2 = code13 + lanes
    return ring, code13, code2, code2 + (lanes + 1) // 2


EMPTY = 25
FREE = NZ - EMPTY
WEIGHTS = [W_REST] + [W_AXIS] * 6 + [W_DIAG] * 12
LEVEL = [i for i, v in enumerate(VELOCITIES) if v[2] < 1]
OWN_PHI = 4


def turned(axis, outward):
    return [i for i, v in enumerate(VELOCITIES) if v[axis] == outward and sum(map(abs, v)) == 2]


def total(values):
    values = list(values)
    while len(values) > 1:
        values = [a + b for a, b in zip(values[::2], values[1::2])] + (
            [values[-1]] if len(values) % 2 else []
        )
    return values[0]


def along(vector, three):
    terms = None
    for c, value in zip(vector, three):
        if c == 0:
            continue
        if terms is None:
            terms = value if c > 0 else -value
        else:
            terms = terms + value if c > 0 else terms - value
    return terms


def moments(f):
    plus = {i: f[i] + f[o] for i, o in PAIRS}
    minus = {i: f[i] - f[o] for i, o in PAIRS}
    rho = total([f[0]] + [plus[i] for i, _ in PAIRS])
    rinv = 1.0 / rho
    u = []
    for axis in range(3):
        terms = [
            minus[i] if VELOCITIES[i][axis] > 0 else -minus[i]
            for i, _ in PAIRS
            if VELOCITIES[i][axis] != 0
        ]
        u.append(total(terms) * rinv + SHIFT[axis])
    return plus, minus, rho, rinv, u


def coefficients(kind, phi, rinv):
    baffle = kind == 3.0
    gas = kind == 0.0
    even = jnp.where(gas, 0.0, jnp.where(baffle, 0.5 - 0.5 * OMEGA * phi, 0.5 * (1.0 - OMEGA)))
    odd = jnp.where(
        gas, 0.0, jnp.where(baffle, (1.0 - 0.5 * OMEGA) * phi - 0.5, 0.5 * (1.0 - OMEGA))
    )
    slope = jnp.where(
        baffle,
        OMEGA * phi,
        jnp.where(kind == 1.0, OMEGA, jnp.where(kind == 2.0, OMEGA * rinv, 0.0)),
    )
    return even, odd, slope


def collide(f, kind, phi, parts):
    plus, minus, rho, rinv, u = parts
    even, odd, slope = coefficients(kind, phi, rinv)
    scale = slope * rho
    rest = 1.0 - 1.5 * (u[0] * u[0] + u[1] * u[1] + u[2] * u[2])
    base = scale * rest + jnp.where(kind == 0.0, 1.0, 0.0)
    out = [None] * Q
    out[0] = 2.0 * even * f[0] + W_REST * base
    for weight, pairs in ((W_AXIS, PAIRS[:3]), (W_DIAG, PAIRS[3:])):
        flat = weight * base
        three = (3.0 * weight) * scale
        for i, o in pairs:
            cu = along(VELOCITIES[i], u)
            lin = three * cu
            ev = even * plus[i] + (flat + 1.5 * lin * cu)
            od = odd * minus[i] + lin
            out[i] = ev + od
            out[o] = ev - od
    return out


def collide_back(b, kind, phi, rho, rinv, u, state=None):
    even, odd, slope = coefficients(kind, phi, rinv)
    plus = {i: b[i] + b[o] for i, o in PAIRS}
    minus = {i: b[i] - b[o] for i, o in PAIRS}
    rest = 1.0 - 1.5 * (u[0] * u[0] + u[1] * u[1] + u[2] * u[2])
    u_half = [1.5 * c for c in u]
    weighted = W_REST * b[0]
    energy = 0.0
    vector = [0.0, 0.0, 0.0]
    for weight, pairs in ((W_AXIS, PAIRS[:3]), (W_DIAG, PAIRS[3:])):
        weighted = weighted + weight * total([plus[i] for i, _ in pairs])
        energies, parts = [], ([], [], [])
        for i, _ in pairs:
            cu = along(VELOCITIES[i], u)
            half = along(VELOCITIES[i], u_half) * plus[i]
            first = minus[i] + half
            energies.append(cu * first)
            second = first + half
            for axis in range(3):
                c = VELOCITIES[i][axis]
                if c:
                    parts[axis].append(second if c > 0 else -second)
        energy = energy + (3.0 * weight) * total(energies)
        vector = [vector[k] + (3.0 * weight) * total(parts[k]) for k in range(3)]
    energy = energy + rest * weighted
    vector = [vector[k] - (3.0 * weighted) * u[k] for k in range(3)]
    push = [slope * v for v in vector]
    inner = total([push[k] * (u[k] - SHIFT[k]) for k in range(3)])
    shared = jnp.where(kind == 2.0, 0.0, slope) * energy - inner
    out = [None] * Q
    out[0] = 2.0 * even * b[0] + shared
    for i, o in PAIRS:
        ev = even * plus[i] + shared
        od = odd * minus[i] + along(VELOCITIES[i], push)
        out[i] = ev + od
        out[o] = ev - od
    if state is None:
        return out, None
    evens = total([plus[i] * (state[i] + state[o]) for i, o in PAIRS])
    odds = total([minus[i] * (state[i] - state[o]) for i, o in PAIRS])
    term = (
        -OMEGA * (b[0] * state[0] + 0.5 * evens)
        + (1.0 - 0.5 * OMEGA) * odds
        + OMEGA * rho * energy
    )
    return out, jnp.where(kind == 3.0, term, 0.0)


def wall_masks(sign_rows, own_low, own_high, edges):
    lane = lax.broadcasted_iota(jnp.int32, (ROWS, LANES), 1)
    row = lax.broadcasted_iota(jnp.int32, (ROWS, LANES), 0)
    x_low, x_high, y_low, y_high = edges
    depth = lane % NZ
    masks = {}
    masks[2, 1] = depth == 0
    masks[2, -1] = depth == NZ - 1
    masks[1, 1] = lane < jnp.where(own_low, y_low * NZ, 0)
    masks[1, -1] = lane >= jnp.where(own_high, LANES - y_high * NZ, LANES)
    if sign_rows:
        masks[0, 1] = row < x_low
        masks[0, -1] = row >= ROWS - x_high
    return masks


def stream_tile(load, sign, masks, lane):
    cross_low, cross_high = lane >= LANES - NZ, lane < NZ
    combined = {}
    out = []
    for i, vector in enumerate(VELOCITIES):
        v = tuple(sign * c for c in vector)
        value = load(i, 0, -v[0], v[1])
        if v[1] == 1:
            value = jnp.where(cross_low, load(i, -1, -v[0], 1), value)
        elif v[1] == -1:
            value = jnp.where(cross_high, load(i, 1, -v[0], -1), value)
        amount = (v[1] * NZ + v[2]) % LANES
        if amount:
            value = pltpu.roll(value, amount, 1)
        outside = None
        if v not in combined:
            for axis in range(3):
                if v[axis] and (axis, v[axis]) in masks:
                    wall = masks[axis, v[axis]]
                    outside = wall if outside is None else outside | wall
            combined[v] = outside
        outside = combined[v]
        if outside is not None:
            value = jnp.where(outside, load(OPPOSITE[i], 0, 0, 0), value)
        out.append(value)
    return out


def iotas():
    row = lax.broadcasted_iota(jnp.int32, (ROWS, LANES), 0)
    lane = lax.broadcasted_iota(jnp.int32, (ROWS, LANES), 1)
    return row, lane, lane // NZ, lane % NZ


def columns(value, count):
    amount = (count * NZ) % LANES
    return pltpu.roll(value, amount, 1) if amount else value


def lines(value, count):
    amount = count % ROWS
    return pltpu.roll(value, amount, 0) if amount else value


class Layout:
    def __init__(self, count, guests, fills):
        self.fills = fills
        hosts = [at for at in fills if at not in guests]
        self.hosts = {at: hosts[4 * n : 4 * n + 4] for n, at in enumerate(guests)}
        self.guests = guests
        kept = [at for at in range(count) if at not in guests]
        self.place = {at: n for n, at in enumerate(kept)}
        self.size = len(kept)


class Packing:
    def __init__(self, ref, layout):
        self.ref, self.layout, self.held = ref, layout, {}

    def __setitem__(self, at, value):
        if at in self.layout.guests:
            self.held[at] = value
        else:
            self.ref[self.layout.place[at]] = value

    def finish(self):
        row, lane, column, depth = iotas()
        spare = depth >= EMPTY
        for at, value in self.held.items():
            for k, host in enumerate(self.layout.hosts[at]):
                place = self.layout.place[host]
                moved = pltpu.roll(value, EMPTY - FREE * k, 1)
                self.ref[place] = jnp.where(spare, moved, self.ref[place])
        for place in range(self.layout.size, self.ref.shape[0]):
            self.ref[place] = jnp.zeros((ROWS, LANES), jnp.float32)


class Unpacking:
    def __init__(self, source, layout):
        self.source, self.layout, self.cache = source, layout, {}
        self.changed = set(layout.guests).union(*layout.hosts.values())

    def __getitem__(self, at):
        if at not in self.cache:
            self.cache[at] = self.read(at)
        return self.cache[at]

    def read(self, at):
        row, lane, column, depth = iotas()
        layout = self.layout
        if at in layout.guests:
            value = None
            for k, host in enumerate(layout.hosts[at]):
                tile = self.source[layout.place[host]]
                moved = pltpu.roll(tile, LANES - (EMPTY - FREE * k), 1)
                value = moved if value is None else jnp.where(depth >= FREE * k, moved, value)
        else:
            value = self.source[layout.place[at]]
        if at in self.changed:
            value = jnp.where(depth >= EMPTY, layout.fills[at], value)
        return value


def layouts():
    y_fills = {2 * i + t: WEIGHTS[i] for i in LEVEL for t in range(2)}
    y_fills.update({Y_POP: W_DIAG, Y_CODE2: 0.0})
    out = [Layout(Y_TILES, [2 * i for i in LEVEL[:6]], y_fills)]
    for lanes, count in ((3, 10), (1, 4)):
        ring, _, code2, tiles = x_places(lanes)
        fills = {ring + n: WEIGHTS[2 * n] for n in range(1, X_HALVES)}
        fills.update({at: 0.0 for at in range(code2, tiles)})
        fills.update({X_LANE * n + i: WEIGHTS[i] for n in range(lanes) for i in LEVEL})
        guests = [X_LANE * (lanes - 1) + i for i in LEVEL[:count]]
        out.append(Layout(tiles, guests, fills))
    return out


class Pick:
    def __init__(self, flag, first, second):
        self.flag, self.first, self.second = flag, first, second

    def __getitem__(self, at):
        return jnp.where(self.flag, self.first[at], self.second[at])


class Deal:
    def __init__(self, even, first, second, layout, skip=0):
        self.even, self.skip, self.held = even, skip, {}
        self.first, self.second = Packing(first, layout), Packing(second, layout)

    def put(self, way, at, value):
        if (-way, at) not in self.held:
            self.held[way, at] = value
            return
        other = self.held.pop((-way, at))
        up, down = (value, other) if way == 1 else (other, value)
        self.first[at - self.skip] = jnp.where(self.even, up, down)
        self.second[at - self.skip] = jnp.where(self.even, down, up)

    def put_both(self, at, value):
        self.first[at - self.skip] = value
        self.second[at - self.skip] = value

    def finish(self):
        self.first.finish()
        self.second.finish()


def is_even(axis):
    return lax.rem(lax.axis_index(axis), 2) == 0


def pack_own(
    f_hbm,
    cot_hbm,
    codes_hbm,
    panels_hbm,
    porosity_hbm,
    first_ref,
    second_ref,
    own_ref,
    state_ref,
    own_cot_ref,
    field_ref,
    names_ref,
    f_ref,
    cot_ref,
    codes_ref,
    panels_ref,
    porosity_ref,
    sems,
):
    pieces = (
        (panels_hbm, panels_ref),
        (porosity_hbm, porosity_ref),
        (f_hbm, f_ref),
        (codes_hbm, codes_ref),
        (cot_hbm, cot_ref),
    )
    copies = [
        pltpu.make_async_copy(source, target, sems.at[n])
        for n, (source, target) in enumerate(pieces)
    ]
    for copy in copies:
        copy.start()
    for copy in copies[:4]:
        copy.wait()
    deal = Deal(is_even("gy"), first_ref, second_ref, layouts()[0])
    row, lane, column, depth = iotas()
    top = depth == NZ - 1

    def tile_of(ref, i, t):
        return ref[i, :, pl.ds(t * LANES, LANES)]

    codes, phis = [], []
    for t in range(2):
        names = panels_ref[0, t * LANES], panels_ref[4, t * LANES]
        phi = jnp.where(row < 4, porosity_ref[names[0]], porosity_ref[names[1]])
        names_ref[t] = jnp.where(row < 4, names[0], names[1])
        kinds = [tile_of(codes_ref, s, t).astype(jnp.float32) for s in range(STEPS)]
        f = [tile_of(f_ref, i, t) for i in range(Q)]
        g = collide(f, kinds[0], phi, moments(f))
        for i in range(Q):
            own_ref[2 * i + t] = g[i]
            state_ref[2 * i + t] = f[i]
        for s in range(STEPS):
            field_ref[2 * s + t] = kinds[s]
        field_ref[2 * OWN_PHI + t] = phi
        codes.append([jnp.where(top, phi, kinds[1]), kinds[2], kinds[3]])
    copies[4].wait()
    for i in range(Q):
        for way in (1, -1):
            near, far = (1, 0) if way == 1 else (0, 1)
            deep = 3 - way * VELOCITIES[i][1]
            cot = tile_of(cot_ref, i, near)
            g_far = own_ref[2 * i + far]
            if way == 1:
                mixed = jnp.where(column >= deep, g_far, columns(cot, deep - 4))
            else:
                mixed = jnp.where(column < 4 - deep, g_far, columns(cot, 4 - deep))
            deal.put(way, 2 * i, mixed if far == 0 else own_ref[2 * i])
            deal.put(way, 2 * i + 1, mixed if far == 1 else own_ref[2 * i + 1])
    for way in (1, -1):
        near, far = (1, 0) if way == 1 else (0, 1)
        outer = 3 if way == 1 else 0
        deal.put(way, Y_CODE1, codes[near][0])
        deal.put(way, Y_CODE2, codes[near][1])
        outside = columns(codes[far][0], 3 - 2 * outer)
        deal.put(way, Y_CODE3, jnp.where(column == 3 - outer, outside, codes[near][2]))
        extra = None
        for k, i in enumerate(turned(1, -way)):
            value = columns(own_ref[2 * i + far], k - outer)
            extra = value if extra is None else jnp.where(column == k, value, extra)
        deal.put(way, Y_POP, extra)
        extra = None
        for k, i in enumerate(turned(1, way)):
            value = columns(tile_of(cot_ref, i, near), k - (1 if way == 1 else 2))
            extra = value if extra is None else jnp.where(column == k, value, extra)
        deal.put(way, Y_COT, extra)
    deal.finish()
    for t in range(2):
        for i in range(Q):
            own_cot_ref[2 * i + t] = tile_of(cot_ref, i, t)


def is_right(near):
    return is_even("gy") if near else jnp.logical_not(is_even("gy"))


def half_lanes(right):
    row, lane, column, depth = iotas()
    return lane // (LANES // 2) == jnp.where(right, 0, 1)


def from_y(message_ref, near):
    row, lane, column, depth = iotas()
    ref = Unpacking(message_ref, layouts()[0])
    right = is_right(near)

    def population(i):
        return jnp.where(right, ref[2 * i], ref[2 * i + 1])

    def cotangent(i):
        values = []
        for way, place, far in ((1, 1, 0), (-1, 2, 1)):
            deep = 3 - way * VELOCITIES[i][1]
            value = columns(ref[2 * i + far], way * (4 - deep))
            if i in turned(1, way):
                extra = columns(ref[Y_COT], place - turned(1, way).index(i))
                value = jnp.where(column == place, extra, value)
            values.append(value)
        return jnp.where(right, values[1], values[0])

    def codes(s):
        return ref[(Y_CODE1, Y_CODE2, Y_CODE3)[s - 1]]

    def outer(i):
        left, above = ref[2 * i], ref[2 * i + 1]
        if i in turned(1, 1):
            above = columns(ref[Y_POP], -turned(1, 1).index(i))
        if i in turned(1, -1):
            left = columns(ref[Y_POP], 3 - turned(1, -1).index(i))
        return jnp.where(right, above, left)

    def outer_code():
        return jnp.where(right, columns(ref[Y_CODE3], 1), columns(ref[Y_CODE3], 3))

    return population, cotangent, codes, outer, outer_code


def mix_lines(deal, at, pop, cot, deep, way):
    row, lane, column, depth = iotas()
    if way == 1:
        mixed = jnp.where(row >= deep, pop, lines(cot, deep))
    else:
        mixed = jnp.where(row < ROWS - deep, pop, lines(cot, -deep))
    deal.put(way, at, mixed)


def pack_lines(deal, first, population, cotangent):
    row, lane, column, depth = iotas()

    for i in range(Q):
        pop, cot = population(i), cotangent(i)
        for way in (1, -1):
            mix_lines(deal, first + i, pop, cot, 3 - way * VELOCITIES[i][0], way)
    for way in (1, -1):
        extra = None
        for k, i in enumerate(turned(0, -way)):
            value = lines(population(i), k - (3 if way == 1 else 4))
            extra = value if extra is None else jnp.where(row == k, value, extra)
        for k, i in enumerate(turned(0, way)):
            value = lines(cotangent(i), 4 + k - (5 if way == 1 else 2))
            extra = jnp.where(row == 4 + k, value, extra)
        deal.put(way, first + X_EXTRA, extra)


def pack_neighbour(deal, lanes, message_ref, near):
    ring, code13, code2, tiles = x_places(lanes)
    population, cotangent, codes, outer, outer_code = from_y(message_ref, near)
    pack_lines(deal, X_LANE * (lanes - 1), population, cotangent)
    kept = half_lanes(is_right(near))
    for n in range(X_HALVES):
        first, second = (outer(2 * n - 1), outer(2 * n)) if n else (outer(0), outer_code())
        deal.put_both(ring + n, jnp.where(kept, first, pltpu.roll(second, LANES // 2, 1)))
    for way in (1, -1):
        mix_lines(deal, code13 + lanes - 1, codes(1), codes(3), 3, way)
    deal.put_both(tiles - 1, codes(2))


def pack_near(own_ref, cot_ref, field_ref, message_ref, first_ref, second_ref):
    row, lane, column, depth = iotas()
    deal = Deal(is_even("gx"), first_ref, second_ref, layouts()[1])
    ring, code13, code2, tiles = x_places(3)
    for t in range(2):
        pack_lines(
            deal,
            X_LANE * t,
            lambda i: own_ref[2 * i + t],
            lambda i: cot_ref[2 * i + t],
        )
        code = jnp.where(depth == NZ - 1, field_ref[2 * OWN_PHI + t], field_ref[2 + t])
        for way in (1, -1):
            mix_lines(deal, code13 + t, code, field_ref[6 + t], 3, way)
    first, second = field_ref[4], lines(field_ref[5], 4)
    deal.put(1, code2, jnp.where(row >= 4, first, second))
    deal.put(-1, code2, jnp.where(row < 4, first, second))
    pack_neighbour(deal, 3, message_ref, True)
    deal.finish()


def pack_far(message_ref, first_ref, second_ref):
    deal = Deal(is_even("gx"), first_ref, second_ref, layouts()[2])
    pack_neighbour(deal, 1, message_ref, False)
    deal.finish()


def from_x(ref, n, way, lanes):
    row, lane, column, depth = iotas()
    ring, code13, code2, _ = x_places(lanes)
    first = X_LANE * n

    def population(i):
        value = ref[first + i]
        if i in turned(0, -way):
            place = 3 if way == 1 else 4
            extra = lines(ref[first + X_EXTRA], place - turned(0, -way).index(i))
            value = jnp.where(row == place, extra, value)
        return value

    def cotangent(i):
        value = lines(ref[first + i], -way * (3 - way * VELOCITIES[i][0]))
        if i in turned(0, way):
            place = 5 if way == 1 else 2
            extra = lines(ref[first + X_EXTRA], place - 4 - turned(0, way).index(i))
            value = jnp.where(row == place, extra, value)
        return value

    def codes(s):
        if s == 2:
            return lines(ref[code2 + n // 2], 4 * (n % 2))
        value = ref[code13 + n]
        return value if s == 1 else lines(value, -3 * way)

    def outer(i):
        value = ref[ring + (i + 1) // 2]
        return pltpu.roll(value, LANES // 2, 1) if i and i % 2 == 0 else value

    def outer_code():
        return pltpu.roll(ref[ring], LANES // 2, 1)

    return population, cotangent, codes, outer, outer_code


def sides(first_ref, second_ref, axis, layout):
    even = is_even(axis)
    picks = Pick(even, second_ref, first_ref), Pick(even, first_ref, second_ref)
    return [Unpacking(pick, layout) for pick in picks]


def own_rows(step=0):
    return pl.ds(ROWS + step, ROWS)


def halo_rows(step=0):
    return pl.ds({0: 2 * ROWS, -1: 2 * ROWS - 1, 1: 1}[step], ROWS)


def put_halo(ref, at, halo):
    ref[at, pl.ds(0, ROWS), :] = halo
    ref[at, halo_rows(), :] = halo


def put_ring(ref, at, own, halo):
    ref[at, own_rows(), :] = own
    put_halo(ref, at, halo)


def expand(code):
    row, lane, column, depth = iotas()
    top = depth == NZ - 1
    phi = jnp.where(top, code, 0.0)
    for step in (1, 2, 4, 8, 16):
        phi = phi + pltpu.roll(phi, LANES - step, 1)
    return jnp.where(top, 0.0, code), phi


def lay_own(c, population, cotangent, codes, code_phi, pop, cot, wide, field):
    for i in range(Q):
        pop[5 * i + c, pl.ds(2 * ROWS, ROWS), :] = population(i)
        if cotangent is not None:
            cot[4 * i + c - 1, own_rows(), :] = cotangent(i)
    for n in range(2):
        wide[n, c, 1] = code_phi[n]
    if cotangent is not None:
        field[0, c - 1, 0], field[1, c - 1, 0] = code_phi[1], code_phi[0]
        for s in (2, 3):
            field[s, c - 1, 0] = codes(s)


def lay_halo(c, below, above, pop, cot, wide, field):
    row, lane, column, depth = iotas()
    before, behind = expand(below[2](1)), expand(above[2](1))
    for n in range(2):
        wide[n, c, 0], wide[n, c, 2] = before[n], behind[n]
    for i in range(Q):
        pop[5 * i + c, pl.ds(ROWS, ROWS), :] = below[0](i)
        pop[5 * i + c, pl.ds(3 * ROWS, ROWS), :] = above[0](i)
        if below[1] is not None:
            put_halo(cot, 4 * i + c - 1, jnp.where(row < 4, above[1](i), below[1](i)))
    if below[1] is not None:
        for n, place in ((0, 1), (1, 0)):
            field[place, c - 1, 1] = jnp.where(row < 4, behind[n], before[n])
        for s in (2, 3):
            field[s, c - 1, 1] = jnp.where(row < 4, above[2](s), below[2](s))


def near_tile():
    return jnp.where(is_right(True), 4, 1)


def lay_out(
    near_y_ref,
    far_y_ref,
    first_near_ref,
    second_near_ref,
    own_ref,
    field_ref,
    cot_ref,
    pop,
    cot,
    wide,
    field,
):
    spaces = pop, cot, wide, field
    below, above = sides(first_near_ref, second_near_ref, "gx", layouts()[1])
    for t in range(2):
        lay_own(
            2 + t,
            lambda i: own_ref[2 * i + t],
            lambda i: cot_ref[2 * i + t],
            lambda s: field_ref[2 * s + t],
            (field_ref[2 + t], field_ref[2 * OWN_PHI + t]),
            *spaces,
        )
        lay_halo(2 + t, from_x(below, t, 1, 3), from_x(above, t, -1, 3), *spaces)
    near, far = from_y(near_y_ref, True), from_y(far_y_ref, False)
    for c, (population, cotangent, codes, _, _) in ((near_tile(), near), (5 - near_tile(), far)):
        lay_own(c, population, cotangent, codes, expand(codes(1)), *spaces)
    kept = half_lanes(is_right(True))
    lay_own(
        0,
        lambda i: jnp.where(kept, near[3](i), far[3](i)),
        None,
        None,
        expand(jnp.where(kept, near[4](), far[4]())),
        *spaces,
    )
    lay_halo(near_tile(), from_x(below, 2, 1, 3), from_x(above, 2, -1, 3), *spaces)


def lay_far(near_refs, far_refs, spaces):
    nears, fars = (
        [
            from_x(ref, lanes - 1, way, lanes)
            for ref, way in zip(sides(*refs, "gx", layout), (1, -1))
        ]
        for refs, layout, lanes in zip((near_refs, far_refs), layouts()[1:], (3, 1))
    )
    lay_halo(5 - near_tile(), *fars, *spaces)
    kept = half_lanes(is_right(True))
    ring = [
        (
            lambda i, near=near, far=far: jnp.where(kept, near[3](i), far[3](i)),
            None,
            lambda s, near=near, far=far: jnp.where(kept, near[4](), far[4]()),
        )
        for near, far in zip(nears, fars)
    ]
    lay_halo(0, *ring, *spaces)


def steps_kernel(
    sizes,
    state_ref,
    own_field_ref,
    names_ref,
    first_near_ref,
    second_near_ref,
    first_far_ref,
    second_far_ref,
    *refs,
):
    adjoint_ref, panel_ref, pop_a, ring_a, wide, field, pop_b, ring_b, saved, mom, grad = refs[4:]
    size_x, size_y = sizes
    lay_far(
        (first_near_ref, second_near_ref),
        (first_far_ref, second_far_ref),
        (pop_a, ring_a, wide, field),
    )

    at_x, at_y = lax.axis_index("gx"), lax.axis_index("gy")
    edges = (
        jnp.where(at_x == 0, 1, 0),
        jnp.where(at_x == size_x - 1, 1, 0),
        jnp.where(at_y == 0, 1, 0),
        jnp.where(at_y == size_y - 1, 1, 0),
    )
    row, lane, column, depth = iotas()
    after = row < 4

    def masks_of(tile, first, r):
        return wall_masks(r == 0, tile == first, tile == first + 1, edges)

    def neighbours(tile, tiles):
        if isinstance(tile, int):
            return {0: tile, -1: (tile - 1) % tiles, 1: (tile + 1) % tiles}
        return {0: tile, -1: lax.rem(tile + tiles - 1, tiles), 1: lax.rem(tile + 1, tiles)}

    def from_wide(ref, tile, r):
        step = neighbours(tile, 5)

        def load(i, tile_step, row_step, move):
            at = 5 * i + step[tile_step]
            before, own, behind = (ref[at, pl.ds(ROWS * n + row_step, ROWS), :] for n in (1, 2, 3))
            return (own, jnp.where(after, behind, before), before, behind)[r]

        return load

    def from_ring(ref, tile, tiles, r):
        step = neighbours(tile, tiles)

        def load(i, tile_step, row_step, move):
            rows = own_rows(row_step) if r == 0 else halo_rows(row_step)
            return ref[tiles * i + step[tile_step], rows, :]

        return load

    def from_outer(ref, r):
        def load(i, tile_step, row_step, move):
            rows = own_rows(row_step) if r == 0 else halo_rows(row_step)
            if tile_step:
                return ref[4 * i + (2 if tile_step < 0 else 1), rows, :]
            cut = {0: 2, 1: 1, -1: 3}[move]
            return jnp.where(column < cut, ref[4 * i + 3, rows, :], ref[4 * i, rows, :])

        return load

    def note(s, tile, r, parts):
        for n, value in enumerate(parts[2:4] + tuple(parts[4])):
            mom[s - 1, n, tile, r] = value

    def first_step(tile, carry):
        place = lax.rem(tile + 4, 5)
        halo = []
        for r in (2, 0, 3):
            f = stream_tile(from_wide(pop_a, tile, r), 1, masks_of(tile, 2, r), lane)
            parts = moments(f)
            if r == 0:
                note(1, place, 0, parts)
                for i in range(Q):
                    saved[0, i, place] = f[i]
            else:
                halo.append(parts[2:4] + tuple(parts[4]))
            at = {2: 0, 0: 1, 3: 2}[r]
            g = collide(f, wide[0, tile, at], wide[1, tile, at], parts)
            for i in range(Q):
                pop_b[5 * i + tile, pl.ds(ROWS * (at + 1), ROWS), :] = g[i]
        for n in range(5):
            mom[0, n, place, 1] = jnp.where(after, halo[1][n], halo[0][n])
        return carry

    lax.fori_loop(0, 5, first_step, 0)

    def second_step(tile, carry):
        out = []
        for r in range(2):
            f = stream_tile(from_wide(pop_b, tile + 1, r), 1, masks_of(tile, 1, r), lane)
            parts = moments(f)
            note(2, tile, r, parts)
            if r == 0:
                for i in range(Q):
                    saved[1, i, tile] = f[i]
            out.append(collide(f, field[2, tile, r], field[0, tile, r], parts))
        for i in range(Q):
            put_ring(ring_b, 4 * i + tile, out[0][i], out[1][i])
        return carry

    lax.fori_loop(0, 4, second_step, 0)

    def third_step(tile, carry):
        for r in range(2):
            f = stream_tile(from_ring(ring_b, tile, 4, r), 1, masks_of(tile, 1, r), lane)
            note(3, tile, r, moments(f))
            if r == 0:
                for i in range(Q):
                    saved[2, i, tile] = f[i]
        return carry

    lax.fori_loop(0, 4, third_step, 0)

    def back_tile(load, s, tile, r, own):
        b = stream_tile(load, -1, masks_of(4 if tile is None else tile, 1, r), lane)

        def read(get):
            return jnp.where(column < 2, get(3), get(0)) if tile is None else get(tile)

        rho, rinv, *u = [read(lambda at: mom[s - 1, n, at, r]) for n in range(5)]
        kind, phi = read(lambda at: field[s, at, r]), read(lambda at: field[0, at, r])
        state = [saved[s - 1, i, tile] for i in range(Q)] if own else None
        back, term = collide_back(b, kind, phi, rho, rinv, u, state)
        if own:
            grad[tile] = term if s == 3 else grad[tile] + term
        return back

    def last_step(tile, carry):
        out = [back_tile(from_ring(ring_a, tile, 4, r), 3, tile, r, r == 0) for r in range(2)]
        for i in range(Q):
            put_ring(ring_b, 4 * i + tile, out[0][i], out[1][i])
        return carry

    lax.fori_loop(0, 4, last_step, 0)

    for k, tile in enumerate((1, 2, None)):
        out = []
        for r in range(2):
            load = from_outer(ring_b, r) if tile is None else from_ring(ring_b, tile, 4, r)
            out.append(back_tile(load, 2, tile, r, r == 0 and tile is not None))
        for i in range(Q):
            put_ring(ring_a, 3 * i + k, out[0][i], out[1][i])

    for k, tile in enumerate((1, 2, None)):
        out = []
        for r in range(2):
            load = from_ring(ring_a, k, 3, r)
            out.append(back_tile(load, 1, tile, r, r == 0 and tile is not None))
        for i in range(Q):
            put_ring(ring_b, 3 * i + k, out[0][i], out[1][i])

    panel = lax.broadcasted_iota(jnp.int32, panel_ref.shape, 1)
    sums = jnp.zeros(panel_ref.shape, jnp.float32)
    for t in range(2):
        b = stream_tile(from_ring(ring_b, t, 3, 0), -1, masks_of(t, 0, 0), lane)
        f = [state_ref[2 * i + t] for i in range(Q)]
        kind, phi = own_field_ref[t], own_field_ref[2 * OWN_PHI + t]
        _, _, rho, rinv, u = moments(f)
        back, term = collide_back(b, kind, phi, rho, rinv, u, f)
        for i in range(Q):
            adjoint_ref[i, :, pl.ds(t * LANES, LANES)] = back[i]
        term = term + grad[t + 1]
        for part in range(2):
            amount = jnp.sum(jnp.where((row < 4) == (part == 0), term, 0.0))
            name = names_ref[t, 4 * part : 4 * part + 1, 0:1]
            sums = sums + jnp.where(panel == name, amount, 0.0)
    panel_ref[...] = sums


def finish(parts_ref, adjoint_ref, sums_hbm, adjoint_hbm, sums_ref, sems):
    adjoint_copy = pltpu.make_async_copy(adjoint_ref, adjoint_hbm, sems.at[0])
    adjoint_copy.start()
    sums_ref[...] = jnp.sum(parts_ref[...], axis=0)
    sums_copy = pltpu.make_async_copy(sums_ref, sums_hbm, sems.at[1])
    sums_copy.start()
    sums_copy.wait()
    adjoint_copy.wait()


VMEM = pl.BlockSpec(memory_space=pltpu.VMEM)
HBM = pl.BlockSpec(memory_space=pltpu.HBM)


def shape_of(*dims):
    return jax.ShapeDtypeStruct(dims, jnp.float32)


def tiles_of(count):
    return shape_of(count, ROWS, LANES)


def on_device(sizes, checkpoint, cotangent, cell_codes, porosity, baffle_index):
    size_x, size_y = sizes
    panels = porosity.shape[0]
    devices = size_x * size_y
    y_layout, near_layout, far_layout = layouts()

    params = pltpu.CompilerParams(vmem_limit_bytes=32 * 1024 * 1024)

    def call(kernel, out_shape, in_specs, scratch=(), name=None, aliases={}):
        return pl.pallas_call(
            kernel,
            out_shape=out_shape,
            in_specs=in_specs,
            out_specs=jax.tree.map(lambda _: VMEM, out_shape),
            scratch_shapes=scratch,
            input_output_aliases=aliases,
            compiler_params=params,
            name=name,
        )

    def swap(value, axis, size):
        return lax.ppermute(value, axis, [(i, i ^ 1) for i in range(size) if i ^ 1 < size])

    def swap_between(value, axis, size):
        pairs = [(i, i + 1) for i in range(1, size - 1, 2)]
        return lax.ppermute(value, axis, pairs + [(j, i) for i, j in pairs])

    def swap_inner(value):
        pairs = [
            (i * size_y + y, (i + 1) * size_y + y)
            for i in range(1, size_x - 1, 2)
            for y in range(1, size_y - 1)
        ]
        return lax.ppermute(value, ("gx", "gy"), pairs + [(j, i) for i, j in pairs])

    arguments = [
        pltpu.with_memory_space_constraint(value, pltpu.HBM)
        for value in (checkpoint, cotangent, cell_codes, baffle_index, porosity)
    ]
    near_y, far_y, own, state, cot, field, names = call(
        pack_own,
        (tiles_of(y_layout.size),) * 2
        + (tiles_of(2 * Q),) * 3
        + (tiles_of(2 * OWN_PHI + 2), jax.ShapeDtypeStruct((2, ROWS, LANES), jnp.int32)),
        [HBM] * 5,
        [
            pltpu.VMEM((Q, ROWS, 2 * LANES), jnp.float32),
            pltpu.VMEM((Q, ROWS, 2 * LANES), jnp.float32),
            pltpu.VMEM((STEPS, ROWS, 2 * LANES), jnp.int32),
            pltpu.SMEM(baffle_index.shape, jnp.int32),
            pltpu.SMEM(porosity.shape, jnp.float32),
            pltpu.SemaphoreType.DMA((5,)),
        ],
        name="pack_own",
    )(*arguments)
    near_y = swap(near_y, "gy", size_y)
    far_y = swap_between(far_y, "gy", size_y)
    first_near, second_near = call(
        pack_near,
        (tiles_of(near_layout.size), tiles_of(near_layout.size + 1)),
        [VMEM] * 4,
        name="pack_near",
    )(own, cot, field, near_y)
    second_near = swap_between(second_near, "gx", size_x)
    first_near = swap(first_near, "gx", size_x)
    first_far, second_far = call(
        pack_far,
        (tiles_of(far_layout.size), tiles_of(far_layout.size + 1)),
        [VMEM],
        name="pack_far",
    )(far_y)
    second_far = swap_inner(second_far)
    first_far = swap(first_far, "gx", size_x)
    spaces = (
        shape_of(5 * Q, 5 * ROWS, LANES),
        shape_of(4 * Q, 3 * ROWS, LANES),
        shape_of(2, 5, 3, ROWS, LANES),
        shape_of(4, 4, 2, ROWS, LANES),
    )
    laid = call(lay_out, spaces, [VMEM] * 7, name="lay_out")(
        near_y, far_y, first_near, second_near, own, field, cot
    )
    adjoint, sums, *_ = call(
        functools.partial(steps_kernel, sizes),
        (pltpu.VMEM((Q, ROWS, 2 * LANES), jnp.float32), shape_of(devices, panels)) + spaces,
        [VMEM] * 11,
        [
            pltpu.VMEM((5 * Q, 5 * ROWS, LANES), jnp.float32),
            pltpu.VMEM((4 * Q, 3 * ROWS, LANES), jnp.float32),
            pltpu.VMEM((3, Q, 5, ROWS, LANES), jnp.float32),
            pltpu.VMEM((3, 5, 5, 2, ROWS, LANES), jnp.float32),
            pltpu.VMEM((4, ROWS, LANES), jnp.float32),
        ],
        name="steps",
        aliases={7 + n: 2 + n for n in range(4)},
    )(state, field, names, first_near, second_near, first_far, second_far, *laid)
    gathered = lax.all_to_all(sums, ("gx", "gy"), 0, 0, tiled=True)
    totals, adjoint = pl.pallas_call(
        finish,
        out_shape=(shape_of(1, panels), shape_of(Q, ROWS, 2 * LANES)),
        in_specs=[VMEM, VMEM],
        out_specs=(HBM, HBM),
        scratch_shapes=[pltpu.VMEM((1, panels), jnp.float32), pltpu.SemaphoreType.DMA((2,))],
        compiler_params=params,
        name="finish",
    )(gathered.reshape(devices, 1, panels), adjoint)
    return adjoint, totals.reshape(panels)


def solution(mesh):
    sizes = (mesh.shape["gx"], mesh.shape["gy"])
    in_specs = (P(None, "gx", "gy"), P(None, "gx", "gy"), P(None, "gx", "gy"), P(), P("gx", "gy"))
    out_specs = (P(None, "gx", "gy"), P())
    return jax.shard_map(
        functools.partial(on_device, sizes),
        mesh=mesh,
        in_specs=in_specs,
        out_specs=out_specs,
        check_vma=False,
    )
```

```python
import functools

import jax
import jax.numpy as jnp
import numpy as np
from jax import lax
from jax.experimental import pallas as pl
from jax.experimental.pallas import tpu as pltpu
from jax.sharding import PartitionSpec as P

Q = 19
STEPS = 4
NZ = 32
ROWS = 8
LANES = 128
OMEGA = 1.6
ACCEL = (0.002, 0.0, -0.003)
SHIFT = tuple(a / OMEGA for a in ACCEL)

VELOCITIES = [
    (0, 0, 0),
    (1, 0, 0),
    (-1, 0, 0),
    (0, 1, 0),
    (0, -1, 0),
    (0, 0, 1),
    (0, 0, -1),
    (1, 1, 0),
    (-1, -1, 0),
    (1, -1, 0),
    (-1, 1, 0),
    (1, 0, 1),
    (-1, 0, -1),
    (1, 0, -1),
    (-1, 0, 1),
    (0, 1, 1),
    (0, -1, -1),
    (0, 1, -1),
    (0, -1, 1),
]
OPPOSITE = [0, 2, 1, 4, 3, 6, 5, 8, 7, 10, 9, 12, 11, 14, 13, 16, 15, 18, 17]
PAIRS = [(i, i + 1) for i in range(1, Q, 2)]
W_REST, W_AXIS, W_DIAG = 1.0 / 3.0, 1.0 / 18.0, 1.0 / 36.0

Y_CODE1, Y_CODE2, Y_CODE3, Y_POP, Y_COT = 38, 39, 40, 41, 42
Y_TILES = 43
X_EXTRA = 19
X_LANE = 20
X_HALVES = 10


def x_places(lanes):
    ring = X_LANE * lanes
    code13 = ring + X_HALVES
    code2 = code13 + lanes
    return ring, code13, code2, code2 + (lanes + 1) // 2


EMPTY = 25
FREE = NZ - EMPTY
WEIGHTS = [W_REST] + [W_AXIS] * 6 + [W_DIAG] * 12
LEVEL = [i for i, v in enumerate(VELOCITIES) if v[2] < 1]
OWN_PHI = 4


def turned(axis, outward):
    return [i for i, v in enumerate(VELOCITIES) if v[axis] == outward and sum(map(abs, v)) == 2]


def total(values):
    values = list(values)
    while len(values) > 1:
        values = [a + b for a, b in zip(values[::2], values[1::2])] + (
            [values[-1]] if len(values) % 2 else []
        )
    return values[0]


def along(vector, three):
    terms = None
    for c, value in zip(vector, three):
        if c == 0:
            continue
        if terms is None:
            terms = value if c > 0 else -value
        else:
            terms = terms + value if c > 0 else terms - value
    return terms


def moments(f):
    plus = {i: f[i] + f[o] for i, o in PAIRS}
    minus = {i: f[i] - f[o] for i, o in PAIRS}
    rho = total([f[0]] + [plus[i] for i, _ in PAIRS])
    rinv = 1.0 / rho
    u = []
    for axis in range(3):
        terms = [
            minus[i] if VELOCITIES[i][axis] > 0 else -minus[i]
            for i, _ in PAIRS
            if VELOCITIES[i][axis] != 0
        ]
        u.append(total(terms) * rinv + SHIFT[axis])
    return plus, minus, rho, rinv, u


def coefficients(kind, phi, rinv):
    baffle = kind == 3.0
    gas = kind == 0.0
    even = jnp.where(gas, 0.0, jnp.where(baffle, 0.5 - 0.5 * OMEGA * phi, 0.5 * (1.0 - OMEGA)))
    odd = jnp.where(
        gas, 0.0, jnp.where(baffle, (1.0 - 0.5 * OMEGA) * phi - 0.5, 0.5 * (1.0 - OMEGA))
    )
    slope = jnp.where(
        baffle,
        OMEGA * phi,
        jnp.where(kind == 1.0, OMEGA, jnp.where(kind == 2.0, OMEGA * rinv, 0.0)),
    )
    return even, odd, slope


def collide(f, kind, phi, parts):
    plus, minus, rho, rinv, u = parts
    even, odd, slope = coefficients(kind, phi, rinv)
    scale = slope * rho
    rest = 1.0 - 1.5 * (u[0] * u[0] + u[1] * u[1] + u[2] * u[2])
    base = scale * rest + jnp.where(kind == 0.0, 1.0, 0.0)
    out = [None] * Q
    out[0] = 2.0 * even * f[0] + W_REST * base
    for weight, pairs in ((W_AXIS, PAIRS[:3]), (W_DIAG, PAIRS[3:])):
        flat = weight * base
        three = (3.0 * weight) * scale
        for i, o in pairs:
            cu = along(VELOCITIES[i], u)
            lin = three * cu
            ev = even * plus[i] + (flat + 1.5 * lin * cu)
            od = odd * minus[i] + lin
            out[i] = ev + od
            out[o] = ev - od
    return out


def collide_back(b, kind, phi, rho, rinv, u, state=None):
    even, odd, slope = coefficients(kind, phi, rinv)
    plus = {i: b[i] + b[o] for i, o in PAIRS}
    minus = {i: b[i] - b[o] for i, o in PAIRS}
    rest = 1.0 - 1.5 * (u[0] * u[0] + u[1] * u[1] + u[2] * u[2])
    u_half = [1.5 * c for c in u]
    weighted = W_REST * b[0]
    energy = 0.0
    vector = [0.0, 0.0, 0.0]
    for weight, pairs in ((W_AXIS, PAIRS[:3]), (W_DIAG, PAIRS[3:])):
        weighted = weighted + weight * total([plus[i] for i, _ in pairs])
        energies, parts = [], ([], [], [])
        for i, _ in pairs:
            cu = along(VELOCITIES[i], u)
            half = along(VELOCITIES[i], u_half) * plus[i]
            first = minus[i] + half
            energies.append(cu * first)
            second = first + half
            for axis in range(3):
                c = VELOCITIES[i][axis]
                if c:
                    parts[axis].append(second if c > 0 else -second)
        energy = energy + (3.0 * weight) * total(energies)
        vector = [vector[k] + (3.0 * weight) * total(parts[k]) for k in range(3)]
    energy = energy + rest * weighted
    vector = [vector[k] - (3.0 * weighted) * u[k] for k in range(3)]
    push = [slope * v for v in vector]
    inner = total([push[k] * (u[k] - SHIFT[k]) for k in range(3)])
    shared = jnp.where(kind == 2.0, 0.0, slope) * energy - inner
    out = [None] * Q
    out[0] = 2.0 * even * b[0] + shared
    for i, o in PAIRS:
        ev = even * plus[i] + shared
        od = odd * minus[i] + along(VELOCITIES[i], push)
        out[i] = ev + od
        out[o] = ev - od
    if state is None:
        return out, None
    evens = total([plus[i] * (state[i] + state[o]) for i, o in PAIRS])
    odds = total([minus[i] * (state[i] - state[o]) for i, o in PAIRS])
    term = (
        -OMEGA * (b[0] * state[0] + 0.5 * evens)
        + (1.0 - 0.5 * OMEGA) * odds
        + OMEGA * rho * energy
    )
    return out, jnp.where(kind == 3.0, term, 0.0)


def wall_masks(sign_rows, own_low, own_high, edges):
    lane = lax.broadcasted_iota(jnp.int32, (ROWS, LANES), 1)
    row = lax.broadcasted_iota(jnp.int32, (ROWS, LANES), 0)
    x_low, x_high, y_low, y_high = edges
    depth = lane % NZ
    masks = {}
    masks[2, 1] = depth == 0
    masks[2, -1] = depth == NZ - 1
    masks[1, 1] = lane < jnp.where(own_low, y_low * NZ, 0)
    masks[1, -1] = lane >= jnp.where(own_high, LANES - y_high * NZ, LANES)
    if sign_rows:
        masks[0, 1] = row < x_low
        masks[0, -1] = row >= ROWS - x_high
    return masks


def stream_tile(load, sign, masks, lane):
    cross_low, cross_high = lane >= LANES - NZ, lane < NZ
    combined = {}
    out = []
    for i, vector in enumerate(VELOCITIES):
        v = tuple(sign * c for c in vector)
        value = load(i, 0, -v[0], v[1])
        if v[1] == 1:
            value = jnp.where(cross_low, load(i, -1, -v[0], 1), value)
        elif v[1] == -1:
            value = jnp.where(cross_high, load(i, 1, -v[0], -1), value)
        amount = (v[1] * NZ + v[2]) % LANES
        if amount:
            value = pltpu.roll(value, amount, 1)
        outside = None
        if v not in combined:
            for axis in range(3):
                if v[axis] and (axis, v[axis]) in masks:
                    wall = masks[axis, v[axis]]
                    outside = wall if outside is None else outside | wall
            combined[v] = outside
        outside = combined[v]
        if outside is not None:
            value = jnp.where(outside, load(OPPOSITE[i], 0, 0, 0), value)
        out.append(value)
    return out


def iotas():
    row = lax.broadcasted_iota(jnp.int32, (ROWS, LANES), 0)
    lane = lax.broadcasted_iota(jnp.int32, (ROWS, LANES), 1)
    return row, lane, lane // NZ, lane % NZ


def columns(value, count):
    amount = (count * NZ) % LANES
    return pltpu.roll(value, amount, 1) if amount else value


def lines(value, count):
    amount = count % ROWS
    return pltpu.roll(value, amount, 0) if amount else value


class Layout:
    def __init__(self, count, guests, fills):
        self.fills = fills
        hosts = [at for at in fills if at not in guests]
        self.hosts = {at: hosts[4 * n : 4 * n + 4] for n, at in enumerate(guests)}
        self.guests = guests
        kept = [at for at in range(count) if at not in guests]
        self.place = {at: n for n, at in enumerate(kept)}
        self.size = len(kept)


class Packing:
    def __init__(self, ref, layout):
        self.ref, self.layout, self.held = ref, layout, {}

    def __setitem__(self, at, value):
        if at in self.layout.guests:
            self.held[at] = value
        else:
            self.ref[self.layout.place[at]] = value

    def finish(self):
        row, lane, column, depth = iotas()
        spare = depth >= EMPTY
        for at, value in self.held.items():
            for k, host in enumerate(self.layout.hosts[at]):
                place = self.layout.place[host]
                moved = pltpu.roll(value, EMPTY - FREE * k, 1)
                self.ref[place] = jnp.where(spare, moved, self.ref[place])
        for place in range(self.layout.size, self.ref.shape[0]):
            self.ref[place] = jnp.zeros((ROWS, LANES), jnp.float32)


class Unpacking:
    def __init__(self, source, layout):
        self.source, self.layout, self.cache = source, layout, {}
        self.changed = set(layout.guests).union(*layout.hosts.values())

    def __getitem__(self, at):
        if at not in self.cache:
            self.cache[at] = self.read(at)
        return self.cache[at]

    def read(self, at):
        row, lane, column, depth = iotas()
        layout = self.layout
        if at in layout.guests:
            value = None
            for k, host in enumerate(layout.hosts[at]):
                tile = self.source[layout.place[host]]
                moved = pltpu.roll(tile, LANES - (EMPTY - FREE * k), 1)
                value = moved if value is None else jnp.where(depth >= FREE * k, moved, value)
        else:
            value = self.source[layout.place[at]]
        if at in self.changed:
            value = jnp.where(depth >= EMPTY, layout.fills[at], value)
        return value


def layouts():
    y_fills = {2 * i + t: WEIGHTS[i] for i in LEVEL for t in range(2)}
    y_fills.update({Y_POP: W_DIAG, Y_CODE2: 0.0})
    out = [Layout(Y_TILES, [2 * i for i in LEVEL[:6]], y_fills)]
    for lanes, count in ((3, 10), (1, 4)):
        ring, _, code2, tiles = x_places(lanes)
        fills = {ring + n: WEIGHTS[2 * n] for n in range(1, X_HALVES)}
        fills.update({at: 0.0 for at in range(code2, tiles)})
        fills.update({X_LANE * n + i: WEIGHTS[i] for n in range(lanes) for i in LEVEL})
        guests = [X_LANE * (lanes - 1) + i for i in LEVEL[:count]]
        out.append(Layout(tiles, guests, fills))
    return out


class Pick:
    def __init__(self, flag, first, second):
        self.flag, self.first, self.second = flag, first, second

    def __getitem__(self, at):
        return jnp.where(self.flag, self.first[at], self.second[at])


class Deal:
    def __init__(self, even, first, second, layout, skip=0):
        self.even, self.skip, self.held = even, skip, {}
        self.first, self.second = Packing(first, layout), Packing(second, layout)

    def put(self, way, at, value):
        if (-way, at) not in self.held:
            self.held[way, at] = value
            return
        other = self.held.pop((-way, at))
        up, down = (value, other) if way == 1 else (other, value)
        self.first[at - self.skip] = jnp.where(self.even, up, down)
        self.second[at - self.skip] = jnp.where(self.even, down, up)

    def put_both(self, at, value):
        self.first[at - self.skip] = value
        self.second[at - self.skip] = value

    def finish(self):
        self.first.finish()
        self.second.finish()


def is_even(axis):
    return lax.rem(lax.axis_index(axis), 2) == 0


def pack_own(
    f_hbm,
    cot_hbm,
    codes_hbm,
    panels_hbm,
    porosity_hbm,
    first_ref,
    second_ref,
    own_ref,
    state_ref,
    own_cot_ref,
    field_ref,
    names_ref,
    f_ref,
    cot_ref,
    codes_ref,
    panels_ref,
    porosity_ref,
    sems,
):
    pieces = (
        (panels_hbm, panels_ref),
        (porosity_hbm, porosity_ref),
        (f_hbm, f_ref),
        (codes_hbm, codes_ref),
        (cot_hbm, cot_ref),
    )
    copies = [
        pltpu.make_async_copy(source, target, sems.at[n])
        for n, (source, target) in enumerate(pieces)
    ]
    for copy in copies:
        copy.start()
    for copy in copies[:4]:
        copy.wait()
    deal = Deal(is_even("gy"), first_ref, second_ref, layouts()[0])
    row, lane, column, depth = iotas()
    top = depth == NZ - 1

    def tile_of(ref, i, t):
        return ref[i, :, pl.ds(t * LANES, LANES)]

    codes, phis = [], []
    for t in range(2):
        names = panels_ref[0, t * LANES], panels_ref[4, t * LANES]
        phi = jnp.where(row < 4, porosity_ref[names[0]], porosity_ref[names[1]])
        names_ref[t] = jnp.where(row < 4, names[0], names[1])
        kinds = [tile_of(codes_ref, s, t).astype(jnp.float32) for s in range(STEPS)]
        f = [tile_of(f_ref, i, t) for i in range(Q)]
        g = collide(f, kinds[0], phi, moments(f))
        for i in range(Q):
            own_ref[2 * i + t] = g[i]
            state_ref[2 * i + t] = f[i]
        for s in range(STEPS):
            field_ref[2 * s + t] = kinds[s]
        field_ref[2 * OWN_PHI + t] = phi
        codes.append([jnp.where(top, phi, kinds[1]), kinds[2], kinds[3]])
    copies[4].wait()
    for i in range(Q):
        for way in (1, -1):
            near, far = (1, 0) if way == 1 else (0, 1)
            deep = 3 - way * VELOCITIES[i][1]
            cot = tile_of(cot_ref, i, near)
            g_far = own_ref[2 * i + far]
            if way == 1:
                mixed = jnp.where(column >= deep, g_far, columns(cot, deep - 4))
            else:
                mixed = jnp.where(column < 4 - deep, g_far, columns(cot, 4 - deep))
            deal.put(way, 2 * i, mixed if far == 0 else own_ref[2 * i])
            deal.put(way, 2 * i + 1, mixed if far == 1 else own_ref[2 * i + 1])
    for way in (1, -1):
        near, far = (1, 0) if way == 1 else (0, 1)
        outer = 3 if way == 1 else 0
        deal.put(way, Y_CODE1, codes[near][0])
        deal.put(way, Y_CODE2, codes[near][1])
        outside = columns(codes[far][0], 3 - 2 * outer)
        deal.put(way, Y_CODE3, jnp.where(column == 3 - outer, outside, codes[near][2]))
        extra = None
        for k, i in enumerate(turned(1, -way)):
            value = columns(own_ref[2 * i + far], k - outer)
            extra = value if extra is None else jnp.where(column == k, value, extra)
        deal.put(way, Y_POP, extra)
        extra = None
        for k, i in enumerate(turned(1, way)):
            value = columns(tile_of(cot_ref, i, near), k - (1 if way == 1 else 2))
            extra = value if extra is None else jnp.where(column == k, value, extra)
        deal.put(way, Y_COT, extra)
    deal.finish()
    for t in range(2):
        for i in range(Q):
            own_cot_ref[2 * i + t] = tile_of(cot_ref, i, t)


def is_right(near):
    return is_even("gy") if near else jnp.logical_not(is_even("gy"))


def half_lanes(right):
    row, lane, column, depth = iotas()
    return lane // (LANES // 2) == jnp.where(right, 0, 1)


def from_y(message_ref, near):
    row, lane, column, depth = iotas()
    ref = Unpacking(message_ref, layouts()[0])
    right = is_right(near)

    def population(i):
        return jnp.where(right, ref[2 * i], ref[2 * i + 1])

    def cotangent(i):
        values = []
        for way, place, far in ((1, 1, 0), (-1, 2, 1)):
            deep = 3 - way * VELOCITIES[i][1]
            value = columns(ref[2 * i + far], way * (4 - deep))
            if i in turned(1, way):
                extra = columns(ref[Y_COT], place - turned(1, way).index(i))
                value = jnp.where(column == place, extra, value)
            values.append(value)
        return jnp.where(right, values[1], values[0])

    def codes(s):
        return ref[(Y_CODE1, Y_CODE2, Y_CODE3)[s - 1]]

    def outer(i):
        left, above = ref[2 * i], ref[2 * i + 1]
        if i in turned(1, 1):
            above = columns(ref[Y_POP], -turned(1, 1).index(i))
        if i in turned(1, -1):
            left = columns(ref[Y_POP], 3 - turned(1, -1).index(i))
        return jnp.where(right, above, left)

    def outer_code():
        return jnp.where(right, columns(ref[Y_CODE3], 1), columns(ref[Y_CODE3], 3))

    return population, cotangent, codes, outer, outer_code


def mix_lines(deal, at, pop, cot, deep, way):
    row, lane, column, depth = iotas()
    if way == 1:
        mixed = jnp.where(row >= deep, pop, lines(cot, deep))
    else:
        mixed = jnp.where(row < ROWS - deep, pop, lines(cot, -deep))
    deal.put(way, at, mixed)


def pack_lines(deal, first, population, cotangent):
    row, lane, column, depth = iotas()

    for i in range(Q):
        pop, cot = population(i), cotangent(i)
        for way in (1, -1):
            mix_lines(deal, first + i, pop, cot, 3 - way * VELOCITIES[i][0], way)
    for way in (1, -1):
        extra = None
        for k, i in enumerate(turned(0, -way)):
            value = lines(population(i), k - (3 if way == 1 else 4))
            extra = value if extra is None else jnp.where(row == k, value, extra)
        for k, i in enumerate(turned(0, way)):
            value = lines(cotangent(i), 4 + k - (5 if way == 1 else 2))
            extra = jnp.where(row == 4 + k, value, extra)
        deal.put(way, first + X_EXTRA, extra)


def pack_neighbour(deal, lanes, message_ref, near):
    ring, code13, code2, tiles = x_places(lanes)
    population, cotangent, codes, outer, outer_code = from_y(message_ref, near)
    pack_lines(deal, X_LANE * (lanes - 1), population, cotangent)
    kept = half_lanes(is_right(near))
    for n in range(X_HALVES):
        first, second = (outer(2 * n - 1), outer(2 * n)) if n else (outer(0), outer_code())
        deal.put_both(ring + n, jnp.where(kept, first, pltpu.roll(second, LANES // 2, 1)))
    for way in (1, -1):
        mix_lines(deal, code13 + lanes - 1, codes(1), codes(3), 3, way)
    deal.put_both(tiles - 1, codes(2))


def pack_near(own_ref, cot_ref, field_ref, message_ref, first_ref, second_ref):
    row, lane, column, depth = iotas()
    deal = Deal(is_even("gx"), first_ref, second_ref, layouts()[1])
    ring, code13, code2, tiles = x_places(3)
    for t in range(2):
        pack_lines(
            deal,
            X_LANE * t,
            lambda i: own_ref[2 * i + t],
            lambda i: cot_ref[2 * i + t],
        )
        code = jnp.where(depth == NZ - 1, field_ref[2 * OWN_PHI + t], field_ref[2 + t])
        for way in (1, -1):
            mix_lines(deal, code13 + t, code, field_ref[6 + t], 3, way)
    first, second = field_ref[4], lines(field_ref[5], 4)
    deal.put(1, code2, jnp.where(row >= 4, first, second))
    deal.put(-1, code2, jnp.where(row < 4, first, second))
    pack_neighbour(deal, 3, message_ref, True)
    deal.finish()


def pack_far(message_ref, first_ref, second_ref):
    deal = Deal(is_even("gx"), first_ref, second_ref, layouts()[2])
    pack_neighbour(deal, 1, message_ref, False)
    deal.finish()


def from_x(ref, n, way, lanes):
    row, lane, column, depth = iotas()
    ring, code13, code2, _ = x_places(lanes)
    first = X_LANE * n

    def population(i):
        value = ref[first + i]
        if i in turned(0, -way):
            place = 3 if way == 1 else 4
            extra = lines(ref[first + X_EXTRA], place - turned(0, -way).index(i))
            value = jnp.where(row == place, extra, value)
        return value

    def cotangent(i):
        value = lines(ref[first + i], -way * (3 - way * VELOCITIES[i][0]))
        if i in turned(0, way):
            place = 5 if way == 1 else 2
            extra = lines(ref[first + X_EXTRA], place - 4 - turned(0, way).index(i))
            value = jnp.where(row == place, extra, value)
        return value

    def codes(s):
        if s == 2:
            return lines(ref[code2 + n // 2], 4 * (n % 2))
        value = ref[code13 + n]
        return value if s == 1 else lines(value, -3 * way)

    def outer(i):
        value = ref[ring + (i + 1) // 2]
        return pltpu.roll(value, LANES // 2, 1) if i and i % 2 == 0 else value

    def outer_code():
        return pltpu.roll(ref[ring], LANES // 2, 1)

    return population, cotangent, codes, outer, outer_code


def sides(first_ref, second_ref, axis, layout):
    even = is_even(axis)
    picks = Pick(even, second_ref, first_ref), Pick(even, first_ref, second_ref)
    return [Unpacking(pick, layout) for pick in picks]


def own_rows(step=0):
    return pl.ds(ROWS + step, ROWS)


def halo_rows(step=0):
    return pl.ds({0: 2 * ROWS, -1: 2 * ROWS - 1, 1: 1}[step], ROWS)


def put_halo(ref, at, halo):
    ref[at, pl.ds(0, ROWS), :] = halo
    ref[at, halo_rows(), :] = halo


def put_ring(ref, at, own, halo):
    ref[at, own_rows(), :] = own
    put_halo(ref, at, halo)


def expand(code):
    row, lane, column, depth = iotas()
    top = depth == NZ - 1
    phi = jnp.where(top, code, 0.0)
    for step in (1, 2, 4, 8, 16):
        phi = phi + pltpu.roll(phi, LANES - step, 1)
    return jnp.where(top, 0.0, code), phi


def lay_own(c, population, cotangent, codes, code_phi, pop, cot, wide, field):
    for i in range(Q):
        pop[5 * i + c, pl.ds(2 * ROWS, ROWS), :] = population(i)
        if cotangent is not None:
            cot[4 * i + c - 1, own_rows(), :] = cotangent(i)
    for n in range(2):
        wide[n, c, 1] = code_phi[n]
    if cotangent is not None:
        field[0, c - 1, 0], field[1, c - 1, 0] = code_phi[1], code_phi[0]
        for s in (2, 3):
            field[s, c - 1, 0] = codes(s)


def lay_halo(c, below, above, pop, cot, wide, field):
    row, lane, column, depth = iotas()
    before, behind = expand(below[2](1)), expand(above[2](1))
    for n in range(2):
        wide[n, c, 0], wide[n, c, 2] = before[n], behind[n]
    for i in range(Q):
        pop[5 * i + c, pl.ds(ROWS, ROWS), :] = below[0](i)
        pop[5 * i + c, pl.ds(3 * ROWS, ROWS), :] = above[0](i)
        if below[1] is not None:
            put_halo(cot, 4 * i + c - 1, jnp.where(row < 4, above[1](i), below[1](i)))
    if below[1] is not None:
        for n, place in ((0, 1), (1, 0)):
            field[place, c - 1, 1] = jnp.where(row < 4, behind[n], before[n])
        for s in (2, 3):
            field[s, c - 1, 1] = jnp.where(row < 4, above[2](s), below[2](s))


def near_tile():
    return jnp.where(is_right(True), 4, 1)


def lay_out(
    near_y_ref,
    far_y_ref,
    first_near_ref,
    second_near_ref,
    own_ref,
    field_ref,
    cot_ref,
    pop,
    cot,
    wide,
    field,
):
    spaces = pop, cot, wide, field
    below, above = sides(first_near_ref, second_near_ref, "gx", layouts()[1])
    for t in range(2):
        lay_own(
            2 + t,
            lambda i: own_ref[2 * i + t],
            lambda i: cot_ref[2 * i + t],
            lambda s: field_ref[2 * s + t],
            (field_ref[2 + t], field_ref[2 * OWN_PHI + t]),
            *spaces,
        )
        lay_halo(2 + t, from_x(below, t, 1, 3), from_x(above, t, -1, 3), *spaces)
    near, far = from_y(near_y_ref, True), from_y(far_y_ref, False)
    for c, (population, cotangent, codes, _, _) in ((near_tile(), near), (5 - near_tile(), far)):
        lay_own(c, population, cotangent, codes, expand(codes(1)), *spaces)
    kept = half_lanes(is_right(True))
    lay_own(
        0,
        lambda i: jnp.where(kept, near[3](i), far[3](i)),
        None,
        None,
        expand(jnp.where(kept, near[4](), far[4]())),
        *spaces,
    )
    lay_halo(near_tile(), from_x(below, 2, 1, 3), from_x(above, 2, -1, 3), *spaces)


def lay_far(near_refs, far_refs, spaces):
    nears, fars = (
        [
            from_x(ref, lanes - 1, way, lanes)
            for ref, way in zip(sides(*refs, "gx", layout), (1, -1))
        ]
        for refs, layout, lanes in zip((near_refs, far_refs), layouts()[1:], (3, 1))
    )
    lay_halo(5 - near_tile(), *fars, *spaces)
    kept = half_lanes(is_right(True))
    ring = [
        (
            lambda i, near=near, far=far: jnp.where(kept, near[3](i), far[3](i)),
            None,
            lambda s, near=near, far=far: jnp.where(kept, near[4](), far[4]()),
        )
        for near, far in zip(nears, fars)
    ]
    lay_halo(0, *ring, *spaces)


def steps_kernel(
    sizes,
    state_ref,
    own_field_ref,
    names_ref,
    first_near_ref,
    second_near_ref,
    first_far_ref,
    second_far_ref,
    *refs,
):
    adjoint_ref, panel_ref, pop_a, ring_a, wide, field, pop_b, ring_b, saved, mom, grad = refs[4:]
    size_x, size_y = sizes
    lay_far(
        (first_near_ref, second_near_ref),
        (first_far_ref, second_far_ref),
        (pop_a, ring_a, wide, field),
    )

    at_x, at_y = lax.axis_index("gx"), lax.axis_index("gy")
    edges = (
        jnp.where(at_x == 0, 1, 0),
        jnp.where(at_x == size_x - 1, 1, 0),
        jnp.where(at_y == 0, 1, 0),
        jnp.where(at_y == size_y - 1, 1, 0),
    )
    row, lane, column, depth = iotas()
    after = row < 4

    def masks_of(tile, first, r):
        return wall_masks(r == 0, tile == first, tile == first + 1, edges)

    def neighbours(tile, tiles):
        if isinstance(tile, int):
            return {0: tile, -1: (tile - 1) % tiles, 1: (tile + 1) % tiles}
        return {0: tile, -1: lax.rem(tile + tiles - 1, tiles), 1: lax.rem(tile + 1, tiles)}

    def from_wide(ref, tile, r):
        step = neighbours(tile, 5)

        def load(i, tile_step, row_step, move):
            at = 5 * i + step[tile_step]
            before, own, behind = (ref[at, pl.ds(ROWS * n + row_step, ROWS), :] for n in (1, 2, 3))
            return (own, jnp.where(after, behind, before), before, behind)[r]

        return load

    def from_ring(ref, tile, tiles, r):
        step = neighbours(tile, tiles)

        def load(i, tile_step, row_step, move):
            rows = own_rows(row_step) if r == 0 else halo_rows(row_step)
            return ref[tiles * i + step[tile_step], rows, :]

        return load

    def from_outer(ref, r):
        def load(i, tile_step, row_step, move):
            rows = own_rows(row_step) if r == 0 else halo_rows(row_step)
            if tile_step:
                return ref[4 * i + (2 if tile_step < 0 else 1), rows, :]
            cut = {0: 2, 1: 1, -1: 3}[move]
            return jnp.where(column < cut, ref[4 * i + 3, rows, :], ref[4 * i, rows, :])

        return load

    def note(s, tile, r, parts):
        for n, value in enumerate(parts[2:4] + tuple(parts[4])):
            mom[s - 1, n, tile, r] = value

    def first_step(tile, carry):
        place = lax.rem(tile + 4, 5)
        halo = []
        for r in (2, 0, 3):
            f = stream_tile(from_wide(pop_a, tile, r), 1, masks_of(tile, 2, r), lane)
            parts = moments(f)
            if r == 0:
                note(1, place, 0, parts)
                for i in range(Q):
                    saved[0, i, place] = f[i]
            else:
                halo.append(parts[2:4] + tuple(parts[4]))
            at = {2: 0, 0: 1, 3: 2}[r]
            g = collide(f, wide[0, tile, at], wide[1, tile, at], parts)
            for i in range(Q):
                pop_b[5 * i + tile, pl.ds(ROWS * (at + 1), ROWS), :] = g[i]
        for n in range(5):
            mom[0, n, place, 1] = jnp.where(after, halo[1][n], halo[0][n])
        return carry

    lax.fori_loop(0, 5, first_step, 0)

    def second_step(tile, carry):
        out = []
        for r in range(2):
            f = stream_tile(from_wide(pop_b, tile + 1, r), 1, masks_of(tile, 1, r), lane)
            parts = moments(f)
            note(2, tile, r, parts)
            if r == 0:
                for i in range(Q):
                    saved[1, i, tile] = f[i]
            out.append(collide(f, field[2, tile, r], field[0, tile, r], parts))
        for i in range(Q):
            put_ring(ring_b, 4 * i + tile, out[0][i], out[1][i])
        return carry

    lax.fori_loop(0, 4, second_step, 0, unroll=2)

    def third_step(tile, carry):
        for r in range(2):
            f = stream_tile(from_ring(ring_b, tile, 4, r), 1, masks_of(tile, 1, r), lane)
            note(3, tile, r, moments(f))
            if r == 0:
                for i in range(Q):
                    saved[2, i, tile] = f[i]
        return carry

    lax.fori_loop(0, 4, third_step, 0, unroll=2)

    def back_tile(load, s, tile, r, own):
        b = stream_tile(load, -1, masks_of(4 if tile is None else tile, 1, r), lane)

        def read(get):
            return jnp.where(column < 2, get(3), get(0)) if tile is None else get(tile)

        rho, rinv, *u = [read(lambda at: mom[s - 1, n, at, r]) for n in range(5)]
        kind, phi = read(lambda at: field[s, at, r]), read(lambda at: field[0, at, r])
        state = [saved[s - 1, i, tile] for i in range(Q)] if own else None
        back, term = collide_back(b, kind, phi, rho, rinv, u, state)
        if own:
            grad[tile] = term if s == 3 else grad[tile] + term
        return back

    def last_step(tile, carry):
        out = [back_tile(from_ring(ring_a, tile, 4, r), 3, tile, r, r == 0) for r in range(2)]
        for i in range(Q):
            put_ring(ring_b, 4 * i + tile, out[0][i], out[1][i])
        return carry

    lax.fori_loop(0, 4, last_step, 0, unroll=2)

    for k, tile in enumerate((1, 2, None)):
        out = []
        for r in range(2):
            load = from_outer(ring_b, r) if tile is None else from_ring(ring_b, tile, 4, r)
            out.append(back_tile(load, 2, tile, r, r == 0 and tile is not None))
        for i in range(Q):
            put_ring(ring_a, 3 * i + k, out[0][i], out[1][i])

    for k, tile in enumerate((1, 2, None)):
        out = []
        for r in range(2):
            load = from_ring(ring_a, k, 3, r)
            out.append(back_tile(load, 1, tile, r, r == 0 and tile is not None))
        for i in range(Q):
            put_ring(ring_b, 3 * i + k, out[0][i], out[1][i])

    panel = lax.broadcasted_iota(jnp.int32, panel_ref.shape, 1)
    sums = jnp.zeros(panel_ref.shape, jnp.float32)
    for t in range(2):
        b = stream_tile(from_ring(ring_b, t, 3, 0), -1, masks_of(t, 0, 0), lane)
        f = [state_ref[2 * i + t] for i in range(Q)]
        kind, phi = own_field_ref[t], own_field_ref[2 * OWN_PHI + t]
        _, _, rho, rinv, u = moments(f)
        back, term = collide_back(b, kind, phi, rho, rinv, u, f)
        for i in range(Q):
            adjoint_ref[i, :, pl.ds(t * LANES, LANES)] = back[i]
        term = term + grad[t + 1]
        for part in range(2):
            amount = jnp.sum(jnp.where((row < 4) == (part == 0), term, 0.0))
            name = names_ref[t, 4 * part : 4 * part + 1, 0:1]
            sums = sums + jnp.where(panel == name, amount, 0.0)
    panel_ref[...] = sums


def finish(parts_ref, adjoint_ref, sums_hbm, adjoint_hbm, sums_ref, sems):
    adjoint_copy = pltpu.make_async_copy(adjoint_ref, adjoint_hbm, sems.at[0])
    adjoint_copy.start()
    sums_ref[...] = jnp.sum(parts_ref[...], axis=0)
    sums_copy = pltpu.make_async_copy(sums_ref, sums_hbm, sems.at[1])
    sums_copy.start()
    sums_copy.wait()
    adjoint_copy.wait()


VMEM = pl.BlockSpec(memory_space=pltpu.VMEM)
HBM = pl.BlockSpec(memory_space=pltpu.HBM)


def shape_of(*dims):
    return jax.ShapeDtypeStruct(dims, jnp.float32)


def tiles_of(count):
    return shape_of(count, ROWS, LANES)


def on_device(sizes, checkpoint, cotangent, cell_codes, porosity, baffle_index):
    size_x, size_y = sizes
    panels = porosity.shape[0]
    devices = size_x * size_y
    y_layout, near_layout, far_layout = layouts()

    params = pltpu.CompilerParams(vmem_limit_bytes=32 * 1024 * 1024)

    def call(kernel, out_shape, in_specs, scratch=(), name=None, aliases={}):
        return pl.pallas_call(
            kernel,
            out_shape=out_shape,
            in_specs=in_specs,
            out_specs=jax.tree.map(lambda _: VMEM, out_shape),
            scratch_shapes=scratch,
            input_output_aliases=aliases,
            compiler_params=params,
            name=name,
        )

    def swap(value, axis, size):
        return lax.ppermute(value, axis, [(i, i ^ 1) for i in range(size) if i ^ 1 < size])

    def swap_between(value, axis, size):
        pairs = [(i, i + 1) for i in range(1, size - 1, 2)]
        return lax.ppermute(value, axis, pairs + [(j, i) for i, j in pairs])

    def swap_inner(value):
        pairs = [
            (i * size_y + y, (i + 1) * size_y + y)
            for i in range(1, size_x - 1, 2)
            for y in range(1, size_y - 1)
        ]
        return lax.ppermute(value, ("gx", "gy"), pairs + [(j, i) for i, j in pairs])

    arguments = [
        pltpu.with_memory_space_constraint(value, pltpu.HBM)
        for value in (checkpoint, cotangent, cell_codes, baffle_index, porosity)
    ]
    near_y, far_y, own, state, cot, field, names = call(
        pack_own,
        (tiles_of(y_layout.size),) * 2
        + (tiles_of(2 * Q),) * 3
        + (tiles_of(2 * OWN_PHI + 2), jax.ShapeDtypeStruct((2, ROWS, LANES), jnp.int32)),
        [HBM] * 5,
        [
            pltpu.VMEM((Q, ROWS, 2 * LANES), jnp.float32),
            pltpu.VMEM((Q, ROWS, 2 * LANES), jnp.float32),
            pltpu.VMEM((STEPS, ROWS, 2 * LANES), jnp.int32),
            pltpu.SMEM(baffle_index.shape, jnp.int32),
            pltpu.SMEM(porosity.shape, jnp.float32),
            pltpu.SemaphoreType.DMA((5,)),
        ],
        name="pack_own",
    )(*arguments)
    near_y = swap(near_y, "gy", size_y)
    far_y = swap_between(far_y, "gy", size_y)
    first_near, second_near = call(
        pack_near,
        (tiles_of(near_layout.size), tiles_of(near_layout.size + 1)),
        [VMEM] * 4,
        name="pack_near",
    )(own, cot, field, near_y)
    second_near = swap_between(second_near, "gx", size_x)
    first_near = swap(first_near, "gx", size_x)
    first_far, second_far = call(
        pack_far,
        (tiles_of(far_layout.size), tiles_of(far_layout.size + 1)),
        [VMEM],
        name="pack_far",
    )(far_y)
    second_far = swap_inner(second_far)
    first_far = swap(first_far, "gx", size_x)
    spaces = (
        shape_of(5 * Q, 5 * ROWS, LANES),
        shape_of(4 * Q, 3 * ROWS, LANES),
        shape_of(2, 5, 3, ROWS, LANES),
        shape_of(4, 4, 2, ROWS, LANES),
    )
    laid = call(lay_out, spaces, [VMEM] * 7, name="lay_out")(
        near_y, far_y, first_near, second_near, own, field, cot
    )
    adjoint, sums, *_ = call(
        functools.partial(steps_kernel, sizes),
        (pltpu.VMEM((Q, ROWS, 2 * LANES), jnp.float32), shape_of(devices, panels)) + spaces,
        [VMEM] * 11,
        [
            pltpu.VMEM((5 * Q, 5 * ROWS, LANES), jnp.float32),
            pltpu.VMEM((4 * Q, 3 * ROWS, LANES), jnp.float32),
            pltpu.VMEM((3, Q, 5, ROWS, LANES), jnp.float32),
            pltpu.VMEM((3, 5, 5, 2, ROWS, LANES), jnp.float32),
            pltpu.VMEM((4, ROWS, LANES), jnp.float32),
        ],
        name="steps",
        aliases={7 + n: 2 + n for n in range(4)},
    )(state, field, names, first_near, second_near, first_far, second_far, *laid)
    gathered = lax.all_to_all(sums, ("gx", "gy"), 0, 0, tiled=True)
    totals, adjoint = pl.pallas_call(
        finish,
        out_shape=(shape_of(1, panels), shape_of(Q, ROWS, 2 * LANES)),
        in_specs=[VMEM, VMEM],
        out_specs=(HBM, HBM),
        scratch_shapes=[pltpu.VMEM((1, panels), jnp.float32), pltpu.SemaphoreType.DMA((2,))],
        compiler_params=params,
        name="finish",
    )(gathered.reshape(devices, 1, panels), adjoint)
    return adjoint, totals.reshape(panels)


def solution(mesh):
    sizes = (mesh.shape["gx"], mesh.shape["gy"])
    in_specs = (P(None, "gx", "gy"), P(None, "gx", "gy"), P(None, "gx", "gy"), P(), P("gx", "gy"))
    out_specs = (P(None, "gx", "gy"), P())
    return jax.shard_map(
        functools.partial(on_device, sizes),
        mesh=mesh,
        in_specs=in_specs,
        out_specs=out_specs,
        check_vma=False,
    )
```

```python
import functools

import jax
import jax.numpy as jnp
import numpy as np
from jax import lax
from jax.experimental import pallas as pl
from jax.experimental.pallas import tpu as pltpu
from jax.sharding import PartitionSpec as P

Q = 19
STEPS = 4
NZ = 32
ROWS = 8
LANES = 128
OMEGA = 1.6
ACCEL = (0.002, 0.0, -0.003)
SHIFT = tuple(a / OMEGA for a in ACCEL)

VELOCITIES = [
    (0, 0, 0),
    (1, 0, 0),
    (-1, 0, 0),
    (0, 1, 0),
    (0, -1, 0),
    (0, 0, 1),
    (0, 0, -1),
    (1, 1, 0),
    (-1, -1, 0),
    (1, -1, 0),
    (-1, 1, 0),
    (1, 0, 1),
    (-1, 0, -1),
    (1, 0, -1),
    (-1, 0, 1),
    (0, 1, 1),
    (0, -1, -1),
    (0, 1, -1),
    (0, -1, 1),
]
OPPOSITE = [0, 2, 1, 4, 3, 6, 5, 8, 7, 10, 9, 12, 11, 14, 13, 16, 15, 18, 17]
PAIRS = [(i, i + 1) for i in range(1, Q, 2)]
W_REST, W_AXIS, W_DIAG = 1.0 / 3.0, 1.0 / 18.0, 1.0 / 36.0

Y_CODE1, Y_CODE2, Y_CODE3, Y_POP, Y_COT = 38, 39, 40, 41, 42
Y_TILES = 43
X_EXTRA = 19
X_LANE = 20
X_HALVES = 10


def x_places(lanes):
    ring = X_LANE * lanes
    code13 = ring + X_HALVES
    code2 = code13 + lanes
    return ring, code13, code2, code2 + (lanes + 1) // 2


EMPTY = 25
FREE = NZ - EMPTY
WEIGHTS = [W_REST] + [W_AXIS] * 6 + [W_DIAG] * 12
LEVEL = [i for i, v in enumerate(VELOCITIES) if v[2] < 1]
OWN_PHI = 4


def turned(axis, outward):
    return [i for i, v in enumerate(VELOCITIES) if v[axis] == outward and sum(map(abs, v)) == 2]


def total(values):
    values = list(values)
    while len(values) > 1:
        values = [a + b for a, b in zip(values[::2], values[1::2])] + (
            [values[-1]] if len(values) % 2 else []
        )
    return values[0]


def along(vector, three):
    terms = None
    for c, value in zip(vector, three):
        if c == 0:
            continue
        if terms is None:
            terms = value if c > 0 else -value
        else:
            terms = terms + value if c > 0 else terms - value
    return terms


def moments(f):
    plus = {i: f[i] + f[o] for i, o in PAIRS}
    minus = {i: f[i] - f[o] for i, o in PAIRS}
    rho = total([f[0]] + [plus[i] for i, _ in PAIRS])
    rinv = 1.0 / rho
    u = []
    for axis in range(3):
        terms = [
            minus[i] if VELOCITIES[i][axis] > 0 else -minus[i]
            for i, _ in PAIRS
            if VELOCITIES[i][axis] != 0
        ]
        u.append(total(terms) * rinv + SHIFT[axis])
    return plus, minus, rho, rinv, u


def coefficients(kind, phi, rinv):
    baffle = kind == 3.0
    gas = kind == 0.0
    even = jnp.where(gas, 0.0, jnp.where(baffle, 0.5 - 0.5 * OMEGA * phi, 0.5 * (1.0 - OMEGA)))
    odd = jnp.where(
        gas, 0.0, jnp.where(baffle, (1.0 - 0.5 * OMEGA) * phi - 0.5, 0.5 * (1.0 - OMEGA))
    )
    slope = jnp.where(
        baffle,
        OMEGA * phi,
        jnp.where(kind == 1.0, OMEGA, jnp.where(kind == 2.0, OMEGA * rinv, 0.0)),
    )
    return even, odd, slope


def collide(f, kind, phi, parts):
    plus, minus, rho, rinv, u = parts
    even, odd, slope = coefficients(kind, phi, rinv)
    scale = slope * rho
    rest = 1.0 - 1.5 * (u[0] * u[0] + u[1] * u[1] + u[2] * u[2])
    base = scale * rest + jnp.where(kind == 0.0, 1.0, 0.0)
    out = [None] * Q
    out[0] = 2.0 * even * f[0] + W_REST * base
    for weight, pairs in ((W_AXIS, PAIRS[:3]), (W_DIAG, PAIRS[3:])):
        flat = weight * base
        three = (3.0 * weight) * scale
        for i, o in pairs:
            cu = along(VELOCITIES[i], u)
            lin = three * cu
            ev = even * plus[i] + (flat + 1.5 * lin * cu)
            od = odd * minus[i] + lin
            out[i] = ev + od
            out[o] = ev - od
    return out


def collide_back(b, kind, phi, rho, rinv, u, state=None):
    even, odd, slope = coefficients(kind, phi, rinv)
    plus = {i: b[i] + b[o] for i, o in PAIRS}
    minus = {i: b[i] - b[o] for i, o in PAIRS}
    rest = 1.0 - 1.5 * (u[0] * u[0] + u[1] * u[1] + u[2] * u[2])
    u_half = [1.5 * c for c in u]
    weighted = W_REST * b[0]
    energy = 0.0
    vector = [0.0, 0.0, 0.0]
    for weight, pairs in ((W_AXIS, PAIRS[:3]), (W_DIAG, PAIRS[3:])):
        weighted = weighted + weight * total([plus[i] for i, _ in pairs])
        energies, parts = [], ([], [], [])
        for i, _ in pairs:
            cu = along(VELOCITIES[i], u)
            half = along(VELOCITIES[i], u_half) * plus[i]
            first = minus[i] + half
            energies.append(cu * first)
            second = first + half
            for axis in range(3):
                c = VELOCITIES[i][axis]
                if c:
                    parts[axis].append(second if c > 0 else -second)
        energy = energy + (3.0 * weight) * total(energies)
        vector = [vector[k] + (3.0 * weight) * total(parts[k]) for k in range(3)]
    energy = energy + rest * weighted
    vector = [vector[k] - (3.0 * weighted) * u[k] for k in range(3)]
    push = [slope * v for v in vector]
    inner = total([push[k] * (u[k] - SHIFT[k]) for k in range(3)])
    shared = jnp.where(kind == 2.0, 0.0, slope) * energy - inner
    out = [None] * Q
    out[0] = 2.0 * even * b[0] + shared
    for i, o in PAIRS:
        ev = even * plus[i] + shared
        od = odd * minus[i] + along(VELOCITIES[i], push)
        out[i] = ev + od
        out[o] = ev - od
    if state is None:
        return out, None
    evens = total([plus[i] * (state[i] + state[o]) for i, o in PAIRS])
    odds = total([minus[i] * (state[i] - state[o]) for i, o in PAIRS])
    term = (
        -OMEGA * (b[0] * state[0] + 0.5 * evens)
        + (1.0 - 0.5 * OMEGA) * odds
        + OMEGA * rho * energy
    )
    return out, jnp.where(kind == 3.0, term, 0.0)


def wall_masks(sign_rows, own_low, own_high, edges):
    lane = lax.broadcasted_iota(jnp.int32, (ROWS, LANES), 1)
    row = lax.broadcasted_iota(jnp.int32, (ROWS, LANES), 0)
    x_low, x_high, y_low, y_high = edges
    depth = lane % NZ
    masks = {}
    masks[2, 1] = depth == 0
    masks[2, -1] = depth == NZ - 1
    masks[1, 1] = lane < jnp.where(own_low, y_low * NZ, 0)
    masks[1, -1] = lane >= jnp.where(own_high, LANES - y_high * NZ, LANES)
    if sign_rows:
        masks[0, 1] = row < x_low
        masks[0, -1] = row >= ROWS - x_high
    return masks


def stream_tile(load, sign, masks, lane):
    cross_low, cross_high = lane >= LANES - NZ, lane < NZ
    combined = {}
    out = []
    for i, vector in enumerate(VELOCITIES):
        v = tuple(sign * c for c in vector)
        value = load(i, 0, -v[0], v[1])
        if v[1] == 1:
            value = jnp.where(cross_low, load(i, -1, -v[0], 1), value)
        elif v[1] == -1:
            value = jnp.where(cross_high, load(i, 1, -v[0], -1), value)
        amount = (v[1] * NZ + v[2]) % LANES
        if amount:
            value = pltpu.roll(value, amount, 1)
        outside = None
        if v not in combined:
            for axis in range(3):
                if v[axis] and (axis, v[axis]) in masks:
                    wall = masks[axis, v[axis]]
                    outside = wall if outside is None else outside | wall
            combined[v] = outside
        outside = combined[v]
        if outside is not None:
            value = jnp.where(outside, load(OPPOSITE[i], 0, 0, 0), value)
        out.append(value)
    return out


def iotas():
    row = lax.broadcasted_iota(jnp.int32, (ROWS, LANES), 0)
    lane = lax.broadcasted_iota(jnp.int32, (ROWS, LANES), 1)
    return row, lane, lane // NZ, lane % NZ


def columns(value, count):
    amount = (count * NZ) % LANES
    return pltpu.roll(value, amount, 1) if amount else value


def lines(value, count):
    amount = count % ROWS
    return pltpu.roll(value, amount, 0) if amount else value


class Layout:
    def __init__(self, count, guests, fills):
        self.fills = fills
        hosts = [at for at in fills if at not in guests]
        self.hosts = {at: hosts[4 * n : 4 * n + 4] for n, at in enumerate(guests)}
        self.guests = guests
        kept = [at for at in range(count) if at not in guests]
        self.place = {at: n for n, at in enumerate(kept)}
        self.size = len(kept)


class Packing:
    def __init__(self, ref, layout):
        self.ref, self.layout, self.held = ref, layout, {}

    def __setitem__(self, at, value):
        if at in self.layout.guests:
            self.held[at] = value
        else:
            self.ref[self.layout.place[at]] = value

    def finish(self):
        row, lane, column, depth = iotas()
        spare = depth >= EMPTY
        for at, value in self.held.items():
            for k, host in enumerate(self.layout.hosts[at]):
                place = self.layout.place[host]
                moved = pltpu.roll(value, EMPTY - FREE * k, 1)
                self.ref[place] = jnp.where(spare, moved, self.ref[place])
        for place in range(self.layout.size, self.ref.shape[0]):
            self.ref[place] = jnp.zeros((ROWS, LANES), jnp.float32)


class Unpacking:
    def __init__(self, source, layout):
        self.source, self.layout, self.cache = source, layout, {}
        self.changed = set(layout.guests).union(*layout.hosts.values())

    def __getitem__(self, at):
        if at not in self.cache:
            self.cache[at] = self.read(at)
        return self.cache[at]

    def read(self, at):
        row, lane, column, depth = iotas()
        layout = self.layout
        if at in layout.guests:
            value = None
            for k, host in enumerate(layout.hosts[at]):
                tile = self.source[layout.place[host]]
                moved = pltpu.roll(tile, LANES - (EMPTY - FREE * k), 1)
                value = moved if value is None else jnp.where(depth >= FREE * k, moved, value)
        else:
            value = self.source[layout.place[at]]
        if at in self.changed:
            value = jnp.where(depth >= EMPTY, layout.fills[at], value)
        return value


def layouts():
    y_fills = {2 * i + t: WEIGHTS[i] for i in LEVEL for t in range(2)}
    y_fills.update({Y_POP: W_DIAG, Y_CODE2: 0.0})
    out = [Layout(Y_TILES, [2 * i for i in LEVEL[:6]], y_fills)]
    for lanes, count in ((3, 10), (1, 4)):
        ring, _, code2, tiles = x_places(lanes)
        fills = {ring + n: WEIGHTS[2 * n] for n in range(1, X_HALVES)}
        fills.update({at: 0.0 for at in range(code2, tiles)})
        fills.update({X_LANE * n + i: WEIGHTS[i] for n in range(lanes) for i in LEVEL})
        guests = [X_LANE * (lanes - 1) + i for i in LEVEL[:count]]
        out.append(Layout(tiles, guests, fills))
    return out


class Pick:
    def __init__(self, flag, first, second):
        self.flag, self.first, self.second = flag, first, second

    def __getitem__(self, at):
        return jnp.where(self.flag, self.first[at], self.second[at])


class Deal:
    def __init__(self, even, first, second, layout, skip=0):
        self.even, self.skip, self.held = even, skip, {}
        self.first, self.second = Packing(first, layout), Packing(second, layout)

    def put(self, way, at, value):
        if (-way, at) not in self.held:
            self.held[way, at] = value
            return
        other = self.held.pop((-way, at))
        up, down = (value, other) if way == 1 else (other, value)
        self.first[at - self.skip] = jnp.where(self.even, up, down)
        self.second[at - self.skip] = jnp.where(self.even, down, up)

    def put_both(self, at, value):
        self.first[at - self.skip] = value
        self.second[at - self.skip] = value

    def finish(self):
        self.first.finish()
        self.second.finish()


def is_even(axis):
    return lax.rem(lax.axis_index(axis), 2) == 0


def pack_own(
    f_hbm,
    cot_hbm,
    codes_hbm,
    panels_hbm,
    porosity_hbm,
    first_ref,
    second_ref,
    own_ref,
    state_ref,
    own_cot_ref,
    field_ref,
    names_ref,
    f_ref,
    cot_ref,
    codes_ref,
    panels_ref,
    porosity_ref,
    sems,
):
    pieces = (
        (panels_hbm, panels_ref),
        (porosity_hbm, porosity_ref),
        (f_hbm, f_ref),
        (codes_hbm, codes_ref),
        (cot_hbm, cot_ref),
    )
    copies = [
        pltpu.make_async_copy(source, target, sems.at[n])
        for n, (source, target) in enumerate(pieces)
    ]
    for copy in copies:
        copy.start()
    for copy in copies[:4]:
        copy.wait()
    deal = Deal(is_even("gy"), first_ref, second_ref, layouts()[0])
    row, lane, column, depth = iotas()
    top = depth == NZ - 1

    def tile_of(ref, i, t):
        return ref[i, :, pl.ds(t * LANES, LANES)]

    codes, phis = [], []
    for t in range(2):
        names = panels_ref[0, t * LANES], panels_ref[4, t * LANES]
        phi = jnp.where(row < 4, porosity_ref[names[0]], porosity_ref[names[1]])
        names_ref[t] = jnp.where(row < 4, names[0], names[1])
        kinds = [tile_of(codes_ref, s, t).astype(jnp.float32) for s in range(STEPS)]
        f = [tile_of(f_ref, i, t) for i in range(Q)]
        g = collide(f, kinds[0], phi, moments(f))
        for i in range(Q):
            own_ref[2 * i + t] = g[i]
            state_ref[2 * i + t] = f[i]
        for s in range(STEPS):
            field_ref[2 * s + t] = kinds[s]
        field_ref[2 * OWN_PHI + t] = phi
        codes.append([jnp.where(top, phi, kinds[1]), kinds[2], kinds[3]])
    copies[4].wait()
    for i in range(Q):
        for way in (1, -1):
            near, far = (1, 0) if way == 1 else (0, 1)
            deep = 3 - way * VELOCITIES[i][1]
            cot = tile_of(cot_ref, i, near)
            g_far = own_ref[2 * i + far]
            if way == 1:
                mixed = jnp.where(column >= deep, g_far, columns(cot, deep - 4))
            else:
                mixed = jnp.where(column < 4 - deep, g_far, columns(cot, 4 - deep))
            deal.put(way, 2 * i, mixed if far == 0 else own_ref[2 * i])
            deal.put(way, 2 * i + 1, mixed if far == 1 else own_ref[2 * i + 1])
    for way in (1, -1):
        near, far = (1, 0) if way == 1 else (0, 1)
        outer = 3 if way == 1 else 0
        deal.put(way, Y_CODE1, codes[near][0])
        deal.put(way, Y_CODE2, codes[near][1])
        outside = columns(codes[far][0], 3 - 2 * outer)
        deal.put(way, Y_CODE3, jnp.where(column == 3 - outer, outside, codes[near][2]))
        extra = None
        for k, i in enumerate(turned(1, -way)):
            value = columns(own_ref[2 * i + far], k - outer)
            extra = value if extra is None else jnp.where(column == k, value, extra)
        deal.put(way, Y_POP, extra)
        extra = None
        for k, i in enumerate(turned(1, way)):
            value = columns(tile_of(cot_ref, i, near), k - (1 if way == 1 else 2))
            extra = value if extra is None else jnp.where(column == k, value, extra)
        deal.put(way, Y_COT, extra)
    deal.finish()
    for t in range(2):
        for i in range(Q):
            own_cot_ref[2 * i + t] = tile_of(cot_ref, i, t)


def is_right(near):
    return is_even("gy") if near else jnp.logical_not(is_even("gy"))


def half_lanes(right):
    row, lane, column, depth = iotas()
    return lane // (LANES // 2) == jnp.where(right, 0, 1)


def from_y(message_ref, near):
    row, lane, column, depth = iotas()
    ref = Unpacking(message_ref, layouts()[0])
    right = is_right(near)

    def population(i):
        return jnp.where(right, ref[2 * i], ref[2 * i + 1])

    def cotangent(i):
        values = []
        for way, place, far in ((1, 1, 0), (-1, 2, 1)):
            deep = 3 - way * VELOCITIES[i][1]
            value = columns(ref[2 * i + far], way * (4 - deep))
            if i in turned(1, way):
                extra = columns(ref[Y_COT], place - turned(1, way).index(i))
                value = jnp.where(column == place, extra, value)
            values.append(value)
        return jnp.where(right, values[1], values[0])

    def codes(s):
        return ref[(Y_CODE1, Y_CODE2, Y_CODE3)[s - 1]]

    def outer(i):
        left, above = ref[2 * i], ref[2 * i + 1]
        if i in turned(1, 1):
            above = columns(ref[Y_POP], -turned(1, 1).index(i))
        if i in turned(1, -1):
            left = columns(ref[Y_POP], 3 - turned(1, -1).index(i))
        return jnp.where(right, above, left)

    def outer_code():
        return jnp.where(right, columns(ref[Y_CODE3], 1), columns(ref[Y_CODE3], 3))

    return population, cotangent, codes, outer, outer_code


def mix_lines(deal, at, pop, cot, deep, way):
    row, lane, column, depth = iotas()
    if way == 1:
        mixed = jnp.where(row >= deep, pop, lines(cot, deep))
    else:
        mixed = jnp.where(row < ROWS - deep, pop, lines(cot, -deep))
    deal.put(way, at, mixed)


def pack_lines(deal, first, population, cotangent):
    row, lane, column, depth = iotas()

    for i in range(Q):
        pop, cot = population(i), cotangent(i)
        for way in (1, -1):
            mix_lines(deal, first + i, pop, cot, 3 - way * VELOCITIES[i][0], way)
    for way in (1, -1):
        extra = None
        for k, i in enumerate(turned(0, -way)):
            value = lines(population(i), k - (3 if way == 1 else 4))
            extra = value if extra is None else jnp.where(row == k, value, extra)
        for k, i in enumerate(turned(0, way)):
            value = lines(cotangent(i), 4 + k - (5 if way == 1 else 2))
            extra = jnp.where(row == 4 + k, value, extra)
        deal.put(way, first + X_EXTRA, extra)


def pack_neighbour(deal, lanes, message_ref, near):
    ring, code13, code2, tiles = x_places(lanes)
    population, cotangent, codes, outer, outer_code = from_y(message_ref, near)
    pack_lines(deal, X_LANE * (lanes - 1), population, cotangent)
    kept = half_lanes(is_right(near))
    for n in range(X_HALVES):
        first, second = (outer(2 * n - 1), outer(2 * n)) if n else (outer(0), outer_code())
        deal.put_both(ring + n, jnp.where(kept, first, pltpu.roll(second, LANES // 2, 1)))
    for way in (1, -1):
        mix_lines(deal, code13 + lanes - 1, codes(1), codes(3), 3, way)
    deal.put_both(tiles - 1, codes(2))


def pack_near(own_ref, cot_ref, field_ref, message_ref, first_ref, second_ref):
    row, lane, column, depth = iotas()
    deal = Deal(is_even("gx"), first_ref, second_ref, layouts()[1])
    ring, code13, code2, tiles = x_places(3)
    for t in range(2):
        pack_lines(
            deal,
            X_LANE * t,
            lambda i: own_ref[2 * i + t],
            lambda i: cot_ref[2 * i + t],
        )
        code = jnp.where(depth == NZ - 1, field_ref[2 * OWN_PHI + t], field_ref[2 + t])
        for way in (1, -1):
            mix_lines(deal, code13 + t, code, field_ref[6 + t], 3, way)
    first, second = field_ref[4], lines(field_ref[5], 4)
    deal.put(1, code2, jnp.where(row >= 4, first, second))
    deal.put(-1, code2, jnp.where(row < 4, first, second))
    pack_neighbour(deal, 3, message_ref, True)
    deal.finish()


def pack_far(message_ref, first_ref, second_ref):
    deal = Deal(is_even("gx"), first_ref, second_ref, layouts()[2])
    pack_neighbour(deal, 1, message_ref, False)
    deal.finish()


def from_x(ref, n, way, lanes):
    row, lane, column, depth = iotas()
    ring, code13, code2, _ = x_places(lanes)
    first = X_LANE * n

    def population(i):
        value = ref[first + i]
        if i in turned(0, -way):
            place = 3 if way == 1 else 4
            extra = lines(ref[first + X_EXTRA], place - turned(0, -way).index(i))
            value = jnp.where(row == place, extra, value)
        return value

    def cotangent(i):
        value = lines(ref[first + i], -way * (3 - way * VELOCITIES[i][0]))
        if i in turned(0, way):
            place = 5 if way == 1 else 2
            extra = lines(ref[first + X_EXTRA], place - 4 - turned(0, way).index(i))
            value = jnp.where(row == place, extra, value)
        return value

    def codes(s):
        if s == 2:
            return lines(ref[code2 + n // 2], 4 * (n % 2))
        value = ref[code13 + n]
        return value if s == 1 else lines(value, -3 * way)

    def outer(i):
        value = ref[ring + (i + 1) // 2]
        return pltpu.roll(value, LANES // 2, 1) if i and i % 2 == 0 else value

    def outer_code():
        return pltpu.roll(ref[ring], LANES // 2, 1)

    return population, cotangent, codes, outer, outer_code


def sides(first_ref, second_ref, axis, layout):
    even = is_even(axis)
    picks = Pick(even, second_ref, first_ref), Pick(even, first_ref, second_ref)
    return [Unpacking(pick, layout) for pick in picks]


def own_rows(step=0):
    return pl.ds(ROWS + step, ROWS)


def halo_rows(step=0):
    return pl.ds({0: 2 * ROWS, -1: 2 * ROWS - 1, 1: 1}[step], ROWS)


def put_halo(ref, at, halo):
    ref[at, pl.ds(0, ROWS), :] = halo
    ref[at, halo_rows(), :] = halo


def put_ring(ref, at, own, halo):
    ref[at, own_rows(), :] = own
    put_halo(ref, at, halo)


def expand(code):
    row, lane, column, depth = iotas()
    top = depth == NZ - 1
    phi = jnp.where(top, code, 0.0)
    for step in (1, 2, 4, 8, 16):
        phi = phi + pltpu.roll(phi, LANES - step, 1)
    return jnp.where(top, 0.0, code), phi


def lay_own(c, population, cotangent, codes, code_phi, pop, cot, wide, field):
    for i in range(Q):
        pop[5 * i + c, pl.ds(2 * ROWS, ROWS), :] = population(i)
        if cotangent is not None:
            cot[4 * i + c - 1, own_rows(), :] = cotangent(i)
    for n in range(2):
        wide[n, c, 1] = code_phi[n]
    if cotangent is not None:
        field[0, c - 1, 0], field[1, c - 1, 0] = code_phi[1], code_phi[0]
        for s in (2, 3):
            field[s, c - 1, 0] = codes(s)


def lay_halo(c, below, above, pop, cot, wide, field):
    row, lane, column, depth = iotas()
    before, behind = expand(below[2](1)), expand(above[2](1))
    for n in range(2):
        wide[n, c, 0], wide[n, c, 2] = before[n], behind[n]
    for i in range(Q):
        pop[5 * i + c, pl.ds(ROWS, ROWS), :] = below[0](i)
        pop[5 * i + c, pl.ds(3 * ROWS, ROWS), :] = above[0](i)
        if below[1] is not None:
            put_halo(cot, 4 * i + c - 1, jnp.where(row < 4, above[1](i), below[1](i)))
    if below[1] is not None:
        for n, place in ((0, 1), (1, 0)):
            field[place, c - 1, 1] = jnp.where(row < 4, behind[n], before[n])
        for s in (2, 3):
            field[s, c - 1, 1] = jnp.where(row < 4, above[2](s), below[2](s))


def near_tile():
    return jnp.where(is_right(True), 4, 1)


def lay_out(
    near_y_ref,
    far_y_ref,
    first_near_ref,
    second_near_ref,
    own_ref,
    field_ref,
    cot_ref,
    pop,
    cot,
    wide,
    field,
):
    spaces = pop, cot, wide, field
    below, above = sides(first_near_ref, second_near_ref, "gx", layouts()[1])
    for t in range(2):
        lay_own(
            2 + t,
            lambda i: own_ref[2 * i + t],
            lambda i: cot_ref[2 * i + t],
            lambda s: field_ref[2 * s + t],
            (field_ref[2 + t], field_ref[2 * OWN_PHI + t]),
            *spaces,
        )
        lay_halo(2 + t, from_x(below, t, 1, 3), from_x(above, t, -1, 3), *spaces)
    near, far = from_y(near_y_ref, True), from_y(far_y_ref, False)
    for c, (population, cotangent, codes, _, _) in ((near_tile(), near), (5 - near_tile(), far)):
        lay_own(c, population, cotangent, codes, expand(codes(1)), *spaces)
    kept = half_lanes(is_right(True))
    lay_own(
        0,
        lambda i: jnp.where(kept, near[3](i), far[3](i)),
        None,
        None,
        expand(jnp.where(kept, near[4](), far[4]())),
        *spaces,
    )
    lay_halo(near_tile(), from_x(below, 2, 1, 3), from_x(above, 2, -1, 3), *spaces)


def lay_far(near_refs, far_refs, spaces):
    nears, fars = (
        [
            from_x(ref, lanes - 1, way, lanes)
            for ref, way in zip(sides(*refs, "gx", layout), (1, -1))
        ]
        for refs, layout, lanes in zip((near_refs, far_refs), layouts()[1:], (3, 1))
    )
    lay_halo(5 - near_tile(), *fars, *spaces)
    kept = half_lanes(is_right(True))
    ring = [
        (
            lambda i, near=near, far=far: jnp.where(kept, near[3](i), far[3](i)),
            None,
            lambda s, near=near, far=far: jnp.where(kept, near[4](), far[4]()),
        )
        for near, far in zip(nears, fars)
    ]
    lay_halo(0, *ring, *spaces)


def steps_kernel(
    sizes,
    state_ref,
    own_field_ref,
    names_ref,
    first_near_ref,
    second_near_ref,
    first_far_ref,
    second_far_ref,
    *refs,
):
    adjoint_ref, panel_ref, pop_a, ring_a, wide, field, pop_b, ring_b, saved, mom, grad = refs[4:]
    size_x, size_y = sizes
    lay_far(
        (first_near_ref, second_near_ref),
        (first_far_ref, second_far_ref),
        (pop_a, ring_a, wide, field),
    )

    at_x, at_y = lax.axis_index("gx"), lax.axis_index("gy")
    edges = (
        jnp.where(at_x == 0, 1, 0),
        jnp.where(at_x == size_x - 1, 1, 0),
        jnp.where(at_y == 0, 1, 0),
        jnp.where(at_y == size_y - 1, 1, 0),
    )
    row, lane, column, depth = iotas()
    after = row < 4

    def masks_of(tile, first, r):
        return wall_masks(r == 0, tile == first, tile == first + 1, edges)

    def neighbours(tile, tiles):
        if isinstance(tile, int):
            return {0: tile, -1: (tile - 1) % tiles, 1: (tile + 1) % tiles}
        return {0: tile, -1: lax.rem(tile + tiles - 1, tiles), 1: lax.rem(tile + 1, tiles)}

    def from_wide(ref, tile, r):
        step = neighbours(tile, 5)

        def load(i, tile_step, row_step, move):
            at = 5 * i + step[tile_step]
            before, own, behind = (ref[at, pl.ds(ROWS * n + row_step, ROWS), :] for n in (1, 2, 3))
            return (own, jnp.where(after, behind, before), before, behind)[r]

        return load

    def from_ring(ref, tile, tiles, r):
        step = neighbours(tile, tiles)

        def load(i, tile_step, row_step, move):
            rows = own_rows(row_step) if r == 0 else halo_rows(row_step)
            return ref[tiles * i + step[tile_step], rows, :]

        return load

    def from_outer(ref, r):
        def load(i, tile_step, row_step, move):
            rows = own_rows(row_step) if r == 0 else halo_rows(row_step)
            if tile_step:
                return ref[4 * i + (2 if tile_step < 0 else 1), rows, :]
            cut = {0: 2, 1: 1, -1: 3}[move]
            return jnp.where(column < cut, ref[4 * i + 3, rows, :], ref[4 * i, rows, :])

        return load

    def note(s, tile, r, parts):
        for n, value in enumerate(parts[2:4] + tuple(parts[4])):
            mom[s - 1, n, tile, r] = value

    def first_step(tile, carry):
        place = lax.rem(tile + 4, 5)
        halo = []
        for r in (2, 0, 3):
            f = stream_tile(from_wide(pop_a, tile, r), 1, masks_of(tile, 2, r), lane)
            parts = moments(f)
            if r == 0:
                note(1, place, 0, parts)
                for i in range(Q):
                    saved[0, i, place] = f[i]
            else:
                halo.append(parts[2:4] + tuple(parts[4]))
            at = {2: 0, 0: 1, 3: 2}[r]
            g = collide(f, wide[0, tile, at], wide[1, tile, at], parts)
            for i in range(Q):
                pop_b[5 * i + tile, pl.ds(ROWS * (at + 1), ROWS), :] = g[i]
        for n in range(5):
            mom[0, n, place, 1] = jnp.where(after, halo[1][n], halo[0][n])
        return carry

    lax.fori_loop(0, 5, first_step, 0, unroll=True)

    def second_step(tile, carry):
        out = []
        for r in range(2):
            f = stream_tile(from_wide(pop_b, tile + 1, r), 1, masks_of(tile, 1, r), lane)
            parts = moments(f)
            note(2, tile, r, parts)
            if r == 0:
                for i in range(Q):
                    saved[1, i, tile] = f[i]
            out.append(collide(f, field[2, tile, r], field[0, tile, r], parts))
        for i in range(Q):
            put_ring(ring_b, 4 * i + tile, out[0][i], out[1][i])
        return carry

    lax.fori_loop(0, 4, second_step, 0, unroll=True)

    def third_step(tile, carry):
        for r in range(2):
            f = stream_tile(from_ring(ring_b, tile, 4, r), 1, masks_of(tile, 1, r), lane)
            note(3, tile, r, moments(f))
            if r == 0:
                for i in range(Q):
                    saved[2, i, tile] = f[i]
        return carry

    lax.fori_loop(0, 4, third_step, 0, unroll=True)

    def back_tile(load, s, tile, r, own):
        b = stream_tile(load, -1, masks_of(4 if tile is None else tile, 1, r), lane)

        def read(get):
            return jnp.where(column < 2, get(3), get(0)) if tile is None else get(tile)

        rho, rinv, *u = [read(lambda at: mom[s - 1, n, at, r]) for n in range(5)]
        kind, phi = read(lambda at: field[s, at, r]), read(lambda at: field[0, at, r])
        state = [saved[s - 1, i, tile] for i in range(Q)] if own else None
        back, term = collide_back(b, kind, phi, rho, rinv, u, state)
        if own:
            grad[tile] = term if s == 3 else grad[tile] + term
        return back

    def last_step(tile, carry):
        out = [back_tile(from_ring(ring_a, tile, 4, r), 3, tile, r, r == 0) for r in range(2)]
        for i in range(Q):
            put_ring(ring_b, 4 * i + tile, out[0][i], out[1][i])
        return carry

    lax.fori_loop(0, 4, last_step, 0, unroll=True)

    for k, tile in enumerate((1, 2, None)):
        out = []
        for r in range(2):
            load = from_outer(ring_b, r) if tile is None else from_ring(ring_b, tile, 4, r)
            out.append(back_tile(load, 2, tile, r, r == 0 and tile is not None))
        for i in range(Q):
            put_ring(ring_a, 3 * i + k, out[0][i], out[1][i])

    for k, tile in enumerate((1, 2, None)):
        out = []
        for r in range(2):
            load = from_ring(ring_a, k, 3, r)
            out.append(back_tile(load, 1, tile, r, r == 0 and tile is not None))
        for i in range(Q):
            put_ring(ring_b, 3 * i + k, out[0][i], out[1][i])

    panel = lax.broadcasted_iota(jnp.int32, panel_ref.shape, 1)
    sums = jnp.zeros(panel_ref.shape, jnp.float32)
    for t in range(2):
        b = stream_tile(from_ring(ring_b, t, 3, 0), -1, masks_of(t, 0, 0), lane)
        f = [state_ref[2 * i + t] for i in range(Q)]
        kind, phi = own_field_ref[t], own_field_ref[2 * OWN_PHI + t]
        _, _, rho, rinv, u = moments(f)
        back, term = collide_back(b, kind, phi, rho, rinv, u, f)
        for i in range(Q):
            adjoint_ref[i, :, pl.ds(t * LANES, LANES)] = back[i]
        term = term + grad[t + 1]
        for part in range(2):
            amount = jnp.sum(jnp.where((row < 4) == (part == 0), term, 0.0))
            name = names_ref[t, 4 * part : 4 * part + 1, 0:1]
            sums = sums + jnp.where(panel == name, amount, 0.0)
    panel_ref[...] = sums


def finish(parts_ref, adjoint_ref, sums_hbm, adjoint_hbm, sums_ref, sems):
    adjoint_copy = pltpu.make_async_copy(adjoint_ref, adjoint_hbm, sems.at[0])
    adjoint_copy.start()
    sums_ref[...] = jnp.sum(parts_ref[...], axis=0)
    sums_copy = pltpu.make_async_copy(sums_ref, sums_hbm, sems.at[1])
    sums_copy.start()
    sums_copy.wait()
    adjoint_copy.wait()


VMEM = pl.BlockSpec(memory_space=pltpu.VMEM)
HBM = pl.BlockSpec(memory_space=pltpu.HBM)


def shape_of(*dims):
    return jax.ShapeDtypeStruct(dims, jnp.float32)


def tiles_of(count):
    return shape_of(count, ROWS, LANES)


def on_device(sizes, checkpoint, cotangent, cell_codes, porosity, baffle_index):
    size_x, size_y = sizes
    panels = porosity.shape[0]
    devices = size_x * size_y
    y_layout, near_layout, far_layout = layouts()

    params = pltpu.CompilerParams(vmem_limit_bytes=32 * 1024 * 1024)

    def call(kernel, out_shape, in_specs, scratch=(), name=None, aliases={}):
        return pl.pallas_call(
            kernel,
            out_shape=out_shape,
            in_specs=in_specs,
            out_specs=jax.tree.map(lambda _: VMEM, out_shape),
            scratch_shapes=scratch,
            input_output_aliases=aliases,
            compiler_params=params,
            name=name,
        )

    def swap(value, axis, size):
        return lax.ppermute(value, axis, [(i, i ^ 1) for i in range(size) if i ^ 1 < size])

    def swap_between(value, axis, size):
        pairs = [(i, i + 1) for i in range(1, size - 1, 2)]
        return lax.ppermute(value, axis, pairs + [(j, i) for i, j in pairs])

    def swap_inner(value):
        pairs = [
            (i * size_y + y, (i + 1) * size_y + y)
            for i in range(1, size_x - 1, 2)
            for y in range(1, size_y - 1)
        ]
        return lax.ppermute(value, ("gx", "gy"), pairs + [(j, i) for i, j in pairs])

    arguments = [
        pltpu.with_memory_space_constraint(value, pltpu.HBM)
        for value in (checkpoint, cotangent, cell_codes, baffle_index, porosity)
    ]
    near_y, far_y, own, state, cot, field, names = call(
        pack_own,
        (tiles_of(y_layout.size),) * 2
        + (tiles_of(2 * Q),) * 3
        + (tiles_of(2 * OWN_PHI + 2), jax.ShapeDtypeStruct((2, ROWS, LANES), jnp.int32)),
        [HBM] * 5,
        [
            pltpu.VMEM((Q, ROWS, 2 * LANES), jnp.float32),
            pltpu.VMEM((Q, ROWS, 2 * LANES), jnp.float32),
            pltpu.VMEM((STEPS, ROWS, 2 * LANES), jnp.int32),
            pltpu.SMEM(baffle_index.shape, jnp.int32),
            pltpu.SMEM(porosity.shape, jnp.float32),
            pltpu.SemaphoreType.DMA((5,)),
        ],
        name="pack_own",
    )(*arguments)
    near_y = swap(near_y, "gy", size_y)
    far_y = swap_between(far_y, "gy", size_y)
    first_near, second_near = call(
        pack_near,
        (tiles_of(near_layout.size), tiles_of(near_layout.size + 1)),
        [VMEM] * 4,
        name="pack_near",
    )(own, cot, field, near_y)
    second_near = swap_between(second_near, "gx", size_x)
    first_near = swap(first_near, "gx", size_x)
    first_far, second_far = call(
        pack_far,
        (tiles_of(far_layout.size), tiles_of(far_layout.size + 1)),
        [VMEM],
        name="pack_far",
    )(far_y)
    second_far = swap_inner(second_far)
    first_far = swap(first_far, "gx", size_x)
    spaces = (
        shape_of(5 * Q, 5 * ROWS, LANES),
        shape_of(4 * Q, 3 * ROWS, LANES),
        shape_of(2, 5, 3, ROWS, LANES),
        shape_of(4, 4, 2, ROWS, LANES),
    )
    laid = call(lay_out, spaces, [VMEM] * 7, name="lay_out")(
        near_y, far_y, first_near, second_near, own, field, cot
    )
    adjoint, sums, *_ = call(
        functools.partial(steps_kernel, sizes),
        (pltpu.VMEM((Q, ROWS, 2 * LANES), jnp.float32), shape_of(devices, panels)) + spaces,
        [VMEM] * 11,
        [
            pltpu.VMEM((5 * Q, 5 * ROWS, LANES), jnp.float32),
            pltpu.VMEM((4 * Q, 3 * ROWS, LANES), jnp.float32),
            pltpu.VMEM((3, Q, 5, ROWS, LANES), jnp.float32),
            pltpu.VMEM((3, 5, 5, 2, ROWS, LANES), jnp.float32),
            pltpu.VMEM((4, ROWS, LANES), jnp.float32),
        ],
        name="steps",
        aliases={7 + n: 2 + n for n in range(4)},
    )(state, field, names, first_near, second_near, first_far, second_far, *laid)
    gathered = lax.all_to_all(sums, ("gx", "gy"), 0, 0, tiled=True)
    totals, adjoint = pl.pallas_call(
        finish,
        out_shape=(shape_of(1, panels), shape_of(Q, ROWS, 2 * LANES)),
        in_specs=[VMEM, VMEM],
        out_specs=(HBM, HBM),
        scratch_shapes=[pltpu.VMEM((1, panels), jnp.float32), pltpu.SemaphoreType.DMA((2,))],
        compiler_params=params,
        name="finish",
    )(gathered.reshape(devices, 1, panels), adjoint)
    return adjoint, totals.reshape(panels)


def solution(mesh):
    sizes = (mesh.shape["gx"], mesh.shape["gy"])
    in_specs = (P(None, "gx", "gy"), P(None, "gx", "gy"), P(None, "gx", "gy"), P(), P("gx", "gy"))
    out_specs = (P(None, "gx", "gy"), P())
    return jax.shard_map(
        functools.partial(on_device, sizes),
        mesh=mesh,
        in_specs=in_specs,
        out_specs=out_specs,
        check_vma=False,
    )
```

```python
import functools

import jax
import jax.numpy as jnp
import numpy as np
from jax import lax
from jax.experimental import pallas as pl
from jax.experimental.pallas import tpu as pltpu
from jax.sharding import PartitionSpec as P

Q = 19
STEPS = 4
NZ = 32
ROWS = 8
LANES = 128
OMEGA = 1.6
ACCEL = (0.002, 0.0, -0.003)
SHIFT = tuple(a / OMEGA for a in ACCEL)

VELOCITIES = [
    (0, 0, 0),
    (1, 0, 0),
    (-1, 0, 0),
    (0, 1, 0),
    (0, -1, 0),
    (0, 0, 1),
    (0, 0, -1),
    (1, 1, 0),
    (-1, -1, 0),
    (1, -1, 0),
    (-1, 1, 0),
    (1, 0, 1),
    (-1, 0, -1),
    (1, 0, -1),
    (-1, 0, 1),
    (0, 1, 1),
    (0, -1, -1),
    (0, 1, -1),
    (0, -1, 1),
]
OPPOSITE = [0, 2, 1, 4, 3, 6, 5, 8, 7, 10, 9, 12, 11, 14, 13, 16, 15, 18, 17]
PAIRS = [(i, i + 1) for i in range(1, Q, 2)]
W_REST, W_AXIS, W_DIAG = 1.0 / 3.0, 1.0 / 18.0, 1.0 / 36.0

Y_CODE1, Y_CODE2, Y_CODE3, Y_POP, Y_COT = 38, 39, 40, 41, 42
Y_TILES = 43
X_EXTRA = 19
X_LANE = 20
X_HALVES = 10


def x_places(lanes):
    ring = X_LANE * lanes
    code13 = ring + X_HALVES
    code2 = code13 + lanes
    return ring, code13, code2, code2 + (lanes + 1) // 2


EMPTY = 25
FREE = NZ - EMPTY
WEIGHTS = [W_REST] + [W_AXIS] * 6 + [W_DIAG] * 12
LEVEL = [i for i, v in enumerate(VELOCITIES) if v[2] < 1]
OWN_PHI = 4


def turned(axis, outward):
    return [i for i, v in enumerate(VELOCITIES) if v[axis] == outward and sum(map(abs, v)) == 2]


def total(values):
    values = list(values)
    while len(values) > 1:
        values = [a + b for a, b in zip(values[::2], values[1::2])] + (
            [values[-1]] if len(values) % 2 else []
        )
    return values[0]


def along(vector, three):
    terms = None
    for c, value in zip(vector, three):
        if c == 0:
            continue
        if terms is None:
            terms = value if c > 0 else -value
        else:
            terms = terms + value if c > 0 else terms - value
    return terms


def moments(f):
    plus = {i: f[i] + f[o] for i, o in PAIRS}
    minus = {i: f[i] - f[o] for i, o in PAIRS}
    rho = total([f[0]] + [plus[i] for i, _ in PAIRS])
    rinv = 1.0 / rho
    u = []
    for axis in range(3):
        terms = [
            minus[i] if VELOCITIES[i][axis] > 0 else -minus[i]
            for i, _ in PAIRS
            if VELOCITIES[i][axis] != 0
        ]
        u.append(total(terms) * rinv + SHIFT[axis])
    return plus, minus, rho, rinv, u


def coefficients(kind, phi, rinv):
    baffle = kind == 3.0
    gas = kind == 0.0
    even = jnp.where(gas, 0.0, jnp.where(baffle, 0.5 - 0.5 * OMEGA * phi, 0.5 * (1.0 - OMEGA)))
    odd = jnp.where(
        gas, 0.0, jnp.where(baffle, (1.0 - 0.5 * OMEGA) * phi - 0.5, 0.5 * (1.0 - OMEGA))
    )
    slope = jnp.where(
        baffle,
        OMEGA * phi,
        jnp.where(kind == 1.0, OMEGA, jnp.where(kind == 2.0, OMEGA * rinv, 0.0)),
    )
    return even, odd, slope


def collide(f, kind, phi, parts):
    plus, minus, rho, rinv, u = parts
    even, odd, slope = coefficients(kind, phi, rinv)
    scale = slope * rho
    rest = 1.0 - 1.5 * (u[0] * u[0] + u[1] * u[1] + u[2] * u[2])
    base = scale * rest + jnp.where(kind == 0.0, 1.0, 0.0)
    out = [None] * Q
    out[0] = 2.0 * even * f[0] + W_REST * base
    for weight, pairs in ((W_AXIS, PAIRS[:3]), (W_DIAG, PAIRS[3:])):
        flat = weight * base
        three = (3.0 * weight) * scale
        for i, o in pairs:
            cu = along(VELOCITIES[i], u)
            lin = three * cu
            ev = even * plus[i] + (flat + 1.5 * lin * cu)
            od = odd * minus[i] + lin
            out[i] = ev + od
            out[o] = ev - od
    return out


def collide_back(b, kind, phi, rho, rinv, u, state=None):
    even, odd, slope = coefficients(kind, phi, rinv)
    plus = {i: b[i] + b[o] for i, o in PAIRS}
    minus = {i: b[i] - b[o] for i, o in PAIRS}
    rest = 1.0 - 1.5 * (u[0] * u[0] + u[1] * u[1] + u[2] * u[2])
    u_half = [1.5 * c for c in u]
    weighted = W_REST * b[0]
    energy = 0.0
    vector = [0.0, 0.0, 0.0]
    for weight, pairs in ((W_AXIS, PAIRS[:3]), (W_DIAG, PAIRS[3:])):
        weighted = weighted + weight * total([plus[i] for i, _ in pairs])
        energies, parts = [], ([], [], [])
        for i, _ in pairs:
            cu = along(VELOCITIES[i], u)
            half = along(VELOCITIES[i], u_half) * plus[i]
            first = minus[i] + half
            energies.append(cu * first)
            second = first + half
            for axis in range(3):
                c = VELOCITIES[i][axis]
                if c:
                    parts[axis].append(second if c > 0 else -second)
        energy = energy + (3.0 * weight) * total(energies)
        vector = [vector[k] + (3.0 * weight) * total(parts[k]) for k in range(3)]
    energy = energy + rest * weighted
    vector = [vector[k] - (3.0 * weighted) * u[k] for k in range(3)]
    push = [slope * v for v in vector]
    inner = total([push[k] * (u[k] - SHIFT[k]) for k in range(3)])
    shared = jnp.where(kind == 2.0, 0.0, slope) * energy - inner
    out = [None] * Q
    out[0] = 2.0 * even * b[0] + shared
    for i, o in PAIRS:
        ev = even * plus[i] + shared
        od = odd * minus[i] + along(VELOCITIES[i], push)
        out[i] = ev + od
        out[o] = ev - od
    if state is None:
        return out, None
    evens = total([plus[i] * (state[i] + state[o]) for i, o in PAIRS])
    odds = total([minus[i] * (state[i] - state[o]) for i, o in PAIRS])
    term = (
        -OMEGA * (b[0] * state[0] + 0.5 * evens)
        + (1.0 - 0.5 * OMEGA) * odds
        + OMEGA * rho * energy
    )
    return out, jnp.where(kind == 3.0, term, 0.0)


def wall_masks(sign_rows, own_low, own_high, edges):
    lane = lax.broadcasted_iota(jnp.int32, (ROWS, LANES), 1)
    row = lax.broadcasted_iota(jnp.int32, (ROWS, LANES), 0)
    x_low, x_high, y_low, y_high = edges
    depth = lane % NZ
    masks = {}
    masks[2, 1] = depth == 0
    masks[2, -1] = depth == NZ - 1
    masks[1, 1] = lane < jnp.where(own_low, y_low * NZ, 0)
    masks[1, -1] = lane >= jnp.where(own_high, LANES - y_high * NZ, LANES)
    if sign_rows:
        masks[0, 1] = row < x_low
        masks[0, -1] = row >= ROWS - x_high
    return masks


def stream_tile(load, sign, masks, lane):
    cross_low, cross_high = lane >= LANES - NZ, lane < NZ
    combined = {}
    out = []
    for i, vector in enumerate(VELOCITIES):
        v = tuple(sign * c for c in vector)
        value = load(i, 0, -v[0], v[1])
        if v[1] == 1:
            value = jnp.where(cross_low, load(i, -1, -v[0], 1), value)
        elif v[1] == -1:
            value = jnp.where(cross_high, load(i, 1, -v[0], -1), value)
        amount = (v[1] * NZ + v[2]) % LANES
        if amount:
            value = pltpu.roll(value, amount, 1)
        outside = None
        if v not in combined:
            for axis in range(3):
                if v[axis] and (axis, v[axis]) in masks:
                    wall = masks[axis, v[axis]]
                    outside = wall if outside is None else outside | wall
            combined[v] = outside
        outside = combined[v]
        if outside is not None:
            value = jnp.where(outside, load(OPPOSITE[i], 0, 0, 0), value)
        out.append(value)
    return out


def iotas():
    row = lax.broadcasted_iota(jnp.int32, (ROWS, LANES), 0)
    lane = lax.broadcasted_iota(jnp.int32, (ROWS, LANES), 1)
    return row, lane, lane // NZ, lane % NZ


def columns(value, count):
    amount = (count * NZ) % LANES
    return pltpu.roll(value, amount, 1) if amount else value


def lines(value, count):
    amount = count % ROWS
    return pltpu.roll(value, amount, 0) if amount else value


class Layout:
    def __init__(self, count, guests, fills):
        self.fills = fills
        hosts = [at for at in fills if at not in guests]
        self.hosts = {at: hosts[4 * n : 4 * n + 4] for n, at in enumerate(guests)}
        self.guests = guests
        kept = [at for at in range(count) if at not in guests]
        self.place = {at: n for n, at in enumerate(kept)}
        self.size = len(kept)


class Packing:
    def __init__(self, ref, layout):
        self.ref, self.layout, self.held = ref, layout, {}

    def __setitem__(self, at, value):
        if at in self.layout.guests:
            self.held[at] = value
        else:
            self.ref[self.layout.place[at]] = value

    def finish(self):
        row, lane, column, depth = iotas()
        spare = depth >= EMPTY
        for at, value in self.held.items():
            for k, host in enumerate(self.layout.hosts[at]):
                place = self.layout.place[host]
                moved = pltpu.roll(value, EMPTY - FREE * k, 1)
                self.ref[place] = jnp.where(spare, moved, self.ref[place])
        for place in range(self.layout.size, self.ref.shape[0]):
            self.ref[place] = jnp.zeros((ROWS, LANES), jnp.float32)


class Unpacking:
    def __init__(self, source, layout):
        self.source, self.layout, self.cache = source, layout, {}
        self.changed = set(layout.guests).union(*layout.hosts.values())

    def __getitem__(self, at):
        if at not in self.cache:
            self.cache[at] = self.read(at)
        return self.cache[at]

    def read(self, at):
        row, lane, column, depth = iotas()
        layout = self.layout
        if at in layout.guests:
            value = None
            for k, host in enumerate(layout.hosts[at]):
                tile = self.source[layout.place[host]]
                moved = pltpu.roll(tile, LANES - (EMPTY - FREE * k), 1)
                value = moved if value is None else jnp.where(depth >= FREE * k, moved, value)
        else:
            value = self.source[layout.place[at]]
        if at in self.changed:
            value = jnp.where(depth >= EMPTY, layout.fills[at], value)
        return value


def layouts():
    y_fills = {2 * i + t: WEIGHTS[i] for i in LEVEL for t in range(2)}
    y_fills.update({Y_POP: W_DIAG, Y_CODE2: 0.0})
    out = [Layout(Y_TILES, [2 * i for i in LEVEL[:6]], y_fills)]
    for lanes, count in ((3, 10), (1, 4)):
        ring, _, code2, tiles = x_places(lanes)
        fills = {ring + n: WEIGHTS[2 * n] for n in range(1, X_HALVES)}
        fills.update({at: 0.0 for at in range(code2, tiles)})
        fills.update({X_LANE * n + i: WEIGHTS[i] for n in range(lanes) for i in LEVEL})
        guests = [X_LANE * (lanes - 1) + i for i in LEVEL[:count]]
        out.append(Layout(tiles, guests, fills))
    return out


class Pick:
    def __init__(self, flag, first, second):
        self.flag, self.first, self.second = flag, first, second

    def __getitem__(self, at):
        return jnp.where(self.flag, self.first[at], self.second[at])


class Deal:
    def __init__(self, even, first, second, layout, skip=0):
        self.even, self.skip, self.held = even, skip, {}
        self.first, self.second = Packing(first, layout), Packing(second, layout)

    def put(self, way, at, value):
        if (-way, at) not in self.held:
            self.held[way, at] = value
            return
        other = self.held.pop((-way, at))
        up, down = (value, other) if way == 1 else (other, value)
        self.first[at - self.skip] = jnp.where(self.even, up, down)
        self.second[at - self.skip] = jnp.where(self.even, down, up)

    def put_both(self, at, value):
        self.first[at - self.skip] = value
        self.second[at - self.skip] = value

    def finish(self):
        self.first.finish()
        self.second.finish()


def is_even(axis):
    return lax.rem(lax.axis_index(axis), 2) == 0


def pack_own(
    f_hbm,
    cot_hbm,
    codes_hbm,
    panels_hbm,
    porosity_hbm,
    first_ref,
    second_ref,
    own_ref,
    state_ref,
    own_cot_ref,
    field_ref,
    names_ref,
    f_ref,
    cot_ref,
    codes_ref,
    panels_ref,
    porosity_ref,
    sems,
):
    pieces = (
        (panels_hbm, panels_ref),
        (porosity_hbm, porosity_ref),
        (f_hbm, f_ref),
        (codes_hbm, codes_ref),
        (cot_hbm, cot_ref),
    )
    copies = [
        pltpu.make_async_copy(source, target, sems.at[n])
        for n, (source, target) in enumerate(pieces)
    ]
    for copy in copies:
        copy.start()
    for copy in copies[:4]:
        copy.wait()
    deal = Deal(is_even("gy"), first_ref, second_ref, layouts()[0])
    row, lane, column, depth = iotas()
    top = depth == NZ - 1

    def tile_of(ref, i, t):
        return ref[i, :, pl.ds(t * LANES, LANES)]

    codes, phis = [], []
    for t in range(2):
        names = panels_ref[0, t * LANES], panels_ref[4, t * LANES]
        phi = jnp.where(row < 4, porosity_ref[names[0]], porosity_ref[names[1]])
        names_ref[t] = jnp.where(row < 4, names[0], names[1])
        kinds = [tile_of(codes_ref, s, t).astype(jnp.float32) for s in range(STEPS)]
        f = [tile_of(f_ref, i, t) for i in range(Q)]
        g = collide(f, kinds[0], phi, moments(f))
        for i in range(Q):
            own_ref[2 * i + t] = g[i]
            state_ref[2 * i + t] = f[i]
        for s in range(STEPS):
            field_ref[2 * s + t] = kinds[s]
        field_ref[2 * OWN_PHI + t] = phi
        codes.append([jnp.where(top, phi, kinds[1]), kinds[2], kinds[3]])
    copies[4].wait()
    for i in range(Q):
        for way in (1, -1):
            near, far = (1, 0) if way == 1 else (0, 1)
            deep = 3 - way * VELOCITIES[i][1]
            cot = tile_of(cot_ref, i, near)
            g_far = own_ref[2 * i + far]
            if way == 1:
                mixed = jnp.where(column >= deep, g_far, columns(cot, deep - 4))
            else:
                mixed = jnp.where(column < 4 - deep, g_far, columns(cot, 4 - deep))
            deal.put(way, 2 * i, mixed if far == 0 else own_ref[2 * i])
            deal.put(way, 2 * i + 1, mixed if far == 1 else own_ref[2 * i + 1])
    for way in (1, -1):
        near, far = (1, 0) if way == 1 else (0, 1)
        outer = 3 if way == 1 else 0
        deal.put(way, Y_CODE1, codes[near][0])
        deal.put(way, Y_CODE2, codes[near][1])
        outside = columns(codes[far][0], 3 - 2 * outer)
        deal.put(way, Y_CODE3, jnp.where(column == 3 - outer, outside, codes[near][2]))
        extra = None
        for k, i in enumerate(turned(1, -way)):
            value = columns(own_ref[2 * i + far], k - outer)
            extra = value if extra is None else jnp.where(column == k, value, extra)
        deal.put(way, Y_POP, extra)
        extra = None
        for k, i in enumerate(turned(1, way)):
            value = columns(tile_of(cot_ref, i, near), k - (1 if way == 1 else 2))
            extra = value if extra is None else jnp.where(column == k, value, extra)
        deal.put(way, Y_COT, extra)
    deal.finish()
    for t in range(2):
        for i in range(Q):
            own_cot_ref[2 * i + t] = tile_of(cot_ref, i, t)


def by_parity(body):
    even = is_even("gy")
    pl.when(even)(lambda: body(True))
    pl.when(jnp.logical_not(even))(lambda: body(False))


def half_lanes(right):
    row, lane, column, depth = iotas()
    return lane < LANES // 2 if right else lane >= LANES // 2


def from_y(message_ref, right):
    row, lane, column, depth = iotas()
    ref = Unpacking(message_ref, layouts()[0])
    way, place, far = (-1, 2, 1) if right else (1, 1, 0)

    def population(i):
        return ref[2 * i + 1 - far]

    def cotangent(i):
        deep = 3 - way * VELOCITIES[i][1]
        value = columns(ref[2 * i + far], way * (4 - deep))
        if i in turned(1, way):
            extra = columns(ref[Y_COT], place - turned(1, way).index(i))
            value = jnp.where(column == place, extra, value)
        return value

    def codes(s):
        return ref[(Y_CODE1, Y_CODE2, Y_CODE3)[s - 1]]

    def outer(i):
        if i in turned(1, -way):
            return columns(ref[Y_POP], (0 if right else 3) - turned(1, -way).index(i))
        return ref[2 * i + far]

    def outer_code():
        return columns(ref[Y_CODE3], 1 if right else 3)

    return population, cotangent, codes, outer, outer_code


def mix_lines(deal, at, pop, cot, deep, way):
    row, lane, column, depth = iotas()
    if way == 1:
        mixed = jnp.where(row >= deep, pop, lines(cot, deep))
    else:
        mixed = jnp.where(row < ROWS - deep, pop, lines(cot, -deep))
    deal.put(way, at, mixed)


def pack_lines(deal, first, population, cotangent):
    row, lane, column, depth = iotas()

    for i in range(Q):
        pop, cot = population(i), cotangent(i)
        for way in (1, -1):
            mix_lines(deal, first + i, pop, cot, 3 - way * VELOCITIES[i][0], way)
    for way in (1, -1):
        extra = None
        for k, i in enumerate(turned(0, -way)):
            value = lines(population(i), k - (3 if way == 1 else 4))
            extra = value if extra is None else jnp.where(row == k, value, extra)
        for k, i in enumerate(turned(0, way)):
            value = lines(cotangent(i), 4 + k - (5 if way == 1 else 2))
            extra = jnp.where(row == 4 + k, value, extra)
        deal.put(way, first + X_EXTRA, extra)


def pack_neighbour(deal, lanes, message_ref, right):
    ring, code13, code2, tiles = x_places(lanes)
    population, cotangent, codes, outer, outer_code = from_y(message_ref, right)
    pack_lines(deal, X_LANE * (lanes - 1), population, cotangent)
    kept = half_lanes(right)
    for n in range(X_HALVES):
        first, second = (outer(2 * n - 1), outer(2 * n)) if n else (outer(0), outer_code())
        deal.put_both(ring + n, jnp.where(kept, first, pltpu.roll(second, LANES // 2, 1)))
    for way in (1, -1):
        mix_lines(deal, code13 + lanes - 1, codes(1), codes(3), 3, way)
    deal.put_both(tiles - 1, codes(2))


def pack_near(own_ref, cot_ref, field_ref, message_ref, first_ref, second_ref):
    row, lane, column, depth = iotas()
    deal = Deal(is_even("gx"), first_ref, second_ref, layouts()[1])
    ring, code13, code2, tiles = x_places(3)
    for t in range(2):
        pack_lines(
            deal,
            X_LANE * t,
            lambda i: own_ref[2 * i + t],
            lambda i: cot_ref[2 * i + t],
        )
        code = jnp.where(depth == NZ - 1, field_ref[2 * OWN_PHI + t], field_ref[2 + t])
        for way in (1, -1):
            mix_lines(deal, code13 + t, code, field_ref[6 + t], 3, way)
    first, second = field_ref[4], lines(field_ref[5], 4)
    deal.put(1, code2, jnp.where(row >= 4, first, second))
    deal.put(-1, code2, jnp.where(row < 4, first, second))

    def neighbour(even):
        pack_neighbour(deal, 3, message_ref, even)
        deal.finish()

    by_parity(neighbour)


def pack_far(message_ref, first_ref, second_ref):
    even_x = is_even("gx")

    def neighbour(even):
        deal = Deal(even_x, first_ref, second_ref, layouts()[2])
        pack_neighbour(deal, 1, message_ref, not even)
        deal.finish()

    by_parity(neighbour)


def from_x(ref, n, way, lanes):
    row, lane, column, depth = iotas()
    ring, code13, code2, _ = x_places(lanes)
    first = X_LANE * n

    def population(i):
        value = ref[first + i]
        if i in turned(0, -way):
            place = 3 if way == 1 else 4
            extra = lines(ref[first + X_EXTRA], place - turned(0, -way).index(i))
            value = jnp.where(row == place, extra, value)
        return value

    def cotangent(i):
        value = lines(ref[first + i], -way * (3 - way * VELOCITIES[i][0]))
        if i in turned(0, way):
            place = 5 if way == 1 else 2
            extra = lines(ref[first + X_EXTRA], place - 4 - turned(0, way).index(i))
            value = jnp.where(row == place, extra, value)
        return value

    def codes(s):
        if s == 2:
            return lines(ref[code2 + n // 2], 4 * (n % 2))
        value = ref[code13 + n]
        return value if s == 1 else lines(value, -3 * way)

    def outer(i):
        value = ref[ring + (i + 1) // 2]
        return pltpu.roll(value, LANES // 2, 1) if i and i % 2 == 0 else value

    def outer_code():
        return pltpu.roll(ref[ring], LANES // 2, 1)

    return population, cotangent, codes, outer, outer_code


def sides(first_ref, second_ref, axis, layout):
    even = is_even(axis)
    picks = Pick(even, second_ref, first_ref), Pick(even, first_ref, second_ref)
    return [Unpacking(pick, layout) for pick in picks]


def own_rows(step=0):
    return pl.ds(ROWS + step, ROWS)


def halo_rows(step=0):
    return pl.ds({0: 2 * ROWS, -1: 2 * ROWS - 1, 1: 1}[step], ROWS)


def put_halo(ref, at, halo):
    ref[at, pl.ds(0, ROWS), :] = halo
    ref[at, halo_rows(), :] = halo


def put_ring(ref, at, own, halo):
    ref[at, own_rows(), :] = own
    put_halo(ref, at, halo)


def expand(code):
    row, lane, column, depth = iotas()
    top = depth == NZ - 1
    phi = jnp.where(top, code, 0.0)
    for step in (1, 2, 4, 8, 16):
        phi = phi + pltpu.roll(phi, LANES - step, 1)
    return jnp.where(top, 0.0, code), phi


def lay_own(c, population, cotangent, codes, code_phi, pop, cot, wide, field):
    for i in range(Q):
        pop[5 * i + c, pl.ds(2 * ROWS, ROWS), :] = population(i)
        if cotangent is not None:
            cot[4 * i + c - 1, own_rows(), :] = cotangent(i)
    for n in range(2):
        wide[n, c, 1] = code_phi[n]
    if cotangent is not None:
        field[0, c - 1, 0], field[1, c - 1, 0] = code_phi[1], code_phi[0]
        for s in (2, 3):
            field[s, c - 1, 0] = codes(s)


def lay_halo(c, below, above, pop, cot, wide, field):
    row, lane, column, depth = iotas()
    before, behind = expand(below[2](1)), expand(above[2](1))
    for n in range(2):
        wide[n, c, 0], wide[n, c, 2] = before[n], behind[n]
    for i in range(Q):
        pop[5 * i + c, pl.ds(ROWS, ROWS), :] = below[0](i)
        pop[5 * i + c, pl.ds(3 * ROWS, ROWS), :] = above[0](i)
        if below[1] is not None:
            put_halo(cot, 4 * i + c - 1, jnp.where(row < 4, above[1](i), below[1](i)))
    if below[1] is not None:
        for n, place in ((0, 1), (1, 0)):
            field[place, c - 1, 1] = jnp.where(row < 4, behind[n], before[n])
        for s in (2, 3):
            field[s, c - 1, 1] = jnp.where(row < 4, above[2](s), below[2](s))


def near_tile(even):
    return 4 if even else 1


def lay_out(
    near_y_ref,
    far_y_ref,
    first_near_ref,
    second_near_ref,
    own_ref,
    field_ref,
    cot_ref,
    pop,
    cot,
    wide,
    field,
):
    spaces = pop, cot, wide, field
    below, above = sides(first_near_ref, second_near_ref, "gx", layouts()[1])
    for t in range(2):
        lay_own(
            2 + t,
            lambda i: own_ref[2 * i + t],
            lambda i: cot_ref[2 * i + t],
            lambda s: field_ref[2 * s + t],
            (field_ref[2 + t], field_ref[2 * OWN_PHI + t]),
            *spaces,
        )
        lay_halo(2 + t, from_x(below, t, 1, 3), from_x(above, t, -1, 3), *spaces)

    def neighbours(even):
        place = near_tile(even)
        below, above = sides(first_near_ref, second_near_ref, "gx", layouts()[1])
        near, far = from_y(near_y_ref, even), from_y(far_y_ref, not even)
        for c, (population, cotangent, codes, _, _) in ((place, near), (5 - place, far)):
            lay_own(c, population, cotangent, codes, expand(codes(1)), *spaces)
        kept = half_lanes(even)
        lay_own(
            0,
            lambda i: jnp.where(kept, near[3](i), far[3](i)),
            None,
            None,
            expand(jnp.where(kept, near[4](), far[4]())),
            *spaces,
        )
        lay_halo(place, from_x(below, 2, 1, 3), from_x(above, 2, -1, 3), *spaces)

    by_parity(neighbours)


def lay_far(even, near_refs, far_refs, spaces):
    nears, fars = (
        [
            from_x(ref, lanes - 1, way, lanes)
            for ref, way in zip(sides(*refs, "gx", layout), (1, -1))
        ]
        for refs, layout, lanes in zip((near_refs, far_refs), layouts()[1:], (3, 1))
    )
    lay_halo(5 - near_tile(even), *fars, *spaces)
    kept = half_lanes(even)
    ring = [
        (
            lambda i, near=near, far=far: jnp.where(kept, near[3](i), far[3](i)),
            None,
            lambda s, near=near, far=far: jnp.where(kept, near[4](), far[4]()),
        )
        for near, far in zip(nears, fars)
    ]
    lay_halo(0, *ring, *spaces)


def steps_kernel(
    sizes,
    state_ref,
    own_field_ref,
    names_ref,
    first_near_ref,
    second_near_ref,
    first_far_ref,
    second_far_ref,
    *refs,
):
    adjoint_ref, panel_ref, pop_a, ring_a, wide, field, pop_b, ring_b, saved, mom, grad = refs[4:]
    size_x, size_y = sizes
    by_parity(
        lambda even: lay_far(
            even,
            (first_near_ref, second_near_ref),
            (first_far_ref, second_far_ref),
            (pop_a, ring_a, wide, field),
        )
    )

    at_x, at_y = lax.axis_index("gx"), lax.axis_index("gy")
    edges = (
        jnp.where(at_x == 0, 1, 0),
        jnp.where(at_x == size_x - 1, 1, 0),
        jnp.where(at_y == 0, 1, 0),
        jnp.where(at_y == size_y - 1, 1, 0),
    )
    row, lane, column, depth = iotas()
    after = row < 4

    def masks_of(tile, first, r):
        return wall_masks(r == 0, tile == first, tile == first + 1, edges)

    def neighbours(tile, tiles):
        if isinstance(tile, int):
            return {0: tile, -1: (tile - 1) % tiles, 1: (tile + 1) % tiles}
        return {0: tile, -1: lax.rem(tile + tiles - 1, tiles), 1: lax.rem(tile + 1, tiles)}

    def from_wide(ref, tile, r):
        step = neighbours(tile, 5)

        def load(i, tile_step, row_step, move):
            at = 5 * i + step[tile_step]
            before, own, behind = (ref[at, pl.ds(ROWS * n + row_step, ROWS), :] for n in (1, 2, 3))
            return (own, jnp.where(after, behind, before), before, behind)[r]

        return load

    def from_ring(ref, tile, tiles, r):
        step = neighbours(tile, tiles)

        def load(i, tile_step, row_step, move):
            rows = own_rows(row_step) if r == 0 else halo_rows(row_step)
            return ref[tiles * i + step[tile_step], rows, :]

        return load

    def from_outer(ref, r):
        def load(i, tile_step, row_step, move):
            rows = own_rows(row_step) if r == 0 else halo_rows(row_step)
            if tile_step:
                return ref[4 * i + (2 if tile_step < 0 else 1), rows, :]
            cut = {0: 2, 1: 1, -1: 3}[move]
            return jnp.where(column < cut, ref[4 * i + 3, rows, :], ref[4 * i, rows, :])

        return load

    def note(s, tile, r, parts):
        for n, value in enumerate(parts[2:4] + tuple(parts[4])):
            mom[s - 1, n, tile, r] = value

    def first_step(tile, carry):
        place = lax.rem(tile + 4, 5)
        halo = []
        for r in (2, 0, 3):
            f = stream_tile(from_wide(pop_a, tile, r), 1, masks_of(tile, 2, r), lane)
            parts = moments(f)
            if r == 0:
                note(1, place, 0, parts)
                for i in range(Q):
                    saved[0, i, place] = f[i]
            else:
                halo.append(parts[2:4] + tuple(parts[4]))
            at = {2: 0, 0: 1, 3: 2}[r]
            g = collide(f, wide[0, tile, at], wide[1, tile, at], parts)
            for i in range(Q):
                pop_b[5 * i + tile, pl.ds(ROWS * (at + 1), ROWS), :] = g[i]
        for n in range(5):
            mom[0, n, place, 1] = jnp.where(after, halo[1][n], halo[0][n])
        return carry

    lax.fori_loop(0, 5, first_step, 0, unroll=True)

    def second_step(tile, carry):
        out = []
        for r in range(2):
            f = stream_tile(from_wide(pop_b, tile + 1, r), 1, masks_of(tile, 1, r), lane)
            parts = moments(f)
            note(2, tile, r, parts)
            if r == 0:
                for i in range(Q):
                    saved[1, i, tile] = f[i]
            out.append(collide(f, field[2, tile, r], field[0, tile, r], parts))
        for i in range(Q):
            put_ring(ring_b, 4 * i + tile, out[0][i], out[1][i])
        return carry

    lax.fori_loop(0, 4, second_step, 0, unroll=True)

    def third_step(tile, carry):
        for r in range(2):
            f = stream_tile(from_ring(ring_b, tile, 4, r), 1, masks_of(tile, 1, r), lane)
            note(3, tile, r, moments(f))
            if r == 0:
                for i in range(Q):
                    saved[2, i, tile] = f[i]
        return carry

    lax.fori_loop(0, 4, third_step, 0, unroll=True)

    def back_tile(load, s, tile, r, own):
        b = stream_tile(load, -1, masks_of(4 if tile is None else tile, 1, r), lane)

        def read(get):
            return jnp.where(column < 2, get(3), get(0)) if tile is None else get(tile)

        rho, rinv, *u = [read(lambda at: mom[s - 1, n, at, r]) for n in range(5)]
        kind, phi = read(lambda at: field[s, at, r]), read(lambda at: field[0, at, r])
        state = [saved[s - 1, i, tile] for i in range(Q)] if own else None
        back, term = collide_back(b, kind, phi, rho, rinv, u, state)
        if own:
            grad[tile] = term if s == 3 else grad[tile] + term
        return back

    def last_step(tile, carry):
        out = [back_tile(from_ring(ring_a, tile, 4, r), 3, tile, r, r == 0) for r in range(2)]
        for i in range(Q):
            put_ring(ring_b, 4 * i + tile, out[0][i], out[1][i])
        return carry

    lax.fori_loop(0, 4, last_step, 0, unroll=True)

    for k, tile in enumerate((1, 2, None)):
        out = []
        for r in range(2):
            load = from_outer(ring_b, r) if tile is None else from_ring(ring_b, tile, 4, r)
            out.append(back_tile(load, 2, tile, r, r == 0 and tile is not None))
        for i in range(Q):
            put_ring(ring_a, 3 * i + k, out[0][i], out[1][i])

    for k, tile in enumerate((1, 2, None)):
        out = []
        for r in range(2):
            load = from_ring(ring_a, k, 3, r)
            out.append(back_tile(load, 1, tile, r, r == 0 and tile is not None))
        for i in range(Q):
            put_ring(ring_b, 3 * i + k, out[0][i], out[1][i])

    panel = lax.broadcasted_iota(jnp.int32, panel_ref.shape, 1)
    sums = jnp.zeros(panel_ref.shape, jnp.float32)
    for t in range(2):
        b = stream_tile(from_ring(ring_b, t, 3, 0), -1, masks_of(t, 0, 0), lane)
        f = [state_ref[2 * i + t] for i in range(Q)]
        kind, phi = own_field_ref[t], own_field_ref[2 * OWN_PHI + t]
        _, _, rho, rinv, u = moments(f)
        back, term = collide_back(b, kind, phi, rho, rinv, u, f)
        for i in range(Q):
            adjoint_ref[i, :, pl.ds(t * LANES, LANES)] = back[i]
        term = term + grad[t + 1]
        for part in range(2):
            amount = jnp.sum(jnp.where((row < 4) == (part == 0), term, 0.0))
            name = names_ref[t, 4 * part : 4 * part + 1, 0:1]
            sums = sums + jnp.where(panel == name, amount, 0.0)
    panel_ref[...] = sums


def finish(parts_ref, adjoint_ref, sums_hbm, adjoint_hbm, sums_ref, sems):
    adjoint_copy = pltpu.make_async_copy(adjoint_ref, adjoint_hbm, sems.at[0])
    adjoint_copy.start()
    sums_ref[...] = jnp.sum(parts_ref[...], axis=0)
    sums_copy = pltpu.make_async_copy(sums_ref, sums_hbm, sems.at[1])
    sums_copy.start()
    sums_copy.wait()
    adjoint_copy.wait()


VMEM = pl.BlockSpec(memory_space=pltpu.VMEM)
HBM = pl.BlockSpec(memory_space=pltpu.HBM)


def shape_of(*dims):
    return jax.ShapeDtypeStruct(dims, jnp.float32)


def tiles_of(count):
    return shape_of(count, ROWS, LANES)


def on_device(sizes, checkpoint, cotangent, cell_codes, porosity, baffle_index):
    size_x, size_y = sizes
    panels = porosity.shape[0]
    devices = size_x * size_y
    y_layout, near_layout, far_layout = layouts()

    params = pltpu.CompilerParams(vmem_limit_bytes=32 * 1024 * 1024)

    def call(kernel, out_shape, in_specs, scratch=(), name=None, aliases={}):
        return pl.pallas_call(
            kernel,
            out_shape=out_shape,
            in_specs=in_specs,
            out_specs=jax.tree.map(lambda _: VMEM, out_shape),
            scratch_shapes=scratch,
            input_output_aliases=aliases,
            compiler_params=params,
            name=name,
        )

    def swap(value, axis, size):
        return lax.ppermute(value, axis, [(i, i ^ 1) for i in range(size) if i ^ 1 < size])

    def swap_between(value, axis, size):
        pairs = [(i, i + 1) for i in range(1, size - 1, 2)]
        return lax.ppermute(value, axis, pairs + [(j, i) for i, j in pairs])

    def swap_inner(value):
        pairs = [
            (i * size_y + y, (i + 1) * size_y + y)
            for i in range(1, size_x - 1, 2)
            for y in range(1, size_y - 1)
        ]
        return lax.ppermute(value, ("gx", "gy"), pairs + [(j, i) for i, j in pairs])

    arguments = [
        pltpu.with_memory_space_constraint(value, pltpu.HBM)
        for value in (checkpoint, cotangent, cell_codes, baffle_index, porosity)
    ]
    near_y, far_y, own, state, cot, field, names = call(
        pack_own,
        (tiles_of(y_layout.size),) * 2
        + (tiles_of(2 * Q),) * 3
        + (tiles_of(2 * OWN_PHI + 2), jax.ShapeDtypeStruct((2, ROWS, LANES), jnp.int32)),
        [HBM] * 5,
        [
            pltpu.VMEM((Q, ROWS, 2 * LANES), jnp.float32),
            pltpu.VMEM((Q, ROWS, 2 * LANES), jnp.float32),
            pltpu.VMEM((STEPS, ROWS, 2 * LANES), jnp.int32),
            pltpu.SMEM(baffle_index.shape, jnp.int32),
            pltpu.SMEM(porosity.shape, jnp.float32),
            pltpu.SemaphoreType.DMA((5,)),
        ],
        name="pack_own",
    )(*arguments)
    near_y = swap(near_y, "gy", size_y)
    far_y = swap_between(far_y, "gy", size_y)
    first_near, second_near = call(
        pack_near,
        (tiles_of(near_layout.size), tiles_of(near_layout.size + 1)),
        [VMEM] * 4,
        name="pack_near",
    )(own, cot, field, near_y)
    second_near = swap_between(second_near, "gx", size_x)
    first_near = swap(first_near, "gx", size_x)
    first_far, second_far = call(
        pack_far,
        (tiles_of(far_layout.size), tiles_of(far_layout.size + 1)),
        [VMEM],
        name="pack_far",
    )(far_y)
    second_far = swap_inner(second_far)
    first_far = swap(first_far, "gx", size_x)
    spaces = (
        shape_of(5 * Q, 5 * ROWS, LANES),
        shape_of(4 * Q, 3 * ROWS, LANES),
        shape_of(2, 5, 3, ROWS, LANES),
        shape_of(4, 4, 2, ROWS, LANES),
    )
    laid = call(lay_out, spaces, [VMEM] * 7, name="lay_out")(
        near_y, far_y, first_near, second_near, own, field, cot
    )
    adjoint, sums, *_ = call(
        functools.partial(steps_kernel, sizes),
        (pltpu.VMEM((Q, ROWS, 2 * LANES), jnp.float32), shape_of(devices, panels)) + spaces,
        [VMEM] * 11,
        [
            pltpu.VMEM((5 * Q, 5 * ROWS, LANES), jnp.float32),
            pltpu.VMEM((4 * Q, 3 * ROWS, LANES), jnp.float32),
            pltpu.VMEM((3, Q, 5, ROWS, LANES), jnp.float32),
            pltpu.VMEM((3, 5, 5, 2, ROWS, LANES), jnp.float32),
            pltpu.VMEM((4, ROWS, LANES), jnp.float32),
        ],
        name="steps",
        aliases={7 + n: 2 + n for n in range(4)},
    )(state, field, names, first_near, second_near, first_far, second_far, *laid)
    gathered = lax.all_to_all(sums, ("gx", "gy"), 0, 0, tiled=True)
    totals, adjoint = pl.pallas_call(
        finish,
        out_shape=(shape_of(1, panels), shape_of(Q, ROWS, 2 * LANES)),
        in_specs=[VMEM, VMEM],
        out_specs=(HBM, HBM),
        scratch_shapes=[pltpu.VMEM((1, panels), jnp.float32), pltpu.SemaphoreType.DMA((2,))],
        compiler_params=params,
        name="finish",
    )(gathered.reshape(devices, 1, panels), adjoint)
    return adjoint, totals.reshape(panels)


def solution(mesh):
    sizes = (mesh.shape["gx"], mesh.shape["gy"])
    in_specs = (P(None, "gx", "gy"), P(None, "gx", "gy"), P(None, "gx", "gy"), P(), P("gx", "gy"))
    out_specs = (P(None, "gx", "gy"), P())
    return jax.shard_map(
        functools.partial(on_device, sizes),
        mesh=mesh,
        in_specs=in_specs,
        out_specs=out_specs,
        check_vma=False,
    )
```

```python
import functools

import jax
import jax.numpy as jnp
import numpy as np
from jax import lax
from jax.experimental import pallas as pl
from jax.experimental.pallas import tpu as pltpu
from jax.sharding import PartitionSpec as P

Q = 19
STEPS = 4
NZ = 32
ROWS = 8
LANES = 128
OMEGA = 1.6
ACCEL = (0.002, 0.0, -0.003)
SHIFT = tuple(a / OMEGA for a in ACCEL)

VELOCITIES = [
    (0, 0, 0),
    (1, 0, 0),
    (-1, 0, 0),
    (0, 1, 0),
    (0, -1, 0),
    (0, 0, 1),
    (0, 0, -1),
    (1, 1, 0),
    (-1, -1, 0),
    (1, -1, 0),
    (-1, 1, 0),
    (1, 0, 1),
    (-1, 0, -1),
    (1, 0, -1),
    (-1, 0, 1),
    (0, 1, 1),
    (0, -1, -1),
    (0, 1, -1),
    (0, -1, 1),
]
OPPOSITE = [0, 2, 1, 4, 3, 6, 5, 8, 7, 10, 9, 12, 11, 14, 13, 16, 15, 18, 17]
PAIRS = [(i, i + 1) for i in range(1, Q, 2)]
W_REST, W_AXIS, W_DIAG = 1.0 / 3.0, 1.0 / 18.0, 1.0 / 36.0

Y_CODE1, Y_CODE2, Y_CODE3, Y_POP, Y_COT = 38, 39, 40, 41, 42
Y_TILES = 43
X_EXTRA = 19
X_LANE = 20
X_HALVES = 10


def x_places(lanes):
    ring = X_LANE * lanes
    code13 = ring + X_HALVES
    code2 = code13 + lanes
    return ring, code13, code2, code2 + (lanes + 1) // 2


EMPTY = 25
FREE = NZ - EMPTY
WEIGHTS = [W_REST] + [W_AXIS] * 6 + [W_DIAG] * 12
LEVEL = [i for i, v in enumerate(VELOCITIES) if v[2] < 1]
OWN_PHI = 4


def turned(axis, outward):
    return [i for i, v in enumerate(VELOCITIES) if v[axis] == outward and sum(map(abs, v)) == 2]


def total(values):
    values = list(values)
    while len(values) > 1:
        values = [a + b for a, b in zip(values[::2], values[1::2])] + (
            [values[-1]] if len(values) % 2 else []
        )
    return values[0]


def along(vector, three):
    terms = None
    for c, value in zip(vector, three):
        if c == 0:
            continue
        if terms is None:
            terms = value if c > 0 else -value
        else:
            terms = terms + value if c > 0 else terms - value
    return terms


def moments(f):
    plus = {i: f[i] + f[o] for i, o in PAIRS}
    minus = {i: f[i] - f[o] for i, o in PAIRS}
    rho = total([f[0]] + [plus[i] for i, _ in PAIRS])
    rinv = 1.0 / rho
    u = []
    for axis in range(3):
        terms = [
            minus[i] if VELOCITIES[i][axis] > 0 else -minus[i]
            for i, _ in PAIRS
            if VELOCITIES[i][axis] != 0
        ]
        u.append(total(terms) * rinv + SHIFT[axis])
    return plus, minus, rho, rinv, u


def coefficients(kind, phi, rinv):
    baffle = kind == 3.0
    gas = kind == 0.0
    even = jnp.where(gas, 0.0, jnp.where(baffle, 0.5 - 0.5 * OMEGA * phi, 0.5 * (1.0 - OMEGA)))
    odd = jnp.where(
        gas, 0.0, jnp.where(baffle, (1.0 - 0.5 * OMEGA) * phi - 0.5, 0.5 * (1.0 - OMEGA))
    )
    slope = jnp.where(
        baffle,
        OMEGA * phi,
        jnp.where(kind == 1.0, OMEGA, jnp.where(kind == 2.0, OMEGA * rinv, 0.0)),
    )
    return even, odd, slope


def collide(f, kind, phi, parts):
    plus, minus, rho, rinv, u = parts
    even, odd, slope = coefficients(kind, phi, rinv)
    scale = slope * rho
    rest = 1.0 - 1.5 * (u[0] * u[0] + u[1] * u[1] + u[2] * u[2])
    base = scale * rest + jnp.where(kind == 0.0, 1.0, 0.0)
    out = [None] * Q
    out[0] = 2.0 * even * f[0] + W_REST * base
    for weight, pairs in ((W_AXIS, PAIRS[:3]), (W_DIAG, PAIRS[3:])):
        flat = weight * base
        three = (3.0 * weight) * scale
        for i, o in pairs:
            cu = along(VELOCITIES[i], u)
            lin = three * cu
            ev = even * plus[i] + (flat + 1.5 * lin * cu)
            od = odd * minus[i] + lin
            out[i] = ev + od
            out[o] = ev - od
    return out


def collide_back(b, kind, phi, rho, rinv, u, state=None):
    even, odd, slope = coefficients(kind, phi, rinv)
    plus = {i: b[i] + b[o] for i, o in PAIRS}
    minus = {i: b[i] - b[o] for i, o in PAIRS}
    rest = 1.0 - 1.5 * (u[0] * u[0] + u[1] * u[1] + u[2] * u[2])
    u_half = [1.5 * c for c in u]
    weighted = W_REST * b[0]
    energy = 0.0
    vector = [0.0, 0.0, 0.0]
    for weight, pairs in ((W_AXIS, PAIRS[:3]), (W_DIAG, PAIRS[3:])):
        weighted = weighted + weight * total([plus[i] for i, _ in pairs])
        energies, parts = [], ([], [], [])
        for i, _ in pairs:
            cu = along(VELOCITIES[i], u)
            half = along(VELOCITIES[i], u_half) * plus[i]
            first = minus[i] + half
            energies.append(cu * first)
            second = first + half
            for axis in range(3):
                c = VELOCITIES[i][axis]
                if c:
                    parts[axis].append(second if c > 0 else -second)
        energy = energy + (3.0 * weight) * total(energies)
        vector = [vector[k] + (3.0 * weight) * total(parts[k]) for k in range(3)]
    energy = energy + rest * weighted
    vector = [vector[k] - (3.0 * weighted) * u[k] for k in range(3)]
    push = [slope * v for v in vector]
    inner = total([push[k] * (u[k] - SHIFT[k]) for k in range(3)])
    shared = jnp.where(kind == 2.0, 0.0, slope) * energy - inner
    out = [None] * Q
    out[0] = 2.0 * even * b[0] + shared
    for i, o in PAIRS:
        ev = even * plus[i] + shared
        od = odd * minus[i] + along(VELOCITIES[i], push)
        out[i] = ev + od
        out[o] = ev - od
    if state is None:
        return out, None
    evens = total([plus[i] * (state[i] + state[o]) for i, o in PAIRS])
    odds = total([minus[i] * (state[i] - state[o]) for i, o in PAIRS])
    term = (
        -OMEGA * (b[0] * state[0] + 0.5 * evens)
        + (1.0 - 0.5 * OMEGA) * odds
        + OMEGA * rho * energy
    )
    return out, jnp.where(kind == 3.0, term, 0.0)


def wall_masks(sign_rows, own_low, own_high, edges):
    lane = lax.broadcasted_iota(jnp.int32, (ROWS, LANES), 1)
    row = lax.broadcasted_iota(jnp.int32, (ROWS, LANES), 0)
    x_low, x_high, y_low, y_high = edges
    depth = lane % NZ
    masks = {}
    masks[2, 1] = depth == 0
    masks[2, -1] = depth == NZ - 1
    masks[1, 1] = lane < jnp.where(own_low, y_low * NZ, 0)
    masks[1, -1] = lane >= jnp.where(own_high, LANES - y_high * NZ, LANES)
    if sign_rows:
        masks[0, 1] = row < x_low
        masks[0, -1] = row >= ROWS - x_high
    return masks


def stream_tile(load, sign, masks, lane):
    cross_low, cross_high = lane >= LANES - NZ, lane < NZ
    combined = {}
    out = []
    for i, vector in enumerate(VELOCITIES):
        v = tuple(sign * c for c in vector)
        value = load(i, 0, -v[0], v[1])
        if v[1] == 1:
            value = jnp.where(cross_low, load(i, -1, -v[0], 1), value)
        elif v[1] == -1:
            value = jnp.where(cross_high, load(i, 1, -v[0], -1), value)
        amount = (v[1] * NZ + v[2]) % LANES
        if amount:
            value = pltpu.roll(value, amount, 1)
        outside = None
        if v not in combined:
            for axis in range(3):
                if v[axis] and (axis, v[axis]) in masks:
                    wall = masks[axis, v[axis]]
                    outside = wall if outside is None else outside | wall
            combined[v] = outside
        outside = combined[v]
        if outside is not None:
            value = jnp.where(outside, load(OPPOSITE[i], 0, 0, 0), value)
        out.append(value)
    return out


def iotas():
    row = lax.broadcasted_iota(jnp.int32, (ROWS, LANES), 0)
    lane = lax.broadcasted_iota(jnp.int32, (ROWS, LANES), 1)
    return row, lane, lane // NZ, lane % NZ


def columns(value, count):
    amount = (count * NZ) % LANES
    return pltpu.roll(value, amount, 1) if amount else value


def lines(value, count):
    amount = count % ROWS
    return pltpu.roll(value, amount, 0) if amount else value


class Layout:
    def __init__(self, count, guests, fills):
        self.fills = fills
        hosts = [at for at in fills if at not in guests]
        self.hosts = {at: hosts[4 * n : 4 * n + 4] for n, at in enumerate(guests)}
        self.guests = guests
        kept = [at for at in range(count) if at not in guests]
        self.place = {at: n for n, at in enumerate(kept)}
        self.size = len(kept)


class Packing:
    def __init__(self, ref, layout):
        self.ref, self.layout, self.held = ref, layout, {}

    def __setitem__(self, at, value):
        if at in self.layout.guests:
            self.held[at] = value
        else:
            self.ref[self.layout.place[at]] = value

    def finish(self):
        row, lane, column, depth = iotas()
        spare = depth >= EMPTY
        for at, value in self.held.items():
            for k, host in enumerate(self.layout.hosts[at]):
                place = self.layout.place[host]
                moved = pltpu.roll(value, EMPTY - FREE * k, 1)
                self.ref[place] = jnp.where(spare, moved, self.ref[place])
        for place in range(self.layout.size, self.ref.shape[0]):
            self.ref[place] = jnp.zeros((ROWS, LANES), jnp.float32)


class Unpacking:
    def __init__(self, source, layout):
        self.source, self.layout, self.cache = source, layout, {}
        self.changed = set(layout.guests).union(*layout.hosts.values())

    def __getitem__(self, at):
        if at not in self.cache:
            self.cache[at] = self.read(at)
        return self.cache[at]

    def read(self, at):
        row, lane, column, depth = iotas()
        layout = self.layout
        if at in layout.guests:
            value = None
            for k, host in enumerate(layout.hosts[at]):
                tile = self.source[layout.place[host]]
                moved = pltpu.roll(tile, LANES - (EMPTY - FREE * k), 1)
                value = moved if value is None else jnp.where(depth >= FREE * k, moved, value)
        else:
            value = self.source[layout.place[at]]
        if at in self.changed:
            value = jnp.where(depth >= EMPTY, layout.fills[at], value)
        return value


def layouts():
    y_fills = {2 * i + t: WEIGHTS[i] for i in LEVEL for t in range(2)}
    y_fills.update({Y_POP: W_DIAG, Y_CODE2: 0.0})
    out = [Layout(Y_TILES, [2 * i for i in LEVEL[:6]], y_fills)]
    for lanes, count in ((3, 10), (1, 4)):
        ring, _, code2, tiles = x_places(lanes)
        fills = {ring + n: WEIGHTS[2 * n] for n in range(1, X_HALVES)}
        fills.update({at: 0.0 for at in range(code2, tiles)})
        fills.update({X_LANE * n + i: WEIGHTS[i] for n in range(lanes) for i in LEVEL})
        guests = [X_LANE * (lanes - 1) + i for i in LEVEL[:count]]
        out.append(Layout(tiles, guests, fills))
    return out


class Pick:
    def __init__(self, flag, first, second):
        self.flag, self.first, self.second = flag, first, second

    def __getitem__(self, at):
        return jnp.where(self.flag, self.first[at], self.second[at])


class Deal:
    def __init__(self, even, first, second, layout, skip=0):
        self.even, self.skip, self.held = even, skip, {}
        self.first, self.second = Packing(first, layout), Packing(second, layout)

    def put(self, way, at, value):
        if (-way, at) not in self.held:
            self.held[way, at] = value
            return
        other = self.held.pop((-way, at))
        up, down = (value, other) if way == 1 else (other, value)
        self.first[at - self.skip] = jnp.where(self.even, up, down)
        self.second[at - self.skip] = jnp.where(self.even, down, up)

    def put_both(self, at, value):
        self.first[at - self.skip] = value
        self.second[at - self.skip] = value

    def finish(self):
        self.first.finish()
        self.second.finish()


def is_even(axis):
    return lax.rem(lax.axis_index(axis), 2) == 0


def pack_own(
    f_hbm,
    cot_hbm,
    codes_hbm,
    panels_hbm,
    porosity_hbm,
    first_ref,
    second_ref,
    own_ref,
    state_ref,
    own_cot_ref,
    field_ref,
    names_ref,
    f_ref,
    cot_ref,
    codes_ref,
    panels_ref,
    porosity_ref,
    sems,
):
    pieces = (
        (panels_hbm, panels_ref),
        (porosity_hbm, porosity_ref),
        (f_hbm, f_ref),
        (codes_hbm, codes_ref),
        (cot_hbm, cot_ref),
    )
    copies = [
        pltpu.make_async_copy(source, target, sems.at[n])
        for n, (source, target) in enumerate(pieces)
    ]
    for copy in copies:
        copy.start()
    for copy in copies[:4]:
        copy.wait()
    deal = Deal(is_even("gy"), first_ref, second_ref, layouts()[0])
    row, lane, column, depth = iotas()
    top = depth == NZ - 1

    def tile_of(ref, i, t):
        return ref[i, :, pl.ds(t * LANES, LANES)]

    codes, phis = [], []
    for t in range(2):
        names = panels_ref[0, t * LANES], panels_ref[4, t * LANES]
        phi = jnp.where(row < 4, porosity_ref[names[0]], porosity_ref[names[1]])
        names_ref[t] = jnp.where(row < 4, names[0], names[1])
        kinds = [tile_of(codes_ref, s, t).astype(jnp.float32) for s in range(STEPS)]
        f = [tile_of(f_ref, i, t) for i in range(Q)]
        g = collide(f, kinds[0], phi, moments(f))
        for i in range(Q):
            own_ref[2 * i + t] = g[i]
            state_ref[2 * i + t] = f[i]
        for s in range(STEPS):
            field_ref[2 * s + t] = kinds[s]
        field_ref[2 * OWN_PHI + t] = phi
        codes.append([jnp.where(top, phi, kinds[1]), kinds[2], kinds[3]])
    copies[4].wait()
    for i in range(Q):
        for way in (1, -1):
            near, far = (1, 0) if way == 1 else (0, 1)
            deep = 3 - way * VELOCITIES[i][1]
            cot = tile_of(cot_ref, i, near)
            g_far = own_ref[2 * i + far]
            if way == 1:
                mixed = jnp.where(column >= deep, g_far, columns(cot, deep - 4))
            else:
                mixed = jnp.where(column < 4 - deep, g_far, columns(cot, 4 - deep))
            deal.put(way, 2 * i, mixed if far == 0 else own_ref[2 * i])
            deal.put(way, 2 * i + 1, mixed if far == 1 else own_ref[2 * i + 1])
    for way in (1, -1):
        near, far = (1, 0) if way == 1 else (0, 1)
        outer = 3 if way == 1 else 0
        deal.put(way, Y_CODE1, codes[near][0])
        deal.put(way, Y_CODE2, codes[near][1])
        outside = columns(codes[far][0], 3 - 2 * outer)
        deal.put(way, Y_CODE3, jnp.where(column == 3 - outer, outside, codes[near][2]))
        extra = None
        for k, i in enumerate(turned(1, -way)):
            value = columns(own_ref[2 * i + far], k - outer)
            extra = value if extra is None else jnp.where(column == k, value, extra)
        deal.put(way, Y_POP, extra)
        extra = None
        for k, i in enumerate(turned(1, way)):
            value = columns(tile_of(cot_ref, i, near), k - (1 if way == 1 else 2))
            extra = value if extra is None else jnp.where(column == k, value, extra)
        deal.put(way, Y_COT, extra)
    deal.finish()
    for t in range(2):
        for i in range(Q):
            own_cot_ref[2 * i + t] = tile_of(cot_ref, i, t)


def is_right(near):
    return is_even("gy") if near else jnp.logical_not(is_even("gy"))


def half_lanes(right):
    row, lane, column, depth = iotas()
    return lane // (LANES // 2) == jnp.where(right, 0, 1)


def from_y(message_ref, near):
    row, lane, column, depth = iotas()
    ref = Unpacking(message_ref, layouts()[0])
    right = is_right(near)

    def population(i):
        return jnp.where(right, ref[2 * i], ref[2 * i + 1])

    def cotangent(i):
        values = []
        for way, place, far in ((1, 1, 0), (-1, 2, 1)):
            deep = 3 - way * VELOCITIES[i][1]
            value = columns(ref[2 * i + far], way * (4 - deep))
            if i in turned(1, way):
                extra = columns(ref[Y_COT], place - turned(1, way).index(i))
                value = jnp.where(column == place, extra, value)
            values.append(value)
        return jnp.where(right, values[1], values[0])

    def codes(s):
        return ref[(Y_CODE1, Y_CODE2, Y_CODE3)[s - 1]]

    def outer(i):
        left, above = ref[2 * i], ref[2 * i + 1]
        if i in turned(1, 1):
            above = columns(ref[Y_POP], -turned(1, 1).index(i))
        if i in turned(1, -1):
            left = columns(ref[Y_POP], 3 - turned(1, -1).index(i))
        return jnp.where(right, above, left)

    def outer_code():
        return jnp.where(right, columns(ref[Y_CODE3], 1), columns(ref[Y_CODE3], 3))

    return population, cotangent, codes, outer, outer_code


def mix_lines(deal, at, pop, cot, deep, way):
    row, lane, column, depth = iotas()
    if way == 1:
        mixed = jnp.where(row >= deep, pop, lines(cot, deep))
    else:
        mixed = jnp.where(row < ROWS - deep, pop, lines(cot, -deep))
    deal.put(way, at, mixed)


def pack_lines(deal, first, population, cotangent):
    row, lane, column, depth = iotas()

    for i in range(Q):
        pop, cot = population(i), cotangent(i)
        for way in (1, -1):
            mix_lines(deal, first + i, pop, cot, 3 - way * VELOCITIES[i][0], way)
    for way in (1, -1):
        extra = None
        for k, i in enumerate(turned(0, -way)):
            value = lines(population(i), k - (3 if way == 1 else 4))
            extra = value if extra is None else jnp.where(row == k, value, extra)
        for k, i in enumerate(turned(0, way)):
            value = lines(cotangent(i), 4 + k - (5 if way == 1 else 2))
            extra = jnp.where(row == 4 + k, value, extra)
        deal.put(way, first + X_EXTRA, extra)


def pack_neighbour(deal, lanes, message_ref, near):
    ring, code13, code2, tiles = x_places(lanes)
    population, cotangent, codes, outer, outer_code = from_y(message_ref, near)
    pack_lines(deal, X_LANE * (lanes - 1), population, cotangent)
    kept = half_lanes(is_right(near))
    for n in range(X_HALVES):
        first, second = (outer(2 * n - 1), outer(2 * n)) if n else (outer(0), outer_code())
        deal.put_both(ring + n, jnp.where(kept, first, pltpu.roll(second, LANES // 2, 1)))
    for way in (1, -1):
        mix_lines(deal, code13 + lanes - 1, codes(1), codes(3), 3, way)
    deal.put_both(tiles - 1, codes(2))


def pack_near(own_ref, cot_ref, field_ref, message_ref, first_ref, second_ref):
    row, lane, column, depth = iotas()
    deal = Deal(is_even("gx"), first_ref, second_ref, layouts()[1])
    ring, code13, code2, tiles = x_places(3)
    for t in range(2):
        pack_lines(
            deal,
            X_LANE * t,
            lambda i: own_ref[2 * i + t],
            lambda i: cot_ref[2 * i + t],
        )
        code = jnp.where(depth == NZ - 1, field_ref[2 * OWN_PHI + t], field_ref[2 + t])
        for way in (1, -1):
            mix_lines(deal, code13 + t, code, field_ref[6 + t], 3, way)
    first, second = field_ref[4], lines(field_ref[5], 4)
    deal.put(1, code2, jnp.where(row >= 4, first, second))
    deal.put(-1, code2, jnp.where(row < 4, first, second))
    pack_neighbour(deal, 3, message_ref, True)
    deal.finish()


def pack_far(message_ref, first_ref, second_ref):
    deal = Deal(is_even("gx"), first_ref, second_ref, layouts()[2])
    pack_neighbour(deal, 1, message_ref, False)
    deal.finish()


def from_x(ref, n, way, lanes):
    row, lane, column, depth = iotas()
    ring, code13, code2, _ = x_places(lanes)
    first = X_LANE * n

    def population(i):
        value = ref[first + i]
        if i in turned(0, -way):
            place = 3 if way == 1 else 4
            extra = lines(ref[first + X_EXTRA], place - turned(0, -way).index(i))
            value = jnp.where(row == place, extra, value)
        return value

    def cotangent(i):
        value = lines(ref[first + i], -way * (3 - way * VELOCITIES[i][0]))
        if i in turned(0, way):
            place = 5 if way == 1 else 2
            extra = lines(ref[first + X_EXTRA], place - 4 - turned(0, way).index(i))
            value = jnp.where(row == place, extra, value)
        return value

    def codes(s):
        if s == 2:
            return lines(ref[code2 + n // 2], 4 * (n % 2))
        value = ref[code13 + n]
        return value if s == 1 else lines(value, -3 * way)

    def outer(i):
        value = ref[ring + (i + 1) // 2]
        return pltpu.roll(value, LANES // 2, 1) if i and i % 2 == 0 else value

    def outer_code():
        return pltpu.roll(ref[ring], LANES // 2, 1)

    return population, cotangent, codes, outer, outer_code


def sides(first_ref, second_ref, axis, layout):
    even = is_even(axis)
    picks = Pick(even, second_ref, first_ref), Pick(even, first_ref, second_ref)
    return [Unpacking(pick, layout) for pick in picks]


def own_rows(step=0):
    return pl.ds(ROWS + step, ROWS)


def halo_rows(step=0):
    return pl.ds({0: 2 * ROWS, -1: 2 * ROWS - 1, 1: 1}[step], ROWS)


def put_halo(ref, at, halo):
    ref[at, pl.ds(0, ROWS), :] = halo
    ref[at, halo_rows(), :] = halo


def put_ring(ref, at, own, halo):
    ref[at, own_rows(), :] = own
    put_halo(ref, at, halo)


def expand(code):
    row, lane, column, depth = iotas()
    top = depth == NZ - 1
    phi = jnp.where(top, code, 0.0)
    for step in (1, 2, 4, 8, 16):
        phi = phi + pltpu.roll(phi, LANES - step, 1)
    return jnp.where(top, 0.0, code), phi


def in_groups(size=8):
    return [range(first, min(first + size, Q)) for first in range(0, Q, size)]


def lay_own(c, population, cotangent, codes, code_phi, pop, cot, wide, field):
    for group in in_groups():
        pops = [population(i) for i in group]
        cots = [cotangent(i) for i in group] if cotangent is not None else []
        for i, value in zip(group, pops):
            pop[5 * i + c, pl.ds(2 * ROWS, ROWS), :] = value
        for i, value in zip(group, cots):
            cot[4 * i + c - 1, own_rows(), :] = value
    for n in range(2):
        wide[n, c, 1] = code_phi[n]
    if cotangent is not None:
        field[0, c - 1, 0], field[1, c - 1, 0] = code_phi[1], code_phi[0]
        for s in (2, 3):
            field[s, c - 1, 0] = codes(s)


def lay_halo(c, below, above, pop, cot, wide, field):
    row, lane, column, depth = iotas()
    for group in in_groups():
        pops = [(below[0](i), above[0](i)) for i in group]
        cots = []
        if below[1] is not None:
            cots = [jnp.where(row < 4, above[1](i), below[1](i)) for i in group]
        for i, (before, behind) in zip(group, pops):
            pop[5 * i + c, pl.ds(ROWS, ROWS), :] = before
            pop[5 * i + c, pl.ds(3 * ROWS, ROWS), :] = behind
        for i, value in zip(group, cots):
            put_halo(cot, 4 * i + c - 1, value)
    before, behind = expand(below[2](1)), expand(above[2](1))
    for n in range(2):
        wide[n, c, 0], wide[n, c, 2] = before[n], behind[n]
    if below[1] is not None:
        for n, place in ((0, 1), (1, 0)):
            field[place, c - 1, 1] = jnp.where(row < 4, behind[n], before[n])
        for s in (2, 3):
            field[s, c - 1, 1] = jnp.where(row < 4, above[2](s), below[2](s))


def near_tile():
    return jnp.where(is_right(True), 4, 1)


def lay_out(
    near_y_ref,
    far_y_ref,
    first_near_ref,
    second_near_ref,
    own_ref,
    field_ref,
    cot_ref,
    pop,
    cot,
    wide,
    field,
):
    spaces = pop, cot, wide, field
    below, above = sides(first_near_ref, second_near_ref, "gx", layouts()[1])
    for t in range(2):
        lay_own(
            2 + t,
            lambda i: own_ref[2 * i + t],
            lambda i: cot_ref[2 * i + t],
            lambda s: field_ref[2 * s + t],
            (field_ref[2 + t], field_ref[2 * OWN_PHI + t]),
            *spaces,
        )
        lay_halo(2 + t, from_x(below, t, 1, 3), from_x(above, t, -1, 3), *spaces)
    near, far = from_y(near_y_ref, True), from_y(far_y_ref, False)
    for c, (population, cotangent, codes, _, _) in ((near_tile(), near), (5 - near_tile(), far)):
        lay_own(c, population, cotangent, codes, expand(codes(1)), *spaces)
    kept = half_lanes(is_right(True))
    lay_own(
        0,
        lambda i: jnp.where(kept, near[3](i), far[3](i)),
        None,
        None,
        expand(jnp.where(kept, near[4](), far[4]())),
        *spaces,
    )
    lay_halo(near_tile(), from_x(below, 2, 1, 3), from_x(above, 2, -1, 3), *spaces)


def lay_far(near_refs, far_refs, spaces):
    nears, fars = (
        [
            from_x(ref, lanes - 1, way, lanes)
            for ref, way in zip(sides(*refs, "gx", layout), (1, -1))
        ]
        for refs, layout, lanes in zip((near_refs, far_refs), layouts()[1:], (3, 1))
    )
    lay_halo(5 - near_tile(), *fars, *spaces)
    kept = half_lanes(is_right(True))
    ring = [
        (
            lambda i, near=near, far=far: jnp.where(kept, near[3](i), far[3](i)),
            None,
            lambda s, near=near, far=far: jnp.where(kept, near[4](), far[4]()),
        )
        for near, far in zip(nears, fars)
    ]
    lay_halo(0, *ring, *spaces)


def steps_kernel(
    sizes,
    state_ref,
    own_field_ref,
    names_ref,
    first_near_ref,
    second_near_ref,
    first_far_ref,
    second_far_ref,
    *refs,
):
    adjoint_ref, panel_ref, pop_a, ring_a, wide, field, pop_b, ring_b, saved, mom, grad = refs[4:]
    size_x, size_y = sizes
    lay_far(
        (first_near_ref, second_near_ref),
        (first_far_ref, second_far_ref),
        (pop_a, ring_a, wide, field),
    )

    at_x, at_y = lax.axis_index("gx"), lax.axis_index("gy")
    edges = (
        jnp.where(at_x == 0, 1, 0),
        jnp.where(at_x == size_x - 1, 1, 0),
        jnp.where(at_y == 0, 1, 0),
        jnp.where(at_y == size_y - 1, 1, 0),
    )
    row, lane, column, depth = iotas()
    after = row < 4

    def masks_of(tile, first, r):
        return wall_masks(r == 0, tile == first, tile == first + 1, edges)

    def neighbours(tile, tiles):
        if isinstance(tile, int):
            return {0: tile, -1: (tile - 1) % tiles, 1: (tile + 1) % tiles}
        return {0: tile, -1: lax.rem(tile + tiles - 1, tiles), 1: lax.rem(tile + 1, tiles)}

    def from_wide(ref, tile, r):
        step = neighbours(tile, 5)

        def load(i, tile_step, row_step, move):
            at = 5 * i + step[tile_step]
            before, own, behind = (ref[at, pl.ds(ROWS * n + row_step, ROWS), :] for n in (1, 2, 3))
            return (own, jnp.where(after, behind, before), before, behind)[r]

        return load

    def from_ring(ref, tile, tiles, r):
        step = neighbours(tile, tiles)

        def load(i, tile_step, row_step, move):
            rows = own_rows(row_step) if r == 0 else halo_rows(row_step)
            return ref[tiles * i + step[tile_step], rows, :]

        return load

    def from_outer(ref, r):
        def load(i, tile_step, row_step, move):
            rows = own_rows(row_step) if r == 0 else halo_rows(row_step)
            if tile_step:
                return ref[4 * i + (2 if tile_step < 0 else 1), rows, :]
            cut = {0: 2, 1: 1, -1: 3}[move]
            return jnp.where(column < cut, ref[4 * i + 3, rows, :], ref[4 * i, rows, :])

        return load

    def note(s, tile, r, parts):
        for n, value in enumerate(parts[2:4] + tuple(parts[4])):
            mom[s - 1, n, tile, r] = value

    def first_step(tile, carry):
        place = lax.rem(tile + 4, 5)
        halo = []
        for r in (2, 0, 3):
            f = stream_tile(from_wide(pop_a, tile, r), 1, masks_of(tile, 2, r), lane)
            parts = moments(f)
            if r == 0:
                note(1, place, 0, parts)
                for i in range(Q):
                    saved[0, i, place] = f[i]
            else:
                halo.append(parts[2:4] + tuple(parts[4]))
            at = {2: 0, 0: 1, 3: 2}[r]
            g = collide(f, wide[0, tile, at], wide[1, tile, at], parts)
            for i in range(Q):
                pop_b[5 * i + tile, pl.ds(ROWS * (at + 1), ROWS), :] = g[i]
        for n in range(5):
            mom[0, n, place, 1] = jnp.where(after, halo[1][n], halo[0][n])
        return carry

    lax.fori_loop(0, 5, first_step, 0, unroll=True)

    def second_step(tile, carry):
        out = []
        for r in range(2):
            f = stream_tile(from_wide(pop_b, tile + 1, r), 1, masks_of(tile, 1, r), lane)
            parts = moments(f)
            note(2, tile, r, parts)
            if r == 0:
                for i in range(Q):
                    saved[1, i, tile] = f[i]
            out.append(collide(f, field[2, tile, r], field[0, tile, r], parts))
        for i in range(Q):
            put_ring(ring_b, 4 * i + tile, out[0][i], out[1][i])
        return carry

    lax.fori_loop(0, 4, second_step, 0, unroll=True)

    def third_step(tile, carry):
        for r in range(2):
            f = stream_tile(from_ring(ring_b, tile, 4, r), 1, masks_of(tile, 1, r), lane)
            note(3, tile, r, moments(f))
            if r == 0:
                for i in range(Q):
                    saved[2, i, tile] = f[i]
        return carry

    lax.fori_loop(0, 4, third_step, 0, unroll=True)

    def back_tile(load, s, tile, r, own):
        b = stream_tile(load, -1, masks_of(4 if tile is None else tile, 1, r), lane)

        def read(get):
            return jnp.where(column < 2, get(3), get(0)) if tile is None else get(tile)

        rho, rinv, *u = [read(lambda at: mom[s - 1, n, at, r]) for n in range(5)]
        kind, phi = read(lambda at: field[s, at, r]), read(lambda at: field[0, at, r])
        state = [saved[s - 1, i, tile] for i in range(Q)] if own else None
        back, term = collide_back(b, kind, phi, rho, rinv, u, state)
        if own:
            grad[tile] = term if s == 3 else grad[tile] + term
        return back

    def last_step(tile, carry):
        out = [back_tile(from_ring(ring_a, tile, 4, r), 3, tile, r, r == 0) for r in range(2)]
        for i in range(Q):
            put_ring(ring_b, 4 * i + tile, out[0][i], out[1][i])
        return carry

    lax.fori_loop(0, 4, last_step, 0, unroll=True)

    for k, tile in enumerate((1, 2, None)):
        out = []
        for r in range(2):
            load = from_outer(ring_b, r) if tile is None else from_ring(ring_b, tile, 4, r)
            out.append(back_tile(load, 2, tile, r, r == 0 and tile is not None))
        for i in range(Q):
            put_ring(ring_a, 3 * i + k, out[0][i], out[1][i])

    for k, tile in enumerate((1, 2, None)):
        out = []
        for r in range(2):
            load = from_ring(ring_a, k, 3, r)
            out.append(back_tile(load, 1, tile, r, r == 0 and tile is not None))
        for i in range(Q):
            put_ring(ring_b, 3 * i + k, out[0][i], out[1][i])

    panel = lax.broadcasted_iota(jnp.int32, panel_ref.shape, 1)
    sums = jnp.zeros(panel_ref.shape, jnp.float32)
    for t in range(2):
        b = stream_tile(from_ring(ring_b, t, 3, 0), -1, masks_of(t, 0, 0), lane)
        f = [state_ref[2 * i + t] for i in range(Q)]
        kind, phi = own_field_ref[t], own_field_ref[2 * OWN_PHI + t]
        _, _, rho, rinv, u = moments(f)
        back, term = collide_back(b, kind, phi, rho, rinv, u, f)
        for i in range(Q):
            adjoint_ref[i, :, pl.ds(t * LANES, LANES)] = back[i]
        term = term + grad[t + 1]
        for part in range(2):
            amount = jnp.sum(jnp.where((row < 4) == (part == 0), term, 0.0))
            name = names_ref[t, 4 * part : 4 * part + 1, 0:1]
            sums = sums + jnp.where(panel == name, amount, 0.0)
    panel_ref[...] = sums


def finish(parts_ref, adjoint_ref, sums_hbm, adjoint_hbm, sums_ref, sems):
    adjoint_copy = pltpu.make_async_copy(adjoint_ref, adjoint_hbm, sems.at[0])
    adjoint_copy.start()
    sums_ref[...] = jnp.sum(parts_ref[...], axis=0)
    sums_copy = pltpu.make_async_copy(sums_ref, sums_hbm, sems.at[1])
    sums_copy.start()
    sums_copy.wait()
    adjoint_copy.wait()


VMEM = pl.BlockSpec(memory_space=pltpu.VMEM)
HBM = pl.BlockSpec(memory_space=pltpu.HBM)


def shape_of(*dims):
    return jax.ShapeDtypeStruct(dims, jnp.float32)


def tiles_of(count):
    return shape_of(count, ROWS, LANES)


def on_device(sizes, checkpoint, cotangent, cell_codes, porosity, baffle_index):
    size_x, size_y = sizes
    panels = porosity.shape[0]
    devices = size_x * size_y
    y_layout, near_layout, far_layout = layouts()

    params = pltpu.CompilerParams(vmem_limit_bytes=32 * 1024 * 1024)

    def call(kernel, out_shape, in_specs, scratch=(), name=None, aliases={}):
        return pl.pallas_call(
            kernel,
            out_shape=out_shape,
            in_specs=in_specs,
            out_specs=jax.tree.map(lambda _: VMEM, out_shape),
            scratch_shapes=scratch,
            input_output_aliases=aliases,
            compiler_params=params,
            name=name,
        )

    def swap(value, axis, size):
        return lax.ppermute(value, axis, [(i, i ^ 1) for i in range(size) if i ^ 1 < size])

    def swap_between(value, axis, size):
        pairs = [(i, i + 1) for i in range(1, size - 1, 2)]
        return lax.ppermute(value, axis, pairs + [(j, i) for i, j in pairs])

    def swap_inner(value):
        pairs = [
            (i * size_y + y, (i + 1) * size_y + y)
            for i in range(1, size_x - 1, 2)
            for y in range(1, size_y - 1)
        ]
        return lax.ppermute(value, ("gx", "gy"), pairs + [(j, i) for i, j in pairs])

    arguments = [
        pltpu.with_memory_space_constraint(value, pltpu.HBM)
        for value in (checkpoint, cotangent, cell_codes, baffle_index, porosity)
    ]
    near_y, far_y, own, state, cot, field, names = call(
        pack_own,
        (tiles_of(y_layout.size),) * 2
        + (tiles_of(2 * Q),) * 3
        + (tiles_of(2 * OWN_PHI + 2), jax.ShapeDtypeStruct((2, ROWS, LANES), jnp.int32)),
        [HBM] * 5,
        [
            pltpu.VMEM((Q, ROWS, 2 * LANES), jnp.float32),
            pltpu.VMEM((Q, ROWS, 2 * LANES), jnp.float32),
            pltpu.VMEM((STEPS, ROWS, 2 * LANES), jnp.int32),
            pltpu.SMEM(baffle_index.shape, jnp.int32),
            pltpu.SMEM(porosity.shape, jnp.float32),
            pltpu.SemaphoreType.DMA((5,)),
        ],
        name="pack_own",
    )(*arguments)
    near_y = swap(near_y, "gy", size_y)
    far_y = swap_between(far_y, "gy", size_y)
    first_near, second_near = call(
        pack_near,
        (tiles_of(near_layout.size), tiles_of(near_layout.size + 1)),
        [VMEM] * 4,
        name="pack_near",
    )(own, cot, field, near_y)
    second_near = swap_between(second_near, "gx", size_x)
    first_near = swap(first_near, "gx", size_x)
    first_far, second_far = call(
        pack_far,
        (tiles_of(far_layout.size), tiles_of(far_layout.size + 1)),
        [VMEM],
        name="pack_far",
    )(far_y)
    second_far = swap_inner(second_far)
    first_far = swap(first_far, "gx", size_x)
    spaces = (
        shape_of(5 * Q, 5 * ROWS, LANES),
        shape_of(4 * Q, 3 * ROWS, LANES),
        shape_of(2, 5, 3, ROWS, LANES),
        shape_of(4, 4, 2, ROWS, LANES),
    )
    laid = call(lay_out, spaces, [VMEM] * 7, name="lay_out")(
        near_y, far_y, first_near, second_near, own, field, cot
    )
    adjoint, sums, *_ = call(
        functools.partial(steps_kernel, sizes),
        (pltpu.VMEM((Q, ROWS, 2 * LANES), jnp.float32), shape_of(devices, panels)) + spaces,
        [VMEM] * 11,
        [
            pltpu.VMEM((5 * Q, 5 * ROWS, LANES), jnp.float32),
            pltpu.VMEM((4 * Q, 3 * ROWS, LANES), jnp.float32),
            pltpu.VMEM((3, Q, 5, ROWS, LANES), jnp.float32),
            pltpu.VMEM((3, 5, 5, 2, ROWS, LANES), jnp.float32),
            pltpu.VMEM((4, ROWS, LANES), jnp.float32),
        ],
        name="steps",
        aliases={7 + n: 2 + n for n in range(4)},
    )(state, field, names, first_near, second_near, first_far, second_far, *laid)
    gathered = lax.all_to_all(sums, ("gx", "gy"), 0, 0, tiled=True)
    totals, adjoint = pl.pallas_call(
        finish,
        out_shape=(shape_of(1, panels), shape_of(Q, ROWS, 2 * LANES)),
        in_specs=[VMEM, VMEM],
        out_specs=(HBM, HBM),
        scratch_shapes=[pltpu.VMEM((1, panels), jnp.float32), pltpu.SemaphoreType.DMA((2,))],
        compiler_params=params,
        name="finish",
    )(gathered.reshape(devices, 1, panels), adjoint)
    return adjoint, totals.reshape(panels)


def solution(mesh):
    sizes = (mesh.shape["gx"], mesh.shape["gy"])
    in_specs = (P(None, "gx", "gy"), P(None, "gx", "gy"), P(None, "gx", "gy"), P(), P("gx", "gy"))
    out_specs = (P(None, "gx", "gy"), P())
    return jax.shard_map(
        functools.partial(on_device, sizes),
        mesh=mesh,
        in_specs=in_specs,
        out_specs=out_specs,
        check_vma=False,
    )
```

```python
import functools

import jax
import jax.numpy as jnp
import numpy as np
from jax import lax
from jax.experimental import pallas as pl
from jax.experimental.pallas import tpu as pltpu
from jax.sharding import PartitionSpec as P

Q = 19
STEPS = 4
NZ = 32
ROWS = 8
LANES = 128
OMEGA = 1.6
ACCEL = (0.002, 0.0, -0.003)
SHIFT = tuple(a / OMEGA for a in ACCEL)

VELOCITIES = [
    (0, 0, 0),
    (1, 0, 0),
    (-1, 0, 0),
    (0, 1, 0),
    (0, -1, 0),
    (0, 0, 1),
    (0, 0, -1),
    (1, 1, 0),
    (-1, -1, 0),
    (1, -1, 0),
    (-1, 1, 0),
    (1, 0, 1),
    (-1, 0, -1),
    (1, 0, -1),
    (-1, 0, 1),
    (0, 1, 1),
    (0, -1, -1),
    (0, 1, -1),
    (0, -1, 1),
]
OPPOSITE = [0, 2, 1, 4, 3, 6, 5, 8, 7, 10, 9, 12, 11, 14, 13, 16, 15, 18, 17]
PAIRS = [(i, i + 1) for i in range(1, Q, 2)]
W_REST, W_AXIS, W_DIAG = 1.0 / 3.0, 1.0 / 18.0, 1.0 / 36.0

Y_CODE1, Y_CODE2, Y_CODE3, Y_POP, Y_COT = 38, 39, 40, 41, 42
Y_TILES = 43
X_EXTRA = 19
X_LANE = 20
X_HALVES = 10


def x_places(lanes):
    ring = X_LANE * lanes
    code13 = ring + X_HALVES
    code2 = code13 + lanes
    return ring, code13, code2, code2 + (lanes + 1) // 2


EMPTY = 25
FREE = NZ - EMPTY
WEIGHTS = [W_REST] + [W_AXIS] * 6 + [W_DIAG] * 12
LEVEL = [i for i, v in enumerate(VELOCITIES) if v[2] < 1]
OWN_PHI = 4


def turned(axis, outward):
    return [i for i, v in enumerate(VELOCITIES) if v[axis] == outward and sum(map(abs, v)) == 2]


def total(values):
    values = list(values)
    while len(values) > 1:
        values = [a + b for a, b in zip(values[::2], values[1::2])] + (
            [values[-1]] if len(values) % 2 else []
        )
    return values[0]


def along(vector, three):
    terms = None
    for c, value in zip(vector, three):
        if c == 0:
            continue
        if terms is None:
            terms = value if c > 0 else -value
        else:
            terms = terms + value if c > 0 else terms - value
    return terms


def moments(f):
    plus = {i: f[i] + f[o] for i, o in PAIRS}
    minus = {i: f[i] - f[o] for i, o in PAIRS}
    rho = total([f[0]] + [plus[i] for i, _ in PAIRS])
    rinv = 1.0 / rho
    u = []
    for axis in range(3):
        terms = [
            minus[i] if VELOCITIES[i][axis] > 0 else -minus[i]
            for i, _ in PAIRS
            if VELOCITIES[i][axis] != 0
        ]
        u.append(total(terms) * rinv + SHIFT[axis])
    return plus, minus, rho, rinv, u


def coefficients(kind, phi, rinv):
    baffle = kind == 3.0
    gas = kind == 0.0
    even = jnp.where(gas, 0.0, jnp.where(baffle, 0.5 - 0.5 * OMEGA * phi, 0.5 * (1.0 - OMEGA)))
    odd = jnp.where(
        gas, 0.0, jnp.where(baffle, (1.0 - 0.5 * OMEGA) * phi - 0.5, 0.5 * (1.0 - OMEGA))
    )
    slope = jnp.where(
        baffle,
        OMEGA * phi,
        jnp.where(kind == 1.0, OMEGA, jnp.where(kind == 2.0, OMEGA * rinv, 0.0)),
    )
    return even, odd, slope


def collide(f, kind, phi, parts):
    plus, minus, rho, rinv, u = parts
    even, odd, slope = coefficients(kind, phi, rinv)
    scale = slope * rho
    rest = 1.0 - 1.5 * (u[0] * u[0] + u[1] * u[1] + u[2] * u[2])
    base = scale * rest + jnp.where(kind == 0.0, 1.0, 0.0)
    out = [None] * Q
    out[0] = 2.0 * even * f[0] + W_REST * base
    for weight, pairs in ((W_AXIS, PAIRS[:3]), (W_DIAG, PAIRS[3:])):
        flat = weight * base
        three = (3.0 * weight) * scale
        for i, o in pairs:
            cu = along(VELOCITIES[i], u)
            lin = three * cu
            ev = even * plus[i] + (flat + 1.5 * lin * cu)
            od = odd * minus[i] + lin
            out[i] = ev + od
            out[o] = ev - od
    return out


def collide_back(b, kind, phi, rho, rinv, u, state=None):
    even, odd, slope = coefficients(kind, phi, rinv)
    plus = {i: b[i] + b[o] for i, o in PAIRS}
    minus = {i: b[i] - b[o] for i, o in PAIRS}
    rest = 1.0 - 1.5 * (u[0] * u[0] + u[1] * u[1] + u[2] * u[2])
    u_half = [1.5 * c for c in u]
    weighted = W_REST * b[0]
    energy = 0.0
    vector = [0.0, 0.0, 0.0]
    for weight, pairs in ((W_AXIS, PAIRS[:3]), (W_DIAG, PAIRS[3:])):
        weighted = weighted + weight * total([plus[i] for i, _ in pairs])
        energies, parts = [], ([], [], [])
        for i, _ in pairs:
            cu = along(VELOCITIES[i], u)
            half = along(VELOCITIES[i], u_half) * plus[i]
            first = minus[i] + half
            energies.append(cu * first)
            second = first + half
            for axis in range(3):
                c = VELOCITIES[i][axis]
                if c:
                    parts[axis].append(second if c > 0 else -second)
        energy = energy + (3.0 * weight) * total(energies)
        vector = [vector[k] + (3.0 * weight) * total(parts[k]) for k in range(3)]
    energy = energy + rest * weighted
    vector = [vector[k] - (3.0 * weighted) * u[k] for k in range(3)]
    push = [slope * v for v in vector]
    inner = total([push[k] * (u[k] - SHIFT[k]) for k in range(3)])
    shared = jnp.where(kind == 2.0, 0.0, slope) * energy - inner
    out = [None] * Q
    out[0] = 2.0 * even * b[0] + shared
    for i, o in PAIRS:
        ev = even * plus[i] + shared
        od = odd * minus[i] + along(VELOCITIES[i], push)
        out[i] = ev + od
        out[o] = ev - od
    if state is None:
        return out, None
    evens = total([plus[i] * (state[i] + state[o]) for i, o in PAIRS])
    odds = total([minus[i] * (state[i] - state[o]) for i, o in PAIRS])
    term = (
        -OMEGA * (b[0] * state[0] + 0.5 * evens)
        + (1.0 - 0.5 * OMEGA) * odds
        + OMEGA * rho * energy
    )
    return out, jnp.where(kind == 3.0, term, 0.0)


def wall_masks(sign_rows, own_low, own_high, edges):
    lane = lax.broadcasted_iota(jnp.int32, (ROWS, LANES), 1)
    row = lax.broadcasted_iota(jnp.int32, (ROWS, LANES), 0)
    x_low, x_high, y_low, y_high = edges
    depth = lane % NZ
    masks = {}
    masks[2, 1] = depth == 0
    masks[2, -1] = depth == NZ - 1
    masks[1, 1] = lane < jnp.where(own_low, y_low * NZ, 0)
    masks[1, -1] = lane >= jnp.where(own_high, LANES - y_high * NZ, LANES)
    if sign_rows:
        masks[0, 1] = row < x_low
        masks[0, -1] = row >= ROWS - x_high
    return masks


def stream_tile(load, sign, masks, lane):
    cross_low, cross_high = lane >= LANES - NZ, lane < NZ
    combined = {}
    out = []
    for i, vector in enumerate(VELOCITIES):
        v = tuple(sign * c for c in vector)
        value = load(i, 0, -v[0], v[1])
        if v[1] == 1:
            value = jnp.where(cross_low, load(i, -1, -v[0], 1), value)
        elif v[1] == -1:
            value = jnp.where(cross_high, load(i, 1, -v[0], -1), value)
        amount = (v[1] * NZ + v[2]) % LANES
        if amount:
            value = pltpu.roll(value, amount, 1)
        outside = None
        if v not in combined:
            for axis in range(3):
                if v[axis] and (axis, v[axis]) in masks:
                    wall = masks[axis, v[axis]]
                    outside = wall if outside is None else outside | wall
            combined[v] = outside
        outside = combined[v]
        if outside is not None:
            value = jnp.where(outside, load(OPPOSITE[i], 0, 0, 0), value)
        out.append(value)
    return out


def iotas():
    row = lax.broadcasted_iota(jnp.int32, (ROWS, LANES), 0)
    lane = lax.broadcasted_iota(jnp.int32, (ROWS, LANES), 1)
    return row, lane, lane // NZ, lane % NZ


def columns(value, count):
    amount = (count * NZ) % LANES
    return pltpu.roll(value, amount, 1) if amount else value


def lines(value, count):
    amount = count % ROWS
    return pltpu.roll(value, amount, 0) if amount else value


class Layout:
    def __init__(self, count, guests, fills):
        self.fills = fills
        hosts = [at for at in fills if at not in guests]
        self.hosts = {at: hosts[4 * n : 4 * n + 4] for n, at in enumerate(guests)}
        self.guests = guests
        kept = [at for at in range(count) if at not in guests]
        self.place = {at: n for n, at in enumerate(kept)}
        self.size = len(kept)


class Packing:
    def __init__(self, ref, layout):
        self.ref, self.layout, self.held = ref, layout, {}

    def __setitem__(self, at, value):
        if at in self.layout.guests:
            self.held[at] = value
        else:
            self.ref[self.layout.place[at]] = value

    def finish(self):
        row, lane, column, depth = iotas()
        spare = depth >= EMPTY
        for at, value in self.held.items():
            for k, host in enumerate(self.layout.hosts[at]):
                place = self.layout.place[host]
                moved = pltpu.roll(value, EMPTY - FREE * k, 1)
                self.ref[place] = jnp.where(spare, moved, self.ref[place])
        for place in range(self.layout.size, self.ref.shape[0]):
            self.ref[place] = jnp.zeros((ROWS, LANES), jnp.float32)


class Unpacking:
    def __init__(self, source, layout):
        self.source, self.layout, self.cache = source, layout, {}
        self.changed = set(layout.guests).union(*layout.hosts.values())

    def __getitem__(self, at):
        if at not in self.cache:
            self.cache[at] = self.read(at)
        return self.cache[at]

    def read(self, at):
        row, lane, column, depth = iotas()
        layout = self.layout
        if at in layout.guests:
            value = None
            for k, host in enumerate(layout.hosts[at]):
                tile = self.source[layout.place[host]]
                moved = pltpu.roll(tile, LANES - (EMPTY - FREE * k), 1)
                value = moved if value is None else jnp.where(depth >= FREE * k, moved, value)
        else:
            value = self.source[layout.place[at]]
        if at in self.changed:
            value = jnp.where(depth >= EMPTY, layout.fills[at], value)
        return value


def layouts():
    y_fills = {2 * i + t: WEIGHTS[i] for i in LEVEL for t in range(2)}
    y_fills.update({Y_POP: W_DIAG, Y_CODE2: 0.0})
    out = [Layout(Y_TILES, [2 * i for i in LEVEL[:6]], y_fills)]
    for lanes, count in ((3, 10), (1, 4)):
        ring, _, code2, tiles = x_places(lanes)
        fills = {ring + n: WEIGHTS[2 * n] for n in range(1, X_HALVES)}
        fills.update({at: 0.0 for at in range(code2, tiles)})
        fills.update({X_LANE * n + i: WEIGHTS[i] for n in range(lanes) for i in LEVEL})
        guests = [X_LANE * (lanes - 1) + i for i in LEVEL[:count]]
        out.append(Layout(tiles, guests, fills))
    return out


class Pick:
    def __init__(self, flag, first, second):
        self.flag, self.first, self.second = flag, first, second

    def __getitem__(self, at):
        return jnp.where(self.flag, self.first[at], self.second[at])


class Deal:
    def __init__(self, even, first, second, layout):
        self.even, self.held, self.ready = even, {}, []
        self.first, self.second = Packing(first, layout), Packing(second, layout)

    def put(self, way, at, value):
        if (-way, at) not in self.held:
            self.held[way, at] = value
            return
        other = self.held.pop((-way, at))
        up, down = (value, other) if way == 1 else (other, value)
        self.add(at, jnp.where(self.even, up, down), jnp.where(self.even, down, up))

    def put_both(self, at, value):
        self.add(at, value, value)

    def add(self, *entry):
        self.ready.append(entry)
        if len(self.ready) == 8:
            self.write()

    def write(self):
        for at, first, second in self.ready:
            self.first[at] = first
            self.second[at] = second
        self.ready = []

    def finish(self):
        self.write()
        self.first.finish()
        self.second.finish()


def is_even(axis):
    return lax.rem(lax.axis_index(axis), 2) == 0


def pack_own(
    f_hbm,
    cot_hbm,
    codes_hbm,
    panels_hbm,
    porosity_hbm,
    first_ref,
    second_ref,
    own_ref,
    state_ref,
    own_cot_ref,
    field_ref,
    names_ref,
    f_ref,
    cot_ref,
    codes_ref,
    panels_ref,
    porosity_ref,
    sems,
):
    pieces = (
        (panels_hbm, panels_ref),
        (porosity_hbm, porosity_ref),
        (f_hbm, f_ref),
        (codes_hbm, codes_ref),
        (cot_hbm, cot_ref),
    )
    copies = [
        pltpu.make_async_copy(source, target, sems.at[n])
        for n, (source, target) in enumerate(pieces)
    ]
    for copy in copies:
        copy.start()
    for copy in copies[:4]:
        copy.wait()
    deal = Deal(is_even("gy"), first_ref, second_ref, layouts()[0])
    row, lane, column, depth = iotas()
    top = depth == NZ - 1

    def tile_of(ref, i, t):
        return ref[i, :, pl.ds(t * LANES, LANES)]

    codes, phis = [], []
    for t in range(2):
        names = panels_ref[0, t * LANES], panels_ref[4, t * LANES]
        phi = jnp.where(row < 4, porosity_ref[names[0]], porosity_ref[names[1]])
        names_ref[t] = jnp.where(row < 4, names[0], names[1])
        kinds = [tile_of(codes_ref, s, t).astype(jnp.float32) for s in range(STEPS)]
        f = [tile_of(f_ref, i, t) for i in range(Q)]
        g = collide(f, kinds[0], phi, moments(f))
        for i in range(Q):
            own_ref[2 * i + t] = g[i]
            state_ref[2 * i + t] = f[i]
        for s in range(STEPS):
            field_ref[2 * s + t] = kinds[s]
        field_ref[2 * OWN_PHI + t] = phi
        codes.append([jnp.where(top, phi, kinds[1]), kinds[2], kinds[3]])
    copies[4].wait()
    for i in range(Q):
        for way in (1, -1):
            near, far = (1, 0) if way == 1 else (0, 1)
            deep = 3 - way * VELOCITIES[i][1]
            cot = tile_of(cot_ref, i, near)
            g_far = own_ref[2 * i + far]
            if way == 1:
                mixed = jnp.where(column >= deep, g_far, columns(cot, deep - 4))
            else:
                mixed = jnp.where(column < 4 - deep, g_far, columns(cot, 4 - deep))
            deal.put(way, 2 * i, mixed if far == 0 else own_ref[2 * i])
            deal.put(way, 2 * i + 1, mixed if far == 1 else own_ref[2 * i + 1])
    for way in (1, -1):
        near, far = (1, 0) if way == 1 else (0, 1)
        outer = 3 if way == 1 else 0
        deal.put(way, Y_CODE1, codes[near][0])
        deal.put(way, Y_CODE2, codes[near][1])
        outside = columns(codes[far][0], 3 - 2 * outer)
        deal.put(way, Y_CODE3, jnp.where(column == 3 - outer, outside, codes[near][2]))
        extra = None
        for k, i in enumerate(turned(1, -way)):
            value = columns(own_ref[2 * i + far], k - outer)
            extra = value if extra is None else jnp.where(column == k, value, extra)
        deal.put(way, Y_POP, extra)
        extra = None
        for k, i in enumerate(turned(1, way)):
            value = columns(tile_of(cot_ref, i, near), k - (1 if way == 1 else 2))
            extra = value if extra is None else jnp.where(column == k, value, extra)
        deal.put(way, Y_COT, extra)
    deal.finish()
    for t in range(2):
        for i in range(Q):
            own_cot_ref[2 * i + t] = tile_of(cot_ref, i, t)


def is_right(near):
    return is_even("gy") if near else jnp.logical_not(is_even("gy"))


def half_lanes(right):
    row, lane, column, depth = iotas()
    return lane // (LANES // 2) == jnp.where(right, 0, 1)


def from_y(message_ref, near):
    row, lane, column, depth = iotas()
    ref = Unpacking(message_ref, layouts()[0])
    right = is_right(near)

    def population(i):
        return jnp.where(right, ref[2 * i], ref[2 * i + 1])

    def cotangent(i):
        values = []
        for way, place, far in ((1, 1, 0), (-1, 2, 1)):
            deep = 3 - way * VELOCITIES[i][1]
            value = columns(ref[2 * i + far], way * (4 - deep))
            if i in turned(1, way):
                extra = columns(ref[Y_COT], place - turned(1, way).index(i))
                value = jnp.where(column == place, extra, value)
            values.append(value)
        return jnp.where(right, values[1], values[0])

    def codes(s):
        return ref[(Y_CODE1, Y_CODE2, Y_CODE3)[s - 1]]

    def outer(i):
        left, above = ref[2 * i], ref[2 * i + 1]
        if i in turned(1, 1):
            above = columns(ref[Y_POP], -turned(1, 1).index(i))
        if i in turned(1, -1):
            left = columns(ref[Y_POP], 3 - turned(1, -1).index(i))
        return jnp.where(right, above, left)

    def outer_code():
        return jnp.where(right, columns(ref[Y_CODE3], 1), columns(ref[Y_CODE3], 3))

    return population, cotangent, codes, outer, outer_code


def mix_lines(deal, at, pop, cot, deep, way):
    row, lane, column, depth = iotas()
    if way == 1:
        mixed = jnp.where(row >= deep, pop, lines(cot, deep))
    else:
        mixed = jnp.where(row < ROWS - deep, pop, lines(cot, -deep))
    deal.put(way, at, mixed)


def pack_lines(deal, first, population, cotangent):
    row, lane, column, depth = iotas()

    for i in range(Q):
        pop, cot = population(i), cotangent(i)
        for way in (1, -1):
            mix_lines(deal, first + i, pop, cot, 3 - way * VELOCITIES[i][0], way)
    for way in (1, -1):
        extra = None
        for k, i in enumerate(turned(0, -way)):
            value = lines(population(i), k - (3 if way == 1 else 4))
            extra = value if extra is None else jnp.where(row == k, value, extra)
        for k, i in enumerate(turned(0, way)):
            value = lines(cotangent(i), 4 + k - (5 if way == 1 else 2))
            extra = jnp.where(row == 4 + k, value, extra)
        deal.put(way, first + X_EXTRA, extra)


def pack_neighbour(deal, lanes, message_ref, near):
    ring, code13, code2, tiles = x_places(lanes)
    population, cotangent, codes, outer, outer_code = from_y(message_ref, near)
    pack_lines(deal, X_LANE * (lanes - 1), population, cotangent)
    kept = half_lanes(is_right(near))
    for n in range(X_HALVES):
        first, second = (outer(2 * n - 1), outer(2 * n)) if n else (outer(0), outer_code())
        deal.put_both(ring + n, jnp.where(kept, first, pltpu.roll(second, LANES // 2, 1)))
    for way in (1, -1):
        mix_lines(deal, code13 + lanes - 1, codes(1), codes(3), 3, way)
    deal.put_both(tiles - 1, codes(2))


def pack_near(own_ref, cot_ref, field_ref, message_ref, first_ref, second_ref):
    row, lane, column, depth = iotas()
    deal = Deal(is_even("gx"), first_ref, second_ref, layouts()[1])
    ring, code13, code2, tiles = x_places(3)
    for t in range(2):
        pack_lines(
            deal,
            X_LANE * t,
            lambda i: own_ref[2 * i + t],
            lambda i: cot_ref[2 * i + t],
        )
        code = jnp.where(depth == NZ - 1, field_ref[2 * OWN_PHI + t], field_ref[2 + t])
        for way in (1, -1):
            mix_lines(deal, code13 + t, code, field_ref[6 + t], 3, way)
    first, second = field_ref[4], lines(field_ref[5], 4)
    deal.put(1, code2, jnp.where(row >= 4, first, second))
    deal.put(-1, code2, jnp.where(row < 4, first, second))
    pack_neighbour(deal, 3, message_ref, True)
    deal.finish()


def pack_far(message_ref, first_ref, second_ref):
    deal = Deal(is_even("gx"), first_ref, second_ref, layouts()[2])
    pack_neighbour(deal, 1, message_ref, False)
    deal.finish()


def from_x(ref, n, way, lanes):
    row, lane, column, depth = iotas()
    ring, code13, code2, _ = x_places(lanes)
    first = X_LANE * n

    def population(i):
        value = ref[first + i]
        if i in turned(0, -way):
            place = 3 if way == 1 else 4
            extra = lines(ref[first + X_EXTRA], place - turned(0, -way).index(i))
            value = jnp.where(row == place, extra, value)
        return value

    def cotangent(i):
        value = lines(ref[first + i], -way * (3 - way * VELOCITIES[i][0]))
        if i in turned(0, way):
            place = 5 if way == 1 else 2
            extra = lines(ref[first + X_EXTRA], place - 4 - turned(0, way).index(i))
            value = jnp.where(row == place, extra, value)
        return value

    def codes(s):
        if s == 2:
            return lines(ref[code2 + n // 2], 4 * (n % 2))
        value = ref[code13 + n]
        return value if s == 1 else lines(value, -3 * way)

    def outer(i):
        value = ref[ring + (i + 1) // 2]
        return pltpu.roll(value, LANES // 2, 1) if i and i % 2 == 0 else value

    def outer_code():
        return pltpu.roll(ref[ring], LANES // 2, 1)

    return population, cotangent, codes, outer, outer_code


def sides(first_ref, second_ref, axis, layout):
    even = is_even(axis)
    picks = Pick(even, second_ref, first_ref), Pick(even, first_ref, second_ref)
    return [Unpacking(pick, layout) for pick in picks]


def own_rows(step=0):
    return pl.ds(ROWS + step, ROWS)


def halo_rows(step=0):
    return pl.ds({0: 2 * ROWS, -1: 2 * ROWS - 1, 1: 1}[step], ROWS)


def put_halo(ref, at, halo):
    ref[at, pl.ds(0, ROWS), :] = halo
    ref[at, halo_rows(), :] = halo


def put_ring(ref, at, own, halo):
    ref[at, own_rows(), :] = own
    put_halo(ref, at, halo)


def expand(code):
    row, lane, column, depth = iotas()
    top = depth == NZ - 1
    phi = jnp.where(top, code, 0.0)
    for step in (1, 2, 4, 8, 16):
        phi = phi + pltpu.roll(phi, LANES - step, 1)
    return jnp.where(top, 0.0, code), phi


def in_groups(size=8):
    return [range(first, min(first + size, Q)) for first in range(0, Q, size)]


def lay_own(c, population, cotangent, codes, code_phi, pop, cot, wide, field):
    for group in in_groups():
        pops = [population(i) for i in group]
        cots = [cotangent(i) for i in group] if cotangent is not None else []
        for i, value in zip(group, pops):
            pop[5 * i + c, pl.ds(2 * ROWS, ROWS), :] = value
        for i, value in zip(group, cots):
            cot[4 * i + c - 1, own_rows(), :] = value
    for n in range(2):
        wide[n, c, 1] = code_phi[n]
    if cotangent is not None:
        field[0, c - 1, 0], field[1, c - 1, 0] = code_phi[1], code_phi[0]
        for s in (2, 3):
            field[s, c - 1, 0] = codes(s)


def lay_halo(c, below, above, pop, cot, wide, field):
    row, lane, column, depth = iotas()
    for group in in_groups():
        pops = [(below[0](i), above[0](i)) for i in group]
        cots = []
        if below[1] is not None:
            cots = [jnp.where(row < 4, above[1](i), below[1](i)) for i in group]
        for i, (before, behind) in zip(group, pops):
            pop[5 * i + c, pl.ds(ROWS, ROWS), :] = before
            pop[5 * i + c, pl.ds(3 * ROWS, ROWS), :] = behind
        for i, value in zip(group, cots):
            put_halo(cot, 4 * i + c - 1, value)
    before, behind = expand(below[2](1)), expand(above[2](1))
    for n in range(2):
        wide[n, c, 0], wide[n, c, 2] = before[n], behind[n]
    if below[1] is not None:
        for n, place in ((0, 1), (1, 0)):
            field[place, c - 1, 1] = jnp.where(row < 4, behind[n], before[n])
        for s in (2, 3):
            field[s, c - 1, 1] = jnp.where(row < 4, above[2](s), below[2](s))


def near_tile():
    return jnp.where(is_right(True), 4, 1)


def lay_out(
    near_y_ref,
    far_y_ref,
    first_near_ref,
    second_near_ref,
    own_ref,
    field_ref,
    cot_ref,
    pop,
    cot,
    wide,
    field,
):
    spaces = pop, cot, wide, field
    below, above = sides(first_near_ref, second_near_ref, "gx", layouts()[1])
    for t in range(2):
        lay_own(
            2 + t,
            lambda i: own_ref[2 * i + t],
            lambda i: cot_ref[2 * i + t],
            lambda s: field_ref[2 * s + t],
            (field_ref[2 + t], field_ref[2 * OWN_PHI + t]),
            *spaces,
        )
        lay_halo(2 + t, from_x(below, t, 1, 3), from_x(above, t, -1, 3), *spaces)
    near, far = from_y(near_y_ref, True), from_y(far_y_ref, False)
    for c, (population, cotangent, codes, _, _) in ((near_tile(), near), (5 - near_tile(), far)):
        lay_own(c, population, cotangent, codes, expand(codes(1)), *spaces)
    kept = half_lanes(is_right(True))
    lay_own(
        0,
        lambda i: jnp.where(kept, near[3](i), far[3](i)),
        None,
        None,
        expand(jnp.where(kept, near[4](), far[4]())),
        *spaces,
    )
    lay_halo(near_tile(), from_x(below, 2, 1, 3), from_x(above, 2, -1, 3), *spaces)


def lay_far(near_refs, far_refs, spaces):
    nears, fars = (
        [
            from_x(ref, lanes - 1, way, lanes)
            for ref, way in zip(sides(*refs, "gx", layout), (1, -1))
        ]
        for refs, layout, lanes in zip((near_refs, far_refs), layouts()[1:], (3, 1))
    )
    lay_halo(5 - near_tile(), *fars, *spaces)
    kept = half_lanes(is_right(True))
    ring = [
        (
            lambda i, near=near, far=far: jnp.where(kept, near[3](i), far[3](i)),
            None,
            lambda s, near=near, far=far: jnp.where(kept, near[4](), far[4]()),
        )
        for near, far in zip(nears, fars)
    ]
    lay_halo(0, *ring, *spaces)


def steps_kernel(
    sizes,
    state_ref,
    own_field_ref,
    names_ref,
    first_near_ref,
    second_near_ref,
    first_far_ref,
    second_far_ref,
    *refs,
):
    adjoint_ref, panel_ref, pop_a, ring_a, wide, field, pop_b, ring_b, saved, mom, grad = refs[4:]
    size_x, size_y = sizes
    lay_far(
        (first_near_ref, second_near_ref),
        (first_far_ref, second_far_ref),
        (pop_a, ring_a, wide, field),
    )

    at_x, at_y = lax.axis_index("gx"), lax.axis_index("gy")
    edges = (
        jnp.where(at_x == 0, 1, 0),
        jnp.where(at_x == size_x - 1, 1, 0),
        jnp.where(at_y == 0, 1, 0),
        jnp.where(at_y == size_y - 1, 1, 0),
    )
    row, lane, column, depth = iotas()
    after = row < 4

    def masks_of(tile, first, r):
        return wall_masks(r == 0, tile == first, tile == first + 1, edges)

    def neighbours(tile, tiles):
        if isinstance(tile, int):
            return {0: tile, -1: (tile - 1) % tiles, 1: (tile + 1) % tiles}
        return {0: tile, -1: lax.rem(tile + tiles - 1, tiles), 1: lax.rem(tile + 1, tiles)}

    def from_wide(ref, tile, r):
        step = neighbours(tile, 5)

        def load(i, tile_step, row_step, move):
            at = 5 * i + step[tile_step]
            before, own, behind = (ref[at, pl.ds(ROWS * n + row_step, ROWS), :] for n in (1, 2, 3))
            return (own, jnp.where(after, behind, before), before, behind)[r]

        return load

    def from_ring(ref, tile, tiles, r):
        step = neighbours(tile, tiles)

        def load(i, tile_step, row_step, move):
            rows = own_rows(row_step) if r == 0 else halo_rows(row_step)
            return ref[tiles * i + step[tile_step], rows, :]

        return load

    def from_outer(ref, r):
        def load(i, tile_step, row_step, move):
            rows = own_rows(row_step) if r == 0 else halo_rows(row_step)
            if tile_step:
                return ref[4 * i + (2 if tile_step < 0 else 1), rows, :]
            cut = {0: 2, 1: 1, -1: 3}[move]
            return jnp.where(column < cut, ref[4 * i + 3, rows, :], ref[4 * i, rows, :])

        return load

    def note(s, tile, r, parts):
        for n, value in enumerate(parts[2:4] + tuple(parts[4])):
            mom[s - 1, n, tile, r] = value

    def first_step(tile, carry):
        place = lax.rem(tile + 4, 5)
        halo = []
        for r in (2, 0, 3):
            f = stream_tile(from_wide(pop_a, tile, r), 1, masks_of(tile, 2, r), lane)
            parts = moments(f)
            at = {2: 0, 0: 1, 3: 2}[r]
            g = collide(f, wide[0, tile, at], wide[1, tile, at], parts)
            if r == 0:
                note(1, place, 0, parts)
                for i in range(Q):
                    saved[0, i, place] = f[i]
            else:
                halo.append(parts[2:4] + tuple(parts[4]))
            for i in range(Q):
                pop_b[5 * i + tile, pl.ds(ROWS * (at + 1), ROWS), :] = g[i]
        for n in range(5):
            mom[0, n, place, 1] = jnp.where(after, halo[1][n], halo[0][n])
        return carry

    lax.fori_loop(0, 5, first_step, 0, unroll=True)

    def second_step(tile, carry):
        out = []
        for r in range(2):
            f = stream_tile(from_wide(pop_b, tile + 1, r), 1, masks_of(tile, 1, r), lane)
            parts = moments(f)
            out.append((f, parts, collide(f, field[2, tile, r], field[0, tile, r], parts)))
        for r in range(2):
            note(2, tile, r, out[r][1])
        for i in range(Q):
            saved[1, i, tile] = out[0][0][i]
            put_ring(ring_b, 4 * i + tile, out[0][2][i], out[1][2][i])
        return carry

    lax.fori_loop(0, 4, second_step, 0, unroll=True)

    def third_step(tile, carry):
        out = []
        for r in range(2):
            f = stream_tile(from_ring(ring_b, tile, 4, r), 1, masks_of(tile, 1, r), lane)
            out.append((f, moments(f)))
        for r in range(2):
            note(3, tile, r, out[r][1])
        for i in range(Q):
            saved[2, i, tile] = out[0][0][i]
        return carry

    lax.fori_loop(0, 4, third_step, 0, unroll=True)

    def back_tile(load, s, tile, r, own):
        b = stream_tile(load, -1, masks_of(4 if tile is None else tile, 1, r), lane)

        def read(get):
            return jnp.where(column < 2, get(3), get(0)) if tile is None else get(tile)

        rho, rinv, *u = [read(lambda at: mom[s - 1, n, at, r]) for n in range(5)]
        kind, phi = read(lambda at: field[s, at, r]), read(lambda at: field[0, at, r])
        state = [saved[s - 1, i, tile] for i in range(Q)] if own else None
        back, term = collide_back(b, kind, phi, rho, rinv, u, state)
        if own:
            grad[tile] = term if s == 3 else grad[tile] + term
        return back

    def last_step(tile, carry):
        out = [back_tile(from_ring(ring_a, tile, 4, r), 3, tile, r, r == 0) for r in range(2)]
        for i in range(Q):
            put_ring(ring_b, 4 * i + tile, out[0][i], out[1][i])
        return carry

    lax.fori_loop(0, 4, last_step, 0, unroll=True)

    for k, tile in enumerate((1, 2, None)):
        out = []
        for r in range(2):
            load = from_outer(ring_b, r) if tile is None else from_ring(ring_b, tile, 4, r)
            out.append(back_tile(load, 2, tile, r, r == 0 and tile is not None))
        for i in range(Q):
            put_ring(ring_a, 3 * i + k, out[0][i], out[1][i])

    for k, tile in enumerate((1, 2, None)):
        out = []
        for r in range(2):
            load = from_ring(ring_a, k, 3, r)
            out.append(back_tile(load, 1, tile, r, r == 0 and tile is not None))
        for i in range(Q):
            put_ring(ring_b, 3 * i + k, out[0][i], out[1][i])

    panel = lax.broadcasted_iota(jnp.int32, panel_ref.shape, 1)
    sums = jnp.zeros(panel_ref.shape, jnp.float32)
    for t in range(2):
        b = stream_tile(from_ring(ring_b, t, 3, 0), -1, masks_of(t, 0, 0), lane)
        f = [state_ref[2 * i + t] for i in range(Q)]
        kind, phi = own_field_ref[t], own_field_ref[2 * OWN_PHI + t]
        _, _, rho, rinv, u = moments(f)
        back, term = collide_back(b, kind, phi, rho, rinv, u, f)
        for i in range(Q):
            adjoint_ref[i, :, pl.ds(t * LANES, LANES)] = back[i]
        term = term + grad[t + 1]
        for part in range(2):
            amount = jnp.sum(jnp.where((row < 4) == (part == 0), term, 0.0))
            name = names_ref[t, 4 * part : 4 * part + 1, 0:1]
            sums = sums + jnp.where(panel == name, amount, 0.0)
    panel_ref[...] = sums


def finish(parts_ref, adjoint_ref, sums_hbm, adjoint_hbm, sums_ref, sems):
    adjoint_copy = pltpu.make_async_copy(adjoint_ref, adjoint_hbm, sems.at[0])
    adjoint_copy.start()
    sums_ref[...] = jnp.sum(parts_ref[...], axis=0)
    sums_copy = pltpu.make_async_copy(sums_ref, sums_hbm, sems.at[1])
    sums_copy.start()
    sums_copy.wait()
    adjoint_copy.wait()


VMEM = pl.BlockSpec(memory_space=pltpu.VMEM)
HBM = pl.BlockSpec(memory_space=pltpu.HBM)


def shape_of(*dims):
    return jax.ShapeDtypeStruct(dims, jnp.float32)


def tiles_of(count):
    return shape_of(count, ROWS, LANES)


def on_device(sizes, checkpoint, cotangent, cell_codes, porosity, baffle_index):
    size_x, size_y = sizes
    panels = porosity.shape[0]
    devices = size_x * size_y
    y_layout, near_layout, far_layout = layouts()

    params = pltpu.CompilerParams(vmem_limit_bytes=32 * 1024 * 1024)

    def call(kernel, out_shape, in_specs, scratch=(), name=None, aliases={}):
        return pl.pallas_call(
            kernel,
            out_shape=out_shape,
            in_specs=in_specs,
            out_specs=jax.tree.map(lambda _: VMEM, out_shape),
            scratch_shapes=scratch,
            input_output_aliases=aliases,
            compiler_params=params,
            name=name,
        )

    def swap(value, axis, size):
        return lax.ppermute(value, axis, [(i, i ^ 1) for i in range(size) if i ^ 1 < size])

    def swap_between(value, axis, size):
        pairs = [(i, i + 1) for i in range(1, size - 1, 2)]
        return lax.ppermute(value, axis, pairs + [(j, i) for i, j in pairs])

    def swap_inner(value):
        pairs = [
            (i * size_y + y, (i + 1) * size_y + y)
            for i in range(1, size_x - 1, 2)
            for y in range(1, size_y - 1)
        ]
        return lax.ppermute(value, ("gx", "gy"), pairs + [(j, i) for i, j in pairs])

    arguments = [
        pltpu.with_memory_space_constraint(value, pltpu.HBM)
        for value in (checkpoint, cotangent, cell_codes, baffle_index, porosity)
    ]
    near_y, far_y, own, state, cot, field, names = call(
        pack_own,
        (tiles_of(y_layout.size),) * 2
        + (tiles_of(2 * Q),) * 3
        + (tiles_of(2 * OWN_PHI + 2), jax.ShapeDtypeStruct((2, ROWS, LANES), jnp.int32)),
        [HBM] * 5,
        [
            pltpu.VMEM((Q, ROWS, 2 * LANES), jnp.float32),
            pltpu.VMEM((Q, ROWS, 2 * LANES), jnp.float32),
            pltpu.VMEM((STEPS, ROWS, 2 * LANES), jnp.int32),
            pltpu.SMEM(baffle_index.shape, jnp.int32),
            pltpu.SMEM(porosity.shape, jnp.float32),
            pltpu.SemaphoreType.DMA((5,)),
        ],
        name="pack_own",
    )(*arguments)
    near_y = swap(near_y, "gy", size_y)
    far_y = swap_between(far_y, "gy", size_y)
    first_near, second_near = call(
        pack_near,
        (tiles_of(near_layout.size), tiles_of(near_layout.size + 1)),
        [VMEM] * 4,
        name="pack_near",
    )(own, cot, field, near_y)
    second_near = swap_between(second_near, "gx", size_x)
    first_near = swap(first_near, "gx", size_x)
    first_far, second_far = call(
        pack_far,
        (tiles_of(far_layout.size), tiles_of(far_layout.size + 1)),
        [VMEM],
        name="pack_far",
    )(far_y)
    second_far = swap_inner(second_far)
    first_far = swap(first_far, "gx", size_x)
    spaces = (
        shape_of(5 * Q, 5 * ROWS, LANES),
        shape_of(4 * Q, 3 * ROWS, LANES),
        shape_of(2, 5, 3, ROWS, LANES),
        shape_of(4, 4, 2, ROWS, LANES),
    )
    laid = call(lay_out, spaces, [VMEM] * 7, name="lay_out")(
        near_y, far_y, first_near, second_near, own, field, cot
    )
    adjoint, sums, *_ = call(
        functools.partial(steps_kernel, sizes),
        (pltpu.VMEM((Q, ROWS, 2 * LANES), jnp.float32), shape_of(devices, panels)) + spaces,
        [VMEM] * 11,
        [
            pltpu.VMEM((5 * Q, 5 * ROWS, LANES), jnp.float32),
            pltpu.VMEM((4 * Q, 3 * ROWS, LANES), jnp.float32),
            pltpu.VMEM((3, Q, 5, ROWS, LANES), jnp.float32),
            pltpu.VMEM((3, 5, 5, 2, ROWS, LANES), jnp.float32),
            pltpu.VMEM((4, ROWS, LANES), jnp.float32),
        ],
        name="steps",
        aliases={7 + n: 2 + n for n in range(4)},
    )(state, field, names, first_near, second_near, first_far, second_far, *laid)
    gathered = lax.all_to_all(sums, ("gx", "gy"), 0, 0, tiled=True)
    totals, adjoint = pl.pallas_call(
        finish,
        out_shape=(shape_of(1, panels), shape_of(Q, ROWS, 2 * LANES)),
        in_specs=[VMEM, VMEM],
        out_specs=(HBM, HBM),
        scratch_shapes=[pltpu.VMEM((1, panels), jnp.float32), pltpu.SemaphoreType.DMA((2,))],
        compiler_params=params,
        name="finish",
    )(gathered.reshape(devices, 1, panels), adjoint)
    return adjoint, totals.reshape(panels)


def solution(mesh):
    sizes = (mesh.shape["gx"], mesh.shape["gy"])
    in_specs = (P(None, "gx", "gy"), P(None, "gx", "gy"), P(None, "gx", "gy"), P(), P("gx", "gy"))
    out_specs = (P(None, "gx", "gy"), P())
    return jax.shard_map(
        functools.partial(on_device, sizes),
        mesh=mesh,
        in_specs=in_specs,
        out_specs=out_specs,
        check_vma=False,
    )
```

```python
import functools

import jax
import jax.numpy as jnp
import numpy as np
from jax import lax
from jax.experimental import pallas as pl
from jax.experimental.pallas import tpu as pltpu
from jax.sharding import PartitionSpec as P

Q = 19
STEPS = 4
NZ = 32
ROWS = 8
LANES = 128
OMEGA = 1.6
ACCEL = (0.002, 0.0, -0.003)
SHIFT = tuple(a / OMEGA for a in ACCEL)

VELOCITIES = [
    (0, 0, 0),
    (1, 0, 0),
    (-1, 0, 0),
    (0, 1, 0),
    (0, -1, 0),
    (0, 0, 1),
    (0, 0, -1),
    (1, 1, 0),
    (-1, -1, 0),
    (1, -1, 0),
    (-1, 1, 0),
    (1, 0, 1),
    (-1, 0, -1),
    (1, 0, -1),
    (-1, 0, 1),
    (0, 1, 1),
    (0, -1, -1),
    (0, 1, -1),
    (0, -1, 1),
]
OPPOSITE = [0, 2, 1, 4, 3, 6, 5, 8, 7, 10, 9, 12, 11, 14, 13, 16, 15, 18, 17]
PAIRS = [(i, i + 1) for i in range(1, Q, 2)]
W_REST, W_AXIS, W_DIAG = 1.0 / 3.0, 1.0 / 18.0, 1.0 / 36.0

Y_CODE1, Y_CODE2, Y_CODE3, Y_POP, Y_COT = 38, 39, 40, 41, 42
Y_TILES = 43
X_EXTRA = 19
X_LANE = 20
X_HALVES = 10


def x_places(lanes):
    ring = X_LANE * lanes
    code13 = ring + X_HALVES
    code2 = code13 + lanes
    return ring, code13, code2, code2 + (lanes + 1) // 2


EMPTY = 25
FREE = NZ - EMPTY
WEIGHTS = [W_REST] + [W_AXIS] * 6 + [W_DIAG] * 12
LEVEL = [i for i, v in enumerate(VELOCITIES) if v[2] < 1]
OWN_PHI = 4


def turned(axis, outward):
    return [i for i, v in enumerate(VELOCITIES) if v[axis] == outward and sum(map(abs, v)) == 2]


def total(values):
    values = list(values)
    while len(values) > 1:
        values = [a + b for a, b in zip(values[::2], values[1::2])] + (
            [values[-1]] if len(values) % 2 else []
        )
    return values[0]


def along(vector, three):
    terms = None
    for c, value in zip(vector, three):
        if c == 0:
            continue
        if terms is None:
            terms = value if c > 0 else -value
        else:
            terms = terms + value if c > 0 else terms - value
    return terms


def moments(f):
    plus = {i: f[i] + f[o] for i, o in PAIRS}
    minus = {i: f[i] - f[o] for i, o in PAIRS}
    rho = total([f[0]] + [plus[i] for i, _ in PAIRS])
    rinv = 1.0 / rho
    u = []
    for axis in range(3):
        terms = [
            minus[i] if VELOCITIES[i][axis] > 0 else -minus[i]
            for i, _ in PAIRS
            if VELOCITIES[i][axis] != 0
        ]
        u.append(total(terms) * rinv + SHIFT[axis])
    return plus, minus, rho, rinv, u


def coefficients(kind, phi, rinv):
    baffle = kind == 3.0
    gas = kind == 0.0
    even = jnp.where(gas, 0.0, jnp.where(baffle, 0.5 - 0.5 * OMEGA * phi, 0.5 * (1.0 - OMEGA)))
    odd = jnp.where(
        gas, 0.0, jnp.where(baffle, (1.0 - 0.5 * OMEGA) * phi - 0.5, 0.5 * (1.0 - OMEGA))
    )
    slope = jnp.where(
        baffle,
        OMEGA * phi,
        jnp.where(kind == 1.0, OMEGA, jnp.where(kind == 2.0, OMEGA * rinv, 0.0)),
    )
    return even, odd, slope


def collide(f, kind, phi, parts):
    plus, minus, rho, rinv, u = parts
    even, odd, slope = coefficients(kind, phi, rinv)
    scale = slope * rho
    rest = 1.0 - 1.5 * (u[0] * u[0] + u[1] * u[1] + u[2] * u[2])
    base = scale * rest + jnp.where(kind == 0.0, 1.0, 0.0)
    out = [None] * Q
    out[0] = 2.0 * even * f[0] + W_REST * base
    for weight, pairs in ((W_AXIS, PAIRS[:3]), (W_DIAG, PAIRS[3:])):
        flat = weight * base
        three = (3.0 * weight) * scale
        for i, o in pairs:
            cu = along(VELOCITIES[i], u)
            lin = three * cu
            ev = even * plus[i] + (flat + 1.5 * lin * cu)
            od = odd * minus[i] + lin
            out[i] = ev + od
            out[o] = ev - od
    return out


def collide_back(b, kind, phi, rho, rinv, u, state=None):
    even, odd, slope = coefficients(kind, phi, rinv)
    plus = {i: b[i] + b[o] for i, o in PAIRS}
    minus = {i: b[i] - b[o] for i, o in PAIRS}
    rest = 1.0 - 1.5 * (u[0] * u[0] + u[1] * u[1] + u[2] * u[2])
    u_half = [1.5 * c for c in u]
    weighted = W_REST * b[0]
    energy = 0.0
    vector = [0.0, 0.0, 0.0]
    for weight, pairs in ((W_AXIS, PAIRS[:3]), (W_DIAG, PAIRS[3:])):
        weighted = weighted + weight * total([plus[i] for i, _ in pairs])
        energies, parts = [], ([], [], [])
        for i, _ in pairs:
            cu = along(VELOCITIES[i], u)
            half = along(VELOCITIES[i], u_half) * plus[i]
            first = minus[i] + half
            energies.append(cu * first)
            second = first + half
            for axis in range(3):
                c = VELOCITIES[i][axis]
                if c:
                    parts[axis].append(second if c > 0 else -second)
        energy = energy + (3.0 * weight) * total(energies)
        vector = [vector[k] + (3.0 * weight) * total(parts[k]) for k in range(3)]
    energy = energy + rest * weighted
    vector = [vector[k] - (3.0 * weighted) * u[k] for k in range(3)]
    push = [slope * v for v in vector]
    inner = total([push[k] * (u[k] - SHIFT[k]) for k in range(3)])
    shared = jnp.where(kind == 2.0, 0.0, slope) * energy - inner
    out = [None] * Q
    out[0] = 2.0 * even * b[0] + shared
    for i, o in PAIRS:
        ev = even * plus[i] + shared
        od = odd * minus[i] + along(VELOCITIES[i], push)
        out[i] = ev + od
        out[o] = ev - od
    if state is None:
        return out, None
    evens = total([plus[i] * (state[i] + state[o]) for i, o in PAIRS])
    odds = total([minus[i] * (state[i] - state[o]) for i, o in PAIRS])
    term = (
        -OMEGA * (b[0] * state[0] + 0.5 * evens)
        + (1.0 - 0.5 * OMEGA) * odds
        + OMEGA * rho * energy
    )
    return out, jnp.where(kind == 3.0, term, 0.0)


def wall_masks(sign_rows, own_low, own_high, edges):
    lane = lax.broadcasted_iota(jnp.int32, (ROWS, LANES), 1)
    row = lax.broadcasted_iota(jnp.int32, (ROWS, LANES), 0)
    x_low, x_high, y_low, y_high = edges
    depth = lane % NZ
    masks = {}
    masks[2, 1] = depth == 0
    masks[2, -1] = depth == NZ - 1
    masks[1, 1] = lane < jnp.where(own_low, y_low * NZ, 0)
    masks[1, -1] = lane >= jnp.where(own_high, LANES - y_high * NZ, LANES)
    if sign_rows:
        masks[0, 1] = row < x_low
        masks[0, -1] = row >= ROWS - x_high
    return masks


def stream_tile(load, sign, masks, lane):
    cross_low, cross_high = lane >= LANES - NZ, lane < NZ
    combined = {}
    out = []
    for i, vector in enumerate(VELOCITIES):
        v = tuple(sign * c for c in vector)
        value = load(i, 0, -v[0], v[1])
        if v[1] == 1:
            value = jnp.where(cross_low, load(i, -1, -v[0], 1), value)
        elif v[1] == -1:
            value = jnp.where(cross_high, load(i, 1, -v[0], -1), value)
        amount = (v[1] * NZ + v[2]) % LANES
        if amount:
            value = pltpu.roll(value, amount, 1)
        outside = None
        if v not in combined:
            for axis in range(3):
                if v[axis] and (axis, v[axis]) in masks:
                    wall = masks[axis, v[axis]]
                    outside = wall if outside is None else outside | wall
            combined[v] = outside
        outside = combined[v]
        if outside is not None:
            value = jnp.where(outside, load(OPPOSITE[i], 0, 0, 0), value)
        out.append(value)
    return out


def iotas():
    row = lax.broadcasted_iota(jnp.int32, (ROWS, LANES), 0)
    lane = lax.broadcasted_iota(jnp.int32, (ROWS, LANES), 1)
    return row, lane, lane // NZ, lane % NZ


def columns(value, count):
    amount = (count * NZ) % LANES
    return pltpu.roll(value, amount, 1) if amount else value


def lines(value, count):
    amount = count % ROWS
    return pltpu.roll(value, amount, 0) if amount else value


class Layout:
    def __init__(self, count, guests, fills):
        self.fills = fills
        hosts = [at for at in fills if at not in guests]
        self.hosts = {at: hosts[4 * n : 4 * n + 4] for n, at in enumerate(guests)}
        self.guests = guests
        kept = [at for at in range(count) if at not in guests]
        self.place = {at: n for n, at in enumerate(kept)}
        self.size = len(kept)


class Packing:
    def __init__(self, ref, layout):
        self.ref, self.layout, self.held = ref, layout, {}

    def __setitem__(self, at, value):
        if at in self.layout.guests:
            self.held[at] = value
        else:
            self.ref[self.layout.place[at]] = value

    def finish(self):
        row, lane, column, depth = iotas()
        spare = depth >= EMPTY
        for at, value in self.held.items():
            for k, host in enumerate(self.layout.hosts[at]):
                place = self.layout.place[host]
                moved = pltpu.roll(value, EMPTY - FREE * k, 1)
                self.ref[place] = jnp.where(spare, moved, self.ref[place])
        for place in range(self.layout.size, self.ref.shape[0]):
            self.ref[place] = jnp.zeros((ROWS, LANES), jnp.float32)


class Unpacking:
    def __init__(self, source, layout):
        self.source, self.layout, self.cache = source, layout, {}
        self.changed = set(layout.guests).union(*layout.hosts.values())

    def __getitem__(self, at):
        if at not in self.cache:
            self.cache[at] = self.read(at)
        return self.cache[at]

    def read(self, at):
        row, lane, column, depth = iotas()
        layout = self.layout
        if at in layout.guests:
            value = None
            for k, host in enumerate(layout.hosts[at]):
                tile = self.source[layout.place[host]]
                moved = pltpu.roll(tile, LANES - (EMPTY - FREE * k), 1)
                value = moved if value is None else jnp.where(depth >= FREE * k, moved, value)
        else:
            value = self.source[layout.place[at]]
        if at in self.changed:
            value = jnp.where(depth >= EMPTY, layout.fills[at], value)
        return value


def layouts():
    y_fills = {2 * i + t: WEIGHTS[i] for i in LEVEL for t in range(2)}
    y_fills.update({Y_POP: W_DIAG, Y_CODE2: 0.0})
    out = [Layout(Y_TILES, [2 * i for i in LEVEL[:6]], y_fills)]
    for lanes, count in ((3, 10), (1, 4)):
        ring, _, code2, tiles = x_places(lanes)
        fills = {ring + n: WEIGHTS[2 * n] for n in range(1, X_HALVES)}
        fills.update({at: 0.0 for at in range(code2, tiles)})
        fills.update({X_LANE * n + i: WEIGHTS[i] for n in range(lanes) for i in LEVEL})
        guests = [X_LANE * (lanes - 1) + i for i in LEVEL[:count]]
        out.append(Layout(tiles, guests, fills))
    return out


class Pick:
    def __init__(self, flag, first, second):
        self.flag, self.first, self.second = flag, first, second

    def __getitem__(self, at):
        return jnp.where(self.flag, self.first[at], self.second[at])


class Deal:
    def __init__(self, even, first, second, layout):
        self.even, self.held, self.ready = even, {}, []
        self.first, self.second = Packing(first, layout), Packing(second, layout)

    def put(self, way, at, value):
        if (-way, at) not in self.held:
            self.held[way, at] = value
            return
        other = self.held.pop((-way, at))
        up, down = (value, other) if way == 1 else (other, value)
        self.add(at, jnp.where(self.even, up, down), jnp.where(self.even, down, up))

    def put_both(self, at, value):
        self.add(at, value, value)

    def add(self, *entry):
        self.ready.append(entry)
        if len(self.ready) == 8:
            self.write()

    def write(self):
        for at, first, second in self.ready:
            self.first[at] = first
            self.second[at] = second
        self.ready = []

    def finish(self):
        self.write()
        self.first.finish()
        self.second.finish()


def is_even(axis):
    return lax.rem(lax.axis_index(axis), 2) == 0


def pack_own(
    f_hbm,
    cot_hbm,
    codes_hbm,
    panels_hbm,
    porosity_hbm,
    first_ref,
    second_ref,
    own_ref,
    state_ref,
    own_cot_ref,
    field_ref,
    names_ref,
    f_ref,
    cot_ref,
    codes_ref,
    panels_ref,
    porosity_ref,
    sems,
):
    pieces = (
        (panels_hbm, panels_ref),
        (porosity_hbm, porosity_ref),
        (f_hbm, f_ref),
        (codes_hbm, codes_ref),
        (cot_hbm, cot_ref),
    )
    copies = [
        pltpu.make_async_copy(source, target, sems.at[n])
        for n, (source, target) in enumerate(pieces)
    ]
    for copy in copies:
        copy.start()
    for copy in copies[:4]:
        copy.wait()
    deal = Deal(is_even("gy"), first_ref, second_ref, layouts()[0])
    row, lane, column, depth = iotas()
    top = depth == NZ - 1

    def tile_of(ref, i, t):
        return ref[i, :, pl.ds(t * LANES, LANES)]

    codes, phis = [], []
    for t in range(2):
        names = panels_ref[0, t * LANES], panels_ref[4, t * LANES]
        phi = jnp.where(row < 4, porosity_ref[names[0]], porosity_ref[names[1]])
        names_ref[t] = jnp.where(row < 4, names[0], names[1])
        kinds = [tile_of(codes_ref, s, t).astype(jnp.float32) for s in range(STEPS)]
        f = [tile_of(f_ref, i, t) for i in range(Q)]
        g = collide(f, kinds[0], phi, moments(f))
        for i in range(Q):
            own_ref[2 * i + t] = g[i]
            state_ref[2 * i + t] = f[i]
        for s in range(STEPS):
            field_ref[2 * s + t] = kinds[s]
        field_ref[2 * OWN_PHI + t] = phi
        codes.append([jnp.where(top, phi, kinds[1]), kinds[2], kinds[3]])
    copies[4].wait()
    for i in range(Q):
        for way in (1, -1):
            near, far = (1, 0) if way == 1 else (0, 1)
            deep = 3 - way * VELOCITIES[i][1]
            cot = tile_of(cot_ref, i, near)
            g_far = own_ref[2 * i + far]
            if way == 1:
                mixed = jnp.where(column >= deep, g_far, columns(cot, deep - 4))
            else:
                mixed = jnp.where(column < 4 - deep, g_far, columns(cot, 4 - deep))
            deal.put(way, 2 * i, mixed if far == 0 else own_ref[2 * i])
            deal.put(way, 2 * i + 1, mixed if far == 1 else own_ref[2 * i + 1])
    for way in (1, -1):
        near, far = (1, 0) if way == 1 else (0, 1)
        outer = 3 if way == 1 else 0
        deal.put(way, Y_CODE1, codes[near][0])
        deal.put(way, Y_CODE2, codes[near][1])
        outside = columns(codes[far][0], 3 - 2 * outer)
        deal.put(way, Y_CODE3, jnp.where(column == 3 - outer, outside, codes[near][2]))
        extra = None
        for k, i in enumerate(turned(1, -way)):
            value = columns(own_ref[2 * i + far], k - outer)
            extra = value if extra is None else jnp.where(column == k, value, extra)
        deal.put(way, Y_POP, extra)
        extra = None
        for k, i in enumerate(turned(1, way)):
            value = columns(tile_of(cot_ref, i, near), k - (1 if way == 1 else 2))
            extra = value if extra is None else jnp.where(column == k, value, extra)
        deal.put(way, Y_COT, extra)
    deal.finish()
    for t in range(2):
        for i in range(Q):
            own_cot_ref[2 * i + t] = tile_of(cot_ref, i, t)


def is_right(near):
    return is_even("gy") if near else jnp.logical_not(is_even("gy"))


def half_lanes(right):
    row, lane, column, depth = iotas()
    return lane // (LANES // 2) == jnp.where(right, 0, 1)


def choose(flag, first, second):
    if isinstance(flag, bool):
        return first() if flag else second()
    return jnp.where(flag, first(), second())


def from_y(message_ref, right):
    row, lane, column, depth = iotas()
    ref = Unpacking(message_ref, layouts()[0])

    def population(i):
        return choose(right, lambda: ref[2 * i], lambda: ref[2 * i + 1])

    def cotangent(i):
        def of(way, place, far):
            deep = 3 - way * VELOCITIES[i][1]
            value = columns(ref[2 * i + far], way * (4 - deep))
            if i in turned(1, way):
                extra = columns(ref[Y_COT], place - turned(1, way).index(i))
                value = jnp.where(column == place, extra, value)
            return value

        return choose(right, lambda: of(-1, 2, 1), lambda: of(1, 1, 0))

    def codes(s):
        return ref[(Y_CODE1, Y_CODE2, Y_CODE3)[s - 1]]

    def outer(i):
        def of(way, far):
            if i in turned(1, -way):
                first = 0 if way == -1 else 3
                return columns(ref[Y_POP], first - turned(1, -way).index(i))
            return ref[2 * i + far]

        return choose(right, lambda: of(-1, 1), lambda: of(1, 0))

    def outer_code():
        tile = ref[Y_CODE3]
        return choose(right, lambda: columns(tile, 1), lambda: columns(tile, 3))

    return population, cotangent, codes, outer, outer_code


def mix_lines(deal, at, pop, cot, deep, way):
    row, lane, column, depth = iotas()
    if way == 1:
        mixed = jnp.where(row >= deep, pop, lines(cot, deep))
    else:
        mixed = jnp.where(row < ROWS - deep, pop, lines(cot, -deep))
    deal.put(way, at, mixed)


def pack_lines(deal, first, population, cotangent):
    row, lane, column, depth = iotas()

    for i in range(Q):
        pop, cot = population(i), cotangent(i)
        for way in (1, -1):
            mix_lines(deal, first + i, pop, cot, 3 - way * VELOCITIES[i][0], way)
    for way in (1, -1):
        extra = None
        for k, i in enumerate(turned(0, -way)):
            value = lines(population(i), k - (3 if way == 1 else 4))
            extra = value if extra is None else jnp.where(row == k, value, extra)
        for k, i in enumerate(turned(0, way)):
            value = lines(cotangent(i), 4 + k - (5 if way == 1 else 2))
            extra = jnp.where(row == 4 + k, value, extra)
        deal.put(way, first + X_EXTRA, extra)


def pack_neighbour(deal, lanes, message_ref, right):
    ring, code13, code2, tiles = x_places(lanes)
    population, cotangent, codes, outer, outer_code = from_y(message_ref, right)
    pack_lines(deal, X_LANE * (lanes - 1), population, cotangent)
    kept = half_lanes(right)
    for n in range(X_HALVES):
        first, second = (outer(2 * n - 1), outer(2 * n)) if n else (outer(0), outer_code())
        deal.put_both(ring + n, jnp.where(kept, first, pltpu.roll(second, LANES // 2, 1)))
    for way in (1, -1):
        mix_lines(deal, code13 + lanes - 1, codes(1), codes(3), 3, way)
    deal.put_both(tiles - 1, codes(2))


def pack_near(own_ref, cot_ref, field_ref, message_ref, first_ref, second_ref):
    row, lane, column, depth = iotas()
    deal = Deal(is_even("gx"), first_ref, second_ref, layouts()[1])
    ring, code13, code2, tiles = x_places(3)
    for t in range(2):
        pack_lines(
            deal,
            X_LANE * t,
            lambda i: own_ref[2 * i + t],
            lambda i: cot_ref[2 * i + t],
        )
        code = jnp.where(depth == NZ - 1, field_ref[2 * OWN_PHI + t], field_ref[2 + t])
        for way in (1, -1):
            mix_lines(deal, code13 + t, code, field_ref[6 + t], 3, way)
    first, second = field_ref[4], lines(field_ref[5], 4)
    deal.put(1, code2, jnp.where(row >= 4, first, second))
    deal.put(-1, code2, jnp.where(row < 4, first, second))
    pack_neighbour(deal, 3, message_ref, is_right(True))
    deal.finish()


def pack_far(message_ref, first_ref, second_ref):
    even_x = is_even("gx")

    def pack(right):
        deal = Deal(even_x, first_ref, second_ref, layouts()[2])
        pack_neighbour(deal, 1, message_ref, right)
        deal.finish()

    above = is_right(False)
    pl.when(above)(lambda: pack(True))
    pl.when(jnp.logical_not(above))(lambda: pack(False))


def from_x(ref, n, way, lanes):
    row, lane, column, depth = iotas()
    ring, code13, code2, _ = x_places(lanes)
    first = X_LANE * n

    def population(i):
        value = ref[first + i]
        if i in turned(0, -way):
            place = 3 if way == 1 else 4
            extra = lines(ref[first + X_EXTRA], place - turned(0, -way).index(i))
            value = jnp.where(row == place, extra, value)
        return value

    def cotangent(i):
        value = lines(ref[first + i], -way * (3 - way * VELOCITIES[i][0]))
        if i in turned(0, way):
            place = 5 if way == 1 else 2
            extra = lines(ref[first + X_EXTRA], place - 4 - turned(0, way).index(i))
            value = jnp.where(row == place, extra, value)
        return value

    def codes(s):
        if s == 2:
            return lines(ref[code2 + n // 2], 4 * (n % 2))
        value = ref[code13 + n]
        return value if s == 1 else lines(value, -3 * way)

    def outer(i):
        value = ref[ring + (i + 1) // 2]
        return pltpu.roll(value, LANES // 2, 1) if i and i % 2 == 0 else value

    def outer_code():
        return pltpu.roll(ref[ring], LANES // 2, 1)

    return population, cotangent, codes, outer, outer_code


def sides(first_ref, second_ref, axis, layout):
    even = is_even(axis)
    picks = Pick(even, second_ref, first_ref), Pick(even, first_ref, second_ref)
    return [Unpacking(pick, layout) for pick in picks]


def own_rows(step=0):
    return pl.ds(ROWS + step, ROWS)


def halo_rows(step=0):
    return pl.ds({0: 2 * ROWS, -1: 2 * ROWS - 1, 1: 1}[step], ROWS)


def put_halo(ref, at, halo):
    ref[at, pl.ds(0, ROWS), :] = halo
    ref[at, halo_rows(), :] = halo


def put_ring(ref, at, own, halo):
    ref[at, own_rows(), :] = own
    put_halo(ref, at, halo)


def expand(code):
    row, lane, column, depth = iotas()
    top = depth == NZ - 1
    phi = jnp.where(top, code, 0.0)
    for step in (1, 2, 4, 8, 16):
        phi = phi + pltpu.roll(phi, LANES - step, 1)
    return jnp.where(top, 0.0, code), phi


def in_groups(size=10):
    return [range(first, min(first + size, Q)) for first in range(0, Q, size)]


def lay_own(c, population, cotangent, codes, code_phi, pop, cot, wide, field):
    for group in in_groups():
        pops = [population(i) for i in group]
        cots = [cotangent(i) for i in group] if cotangent is not None else []
        for i, value in zip(group, pops):
            pop[5 * i + c, pl.ds(2 * ROWS, ROWS), :] = value
        for i, value in zip(group, cots):
            cot[4 * i + c - 1, own_rows(), :] = value
    for n in range(2):
        wide[n, c, 1] = code_phi[n]
    if cotangent is not None:
        field[0, c - 1, 0], field[1, c - 1, 0] = code_phi[1], code_phi[0]
        for s in (2, 3):
            field[s, c - 1, 0] = codes(s)


def lay_halo(c, below, above, pop, cot, wide, field):
    row, lane, column, depth = iotas()
    for group in in_groups():
        pops = [(below[0](i), above[0](i)) for i in group]
        cots = []
        if below[1] is not None:
            cots = [jnp.where(row < 4, above[1](i), below[1](i)) for i in group]
        for i, (before, behind) in zip(group, pops):
            pop[5 * i + c, pl.ds(ROWS, ROWS), :] = before
            pop[5 * i + c, pl.ds(3 * ROWS, ROWS), :] = behind
        for i, value in zip(group, cots):
            put_halo(cot, 4 * i + c - 1, value)
    before, behind = expand(below[2](1)), expand(above[2](1))
    for n in range(2):
        wide[n, c, 0], wide[n, c, 2] = before[n], behind[n]
    if below[1] is not None:
        for n, place in ((0, 1), (1, 0)):
            field[place, c - 1, 1] = jnp.where(row < 4, behind[n], before[n])
        for s in (2, 3):
            field[s, c - 1, 1] = jnp.where(row < 4, above[2](s), below[2](s))


def near_tile():
    return jnp.where(is_right(True), 4, 1)


def lay_out(
    near_y_ref,
    far_y_ref,
    first_near_ref,
    second_near_ref,
    own_ref,
    field_ref,
    cot_ref,
    pop,
    cot,
    wide,
    field,
):
    spaces = pop, cot, wide, field
    below, above = sides(first_near_ref, second_near_ref, "gx", layouts()[1])
    for t in range(2):
        lay_own(
            2 + t,
            lambda i: own_ref[2 * i + t],
            lambda i: cot_ref[2 * i + t],
            lambda s: field_ref[2 * s + t],
            (field_ref[2 + t], field_ref[2 * OWN_PHI + t]),
            *spaces,
        )
        lay_halo(2 + t, from_x(below, t, 1, 3), from_x(above, t, -1, 3), *spaces)
    near, far = from_y(near_y_ref, is_right(True)), from_y(far_y_ref, is_right(False))
    for c, (population, cotangent, codes, _, _) in ((near_tile(), near), (5 - near_tile(), far)):
        lay_own(c, population, cotangent, codes, expand(codes(1)), *spaces)
    kept = half_lanes(is_right(True))
    lay_own(
        0,
        lambda i: jnp.where(kept, near[3](i), far[3](i)),
        None,
        None,
        expand(jnp.where(kept, near[4](), far[4]())),
        *spaces,
    )
    lay_halo(near_tile(), from_x(below, 2, 1, 3), from_x(above, 2, -1, 3), *spaces)


def lay_far(near_refs, far_refs, spaces):
    nears, fars = (
        [
            from_x(ref, lanes - 1, way, lanes)
            for ref, way in zip(sides(*refs, "gx", layout), (1, -1))
        ]
        for refs, layout, lanes in zip((near_refs, far_refs), layouts()[1:], (3, 1))
    )
    lay_halo(5 - near_tile(), *fars, *spaces)
    kept = half_lanes(is_right(True))
    ring = [
        (
            lambda i, near=near, far=far: jnp.where(kept, near[3](i), far[3](i)),
            None,
            lambda s, near=near, far=far: jnp.where(kept, near[4](), far[4]()),
        )
        for near, far in zip(nears, fars)
    ]
    lay_halo(0, *ring, *spaces)


def steps_kernel(
    sizes,
    state_ref,
    own_field_ref,
    names_ref,
    first_near_ref,
    second_near_ref,
    first_far_ref,
    second_far_ref,
    *refs,
):
    adjoint_ref, panel_ref, pop_a, ring_a, wide, field, pop_b, ring_b, saved, mom, grad = refs[4:]
    size_x, size_y = sizes
    lay_far(
        (first_near_ref, second_near_ref),
        (first_far_ref, second_far_ref),
        (pop_a, ring_a, wide, field),
    )

    at_x, at_y = lax.axis_index("gx"), lax.axis_index("gy")
    edges = (
        jnp.where(at_x == 0, 1, 0),
        jnp.where(at_x == size_x - 1, 1, 0),
        jnp.where(at_y == 0, 1, 0),
        jnp.where(at_y == size_y - 1, 1, 0),
    )
    row, lane, column, depth = iotas()
    after = row < 4

    def masks_of(tile, first, r):
        return wall_masks(r == 0, tile == first, tile == first + 1, edges)

    def neighbours(tile, tiles):
        if isinstance(tile, int):
            return {0: tile, -1: (tile - 1) % tiles, 1: (tile + 1) % tiles}
        return {0: tile, -1: lax.rem(tile + tiles - 1, tiles), 1: lax.rem(tile + 1, tiles)}

    def from_wide(ref, tile, r):
        step = neighbours(tile, 5)

        def load(i, tile_step, row_step, move):
            at = 5 * i + step[tile_step]
            before, own, behind = (ref[at, pl.ds(ROWS * n + row_step, ROWS), :] for n in (1, 2, 3))
            return (own, jnp.where(after, behind, before), before, behind)[r]

        return load

    def from_ring(ref, tile, tiles, r):
        step = neighbours(tile, tiles)

        def load(i, tile_step, row_step, move):
            rows = own_rows(row_step) if r == 0 else halo_rows(row_step)
            return ref[tiles * i + step[tile_step], rows, :]

        return load

    def from_outer(ref, r):
        def load(i, tile_step, row_step, move):
            rows = own_rows(row_step) if r == 0 else halo_rows(row_step)
            if tile_step:
                return ref[4 * i + (2 if tile_step < 0 else 1), rows, :]
            cut = {0: 2, 1: 1, -1: 3}[move]
            return jnp.where(column < cut, ref[4 * i + 3, rows, :], ref[4 * i, rows, :])

        return load

    def note(s, tile, r, parts):
        for n, value in enumerate(parts[2:4] + tuple(parts[4])):
            mom[s - 1, n, tile, r] = value

    def first_step(tile, carry):
        place = lax.rem(tile + 4, 5)
        halo = []
        for r in (2, 0, 3):
            f = stream_tile(from_wide(pop_a, tile, r), 1, masks_of(tile, 2, r), lane)
            parts = moments(f)
            at = {2: 0, 0: 1, 3: 2}[r]
            g = collide(f, wide[0, tile, at], wide[1, tile, at], parts)
            if r == 0:
                note(1, place, 0, parts)
                for i in range(Q):
                    saved[0, i, place] = f[i]
            else:
                halo.append(parts[2:4] + tuple(parts[4]))
            for i in range(Q):
                pop_b[5 * i + tile, pl.ds(ROWS * (at + 1), ROWS), :] = g[i]
        for n in range(5):
            mom[0, n, place, 1] = jnp.where(after, halo[1][n], halo[0][n])
        return carry

    lax.fori_loop(0, 5, first_step, 0, unroll=True)

    def second_step(tile, carry):
        out = []
        for r in range(2):
            f = stream_tile(from_wide(pop_b, tile + 1, r), 1, masks_of(tile, 1, r), lane)
            parts = moments(f)
            out.append((f, parts, collide(f, field[2, tile, r], field[0, tile, r], parts)))
        for r in range(2):
            note(2, tile, r, out[r][1])
        for i in range(Q):
            saved[1, i, tile] = out[0][0][i]
            put_ring(ring_b, 4 * i + tile, out[0][2][i], out[1][2][i])
        return carry

    lax.fori_loop(0, 4, second_step, 0, unroll=True)

    def third_step(tile, carry):
        out = []
        for r in range(2):
            f = stream_tile(from_ring(ring_b, tile, 4, r), 1, masks_of(tile, 1, r), lane)
            out.append((f, moments(f)))
        for r in range(2):
            note(3, tile, r, out[r][1])
        for i in range(Q):
            saved[2, i, tile] = out[0][0][i]
        return carry

    lax.fori_loop(0, 4, third_step, 0, unroll=True)

    def back_tile(load, s, tile, r, own):
        b = stream_tile(load, -1, masks_of(4 if tile is None else tile, 1, r), lane)

        def read(get):
            return jnp.where(column < 2, get(3), get(0)) if tile is None else get(tile)

        rho, rinv, *u = [read(lambda at: mom[s - 1, n, at, r]) for n in range(5)]
        kind, phi = read(lambda at: field[s, at, r]), read(lambda at: field[0, at, r])
        state = [saved[s - 1, i, tile] for i in range(Q)] if own else None
        back, term = collide_back(b, kind, phi, rho, rinv, u, state)
        if own:
            grad[tile] = term if s == 3 else grad[tile] + term
        return back

    def last_step(tile, carry):
        out = [back_tile(from_ring(ring_a, tile, 4, r), 3, tile, r, r == 0) for r in range(2)]
        for i in range(Q):
            put_ring(ring_b, 4 * i + tile, out[0][i], out[1][i])
        return carry

    lax.fori_loop(0, 4, last_step, 0, unroll=True)

    for k, tile in enumerate((1, 2, None)):
        out = []
        for r in range(2):
            load = from_outer(ring_b, r) if tile is None else from_ring(ring_b, tile, 4, r)
            out.append(back_tile(load, 2, tile, r, r == 0 and tile is not None))
        for i in range(Q):
            put_ring(ring_a, 3 * i + k, out[0][i], out[1][i])

    for k, tile in enumerate((1, 2, None)):
        out = []
        for r in range(2):
            load = from_ring(ring_a, k, 3, r)
            out.append(back_tile(load, 1, tile, r, r == 0 and tile is not None))
        for i in range(Q):
            put_ring(ring_b, 3 * i + k, out[0][i], out[1][i])

    panel = lax.broadcasted_iota(jnp.int32, panel_ref.shape, 1)
    sums = jnp.zeros(panel_ref.shape, jnp.float32)
    for t in range(2):
        b = stream_tile(from_ring(ring_b, t, 3, 0), -1, masks_of(t, 0, 0), lane)
        f = [state_ref[2 * i + t] for i in range(Q)]
        kind, phi = own_field_ref[t], own_field_ref[2 * OWN_PHI + t]
        _, _, rho, rinv, u = moments(f)
        back, term = collide_back(b, kind, phi, rho, rinv, u, f)
        for i in range(Q):
            adjoint_ref[i, :, pl.ds(t * LANES, LANES)] = back[i]
        term = term + grad[t + 1]
        for part in range(2):
            amount = jnp.sum(jnp.where((row < 4) == (part == 0), term, 0.0))
            name = names_ref[t, 4 * part : 4 * part + 1, 0:1]
            sums = sums + jnp.where(panel == name, amount, 0.0)
    panel_ref[...] = sums


def finish(parts_ref, adjoint_ref, sums_hbm, adjoint_hbm, sums_ref, sems):
    adjoint_copy = pltpu.make_async_copy(adjoint_ref, adjoint_hbm, sems.at[0])
    adjoint_copy.start()
    sums_ref[...] = jnp.sum(parts_ref[...], axis=0)
    sums_copy = pltpu.make_async_copy(sums_ref, sums_hbm, sems.at[1])
    sums_copy.start()
    sums_copy.wait()
    adjoint_copy.wait()


VMEM = pl.BlockSpec(memory_space=pltpu.VMEM)
HBM = pl.BlockSpec(memory_space=pltpu.HBM)


def shape_of(*dims):
    return jax.ShapeDtypeStruct(dims, jnp.float32)


def tiles_of(count):
    return shape_of(count, ROWS, LANES)


def on_device(sizes, checkpoint, cotangent, cell_codes, porosity, baffle_index):
    size_x, size_y = sizes
    panels = porosity.shape[0]
    devices = size_x * size_y
    y_layout, near_layout, far_layout = layouts()

    params = pltpu.CompilerParams(vmem_limit_bytes=32 * 1024 * 1024)

    def call(kernel, out_shape, in_specs, scratch=(), name=None, aliases={}):
        return pl.pallas_call(
            kernel,
            out_shape=out_shape,
            in_specs=in_specs,
            out_specs=jax.tree.map(lambda _: VMEM, out_shape),
            scratch_shapes=scratch,
            input_output_aliases=aliases,
            compiler_params=params,
            name=name,
        )

    def swap(value, axis, size):
        return lax.ppermute(value, axis, [(i, i ^ 1) for i in range(size) if i ^ 1 < size])

    def swap_between(value, axis, size):
        pairs = [(i, i + 1) for i in range(1, size - 1, 2)]
        return lax.ppermute(value, axis, pairs + [(j, i) for i, j in pairs])

    def swap_inner(value):
        pairs = [
            (i * size_y + y, (i + 1) * size_y + y)
            for i in range(1, size_x - 1, 2)
            for y in range(1, size_y - 1)
        ]
        return lax.ppermute(value, ("gx", "gy"), pairs + [(j, i) for i, j in pairs])

    arguments = [
        pltpu.with_memory_space_constraint(value, pltpu.HBM)
        for value in (checkpoint, cotangent, cell_codes, baffle_index, porosity)
    ]
    near_y, far_y, own, state, cot, field, names = call(
        pack_own,
        (tiles_of(y_layout.size),) * 2
        + (tiles_of(2 * Q),) * 3
        + (tiles_of(2 * OWN_PHI + 2), jax.ShapeDtypeStruct((2, ROWS, LANES), jnp.int32)),
        [HBM] * 5,
        [
            pltpu.VMEM((Q, ROWS, 2 * LANES), jnp.float32),
            pltpu.VMEM((Q, ROWS, 2 * LANES), jnp.float32),
            pltpu.VMEM((STEPS, ROWS, 2 * LANES), jnp.int32),
            pltpu.SMEM(baffle_index.shape, jnp.int32),
            pltpu.SMEM(porosity.shape, jnp.float32),
            pltpu.SemaphoreType.DMA((5,)),
        ],
        name="pack_own",
    )(*arguments)
    near_y = swap(near_y, "gy", size_y)
    far_y = swap_between(far_y, "gy", size_y)
    first_near, second_near = call(
        pack_near,
        (tiles_of(near_layout.size), tiles_of(near_layout.size + 1)),
        [VMEM] * 4,
        name="pack_near",
    )(own, cot, field, near_y)
    second_near = swap_between(second_near, "gx", size_x)
    first_near = swap(first_near, "gx", size_x)
    first_far, second_far = call(
        pack_far,
        (tiles_of(far_layout.size), tiles_of(far_layout.size + 1)),
        [VMEM],
        name="pack_far",
    )(far_y)
    second_far = swap_inner(second_far)
    first_far = swap(first_far, "gx", size_x)
    spaces = (
        shape_of(5 * Q, 5 * ROWS, LANES),
        shape_of(4 * Q, 3 * ROWS, LANES),
        shape_of(2, 5, 3, ROWS, LANES),
        shape_of(4, 4, 2, ROWS, LANES),
    )
    laid = call(lay_out, spaces, [VMEM] * 7, name="lay_out")(
        near_y, far_y, first_near, second_near, own, field, cot
    )
    adjoint, sums, *_ = call(
        functools.partial(steps_kernel, sizes),
        (pltpu.VMEM((Q, ROWS, 2 * LANES), jnp.float32), shape_of(devices, panels)) + spaces,
        [VMEM] * 11,
        [
            pltpu.VMEM((5 * Q, 5 * ROWS, LANES), jnp.float32),
            pltpu.VMEM((4 * Q, 3 * ROWS, LANES), jnp.float32),
            pltpu.VMEM((3, Q, 5, ROWS, LANES), jnp.float32),
            pltpu.VMEM((3, 5, 5, 2, ROWS, LANES), jnp.float32),
            pltpu.VMEM((4, ROWS, LANES), jnp.float32),
        ],
        name="steps",
        aliases={7 + n: 2 + n for n in range(4)},
    )(state, field, names, first_near, second_near, first_far, second_far, *laid)
    gathered = lax.all_to_all(sums, ("gx", "gy"), 0, 0, tiled=True)
    totals, adjoint = pl.pallas_call(
        finish,
        out_shape=(shape_of(1, panels), shape_of(Q, ROWS, 2 * LANES)),
        in_specs=[VMEM, VMEM],
        out_specs=(HBM, HBM),
        scratch_shapes=[pltpu.VMEM((1, panels), jnp.float32), pltpu.SemaphoreType.DMA((2,))],
        compiler_params=params,
        name="finish",
    )(gathered.reshape(devices, 1, panels), adjoint)
    return adjoint, totals.reshape(panels)


def solution(mesh):
    sizes = (mesh.shape["gx"], mesh.shape["gy"])
    in_specs = (P(None, "gx", "gy"), P(None, "gx", "gy"), P(None, "gx", "gy"), P(), P("gx", "gy"))
    out_specs = (P(None, "gx", "gy"), P())
    return jax.shard_map(
        functools.partial(on_device, sizes),
        mesh=mesh,
        in_specs=in_specs,
        out_specs=out_specs,
        check_vma=False,
    )
```

```python
import functools

import jax
import jax.numpy as jnp
import numpy as np
from jax import lax
from jax.experimental import pallas as pl
from jax.experimental.pallas import tpu as pltpu
from jax.sharding import PartitionSpec as P

Q = 19
STEPS = 4
NZ = 32
ROWS = 8
LANES = 128
OMEGA = 1.6
ACCEL = (0.002, 0.0, -0.003)
SHIFT = tuple(a / OMEGA for a in ACCEL)

VELOCITIES = [
    (0, 0, 0),
    (1, 0, 0),
    (-1, 0, 0),
    (0, 1, 0),
    (0, -1, 0),
    (0, 0, 1),
    (0, 0, -1),
    (1, 1, 0),
    (-1, -1, 0),
    (1, -1, 0),
    (-1, 1, 0),
    (1, 0, 1),
    (-1, 0, -1),
    (1, 0, -1),
    (-1, 0, 1),
    (0, 1, 1),
    (0, -1, -1),
    (0, 1, -1),
    (0, -1, 1),
]
OPPOSITE = [0, 2, 1, 4, 3, 6, 5, 8, 7, 10, 9, 12, 11, 14, 13, 16, 15, 18, 17]
PAIRS = [(i, i + 1) for i in range(1, Q, 2)]
W_REST, W_AXIS, W_DIAG = 1.0 / 3.0, 1.0 / 18.0, 1.0 / 36.0

Y_CODE1, Y_CODE2, Y_CODE3, Y_POP, Y_COT = 38, 39, 40, 41, 42
Y_TILES = 43
X_EXTRA = 19
X_LANE = 20
X_HALVES = 10


def x_places(lanes):
    ring = X_LANE * lanes
    code13 = ring + X_HALVES
    code2 = code13 + lanes
    return ring, code13, code2, code2 + (lanes + 1) // 2


EMPTY = 25
FREE = NZ - EMPTY
WEIGHTS = [W_REST] + [W_AXIS] * 6 + [W_DIAG] * 12
LEVEL = [i for i, v in enumerate(VELOCITIES) if v[2] < 1]
OWN_PHI = 4


def turned(axis, outward):
    return [i for i, v in enumerate(VELOCITIES) if v[axis] == outward and sum(map(abs, v)) == 2]


def total(values):
    values = list(values)
    while len(values) > 1:
        values = [a + b for a, b in zip(values[::2], values[1::2])] + (
            [values[-1]] if len(values) % 2 else []
        )
    return values[0]


def along(vector, three):
    terms = None
    for c, value in zip(vector, three):
        if c == 0:
            continue
        if terms is None:
            terms = value if c > 0 else -value
        else:
            terms = terms + value if c > 0 else terms - value
    return terms


def moments(f):
    plus = {i: f[i] + f[o] for i, o in PAIRS}
    minus = {i: f[i] - f[o] for i, o in PAIRS}
    rho = total([f[0]] + [plus[i] for i, _ in PAIRS])
    rinv = 1.0 / rho
    u = []
    for axis in range(3):
        terms = [
            minus[i] if VELOCITIES[i][axis] > 0 else -minus[i]
            for i, _ in PAIRS
            if VELOCITIES[i][axis] != 0
        ]
        u.append(total(terms) * rinv + SHIFT[axis])
    return plus, minus, rho, rinv, u


def coefficients(kind, phi, rinv):
    baffle = kind == 3.0
    gas = kind == 0.0
    even = jnp.where(gas, 0.0, jnp.where(baffle, 0.5 - 0.5 * OMEGA * phi, 0.5 * (1.0 - OMEGA)))
    odd = jnp.where(
        gas, 0.0, jnp.where(baffle, (1.0 - 0.5 * OMEGA) * phi - 0.5, 0.5 * (1.0 - OMEGA))
    )
    slope = jnp.where(
        baffle,
        OMEGA * phi,
        jnp.where(kind == 1.0, OMEGA, jnp.where(kind == 2.0, OMEGA * rinv, 0.0)),
    )
    return even, odd, slope


def collide(f, kind, phi, parts):
    plus, minus, rho, rinv, u = parts
    even, odd, slope = coefficients(kind, phi, rinv)
    scale = slope * rho
    rest = 1.0 - 1.5 * (u[0] * u[0] + u[1] * u[1] + u[2] * u[2])
    base = scale * rest + jnp.where(kind == 0.0, 1.0, 0.0)
    out = [None] * Q
    out[0] = 2.0 * even * f[0] + W_REST * base
    for weight, pairs in ((W_AXIS, PAIRS[:3]), (W_DIAG, PAIRS[3:])):
        flat = weight * base
        three = (3.0 * weight) * scale
        for i, o in pairs:
            cu = along(VELOCITIES[i], u)
            lin = three * cu
            ev = even * plus[i] + (flat + 1.5 * lin * cu)
            od = odd * minus[i] + lin
            out[i] = ev + od
            out[o] = ev - od
    return out


def collide_back(b, kind, phi, rho, rinv, u, state=None):
    even, odd, slope = coefficients(kind, phi, rinv)
    plus = {i: b[i] + b[o] for i, o in PAIRS}
    minus = {i: b[i] - b[o] for i, o in PAIRS}
    rest = 1.0 - 1.5 * (u[0] * u[0] + u[1] * u[1] + u[2] * u[2])
    u_half = [1.5 * c for c in u]
    weighted = W_REST * b[0]
    energy = 0.0
    vector = [0.0, 0.0, 0.0]
    for weight, pairs in ((W_AXIS, PAIRS[:3]), (W_DIAG, PAIRS[3:])):
        weighted = weighted + weight * total([plus[i] for i, _ in pairs])
        energies, parts = [], ([], [], [])
        for i, _ in pairs:
            cu = along(VELOCITIES[i], u)
            half = along(VELOCITIES[i], u_half) * plus[i]
            first = minus[i] + half
            energies.append(cu * first)
            second = first + half
            for axis in range(3):
                c = VELOCITIES[i][axis]
                if c:
                    parts[axis].append(second if c > 0 else -second)
        energy = energy + (3.0 * weight) * total(energies)
        vector = [vector[k] + (3.0 * weight) * total(parts[k]) for k in range(3)]
    energy = energy + rest * weighted
    vector = [vector[k] - (3.0 * weighted) * u[k] for k in range(3)]
    push = [slope * v for v in vector]
    inner = total([push[k] * (u[k] - SHIFT[k]) for k in range(3)])
    shared = jnp.where(kind == 2.0, 0.0, slope) * energy - inner
    out = [None] * Q
    out[0] = 2.0 * even * b[0] + shared
    for i, o in PAIRS:
        ev = even * plus[i] + shared
        od = odd * minus[i] + along(VELOCITIES[i], push)
        out[i] = ev + od
        out[o] = ev - od
    if state is None:
        return out, None
    evens = total([plus[i] * (state[i] + state[o]) for i, o in PAIRS])
    odds = total([minus[i] * (state[i] - state[o]) for i, o in PAIRS])
    term = (
        -OMEGA * (b[0] * state[0] + 0.5 * evens)
        + (1.0 - 0.5 * OMEGA) * odds
        + OMEGA * rho * energy
    )
    return out, jnp.where(kind == 3.0, term, 0.0)


def wall_masks(sign_rows, own_low, own_high, edges):
    lane = lax.broadcasted_iota(jnp.int32, (ROWS, LANES), 1)
    row = lax.broadcasted_iota(jnp.int32, (ROWS, LANES), 0)
    x_low, x_high, y_low, y_high = edges
    depth = lane % NZ
    masks = {}
    masks[2, 1] = depth == 0
    masks[2, -1] = depth == NZ - 1
    masks[1, 1] = lane < jnp.where(own_low, y_low * NZ, 0)
    masks[1, -1] = lane >= jnp.where(own_high, LANES - y_high * NZ, LANES)
    if sign_rows:
        masks[0, 1] = row < x_low
        masks[0, -1] = row >= ROWS - x_high
    return masks


def stream_tile(load, sign, masks, lane):
    cross_low, cross_high = lane >= LANES - NZ, lane < NZ
    combined = {}
    out = []
    for i, vector in enumerate(VELOCITIES):
        v = tuple(sign * c for c in vector)
        value = load(i, 0, -v[0], v[1])
        if v[1] == 1:
            value = jnp.where(cross_low, load(i, -1, -v[0], 1), value)
        elif v[1] == -1:
            value = jnp.where(cross_high, load(i, 1, -v[0], -1), value)
        amount = (v[1] * NZ + v[2]) % LANES
        if amount:
            value = pltpu.roll(value, amount, 1)
        outside = None
        if v not in combined:
            for axis in range(3):
                if v[axis] and (axis, v[axis]) in masks:
                    wall = masks[axis, v[axis]]
                    outside = wall if outside is None else outside | wall
            combined[v] = outside
        outside = combined[v]
        if outside is not None:
            value = jnp.where(outside, load(OPPOSITE[i], 0, 0, 0), value)
        out.append(value)
    return out


def iotas():
    row = lax.broadcasted_iota(jnp.int32, (ROWS, LANES), 0)
    lane = lax.broadcasted_iota(jnp.int32, (ROWS, LANES), 1)
    return row, lane, lane // NZ, lane % NZ


def columns(value, count):
    amount = (count * NZ) % LANES
    return pltpu.roll(value, amount, 1) if amount else value


def lines(value, count):
    amount = count % ROWS
    return pltpu.roll(value, amount, 0) if amount else value


class Layout:
    def __init__(self, count, guests, fills):
        self.fills = fills
        hosts = [at for at in fills if at not in guests]
        self.hosts = {at: hosts[4 * n : 4 * n + 4] for n, at in enumerate(guests)}
        self.guests = guests
        kept = [at for at in range(count) if at not in guests]
        self.place = {at: n for n, at in enumerate(kept)}
        self.size = len(kept)


class Packing:
    def __init__(self, ref, layout):
        self.ref, self.layout, self.held = ref, layout, {}

    def __setitem__(self, at, value):
        if at in self.layout.guests:
            self.held[at] = value
        else:
            self.ref[self.layout.place[at]] = value

    def finish(self):
        row, lane, column, depth = iotas()
        spare = depth >= EMPTY
        for at, value in self.held.items():
            for k, host in enumerate(self.layout.hosts[at]):
                place = self.layout.place[host]
                moved = pltpu.roll(value, EMPTY - FREE * k, 1)
                self.ref[place] = jnp.where(spare, moved, self.ref[place])
        for place in range(self.layout.size, self.ref.shape[0]):
            self.ref[place] = jnp.zeros((ROWS, LANES), jnp.float32)


class Unpacking:
    def __init__(self, source, layout):
        self.source, self.layout, self.cache = source, layout, {}
        self.changed = set(layout.guests).union(*layout.hosts.values())

    def __getitem__(self, at):
        if at not in self.cache:
            self.cache[at] = self.read(at)
        return self.cache[at]

    def read(self, at):
        row, lane, column, depth = iotas()
        layout = self.layout
        if at in layout.guests:
            value = None
            for k, host in enumerate(layout.hosts[at]):
                tile = self.source[layout.place[host]]
                moved = pltpu.roll(tile, LANES - (EMPTY - FREE * k), 1)
                value = moved if value is None else jnp.where(depth >= FREE * k, moved, value)
        else:
            value = self.source[layout.place[at]]
        if at in self.changed:
            value = jnp.where(depth >= EMPTY, layout.fills[at], value)
        return value


def layouts():
    y_fills = {2 * i + t: WEIGHTS[i] for i in LEVEL for t in range(2)}
    y_fills.update({Y_POP: W_DIAG, Y_CODE2: 0.0})
    out = [Layout(Y_TILES, [2 * i for i in LEVEL[:6]], y_fills)]
    for lanes, count in ((3, 10), (1, 4)):
        ring, _, code2, tiles = x_places(lanes)
        fills = {ring + n: WEIGHTS[2 * n] for n in range(1, X_HALVES)}
        fills.update({at: 0.0 for at in range(code2, tiles)})
        fills.update({X_LANE * n + i: WEIGHTS[i] for n in range(lanes) for i in LEVEL})
        guests = [X_LANE * (lanes - 1) + i for i in LEVEL[:count]]
        out.append(Layout(tiles, guests, fills))
    return out


class Pick:
    def __init__(self, flag, first, second):
        self.flag, self.first, self.second = flag, first, second

    def __getitem__(self, at):
        return jnp.where(self.flag, self.first[at], self.second[at])


class Deal:
    def __init__(self, even, first, second, layout):
        self.even, self.held, self.ready = even, {}, []
        self.first, self.second = Packing(first, layout), Packing(second, layout)

    def put(self, way, at, value):
        if (-way, at) not in self.held:
            self.held[way, at] = value
            return
        other = self.held.pop((-way, at))
        up, down = (value, other) if way == 1 else (other, value)
        self.add(at, jnp.where(self.even, up, down), jnp.where(self.even, down, up))

    def put_both(self, at, value):
        self.add(at, value, value)

    def add(self, *entry):
        self.ready.append(entry)
        if len(self.ready) == 8:
            self.write()

    def write(self):
        for at, first, second in self.ready:
            self.first[at] = first
            self.second[at] = second
        self.ready = []

    def finish(self):
        self.write()
        self.first.finish()
        self.second.finish()


def is_even(axis):
    return lax.rem(lax.axis_index(axis), 2) == 0


def pack_own(
    f_hbm,
    cot_hbm,
    codes_hbm,
    panels_hbm,
    porosity_hbm,
    first_ref,
    second_ref,
    own_ref,
    state_ref,
    own_cot_ref,
    field_ref,
    names_ref,
    f_ref,
    cot_ref,
    codes_ref,
    panels_ref,
    porosity_ref,
    sems,
):
    pieces = (
        (panels_hbm, panels_ref),
        (porosity_hbm, porosity_ref),
        (f_hbm, f_ref),
        (codes_hbm, codes_ref),
        (cot_hbm, cot_ref),
    )
    copies = [
        pltpu.make_async_copy(source, target, sems.at[n])
        for n, (source, target) in enumerate(pieces)
    ]
    for copy in copies:
        copy.start()
    for copy in copies[:4]:
        copy.wait()
    deal = Deal(is_even("gy"), first_ref, second_ref, layouts()[0])
    row, lane, column, depth = iotas()
    top = depth == NZ - 1

    def tile_of(ref, i, t):
        return ref[i, :, pl.ds(t * LANES, LANES)]

    codes, phis = [], []
    for t in range(2):
        names = panels_ref[0, t * LANES], panels_ref[4, t * LANES]
        phi = jnp.where(row < 4, porosity_ref[names[0]], porosity_ref[names[1]])
        names_ref[t] = jnp.where(row < 4, names[0], names[1])
        kinds = [tile_of(codes_ref, s, t).astype(jnp.float32) for s in range(STEPS)]
        f = [tile_of(f_ref, i, t) for i in range(Q)]
        g = collide(f, kinds[0], phi, moments(f))
        for i in range(Q):
            own_ref[2 * i + t] = g[i]
            state_ref[2 * i + t] = f[i]
        for s in range(STEPS):
            field_ref[2 * s + t] = kinds[s]
        field_ref[2 * OWN_PHI + t] = phi
        codes.append([jnp.where(top, phi, kinds[1]), kinds[2], kinds[3]])
    copies[4].wait()
    for i in range(Q):
        for way in (1, -1):
            near, far = (1, 0) if way == 1 else (0, 1)
            deep = 3 - way * VELOCITIES[i][1]
            cot = tile_of(cot_ref, i, near)
            g_far = own_ref[2 * i + far]
            if way == 1:
                mixed = jnp.where(column >= deep, g_far, columns(cot, deep - 4))
            else:
                mixed = jnp.where(column < 4 - deep, g_far, columns(cot, 4 - deep))
            deal.put(way, 2 * i, mixed if far == 0 else own_ref[2 * i])
            deal.put(way, 2 * i + 1, mixed if far == 1 else own_ref[2 * i + 1])
    for way in (1, -1):
        near, far = (1, 0) if way == 1 else (0, 1)
        outer = 3 if way == 1 else 0
        deal.put(way, Y_CODE1, codes[near][0])
        deal.put(way, Y_CODE2, codes[near][1])
        outside = columns(codes[far][0], 3 - 2 * outer)
        deal.put(way, Y_CODE3, jnp.where(column == 3 - outer, outside, codes[near][2]))
        extra = None
        for k, i in enumerate(turned(1, -way)):
            value = columns(own_ref[2 * i + far], k - outer)
            extra = value if extra is None else jnp.where(column == k, value, extra)
        deal.put(way, Y_POP, extra)
        extra = None
        for k, i in enumerate(turned(1, way)):
            value = columns(tile_of(cot_ref, i, near), k - (1 if way == 1 else 2))
            extra = value if extra is None else jnp.where(column == k, value, extra)
        deal.put(way, Y_COT, extra)
    deal.finish()
    for t in range(2):
        for i in range(Q):
            own_cot_ref[2 * i + t] = tile_of(cot_ref, i, t)


def is_right(near):
    return is_even("gy") if near else jnp.logical_not(is_even("gy"))


def half_lanes(right):
    row, lane, column, depth = iotas()
    return lane // (LANES // 2) == jnp.where(right, 0, 1)


def choose(flag, first, second):
    if isinstance(flag, bool):
        return first() if flag else second()
    return jnp.where(flag, first(), second())


def from_side(message_ref, right):
    row, lane, column, depth = iotas()
    ref = Unpacking(message_ref, layouts()[0])

    def population(i):
        return choose(right, lambda: ref[2 * i], lambda: ref[2 * i + 1])

    def cotangent(i):
        def of(way, place, far):
            deep = 3 - way * VELOCITIES[i][1]
            value = columns(ref[2 * i + far], way * (4 - deep))
            if i in turned(1, way):
                extra = columns(ref[Y_COT], place - turned(1, way).index(i))
                value = jnp.where(column == place, extra, value)
            return value

        return choose(right, lambda: of(-1, 2, 1), lambda: of(1, 1, 0))

    def codes(s):
        return ref[(Y_CODE1, Y_CODE2, Y_CODE3)[s - 1]]

    def outer(i):
        def of(way, far):
            if i in turned(1, -way):
                first = 0 if way == -1 else 3
                return columns(ref[Y_POP], first - turned(1, -way).index(i))
            return ref[2 * i + far]

        return choose(right, lambda: of(-1, 1), lambda: of(1, 0))

    def outer_code():
        tile = ref[Y_CODE3]
        return choose(right, lambda: columns(tile, 1), lambda: columns(tile, 3))

    return population, cotangent, codes, outer, outer_code


def from_y(message_ref, right):
    row, lane, column, depth = iotas()
    ref = Unpacking(message_ref, layouts()[0])
    if isinstance(right, bool):
        return from_side(message_ref, right)

    def population(i):
        return jnp.where(right, ref[2 * i], ref[2 * i + 1])

    def cotangent(i):
        values = []
        for way, place, far in ((1, 1, 0), (-1, 2, 1)):
            deep = 3 - way * VELOCITIES[i][1]
            value = columns(ref[2 * i + far], way * (4 - deep))
            if i in turned(1, way):
                extra = columns(ref[Y_COT], place - turned(1, way).index(i))
                value = jnp.where(column == place, extra, value)
            values.append(value)
        return jnp.where(right, values[1], values[0])

    def codes(s):
        return ref[(Y_CODE1, Y_CODE2, Y_CODE3)[s - 1]]

    def outer(i):
        left, above = ref[2 * i], ref[2 * i + 1]
        if i in turned(1, 1):
            above = columns(ref[Y_POP], -turned(1, 1).index(i))
        if i in turned(1, -1):
            left = columns(ref[Y_POP], 3 - turned(1, -1).index(i))
        return jnp.where(right, above, left)

    def outer_code():
        return jnp.where(right, columns(ref[Y_CODE3], 1), columns(ref[Y_CODE3], 3))

    return population, cotangent, codes, outer, outer_code


def mix_lines(deal, at, pop, cot, deep, way):
    row, lane, column, depth = iotas()
    if way == 1:
        mixed = jnp.where(row >= deep, pop, lines(cot, deep))
    else:
        mixed = jnp.where(row < ROWS - deep, pop, lines(cot, -deep))
    deal.put(way, at, mixed)


def pack_lines(deal, first, population, cotangent):
    row, lane, column, depth = iotas()

    for i in range(Q):
        pop, cot = population(i), cotangent(i)
        for way in (1, -1):
            mix_lines(deal, first + i, pop, cot, 3 - way * VELOCITIES[i][0], way)
    for way in (1, -1):
        extra = None
        for k, i in enumerate(turned(0, -way)):
            value = lines(population(i), k - (3 if way == 1 else 4))
            extra = value if extra is None else jnp.where(row == k, value, extra)
        for k, i in enumerate(turned(0, way)):
            value = lines(cotangent(i), 4 + k - (5 if way == 1 else 2))
            extra = jnp.where(row == 4 + k, value, extra)
        deal.put(way, first + X_EXTRA, extra)


def pack_neighbour(deal, lanes, message_ref, right):
    ring, code13, code2, tiles = x_places(lanes)
    population, cotangent, codes, outer, outer_code = from_y(message_ref, right)
    pack_lines(deal, X_LANE * (lanes - 1), population, cotangent)
    kept = half_lanes(right)
    for n in range(X_HALVES):
        first, second = (outer(2 * n - 1), outer(2 * n)) if n else (outer(0), outer_code())
        deal.put_both(ring + n, jnp.where(kept, first, pltpu.roll(second, LANES // 2, 1)))
    for way in (1, -1):
        mix_lines(deal, code13 + lanes - 1, codes(1), codes(3), 3, way)
    deal.put_both(tiles - 1, codes(2))


def pack_near(own_ref, cot_ref, field_ref, message_ref, first_ref, second_ref):
    row, lane, column, depth = iotas()
    deal = Deal(is_even("gx"), first_ref, second_ref, layouts()[1])
    ring, code13, code2, tiles = x_places(3)
    for t in range(2):
        pack_lines(
            deal,
            X_LANE * t,
            lambda i: own_ref[2 * i + t],
            lambda i: cot_ref[2 * i + t],
        )
        code = jnp.where(depth == NZ - 1, field_ref[2 * OWN_PHI + t], field_ref[2 + t])
        for way in (1, -1):
            mix_lines(deal, code13 + t, code, field_ref[6 + t], 3, way)
    first, second = field_ref[4], lines(field_ref[5], 4)
    deal.put(1, code2, jnp.where(row >= 4, first, second))
    deal.put(-1, code2, jnp.where(row < 4, first, second))
    pack_neighbour(deal, 3, message_ref, is_right(True))
    deal.finish()


def pack_far(message_ref, first_ref, second_ref):
    even_x = is_even("gx")

    def pack(right):
        deal = Deal(even_x, first_ref, second_ref, layouts()[2])
        pack_neighbour(deal, 1, message_ref, right)
        deal.finish()

    above = is_right(False)
    pl.when(above)(lambda: pack(True))
    pl.when(jnp.logical_not(above))(lambda: pack(False))


def from_x(ref, n, way, lanes):
    row, lane, column, depth = iotas()
    ring, code13, code2, _ = x_places(lanes)
    first = X_LANE * n

    def population(i):
        value = ref[first + i]
        if i in turned(0, -way):
            place = 3 if way == 1 else 4
            extra = lines(ref[first + X_EXTRA], place - turned(0, -way).index(i))
            value = jnp.where(row == place, extra, value)
        return value

    def cotangent(i):
        value = lines(ref[first + i], -way * (3 - way * VELOCITIES[i][0]))
        if i in turned(0, way):
            place = 5 if way == 1 else 2
            extra = lines(ref[first + X_EXTRA], place - 4 - turned(0, way).index(i))
            value = jnp.where(row == place, extra, value)
        return value

    def codes(s):
        if s == 2:
            return lines(ref[code2 + n // 2], 4 * (n % 2))
        value = ref[code13 + n]
        return value if s == 1 else lines(value, -3 * way)

    def outer(i):
        value = ref[ring + (i + 1) // 2]
        return pltpu.roll(value, LANES // 2, 1) if i and i % 2 == 0 else value

    def outer_code():
        return pltpu.roll(ref[ring], LANES // 2, 1)

    return population, cotangent, codes, outer, outer_code


def sides(first_ref, second_ref, axis, layout):
    even = is_even(axis)
    picks = Pick(even, second_ref, first_ref), Pick(even, first_ref, second_ref)
    return [Unpacking(pick, layout) for pick in picks]


def own_rows(step=0):
    return pl.ds(ROWS + step, ROWS)


def halo_rows(step=0):
    return pl.ds({0: 2 * ROWS, -1: 2 * ROWS - 1, 1: 1}[step], ROWS)


def put_halo(ref, at, halo):
    ref[at, pl.ds(0, ROWS), :] = halo
    ref[at, halo_rows(), :] = halo


def put_ring(ref, at, own, halo):
    ref[at, own_rows(), :] = own
    put_halo(ref, at, halo)


def expand(code):
    row, lane, column, depth = iotas()
    top = depth == NZ - 1
    phi = jnp.where(top, code, 0.0)
    for step in (1, 2, 4, 8, 16):
        phi = phi + pltpu.roll(phi, LANES - step, 1)
    return jnp.where(top, 0.0, code), phi


def in_groups(size=8):
    return [range(first, min(first + size, Q)) for first in range(0, Q, size)]


def lay_own(c, population, cotangent, codes, code_phi, pop, cot, wide, field):
    for group in in_groups():
        pops = [population(i) for i in group]
        cots = [cotangent(i) for i in group] if cotangent is not None else []
        for i, value in zip(group, pops):
            pop[5 * i + c, pl.ds(2 * ROWS, ROWS), :] = value
        for i, value in zip(group, cots):
            cot[4 * i + c - 1, own_rows(), :] = value
    for n in range(2):
        wide[n, c, 1] = code_phi[n]
    if cotangent is not None:
        field[0, c - 1, 0], field[1, c - 1, 0] = code_phi[1], code_phi[0]
        for s in (2, 3):
            field[s, c - 1, 0] = codes(s)


def lay_halo(c, below, above, pop, cot, wide, field):
    row, lane, column, depth = iotas()
    for group in in_groups():
        pops = [(below[0](i), above[0](i)) for i in group]
        cots = []
        if below[1] is not None:
            cots = [jnp.where(row < 4, above[1](i), below[1](i)) for i in group]
        for i, (before, behind) in zip(group, pops):
            pop[5 * i + c, pl.ds(ROWS, ROWS), :] = before
            pop[5 * i + c, pl.ds(3 * ROWS, ROWS), :] = behind
        for i, value in zip(group, cots):
            put_halo(cot, 4 * i + c - 1, value)
    before, behind = expand(below[2](1)), expand(above[2](1))
    for n in range(2):
        wide[n, c, 0], wide[n, c, 2] = before[n], behind[n]
    if below[1] is not None:
        for n, place in ((0, 1), (1, 0)):
            field[place, c - 1, 1] = jnp.where(row < 4, behind[n], before[n])
        for s in (2, 3):
            field[s, c - 1, 1] = jnp.where(row < 4, above[2](s), below[2](s))


def near_tile():
    return jnp.where(is_right(True), 4, 1)


def lay_out(
    near_y_ref,
    far_y_ref,
    first_near_ref,
    second_near_ref,
    own_ref,
    field_ref,
    cot_ref,
    pop,
    cot,
    wide,
    field,
):
    spaces = pop, cot, wide, field
    below, above = sides(first_near_ref, second_near_ref, "gx", layouts()[1])
    for t in range(2):
        lay_own(
            2 + t,
            lambda i: own_ref[2 * i + t],
            lambda i: cot_ref[2 * i + t],
            lambda s: field_ref[2 * s + t],
            (field_ref[2 + t], field_ref[2 * OWN_PHI + t]),
            *spaces,
        )
        lay_halo(2 + t, from_x(below, t, 1, 3), from_x(above, t, -1, 3), *spaces)
    near, far = from_y(near_y_ref, is_right(True)), from_y(far_y_ref, is_right(False))
    for c, (population, cotangent, codes, _, _) in ((near_tile(), near), (5 - near_tile(), far)):
        lay_own(c, population, cotangent, codes, expand(codes(1)), *spaces)
    kept = half_lanes(is_right(True))
    lay_own(
        0,
        lambda i: jnp.where(kept, near[3](i), far[3](i)),
        None,
        None,
        expand(jnp.where(kept, near[4](), far[4]())),
        *spaces,
    )
    lay_halo(near_tile(), from_x(below, 2, 1, 3), from_x(above, 2, -1, 3), *spaces)


def lay_far(near_refs, far_refs, spaces):
    nears, fars = (
        [
            from_x(ref, lanes - 1, way, lanes)
            for ref, way in zip(sides(*refs, "gx", layout), (1, -1))
        ]
        for refs, layout, lanes in zip((near_refs, far_refs), layouts()[1:], (3, 1))
    )
    lay_halo(5 - near_tile(), *fars, *spaces)
    kept = half_lanes(is_right(True))
    ring = [
        (
            lambda i, near=near, far=far: jnp.where(kept, near[3](i), far[3](i)),
            None,
            lambda s, near=near, far=far: jnp.where(kept, near[4](), far[4]()),
        )
        for near, far in zip(nears, fars)
    ]
    lay_halo(0, *ring, *spaces)


def steps_kernel(
    sizes,
    state_ref,
    own_field_ref,
    names_ref,
    first_near_ref,
    second_near_ref,
    first_far_ref,
    second_far_ref,
    *refs,
):
    adjoint_ref, panel_ref, pop_a, ring_a, wide, field, pop_b, ring_b, saved, mom, grad = refs[4:]
    size_x, size_y = sizes
    lay_far(
        (first_near_ref, second_near_ref),
        (first_far_ref, second_far_ref),
        (pop_a, ring_a, wide, field),
    )

    at_x, at_y = lax.axis_index("gx"), lax.axis_index("gy")
    edges = (
        jnp.where(at_x == 0, 1, 0),
        jnp.where(at_x == size_x - 1, 1, 0),
        jnp.where(at_y == 0, 1, 0),
        jnp.where(at_y == size_y - 1, 1, 0),
    )
    row, lane, column, depth = iotas()
    after = row < 4

    def masks_of(tile, first, r):
        return wall_masks(r == 0, tile == first, tile == first + 1, edges)

    def neighbours(tile, tiles):
        if isinstance(tile, int):
            return {0: tile, -1: (tile - 1) % tiles, 1: (tile + 1) % tiles}
        return {0: tile, -1: lax.rem(tile + tiles - 1, tiles), 1: lax.rem(tile + 1, tiles)}

    def from_wide(ref, tile, r):
        step = neighbours(tile, 5)

        def load(i, tile_step, row_step, move):
            at = 5 * i + step[tile_step]
            before, own, behind = (ref[at, pl.ds(ROWS * n + row_step, ROWS), :] for n in (1, 2, 3))
            return (own, jnp.where(after, behind, before), before, behind)[r]

        return load

    def from_ring(ref, tile, tiles, r):
        step = neighbours(tile, tiles)

        def load(i, tile_step, row_step, move):
            rows = own_rows(row_step) if r == 0 else halo_rows(row_step)
            return ref[tiles * i + step[tile_step], rows, :]

        return load

    def from_outer(ref, r):
        def load(i, tile_step, row_step, move):
            rows = own_rows(row_step) if r == 0 else halo_rows(row_step)
            if tile_step:
                return ref[4 * i + (2 if tile_step < 0 else 1), rows, :]
            cut = {0: 2, 1: 1, -1: 3}[move]
            return jnp.where(column < cut, ref[4 * i + 3, rows, :], ref[4 * i, rows, :])

        return load

    def note(s, tile, r, parts):
        for n, value in enumerate(parts[2:4] + tuple(parts[4])):
            mom[s - 1, n, tile, r] = value

    def first_step(tile, carry):
        place = lax.rem(tile + 4, 5)
        halo = []
        for r in (2, 0, 3):
            f = stream_tile(from_wide(pop_a, tile, r), 1, masks_of(tile, 2, r), lane)
            parts = moments(f)
            at = {2: 0, 0: 1, 3: 2}[r]
            g = collide(f, wide[0, tile, at], wide[1, tile, at], parts)
            if r == 0:
                note(1, place, 0, parts)
                for i in range(Q):
                    saved[0, i, place] = f[i]
            else:
                halo.append(parts[2:4] + tuple(parts[4]))
            for i in range(Q):
                pop_b[5 * i + tile, pl.ds(ROWS * (at + 1), ROWS), :] = g[i]
        for n in range(5):
            mom[0, n, place, 1] = jnp.where(after, halo[1][n], halo[0][n])
        return carry

    lax.fori_loop(0, 5, first_step, 0, unroll=True)

    def second_step(tile, carry):
        out = []
        for r in range(2):
            f = stream_tile(from_wide(pop_b, tile + 1, r), 1, masks_of(tile, 1, r), lane)
            parts = moments(f)
            out.append((f, parts, collide(f, field[2, tile, r], field[0, tile, r], parts)))
        for r in range(2):
            note(2, tile, r, out[r][1])
        for i in range(Q):
            saved[1, i, tile] = out[0][0][i]
            put_ring(ring_b, 4 * i + tile, out[0][2][i], out[1][2][i])
        return carry

    lax.fori_loop(0, 4, second_step, 0, unroll=True)

    def third_step(tile, carry):
        out = []
        for r in range(2):
            f = stream_tile(from_ring(ring_b, tile, 4, r), 1, masks_of(tile, 1, r), lane)
            out.append((f, moments(f)))
        for r in range(2):
            note(3, tile, r, out[r][1])
        for i in range(Q):
            saved[2, i, tile] = out[0][0][i]
        return carry

    lax.fori_loop(0, 4, third_step, 0, unroll=True)

    def back_tile(load, s, tile, r, own):
        b = stream_tile(load, -1, masks_of(4 if tile is None else tile, 1, r), lane)

        def read(get):
            return jnp.where(column < 2, get(3), get(0)) if tile is None else get(tile)

        rho, rinv, *u = [read(lambda at: mom[s - 1, n, at, r]) for n in range(5)]
        kind, phi = read(lambda at: field[s, at, r]), read(lambda at: field[0, at, r])
        state = [saved[s - 1, i, tile] for i in range(Q)] if own else None
        back, term = collide_back(b, kind, phi, rho, rinv, u, state)
        if own:
            grad[tile] = term if s == 3 else grad[tile] + term
        return back

    def last_step(tile, carry):
        out = [back_tile(from_ring(ring_a, tile, 4, r), 3, tile, r, r == 0) for r in range(2)]
        for i in range(Q):
            put_ring(ring_b, 4 * i + tile, out[0][i], out[1][i])
        return carry

    lax.fori_loop(0, 4, last_step, 0, unroll=True)

    for k, tile in enumerate((1, 2, None)):
        out = []
        for r in range(2):
            load = from_outer(ring_b, r) if tile is None else from_ring(ring_b, tile, 4, r)
            out.append(back_tile(load, 2, tile, r, r == 0 and tile is not None))
        for i in range(Q):
            put_ring(ring_a, 3 * i + k, out[0][i], out[1][i])

    for k, tile in enumerate((1, 2, None)):
        out = []
        for r in range(2):
            load = from_ring(ring_a, k, 3, r)
            out.append(back_tile(load, 1, tile, r, r == 0 and tile is not None))
        for i in range(Q):
            put_ring(ring_b, 3 * i + k, out[0][i], out[1][i])

    panel = lax.broadcasted_iota(jnp.int32, panel_ref.shape, 1)
    sums = jnp.zeros(panel_ref.shape, jnp.float32)
    for t in range(2):
        b = stream_tile(from_ring(ring_b, t, 3, 0), -1, masks_of(t, 0, 0), lane)
        f = [state_ref[2 * i + t] for i in range(Q)]
        kind, phi = own_field_ref[t], own_field_ref[2 * OWN_PHI + t]
        _, _, rho, rinv, u = moments(f)
        back, term = collide_back(b, kind, phi, rho, rinv, u, f)
        for i in range(Q):
            adjoint_ref[i, :, pl.ds(t * LANES, LANES)] = back[i]
        term = term + grad[t + 1]
        for part in range(2):
            amount = jnp.sum(jnp.where((row < 4) == (part == 0), term, 0.0))
            name = names_ref[t, 4 * part : 4 * part + 1, 0:1]
            sums = sums + jnp.where(panel == name, amount, 0.0)
    panel_ref[...] = sums


def finish(parts_ref, adjoint_ref, sums_hbm, adjoint_hbm, sums_ref, sems):
    adjoint_copy = pltpu.make_async_copy(adjoint_ref, adjoint_hbm, sems.at[0])
    adjoint_copy.start()
    sums_ref[...] = jnp.sum(parts_ref[...], axis=0)
    sums_copy = pltpu.make_async_copy(sums_ref, sums_hbm, sems.at[1])
    sums_copy.start()
    sums_copy.wait()
    adjoint_copy.wait()


VMEM = pl.BlockSpec(memory_space=pltpu.VMEM)
HBM = pl.BlockSpec(memory_space=pltpu.HBM)


def shape_of(*dims):
    return jax.ShapeDtypeStruct(dims, jnp.float32)


def tiles_of(count):
    return shape_of(count, ROWS, LANES)


def on_device(sizes, checkpoint, cotangent, cell_codes, porosity, baffle_index):
    size_x, size_y = sizes
    panels = porosity.shape[0]
    devices = size_x * size_y
    y_layout, near_layout, far_layout = layouts()

    params = pltpu.CompilerParams(vmem_limit_bytes=32 * 1024 * 1024)

    def call(kernel, out_shape, in_specs, scratch=(), name=None, aliases={}):
        return pl.pallas_call(
            kernel,
            out_shape=out_shape,
            in_specs=in_specs,
            out_specs=jax.tree.map(lambda _: VMEM, out_shape),
            scratch_shapes=scratch,
            input_output_aliases=aliases,
            compiler_params=params,
            name=name,
        )

    def swap(value, axis, size):
        return lax.ppermute(value, axis, [(i, i ^ 1) for i in range(size) if i ^ 1 < size])

    def swap_between(value, axis, size):
        pairs = [(i, i + 1) for i in range(1, size - 1, 2)]
        return lax.ppermute(value, axis, pairs + [(j, i) for i, j in pairs])

    def swap_inner(value):
        pairs = [
            (i * size_y + y, (i + 1) * size_y + y)
            for i in range(1, size_x - 1, 2)
            for y in range(1, size_y - 1)
        ]
        return lax.ppermute(value, ("gx", "gy"), pairs + [(j, i) for i, j in pairs])

    arguments = [
        pltpu.with_memory_space_constraint(value, pltpu.HBM)
        for value in (checkpoint, cotangent, cell_codes, baffle_index, porosity)
    ]
    near_y, far_y, own, state, cot, field, names = call(
        pack_own,
        (tiles_of(y_layout.size),) * 2
        + (tiles_of(2 * Q),) * 3
        + (tiles_of(2 * OWN_PHI + 2), jax.ShapeDtypeStruct((2, ROWS, LANES), jnp.int32)),
        [HBM] * 5,
        [
            pltpu.VMEM((Q, ROWS, 2 * LANES), jnp.float32),
            pltpu.VMEM((Q, ROWS, 2 * LANES), jnp.float32),
            pltpu.VMEM((STEPS, ROWS, 2 * LANES), jnp.int32),
            pltpu.SMEM(baffle_index.shape, jnp.int32),
            pltpu.SMEM(porosity.shape, jnp.float32),
            pltpu.SemaphoreType.DMA((5,)),
        ],
        name="pack_own",
    )(*arguments)
    near_y = swap(near_y, "gy", size_y)
    far_y = swap_between(far_y, "gy", size_y)
    first_near, second_near = call(
        pack_near,
        (tiles_of(near_layout.size), tiles_of(near_layout.size + 1)),
        [VMEM] * 4,
        name="pack_near",
    )(own, cot, field, near_y)
    second_near = swap_between(second_near, "gx", size_x)
    first_near = swap(first_near, "gx", size_x)
    first_far, second_far = call(
        pack_far,
        (tiles_of(far_layout.size), tiles_of(far_layout.size + 1)),
        [VMEM],
        name="pack_far",
    )(far_y)
    second_far = swap_inner(second_far)
    first_far = swap(first_far, "gx", size_x)
    spaces = (
        shape_of(5 * Q, 5 * ROWS, LANES),
        shape_of(4 * Q, 3 * ROWS, LANES),
        shape_of(2, 5, 3, ROWS, LANES),
        shape_of(4, 4, 2, ROWS, LANES),
    )
    laid = call(lay_out, spaces, [VMEM] * 7, name="lay_out")(
        near_y, far_y, first_near, second_near, own, field, cot
    )
    adjoint, sums, *_ = call(
        functools.partial(steps_kernel, sizes),
        (pltpu.VMEM((Q, ROWS, 2 * LANES), jnp.float32), shape_of(devices, panels)) + spaces,
        [VMEM] * 11,
        [
            pltpu.VMEM((5 * Q, 5 * ROWS, LANES), jnp.float32),
            pltpu.VMEM((4 * Q, 3 * ROWS, LANES), jnp.float32),
            pltpu.VMEM((3, Q, 5, ROWS, LANES), jnp.float32),
            pltpu.VMEM((3, 5, 5, 2, ROWS, LANES), jnp.float32),
            pltpu.VMEM((4, ROWS, LANES), jnp.float32),
        ],
        name="steps",
        aliases={7 + n: 2 + n for n in range(4)},
    )(state, field, names, first_near, second_near, first_far, second_far, *laid)
    gathered = lax.all_to_all(sums, ("gx", "gy"), 0, 0, tiled=True)
    totals, adjoint = pl.pallas_call(
        finish,
        out_shape=(shape_of(1, panels), shape_of(Q, ROWS, 2 * LANES)),
        in_specs=[VMEM, VMEM],
        out_specs=(HBM, HBM),
        scratch_shapes=[pltpu.VMEM((1, panels), jnp.float32), pltpu.SemaphoreType.DMA((2,))],
        compiler_params=params,
        name="finish",
    )(gathered.reshape(devices, 1, panels), adjoint)
    return adjoint, totals.reshape(panels)


def solution(mesh):
    sizes = (mesh.shape["gx"], mesh.shape["gy"])
    in_specs = (P(None, "gx", "gy"), P(None, "gx", "gy"), P(None, "gx", "gy"), P(), P("gx", "gy"))
    out_specs = (P(None, "gx", "gy"), P())
    return jax.shard_map(
        functools.partial(on_device, sizes),
        mesh=mesh,
        in_specs=in_specs,
        out_specs=out_specs,
        check_vma=False,
    )
```
